32 devices in a mesh: dp: 8 (over y, x, core), mp: 4 (over z).
Axes of the slice: x: 2, y: 2, z: 4, core: 2. Of those that a mesh axis runs over, the one named last changes fastest.
Arguments:
- hidden_in: bfloat16 [2, 8, 448, 768], P(None, 'dp', None, 'mp'), may hold values from -6 to 6
- encoder_states: bfloat16 [2, 8, 1500, 768], P(None, 'dp'), may hold values from -6 to 6
- cotangent: bfloat16 [2, 8, 448, 768], P(None, 'dp', None, 'mp'), may hold values from -6 to 6
- self_qkv: bfloat16 [768, 3, 768], P('dp', None, 'mp'), may hold values from -0.21875 to 0.21875
- self_out: bfloat16 [768, 768], P(('mp', 'dp')), may hold values from -1.25 to 1.25
- cross_q: bfloat16 [768, 768], P('dp', 'mp'), may hold values from -0.21875 to 0.21875
- cross_kv: bfloat16 [768, 2, 768], P('dp', None, 'mp'), may hold values from -0.21875 to 0.21875
- cross_out: bfloat16 [768, 768], P(('mp', 'dp')), may hold values from -1.75 to 1.75
- fc_in: bfloat16 [768, 3072], P('dp', 'mp'), may hold values from -0.21875 to 0.21875
- fc_out: bfloat16 [3072, 768], P(('mp', 'dp')), may hold values from -0.109375 to 0.109375
- ln_gain: float32 [4, 768], P(None, 'mp'), may hold values from 0.5 to 1.5
- ln_bias: float32 [4, 768], P(None, 'mp'), may hold values from -1.5 to 1.5
- token_lengths: int32 [2, 8], P(None, 'dp'), may hold values from 1 to 448, as said below
- audio_lengths: int32 [2, 8], P(None, 'dp'), may hold values from 375 to 1500, as said below
- corpus_ids: int32 [2, 8], P(None, 'dp'), may hold values from 0 to 9
- corpus_weights: float32 [10], replicated, may hold values from 0.3 to 3
Outputs:
- layer_out: bfloat16 [2, 8, 448, 768], P(None, 'dp', None, 'mp')
- grad_hidden: float32 [2, 8, 448, 768], P(None, 'dp', None, 'mp')
- grad_encoder: float32 [2, 8, 1500, 768], P(None, 'dp', None, 'mp')
- grad_self_qkv: float32 [768, 3, 768], P('dp', None, 'mp')
- grad_self_out: float32 [768, 768], P(('mp', 'dp'))
- grad_cross_q: float32 [768, 768], P('dp', 'mp')
- grad_cross_kv: float32 [768, 2, 768], P('dp', None, 'mp')
- grad_cross_out: float32 [768, 768], P(('mp', 'dp'))
- grad_fc_in: float32 [768, 3072], P('dp', 'mp')
- grad_fc_out: float32 [3072, 768], P(('mp', 'dp'))
- grad_ln_gain: float32 [4, 768], P(None, ('mp', 'dp'))
- grad_ln_bias: float32 [4, 768], P(None, ('mp', 'dp'))
The draws below stay inside these ranges and needn't reach their ends.
Inputs may be any that keep to these rules, and one draw needn't show every extreme that they name: `token_lengths`: each micro-batch's lengths are independent; some sequence of every draw has all 448 tokens live. `audio_lengths`: some sequence of every draw has all 1500 frames live.
All inputs are finite; a program needn't handle non-finite values.
Results may differ from the reference program's by a relative error of at most 0.017.
Values may be sent and summed in bfloat16 or wider, within the bound.
No kernel may reach another device: no remote copies, remote signals or barrier semaphores. Data moves between devices by JAX's collectives and lax.ppermute only.
A program may use at most 192 MiB of HBM per device.

```python
import math
import jax
import jax.numpy as jnp
from jax import lax

D = 768
HEADS = 12
HEAD_DIM = 64
FF = 3072
FRAMES = 1500
LEN = 448
MICRO = 2
CORPORA = 10
SEQS = 8


def draw_token_lengths(key, part):
    key = jax.random.fold_in(key, 11)
    first, second = jax.random.split(key)
    drawn = jax.random.randint(first, (MICRO * SEQS,), 1, LEN + 1)
    chosen = jax.random.randint(second, (), 0, MICRO * SEQS)
    drawn = jnp.where(jnp.arange(MICRO * SEQS) == chosen, LEN, drawn)
    return drawn.reshape(MICRO, SEQS).astype(jnp.int32)


def draw_audio_lengths(key, part):
    key = jax.random.fold_in(key, 23)
    first, second = jax.random.split(key)
    drawn = jax.random.randint(first, (MICRO * SEQS,), FRAMES // 4, FRAMES + 1)
    chosen = jax.random.randint(second, (), 0, MICRO * SEQS)
    drawn = jnp.where(jnp.arange(MICRO * SEQS) == chosen, FRAMES, drawn)
    return drawn.reshape(MICRO, SEQS).astype(jnp.int32)


def place_ends(values, key, low, top_value):
    shape = values.shape
    spot = [jax.random.randint(jax.random.fold_in(key, axis), (), 0, shape[axis]) for axis in range(len(shape))]
    values = values.at[tuple(spot)].set(low)
    longest = shape.index(max(shape))
    spot[longest] = (spot[longest] + 1) % shape[longest]
    return values.at[tuple(spot)].set(top_value)


def level_of(own_key, dims, shards, smallest, top_value):
    def one(position, shards_of):
        draws = jax.random.uniform(jax.random.fold_in(jax.random.fold_in(own_key, 6), position), (shards_of,), jnp.float32, smallest / len(shards), top_value / len(shards))
        return jnp.repeat(jnp.exp(draws), dims[position] // shards_of).reshape((-1,) + (1,) * (len(dims) - position - 1))

    factor_of = one(*shards[0])
    for cut in shards[1:]:
        factor_of = factor_of * one(*cut)
    return factor_of


def noise(own_key, shape, scale, bound, shards=(), held_as=jnp.bfloat16):
    values = jax.random.normal(own_key, shape, jnp.float32) * scale
    if len(shards) > 0:
        values = level_of(own_key, shape, shards, -0.22, 0.18) * values
    return jnp.clip(values, min=-bound, max=bound).astype(held_as)


def setup_inputs(seed: int = 0) -> dict:
    key_list = jax.random.split(jax.random.key(seed), 17)
    hidden_in = noise(key_list[0], (MICRO, SEQS, LEN, D), 1.0, 6.0, ((1, 8), (3, 4)))
    encoder_states = noise(key_list[1], (MICRO, SEQS, FRAMES, D), 1.0, 6.0, ((1, 8),))
    cotangent = noise(key_list[2], (MICRO, SEQS, LEN, D), 1.0, 6.0, ((1, 8), (3, 4)))
    self_qkv = noise(key_list[3], (D, 3, D), D ** -0.5, 0.21875, ((0, 8), (2, 4)))
    self_out = noise(key_list[4], (D, D), (D // 32) ** -0.5, 1.25, ((0, 32),))
    cross_q = noise(key_list[5], (D, D), D ** -0.5, 0.21875, ((0, 8), (1, 4)))
    cross_kv = noise(key_list[6], (D, 2, D), D ** -0.5, 0.21875, ((0, 8), (2, 4)))
    cross_out = noise(key_list[7], (D, D), (D // 64) ** -0.5, 1.75, ((0, 32),))
    fc_in = noise(key_list[8], (D, FF), D ** -0.5, 0.21875, ((0, 8), (1, 4)))
    fc_out = noise(key_list[9], (FF, D), FF ** -0.5, 0.109375, ((0, 32),))
    ln_gain = jnp.clip(1.0 + 0.1 * jax.random.normal(key_list[10], (4, D), jnp.float32), 0.5, 1.5)
    ln_bias = noise(key_list[11], (4, D), 0.3, 1.5, ((1, 4),), jnp.float32)
    token_lengths = draw_token_lengths(jax.random.fold_in(key_list[16], 71), 0)
    audio_lengths = draw_audio_lengths(jax.random.fold_in(key_list[16], 71), 0)
    corpus_ids = place_ends(jax.random.randint(key_list[14], (MICRO, SEQS), 0, CORPORA), jax.random.fold_in(key_list[14], 1), 0, CORPORA - 1).astype(jnp.int32)
    corpus_weights = jnp.clip(jnp.exp(jax.random.uniform(key_list[15], (CORPORA,), jnp.float32, math.log(0.3), math.log(3.0))), 0.3, 3.0)
    return dict(hidden_in=hidden_in, encoder_states=encoder_states, cotangent=cotangent, self_qkv=self_qkv, self_out=self_out, cross_q=cross_q, cross_kv=cross_kv, cross_out=cross_out, fc_in=fc_in, fc_out=fc_out, ln_gain=ln_gain, ln_bias=ln_bias, token_lengths=token_lengths, audio_lengths=audio_lengths, corpus_ids=corpus_ids, corpus_weights=corpus_weights)


@jax.custom_vjp
def low(v):
    return lax.optimization_barrier(v.astype(jnp.bfloat16)).astype(jnp.float32)

@jax.custom_vjp
def low_back(v):
    return v

def low_keep(v):
    return (low(v), None)

def low_pass(kept, grad):
    return (grad,)

def back_keep(v):
    return (v, None)

def back_low(kept, grad):
    return (low(grad),)
low.defvjp(low_keep, low_pass)
low_back.defvjp(back_keep, back_low)

def matmul(left, right):
    return jnp.matmul(left, right, precision=lax.Precision.HIGHEST)

def both_ways(value):
    return low_back(low(value))

def norm_rows(hidden, scale, shift):
    center = lax.optimization_barrier(jnp.mean(hidden, axis=-1, keepdims=True))
    spread = lax.optimization_barrier(jnp.mean(hidden * hidden, axis=-1, keepdims=True)) - center * center
    return (hidden - center) * lax.rsqrt(spread + 1e-05) * scale + shift

def attend(queries, key_heads, value_heads, allowed):
    scores = jnp.einsum('qhe,khe->hqk', queries, key_heads, precision=lax.Precision.HIGHEST)
    scores = low_back(scores * HEAD_DIM ** (-0.5))
    scores = jnp.where(allowed[None], scores, -1e+30)
    probs = low(jax.nn.softmax(scores, axis=-1))
    mixed = jnp.einsum('hqk,khe->qhe', probs, value_heads, precision=lax.Precision.HIGHEST)
    return both_ways(mixed.reshape(mixed.shape[0], D))

def layer(hidden, encoded, params, tok_len, aud_len):
    query_key_value_weight, self_output_weight, cross_query_weight, proj_ckv, cross_output_weight, up_weight, down_weight, gains, shifts = params
    places = jnp.arange(LEN)
    causal = (places[None, :] <= places[:, None]) & (places[None, :] < tok_len)
    heard = jnp.broadcast_to(jnp.arange(FRAMES)[None, :] < aud_len, (LEN, FRAMES))
    normed = low(norm_rows(hidden, gains[0], shifts[0]))
    packed = both_ways(matmul(normed, query_key_value_weight.reshape(D, 3 * D))).reshape(LEN, 3, HEADS, HEAD_DIM)
    mixed = attend(packed[:, 0], packed[:, 1], packed[:, 2], causal)
    hidden = hidden + low_back(matmul(mixed, self_output_weight))
    normed = low(norm_rows(hidden, gains[1], shifts[1]))
    queries = both_ways(matmul(normed, cross_query_weight)).reshape(LEN, HEADS, HEAD_DIM)
    memory = both_ways(matmul(encoded, proj_ckv.reshape(D, 2 * D))).reshape(FRAMES, 2, HEADS, HEAD_DIM)
    mixed = attend(queries, memory[:, 0], memory[:, 1], heard)
    hidden = hidden + low_back(matmul(mixed, cross_output_weight))
    normed = low(norm_rows(hidden, gains[2], shifts[2]))
    inner_hidden = low(jax.nn.gelu(low_back(matmul(normed, up_weight)), approximate=False))
    hidden = hidden + low_back(matmul(inner_hidden, down_weight))
    return norm_rows(hidden, gains[3], shifts[3])

def flatten(array):
    return array.reshape((MICRO * SEQS,) + array.shape[2:])

def reference(hidden_in, encoder_states, cotangent, self_qkv, self_out, cross_q, cross_kv, cross_out, fc_in, fc_out, ln_gain, ln_bias, token_lengths, audio_lengths, corpus_ids, corpus_weights):
    params = tuple((w.astype(jnp.float32) for w in (self_qkv, self_out, cross_q, cross_kv, cross_out, fc_in, fc_out)))
    params = params + (ln_gain.astype(jnp.float32), ln_bias.astype(jnp.float32))

    def per_sequence(carry, item):
        hidden, encoded, upstream, tok_len, aud_len, corpus = item

        def forward(hidden_value, encoded_value, weights):
            return layer(hidden_value, encoded_value, weights, tok_len, aud_len)
        output, pull = jax.vjp(forward, hidden.astype(jnp.float32), encoded.astype(jnp.float32), params)
        picked = jnp.sum(jnp.where(jnp.arange(CORPORA) == corpus, corpus_weights, 0.0))
        live = (jnp.arange(LEN) < tok_len).astype(jnp.float32)[:, None]
        d_hidden, d_encoded, d_params = pull(upstream.astype(jnp.float32) * picked * live)
        carry = jax.tree.map(jnp.add, carry, d_params)
        return (carry, (output.astype(jnp.bfloat16), d_hidden, d_encoded))
    start = jax.tree.map(jnp.zeros_like, params)
    items = (flatten(hidden_in), flatten(encoder_states), flatten(cotangent), flatten(token_lengths), flatten(audio_lengths), flatten(corpus_ids))
    totals, (outputs, d_hidden, d_encoded) = lax.scan(per_sequence, start, items)
    outputs = outputs.reshape(hidden_in.shape)
    d_hidden = d_hidden.reshape(hidden_in.shape)
    d_encoded = d_encoded.reshape(encoder_states.shape)
    return (outputs, d_hidden, d_encoded, totals[0], totals[1], totals[2], totals[3], totals[4], totals[5], totals[6], totals[7], totals[8])
```

```python
from functools import partial

import jax
import jax.numpy as jnp
from jax import lax
from jax.sharding import PartitionSpec as P

D = 768
HEAD_DIM = 64
BF = jnp.bfloat16
F32 = jnp.float32
AXES = ("dp", "mp")


def dot(spec, left, right):
    return jnp.einsum(spec, left, right, preferred_element_type=F32)


class Place:
    def __init__(self, dp, mp):
        self.dp, self.mp = dp, mp
        self.chips = dp // 2
        self.d = lax.axis_index("dp")
        self.z = lax.axis_index("mp")
        self.core = self.d % 2
        self.xy = self.d // 2
        self.micro = self.z % 2
        self.home = self.z // 2

    def move(self, value, route):
        pairs = []
        for xy in range(self.chips):
            for core in range(2):
                for z in range(self.mp):
                    target = route(xy, core, z)
                    if target is not None:
                        txy, tcore, tz = target
                        pairs.append(
                            ((2 * xy + core) * self.mp + z, (2 * txy + tcore) * self.mp + tz)
                        )
        return lax.ppermute(value, AXES, pairs)

    def swap_core(self, value):
        return self.move(value, lambda xy, core, z: (xy, 1 - core, z))

    def swap_xy(self, value, bit):
        return self.move(value, lambda xy, core, z: (xy ^ bit, core, z))

    def column_out(self, value, k):
        def route(xy, core, z):
            return (xy, z // 2, (2 * (z % 2) + core + k) % 4)

        return self.move(value, route)

    def column_back(self, value, k):
        def route(xy, core, z):
            index = (z - k) % 4
            return (xy, index % 2, 2 * core + index // 2)

        return self.move(value, route)

    def rows_in(self, value, k):
        def route(xy, core, z):
            return (xy, z // 2, 2 * core + (z + k) % 2)

        return self.move(value, route)

    def rows_out(self, value, k):
        def route(xy, core, z):
            return (xy, z // 2, 2 * core + (z % 2 - k) % 2)

        return self.move(value, route)


def gather_weight(place, shard):
    if place.chips != 4:
        whole = lax.all_gather(shard, ("mp", "dp"), axis=0)
        whole = whole.reshape((2, 2, place.dp) + shard.shape)
        return lax.dynamic_index_in_dim(whole, place.core, 0, keepdims=False)
    own = jnp.stack([place.column_out(shard, k) for k in range(4)])
    from_x = place.swap_xy(own, 1)
    from_y = place.swap_xy(own, 2)
    corner_a = place.swap_xy(from_y[:2], 1)
    corner_b = place.swap_xy(from_x[2:], 2)
    pieces = jnp.concatenate([own, from_x, from_y, corner_a, corner_b])
    blocks = []
    for half in range(2):
        for d in range(8):
            slot = (place.z - (2 * half + d % 2)) % 4
            index = ((d // 2) ^ place.xy) * 4 + slot
            blocks.append(lax.dynamic_index_in_dim(pieces, index, 0, keepdims=False))
    return jnp.stack(blocks).reshape((2, 8) + shard.shape)


def add_up(*terms):
    total = terms[0].astype(F32)
    for term in terms[1:]:
        total = total + term.astype(F32)
    return total


def scatter_weight(place, grad):
    shape = grad.shape[2:]
    if place.chips != 4:
        whole = jnp.zeros((2,) + grad.shape, F32)
        whole = lax.dynamic_update_index_in_dim(whole, grad, place.core, 0)
        whole = whole.reshape((4 * place.dp,) + shape)
        return lax.psum_scatter(whole, ("mp", "dp"), scatter_dimension=0, tiled=False)
    grad = grad.astype(BF).reshape((2, 4, 2) + shape)
    here, to_x, to_y, corner = (
        lax.dynamic_index_in_dim(grad, place.xy ^ r, 1, keepdims=False) for r in range(4)
    )
    via_x = place.swap_xy(corner[:1], 1)
    via_y = place.swap_xy(corner[1:], 2)
    to_y = jnp.concatenate([add_up(to_y[:1], via_x).astype(BF), to_y[1:]])
    to_x = jnp.concatenate([to_x[:1], add_up(to_x[1:], via_y).astype(BF)])
    in_x = place.swap_xy(to_x, 1)
    in_y = place.swap_xy(to_y, 2)
    mine = add_up(here, in_x, in_y).astype(BF).reshape((4,) + shape)
    parts = []
    for k in range(4):
        block = lax.dynamic_index_in_dim(mine, (place.z - k) % 4, 0, keepdims=False)
        parts.append(place.column_back(block, k))
    return add_up(*parts)


def rows_to_chip(place, value):
    value = value[:, 0]
    got = []
    for k in range(2):
        block = lax.dynamic_index_in_dim(value, (place.z + k) % 2, 0, keepdims=False)
        got.append(place.rows_in(block, k))
    even = place.micro == 0
    mine = jnp.concatenate(
        [jnp.where(even, got[0], got[1]), jnp.where(even, got[1], got[0])], axis=1
    )
    other = place.swap_core(mine)
    first = place.core == 0
    return jnp.concatenate(
        [jnp.where(first, mine, other), jnp.where(first, other, mine)], axis=1
    )


def rows_from_chip(place, half):
    quarter = half.shape[1] // 2
    even = place.micro == 0
    left, right = half[:, :quarter], half[:, quarter:]
    got = [
        place.rows_out(jnp.where(even, left, right), 0),
        place.rows_out(jnp.where(even, right, left), 1),
    ]
    even = place.z % 2 == 0
    return jnp.stack([jnp.where(even, got[0], got[1]), jnp.where(even, got[1], got[0])])[:, None]


def core_half(place, value):
    width = value.shape[1] // 2
    return lax.dynamic_slice_in_dim(value, place.core * width, width, 1)


def norm(hidden, scale, shift):
    center = jnp.mean(hidden, axis=-1, keepdims=True)
    inverse = lax.rsqrt(jnp.mean(hidden * hidden, axis=-1, keepdims=True) - center * center + 1e-05)
    unit = (hidden - center) * inverse
    return unit * scale + shift, unit, inverse


def norm_back(grad, unit, inverse, scale):
    scaled = grad * scale
    first = jnp.mean(scaled, axis=-1, keepdims=True)
    second = jnp.mean(scaled * unit, axis=-1, keepdims=True)
    d_input = inverse * (scaled - first - unit * second)
    return d_input, jnp.sum(grad * unit, axis=0), jnp.sum(grad, axis=0)


def split_heads(value):
    return value.reshape(value.shape[0], value.shape[1] // HEAD_DIM, HEAD_DIM)


def probabilities(q, k, allowed):
    scores = dot("qhe,khe->hqk", split_heads(q), split_heads(k)) * HEAD_DIM ** (-0.5)
    return jax.nn.softmax(jnp.where(allowed[None], scores, -1e30), axis=-1)


def attend(q, k, v, allowed):
    probs = probabilities(q, k, allowed).astype(BF)
    return dot("hqk,khe->qhe", probs, split_heads(v)).reshape(q.shape).astype(BF)


def attend_back(q, k, v, allowed, d_mixed):
    probs = probabilities(q, k, allowed)
    d_split = split_heads(d_mixed)
    d_probs = dot("qhe,khe->hqk", d_split, split_heads(v))
    dv = dot("hqk,qhe->khe", probs.astype(BF), d_split)
    ds = (probs * (d_probs - jnp.sum(d_probs * probs, axis=-1, keepdims=True))).astype(BF)
    dq = dot("hqk,khe->qhe", ds, split_heads(k)) * HEAD_DIM ** (-0.5)
    dk = dot("hqk,qhe->khe", ds, split_heads(q)) * HEAD_DIM ** (-0.5)
    return (
        dq.reshape(q.shape).astype(BF),
        dk.reshape(k.shape).astype(BF),
        dv.reshape(v.shape).astype(BF),
    )


def per_device(
    dp,
    mp,
    hidden_in,
    encoder_states,
    cotangent,
    self_qkv,
    self_out,
    cross_q,
    cross_kv,
    cross_out,
    fc_in,
    fc_out,
    ln_gain,
    ln_bias,
    token_lengths,
    audio_lengths,
    corpus_ids,
    corpus_weights,
):
    place = Place(dp, mp)
    rows = self_qkv.shape[0]
    out_rows = self_out.shape[0]
    gelu = partial(jax.nn.gelu, approximate=False)

    numbers = jnp.concatenate([token_lengths, audio_lengths, corpus_ids], axis=1)
    other_numbers = place.swap_core(numbers)
    numbers = jnp.where(place.home == place.core, numbers, other_numbers)
    numbers = lax.dynamic_index_in_dim(numbers, place.micro, 0, keepdims=False)
    tok_len, aud_len, corpus = numbers[0], numbers[1], numbers[2]
    norms = lax.all_gather(jnp.concatenate([ln_gain, ln_bias]), "mp", axis=1, tiled=True)
    gains, shifts = norms[:4], norms[4:]

    hidden = rows_to_chip(place, hidden_in)
    encoded = lax.dynamic_index_in_dim(encoder_states[:, 0], place.micro, 0, keepdims=False)
    other_encoded = place.move(
        encoded, lambda xy, core, z: (xy, 1 - core, z) if core == z // 2 else None
    )
    encoded = jnp.where(place.home == place.core, encoded, other_encoded)

    def by_columns(value):
        return value.reshape(2, value.shape[1] * value.shape[2], value.shape[3])

    m1 = by_columns(gather_weight(place, self_qkv.reshape(rows, -1)))
    m2 = by_columns(
        gather_weight(place, jnp.concatenate([cross_kv.reshape(rows, -1), cross_q], axis=1))
    )
    m3 = gather_weight(place, jnp.concatenate([self_out, cross_out]))
    up = by_columns(gather_weight(place, fc_in))
    down = by_columns(gather_weight(place, fc_out))
    cot = rows_to_chip(place, cotangent)

    quarter = D // 4
    half = D // 2

    def columns(value, count):
        value = value.reshape(2, D, count, quarter)
        return value.transpose(1, 2, 0, 3).reshape(D, count, half)

    w_qkv = columns(m1, 3)
    w_kvq = columns(m2, 3)
    w_out = m3[:, :, :out_rows].reshape(half, D)
    w_cout = m3[:, :, out_rows:].reshape(half, D)
    w_up = up.transpose(1, 0, 2).reshape(D, -1)
    w_down = down.reshape(-1, D)

    length = hidden.shape[0]
    frames = encoded.shape[0]
    places = jnp.arange(length)
    causal = (places[None, :] <= places[:, None]) & (places[None, :] < tok_len)
    heard = jnp.broadcast_to(jnp.arange(frames)[None, :] < aud_len, (length, frames))

    def both(value):
        value = value.astype(BF)
        return value.astype(F32) + place.swap_core(value).astype(F32)

    memory = dot("fd,dcg->fcg", encoded, w_kvq[:, :2]).astype(BF)
    hidden0 = hidden.astype(F32)
    normed, unit_one, inverse_one = norm(hidden0, gains[0], shifts[0])
    a = normed.astype(BF)
    packed = dot("nx,xjw->njw", a, w_qkv).astype(BF)
    o1 = attend(packed[:, 0], packed[:, 1], packed[:, 2], causal)
    hidden1 = hidden0 + both(dot("zn,nr->zr", o1, w_out))
    normed, unit_two, inverse_two = norm(hidden1, gains[1], shifts[1])
    c = normed.astype(BF)
    q2 = dot("bk,ku->bu", c, w_kvq[:, 2]).astype(BF)
    o2 = attend(q2, memory[:, 0], memory[:, 1], heard)
    hidden2 = hidden1 + both(dot("zn,nr->zr", o2, w_cout))
    normed, unit_three, inverse_three = norm(hidden2, gains[2], shifts[2])
    m = normed.astype(BF)
    z = dot("bk,ku->bu", m, w_up)
    inner = gelu(z).astype(BF)
    hidden3 = hidden2 + both(dot("zn,nr->zr", inner, w_down))
    final, unit_four, inverse_four = norm(hidden3, gains[3], shifts[3])
    layer_out = rows_from_chip(place, core_half(place, final.astype(BF)))

    picked = jnp.sum(jnp.where(corpus == jnp.arange(corpus_weights.shape[0]), corpus_weights, 0.0))
    live = (places < tok_len).astype(F32)[:, None]
    upstream = cot.astype(F32) * (picked * live)
    d3, gain_four, shift_four = norm_back(upstream, unit_four, inverse_four, gains[3])
    e3 = d3.astype(BF)
    g_down = dot("tw,tg->wg", inner, e3)
    d_inner = dot("iy,py->ip", e3, w_down)
    dz = jax.vjp(gelu, z)[1](d_inner)[0].astype(BF)
    g_up = dot("bm,bg->mg", m, dz)
    part, gain_three, shift_three = norm_back(
        both(dot("cj,rj->cr", dz, w_up)), unit_three, inverse_three, gains[2]
    )
    d2 = d3 + part
    e2 = d2.astype(BF)
    g_cout = dot("tw,tg->wg", o2, e2)
    d_mixed = dot("iy,py->ip", e2, w_cout).astype(BF)
    dq2, dk2, dv2 = attend_back(q2, memory[:, 0], memory[:, 1], heard, d_mixed)
    d_memory = jnp.stack([dk2, dv2], axis=1)
    g_cq = dot("bm,bg->mg", c, dq2)
    g_ckv = dot("fd,fcg->dcg", encoded, d_memory)
    d_encoded = dot("fcg,dcg->fd", d_memory, w_kvq[:, :2])
    part, gain_two, shift_two = norm_back(
        both(dot("cj,rj->cr", dq2, w_kvq[:, 2])), unit_two, inverse_two, gains[1]
    )
    d1 = d2 + part
    e1 = d1.astype(BF)
    g_out = dot("tw,tg->wg", o1, e1)
    d_mixed = dot("iy,py->ip", e1, w_out).astype(BF)
    dq, dk, dv = attend_back(packed[:, 0], packed[:, 1], packed[:, 2], causal, d_mixed)
    d_packed = jnp.stack([dq, dk, dv], axis=1)
    g_qkv = dot("ja,jqm->aqm", a, d_packed)
    part, gain_one, shift_one = norm_back(
        both(dot("eia,bia->eb", d_packed, w_qkv)), unit_one, inverse_one, gains[0]
    )
    grad_hidden = rows_from_chip(place, core_half(place, (d1 + part).astype(BF))).astype(F32)

    d_encoded = d_encoded.astype(BF)
    mine = core_half(place, d_encoded)
    theirs = lax.dynamic_slice_in_dim(d_encoded, (1 - place.core) * half, half, 1)
    mine = add_up(mine, place.swap_core(theirs)).astype(BF)
    grad_encoder = rows_from_chip(place, mine).astype(F32)

    def from_columns(value, count):
        value = value.reshape(D, count, 2, quarter).transpose(2, 0, 1, 3)
        return value.reshape(2, place.dp, rows, count * quarter)

    s_down = scatter_weight(place, g_down.reshape(2, place.dp, -1, D))
    s_up = scatter_weight(
        place, g_up.reshape(D, 2, -1).transpose(1, 0, 2).reshape(2, place.dp, rows, -1)
    )
    g_outs = jnp.concatenate(
        [g_out.reshape(2, place.dp, out_rows, D), g_cout.reshape(2, place.dp, out_rows, D)], axis=2
    )
    s_kvq = scatter_weight(
        place, from_columns(jnp.concatenate([g_ckv, g_cq[:, None]], axis=1), 3)
    )
    s_outs = scatter_weight(place, g_outs)
    s_qkv = scatter_weight(place, from_columns(g_qkv, 3))

    norm_terms = jnp.stack(
        [gain_one, gain_two, gain_three, gain_four, shift_one, shift_two, shift_three, shift_four]
    )
    norm_terms = 0.5 * norm_terms.T
    norm_shares = lax.psum_scatter(norm_terms, ("mp", "dp"), scatter_dimension=0, tiled=True).T
    kv = 2 * quarter
    return (
        layer_out,
        grad_hidden,
        grad_encoder,
        s_qkv.reshape(rows, 3, quarter),
        s_outs[:out_rows],
        s_kvq[:, kv:],
        s_kvq[:, :kv].reshape(rows, 2, quarter),
        s_outs[out_rows:],
        s_up,
        s_down,
        norm_shares[:4],
        norm_shares[4:],
    )


def solution(mesh):
    rows = P(None, "dp", None, "mp")
    columns = P("dp", None, "mp")
    pairs = P("dp", "mp")
    units = P(("mp", "dp"), None)
    each = P(None, "dp")
    return jax.shard_map(
        partial(per_device, mesh.shape["dp"], mesh.shape["mp"]),
        mesh=mesh,
        in_specs=(
            rows,
            P(None, "dp", None, None),
            rows,
            columns,
            units,
            pairs,
            columns,
            units,
            pairs,
            units,
            P(None, "mp"),
            P(None, "mp"),
            each,
            each,
            each,
            P(),
        ),
        out_specs=(
            rows,
            rows,
            rows,
            columns,
            units,
            pairs,
            columns,
            units,
            pairs,
            units,
            P(None, ("mp", "dp")),
            P(None, ("mp", "dp")),
        ),
        check_vma=False,
    )
```

```python
from functools import partial

import jax
import jax.numpy as jnp
from jax import lax
from jax.experimental import pallas as pl
from jax.experimental.pallas import tpu as pltpu
from jax.sharding import PartitionSpec as P

D = 768
HALF = 384
QUARTER = 192
HEAD_DIM = 64
HEADS = 6
CHUNK = 256
BF = jnp.bfloat16
F32 = jnp.float32
AXES = ("dp", "mp")
VMEM = pl.BlockSpec(memory_space=pltpu.VMEM)
ANY = pl.BlockSpec(memory_space=pl.ANY)


def mm(left, right):
    return jnp.dot(left, right, preferred_element_type=F32)


def mm_t(left, right):
    return lax.dot_general(left, right, (((1,), (1,)), ((), ())), preferred_element_type=F32)


def shaped(shape, dtype=BF):
    return jax.ShapeDtypeStruct(shape, dtype)


def run(body, outs, vmem=(), hbm=(), scratch=(), copies=0, flops=0, out_specs=None):
    args = tuple(vmem) + tuple(hbm)
    scratch = list(scratch)
    if copies:
        scratch.append(pltpu.SemaphoreType.DMA((copies,)))
    moved = sum(a.size * a.dtype.itemsize for a in args) + sum(
        o.size * o.dtype.itemsize for o in outs
    )
    return pl.pallas_call(
        body,
        out_shape=tuple(outs),
        in_specs=[VMEM] * len(vmem) + [ANY] * len(hbm),
        out_specs=tuple(out_specs or [VMEM] * len(outs)),
        scratch_shapes=scratch,
        compiler_params=pltpu.CompilerParams(vmem_limit_bytes=56 * 1024 * 1024),
        cost_estimate=pl.CostEstimate(flops=flops, bytes_accessed=moved, transcendentals=0),
    )(*args)


class Copies:
    def __init__(self, sems):
        self.sems, self.open = sems, []

    def start(self, source, target):
        copy = pltpu.make_async_copy(source, target, self.sems.at[len(self.open)])
        copy.start()
        self.open.append(copy)

    def wait(self):
        for copy in self.open:
            copy.wait()


def where_am_i():
    d = lax.axis_index("dp")
    return d % 2, d // 2, lax.axis_index("mp")


class Place:
    def __init__(self, dp, mp):
        self.dp, self.mp = dp, mp
        self.chips = dp // 2
        self.fast = self.chips == 4
        self.d = lax.axis_index("dp")
        self.z = lax.axis_index("mp")
        self.core = self.d % 2
        self.xy = self.d // 2
        self.micro = self.z % 2
        self.home = self.z // 2

    def move(self, value, route):
        pairs = []
        for xy in range(self.chips):
            for core in range(2):
                for z in range(self.mp):
                    target = route(xy, core, z)
                    if target is not None:
                        txy, tcore, tz = target
                        pairs.append(
                            ((2 * xy + core) * self.mp + z, (2 * txy + tcore) * self.mp + tz)
                        )
        return lax.ppermute(value, AXES, pairs)

    def swap_core(self, value):
        return self.move(value, lambda xy, core, z: (xy, 1 - core, z))

    def swap_xy(self, value, bit):
        return self.move(value, lambda xy, core, z: (xy ^ bit, core, z))

    def swap_z(self, value, bit):
        return self.move(value, lambda xy, core, z: (xy, core, z ^ bit))

    def column_out(self, value, k):
        def route(xy, core, z):
            return (xy, z // 2, (2 * (z % 2) + core + k) % 4)

        return self.move(value, route)

    def column_back(self, value, k):
        def route(xy, core, z):
            index = (z - k) % 4
            return (xy, index % 2, 2 * core + index // 2)

        return self.move(value, route)

    def rows_in(self, value, k):
        def route(xy, core, z):
            return (xy, z // 2, 2 * core + (z + k) % 2)

        return self.move(value, route)

    def rows_out(self, value, k):
        def route(xy, core, z):
            return (xy, z // 2, 2 * core + (z % 2 - k) % 2)

        return self.move(value, route)

    def rows_home(self, blocks):
        got = [self.rows_out(block, k) for k, block in enumerate(blocks)]
        even = self.z % 2 == 0
        return jnp.stack([jnp.where(even, got[0], got[1]), jnp.where(even, got[1], got[0])])[
            :, None
        ]


def norm(hidden):
    center = jnp.mean(hidden, axis=-1, keepdims=True)
    spread = jnp.mean(hidden * hidden, axis=-1, keepdims=True) - center * center
    inverse = lax.rsqrt(spread + 1e-05)
    return (hidden - center) * inverse, inverse


def norm_back(grad, unit, inverse, gain):
    scaled = grad * gain
    first = jnp.mean(scaled, axis=-1, keepdims=True)
    second = jnp.mean(scaled * unit, axis=-1, keepdims=True)
    terms = jnp.concatenate(
        [jnp.sum(grad * unit, axis=0, keepdims=True), jnp.sum(grad, axis=0, keepdims=True)], axis=0
    )
    return inverse * (scaled - first - unit * second), terms


def add_up(*terms):
    total = terms[0].astype(F32)
    for term in terms[1:]:
        total = total + term.astype(F32)
    return total


def prepare(own, other, corpus_weights, length):
    def body(weights_ref, own_ref, other_ref, hidden_ref, cot_ref, norms_ref, nums_ref, blocks, sems):
        core, _, z = where_am_i()
        copies = Copies(sems)
        for k in range(2):
            slot = (z % 2 + k) % 2
            copies.start(own_ref.at[k], blocks.at[2 * core + slot])
            copies.start(other_ref.at[k], blocks.at[2 * (1 - core) + slot])
        copies.wait()
        hidden_ref[...] = jnp.concatenate([blocks[b, :length] for b in range(4)], axis=1)
        cot_ref[...] = jnp.concatenate([blocks[b, length : 2 * length] for b in range(4)], axis=1)
        extra = [blocks[b, 2 * length : 2 * length + 32].astype(F32) for b in range(4)]
        norms_ref[...] = jnp.concatenate([e[0:8] + e[8:16] + e[16:24] for e in extra], axis=1)
        row = extra[0][24:25]
        tok = 256.0 * row[:, 0:1] + row[:, 1:2]
        aud = 256.0 * row[:, 2:3] + row[:, 3:4]
        weights = weights_ref[...]
        places = lax.broadcasted_iota(jnp.int32, weights.shape, 1).astype(F32)
        weight = jnp.sum(jnp.where(places == row[:, 4:5], weights, 0.0), axis=1, keepdims=True)
        index = lax.broadcasted_iota(jnp.int32, (8, 128), 0)
        nums_ref[...] = jnp.where(index == 0, tok, jnp.where(index == 1, aud, weight))

    return run(
        body,
        [
            shaped((length, D)),
            shaped((length, D)),
            shaped((8, D), F32),
            shaped((8, 128), F32),
        ],
        vmem=[corpus_weights.reshape(1, -1)],
        hbm=[own, other],
        scratch=[pltpu.VMEM((4,) + own.shape[1:], BF)],
        copies=4,
    )


def attention_shard(self_qkv, self_out, cross_q, cross_kv, cross_out):
    rows = self_qkv.shape[0]
    outs = jnp.stack([self_out, cross_out]).reshape(2, -1, 2, HALF).transpose(0, 2, 1, 3)
    return jnp.concatenate(
        [
            self_qkv.reshape(rows, -1),
            cross_kv.reshape(rows, -1),
            cross_q,
            outs.reshape(rows, HALF),
        ],
        axis=1,
    )


def pack_attention(parts):
    rows = parts[0].shape[0]
    out_rows = rows // 4

    def body(*refs):
        part_refs, (self_ref, cross_ref, shards, sems) = refs[:4], refs[4:]
        _, _, z = where_am_i()
        copies = Copies(sems)
        for k in range(4):
            copies.start(part_refs[k], shards.at[(z - k + 4) % 4])
        copies.wait()
        for cs in range(2):
            low, high = shards[cs], shards[2 + cs]

            def both(at):
                return [low[:, at : at + QUARTER], high[:, at : at + QUARTER]]

            here = pl.ds(cs * rows, rows)
            self_ref[0, here, :] = jnp.concatenate(both(0) + both(192), axis=1)
            self_ref[1, here, 0:HALF] = jnp.concatenate(both(384), axis=1)
            cross_ref[0, here, :] = jnp.concatenate(both(576) + both(768), axis=1)
            cross_ref[1, here, 0:HALF] = jnp.concatenate(both(960), axis=1)
        outs = [shards[i, :, 1152:1536].astype(F32) for i in range(4)]
        for which, ref in enumerate((self_ref, cross_ref)):
            stack = []
            for q in range(2):
                for i in range(4):
                    at = (2 * which + q) * out_rows
                    stack.append(outs[i][at : at + out_rows])
            ref[1, :, HALF:D] = jnp.concatenate(stack, axis=0).astype(BF)

    return run(
        body,
        [shaped((2, 2 * rows, D)), shaped((2, 2 * rows, D))],
        hbm=parts,
        scratch=[pltpu.VMEM((4, rows, 1536), BF)],
        copies=4,
    )


def pack_units(parts):
    rows = parts[0].shape[0]

    def body(*refs):
        part_refs, (out_ref, sems) = refs[:4], refs[4:]
        _, _, z = where_am_i()
        copies = Copies(sems)
        for k in range(4):
            slot = (z - k + 4) % 4
            for which in range(2):
                copies.start(
                    part_refs[k].at[:, pl.ds(which * D, D)],
                    out_ref.at[which, slot // 2, pl.ds((slot % 2) * rows, rows)],
                )
        copies.wait()

    return run(
        body, [shaped((2, 2, 2 * rows, D))], hbm=parts, copies=8, out_specs=[ANY]
    )[0]


def spread(place, own):
    from_x = place.swap_xy(own, 1)
    from_y = place.swap_xy(own, 2)
    far_one = place.swap_xy(from_y[1], 1)
    far_zero = place.swap_xy(from_x[0], 2)
    return [own, from_x, from_y, far_zero, far_one]


def piece_views(refs, which, xy):
    own, from_x, from_y, far_zero, far_one = refs
    return [
        (own.at[which], xy),
        (from_x.at[which], xy ^ 1),
        (from_y.at[which], xy ^ 2),
        ((far_zero, far_one)[which], xy ^ 3),
    ]


def load_wide(copies, refs, which, xy, target, columns=None):
    if len(refs) != 5:
        copies.start(refs[which], target)
        return
    for view, chip in piece_views(refs, which, xy):
        rows = view.shape[0]
        if columns is not None:
            view = view.at[:, pl.ds(0, columns)]
        copies.start(view, target.at[pl.ds(pl.multiple_of(chip * rows, 16), rows)])


def load_out(copies, refs, xy, target):
    if len(refs) != 5:
        copies.start(refs[2], target)
        return
    for view, chip in piece_views(refs, 1, xy):
        rows = view.shape[0] // 4
        for q in range(2):
            for hi in range(2):
                copies.start(
                    view.at[pl.ds((2 * q + hi) * rows, rows), pl.ds(HALF, HALF)],
                    target.at[q, pl.ds(pl.multiple_of(hi * QUARTER + chip * rows, 16), rows)],
                )


def load_units(copies, refs, which, xy, target):
    if len(refs) != 5:
        copies.start(refs[which], target)
        return
    for view, chip in piece_views(refs, which, xy):
        rows = view.shape[1]
        for hi in range(2):
            copies.start(
                view.at[hi], target.at[hi, pl.ds(pl.multiple_of(chip * rows, 16), rows)]
            )


ATTENTION_COPIES = 4 + 4 + 16
UNIT_COPIES = 16


def gather_plain(place, shard):
    whole = lax.all_gather(shard, ("mp", "dp"), axis=0)
    whole = whole.reshape((2, 2, place.dp) + shard.shape)
    return lax.dynamic_index_in_dim(whole, place.core, 0, keepdims=False)


def attention_plain(place, shard):
    mine = gather_plain(place, shard)
    rows = shard.shape[0]

    def columns(at, count):
        value = mine[..., at : at + count * QUARTER].reshape(2, D, count, QUARTER)
        return value.transpose(1, 2, 0, 3).reshape(D, count * HALF)

    outs = mine[..., 1152:].reshape(2, place.dp, 2, 2, rows // 4, HALF)
    outs = outs.transpose(2, 3, 0, 1, 4, 5).reshape(2, 2, HALF, HALF)
    self_w = [columns(0, 2), columns(384, 1), outs[0]]
    cross_w = [columns(576, 2), columns(960, 1), outs[1]]
    return self_w, cross_w


def units_plain(place, shard):
    mine = gather_plain(place, shard)
    return [mine[..., :D].reshape(2, D, D), mine[..., D:].reshape(2, D, D)]


def head_rows(h):
    return pl.ds(pl.multiple_of(h * HEAD_DIM, HEAD_DIM), HEAD_DIM)


def project(left, pair_ref):
    return jnp.concatenate([mm(left, pair_ref[0]), mm(left, pair_ref[1])], axis=1)


def project_t(left, pair_ref):
    return mm_t(left[:, :HALF], pair_ref[0]) + mm_t(left[:, HALF:], pair_ref[1])


def self_forward(hidden, norms, nums, weights):
    length = hidden.shape[0]

    def body(hidden_ref, norms_ref, nums_ref, *refs):
        w_refs, refs = refs[: len(weights)], refs[len(weights) :]
        part_ref, at_ref, qkv_ref, qt_ref, kt_ref, ot_ref, lse_ref = refs[:7]
        w_qk, w_v, w_out, vt, heads, bias, sems = refs[7:]
        _, xy, _ = where_am_i()
        copies = Copies(sems)
        load_wide(copies, w_refs, 0, xy, w_qk)
        load_wide(copies, w_refs, 1, xy, w_v, HALF)
        load_out(copies, w_refs, xy, w_out)
        unit, _ = norm(hidden_ref[...].astype(F32))
        a = (unit * norms_ref[0:1] + norms_ref[4:5]).astype(BF)
        at_ref[...] = a.T
        keys = lax.broadcasted_iota(jnp.int32, (length, length), 0)
        queries = lax.broadcasted_iota(jnp.int32, (length, length), 1)
        allowed = (keys <= queries) & (keys.astype(F32) < nums_ref[0:1, 0:1])
        bias[...] = jnp.where(allowed, 0.0, -1e30)
        copies.wait()
        qk = mm(a, w_qk[...])
        q = (qk[:, :HALF].astype(BF).astype(F32) * HEAD_DIM ** (-0.5)).astype(BF)
        k = qk[:, HALF:].astype(BF)
        v = mm(a, w_v[...]).astype(BF)
        qkv_ref[:, 0:HALF] = q
        qkv_ref[:, HALF : 2 * HALF] = k
        qkv_ref[:, 2 * HALF :] = v
        qt_ref[...] = q.T
        kt_ref[...] = k.T
        vt[...] = v.T
        for h in range(HEADS):
            heads[h] = k[:, h * HEAD_DIM : (h + 1) * HEAD_DIM]

        def head(h, carry):
            s = mm(heads[h], qt_ref[head_rows(h), :]) + bias[...]
            top = jnp.max(s, axis=0, keepdims=True)
            p = jnp.exp(s - top)
            total = jnp.sum(p, axis=0, keepdims=True)
            o = mm(vt[head_rows(h), :], p.astype(BF))
            ot_ref[head_rows(h), :] = (o / total).astype(BF)
            lse_ref[h] = top + jnp.log(total)
            return carry

        lax.fori_loop(0, HEADS, head, 0)
        part_ref[...] = project(ot_ref[...].T, w_out).astype(BF)

    return run(
        body,
        [
            shaped((length, D)),
            shaped((D, length)),
            shaped((length, 3 * HALF)),
            shaped((HALF, length)),
            shaped((HALF, length)),
            shaped((HALF, length)),
            shaped((HEADS, 1, length), F32),
        ],
        vmem=[hidden, norms, nums],
        hbm=weights,
        scratch=[
            pltpu.VMEM((D, D), BF),
            pltpu.VMEM((D, HALF), BF),
            pltpu.VMEM((2, HALF, HALF), BF),
            pltpu.VMEM((HALF, length), BF),
            pltpu.VMEM((HEADS, length, HEAD_DIM), BF),
            pltpu.VMEM((length, length), F32),
        ],
        copies=ATTENTION_COPIES,
        flops=2 * length * D * 4 * HALF + 4 * length * length * HALF,
    )


def cross_memory(encoded, weights):
    frames = encoded.shape[0]

    def body(enc_ref, *refs):
        w_refs, refs = refs[: len(weights)], refs[len(weights) :]
        kv_ref, kvt_ref, et_ref, w_kv, sems = refs
        _, xy, _ = where_am_i()
        copies = Copies(sems)
        load_wide(copies, w_refs, 0, xy, w_kv)
        copies.wait()

        def step(i, carry):
            here = pl.ds(pl.multiple_of(i * CHUNK, CHUNK), CHUNK)
            rows = enc_ref[here, :]
            kv = mm(rows, w_kv[...]).astype(BF)
            kv_ref[here, :] = kv
            kvt_ref[:, here] = kv.T
            et_ref[:, here] = rows.T
            return carry

        lax.fori_loop(0, frames // CHUNK, step, 0)

    return run(
        body,
        [shaped((frames, D)), shaped((D, frames)), shaped((D, frames))],
        vmem=[encoded],
        hbm=weights,
        scratch=[pltpu.VMEM((D, D), BF)],
        copies=4,
        flops=2 * frames * D * D,
    )


def residual(hidden_ref, mine_ref, other_ref):
    return hidden_ref[...].astype(F32) + (mine_ref[...].astype(F32) + other_ref[...].astype(F32))


def cross_forward(hidden, mine, other, norms, nums, kv, kvt, weights):
    length = hidden.shape[0]
    frames = kv.shape[0]

    def body(hidden_ref, mine_ref, other_ref, norms_ref, nums_ref, kv_ref, kvt_ref, *refs):
        w_refs, refs = refs[: len(weights)], refs[len(weights) :]
        part_ref, h_ref, ct_ref, q_ref, qt_ref, ot_ref, lse_ref = refs[:7]
        w_q, w_out, heads, scores, sems = refs[7:]
        _, xy, _ = where_am_i()
        copies = Copies(sems)
        load_wide(copies, w_refs, 1, xy, w_q, HALF)
        load_out(copies, w_refs, xy, w_out)
        h1 = residual(hidden_ref, mine_ref, other_ref)
        h_ref[...] = h1
        unit, _ = norm(h1)
        c = (unit * norms_ref[1:2] + norms_ref[5:6]).astype(BF)
        ct_ref[...] = c.T
        for h in range(HEADS):
            heads[h] = kv_ref[:, h * HEAD_DIM : (h + 1) * HEAD_DIM]
        copies.wait()
        q = mm(c, w_q[...]).astype(BF)
        q = (q.astype(F32) * HEAD_DIM ** (-0.5)).astype(BF)
        q_ref[...] = q
        qt_ref[...] = q.T
        heard = nums_ref[1:2, 0:1]

        def head(h, carry):
            qt = qt_ref[head_rows(h), :]
            top = None
            for at in range(0, frames, CHUNK):
                s = mm(heads[h, at : at + CHUNK], qt)
                place = lax.broadcasted_iota(jnp.int32, s.shape, 0) + at
                s = jnp.where(place.astype(F32) < heard, s, -1e30)
                scores[at : at + CHUNK] = s
                high = jnp.max(s, axis=0, keepdims=True)
                top = high if top is None else jnp.maximum(top, high)
            total, o = 0.0, 0.0
            values = pl.ds(pl.multiple_of(HALF + h * HEAD_DIM, HEAD_DIM), HEAD_DIM)
            for at in range(0, frames, CHUNK):
                p = jnp.exp(scores[at : at + CHUNK] - top)
                total = total + jnp.sum(p, axis=0, keepdims=True)
                o = o + mm(kvt_ref[values, at : at + CHUNK], p.astype(BF))
            ot_ref[head_rows(h), :] = (o / total).astype(BF)
            lse_ref[h] = top + jnp.log(total)
            return carry

        lax.fori_loop(0, HEADS, head, 0)
        part_ref[...] = project(ot_ref[...].T, w_out).astype(BF)

    return run(
        body,
        [
            shaped((length, D)),
            shaped((length, D), F32),
            shaped((D, length)),
            shaped((length, HALF)),
            shaped((HALF, length)),
            shaped((HALF, length)),
            shaped((HEADS, 1, length), F32),
        ],
        vmem=[hidden, mine, other, norms, nums, kv, kvt],
        hbm=weights,
        scratch=[
            pltpu.VMEM((D, HALF), BF),
            pltpu.VMEM((2, HALF, HALF), BF),
            pltpu.VMEM((HEADS, frames, HEAD_DIM), BF),
            pltpu.VMEM((frames, length), F32),
        ],
        copies=4 + 16,
        flops=2 * length * D * 2 * HALF + 4 * length * frames * HALF,
    )


def units_forward(hidden, mine, other, norms, weights):
    length = hidden.shape[0]

    def body(hidden_ref, mine_ref, other_ref, norms_ref, *refs):
        w_refs, refs = refs[: len(weights)], refs[len(weights) :]
        part_ref, h_ref, mt_ref, slope_ref, it_ref = refs[:5]
        w_up, w_down, inner, sems = refs[5:]
        _, xy, _ = where_am_i()
        copies = Copies(sems)
        load_units(copies, w_refs, 0, xy, w_up)
        load_units(copies, w_refs, 1, xy, w_down)
        h2 = residual(hidden_ref, mine_ref, other_ref)
        h_ref[...] = h2
        unit, _ = norm(h2)
        m = (unit * norms_ref[2:3] + norms_ref[6:7]).astype(BF)
        mt_ref[...] = m.T
        copies.wait()
        for hi in range(2):
            for at in range(0, D, CHUNK):
                here = slice(hi * D + at, hi * D + at + CHUNK)
                z = mm(m, w_up[hi, :, at : at + CHUNK])
                share = 0.5 * (1.0 + lax.erf(z * 0.7071067811865476))
                slope = share + z * (0.3989422804014327 * jnp.exp(-0.5 * z * z))
                value = (z * share).astype(BF)
                inner[:, here] = value
                it_ref[here, :] = value.T
                slope_ref[:, here] = slope.astype(BF)
        for at in range(0, D, CHUNK):
            out = mm(inner[:, :D], w_down[0, :, at : at + CHUNK])
            out = out + mm(inner[:, D:], w_down[1, :, at : at + CHUNK])
            part_ref[:, at : at + CHUNK] = out.astype(BF)

    return run(
        body,
        [
            shaped((length, D)),
            shaped((length, D), F32),
            shaped((D, length)),
            shaped((length, 2 * D)),
            shaped((2 * D, length)),
        ],
        vmem=[hidden, mine, other, norms],
        hbm=weights,
        scratch=[
            pltpu.VMEM((2, D, D), BF),
            pltpu.VMEM((2, D, D), BF),
            pltpu.VMEM((length, 2 * D), BF),
        ],
        copies=2 * UNIT_COPIES,
        flops=8 * length * D * D,
    )


def store_blocks(value, blocks, first_ref, second_ref):
    core, _, z = where_am_i()
    for b in range(4):
        blocks[b] = value[:, b * QUARTER : (b + 1) * QUARTER]
    first_ref[...] = blocks[2 * core + z % 2]
    second_ref[...] = blocks[2 * core + (z + 1) % 2]


def units_backward(hidden, mine, other, norms, nums, cot, slope, weights):
    length = hidden.shape[0]

    def body(hidden_ref, mine_ref, other_ref, norms_ref, nums_ref, cot_ref, slope_ref, *refs):
        w_refs, refs = refs[: len(weights)], refs[len(weights) :]
        part_ref, d_ref, e_ref, dz_ref, terms_ref, first_ref, second_ref = refs[:7]
        w_up, w_down, blocks, sems = refs[7:]
        _, xy, _ = where_am_i()
        copies = Copies(sems)
        load_units(copies, w_refs, 1, xy, w_down)
        load_units(copies, w_refs, 0, xy, w_up)
        unit, inverse = norm(residual(hidden_ref, mine_ref, other_ref))
        final = (unit * norms_ref[3:4] + norms_ref[7:8]).astype(BF)
        store_blocks(final, blocks, first_ref, second_ref)
        live = lax.broadcasted_iota(jnp.int32, (length, 1), 0).astype(F32) < nums_ref[0:1, 0:1]
        grad = cot_ref[...].astype(F32) * jnp.where(live, nums_ref[2:3, 0:1], 0.0)
        d3, terms = norm_back(grad, unit, inverse, norms_ref[3:4])
        d_ref[...] = d3
        terms_ref[...] = terms
        e = d3.astype(BF)
        e_ref[...] = e
        copies.wait()
        for hi in range(2):
            for at in range(0, D, CHUNK):
                here = slice(hi * D + at, hi * D + at + CHUNK)
                d_inner = mm_t(e, w_down[hi, at : at + CHUNK, :])
                dz_ref[:, here] = (slope_ref[:, here].astype(F32) * d_inner).astype(BF)
        for at in range(0, D, CHUNK):
            out = mm_t(dz_ref[:, :D], w_up[0, at : at + CHUNK, :])
            out = out + mm_t(dz_ref[:, D:], w_up[1, at : at + CHUNK, :])
            part_ref[:, at : at + CHUNK] = out.astype(BF)

    return run(
        body,
        [
            shaped((length, D)),
            shaped((length, D), F32),
            shaped((length, D)),
            shaped((length, 2 * D)),
            shaped((2, D), F32),
            shaped((length, QUARTER)),
            shaped((length, QUARTER)),
        ],
        vmem=[hidden, mine, other, norms, nums, cot, slope],
        hbm=weights,
        scratch=[
            pltpu.VMEM((2, D, D), BF),
            pltpu.VMEM((2, D, D), BF),
            pltpu.VMEM((4, length, QUARTER), BF),
        ],
        copies=2 * UNIT_COPIES,
        flops=8 * length * D * D,
    )


def step_back(d_ref, hidden_ref, mine_ref, other_ref, gain):
    unit, inverse = norm(hidden_ref[...].astype(F32))
    grad = mine_ref[...].astype(F32) + other_ref[...].astype(F32)
    part, terms = norm_back(grad, unit, inverse, gain)
    return d_ref[...] + part, terms


def cross_backward(d, hidden, mine, other, norms, nums, kv, kvt, q, qt, ot, lse, weights):
    length = hidden.shape[0]
    frames = kv.shape[0]

    def body(
        d_ref, hidden_ref, mine_ref, other_ref, norms_ref, nums_ref, kv_ref, kvt_ref, q_ref,
        qt_ref, ot_ref, lse_ref, *refs
    ):
        w_refs, refs = refs[: len(weights)], refs[len(weights) :]
        part_ref, d_out_ref, e_ref, dq_ref, dkv_ref, terms_ref = refs[:6]
        w_q, w_out, keys, values, queries, grads, dot_t, dk_h, dv_h, dqt, sems = refs[6:]
        _, xy, _ = where_am_i()
        copies = Copies(sems)
        load_wide(copies, w_refs, 1, xy, w_q, HALF)
        load_out(copies, w_refs, xy, w_out)
        d2, terms = step_back(d_ref, hidden_ref, mine_ref, other_ref, norms_ref[2:3])
        d_out_ref[...] = d2
        terms_ref[...] = terms
        e = d2.astype(BF)
        e_ref[...] = e
        for h in range(HEADS):
            lanes = slice(h * HEAD_DIM, (h + 1) * HEAD_DIM)
            keys[h] = kv_ref[:, lanes]
            values[h] = kv_ref[:, HALF + h * HEAD_DIM : HALF + (h + 1) * HEAD_DIM]
            queries[h] = q_ref[:, lanes]
        copies.wait()
        d_mixed = project_t(e, w_out).astype(BF)
        dot_t[...] = d_mixed.T
        for h in range(HEADS):
            grads[h] = d_mixed[:, h * HEAD_DIM : (h + 1) * HEAD_DIM]
        heard = nums_ref[1:2, 0:1]

        def head(h, carry):
            rows = head_rows(h)
            q_t, do_t = qt_ref[rows, :], dot_t[rows, :]
            q_n, do_n = queries[h], grads[h]
            delta = jnp.sum(do_t.astype(F32) * ot_ref[rows, :].astype(F32), axis=0, keepdims=True)
            level = lse_ref[h]
            total = 0.0
            for at in range(0, frames, CHUNK):
                here = slice(at, at + CHUNK)
                s = mm(keys[h, here], q_t)
                place = lax.broadcasted_iota(jnp.int32, s.shape, 0) + at
                s = jnp.where(place.astype(F32) < heard, s, -1e30)
                p = jnp.exp(s - level)
                dp = mm(values[h, here], do_t)
                ds = (p * (dp - delta)).astype(BF)
                dv_h[h, here] = mm(p.astype(BF), do_n).astype(BF)
                dk_h[h, here] = mm(ds, q_n).astype(BF)
                total = total + mm(kvt_ref[rows, here], ds)
            dqt[rows, :] = (total * HEAD_DIM ** (-0.5)).astype(BF)
            return carry

        lax.fori_loop(0, HEADS, head, 0)
        dq = dqt[...].T
        dq_ref[...] = dq
        part_ref[...] = mm_t(dq, w_q[...]).astype(BF)
        for h in range(HEADS):
            lanes = slice(h * HEAD_DIM, (h + 1) * HEAD_DIM)
            dkv_ref[:, lanes] = dk_h[h]
            dkv_ref[:, HALF + h * HEAD_DIM : HALF + (h + 1) * HEAD_DIM] = dv_h[h]

    return run(
        body,
        [
            shaped((length, D)),
            shaped((length, D), F32),
            shaped((length, D)),
            shaped((length, HALF)),
            shaped((frames, D)),
            shaped((2, D), F32),
        ],
        vmem=[d, hidden, mine, other, norms, nums, kv, kvt, q, qt, ot, lse],
        hbm=weights,
        scratch=[
            pltpu.VMEM((D, HALF), BF),
            pltpu.VMEM((2, HALF, HALF), BF),
            pltpu.VMEM((HEADS, frames, HEAD_DIM), BF),
            pltpu.VMEM((HEADS, frames, HEAD_DIM), BF),
            pltpu.VMEM((HEADS, length, HEAD_DIM), BF),
            pltpu.VMEM((HEADS, length, HEAD_DIM), BF),
            pltpu.VMEM((HALF, length), BF),
            pltpu.VMEM((HEADS, frames, HEAD_DIM), BF),
            pltpu.VMEM((HEADS, frames, HEAD_DIM), BF),
            pltpu.VMEM((HALF, length), BF),
        ],
        copies=4 + 16,
        flops=2 * length * D * 2 * HALF + 10 * length * frames * HALF,
    )


def self_backward(d, hidden, mine, other, norms, nums, qkv, qt, kt, ot, lse, weights):
    length = hidden.shape[0]

    def body(
        d_ref, hidden_ref, mine_ref, other_ref, norms_ref, nums_ref, qkv_ref, qt_ref, kt_ref,
        ot_ref, lse_ref, *refs
    ):
        w_refs, refs = refs[: len(weights)], refs[len(weights) :]
        part_ref, d_out_ref, e_ref, dqkv_ref, terms_ref = refs[:5]
        w_qk, w_v, w_out, qkv_h, grads, dot_t, dk_h, dv_h, dqt, bias, sems = refs[5:]
        _, xy, _ = where_am_i()
        copies = Copies(sems)
        load_out(copies, w_refs, xy, w_out)
        load_wide(copies, w_refs, 0, xy, w_qk)
        load_wide(copies, w_refs, 1, xy, w_v, HALF)
        d1, terms = step_back(d_ref, hidden_ref, mine_ref, other_ref, norms_ref[1:2])
        d_out_ref[...] = d1
        terms_ref[...] = terms
        e = d1.astype(BF)
        e_ref[...] = e
        places = lax.broadcasted_iota(jnp.int32, (length, length), 0)
        queries = lax.broadcasted_iota(jnp.int32, (length, length), 1)
        allowed = (places <= queries) & (places.astype(F32) < nums_ref[0:1, 0:1])
        bias[...] = jnp.where(allowed, 0.0, -1e30)
        for j in range(3):
            for h in range(HEADS):
                lanes = slice(j * HALF + h * HEAD_DIM, j * HALF + (h + 1) * HEAD_DIM)
                qkv_h[j * HEADS + h] = qkv_ref[:, lanes]
        copies.wait()
        d_mixed = project_t(e, w_out).astype(BF)
        dot_t[...] = d_mixed.T
        for h in range(HEADS):
            grads[h] = d_mixed[:, h * HEAD_DIM : (h + 1) * HEAD_DIM]

        def head(h, carry):
            rows = head_rows(h)
            do_t, do_n = dot_t[rows, :], grads[h]
            delta = jnp.sum(do_t.astype(F32) * ot_ref[rows, :].astype(F32), axis=0, keepdims=True)
            s = mm(qkv_h[HEADS + h], qt_ref[rows, :]) + bias[...]
            p = jnp.exp(s - lse_ref[h])
            dp = mm(qkv_h[2 * HEADS + h], do_t)
            ds = (p * (dp - delta)).astype(BF)
            dv_h[h] = mm(p.astype(BF), do_n).astype(BF)
            dk_h[h] = mm(ds, qkv_h[h]).astype(BF)
            dqt[rows, :] = (mm(kt_ref[rows, :], ds) * HEAD_DIM ** (-0.5)).astype(BF)
            return carry

        lax.fori_loop(0, HEADS, head, 0)
        dqkv_ref[:, 0:HALF] = dqt[...].T
        for h in range(HEADS):
            lanes = slice(HALF + h * HEAD_DIM, HALF + (h + 1) * HEAD_DIM)
            dqkv_ref[:, lanes] = dk_h[h]
            lanes = slice(2 * HALF + h * HEAD_DIM, 2 * HALF + (h + 1) * HEAD_DIM)
            dqkv_ref[:, lanes] = dv_h[h]
        out = mm_t(dqkv_ref[:, 0 : 2 * HALF], w_qk[...])
        part_ref[...] = (out + mm_t(dqkv_ref[:, 2 * HALF :], w_v[...])).astype(BF)

    return run(
        body,
        [
            shaped((length, D)),
            shaped((length, D), F32),
            shaped((length, D)),
            shaped((length, 3 * HALF)),
            shaped((2, D), F32),
        ],
        vmem=[d, hidden, mine, other, norms, nums, qkv, qt, kt, ot, lse],
        hbm=weights,
        scratch=[
            pltpu.VMEM((D, D), BF),
            pltpu.VMEM((D, HALF), BF),
            pltpu.VMEM((2, HALF, HALF), BF),
            pltpu.VMEM((3 * HEADS, length, HEAD_DIM), BF),
            pltpu.VMEM((HEADS, length, HEAD_DIM), BF),
            pltpu.VMEM((HALF, length), BF),
            pltpu.VMEM((HEADS, length, HEAD_DIM), BF),
            pltpu.VMEM((HEADS, length, HEAD_DIM), BF),
            pltpu.VMEM((HALF, length), BF),
            pltpu.VMEM((length, length), F32),
        ],
        copies=ATTENTION_COPIES,
        flops=2 * length * D * 4 * HALF + 10 * length * length * HALF,
    )


def finish_hidden(d, hidden, mine, other, norms):
    length = hidden.shape[0]

    def body(d_ref, hidden_ref, mine_ref, other_ref, norms_ref, terms_ref, first_ref, second_ref, blocks):
        d0, terms = step_back(d_ref, hidden_ref, mine_ref, other_ref, norms_ref[0:1])
        terms_ref[...] = terms
        store_blocks(d0.astype(BF), blocks, first_ref, second_ref)

    return run(
        body,
        [shaped((2, D), F32), shaped((length, QUARTER)), shaped((length, QUARTER))],
        vmem=[d, hidden, mine, other, norms],
        scratch=[pltpu.VMEM((4, length, QUARTER), BF)],
    )


def finish_encoder(keep, other):
    frames = keep.shape[0]

    def body(keep_ref, other_ref, first_ref, second_ref, blocks):
        _, _, z = where_am_i()
        total = (keep_ref[...].astype(F32) + other_ref[...].astype(F32)).astype(BF)
        blocks[0] = total[:, :QUARTER]
        blocks[1] = total[:, QUARTER:]
        first_ref[...] = blocks[z % 2]
        second_ref[...] = blocks[(z + 1) % 2]

    return run(
        body,
        [shaped((frames, QUARTER)), shaped((frames, QUARTER))],
        vmem=[keep, other],
        scratch=[pltpu.VMEM((2, frames, QUARTER), BF)],
    )


def block_plan(place):
    if not place.fast:
        return 1, (((1, 0, 0),), ((1, 0, 0),))
    first = ((1, 0, 0), (0, 0, 1), (1, 1, 2), (0, 1, 3))
    second = ((1, 0, 0), (1, 1, 1), (0, 0, 2), (0, 1, 3))
    return 4, (first, second)


def grad_outputs(place, shape):
    if place.fast:
        return [shaped((2,) + shape)] * 4
    return [shaped((1,) + shape)] * 4


def units_grads(place, mt, dz, it, e):
    length = e.shape[0]
    count, plan = block_plan(place)
    rows = D // count

    def body(mt_ref, dz_ref, it_ref, e_ref, *outs):
        _, xy, _ = where_am_i()
        for output, slot, offset in plan[0]:
            chip = xy ^ offset if count > 1 else 0
            here = pl.ds(pl.multiple_of(chip * rows, 16), rows)
            for hi in range(2):
                outs[output][slot, hi] = mm(
                    mt_ref[here, :], dz_ref[:, hi * D : (hi + 1) * D]
                ).astype(BF)
        for output, slot, offset in plan[1]:
            chip = xy ^ offset if count > 1 else 0
            for hi in range(2):
                here = pl.ds(pl.multiple_of(hi * D + chip * rows, 16), rows)
                outs[2 + output][slot, hi] = mm(it_ref[here, :], e_ref[...]).astype(BF)

    return run(
        body,
        grad_outputs(place, (2, rows, D)),
        vmem=[mt, dz, it, e],
        flops=8 * length * D * D,
    )


def attention_grads(place, wide_left, wide_right, left, right, ot, e):
    count, plan = block_plan(place)
    rows = D // count
    few = rows // 4

    def body(wide_left_ref, wide_right_ref, left_ref, right_ref, ot_ref, e_ref, *outs):
        _, xy, _ = where_am_i()
        for output, slot, offset in plan[0]:
            chip = xy ^ offset if count > 1 else 0
            here = pl.ds(pl.multiple_of(chip * rows, 16), rows)
            outs[output][slot] = mm(wide_left_ref[here, :], wide_right_ref[...]).astype(BF)
        for output, slot, offset in plan[1]:
            chip = xy ^ offset if count > 1 else 0
            here = pl.ds(pl.multiple_of(chip * rows, 16), rows)
            target = outs[2 + output]
            target[slot, :, 0:HALF] = mm(left_ref[here, :], right_ref[...]).astype(BF)
            for hi in range(2):
                here = pl.ds(pl.multiple_of(hi * QUARTER + chip * few, 16), few)
                both = mm(ot_ref[here, :], e_ref[...]).astype(BF)
                for q in range(2):
                    at = (2 * q + hi) * few
                    target[slot, at : at + few, HALF:D] = both[:, q * HALF : (q + 1) * HALF]

    return run(
        body,
        grad_outputs(place, (rows, D)),
        vmem=[wide_left, wide_right, left, right, ot, e],
        flops=2 * D * D * wide_right.shape[0] + 4 * D * HALF * e.shape[0],
    )


def encoder_grad(dkv, weights, frames):
    padded = dkv.shape[0]

    def body(dkv_ref, *refs):
        w_refs, (keep_ref, send_ref, w_kv, sems) = refs[: len(weights)], refs[len(weights) :]
        core, xy, _ = where_am_i()
        copies = Copies(sems)
        load_wide(copies, w_refs, 0, xy, w_kv)
        copies.wait()
        mine = pl.ds(pl.multiple_of(core * HALF, HALF), HALF)
        theirs = pl.ds(pl.multiple_of((1 - core) * HALF, HALF), HALF)
        for ref, rows in ((send_ref, theirs), (keep_ref, mine)):
            for at in range(0, padded, CHUNK):
                size = min(CHUNK, frames - at)
                value = mm_t(dkv_ref[at : at + CHUNK, :], w_kv[rows, :]).astype(BF)
                ref[at : at + size, :] = value[:size]

    return run(
        body,
        [shaped((frames, HALF)), shaped((frames, HALF))],
        vmem=[dkv],
        hbm=weights,
        scratch=[pltpu.VMEM((D, D), BF)],
        copies=4,
        flops=2 * padded * D * D,
    )


def sum_plane(place, grads):
    left = []
    for part, (first, second) in enumerate(((1, 2), (2, 1))):
        leave, stay = grads[2 * part], grads[2 * part + 1]
        came = place.swap_xy(leave, first)
        onward = place.swap_xy(add_up(stay[1], came[1]).astype(BF), second)
        left.append((stay, came, onward))
    return left


def column_blocks(place, left, attention):
    shape = left[0][2].shape
    rows = shape[-2] // 2
    width = D if attention else 2 * D
    few = rows // 4

    def body(*refs):
        ins, outs, shards = refs[:6], refs[6:10], refs[10]
        _, _, z = where_am_i()
        sums = [
            add_up(ins[3 * part][0], ins[3 * part + 1][0], ins[3 * part + 2][...])
            for part in range(2)
        ]
        for hi in range(2):
            for cs in range(2):
                here = slice(cs * rows, (cs + 1) * rows)
                if attention:
                    lanes = slice(hi * QUARTER, (hi + 1) * QUARTER)
                    lanes_two = slice(HALF + hi * QUARTER, HALF + (hi + 1) * QUARTER)
                    outs_rows = []
                    for p in range(4):
                        at = (2 * (p // 2) + hi) * 2 * few + cs * few
                        side = HALF + (p % 2) * QUARTER
                        outs_rows.append(sums[1][at : at + few, side : side + QUARTER])
                    value = jnp.concatenate(
                        [
                            sums[0][here, lanes],
                            sums[0][here, lanes_two],
                            sums[1][here, lanes],
                            jnp.concatenate(outs_rows, axis=0),
                        ],
                        axis=1,
                    )
                else:
                    value = jnp.concatenate([sums[0][hi, here], sums[1][hi, here]], axis=1)
                shards[2 * hi + cs] = value.astype(BF)
        for k in range(4):
            outs[k][...] = shards[(z - k + 4) % 4]

    return run(
        body,
        [shaped((rows, width))] * 4,
        vmem=[value for part in left for value in part],
        scratch=[pltpu.VMEM((4, rows, width), BF)],
    )


def sum_weights(place, grads, attention):
    if place.fast:
        blocks = column_blocks(place, sum_plane(place, grads), attention)
        return add_up(*[place.column_back(block, k) for k, block in enumerate(blocks)])
    wide, narrow = grads[1][0], grads[3][0]
    rows = D // place.dp
    if attention:
        value = jnp.stack([wide[:, :HALF], wide[:, HALF:], narrow[:, :HALF]], axis=1)
        value = value.reshape(place.dp, rows, 3, 2, QUARTER).transpose(3, 0, 1, 2, 4)
        value = value.reshape(2, place.dp, rows, 3 * QUARTER)
        outs = narrow[:, HALF:].reshape(2, 2, place.dp, rows // 4, 2, QUARTER)
        outs = outs.transpose(1, 2, 0, 4, 3, 5).reshape(2, place.dp, rows, QUARTER)
        value = jnp.concatenate([value, outs], axis=-1)
    else:
        value = jnp.concatenate(
            [wide.reshape(2, place.dp, rows, D), narrow.reshape(2, place.dp, rows, D)], axis=-1
        )
    whole = jnp.zeros((2,) + value.shape, F32)
    whole = lax.dynamic_update_index_in_dim(whole, value.astype(F32), place.core, 0)
    whole = whole.reshape((4 * place.dp,) + value.shape[2:])
    return lax.psum_scatter(whole, ("mp", "dp"), scatter_dimension=0, tiled=False)


def from_quarters(value):
    few = value.shape[0] // 4
    return value.reshape(4, few, QUARTER).transpose(1, 0, 2).reshape(few, D)


def three_parts(value):
    terms = []
    for _ in range(3):
        term = lax.reduce_precision(value, 8, 7)
        terms.append(term.astype(BF))
        value = value - term
    return jnp.concatenate(terms)


def per_device(
    dp,
    mp,
    hidden_in,
    encoder_states,
    cotangent,
    self_qkv,
    self_out,
    cross_q,
    cross_kv,
    cross_out,
    fc_in,
    fc_out,
    ln_gain,
    ln_bias,
    token_lengths,
    audio_lengths,
    corpus_ids,
    corpus_weights,
):
    place = Place(dp, mp)
    length = hidden_in.shape[2]
    frames = encoder_states.shape[2]
    padded = -(-frames // CHUNK) * CHUNK
    rows = self_qkv.shape[0]

    attention = attention_shard(self_qkv, self_out, cross_q, cross_kv, cross_out)
    units = jnp.concatenate([fc_in, fc_out], axis=1)
    if place.fast:
        own_self, own_cross = pack_attention([place.column_out(attention, k) for k in range(4)])
        w_self = spread(place, own_self)
        w_cross = spread(place, own_cross)
        w_units = spread(place, pack_units([place.column_out(units, k) for k in range(4)]))
    else:
        w_self, w_cross = attention_plain(place, attention)
        w_units = units_plain(place, units)

    numbers = jnp.concatenate(
        [
            token_lengths // 256,
            token_lengths % 256,
            audio_lengths // 256,
            audio_lengths % 256,
            corpus_ids,
        ],
        axis=1,
    ).astype(BF)
    numbers = jnp.pad(numbers[:, None, :], ((0, 0), (0, 7), (0, QUARTER - 5)))
    terms = jnp.broadcast_to(
        three_parts(jnp.concatenate([ln_gain, ln_bias]))[None], (2, 24, QUARTER)
    )
    packed = jnp.concatenate([hidden_in[:, 0], cotangent[:, 0], terms, numbers], axis=1)
    got = []
    for k in range(2):
        block = lax.dynamic_index_in_dim(packed, (place.z + k) % 2, 0, keepdims=False)
        got.append(place.rows_in(block, k))
    got = jnp.stack(got)
    hidden, cot, norms, nums = prepare(got, place.swap_core(got), corpus_weights, length)

    encoded = lax.dynamic_index_in_dim(encoder_states[:, 0], place.micro, 0, keepdims=False)
    other = place.move(encoded, lambda xy, core, z: (xy, 1 - core, z) if core == z // 2 else None)
    encoded = jnp.where(place.home == place.core, encoded, other)
    encoded = jnp.pad(encoded, ((0, padded - frames), (0, 0)))

    part1, at, qkv, qt, kt, ot1, lse1 = self_forward(hidden, norms, nums, w_self)
    other1 = place.swap_core(part1)
    kv, kvt, et = cross_memory(encoded, w_cross)
    part2, h1, ct, q2, qt2, ot2, lse2 = cross_forward(
        hidden, part1, other1, norms, nums, kv, kvt, w_cross
    )
    other2 = place.swap_core(part2)
    part3, h2, mt, slope, it = units_forward(h1, part2, other2, norms, w_units)
    other3 = place.swap_core(part3)
    part, d3, e3, dz, terms3, out_a, out_b = units_backward(
        h2, part3, other3, norms, nums, cot, slope, w_units
    )
    other = place.swap_core(part)
    layer_out = place.rows_home((out_a, out_b))
    g_units = units_grads(place, mt, dz, it, e3)
    part, d2, e2, dq2, dkv, terms2 = cross_backward(
        d3, h2, part, other, norms, nums, kv, kvt, q2, qt2, ot2, lse2, w_cross
    )
    other = place.swap_core(part)
    g_cross = attention_grads(place, et, dkv, ct, dq2, ot2, e2)
    keep, send = encoder_grad(dkv, w_cross, frames)
    part, d1, e1, dqkv, terms1 = self_backward(
        d2, h1, part, other, norms, nums, qkv, qt, kt, ot1, lse1, w_self
    )
    other = place.swap_core(part)
    g_self = attention_grads(
        place, at, dqkv[:, : 2 * HALF], at, dqkv[:, 2 * HALF :], ot1, e1
    )
    terms0, out_a, out_b = finish_hidden(d1, hidden, part, other, norms)
    grad_hidden = place.rows_home((out_a, out_b)).astype(F32)
    grad_encoder = place.rows_home(finish_encoder(keep, place.swap_core(send))).astype(F32)

    s_units = sum_weights(place, g_units, False)
    s_cross = sum_weights(place, g_cross, True)
    s_self = sum_weights(place, g_self, True)

    norm_terms = jnp.stack([terms0, terms1, terms2, terms3], axis=1).reshape(8, D)
    bit = 1
    while bit < place.chips:
        norm_terms = norm_terms + place.swap_xy(norm_terms, bit)
        bit *= 2
    for bit in (1, 2):
        norm_terms = norm_terms + place.swap_z(norm_terms, bit)
    few = D // (place.dp * place.mp)
    shares = lax.dynamic_slice_in_dim(norm_terms, (place.z * place.dp + place.d) * few, few, 1)
    return (
        layer_out,
        grad_hidden,
        grad_encoder,
        s_self[:, : 3 * QUARTER].reshape(rows, 3, QUARTER),
        from_quarters(s_self[:, 3 * QUARTER :]),
        s_cross[:, 2 * QUARTER : 3 * QUARTER],
        s_cross[:, : 2 * QUARTER].reshape(rows, 2, QUARTER),
        from_quarters(s_cross[:, 3 * QUARTER :]),
        s_units[:, :D],
        s_units[:, D:],
        shares[:4],
        shares[4:],
    )


def solution(mesh):
    rows = P(None, "dp", None, "mp")
    columns = P("dp", None, "mp")
    pairs = P("dp", "mp")
    units = P(("mp", "dp"), None)
    each = P(None, "dp")
    return jax.shard_map(
        partial(per_device, mesh.shape["dp"], mesh.shape["mp"]),
        mesh=mesh,
        in_specs=(
            rows,
            P(None, "dp", None, None),
            rows,
            columns,
            units,
            pairs,
            columns,
            units,
            pairs,
            units,
            P(None, "mp"),
            P(None, "mp"),
            each,
            each,
            each,
            P(),
        ),
        out_specs=(
            rows,
            rows,
            rows,
            columns,
            units,
            pairs,
            columns,
            units,
            pairs,
            units,
            P(None, ("mp", "dp")),
            P(None, ("mp", "dp")),
        ),
        check_vma=False,
    )
```

```python
from functools import partial

import jax
import jax.numpy as jnp
from jax import lax
from jax.experimental import pallas as pl
from jax.experimental.pallas import tpu as pltpu
from jax.sharding import PartitionSpec as P

D = 768
HALF = 384
QUARTER = 192
HEAD_DIM = 64
HEADS = 6
CHUNK = 256
BF = jnp.bfloat16
F32 = jnp.float32
AXES = ("dp", "mp")
VMEM = pl.BlockSpec(memory_space=pltpu.VMEM)
SMEM = pl.BlockSpec(memory_space=pltpu.SMEM)
ANY = pl.BlockSpec(memory_space=pl.ANY)


def mm(left, right):
    return jnp.dot(left, right, preferred_element_type=F32)


def mm_t(left, right):
    return lax.dot_general(left, right, (((1,), (1,)), ((), ())), preferred_element_type=F32)


def shaped(shape, dtype=BF):
    return jax.ShapeDtypeStruct(shape, dtype)


def run(body, outs, vmem=(), hbm=(), smem=(), scratch=(), copies=0, micros=2, out_specs=None):
    args = tuple(smem) + tuple(vmem) + tuple(hbm)
    scratch = list(scratch)
    if copies:
        scratch.append(pltpu.SemaphoreType.DMA((copies,)))
    moved = sum(a.size * a.dtype.itemsize for a in args) + sum(
        o.size * o.dtype.itemsize for o in outs
    )
    return pl.pallas_call(
        body,
        out_shape=tuple(outs),
        in_specs=[SMEM] * len(smem) + [VMEM] * len(vmem) + [ANY] * len(hbm),
        out_specs=tuple(out_specs or [VMEM] * len(outs)),
        scratch_shapes=scratch,
        compiler_params=pltpu.CompilerParams(vmem_limit_bytes=56 * 1024 * 1024),
        cost_estimate=pl.CostEstimate(
            flops=int(micros * 1.15e9), bytes_accessed=moved, transcendentals=0
        ),
    )(*args)


class Copies:
    def __init__(self, sems):
        self.sems, self.open = sems, []

    def start(self, source, target):
        copy = pltpu.make_async_copy(source, target, self.sems.at[len(self.open)])
        copy.start()
        self.open.append(copy)

    def wait(self):
        for copy in self.open:
            copy.wait()


def where_am_i():
    d = lax.axis_index("dp")
    return d % 2, d // 2, lax.axis_index("mp")


class Place:
    def __init__(self, dp, mp):
        self.dp, self.mp = dp, mp
        self.chips = dp // 2
        self.fast = self.chips == 4
        self.d = lax.axis_index("dp")
        self.z = lax.axis_index("mp")
        self.core = self.d % 2
        self.xy = self.d // 2
        self.micro = self.z % 2
        self.home = self.z // 2

    def move(self, value, route):
        pairs = []
        for xy in range(self.chips):
            for core in range(2):
                for z in range(self.mp):
                    target = route(xy, core, z)
                    if target is not None:
                        txy, tcore, tz = target
                        pairs.append(
                            ((2 * xy + core) * self.mp + z, (2 * txy + tcore) * self.mp + tz)
                        )
        return lax.ppermute(value, AXES, pairs)

    def swap_core(self, value):
        return self.move(value, lambda xy, core, z: (xy, 1 - core, z))

    def swap_xy(self, value, bit):
        return self.move(value, lambda xy, core, z: (xy ^ bit, core, z))

    def swap_z(self, value, bit):
        return self.move(value, lambda xy, core, z: (xy, core, z ^ bit))

    def column_routes(self):
        def route(step, xy, core, z):
            user, j = z // 2, z % 2
            home = core == user
            near = lambda i: (xy, user, 2 * user + i)
            far = lambda i: (xy, user, 2 * (1 - user) + i)
            if step == 0:
                return near(1 - j) if home else far(1 - j)
            if step == 1:
                return far(j) if home else near(j)
            if step == 2:
                return far(1 - j) if home else near(1 - j)
            return None if home else far(j)

        return [partial(route, step) for step in range(4)]

    def column_out(self, shard):
        return [self.move(shard, route) for route in self.column_routes()]

    def column_back(self, blocks):
        got = []
        for block, route in zip(blocks, self.column_routes()):
            turned = {}
            for xy in range(self.chips):
                for core in range(2):
                    for z in range(self.mp):
                        target = route(xy, core, z)
                        if target is not None:
                            turned[target] = (xy, core, z)
            got.append(self.move(block, lambda xy, core, z: turned.get((xy, core, z))))
        at_home = self.core == self.home
        return add_up(got[0], got[1], got[2], jnp.where(at_home, blocks[3], got[3]))

    def rows_in(self, blocks):
        def route(k, xy, core, z):
            target = (xy, z // 2, 2 * core + (z + k) % 2)
            return None if target == (xy, core, z) else target

        got = [self.move(block, partial(route, k)) for k, block in enumerate(blocks)]
        return jnp.stack([jnp.where(self.core == self.home, blocks[0], got[0]), got[1]])

    def rows_home(self, blocks):
        def route(k, xy, core, z):
            target = (xy, z // 2, 2 * core + (z % 2 - k) % 2)
            return None if target == (xy, core, z) else target

        got = [self.move(block, partial(route, k)) for k, block in enumerate(blocks)]
        got[0] = jnp.where(self.core == self.home, blocks[0], got[0])
        even = self.z % 2 == 0
        both = jnp.stack([jnp.where(even, got[0], got[1]), jnp.where(even, got[1], got[0])])
        return both[:, None].transpose(0, 1, 3, 2)


def norm(hidden):
    center = jnp.mean(hidden, axis=-1, keepdims=True)
    spread = jnp.mean(hidden * hidden, axis=-1, keepdims=True) - center * center
    inverse = lax.rsqrt(spread + 1e-05)
    return (hidden - center) * inverse, inverse


def norm_back(grad, unit, inverse, gain):
    scaled = grad * gain
    first = jnp.mean(scaled, axis=-1, keepdims=True)
    second = jnp.mean(scaled * unit, axis=-1, keepdims=True)
    terms = jnp.concatenate(
        [jnp.sum(grad * unit, axis=0, keepdims=True), jnp.sum(grad, axis=0, keepdims=True)], axis=0
    )
    return inverse * (scaled - first - unit * second), terms


def add_up(*terms):
    total = terms[0].astype(F32)
    for term in terms[1:]:
        total = total + term.astype(F32)
    return total


def input_blocks(hidden, cotangent, terms, numbers):
    _, width, length = hidden.shape
    total = 2 * width + 32

    def body(numbers_ref, hidden_ref, cot_ref, terms_ref, *outs):
        _, _, z = where_am_i()
        lanes = lax.broadcasted_iota(jnp.int32, (8, length), 1)
        for k in range(2):
            micro = (z + k) % 2
            outs[k][0:width] = hidden_ref[micro]
            outs[k][width : 2 * width] = cot_ref[micro]
            tok, aud = numbers_ref[0, micro], numbers_ref[1, micro]
            row = jnp.where(lanes == 0, tok // 256, jnp.where(lanes == 1, tok % 256, 0))
            row = jnp.where(lanes == 2, aud // 256, jnp.where(lanes == 3, aud % 256, row))
            row = jnp.where(lanes == 4, numbers_ref[2, micro], row)
            wide = jnp.concatenate(
                [terms_ref[...].astype(F32), jnp.zeros((24, length - width), F32)], axis=1
            )
            outs[k][2 * width : total] = jnp.concatenate([wide, row.astype(F32)], axis=0).astype(BF)

    return run(
        body,
        [shaped((total, length))] * 2,
        smem=[numbers],
        vmem=[hidden, cotangent, terms],
        micros=1,
    )


def prepare(own, other, corpus_weights):
    length = own.shape[2]

    def body(
        weights_ref, own_ref, other_ref, hidden_ref, cot_ref, norms_ref, nums_ref, wide, extra, sems
    ):
        core, _, z = where_am_i()
        copies = Copies(sems)
        for k in range(2):
            slot = (z % 2 + k) % 2
            for ref, user in ((own_ref, core), (other_ref, 1 - core)):
                block = 2 * user + slot
                here = pl.ds(pl.multiple_of(block * QUARTER, QUARTER), QUARTER)
                for which in range(2):
                    copies.start(ref.at[k, pl.ds(which * QUARTER, QUARTER)], wide.at[which, here])
                copies.start(ref.at[k, pl.ds(2 * QUARTER, 32)], extra.at[block])
        copies.wait()
        hidden_ref[...] = wide[0].T
        cot_ref[...] = wide[1].T
        parts = [extra[b].astype(F32) for b in range(4)]
        norms_ref[...] = jnp.concatenate(
            [(e[0:8] + e[8:16] + e[16:24])[:, :QUARTER] for e in parts], axis=1
        )
        row = parts[0][24:25]
        tok = 256.0 * row[:, 0:1] + row[:, 1:2]
        aud = 256.0 * row[:, 2:3] + row[:, 3:4]
        weights = weights_ref[...]
        places = lax.broadcasted_iota(jnp.int32, weights.shape, 1).astype(F32)
        weight = jnp.sum(jnp.where(places == row[:, 4:5], weights, 0.0), axis=1, keepdims=True)
        index = lax.broadcasted_iota(jnp.int32, (8, 128), 0)
        nums_ref[...] = jnp.where(index == 0, tok, jnp.where(index == 1, aud, weight))

    return run(
        body,
        [
            shaped((length, D)),
            shaped((length, D)),
            shaped((8, D), F32),
            shaped((8, 128), F32),
        ],
        vmem=[corpus_weights.reshape(1, -1)],
        hbm=[own, other],
        scratch=[pltpu.VMEM((2, D, length), BF), pltpu.VMEM((4, 32, length), BF)],
        copies=12,
        micros=3,
    )


def quarters(value):
    return jnp.concatenate([value[:, p * QUARTER : (p + 1) * QUARTER] for p in range(4)], axis=0)


def attention_shards(self_qkv, self_out, cross_q, cross_kv, cross_out):
    rows = cross_q.shape[0]

    def body(qkv_ref, out_ref, q_ref, kv_ref, cout_ref, self_ref, cross_ref):
        out = quarters(out_ref[...].astype(F32)).astype(BF)
        self_ref[...] = jnp.concatenate([qkv_ref[0], qkv_ref[1], qkv_ref[2], out], axis=1)
        out = quarters(cout_ref[...].astype(F32)).astype(BF)
        cross_ref[...] = jnp.concatenate([kv_ref[...], q_ref[...], out], axis=1)

    return run(
        body,
        [shaped((rows, D)), shaped((rows, D))],
        vmem=[self_qkv.transpose(1, 0, 2), self_out, cross_q, cross_kv.reshape(rows, -1), cross_out],
        micros=1,
    )


def column_slots():
    core, _, z = where_am_i()
    j = z % 2
    home = 1 - jnp.abs(z // 2 - core)
    same = core + (1 - 2 * core) * (1 - home)
    return home == 1, (2 * (1 - j) + same, 2 * j + 1 - same, 2 * (1 - j) + 1 - same, 2 * j + same)


def bring_column(part_refs, own_ref, shards, sems):
    home, slots = column_slots()
    copies = Copies(sems)
    for k in range(3):
        copies.start(part_refs[k], shards.at[slots[k]])

    @pl.when(home)
    def _():
        copy = pltpu.make_async_copy(own_ref, shards.at[slots[3]], sems.at[3])
        copy.start()
        copy.wait()

    @pl.when(jnp.logical_not(home))
    def _():
        copy = pltpu.make_async_copy(part_refs[3], shards.at[slots[3]], sems.at[3])
        copy.start()
        copy.wait()

    copies.wait()


def pack_attention(parts, own):
    rows = own.shape[0]
    few = rows // 4

    def body(*refs):
        part_refs, own_ref, (out_ref, shards, sems) = refs[:4], refs[4], refs[5:]
        bring_column(part_refs, own_ref, shards, sems)
        for cs in range(2):
            low, high = shards[cs], shards[2 + cs]

            def both(at):
                return [low[:, at : at + QUARTER], high[:, at : at + QUARTER]]

            here = pl.ds(cs * rows, rows)
            out_ref[0, here, :] = jnp.concatenate(both(0) + both(QUARTER), axis=1)
            out_ref[1, here, 0:HALF] = jnp.concatenate(both(HALF), axis=1)
        outs = [shards[i, :, 3 * QUARTER :].astype(F32) for i in range(4)]
        stack = []
        for q in range(2):
            for i in range(4):
                left = outs[i][2 * q * few : (2 * q + 1) * few]
                right = outs[i][(2 * q + 1) * few : (2 * q + 2) * few]
                stack.append(jnp.concatenate([left, right], axis=1))
        out_ref[1, :, HALF:D] = jnp.concatenate(stack, axis=0).astype(BF)

    return run(
        body,
        [shaped((2, 2 * rows, D))],
        hbm=list(parts) + [own],
        scratch=[pltpu.VMEM((4, rows, D), BF)],
        copies=4,
        micros=2.5,
    )[0]


def pack_units(parts, own):
    rows = own.shape[0]

    def body(*refs):
        part_refs, own_ref, (out_ref, shards, sems) = refs[:4], refs[4], refs[5:]
        bring_column(part_refs, own_ref, shards, sems)
        for which in range(2):
            for hi in range(2):
                for cs in range(2):
                    out_ref[which, hi, cs * rows : (cs + 1) * rows] = shards[
                        2 * hi + cs, :, which * D : (which + 1) * D
                    ]

    return run(
        body,
        [shaped((2, 2, 2 * rows, D))],
        hbm=list(parts) + [own],
        scratch=[pltpu.VMEM((4, rows, 2 * D), BF)],
        copies=4,
        micros=2,
    )[0]


def spread(place, own):
    from_x = place.swap_xy(own, 1)
    from_y = place.swap_xy(own, 2)
    far_one = place.swap_xy(from_y[1], 1)
    far_zero = place.swap_xy(from_x[0], 2)
    return [own, from_x, from_y, far_zero, far_one]


def piece_views(refs, which, xy):
    own, from_x, from_y, far_zero, far_one = refs
    return [
        (own.at[which], xy),
        (from_x.at[which], xy ^ 1),
        (from_y.at[which], xy ^ 2),
        ((far_zero, far_one)[which], xy ^ 3),
    ]


def load_wide(copies, refs, which, xy, target, columns=None):
    if len(refs) != 5:
        copies.start(refs[which], target)
        return
    for view, chip in piece_views(refs, which, xy):
        rows = view.shape[0]
        if columns is not None:
            view = view.at[:, pl.ds(0, columns)]
        copies.start(view, target.at[pl.ds(pl.multiple_of(chip * rows, 16), rows)])


def load_out(copies, refs, xy, target):
    if len(refs) != 5:
        copies.start(refs[2], target)
        return
    for view, chip in piece_views(refs, 1, xy):
        rows = view.shape[0] // 4
        for q in range(2):
            for hi in range(2):
                copies.start(
                    view.at[pl.ds((2 * q + hi) * rows, rows), pl.ds(HALF, HALF)],
                    target.at[q, pl.ds(pl.multiple_of(hi * QUARTER + chip * rows, 16), rows)],
                )


def load_units(copies, refs, which, xy, target):
    if len(refs) != 5:
        copies.start(refs[which], target)
        return
    for view, chip in piece_views(refs, which, xy):
        rows = view.shape[1]
        for hi in range(2):
            copies.start(
                view.at[hi], target.at[hi, pl.ds(pl.multiple_of(chip * rows, 16), rows)]
            )


ATTENTION_COPIES = 4 + 4 + 16
UNIT_COPIES = 16


def gather_plain(place, shard):
    whole = lax.all_gather(shard, ("mp", "dp"), axis=0)
    whole = whole.reshape((2, 2, place.dp) + shard.shape)
    return lax.dynamic_index_in_dim(whole, place.core, 0, keepdims=False)


def attention_plain(place, shard):
    mine = gather_plain(place, shard)
    rows = shard.shape[0]

    def columns(at, count):
        value = mine[..., at : at + count * QUARTER].reshape(2, D, count, QUARTER)
        return value.transpose(1, 2, 0, 3).reshape(D, count * HALF)

    out = mine[..., 3 * QUARTER :].reshape(2, place.dp, 2, 2, rows // 4, QUARTER)
    out = out.transpose(2, 0, 1, 4, 3, 5).reshape(2, HALF, HALF)
    return [columns(0, 2), columns(HALF, 1), out]


def units_plain(place, shard):
    mine = gather_plain(place, shard)
    return [mine[..., :D].reshape(2, D, D), mine[..., D:].reshape(2, D, D)]


def head_rows(h):
    return pl.ds(pl.multiple_of(h * HEAD_DIM, HEAD_DIM), HEAD_DIM)


def project(left, pair_ref):
    return jnp.concatenate([mm(left, pair_ref[0]), mm(left, pair_ref[1])], axis=1)


def project_t(left, pair_ref):
    return mm_t(left[:, :HALF], pair_ref[0]) + mm_t(left[:, HALF:], pair_ref[1])


def self_forward(hidden, norms, nums, weights):
    length = hidden.shape[0]

    def body(hidden_ref, norms_ref, nums_ref, *refs):
        w_refs, refs = refs[: len(weights)], refs[len(weights) :]
        part_ref, at_ref, qkv_ref, qt_ref, kt_ref, ot_ref, lse_ref = refs[:7]
        w_qk, w_v, w_out, vt, heads, bias, sems = refs[7:]
        _, xy, _ = where_am_i()
        copies = Copies(sems)
        load_wide(copies, w_refs, 0, xy, w_qk)
        load_wide(copies, w_refs, 1, xy, w_v, HALF)
        load_out(copies, w_refs, xy, w_out)
        unit, _ = norm(hidden_ref[...].astype(F32))
        a = (unit * norms_ref[0:1] + norms_ref[4:5]).astype(BF)
        at_ref[...] = a.T
        keys = lax.broadcasted_iota(jnp.int32, (length, length), 0)
        queries = lax.broadcasted_iota(jnp.int32, (length, length), 1)
        allowed = (keys <= queries) & (keys.astype(F32) < nums_ref[0:1, 0:1])
        bias[...] = jnp.where(allowed, 0.0, -1e30)
        copies.wait()
        qk = mm(a, w_qk[...])
        q = (qk[:, :HALF].astype(BF).astype(F32) * HEAD_DIM ** (-0.5)).astype(BF)
        k = qk[:, HALF:].astype(BF)
        v = mm(a, w_v[...]).astype(BF)
        qkv_ref[:, 0:HALF] = q
        qkv_ref[:, HALF : 2 * HALF] = k
        qkv_ref[:, 2 * HALF :] = v
        qt_ref[...] = q.T
        kt_ref[...] = k.T
        vt[...] = v.T
        for h in range(HEADS):
            heads[h] = k[:, h * HEAD_DIM : (h + 1) * HEAD_DIM]

        def head(h, carry):
            s = mm(heads[h], qt_ref[head_rows(h), :]) + bias[...]
            top = jnp.max(s, axis=0, keepdims=True)
            p = jnp.exp(s - top)
            total = jnp.sum(p, axis=0, keepdims=True)
            o = mm(vt[head_rows(h), :], p.astype(BF))
            ot_ref[head_rows(h), :] = (o / total).astype(BF)
            lse_ref[h] = top + jnp.log(total)
            return carry

        lax.fori_loop(0, HEADS, head, 0)
        part_ref[...] = project(ot_ref[...].T, w_out).astype(BF)

    return run(
        body,
        [
            shaped((length, D)),
            shaped((D, length)),
            shaped((length, 3 * HALF)),
            shaped((HALF, length)),
            shaped((HALF, length)),
            shaped((HALF, length)),
            shaped((HEADS, 1, length), F32),
        ],
        vmem=[hidden, norms, nums],
        hbm=weights,
        scratch=[
            pltpu.VMEM((D, D), BF),
            pltpu.VMEM((D, HALF), BF),
            pltpu.VMEM((2, HALF, HALF), BF),
            pltpu.VMEM((HALF, length), BF),
            pltpu.VMEM((HEADS, length, HEAD_DIM), BF),
            pltpu.VMEM((length, length), F32),
        ],
        copies=ATTENTION_COPIES,
        micros=10,
    )


def cross_memory(encoded, weights):
    frames = encoded.shape[0]

    def body(enc_ref, *refs):
        w_refs, refs = refs[: len(weights)], refs[len(weights) :]
        kv_ref, kvt_ref, et_ref, w_kv, sems = refs
        _, xy, _ = where_am_i()
        copies = Copies(sems)
        load_wide(copies, w_refs, 0, xy, w_kv)
        copies.wait()

        def step(i, carry):
            here = pl.ds(pl.multiple_of(i * CHUNK, CHUNK), CHUNK)
            rows = enc_ref[here, :]
            kv = mm(rows, w_kv[...]).astype(BF)
            kv_ref[here, :] = kv
            kvt_ref[:, here] = kv.T
            et_ref[:, here] = rows.T
            return carry

        lax.fori_loop(0, frames // CHUNK, step, 0)

    return run(
        body,
        [shaped((frames, D)), shaped((D, frames)), shaped((D, frames))],
        vmem=[encoded],
        hbm=weights,
        scratch=[pltpu.VMEM((D, D), BF)],
        copies=4,
        micros=9,
    )


def residual(hidden_ref, mine_ref, other_ref):
    return hidden_ref[...].astype(F32) + (mine_ref[...].astype(F32) + other_ref[...].astype(F32))


def cross_forward(hidden, mine, other, norms, nums, kv, kvt, weights):
    length = hidden.shape[0]
    frames = kv.shape[0]

    def body(hidden_ref, mine_ref, other_ref, norms_ref, nums_ref, kv_ref, kvt_ref, *refs):
        w_refs, refs = refs[: len(weights)], refs[len(weights) :]
        part_ref, h_ref, ct_ref, q_ref, qt_ref, ot_ref, lse_ref = refs[:7]
        w_q, w_out, heads, scores, sems = refs[7:]
        _, xy, _ = where_am_i()
        copies = Copies(sems)
        load_wide(copies, w_refs, 1, xy, w_q, HALF)
        load_out(copies, w_refs, xy, w_out)
        h1 = residual(hidden_ref, mine_ref, other_ref)
        h_ref[...] = h1
        unit, _ = norm(h1)
        c = (unit * norms_ref[1:2] + norms_ref[5:6]).astype(BF)
        ct_ref[...] = c.T
        for h in range(HEADS):
            heads[h] = kv_ref[:, h * HEAD_DIM : (h + 1) * HEAD_DIM]
        copies.wait()
        q = mm(c, w_q[...]).astype(BF)
        q = (q.astype(F32) * HEAD_DIM ** (-0.5)).astype(BF)
        q_ref[...] = q
        qt_ref[...] = q.T
        heard = nums_ref[1:2, 0:1]

        def head(h, carry):
            qt = qt_ref[head_rows(h), :]
            top = None
            for at in range(0, frames, CHUNK):
                s = mm(heads[h, at : at + CHUNK], qt)
                place = lax.broadcasted_iota(jnp.int32, s.shape, 0) + at
                s = jnp.where(place.astype(F32) < heard, s, -1e30)
                scores[at : at + CHUNK] = s
                high = jnp.max(s, axis=0, keepdims=True)
                top = high if top is None else jnp.maximum(top, high)
            total, o = 0.0, 0.0
            values = pl.ds(pl.multiple_of(HALF + h * HEAD_DIM, HEAD_DIM), HEAD_DIM)
            for at in range(0, frames, CHUNK):
                p = jnp.exp(scores[at : at + CHUNK] - top)
                total = total + jnp.sum(p, axis=0, keepdims=True)
                o = o + mm(kvt_ref[values, at : at + CHUNK], p.astype(BF))
            ot_ref[head_rows(h), :] = (o / total).astype(BF)
            lse_ref[h] = top + jnp.log(total)
            return carry

        lax.fori_loop(0, HEADS, head, 0)
        part_ref[...] = project(ot_ref[...].T, w_out).astype(BF)

    return run(
        body,
        [
            shaped((length, D)),
            shaped((length, D), F32),
            shaped((D, length)),
            shaped((length, HALF)),
            shaped((HALF, length)),
            shaped((HALF, length)),
            shaped((HEADS, 1, length), F32),
        ],
        vmem=[hidden, mine, other, norms, nums, kv, kvt],
        hbm=weights,
        scratch=[
            pltpu.VMEM((D, HALF), BF),
            pltpu.VMEM((2, HALF, HALF), BF),
            pltpu.VMEM((HEADS, frames, HEAD_DIM), BF),
            pltpu.VMEM((frames, length), F32),
        ],
        copies=4 + 16,
        micros=16,
    )


def units_forward(hidden, mine, other, norms, weights):
    length = hidden.shape[0]

    def body(hidden_ref, mine_ref, other_ref, norms_ref, *refs):
        w_refs, refs = refs[: len(weights)], refs[len(weights) :]
        part_ref, h_ref, mt_ref, slope_ref, it_ref = refs[:5]
        w_up, w_down, inner, sems = refs[5:]
        _, xy, _ = where_am_i()
        copies = Copies(sems)
        load_units(copies, w_refs, 0, xy, w_up)
        load_units(copies, w_refs, 1, xy, w_down)
        h2 = residual(hidden_ref, mine_ref, other_ref)
        h_ref[...] = h2
        unit, _ = norm(h2)
        m = (unit * norms_ref[2:3] + norms_ref[6:7]).astype(BF)
        mt_ref[...] = m.T
        copies.wait()
        for hi in range(2):
            for at in range(0, D, CHUNK):
                here = slice(hi * D + at, hi * D + at + CHUNK)
                z = mm(m, w_up[hi, :, at : at + CHUNK])
                share = 0.5 * (1.0 + lax.erf(z * 0.7071067811865476))
                slope = share + z * (0.3989422804014327 * jnp.exp(-0.5 * z * z))
                value = (z * share).astype(BF)
                inner[:, here] = value
                it_ref[here, :] = value.T
                slope_ref[:, here] = slope.astype(BF)
        for at in range(0, D, CHUNK):
            out = mm(inner[:, :D], w_down[0, :, at : at + CHUNK])
            out = out + mm(inner[:, D:], w_down[1, :, at : at + CHUNK])
            part_ref[:, at : at + CHUNK] = out.astype(BF)

    return run(
        body,
        [
            shaped((length, D)),
            shaped((length, D), F32),
            shaped((D, length)),
            shaped((length, 2 * D)),
            shaped((2 * D, length)),
        ],
        vmem=[hidden, mine, other, norms],
        hbm=weights,
        scratch=[
            pltpu.VMEM((2, D, D), BF),
            pltpu.VMEM((2, D, D), BF),
            pltpu.VMEM((length, 2 * D), BF),
        ],
        copies=2 * UNIT_COPIES,
        micros=9,
    )


def store_blocks(value, blocks, first_ref, second_ref):
    core, _, z = where_am_i()
    for b in range(4):
        blocks[b] = value[:, b * QUARTER : (b + 1) * QUARTER]
    first_ref[...] = blocks[2 * core + z % 2].T
    second_ref[...] = blocks[2 * core + (z + 1) % 2].T


def units_backward(hidden, mine, other, norms, nums, cot, slope, weights):
    length = hidden.shape[0]

    def body(hidden_ref, mine_ref, other_ref, norms_ref, nums_ref, cot_ref, slope_ref, *refs):
        w_refs, refs = refs[: len(weights)], refs[len(weights) :]
        part_ref, d_ref, e_ref, dz_ref, terms_ref, first_ref, second_ref = refs[:7]
        w_up, w_down, blocks, sems = refs[7:]
        _, xy, _ = where_am_i()
        copies = Copies(sems)
        load_units(copies, w_refs, 1, xy, w_down)
        load_units(copies, w_refs, 0, xy, w_up)
        unit, inverse = norm(residual(hidden_ref, mine_ref, other_ref))
        final = (unit * norms_ref[3:4] + norms_ref[7:8]).astype(BF)
        store_blocks(final, blocks, first_ref, second_ref)
        live = lax.broadcasted_iota(jnp.int32, (length, 1), 0).astype(F32) < nums_ref[0:1, 0:1]
        grad = cot_ref[...].astype(F32) * jnp.where(live, nums_ref[2:3, 0:1], 0.0)
        d3, terms = norm_back(grad, unit, inverse, norms_ref[3:4])
        d_ref[...] = d3
        terms_ref[...] = terms
        e = d3.astype(BF)
        e_ref[...] = e
        copies.wait()
        for hi in range(2):
            for at in range(0, D, CHUNK):
                here = slice(hi * D + at, hi * D + at + CHUNK)
                d_inner = mm_t(e, w_down[hi, at : at + CHUNK, :])
                dz_ref[:, here] = (slope_ref[:, here].astype(F32) * d_inner).astype(BF)
        for at in range(0, D, CHUNK):
            out = mm_t(dz_ref[:, :D], w_up[0, at : at + CHUNK, :])
            out = out + mm_t(dz_ref[:, D:], w_up[1, at : at + CHUNK, :])
            part_ref[:, at : at + CHUNK] = out.astype(BF)

    return run(
        body,
        [
            shaped((length, D)),
            shaped((length, D), F32),
            shaped((length, D)),
            shaped((length, 2 * D)),
            shaped((2, D), F32),
            shaped((QUARTER, length)),
            shaped((QUARTER, length)),
        ],
        vmem=[hidden, mine, other, norms, nums, cot, slope],
        hbm=weights,
        scratch=[
            pltpu.VMEM((2, D, D), BF),
            pltpu.VMEM((2, D, D), BF),
            pltpu.VMEM((4, length, QUARTER), BF),
        ],
        copies=2 * UNIT_COPIES,
        micros=10,
    )


def step_back(d_ref, hidden_ref, mine_ref, other_ref, gain):
    unit, inverse = norm(hidden_ref[...].astype(F32))
    grad = mine_ref[...].astype(F32) + other_ref[...].astype(F32)
    part, terms = norm_back(grad, unit, inverse, gain)
    return d_ref[...] + part, terms


def cross_backward(d, hidden, mine, other, norms, nums, kv, kvt, q, qt, ot, lse, weights):
    length = hidden.shape[0]
    frames = kv.shape[0]

    def body(
        d_ref, hidden_ref, mine_ref, other_ref, norms_ref, nums_ref, kv_ref, kvt_ref, q_ref,
        qt_ref, ot_ref, lse_ref, *refs
    ):
        w_refs, refs = refs[: len(weights)], refs[len(weights) :]
        part_ref, d_out_ref, e_ref, dq_ref, dkv_ref, terms_ref = refs[:6]
        w_q, w_out, keys, values, queries, grads, dot_t, dk_h, dv_h, dqt, sems = refs[6:]
        _, xy, _ = where_am_i()
        copies = Copies(sems)
        load_wide(copies, w_refs, 1, xy, w_q, HALF)
        load_out(copies, w_refs, xy, w_out)
        d2, terms = step_back(d_ref, hidden_ref, mine_ref, other_ref, norms_ref[2:3])
        d_out_ref[...] = d2
        terms_ref[...] = terms
        e = d2.astype(BF)
        e_ref[...] = e
        for h in range(HEADS):
            lanes = slice(h * HEAD_DIM, (h + 1) * HEAD_DIM)
            keys[h] = kv_ref[:, lanes]
            values[h] = kv_ref[:, HALF + h * HEAD_DIM : HALF + (h + 1) * HEAD_DIM]
            queries[h] = q_ref[:, lanes]
        copies.wait()
        d_mixed = project_t(e, w_out).astype(BF)
        dot_t[...] = d_mixed.T
        for h in range(HEADS):
            grads[h] = d_mixed[:, h * HEAD_DIM : (h + 1) * HEAD_DIM]
        heard = nums_ref[1:2, 0:1]

        def head(h, carry):
            rows = head_rows(h)
            q_t, do_t = qt_ref[rows, :], dot_t[rows, :]
            q_n, do_n = queries[h], grads[h]
            delta = jnp.sum(do_t.astype(F32) * ot_ref[rows, :].astype(F32), axis=0, keepdims=True)
            level = lse_ref[h]
            total = 0.0
            for at in range(0, frames, CHUNK):
                here = slice(at, at + CHUNK)
                s = mm(keys[h, here], q_t)
                place = lax.broadcasted_iota(jnp.int32, s.shape, 0) + at
                s = jnp.where(place.astype(F32) < heard, s, -1e30)
                p = jnp.exp(s - level)
                dp = mm(values[h, here], do_t)
                ds = (p * (dp - delta)).astype(BF)
                dv_h[h, here] = mm(p.astype(BF), do_n).astype(BF)
                dk_h[h, here] = mm(ds, q_n).astype(BF)
                total = total + mm(kvt_ref[rows, here], ds)
            dqt[rows, :] = (total * HEAD_DIM ** (-0.5)).astype(BF)
            return carry

        lax.fori_loop(0, HEADS, head, 0)
        dq = dqt[...].T
        dq_ref[...] = dq
        part_ref[...] = mm_t(dq, w_q[...]).astype(BF)
        for h in range(HEADS):
            lanes = slice(h * HEAD_DIM, (h + 1) * HEAD_DIM)
            dkv_ref[:, lanes] = dk_h[h]
            dkv_ref[:, HALF + h * HEAD_DIM : HALF + (h + 1) * HEAD_DIM] = dv_h[h]

    return run(
        body,
        [
            shaped((length, D)),
            shaped((length, D), F32),
            shaped((length, D)),
            shaped((length, HALF)),
            shaped((frames, D)),
            shaped((2, D), F32),
        ],
        vmem=[d, hidden, mine, other, norms, nums, kv, kvt, q, qt, ot, lse],
        hbm=weights,
        scratch=[
            pltpu.VMEM((D, HALF), BF),
            pltpu.VMEM((2, HALF, HALF), BF),
            pltpu.VMEM((HEADS, frames, HEAD_DIM), BF),
            pltpu.VMEM((HEADS, frames, HEAD_DIM), BF),
            pltpu.VMEM((HEADS, length, HEAD_DIM), BF),
            pltpu.VMEM((HEADS, length, HEAD_DIM), BF),
            pltpu.VMEM((HALF, length), BF),
            pltpu.VMEM((HEADS, frames, HEAD_DIM), BF),
            pltpu.VMEM((HEADS, frames, HEAD_DIM), BF),
            pltpu.VMEM((HALF, length), BF),
        ],
        copies=4 + 16,
        micros=24,
    )


def self_backward(d, hidden, mine, other, norms, nums, qkv, qt, kt, ot, lse, weights):
    length = hidden.shape[0]

    def body(
        d_ref, hidden_ref, mine_ref, other_ref, norms_ref, nums_ref, qkv_ref, qt_ref, kt_ref,
        ot_ref, lse_ref, *refs
    ):
        w_refs, refs = refs[: len(weights)], refs[len(weights) :]
        part_ref, d_out_ref, e_ref, dqkv_ref, terms_ref = refs[:5]
        w_qk, w_v, w_out, qkv_h, grads, dot_t, dk_h, dv_h, dqt, bias, sems = refs[5:]
        _, xy, _ = where_am_i()
        copies = Copies(sems)
        load_out(copies, w_refs, xy, w_out)
        load_wide(copies, w_refs, 0, xy, w_qk)
        load_wide(copies, w_refs, 1, xy, w_v, HALF)
        d1, terms = step_back(d_ref, hidden_ref, mine_ref, other_ref, norms_ref[1:2])
        d_out_ref[...] = d1
        terms_ref[...] = terms
        e = d1.astype(BF)
        e_ref[...] = e
        places = lax.broadcasted_iota(jnp.int32, (length, length), 0)
        queries = lax.broadcasted_iota(jnp.int32, (length, length), 1)
        allowed = (places <= queries) & (places.astype(F32) < nums_ref[0:1, 0:1])
        bias[...] = jnp.where(allowed, 0.0, -1e30)
        for j in range(3):
            for h in range(HEADS):
                lanes = slice(j * HALF + h * HEAD_DIM, j * HALF + (h + 1) * HEAD_DIM)
                qkv_h[j * HEADS + h] = qkv_ref[:, lanes]
        copies.wait()
        d_mixed = project_t(e, w_out).astype(BF)
        dot_t[...] = d_mixed.T
        for h in range(HEADS):
            grads[h] = d_mixed[:, h * HEAD_DIM : (h + 1) * HEAD_DIM]

        def head(h, carry):
            rows = head_rows(h)
            do_t, do_n = dot_t[rows, :], grads[h]
            delta = jnp.sum(do_t.astype(F32) * ot_ref[rows, :].astype(F32), axis=0, keepdims=True)
            s = mm(qkv_h[HEADS + h], qt_ref[rows, :]) + bias[...]
            p = jnp.exp(s - lse_ref[h])
            dp = mm(qkv_h[2 * HEADS + h], do_t)
            ds = (p * (dp - delta)).astype(BF)
            dv_h[h] = mm(p.astype(BF), do_n).astype(BF)
            dk_h[h] = mm(ds, qkv_h[h]).astype(BF)
            dqt[rows, :] = (mm(kt_ref[rows, :], ds) * HEAD_DIM ** (-0.5)).astype(BF)
            return carry

        lax.fori_loop(0, HEADS, head, 0)
        dqkv_ref[:, 0:HALF] = dqt[...].T
        for h in range(HEADS):
            lanes = slice(HALF + h * HEAD_DIM, HALF + (h + 1) * HEAD_DIM)
            dqkv_ref[:, lanes] = dk_h[h]
            lanes = slice(2 * HALF + h * HEAD_DIM, 2 * HALF + (h + 1) * HEAD_DIM)
            dqkv_ref[:, lanes] = dv_h[h]
        out = mm_t(dqkv_ref[:, 0 : 2 * HALF], w_qk[...])
        part_ref[...] = (out + mm_t(dqkv_ref[:, 2 * HALF :], w_v[...])).astype(BF)

    return run(
        body,
        [
            shaped((length, D)),
            shaped((length, D), F32),
            shaped((length, D)),
            shaped((length, 3 * HALF)),
            shaped((2, D), F32),
        ],
        vmem=[d, hidden, mine, other, norms, nums, qkv, qt, kt, ot, lse],
        hbm=weights,
        scratch=[
            pltpu.VMEM((D, D), BF),
            pltpu.VMEM((D, HALF), BF),
            pltpu.VMEM((2, HALF, HALF), BF),
            pltpu.VMEM((3 * HEADS, length, HEAD_DIM), BF),
            pltpu.VMEM((HEADS, length, HEAD_DIM), BF),
            pltpu.VMEM((HALF, length), BF),
            pltpu.VMEM((HEADS, length, HEAD_DIM), BF),
            pltpu.VMEM((HEADS, length, HEAD_DIM), BF),
            pltpu.VMEM((HALF, length), BF),
            pltpu.VMEM((length, length), F32),
        ],
        copies=ATTENTION_COPIES,
        micros=14,
    )


def finish_hidden(d, hidden, mine, other, norms, terms1, terms2, terms3):
    length = hidden.shape[0]

    def body(
        d_ref, hidden_ref, mine_ref, other_ref, norms_ref, one, two, three, terms_ref, first_ref,
        second_ref, blocks
    ):
        d0, terms = step_back(d_ref, hidden_ref, mine_ref, other_ref, norms_ref[0:1])
        store_blocks(d0.astype(BF), blocks, first_ref, second_ref)
        for j in range(2):
            here = slice(j, j + 1)
            terms_ref[4 * j : 4 * j + 4] = jnp.concatenate(
                [terms[here], one[here], two[here], three[here]], axis=0
            )

    return run(
        body,
        [shaped((8, D), F32), shaped((QUARTER, length)), shaped((QUARTER, length))],
        vmem=[d, hidden, mine, other, norms, terms1, terms2, terms3],
        scratch=[pltpu.VMEM((4, length, QUARTER), BF)],
        micros=4,
    )


def finish_encoder(keep, other):
    frames = keep.shape[1]

    def body(keep_ref, other_ref, first_ref, second_ref):
        _, _, z = where_am_i()
        for ref, k in ((first_ref, 0), (second_ref, 1)):
            here = pl.ds(pl.multiple_of(((z + k) % 2) * QUARTER, QUARTER), QUARTER)
            total = keep_ref[here, :].astype(F32) + other_ref[here, :].astype(F32)
            ref[...] = total.astype(BF)

    return run(
        body,
        [shaped((QUARTER, frames)), shaped((QUARTER, frames))],
        vmem=[keep, other],
        micros=2,
    )


def block_plan(place):
    if not place.fast:
        return 1, (((1, 0, 0),), ((1, 0, 0),))
    first = ((1, 0, 0), (0, 0, 1), (1, 1, 2), (0, 1, 3))
    second = ((1, 0, 0), (1, 1, 1), (0, 0, 2), (0, 1, 3))
    return 4, (first, second)


def grad_outputs(place, shape):
    if place.fast:
        return [shaped((2,) + shape)] * 4
    return [shaped((1,) + shape)] * 4


def units_grads(place, mt, dz, it, e):
    length = e.shape[0]
    count, plan = block_plan(place)
    rows = D // count

    def body(mt_ref, dz_ref, it_ref, e_ref, *outs):
        _, xy, _ = where_am_i()
        for output, slot, offset in plan[0]:
            chip = xy ^ offset if count > 1 else 0
            here = pl.ds(pl.multiple_of(chip * rows, 16), rows)
            for hi in range(2):
                outs[output][slot, hi] = mm(
                    mt_ref[here, :], dz_ref[:, hi * D : (hi + 1) * D]
                ).astype(BF)
        for output, slot, offset in plan[1]:
            chip = xy ^ offset if count > 1 else 0
            for hi in range(2):
                here = pl.ds(pl.multiple_of(hi * D + chip * rows, 16), rows)
                outs[2 + output][slot, hi] = mm(it_ref[here, :], e_ref[...]).astype(BF)

    return run(
        body,
        grad_outputs(place, (2, rows, D)),
        vmem=[mt, dz, it, e],
        micros=7,
    )


def attention_grads(place, wide_left, wide_right, left, right, ot, e):
    count, plan = block_plan(place)
    rows = D // count
    few = rows // 4

    def body(wide_left_ref, wide_right_ref, left_ref, right_ref, ot_ref, e_ref, *outs):
        _, xy, _ = where_am_i()
        for output, slot, offset in plan[0]:
            chip = xy ^ offset if count > 1 else 0
            here = pl.ds(pl.multiple_of(chip * rows, 16), rows)
            outs[output][slot] = mm(wide_left_ref[here, :], wide_right_ref[...]).astype(BF)
        for output, slot, offset in plan[1]:
            chip = xy ^ offset if count > 1 else 0
            here = pl.ds(pl.multiple_of(chip * rows, 16), rows)
            target = outs[2 + output]
            target[slot, :, 0:HALF] = mm(left_ref[here, :], right_ref[...]).astype(BF)
            for hi in range(2):
                here = pl.ds(pl.multiple_of(hi * QUARTER + chip * few, 16), few)
                both = mm(ot_ref[here, :], e_ref[...]).astype(BF)
                for q in range(2):
                    at = (2 * q + hi) * few
                    target[slot, at : at + few, HALF:D] = both[:, q * HALF : (q + 1) * HALF]

    return run(
        body,
        grad_outputs(place, (rows, D)),
        vmem=[wide_left, wide_right, left, right, ot, e],
        micros=6,
    )


def encoder_grad(dkv, weights, frames):
    padded = dkv.shape[0]

    def body(dkv_ref, *refs):
        w_refs, (keep_ref, send_ref, w_kv, sems) = refs[: len(weights)], refs[len(weights) :]
        core, xy, _ = where_am_i()
        copies = Copies(sems)
        load_wide(copies, w_refs, 0, xy, w_kv)
        copies.wait()
        mine = pl.ds(pl.multiple_of(core * HALF, HALF), HALF)
        theirs = pl.ds(pl.multiple_of((1 - core) * HALF, HALF), HALF)
        for ref, rows in ((send_ref, theirs), (keep_ref, mine)):
            for at in range(0, padded, CHUNK):
                size = min(CHUNK, frames - at)
                value = mm_t(w_kv[rows, :], dkv_ref[at : at + CHUNK, :]).astype(BF)
                ref[:, at : at + size] = value[:, :size]

    return run(
        body,
        [shaped((HALF, frames)), shaped((HALF, frames))],
        vmem=[dkv],
        hbm=weights,
        scratch=[pltpu.VMEM((D, D), BF)],
        copies=4,
        micros=4,
    )


def leave_plane(place, grads):
    return [place.swap_xy(grads[0], 1), place.swap_xy(grads[2], 2)]


def pass_on(grads, came, after):
    shape = grads[1].shape[1:]

    def body(stay0, came0, stay1, came1, *refs):
        out0, out1, held, sems = refs[-4:]
        copies = Copies(sems)
        for i, ref in enumerate((stay0, came0, stay1, came1)):
            copies.start(ref.at[1], held.at[i])
        copies.wait()
        out0[...] = add_up(held[0], held[1]).astype(BF)
        out1[...] = add_up(held[2], held[3]).astype(BF)

    return run(
        body,
        [shaped(shape), shaped(shape)],
        hbm=[grads[1], came[0], grads[3], came[1]] + list(after),
        scratch=[pltpu.VMEM((4,) + shape, BF)],
        copies=4,
        micros=1,
    )


def cross_plane(place, onward):
    return [place.swap_xy(onward[0], 2), place.swap_xy(onward[1], 1)]


def column_blocks(grads, came, onward, attention, norm_terms=(), after=()):
    shape = onward[0].shape
    rows = shape[-2] // 2
    width = D if attention else 2 * D
    few = rows // 4
    extra = 16 if norm_terms else 0

    def body(*refs):
        terms_refs, refs = refs[: len(norm_terms)], refs[len(norm_terms) :]
        ins, outs, (held, shards, sems) = refs[:6], refs[-7:-3], refs[-3:]
        home, slots = column_slots()
        copies = Copies(sems)
        for i, ref in enumerate(ins):
            copies.start(ref if i % 3 == 2 else ref.at[0], held.at[i])
        copies.wait()
        sums = [add_up(held[3 * part], held[3 * part + 1], held[3 * part + 2]) for part in range(2)]
        for hi in range(2):
            for cs in range(2):
                here = slice(cs * rows, (cs + 1) * rows)
                if attention:
                    lanes = slice(hi * QUARTER, (hi + 1) * QUARTER)
                    lanes_two = slice(HALF + hi * QUARTER, HALF + (hi + 1) * QUARTER)
                    outs_rows = []
                    for p in range(4):
                        at = (2 * (p // 2) + hi) * 2 * few + cs * few
                        side = HALF + (p % 2) * QUARTER
                        outs_rows.append(sums[1][at : at + few, side : side + QUARTER])
                    value = jnp.concatenate(
                        [
                            sums[0][here, lanes],
                            sums[0][here, lanes_two],
                            sums[1][here, lanes],
                            jnp.concatenate(outs_rows, axis=0),
                        ],
                        axis=1,
                    )
                else:
                    value = jnp.concatenate([sums[0][hi, here], sums[1][hi, here]], axis=1)
                shards[2 * hi + cs, :rows] = value.astype(BF)
        if norm_terms:
            core, xy, _ = where_am_i()
            terms = add_up(*[ref[...] for ref in terms_refs])
            terms = jnp.concatenate([terms, jnp.zeros_like(terms)], axis=0).astype(BF)
            feature = lax.broadcasted_iota(jnp.int32, (D, D), 0)
            lane = lax.broadcasted_iota(jnp.int32, (D, D), 1)
            for hi in range(2):
                for cs in range(2):
                    offset = (2 * core + hi) * QUARTER + (2 * xy + cs) * few
                    pick = jnp.where((feature == lane + offset) & (lane < few), 1.0, 0.0)
                    shards[2 * hi + cs, rows:] = mm(terms, pick.astype(BF)).astype(BF)
        for k in range(4):
            outs[k][...] = shards[slots[k]]

    ins = [grads[1], came[0], onward[0], grads[3], came[1], onward[1]]
    return run(
        body,
        [shaped((rows + extra, width))] * 4,
        vmem=list(norm_terms),
        hbm=ins + list(after),
        scratch=[pltpu.VMEM((6,) + shape, BF), pltpu.VMEM((4, rows + extra, width), BF)],
        copies=6,
        micros=4,
    )


def sum_plain(place, grads, attention):
    wide, narrow = grads[1][0], grads[3][0]
    rows = D // place.dp
    if attention:
        value = jnp.stack([wide[:, :HALF], wide[:, HALF:], narrow[:, :HALF]], axis=1)
        value = value.reshape(place.dp, rows, 3, 2, QUARTER).transpose(3, 0, 1, 2, 4)
        value = value.reshape(2, place.dp, rows, 3 * QUARTER)
        outs = narrow[:, HALF:].reshape(2, 2, place.dp, rows // 4, 2, QUARTER)
        outs = outs.transpose(1, 2, 0, 4, 3, 5).reshape(2, place.dp, rows, QUARTER)
        value = jnp.concatenate([value, outs], axis=-1)
    else:
        value = jnp.concatenate(
            [wide.reshape(2, place.dp, rows, D), narrow.reshape(2, place.dp, rows, D)], axis=-1
        )
    whole = jnp.zeros((2,) + value.shape, F32)
    whole = lax.dynamic_update_index_in_dim(whole, value.astype(F32), place.core, 0)
    whole = whole.reshape((4 * place.dp,) + value.shape[2:])
    return lax.psum_scatter(whole, ("mp", "dp"), scatter_dimension=0, tiled=False)


def from_quarters(value):
    few = value.shape[0] // 4
    return value.reshape(4, few, QUARTER).transpose(1, 0, 2).reshape(few, D)


def three_parts(value):
    terms = []
    for _ in range(3):
        term = lax.reduce_precision(value, 8, 7)
        terms.append(term.astype(BF))
        value = value - term
    return jnp.concatenate(terms)


def per_device(
    dp,
    mp,
    hidden_in,
    encoder_states,
    cotangent,
    self_qkv,
    self_out,
    cross_q,
    cross_kv,
    cross_out,
    fc_in,
    fc_out,
    ln_gain,
    ln_bias,
    token_lengths,
    audio_lengths,
    corpus_ids,
    corpus_weights,
):
    place = Place(dp, mp)
    length = hidden_in.shape[2]
    frames = encoder_states.shape[2]
    padded = -(-frames // CHUNK) * CHUNK
    rows = self_qkv.shape[0]

    units = jnp.concatenate([fc_in, fc_out], axis=1)
    if place.fast:
        own_self, own_cross = attention_shards(self_qkv, self_out, cross_q, cross_kv, cross_out)
        w_self = spread(place, pack_attention(place.column_out(own_self), own_self))
        w_cross = spread(place, pack_attention(place.column_out(own_cross), own_cross))
        w_units = spread(place, pack_units(place.column_out(units), units))
    else:
        quarter = lambda w: w.reshape(-1, 4, QUARTER).transpose(1, 0, 2).reshape(-1, QUARTER)
        flat = lambda w: w.reshape(rows, -1)
        w_self = attention_plain(
            place, jnp.concatenate([flat(self_qkv), quarter(self_out)], axis=1)
        )
        w_cross = attention_plain(
            place, jnp.concatenate([flat(cross_kv), cross_q, quarter(cross_out)], axis=1)
        )
        w_units = units_plain(place, units)

    turned = lambda value: value[:, 0].transpose(0, 2, 1)
    numbers = jnp.concatenate([token_lengths.T, audio_lengths.T, corpus_ids.T])
    blocks = input_blocks(
        turned(hidden_in),
        turned(cotangent),
        three_parts(jnp.concatenate([ln_gain, ln_bias])),
        numbers,
    )
    got = place.rows_in(blocks)
    hidden, cot, norms, nums = prepare(got, place.swap_core(got), corpus_weights)

    encoded = lax.dynamic_index_in_dim(encoder_states[:, 0], place.micro, 0, keepdims=False)
    other = place.move(encoded, lambda xy, core, z: (xy, 1 - core, z) if core == z // 2 else None)
    encoded = jnp.where(place.home == place.core, encoded, other)
    encoded = jnp.pad(encoded, ((0, padded - frames), (0, 0)))

    part1, at, qkv, qt, kt, ot1, lse1 = self_forward(hidden, norms, nums, w_self)
    other1 = place.swap_core(part1)
    kv, kvt, et = cross_memory(encoded, w_cross)
    part2, h1, ct, q2, qt2, ot2, lse2 = cross_forward(
        hidden, part1, other1, norms, nums, kv, kvt, w_cross
    )
    other2 = place.swap_core(part2)
    part3, h2, mt, slope, it = units_forward(h1, part2, other2, norms, w_units)
    other3 = place.swap_core(part3)
    part, d3, e3, dz, terms3, out_a, out_b = units_backward(
        h2, part3, other3, norms, nums, cot, slope, w_units
    )
    other = place.swap_core(part)
    g_units = units_grads(place, mt, dz, it, e3)
    if place.fast:
        came_units = leave_plane(place, g_units)
    layer_out = place.rows_home((out_a, out_b))
    part, d2, e2, dq2, dkv, terms2 = cross_backward(
        d3, h2, part, other, norms, nums, kv, kvt, q2, qt2, ot2, lse2, w_cross
    )
    other = place.swap_core(part)
    g_cross = attention_grads(place, et, dkv, ct, dq2, ot2, e2)
    if place.fast:
        came_cross = leave_plane(place, g_cross)
    keep, send = encoder_grad(dkv, w_cross, frames)
    if place.fast:
        onward_units = cross_plane(place, pass_on(g_units, came_units, [keep]))
    part, d1, e1, dqkv, terms1 = self_backward(
        d2, h1, part, other, norms, nums, qkv, qt, kt, ot1, lse1, w_self
    )
    other = place.swap_core(part)
    g_self = attention_grads(
        place, at, dqkv[:, : 2 * HALF], at, dqkv[:, 2 * HALF :], ot1, e1
    )
    if place.fast:
        came_self = leave_plane(place, g_self)
    terms, out_a, out_b = finish_hidden(d1, hidden, part, other, norms, terms1, terms2, terms3)
    grad_hidden = place.rows_home((out_a, out_b)).astype(F32)
    grad_encoder = place.rows_home(finish_encoder(keep, place.swap_core(send))).astype(F32)

    few = D // (place.dp * place.mp)
    if place.fast:
        onward_cross = cross_plane(place, pass_on(g_cross, came_cross, [g_self[0]]))
        s_units = place.column_back(column_blocks(g_units, came_units, onward_units, False, (), [g_self[0]]))
        terms = terms + place.swap_xy(terms, 1)
        s_cross = place.column_back(column_blocks(g_cross, came_cross, onward_cross, True, (), [terms]))
        onward_self = cross_plane(place, pass_on(g_self, came_self, []))
        s_self = place.column_back(
            column_blocks(
                g_self, came_self, onward_self, True, (terms, place.swap_xy(terms, 2))
            )
        )
        shares = s_self[rows : rows + 8, :few]
    else:
        s_units = sum_plain(place, g_units, False)
        s_cross = sum_plain(place, g_cross, True)
        s_self = sum_plain(place, g_self, True)
        terms = jnp.where(place.core == 0, terms, 0.0)
        terms = lax.psum(terms, ("dp", "mp"))
        shares = lax.dynamic_slice_in_dim(terms, (place.z * place.dp + place.d) * few, few, 1)
    s_self = s_self[:rows]
    return (
        layer_out,
        grad_hidden,
        grad_encoder,
        s_self[:, : 3 * QUARTER].reshape(rows, 3, QUARTER),
        from_quarters(s_self[:, 3 * QUARTER :]),
        s_cross[:, 2 * QUARTER : 3 * QUARTER],
        s_cross[:, : 2 * QUARTER].reshape(rows, 2, QUARTER),
        from_quarters(s_cross[:, 3 * QUARTER :]),
        s_units[:, :D],
        s_units[:, D:],
        shares[:4],
        shares[4:],
    )


def solution(mesh):
    rows = P(None, "dp", None, "mp")
    columns = P("dp", None, "mp")
    pairs = P("dp", "mp")
    units = P(("mp", "dp"), None)
    each = P(None, "dp")
    return jax.shard_map(
        partial(per_device, mesh.shape["dp"], mesh.shape["mp"]),
        mesh=mesh,
        in_specs=(
            rows,
            P(None, "dp", None, None),
            rows,
            columns,
            units,
            pairs,
            columns,
            units,
            pairs,
            units,
            P(None, "mp"),
            P(None, "mp"),
            each,
            each,
            each,
            P(),
        ),
        out_specs=(
            rows,
            rows,
            rows,
            columns,
            units,
            pairs,
            columns,
            units,
            pairs,
            units,
            P(None, ("mp", "dp")),
            P(None, ("mp", "dp")),
        ),
        check_vma=False,
    )
```

```python
from functools import partial

import jax
import jax.numpy as jnp
from jax import lax
from jax.experimental import pallas as pl
from jax.experimental.pallas import tpu as pltpu
from jax.sharding import Mesh, PartitionSpec as P

D = 768
HALF = 384
QUARTER = 192
HEAD_DIM = 64
HEADS = 6
CHUNK = 256
BF = jnp.bfloat16
F32 = jnp.float32
AXES = ("xy", "core", "mp")
CHIPS = ("xy", "mp")
VMEM = pl.BlockSpec(memory_space=pltpu.VMEM)
SMEM = pl.BlockSpec(memory_space=pltpu.SMEM)
ANY = pl.BlockSpec(memory_space=pl.ANY)


def mm(left, right):
    return jnp.dot(left, right, preferred_element_type=F32)


def mm_t(left, right):
    return lax.dot_general(left, right, (((1,), (1,)), ((), ())), preferred_element_type=F32)


def shaped(shape, dtype=BF):
    return jax.ShapeDtypeStruct(shape, dtype)


def run(body, outs, vmem=(), hbm=(), smem=(), scratch=(), copies=0, micros=2, out_specs=None):
    args = tuple(smem) + tuple(vmem) + tuple(hbm)
    scratch = list(scratch)
    if copies:
        scratch.append(pltpu.SemaphoreType.DMA((copies,)))
    moved = sum(a.size * a.dtype.itemsize for a in args) + sum(
        o.size * o.dtype.itemsize for o in outs
    )
    return pl.pallas_call(
        body,
        out_shape=tuple(outs),
        in_specs=[SMEM] * len(smem) + [VMEM] * len(vmem) + [ANY] * len(hbm),
        out_specs=tuple(out_specs or [VMEM] * len(outs)),
        scratch_shapes=scratch,
        compiler_params=pltpu.CompilerParams(vmem_limit_bytes=56 * 1024 * 1024),
        cost_estimate=pl.CostEstimate(
            flops=int(micros * 1.15e9), bytes_accessed=moved, transcendentals=0
        ),
    )(*args)


class Copies:
    def __init__(self, sems):
        self.sems, self.open = sems, []

    def start(self, source, target):
        copy = pltpu.make_async_copy(source, target, self.sems.at[len(self.open)])
        copy.start()
        self.open.append(copy)

    def wait(self):
        for copy in self.open:
            copy.wait()


def where_am_i():
    return lax.axis_index("core"), lax.axis_index("xy"), lax.axis_index("mp")


class Place:
    def __init__(self, dp, mp):
        self.dp, self.mp = dp, mp
        self.chips = dp // 2
        self.fast = self.chips == 4
        self.z = lax.axis_index("mp")
        self.core = lax.axis_index("core")
        self.xy = lax.axis_index("xy")
        self.d = 2 * self.xy + self.core
        self.micro = self.z % 2
        self.home = self.z // 2

    def move(self, value, route):
        pairs = []
        for xy in range(self.chips):
            for core in range(2):
                for z in range(self.mp):
                    target = route(xy, core, z)
                    if target is not None:
                        txy, tcore, tz = target
                        pairs.append(
                            ((2 * xy + core) * self.mp + z, (2 * txy + tcore) * self.mp + tz)
                        )
        return lax.ppermute(value, AXES, pairs)

    def swap_core(self, value):
        return self.move(value, lambda xy, core, z: (xy, 1 - core, z))

    def swap_xy(self, value, bit):
        return self.move(value, lambda xy, core, z: (xy ^ bit, core, z))

    def swap_z(self, value, bit):
        return self.move(value, lambda xy, core, z: (xy, core, z ^ bit))

    def column_routes(self):
        def route(step, xy, core, z):
            user, j = z // 2, z % 2
            home = core == user
            near = lambda i: (xy, user, 2 * user + i)
            far = lambda i: (xy, user, 2 * (1 - user) + i)
            if step == 0:
                return near(1 - j) if home else far(1 - j)
            if step == 1:
                return far(j) if home else near(j)
            if step == 2:
                return far(1 - j) if home else near(1 - j)
            return None if home else far(j)

        return [partial(route, step) for step in range(4)]

    def column_out(self, shard):
        return [self.move(shard, route) for route in self.column_routes()]

    def column_back(self, blocks):
        got = []
        for block, route in zip(blocks, self.column_routes()):
            turned = {}
            for xy in range(self.chips):
                for core in range(2):
                    for z in range(self.mp):
                        target = route(xy, core, z)
                        if target is not None:
                            turned[target] = (xy, core, z)
            got.append(self.move(block, lambda xy, core, z: turned.get((xy, core, z))))
        at_home = self.core == self.home
        return add_up(got[0], got[1], got[2], jnp.where(at_home, blocks[3], got[3]))

    def rows_in(self, blocks):
        def route(k, xy, core, z):
            target = (xy, z // 2, 2 * core + (z + k) % 2)
            return None if target == (xy, core, z) else target

        got = [self.move(block, partial(route, k)) for k, block in enumerate(blocks)]
        return jnp.stack([jnp.where(self.core == self.home, blocks[0], got[0]), got[1]])

    def rows_home(self, blocks):
        def route(k, xy, core, z):
            target = (xy, z // 2, 2 * core + (z % 2 - k) % 2)
            return None if target == (xy, core, z) else target

        got = [self.move(block, partial(route, k)) for k, block in enumerate(blocks)]
        got[0] = jnp.where(self.core == self.home, blocks[0], got[0])
        even = self.z % 2 == 0
        both = jnp.stack([jnp.where(even, got[0], got[1]), jnp.where(even, got[1], got[0])])
        return both[:, None].transpose(0, 1, 3, 2)


def norm(hidden):
    center = jnp.mean(hidden, axis=-1, keepdims=True)
    spread = jnp.mean(hidden * hidden, axis=-1, keepdims=True) - center * center
    inverse = lax.rsqrt(spread + 1e-05)
    return (hidden - center) * inverse, inverse


def norm_back(grad, unit, inverse, gain):
    scaled = grad * gain
    first = jnp.mean(scaled, axis=-1, keepdims=True)
    second = jnp.mean(scaled * unit, axis=-1, keepdims=True)
    terms = jnp.concatenate(
        [jnp.sum(grad * unit, axis=0, keepdims=True), jnp.sum(grad, axis=0, keepdims=True)], axis=0
    )
    return inverse * (scaled - first - unit * second), terms


def add_up(*terms):
    total = terms[0].astype(F32)
    for term in terms[1:]:
        total = total + term.astype(F32)
    return total


def input_blocks(hidden, cotangent, terms, numbers):
    _, width, length = hidden.shape
    total = 2 * width + 32

    def body(numbers_ref, hidden_ref, cot_ref, terms_ref, *outs):
        _, _, z = where_am_i()
        lanes = lax.broadcasted_iota(jnp.int32, (8, length), 1)
        for k in range(2):
            micro = (z + k) % 2
            outs[k][0:width] = hidden_ref[micro]
            outs[k][width : 2 * width] = cot_ref[micro]
            tok, aud = numbers_ref[0, micro], numbers_ref[1, micro]
            row = jnp.where(lanes == 0, tok // 256, jnp.where(lanes == 1, tok % 256, 0))
            row = jnp.where(lanes == 2, aud // 256, jnp.where(lanes == 3, aud % 256, row))
            row = jnp.where(lanes == 4, numbers_ref[2, micro], row)
            wide = jnp.concatenate(
                [terms_ref[...].astype(F32), jnp.zeros((24, length - width), F32)], axis=1
            )
            outs[k][2 * width : total] = jnp.concatenate([wide, row.astype(F32)], axis=0).astype(BF)

    return run(
        body,
        [shaped((total, length))] * 2,
        smem=[numbers],
        vmem=[hidden, cotangent, terms],
        micros=1,
    )


def prepare(own, other, corpus_weights):
    length = own.shape[2]

    def body(
        weights_ref, own_ref, other_ref, hidden_ref, cot_ref, norms_ref, nums_ref, wide, extra, sems
    ):
        core, _, z = where_am_i()
        copies = Copies(sems)
        for k in range(2):
            slot = (z % 2 + k) % 2
            for ref, user in ((own_ref, core), (other_ref, 1 - core)):
                block = 2 * user + slot
                here = pl.ds(pl.multiple_of(block * QUARTER, QUARTER), QUARTER)
                for which in range(2):
                    copies.start(ref.at[k, pl.ds(which * QUARTER, QUARTER)], wide.at[which, here])
                copies.start(ref.at[k, pl.ds(2 * QUARTER, 32)], extra.at[block])
        copies.wait()
        hidden_ref[...] = wide[0].T
        cot_ref[...] = wide[1].T
        parts = [extra[b].astype(F32) for b in range(4)]
        norms_ref[...] = jnp.concatenate(
            [(e[0:8] + e[8:16] + e[16:24])[:, :QUARTER] for e in parts], axis=1
        )
        row = parts[0][24:25]
        tok = 256.0 * row[:, 0:1] + row[:, 1:2]
        aud = 256.0 * row[:, 2:3] + row[:, 3:4]
        weights = weights_ref[...]
        places = lax.broadcasted_iota(jnp.int32, weights.shape, 1).astype(F32)
        weight = jnp.sum(jnp.where(places == row[:, 4:5], weights, 0.0), axis=1, keepdims=True)
        index = lax.broadcasted_iota(jnp.int32, (8, 128), 0)
        nums_ref[...] = jnp.where(index == 0, tok, jnp.where(index == 1, aud, weight))

    return run(
        body,
        [
            shaped((length, D)),
            shaped((length, D)),
            shaped((8, D), F32),
            shaped((8, 128), F32),
        ],
        vmem=[corpus_weights.reshape(1, -1)],
        hbm=[own, other],
        scratch=[pltpu.VMEM((2, D, length), BF), pltpu.VMEM((4, 32, length), BF)],
        copies=12,
        micros=3,
    )


def quarters(value):
    return jnp.concatenate([value[:, p * QUARTER : (p + 1) * QUARTER] for p in range(4)], axis=0)


def attention_shards(self_qkv, self_out, cross_q, cross_kv, cross_out):
    rows = cross_q.shape[0]

    def body(qkv_ref, out_ref, q_ref, kv_ref, cout_ref, self_ref, cross_ref):
        out = quarters(out_ref[...].astype(F32)).astype(BF)
        self_ref[...] = jnp.concatenate([qkv_ref[0], qkv_ref[1], qkv_ref[2], out], axis=1)
        out = quarters(cout_ref[...].astype(F32)).astype(BF)
        cross_ref[...] = jnp.concatenate([kv_ref[...], q_ref[...], out], axis=1)

    return run(
        body,
        [shaped((rows, D)), shaped((rows, D))],
        vmem=[self_qkv.transpose(1, 0, 2), self_out, cross_q, cross_kv.reshape(rows, -1), cross_out],
        micros=1,
    )


def column_slots():
    core, _, z = where_am_i()
    j = z % 2
    home = 1 - jnp.abs(z // 2 - core)
    same = core + (1 - 2 * core) * (1 - home)
    return home == 1, (2 * (1 - j) + same, 2 * j + 1 - same, 2 * (1 - j) + 1 - same, 2 * j + same)


def bring_column(part_refs, own_ref, shards, sems):
    home, slots = column_slots()
    copies = Copies(sems)
    for k in range(3):
        copies.start(part_refs[k], shards.at[slots[k]])

    @pl.when(home)
    def _():
        copy = pltpu.make_async_copy(own_ref, shards.at[slots[3]], sems.at[3])
        copy.start()
        copy.wait()

    @pl.when(jnp.logical_not(home))
    def _():
        copy = pltpu.make_async_copy(part_refs[3], shards.at[slots[3]], sems.at[3])
        copy.start()
        copy.wait()

    copies.wait()


def pack_attention(parts, own):
    rows = own.shape[0]
    few = rows // 4

    def body(*refs):
        part_refs, own_ref, (out_ref, shards, sems) = refs[:4], refs[4], refs[5:]
        bring_column(part_refs, own_ref, shards, sems)
        for cs in range(2):
            low, high = shards[cs], shards[2 + cs]

            def both(at):
                return [low[:, at : at + QUARTER], high[:, at : at + QUARTER]]

            here = pl.ds(cs * rows, rows)
            out_ref[0, here, :] = jnp.concatenate(both(0) + both(QUARTER), axis=1)
            out_ref[1, here, 0:HALF] = jnp.concatenate(both(HALF), axis=1)
        outs = [shards[i, :, 3 * QUARTER :].astype(F32) for i in range(4)]
        stack = []
        for q in range(2):
            for i in range(4):
                left = outs[i][2 * q * few : (2 * q + 1) * few]
                right = outs[i][(2 * q + 1) * few : (2 * q + 2) * few]
                stack.append(jnp.concatenate([left, right], axis=1))
        out_ref[1, :, HALF:D] = jnp.concatenate(stack, axis=0).astype(BF)

    return run(
        body,
        [shaped((2, 2 * rows, D))],
        hbm=list(parts) + [own],
        scratch=[pltpu.VMEM((4, rows, D), BF)],
        copies=4,
        micros=2.5,
    )[0]


def unit_shard(place, fc_in, fc_out):
    rows = fc_in.shape[0]
    both = fc_in.reshape(rows, place.chips, 2, rows).transpose(2, 0, 1, 3).reshape(2, rows, HALF)
    kept = lax.dynamic_index_in_dim(both, place.core, 0, keepdims=False)
    sent = lax.dynamic_index_in_dim(both, 1 - place.core, 0, keepdims=False)
    came = place.swap_core(sent)
    first = place.core == 0
    left = jnp.concatenate([jnp.where(first, kept, came), jnp.where(first, came, kept)])
    right = jnp.concatenate([fc_out[:, :HALF], fc_out[:, HALF:]])
    return jnp.concatenate([left, right], axis=1)


def gather_units(place, shard):
    whole = lax.all_gather(shard, CHIPS, axis=0)
    if place.fast:
        return [whole]
    rows = shard.shape[0] // 2
    whole = whole.reshape(place.chips, place.mp, 2 * rows, D)
    up = whole[..., :HALF].transpose(0, 2, 1, 3).reshape(D, 2 * D)
    down = whole[..., HALF:].reshape(place.chips, place.mp, 2, rows, HALF)
    return [up, down.transpose(1, 0, 3, 2, 4).reshape(2 * D, D)]


def scatter_units(place, grads):
    total = lax.psum_scatter(grads, CHIPS, scatter_dimension=0, tiled=False)
    rows = total.shape[0] // 2
    kept = lax.dynamic_slice_in_dim(total, place.core * rows, rows, 0)
    sent = lax.dynamic_slice_in_dim(total[:, :HALF], (1 - place.core) * rows, rows, 0)
    came = place.swap_core(sent)
    kept = kept[:, :HALF]
    first = place.core == 0
    both = jnp.stack([jnp.where(first, kept, came), jnp.where(first, came, kept)])
    both = both.reshape(2, rows, place.chips, rows).transpose(1, 2, 0, 3).reshape(rows, D)
    down = jnp.concatenate([total[:rows, HALF:], total[rows:, HALF:]], axis=1)
    return both.astype(F32), down.astype(F32)


def spread(place, own):
    from_x = place.swap_xy(own, 1)
    from_y = place.swap_xy(own, 2)
    far_one = place.swap_xy(from_y[1], 1)
    far_zero = place.swap_xy(from_x[0], 2)
    return [own, from_x, from_y, far_zero, far_one]


def piece_views(refs, which, xy):
    own, from_x, from_y, far_zero, far_one = refs
    return [
        (own.at[which], xy),
        (from_x.at[which], xy ^ 1),
        (from_y.at[which], xy ^ 2),
        ((far_zero, far_one)[which], xy ^ 3),
    ]


def load_wide(copies, refs, which, xy, target, columns=None):
    if len(refs) != 5:
        copies.start(refs[which], target)
        return
    for view, chip in piece_views(refs, which, xy):
        rows = view.shape[0]
        if columns is not None:
            view = view.at[:, pl.ds(0, columns)]
        copies.start(view, target.at[pl.ds(pl.multiple_of(chip * rows, 16), rows)])


def load_out(copies, refs, xy, target):
    if len(refs) != 5:
        copies.start(refs[2], target)
        return
    for view, chip in piece_views(refs, 1, xy):
        rows = view.shape[0] // 4
        for q in range(2):
            for hi in range(2):
                copies.start(
                    view.at[pl.ds((2 * q + hi) * rows, rows), pl.ds(HALF, HALF)],
                    target.at[q, pl.ds(pl.multiple_of(hi * QUARTER + chip * rows, 16), rows)],
                )


def load_units(copies, refs, w_up, w_down):
    if len(refs) == 2:
        if w_up is not None:
            copies.start(refs[0], w_up)
        if w_down is not None:
            copies.start(refs[1], w_down)
        return
    (whole,) = refs
    count, rows, _ = whole.shape
    rows = rows // 2
    chips = count // 4
    for xy in range(chips):
        for z in range(4):
            piece = whole.at[4 * xy + z]
            if w_up is not None:
                copies.start(
                    piece.at[:, pl.ds(0, HALF)],
                    w_up.at[pl.ds(2 * rows * xy, 2 * rows), pl.ds(z * HALF, HALF)],
                )
            if w_down is not None:
                for q in range(2):
                    copies.start(
                        piece.at[pl.ds(q * rows, rows), pl.ds(HALF, HALF)],
                        w_down.at[pl.ds(z * HALF + xy * rows, rows), pl.ds(q * HALF, HALF)],
                    )


ATTENTION_COPIES = 4 + 4 + 16
UNIT_COPIES = 48


def gather_plain(place, shard):
    whole = lax.all_gather(shard, ("mp", "xy", "core"), axis=0)
    whole = whole.reshape((2, 2, place.dp) + shard.shape)
    return lax.dynamic_index_in_dim(whole, place.core, 0, keepdims=False)


def attention_plain(place, shard):
    mine = gather_plain(place, shard)
    rows = shard.shape[0]

    def columns(at, count):
        value = mine[..., at : at + count * QUARTER].reshape(2, D, count, QUARTER)
        return value.transpose(1, 2, 0, 3).reshape(D, count * HALF)

    out = mine[..., 3 * QUARTER :].reshape(2, place.dp, 2, 2, rows // 4, QUARTER)
    out = out.transpose(2, 0, 1, 4, 3, 5).reshape(2, HALF, HALF)
    return [columns(0, 2), columns(HALF, 1), out]


def head_rows(h):
    return pl.ds(pl.multiple_of(h * HEAD_DIM, HEAD_DIM), HEAD_DIM)


def project(left, pair_ref):
    return jnp.concatenate([mm(left, pair_ref[0]), mm(left, pair_ref[1])], axis=1)


def project_t(left, pair_ref):
    return mm_t(left[:, :HALF], pair_ref[0]) + mm_t(left[:, HALF:], pair_ref[1])


def self_forward(hidden, norms, nums, weights):
    length = hidden.shape[0]

    def body(hidden_ref, norms_ref, nums_ref, *refs):
        w_refs, refs = refs[: len(weights)], refs[len(weights) :]
        part_ref, at_ref, qkv_ref, qt_ref, kt_ref, ot_ref, lse_ref = refs[:7]
        w_qk, w_v, w_out, vt, heads, bias, sems = refs[7:]
        _, xy, _ = where_am_i()
        copies = Copies(sems)
        load_wide(copies, w_refs, 0, xy, w_qk)
        load_wide(copies, w_refs, 1, xy, w_v, HALF)
        load_out(copies, w_refs, xy, w_out)
        unit, _ = norm(hidden_ref[...].astype(F32))
        a = (unit * norms_ref[0:1] + norms_ref[4:5]).astype(BF)
        at_ref[...] = a.T
        keys = lax.broadcasted_iota(jnp.int32, (length, length), 0)
        queries = lax.broadcasted_iota(jnp.int32, (length, length), 1)
        allowed = (keys <= queries) & (keys.astype(F32) < nums_ref[0:1, 0:1])
        bias[...] = jnp.where(allowed, 0.0, -1e30)
        copies.wait()
        qk = mm(a, w_qk[...])
        q = (qk[:, :HALF].astype(BF).astype(F32) * HEAD_DIM ** (-0.5)).astype(BF)
        k = qk[:, HALF:].astype(BF)
        v = mm(a, w_v[...]).astype(BF)
        qkv_ref[:, 0:HALF] = q
        qkv_ref[:, HALF : 2 * HALF] = k
        qkv_ref[:, 2 * HALF :] = v
        qt_ref[...] = q.T
        kt_ref[...] = k.T
        vt[...] = v.T
        for h in range(HEADS):
            heads[h] = k[:, h * HEAD_DIM : (h + 1) * HEAD_DIM]

        def head(h, carry):
            s = mm(heads[h], qt_ref[head_rows(h), :]) + bias[...]
            top = jnp.max(s, axis=0, keepdims=True)
            p = jnp.exp(s - top)
            total = jnp.sum(p, axis=0, keepdims=True)
            o = mm(vt[head_rows(h), :], p.astype(BF))
            ot_ref[head_rows(h), :] = (o / total).astype(BF)
            lse_ref[h] = top + jnp.log(total)
            return carry

        lax.fori_loop(0, HEADS, head, 0)
        part_ref[...] = project(ot_ref[...].T, w_out).astype(BF)

    return run(
        body,
        [
            shaped((length, D)),
            shaped((D, length)),
            shaped((length, 3 * HALF)),
            shaped((HALF, length)),
            shaped((HALF, length)),
            shaped((HALF, length)),
            shaped((HEADS, 1, length), F32),
        ],
        vmem=[hidden, norms, nums],
        hbm=weights,
        scratch=[
            pltpu.VMEM((D, D), BF),
            pltpu.VMEM((D, HALF), BF),
            pltpu.VMEM((2, HALF, HALF), BF),
            pltpu.VMEM((HALF, length), BF),
            pltpu.VMEM((HEADS, length, HEAD_DIM), BF),
            pltpu.VMEM((length, length), F32),
        ],
        copies=ATTENTION_COPIES,
        micros=10,
    )


def cross_memory(encoded, weights):
    frames = encoded.shape[0]

    def body(enc_ref, *refs):
        w_refs, refs = refs[: len(weights)], refs[len(weights) :]
        kv_ref, kvt_ref, et_ref, w_kv, sems = refs
        _, xy, _ = where_am_i()
        copies = Copies(sems)
        load_wide(copies, w_refs, 0, xy, w_kv)
        copies.wait()

        def step(i, carry):
            here = pl.ds(pl.multiple_of(i * CHUNK, CHUNK), CHUNK)
            rows = enc_ref[here, :]
            kv = mm(rows, w_kv[...]).astype(BF)
            kv_ref[here, :] = kv
            kvt_ref[:, here] = kv.T
            et_ref[:, here] = rows.T
            return carry

        lax.fori_loop(0, frames // CHUNK, step, 0)

    return run(
        body,
        [shaped((frames, D)), shaped((D, frames)), shaped((D, frames))],
        vmem=[encoded],
        hbm=weights,
        scratch=[pltpu.VMEM((D, D), BF)],
        copies=4,
        micros=9,
    )


def residual(hidden_ref, mine_ref, other_ref):
    return hidden_ref[...].astype(F32) + (mine_ref[...].astype(F32) + other_ref[...].astype(F32))


def cross_forward(hidden, mine, other, norms, nums, kv, kvt, weights):
    length = hidden.shape[0]
    frames = kv.shape[0]

    def body(hidden_ref, mine_ref, other_ref, norms_ref, nums_ref, kv_ref, kvt_ref, *refs):
        w_refs, refs = refs[: len(weights)], refs[len(weights) :]
        part_ref, h_ref, ct_ref, q_ref, qt_ref, ot_ref, lse_ref = refs[:7]
        w_q, w_out, heads, scores, sems = refs[7:]
        _, xy, _ = where_am_i()
        copies = Copies(sems)
        load_wide(copies, w_refs, 1, xy, w_q, HALF)
        load_out(copies, w_refs, xy, w_out)
        h1 = residual(hidden_ref, mine_ref, other_ref)
        h_ref[...] = h1
        unit, _ = norm(h1)
        c = (unit * norms_ref[1:2] + norms_ref[5:6]).astype(BF)
        ct_ref[...] = c.T
        for h in range(HEADS):
            heads[h] = kv_ref[:, h * HEAD_DIM : (h + 1) * HEAD_DIM]
        copies.wait()
        q = mm(c, w_q[...]).astype(BF)
        q = (q.astype(F32) * HEAD_DIM ** (-0.5)).astype(BF)
        q_ref[...] = q
        qt_ref[...] = q.T
        heard = nums_ref[1:2, 0:1]

        def head(h, carry):
            qt = qt_ref[head_rows(h), :]
            top = None
            for at in range(0, frames, CHUNK):
                s = mm(heads[h, at : at + CHUNK], qt)
                place = lax.broadcasted_iota(jnp.int32, s.shape, 0) + at
                s = jnp.where(place.astype(F32) < heard, s, -1e30)
                scores[at : at + CHUNK] = s
                high = jnp.max(s, axis=0, keepdims=True)
                top = high if top is None else jnp.maximum(top, high)
            total, o = 0.0, 0.0
            values = pl.ds(pl.multiple_of(HALF + h * HEAD_DIM, HEAD_DIM), HEAD_DIM)
            for at in range(0, frames, CHUNK):
                p = jnp.exp(scores[at : at + CHUNK] - top)
                total = total + jnp.sum(p, axis=0, keepdims=True)
                o = o + mm(kvt_ref[values, at : at + CHUNK], p.astype(BF))
            ot_ref[head_rows(h), :] = (o / total).astype(BF)
            lse_ref[h] = top + jnp.log(total)
            return carry

        lax.fori_loop(0, HEADS, head, 0)
        part_ref[...] = project(ot_ref[...].T, w_out).astype(BF)

    return run(
        body,
        [
            shaped((length, D)),
            shaped((length, D), F32),
            shaped((D, length)),
            shaped((length, HALF)),
            shaped((HALF, length)),
            shaped((HALF, length)),
            shaped((HEADS, 1, length), F32),
        ],
        vmem=[hidden, mine, other, norms, nums, kv, kvt],
        hbm=weights,
        scratch=[
            pltpu.VMEM((D, HALF), BF),
            pltpu.VMEM((2, HALF, HALF), BF),
            pltpu.VMEM((HEADS, frames, HEAD_DIM), BF),
            pltpu.VMEM((frames, length), F32),
        ],
        copies=4 + 16,
        micros=16,
    )


def units_forward(hidden, mine, other, norms, weights):
    length = hidden.shape[0]

    def body(hidden_ref, mine_ref, other_ref, norms_ref, *refs):
        w_refs, refs = refs[: len(weights)], refs[len(weights) :]
        part_ref, h_ref, mt_ref, slope_ref, it_ref = refs[:5]
        w_up, w_down, inner, sems = refs[5:]
        _, xy, _ = where_am_i()
        copies = Copies(sems)
        load_units(copies, w_refs, w_up, None)
        load_units(copies, w_refs, None, w_down)
        h2 = residual(hidden_ref, mine_ref, other_ref)
        h_ref[...] = h2
        unit, _ = norm(h2)
        m = (unit * norms_ref[2:3] + norms_ref[6:7]).astype(BF)
        mt_ref[...] = m.T
        copies.wait()
        for at in range(0, 2 * D, CHUNK):
            here = slice(at, at + CHUNK)
            z = mm(m, w_up[:, here])
            share = 0.5 * (1.0 + lax.erf(z * 0.7071067811865476))
            slope = share + z * (0.3989422804014327 * jnp.exp(-0.5 * z * z))
            value = (z * share).astype(BF)
            inner[:, here] = value
            it_ref[here, :] = value.T
            slope_ref[:, here] = slope.astype(BF)
        for at in range(0, D, CHUNK):
            part_ref[:, at : at + CHUNK] = mm(inner[...], w_down[:, at : at + CHUNK]).astype(BF)

    return run(
        body,
        [
            shaped((length, D)),
            shaped((length, D), F32),
            shaped((D, length)),
            shaped((length, 2 * D)),
            shaped((2 * D, length)),
        ],
        vmem=[hidden, mine, other, norms],
        hbm=weights,
        scratch=[
            pltpu.VMEM((D, 2 * D), BF),
            pltpu.VMEM((2 * D, D), BF),
            pltpu.VMEM((length, 2 * D), BF),
        ],
        copies=UNIT_COPIES,
        micros=9,
    )


def store_blocks(value, blocks, first_ref, second_ref):
    core, _, z = where_am_i()
    for b in range(4):
        blocks[b] = value[:, b * QUARTER : (b + 1) * QUARTER]
    first_ref[...] = blocks[2 * core + z % 2].T
    second_ref[...] = blocks[2 * core + (z + 1) % 2].T


def units_backward(hidden, mine, other, norms, nums, cot, slope, weights):
    length = hidden.shape[0]

    def body(hidden_ref, mine_ref, other_ref, norms_ref, nums_ref, cot_ref, slope_ref, *refs):
        w_refs, refs = refs[: len(weights)], refs[len(weights) :]
        part_ref, d_ref, e_ref, dz_ref, terms_ref, first_ref, second_ref = refs[:7]
        w_up, w_down, blocks, sems = refs[7:]
        _, xy, _ = where_am_i()
        copies = Copies(sems)
        load_units(copies, w_refs, None, w_down)
        load_units(copies, w_refs, w_up, None)
        unit, inverse = norm(residual(hidden_ref, mine_ref, other_ref))
        final = (unit * norms_ref[3:4] + norms_ref[7:8]).astype(BF)
        store_blocks(final, blocks, first_ref, second_ref)
        live = lax.broadcasted_iota(jnp.int32, (length, 1), 0).astype(F32) < nums_ref[0:1, 0:1]
        grad = cot_ref[...].astype(F32) * jnp.where(live, nums_ref[2:3, 0:1], 0.0)
        d3, terms = norm_back(grad, unit, inverse, norms_ref[3:4])
        d_ref[...] = d3
        terms_ref[...] = terms
        e = d3.astype(BF)
        e_ref[...] = e
        copies.wait()
        for at in range(0, 2 * D, CHUNK):
            here = slice(at, at + CHUNK)
            d_inner = mm_t(e, w_down[here, :])
            dz_ref[:, here] = (slope_ref[:, here].astype(F32) * d_inner).astype(BF)
        for at in range(0, D, CHUNK):
            out = mm_t(dz_ref[...], w_up[at : at + CHUNK, :])
            part_ref[:, at : at + CHUNK] = out.astype(BF)

    return run(
        body,
        [
            shaped((length, D)),
            shaped((length, D), F32),
            shaped((length, D)),
            shaped((length, 2 * D)),
            shaped((2, D), F32),
            shaped((QUARTER, length)),
            shaped((QUARTER, length)),
        ],
        vmem=[hidden, mine, other, norms, nums, cot, slope],
        hbm=weights,
        scratch=[
            pltpu.VMEM((D, 2 * D), BF),
            pltpu.VMEM((2 * D, D), BF),
            pltpu.VMEM((4, length, QUARTER), BF),
        ],
        copies=UNIT_COPIES,
        micros=10,
    )


def step_back(d_ref, hidden_ref, mine_ref, other_ref, gain):
    unit, inverse = norm(hidden_ref[...].astype(F32))
    grad = mine_ref[...].astype(F32) + other_ref[...].astype(F32)
    part, terms = norm_back(grad, unit, inverse, gain)
    return d_ref[...] + part, terms


def cross_backward(d, hidden, mine, other, norms, nums, kv, kvt, q, qt, ot, lse, weights):
    length = hidden.shape[0]
    frames = kv.shape[0]

    def body(
        d_ref, hidden_ref, mine_ref, other_ref, norms_ref, nums_ref, kv_ref, kvt_ref, q_ref,
        qt_ref, ot_ref, lse_ref, *refs
    ):
        w_refs, refs = refs[: len(weights)], refs[len(weights) :]
        part_ref, d_out_ref, e_ref, dq_ref, dkv_ref, terms_ref = refs[:6]
        w_q, w_out, keys, values, queries, grads, dot_t, dk_h, dv_h, dqt, sems = refs[6:]
        _, xy, _ = where_am_i()
        copies = Copies(sems)
        load_wide(copies, w_refs, 1, xy, w_q, HALF)
        load_out(copies, w_refs, xy, w_out)
        d2, terms = step_back(d_ref, hidden_ref, mine_ref, other_ref, norms_ref[2:3])
        d_out_ref[...] = d2
        terms_ref[...] = terms
        e = d2.astype(BF)
        e_ref[...] = e
        for h in range(HEADS):
            lanes = slice(h * HEAD_DIM, (h + 1) * HEAD_DIM)
            keys[h] = kv_ref[:, lanes]
            values[h] = kv_ref[:, HALF + h * HEAD_DIM : HALF + (h + 1) * HEAD_DIM]
            queries[h] = q_ref[:, lanes]
        copies.wait()
        d_mixed = project_t(e, w_out).astype(BF)
        dot_t[...] = d_mixed.T
        for h in range(HEADS):
            grads[h] = d_mixed[:, h * HEAD_DIM : (h + 1) * HEAD_DIM]
        heard = nums_ref[1:2, 0:1]

        def head(h, carry):
            rows = head_rows(h)
            q_t, do_t = qt_ref[rows, :], dot_t[rows, :]
            q_n, do_n = queries[h], grads[h]
            delta = jnp.sum(do_t.astype(F32) * ot_ref[rows, :].astype(F32), axis=0, keepdims=True)
            level = lse_ref[h]
            total = 0.0
            for at in range(0, frames, CHUNK):
                here = slice(at, at + CHUNK)
                s = mm(keys[h, here], q_t)
                place = lax.broadcasted_iota(jnp.int32, s.shape, 0) + at
                s = jnp.where(place.astype(F32) < heard, s, -1e30)
                p = jnp.exp(s - level)
                dp = mm(values[h, here], do_t)
                ds = (p * (dp - delta)).astype(BF)
                dv_h[h, here] = mm(p.astype(BF), do_n).astype(BF)
                dk_h[h, here] = mm(ds, q_n).astype(BF)
                total = total + mm(kvt_ref[rows, here], ds)
            dqt[rows, :] = (total * HEAD_DIM ** (-0.5)).astype(BF)
            return carry

        lax.fori_loop(0, HEADS, head, 0)
        dq = dqt[...].T
        dq_ref[...] = dq
        part_ref[...] = mm_t(dq, w_q[...]).astype(BF)
        for h in range(HEADS):
            lanes = slice(h * HEAD_DIM, (h + 1) * HEAD_DIM)
            dkv_ref[:, lanes] = dk_h[h]
            dkv_ref[:, HALF + h * HEAD_DIM : HALF + (h + 1) * HEAD_DIM] = dv_h[h]

    return run(
        body,
        [
            shaped((length, D)),
            shaped((length, D), F32),
            shaped((length, D)),
            shaped((length, HALF)),
            shaped((frames, D)),
            shaped((2, D), F32),
        ],
        vmem=[d, hidden, mine, other, norms, nums, kv, kvt, q, qt, ot, lse],
        hbm=weights,
        scratch=[
            pltpu.VMEM((D, HALF), BF),
            pltpu.VMEM((2, HALF, HALF), BF),
            pltpu.VMEM((HEADS, frames, HEAD_DIM), BF),
            pltpu.VMEM((HEADS, frames, HEAD_DIM), BF),
            pltpu.VMEM((HEADS, length, HEAD_DIM), BF),
            pltpu.VMEM((HEADS, length, HEAD_DIM), BF),
            pltpu.VMEM((HALF, length), BF),
            pltpu.VMEM((HEADS, frames, HEAD_DIM), BF),
            pltpu.VMEM((HEADS, frames, HEAD_DIM), BF),
            pltpu.VMEM((HALF, length), BF),
        ],
        copies=4 + 16,
        micros=24,
    )


def self_backward(d, hidden, mine, other, norms, nums, qkv, qt, kt, ot, lse, weights):
    length = hidden.shape[0]

    def body(
        d_ref, hidden_ref, mine_ref, other_ref, norms_ref, nums_ref, qkv_ref, qt_ref, kt_ref,
        ot_ref, lse_ref, *refs
    ):
        w_refs, refs = refs[: len(weights)], refs[len(weights) :]
        part_ref, d_out_ref, e_ref, dqkv_ref, terms_ref = refs[:5]
        w_qk, w_v, w_out, qkv_h, grads, dot_t, dk_h, dv_h, dqt, bias, sems = refs[5:]
        _, xy, _ = where_am_i()
        copies = Copies(sems)
        load_out(copies, w_refs, xy, w_out)
        load_wide(copies, w_refs, 0, xy, w_qk)
        load_wide(copies, w_refs, 1, xy, w_v, HALF)
        d1, terms = step_back(d_ref, hidden_ref, mine_ref, other_ref, norms_ref[1:2])
        d_out_ref[...] = d1
        terms_ref[...] = terms
        e = d1.astype(BF)
        e_ref[...] = e
        places = lax.broadcasted_iota(jnp.int32, (length, length), 0)
        queries = lax.broadcasted_iota(jnp.int32, (length, length), 1)
        allowed = (places <= queries) & (places.astype(F32) < nums_ref[0:1, 0:1])
        bias[...] = jnp.where(allowed, 0.0, -1e30)
        for j in range(3):
            for h in range(HEADS):
                lanes = slice(j * HALF + h * HEAD_DIM, j * HALF + (h + 1) * HEAD_DIM)
                qkv_h[j * HEADS + h] = qkv_ref[:, lanes]
        copies.wait()
        d_mixed = project_t(e, w_out).astype(BF)
        dot_t[...] = d_mixed.T
        for h in range(HEADS):
            grads[h] = d_mixed[:, h * HEAD_DIM : (h + 1) * HEAD_DIM]

        def head(h, carry):
            rows = head_rows(h)
            do_t, do_n = dot_t[rows, :], grads[h]
            delta = jnp.sum(do_t.astype(F32) * ot_ref[rows, :].astype(F32), axis=0, keepdims=True)
            s = mm(qkv_h[HEADS + h], qt_ref[rows, :]) + bias[...]
            p = jnp.exp(s - lse_ref[h])
            dp = mm(qkv_h[2 * HEADS + h], do_t)
            ds = (p * (dp - delta)).astype(BF)
            dv_h[h] = mm(p.astype(BF), do_n).astype(BF)
            dk_h[h] = mm(ds, qkv_h[h]).astype(BF)
            dqt[rows, :] = (mm(kt_ref[rows, :], ds) * HEAD_DIM ** (-0.5)).astype(BF)
            return carry

        lax.fori_loop(0, HEADS, head, 0)
        dqkv_ref[:, 0:HALF] = dqt[...].T
        for h in range(HEADS):
            lanes = slice(HALF + h * HEAD_DIM, HALF + (h + 1) * HEAD_DIM)
            dqkv_ref[:, lanes] = dk_h[h]
            lanes = slice(2 * HALF + h * HEAD_DIM, 2 * HALF + (h + 1) * HEAD_DIM)
            dqkv_ref[:, lanes] = dv_h[h]
        out = mm_t(dqkv_ref[:, 0 : 2 * HALF], w_qk[...])
        part_ref[...] = (out + mm_t(dqkv_ref[:, 2 * HALF :], w_v[...])).astype(BF)

    return run(
        body,
        [
            shaped((length, D)),
            shaped((length, D), F32),
            shaped((length, D)),
            shaped((length, 3 * HALF)),
            shaped((2, D), F32),
        ],
        vmem=[d, hidden, mine, other, norms, nums, qkv, qt, kt, ot, lse],
        hbm=weights,
        scratch=[
            pltpu.VMEM((D, D), BF),
            pltpu.VMEM((D, HALF), BF),
            pltpu.VMEM((2, HALF, HALF), BF),
            pltpu.VMEM((3 * HEADS, length, HEAD_DIM), BF),
            pltpu.VMEM((HEADS, length, HEAD_DIM), BF),
            pltpu.VMEM((HALF, length), BF),
            pltpu.VMEM((HEADS, length, HEAD_DIM), BF),
            pltpu.VMEM((HEADS, length, HEAD_DIM), BF),
            pltpu.VMEM((HALF, length), BF),
            pltpu.VMEM((length, length), F32),
        ],
        copies=ATTENTION_COPIES,
        micros=14,
    )


def finish_hidden(d, hidden, mine, other, norms, terms1, terms2, terms3):
    length = hidden.shape[0]

    def body(
        d_ref, hidden_ref, mine_ref, other_ref, norms_ref, one, two, three, terms_ref, first_ref,
        second_ref, blocks
    ):
        d0, terms = step_back(d_ref, hidden_ref, mine_ref, other_ref, norms_ref[0:1])
        store_blocks(d0.astype(BF), blocks, first_ref, second_ref)
        for j in range(2):
            here = slice(j, j + 1)
            terms_ref[4 * j : 4 * j + 4] = jnp.concatenate(
                [terms[here], one[here], two[here], three[here]], axis=0
            )

    return run(
        body,
        [shaped((8, D), F32), shaped((QUARTER, length)), shaped((QUARTER, length))],
        vmem=[d, hidden, mine, other, norms, terms1, terms2, terms3],
        scratch=[pltpu.VMEM((4, length, QUARTER), BF)],
        micros=4,
    )


def finish_encoder(keep, other):
    frames = keep.shape[1]

    def body(keep_ref, other_ref, first_ref, second_ref):
        _, _, z = where_am_i()
        for ref, k in ((first_ref, 0), (second_ref, 1)):
            here = pl.ds(pl.multiple_of(((z + k) % 2) * QUARTER, QUARTER), QUARTER)
            total = keep_ref[here, :].astype(F32) + other_ref[here, :].astype(F32)
            ref[...] = total.astype(BF)

    return run(
        body,
        [shaped((QUARTER, frames)), shaped((QUARTER, frames))],
        vmem=[keep, other],
        micros=2,
    )


def block_plan(place):
    if not place.fast:
        return 1, (((1, 0, 0),), ((1, 0, 0),))
    first = ((1, 0, 0), (0, 0, 1), (1, 1, 2), (0, 1, 3))
    second = ((1, 0, 0), (1, 1, 1), (0, 0, 2), (0, 1, 3))
    return 4, (first, second)


def grad_outputs(place, shape):
    if place.fast:
        return [shaped((2,) + shape)] * 4
    return [shaped((1,) + shape)] * 4


def units_grads(place, mt, dz, it, e):
    chips = place.chips
    rows = D // (2 * chips)

    def body(mt_ref, dz_ref, it_ref, e_ref, out_ref):
        for xy in range(chips):
            left = mm(mt_ref[2 * rows * xy : 2 * rows * (xy + 1), :], dz_ref[...]).astype(BF)
            for z in range(4):
                out_ref[4 * xy + z, :, 0:HALF] = left[:, z * HALF : (z + 1) * HALF]
                at = z * HALF + xy * rows
                right = mm(it_ref[at : at + rows, :], e_ref[...]).astype(BF)
                for q in range(2):
                    out_ref[4 * xy + z, q * rows : (q + 1) * rows, HALF:D] = right[
                        :, q * HALF : (q + 1) * HALF
                    ]

    def plain(mt_ref, dz_ref, it_ref, e_ref, left_ref, right_ref):
        left_ref[...] = mm(mt_ref[...], dz_ref[...]).astype(BF)
        right_ref[...] = mm(it_ref[...], e_ref[...]).astype(BF)

    if place.fast:
        return run(
            body, [shaped((4 * chips, 2 * rows, D))], vmem=[mt, dz, it, e], micros=7
        )[0]
    left, right = run(
        plain, [shaped((D, 2 * D)), shaped((2 * D, D))], vmem=[mt, dz, it, e], micros=7
    )
    left = left.reshape(chips, 2 * rows, 4, HALF).transpose(0, 2, 1, 3)
    right = right.reshape(4, chips, rows, 2, HALF).transpose(1, 0, 3, 2, 4)
    whole = jnp.concatenate([left, right.reshape(chips, 4, 2 * rows, HALF)], axis=-1)
    return whole.reshape(4 * chips, 2 * rows, D)


def attention_grads(place, wide_left, wide_right, left, right, ot, e):
    count, plan = block_plan(place)
    rows = D // count
    few = rows // 4

    def body(wide_left_ref, wide_right_ref, left_ref, right_ref, ot_ref, e_ref, *outs):
        _, xy, _ = where_am_i()
        for output, slot, offset in plan[0]:
            chip = xy ^ offset if count > 1 else 0
            here = pl.ds(pl.multiple_of(chip * rows, 16), rows)
            outs[output][slot] = mm(wide_left_ref[here, :], wide_right_ref[...]).astype(BF)
        for output, slot, offset in plan[1]:
            chip = xy ^ offset if count > 1 else 0
            here = pl.ds(pl.multiple_of(chip * rows, 16), rows)
            target = outs[2 + output]
            target[slot, :, 0:HALF] = mm(left_ref[here, :], right_ref[...]).astype(BF)
            for hi in range(2):
                here = pl.ds(pl.multiple_of(hi * QUARTER + chip * few, 16), few)
                both = mm(ot_ref[here, :], e_ref[...]).astype(BF)
                for q in range(2):
                    at = (2 * q + hi) * few
                    target[slot, at : at + few, HALF:D] = both[:, q * HALF : (q + 1) * HALF]

    return run(
        body,
        grad_outputs(place, (rows, D)),
        vmem=[wide_left, wide_right, left, right, ot, e],
        micros=6,
    )


def encoder_grad(dkv, weights, frames):
    padded = dkv.shape[0]

    def body(dkv_ref, *refs):
        w_refs, (keep_ref, send_ref, w_kv, sems) = refs[: len(weights)], refs[len(weights) :]
        core, xy, _ = where_am_i()
        copies = Copies(sems)
        load_wide(copies, w_refs, 0, xy, w_kv)
        copies.wait()
        mine = pl.ds(pl.multiple_of(core * HALF, HALF), HALF)
        theirs = pl.ds(pl.multiple_of((1 - core) * HALF, HALF), HALF)
        for ref, rows in ((send_ref, theirs), (keep_ref, mine)):
            for at in range(0, padded, CHUNK):
                size = min(CHUNK, frames - at)
                value = mm_t(w_kv[rows, :], dkv_ref[at : at + CHUNK, :]).astype(BF)
                ref[:, at : at + size] = value[:, :size]

    return run(
        body,
        [shaped((HALF, frames)), shaped((HALF, frames))],
        vmem=[dkv],
        hbm=weights,
        scratch=[pltpu.VMEM((D, D), BF)],
        copies=4,
        micros=4,
    )


def leave_plane(place, grads):
    return [place.swap_xy(grads[0], 1), place.swap_xy(grads[2], 2)]


def pass_on(grads, came, after):
    shape = grads[1].shape[1:]

    def body(stay0, came0, stay1, came1, *refs):
        out0, out1, held, sems = refs[-4:]
        copies = Copies(sems)
        for i, ref in enumerate((stay0, came0, stay1, came1)):
            copies.start(ref.at[1], held.at[i])
        copies.wait()
        out0[...] = add_up(held[0], held[1]).astype(BF)
        out1[...] = add_up(held[2], held[3]).astype(BF)

    return run(
        body,
        [shaped(shape), shaped(shape)],
        hbm=[grads[1], came[0], grads[3], came[1]] + list(after),
        scratch=[pltpu.VMEM((4,) + shape, BF)],
        copies=4,
        micros=1,
    )


def cross_plane(place, onward):
    return [place.swap_xy(onward[0], 2), place.swap_xy(onward[1], 1)]


def column_blocks(grads, came, onward, attention, norm_terms=(), after=()):
    shape = onward[0].shape
    rows = shape[-2] // 2
    width = D if attention else 2 * D
    few = rows // 4
    extra = 16 if norm_terms else 0

    def body(*refs):
        terms_refs, refs = refs[: len(norm_terms)], refs[len(norm_terms) :]
        ins, outs, (held, shards, sems) = refs[:6], refs[-7:-3], refs[-3:]
        home, slots = column_slots()
        copies = Copies(sems)
        for i, ref in enumerate(ins):
            copies.start(ref if i % 3 == 2 else ref.at[0], held.at[i])
        copies.wait()
        sums = [add_up(held[3 * part], held[3 * part + 1], held[3 * part + 2]) for part in range(2)]
        for hi in range(2):
            for cs in range(2):
                here = slice(cs * rows, (cs + 1) * rows)
                if attention:
                    lanes = slice(hi * QUARTER, (hi + 1) * QUARTER)
                    lanes_two = slice(HALF + hi * QUARTER, HALF + (hi + 1) * QUARTER)
                    outs_rows = []
                    for p in range(4):
                        at = (2 * (p // 2) + hi) * 2 * few + cs * few
                        side = HALF + (p % 2) * QUARTER
                        outs_rows.append(sums[1][at : at + few, side : side + QUARTER])
                    value = jnp.concatenate(
                        [
                            sums[0][here, lanes],
                            sums[0][here, lanes_two],
                            sums[1][here, lanes],
                            jnp.concatenate(outs_rows, axis=0),
                        ],
                        axis=1,
                    )
                else:
                    value = jnp.concatenate([sums[0][hi, here], sums[1][hi, here]], axis=1)
                shards[2 * hi + cs, :rows] = value.astype(BF)
        if norm_terms:
            core, xy, _ = where_am_i()
            terms = add_up(*[ref[...] for ref in terms_refs])
            terms = jnp.concatenate([terms, jnp.zeros_like(terms)], axis=0).astype(BF)
            feature = lax.broadcasted_iota(jnp.int32, (D, D), 0)
            lane = lax.broadcasted_iota(jnp.int32, (D, D), 1)
            for hi in range(2):
                for cs in range(2):
                    offset = (2 * core + hi) * QUARTER + (2 * xy + cs) * few
                    pick = jnp.where((feature == lane + offset) & (lane < few), 1.0, 0.0)
                    shards[2 * hi + cs, rows:] = mm(terms, pick.astype(BF)).astype(BF)
        for k in range(4):
            outs[k][...] = shards[slots[k]]

    ins = [grads[1], came[0], onward[0], grads[3], came[1], onward[1]]
    return run(
        body,
        [shaped((rows + extra, width))] * 4,
        vmem=list(norm_terms),
        hbm=ins + list(after),
        scratch=[pltpu.VMEM((6,) + shape, BF), pltpu.VMEM((4, rows + extra, width), BF)],
        copies=6,
        micros=4,
    )


def sum_plain(place, grads, attention):
    wide, narrow = grads[1][0], grads[3][0]
    rows = D // place.dp
    if attention:
        value = jnp.stack([wide[:, :HALF], wide[:, HALF:], narrow[:, :HALF]], axis=1)
        value = value.reshape(place.dp, rows, 3, 2, QUARTER).transpose(3, 0, 1, 2, 4)
        value = value.reshape(2, place.dp, rows, 3 * QUARTER)
        outs = narrow[:, HALF:].reshape(2, 2, place.dp, rows // 4, 2, QUARTER)
        outs = outs.transpose(1, 2, 0, 4, 3, 5).reshape(2, place.dp, rows, QUARTER)
        value = jnp.concatenate([value, outs], axis=-1)
    else:
        value = jnp.concatenate(
            [wide.reshape(2, place.dp, rows, D), narrow.reshape(2, place.dp, rows, D)], axis=-1
        )
    whole = jnp.zeros((2,) + value.shape, F32)
    whole = lax.dynamic_update_index_in_dim(whole, value.astype(F32), place.core, 0)
    whole = whole.reshape((4 * place.dp,) + value.shape[2:])
    return lax.psum_scatter(whole, ("mp", "xy", "core"), scatter_dimension=0, tiled=False)


def from_quarters(value):
    few = value.shape[0] // 4
    return value.reshape(4, few, QUARTER).transpose(1, 0, 2).reshape(few, D)


def three_parts(value):
    terms = []
    for _ in range(3):
        term = lax.reduce_precision(value, 8, 7)
        terms.append(term.astype(BF))
        value = value - term
    return jnp.concatenate(terms)


def per_device(
    dp,
    mp,
    hidden_in,
    encoder_states,
    cotangent,
    self_qkv,
    self_out,
    cross_q,
    cross_kv,
    cross_out,
    fc_in,
    fc_out,
    ln_gain,
    ln_bias,
    token_lengths,
    audio_lengths,
    corpus_ids,
    corpus_weights,
):
    place = Place(dp, mp)
    length = hidden_in.shape[2]
    frames = encoder_states.shape[2]
    padded = -(-frames // CHUNK) * CHUNK
    rows = self_qkv.shape[0]

    w_units = gather_units(place, unit_shard(place, fc_in, fc_out))
    if place.fast:
        own_self, own_cross = attention_shards(self_qkv, self_out, cross_q, cross_kv, cross_out)
        w_self = spread(place, pack_attention(place.column_out(own_self), own_self))
        w_cross = spread(place, pack_attention(place.column_out(own_cross), own_cross))
    else:
        quarter = lambda w: w.reshape(-1, 4, QUARTER).transpose(1, 0, 2).reshape(-1, QUARTER)
        flat = lambda w: w.reshape(rows, -1)
        w_self = attention_plain(
            place, jnp.concatenate([flat(self_qkv), quarter(self_out)], axis=1)
        )
        w_cross = attention_plain(
            place, jnp.concatenate([flat(cross_kv), cross_q, quarter(cross_out)], axis=1)
        )

    turned = lambda value: value[:, 0].transpose(0, 2, 1)
    numbers = jnp.concatenate([token_lengths.T, audio_lengths.T, corpus_ids.T])
    blocks = input_blocks(
        turned(hidden_in),
        turned(cotangent),
        three_parts(jnp.concatenate([ln_gain, ln_bias])),
        numbers,
    )
    got = place.rows_in(blocks)
    hidden, cot, norms, nums = prepare(got, place.swap_core(got), corpus_weights)

    encoded = lax.dynamic_index_in_dim(encoder_states[:, 0], place.micro, 0, keepdims=False)
    other = place.move(encoded, lambda xy, core, z: (xy, 1 - core, z) if core == z // 2 else None)
    encoded = jnp.where(place.home == place.core, encoded, other)
    encoded = jnp.pad(encoded, ((0, padded - frames), (0, 0)))

    part1, at, qkv, qt, kt, ot1, lse1 = self_forward(hidden, norms, nums, w_self)
    other1 = place.swap_core(part1)
    kv, kvt, et = cross_memory(encoded, w_cross)
    part2, h1, ct, q2, qt2, ot2, lse2 = cross_forward(
        hidden, part1, other1, norms, nums, kv, kvt, w_cross
    )
    other2 = place.swap_core(part2)
    part3, h2, mt, slope, it = units_forward(h1, part2, other2, norms, w_units)
    other3 = place.swap_core(part3)
    part, d3, e3, dz, terms3, out_a, out_b = units_backward(
        h2, part3, other3, norms, nums, cot, slope, w_units
    )
    other = place.swap_core(part)
    g_units = units_grads(place, mt, dz, it, e3)
    s_up, s_down = scatter_units(place, g_units)
    layer_out = place.rows_home((out_a, out_b))
    part, d2, e2, dq2, dkv, terms2 = cross_backward(
        d3, h2, part, other, norms, nums, kv, kvt, q2, qt2, ot2, lse2, w_cross
    )
    other = place.swap_core(part)
    g_cross = attention_grads(place, et, dkv, ct, dq2, ot2, e2)
    if place.fast:
        came_cross = leave_plane(place, g_cross)
    keep, send = encoder_grad(dkv, w_cross, frames)
    part, d1, e1, dqkv, terms1 = self_backward(
        d2, h1, part, other, norms, nums, qkv, qt, kt, ot1, lse1, w_self
    )
    other = place.swap_core(part)
    g_self = attention_grads(
        place, at, dqkv[:, : 2 * HALF], at, dqkv[:, 2 * HALF :], ot1, e1
    )
    if place.fast:
        came_self = leave_plane(place, g_self)
    terms, out_a, out_b = finish_hidden(d1, hidden, part, other, norms, terms1, terms2, terms3)
    grad_hidden = place.rows_home((out_a, out_b)).astype(F32)
    grad_encoder = place.rows_home(finish_encoder(keep, place.swap_core(send))).astype(F32)

    few = D // (place.dp * place.mp)
    if place.fast:
        onward_cross = cross_plane(place, pass_on(g_cross, came_cross, [g_self[0]]))
        terms = terms + place.swap_xy(terms, 1)
        s_cross = place.column_back(column_blocks(g_cross, came_cross, onward_cross, True, (), [terms]))
        onward_self = cross_plane(place, pass_on(g_self, came_self, []))
        s_self = place.column_back(
            column_blocks(
                g_self, came_self, onward_self, True, (terms, place.swap_xy(terms, 2))
            )
        )
        shares = s_self[rows : rows + 8, :few]
    else:
        s_cross = sum_plain(place, g_cross, True)
        s_self = sum_plain(place, g_self, True)
        terms = jnp.where(place.core == 0, terms, 0.0)
        terms = lax.psum(terms, AXES)
        shares = lax.dynamic_slice_in_dim(terms, (place.z * place.dp + place.d) * few, few, 1)
    s_self = s_self[:rows]
    return (
        layer_out,
        grad_hidden,
        grad_encoder,
        s_self[:, : 3 * QUARTER].reshape(rows, 3, QUARTER),
        from_quarters(s_self[:, 3 * QUARTER :]),
        s_cross[:, 2 * QUARTER : 3 * QUARTER],
        s_cross[:, : 2 * QUARTER].reshape(rows, 2, QUARTER),
        from_quarters(s_cross[:, 3 * QUARTER :]),
        s_up,
        s_down,
        shares[:4],
        shares[4:],
    )


def solution(mesh):
    dp, mp = mesh.shape["dp"], mesh.shape["mp"]
    finer = Mesh(mesh.devices.reshape(dp // 2, 2, mp), AXES)
    both = ("xy", "core")
    rows = P(None, both, None, "mp")
    columns = P(both, None, "mp")
    pairs = P(both, "mp")
    units = P(("mp",) + both, None)
    each = P(None, both)
    return jax.shard_map(
        partial(per_device, dp, mp),
        mesh=finer,
        in_specs=(
            rows,
            P(None, both, None, None),
            rows,
            columns,
            units,
            pairs,
            columns,
            units,
            pairs,
            units,
            P(None, "mp"),
            P(None, "mp"),
            each,
            each,
            each,
            P(),
        ),
        out_specs=(
            rows,
            rows,
            rows,
            columns,
            units,
            pairs,
            columns,
            units,
            pairs,
            units,
            P(None, ("mp",) + both),
            P(None, ("mp",) + both),
        ),
        check_vma=False,
    )
```

```python
from functools import partial

import jax
import jax.numpy as jnp
from jax import lax
from jax.experimental import pallas as pl
from jax.experimental.pallas import tpu as pltpu
from jax.sharding import Mesh, PartitionSpec as P

D = 768
HALF = 384
QUARTER = 192
HEAD_DIM = 64
HEADS = 6
CHUNK = 256
BF = jnp.bfloat16
F32 = jnp.float32
AXES = ("xy", "core", "mp")
CHIPS = ("xy", "mp")
VMEM = pl.BlockSpec(memory_space=pltpu.VMEM)
SMEM = pl.BlockSpec(memory_space=pltpu.SMEM)
ANY = pl.BlockSpec(memory_space=pl.ANY)


def mm(left, right):
    return jnp.dot(left, right, preferred_element_type=F32)


def mm_t(left, right):
    return lax.dot_general(left, right, (((1,), (1,)), ((), ())), preferred_element_type=F32)


def shaped(shape, dtype=BF):
    return jax.ShapeDtypeStruct(shape, dtype)


def run(body, outs, vmem=(), hbm=(), smem=(), scratch=(), copies=0, micros=2, after=()):
    args = tuple(smem) + tuple(vmem) + tuple(hbm)
    count = len(args)
    scratch = list(scratch)
    if copies:
        scratch.append(pltpu.SemaphoreType.DMA((copies,)))
    moved = sum(a.size * a.dtype.itemsize for a in args) + sum(
        o.size * o.dtype.itemsize for o in outs
    )
    return pl.pallas_call(
        lambda *refs: body(*refs[:count], *refs[count + len(after) :]),
        out_shape=tuple(outs),
        in_specs=[SMEM] * len(smem) + [VMEM] * len(vmem) + [ANY] * (len(hbm) + len(after)),
        out_specs=(VMEM,) * len(outs),
        scratch_shapes=scratch,
        compiler_params=pltpu.CompilerParams(vmem_limit_bytes=56 * 1024 * 1024),
        cost_estimate=pl.CostEstimate(
            flops=int(micros * 1.15e9), bytes_accessed=moved, transcendentals=0
        ),
    )(*args, *after)


class Copies:
    def __init__(self, sems):
        self.sems, self.open = sems, []

    def start(self, source, target):
        copy = pltpu.make_async_copy(source, target, self.sems.at[len(self.open)])
        copy.start()
        self.open.append(copy)

    def wait(self):
        for copy in self.open:
            copy.wait()


def where_am_i():
    return lax.axis_index("core"), lax.axis_index("xy"), lax.axis_index("mp")


class Place:
    def __init__(self, dp, mp):
        self.dp, self.mp = dp, mp
        self.chips = dp // 2
        self.fast = self.chips == 4
        self.z = lax.axis_index("mp")
        self.core = lax.axis_index("core")
        self.xy = lax.axis_index("xy")
        self.d = 2 * self.xy + self.core
        self.micro = self.z % 2
        self.home = self.z // 2

    def move(self, value, route):
        pairs = []
        for xy in range(self.chips):
            for core in range(2):
                for z in range(self.mp):
                    target = route(xy, core, z)
                    if target is not None:
                        txy, tcore, tz = target
                        pairs.append(
                            ((2 * xy + core) * self.mp + z, (2 * txy + tcore) * self.mp + tz)
                        )
        return lax.ppermute(value, AXES, pairs)

    def swap_core(self, value):
        return self.move(value, lambda xy, core, z: (xy, 1 - core, z))

    def swap_xy(self, value, bit):
        return self.move(value, lambda xy, core, z: (xy ^ bit, core, z))

    def swap_z(self, value, bit):
        return self.move(value, lambda xy, core, z: (xy, core, z ^ bit))

    def column_routes(self):
        def route(step, xy, core, z):
            user, j = z // 2, z % 2
            home = core == user
            near = lambda i: (xy, user, 2 * user + i)
            far = lambda i: (xy, user, 2 * (1 - user) + i)
            if step == 0:
                return near(1 - j) if home else far(1 - j)
            if step == 1:
                return far(j) if home else near(j)
            if step == 2:
                return far(1 - j) if home else near(1 - j)
            return None if home else far(j)

        return [partial(route, step) for step in range(4)]

    def column_out(self, shard):
        return [self.move(shard, route) for route in self.column_routes()]

    def column_back(self, blocks):
        got = []
        for block, route in zip(blocks, self.column_routes()):
            turned = {}
            for xy in range(self.chips):
                for core in range(2):
                    for z in range(self.mp):
                        target = route(xy, core, z)
                        if target is not None:
                            turned[target] = (xy, core, z)
            got.append(self.move(block, lambda xy, core, z: turned.get((xy, core, z))))
        at_home = self.core == self.home
        return add_up(got[0], got[1], got[2], jnp.where(at_home, blocks[3], got[3]))

    def rows_in(self, blocks):
        def route(k, xy, core, z):
            target = (xy, z // 2, 2 * core + (z + k) % 2)
            return None if target == (xy, core, z) else target

        got = [self.move(block, partial(route, k)) for k, block in enumerate(blocks)]
        return jnp.stack([jnp.where(self.core == self.home, blocks[0], got[0]), got[1]])

    def rows_home(self, blocks):
        def route(k, xy, core, z):
            target = (xy, z // 2, 2 * core + (z % 2 - k) % 2)
            return None if target == (xy, core, z) else target

        got = [self.move(block, partial(route, k)) for k, block in enumerate(blocks)]
        got[0] = jnp.where(self.core == self.home, blocks[0], got[0])
        even = self.z % 2 == 0
        both = jnp.stack([jnp.where(even, got[0], got[1]), jnp.where(even, got[1], got[0])])
        return both[:, None].transpose(0, 1, 3, 2)


def norm(hidden):
    center = jnp.mean(hidden, axis=-1, keepdims=True)
    spread = jnp.mean(hidden * hidden, axis=-1, keepdims=True) - center * center
    inverse = lax.rsqrt(spread + 1e-05)
    return (hidden - center) * inverse, inverse


def norm_back(grad, unit, inverse, gain):
    scaled = grad * gain
    first = jnp.mean(scaled, axis=-1, keepdims=True)
    second = jnp.mean(scaled * unit, axis=-1, keepdims=True)
    terms = jnp.concatenate(
        [jnp.sum(grad * unit, axis=0, keepdims=True), jnp.sum(grad, axis=0, keepdims=True)], axis=0
    )
    return inverse * (scaled - first - unit * second), terms


def add_up(*terms):
    total = terms[0].astype(F32)
    for term in terms[1:]:
        total = total + term.astype(F32)
    return total


def input_blocks(hidden, cotangent, terms, numbers, after=()):
    _, width, length = hidden.shape
    total = 2 * width + 32

    def body(numbers_ref, hidden_ref, cot_ref, terms_ref, *outs):
        _, _, z = where_am_i()
        lanes = lax.broadcasted_iota(jnp.int32, (8, length), 1)
        for k in range(2):
            micro = (z + k) % 2
            outs[k][0:width] = hidden_ref[micro]
            outs[k][width : 2 * width] = cot_ref[micro]
            tok, aud = numbers_ref[0, micro], numbers_ref[1, micro]
            row = jnp.where(lanes == 0, tok // 256, jnp.where(lanes == 1, tok % 256, 0))
            row = jnp.where(lanes == 2, aud // 256, jnp.where(lanes == 3, aud % 256, row))
            row = jnp.where(lanes == 4, numbers_ref[2, micro], row)
            wide = jnp.concatenate(
                [terms_ref[...].astype(F32), jnp.zeros((24, length - width), F32)], axis=1
            )
            outs[k][2 * width : total] = jnp.concatenate([wide, row.astype(F32)], axis=0).astype(BF)

    return run(
        body,
        [shaped((total, length))] * 2,
        smem=[numbers],
        vmem=[hidden, cotangent, terms],
        micros=1,
        after=after,
    )


def prepare(own, other, corpus_weights):
    length = own.shape[2]

    def body(
        weights_ref, own_ref, other_ref, hidden_ref, cot_ref, norms_ref, nums_ref, wide, extra, sems
    ):
        core, _, z = where_am_i()
        copies = Copies(sems)
        for k in range(2):
            slot = (z % 2 + k) % 2
            for ref, user in ((own_ref, core), (other_ref, 1 - core)):
                block = 2 * user + slot
                here = pl.ds(pl.multiple_of(block * QUARTER, QUARTER), QUARTER)
                for which in range(2):
                    copies.start(ref.at[k, pl.ds(which * QUARTER, QUARTER)], wide.at[which, here])
                copies.start(ref.at[k, pl.ds(2 * QUARTER, 32)], extra.at[block])
        copies.wait()
        hidden_ref[...] = wide[0].T
        cot_ref[...] = wide[1].T
        parts = [extra[b].astype(F32) for b in range(4)]
        norms_ref[...] = jnp.concatenate(
            [(e[0:8] + e[8:16] + e[16:24])[:, :QUARTER] for e in parts], axis=1
        )
        row = parts[0][24:25]
        tok = 256.0 * row[:, 0:1] + row[:, 1:2]
        aud = 256.0 * row[:, 2:3] + row[:, 3:4]
        weights = weights_ref[...]
        places = lax.broadcasted_iota(jnp.int32, weights.shape, 1).astype(F32)
        weight = jnp.sum(jnp.where(places == row[:, 4:5], weights, 0.0), axis=1, keepdims=True)
        index = lax.broadcasted_iota(jnp.int32, (8, 128), 0)
        nums_ref[...] = jnp.where(index == 0, tok, jnp.where(index == 1, aud, weight))

    return run(
        body,
        [
            shaped((length, D)),
            shaped((length, D)),
            shaped((8, D), F32),
            shaped((8, 128), F32),
        ],
        vmem=[corpus_weights.reshape(1, -1)],
        hbm=[own, other],
        scratch=[pltpu.VMEM((2, D, length), BF), pltpu.VMEM((4, 32, length), BF)],
        copies=12,
        micros=3,
    )


def quarters(value):
    return jnp.concatenate([value[:, p * QUARTER : (p + 1) * QUARTER] for p in range(4)], axis=0)


def attention_shard(blocks, out, after=()):
    rows = blocks.shape[-2]

    def body(blocks_ref, out_in_ref, out_ref):
        last = quarters(out_in_ref[...].astype(F32)).astype(BF)
        first = [blocks_ref[...]] if len(blocks.shape) == 2 else [blocks_ref[j] for j in range(3)]
        out_ref[...] = jnp.concatenate(first + [last], axis=1)

    return run(body, [shaped((rows, D))], vmem=[blocks, out], micros=1, after=after)[0]


def column_slots():
    core, _, z = where_am_i()
    j = z % 2
    home = 1 - jnp.abs(z // 2 - core)
    same = core + (1 - 2 * core) * (1 - home)
    return home == 1, (2 * (1 - j) + same, 2 * j + 1 - same, 2 * (1 - j) + 1 - same, 2 * j + same)


def bring_column(part_refs, own_ref, shards, sems):
    home, slots = column_slots()
    copies = Copies(sems)
    for k in range(3):
        copies.start(part_refs[k], shards.at[slots[k]])

    @pl.when(home)
    def _():
        copy = pltpu.make_async_copy(own_ref, shards.at[slots[3]], sems.at[3])
        copy.start()
        copy.wait()

    @pl.when(jnp.logical_not(home))
    def _():
        copy = pltpu.make_async_copy(part_refs[3], shards.at[slots[3]], sems.at[3])
        copy.start()
        copy.wait()

    copies.wait()


def pack_attention(parts, own):
    rows = own.shape[0]
    few = rows // 4

    def body(*refs):
        part_refs, own_ref, (out_ref, shards, sems) = refs[:4], refs[4], refs[5:]
        bring_column(part_refs, own_ref, shards, sems)
        for cs in range(2):
            low, high = shards[cs], shards[2 + cs]

            def both(at):
                return [low[:, at : at + QUARTER], high[:, at : at + QUARTER]]

            here = pl.ds(cs * rows, rows)
            out_ref[0, here, :] = jnp.concatenate(both(0) + both(QUARTER), axis=1)
            out_ref[1, here, 0:HALF] = jnp.concatenate(both(HALF), axis=1)
        outs = [shards[i, :, 3 * QUARTER :].astype(F32) for i in range(4)]
        stack = []
        for q in range(2):
            for i in range(4):
                left = outs[i][2 * q * few : (2 * q + 1) * few]
                right = outs[i][(2 * q + 1) * few : (2 * q + 2) * few]
                stack.append(jnp.concatenate([left, right], axis=1))
        out_ref[1, :, HALF:D] = jnp.concatenate(stack, axis=0).astype(BF)

    return run(
        body,
        [shaped((2, 2 * rows, D))],
        hbm=list(parts) + [own],
        scratch=[pltpu.VMEM((4, rows, D), BF)],
        copies=4,
        micros=2.5,
    )[0]


def unit_shards(place, fc_in, fc_out):
    rows = fc_in.shape[0]
    both = fc_in.reshape(rows, place.chips, 2, rows).transpose(2, 0, 1, 3).reshape(2, rows, HALF)
    kept = lax.dynamic_index_in_dim(both, place.core, 0, keepdims=False)
    sent = lax.dynamic_index_in_dim(both, 1 - place.core, 0, keepdims=False)
    came = place.swap_core(sent)
    first = place.core == 0
    left = jnp.concatenate([jnp.where(first, kept, came), jnp.where(first, came, kept)])
    return left, fc_out


def gather_units(place, shards):
    left, right = (lax.all_gather(shard, CHIPS, axis=0) for shard in shards)
    if place.fast:
        return [left, right]
    up = left.reshape(place.chips, place.mp, -1, HALF).transpose(0, 2, 1, 3).reshape(D, 2 * D)
    down = right.reshape(place.chips, place.mp, -1, D).transpose(1, 0, 2, 3).reshape(2 * D, D)
    return [up, down]


def scatter_units(place, grads):
    left, right = (
        lax.psum_scatter(grad, CHIPS, scatter_dimension=0, tiled=False) for grad in grads
    )
    rows = right.shape[0]
    kept = lax.dynamic_slice_in_dim(left, place.core * rows, rows, 0)
    sent = lax.dynamic_slice_in_dim(left, (1 - place.core) * rows, rows, 0)
    came = place.swap_core(sent)
    first = place.core == 0
    both = jnp.stack([jnp.where(first, kept, came), jnp.where(first, came, kept)])
    both = both.reshape(2, rows, place.chips, rows).transpose(1, 2, 0, 3).reshape(rows, D)
    return both.astype(F32), right.astype(F32)


def spread(place, own):
    from_x = place.swap_xy(own, 1)
    from_y = place.swap_xy(own, 2)
    far_one = place.swap_xy(from_y[1], 1)
    far_zero = place.swap_xy(from_x[0], 2)
    return [own, from_x, from_y, far_zero, far_one]


def piece_views(refs, which, xy):
    own, from_x, from_y, far_zero, far_one = refs
    return [
        (own.at[which], xy),
        (from_x.at[which], xy ^ 1),
        (from_y.at[which], xy ^ 2),
        ((far_zero, far_one)[which], xy ^ 3),
    ]


def load_wide(copies, refs, which, xy, target, columns=None):
    if len(refs) != 5:
        copies.start(refs[which], target)
        return
    for view, chip in piece_views(refs, which, xy):
        rows = view.shape[0]
        if columns is not None:
            view = view.at[:, pl.ds(0, columns)]
        copies.start(view, target.at[pl.ds(pl.multiple_of(chip * rows, 16), rows)])


def load_out(copies, refs, xy, target):
    if len(refs) != 5:
        copies.start(refs[2], target)
        return
    for view, chip in piece_views(refs, 1, xy):
        rows = view.shape[0] // 4
        for q in range(2):
            for hi in range(2):
                copies.start(
                    view.at[pl.ds((2 * q + hi) * rows, rows), pl.ds(HALF, HALF)],
                    target.at[q, pl.ds(pl.multiple_of(hi * QUARTER + chip * rows, 16), rows)],
                )


def load_up(copies, ref, w_up):
    if len(ref.shape) == 2:
        copies.start(ref, w_up)
        return
    count, rows, _ = ref.shape
    for i in range(count):
        xy, z = i // 4, i % 4
        copies.start(ref.at[i], w_up.at[pl.ds(rows * xy, rows), pl.ds(z * HALF, HALF)])


def load_down(copies, ref, w_down):
    if len(ref.shape) == 2:
        copies.start(ref, w_down)
        return
    count, rows, _ = ref.shape
    for i in range(count):
        xy, z = i // 4, i % 4
        copies.start(ref.at[i], w_down.at[pl.ds(z * HALF + xy * rows, rows)])


ATTENTION_COPIES = 4 + 4 + 16
UNIT_COPIES = 16


def gather_plain(place, shard):
    whole = lax.all_gather(shard, ("mp", "xy", "core"), axis=0)
    whole = whole.reshape((2, 2, place.dp) + shard.shape)
    return lax.dynamic_index_in_dim(whole, place.core, 0, keepdims=False)


def attention_plain(place, shard):
    mine = gather_plain(place, shard)
    rows = shard.shape[0]

    def columns(at, count):
        value = mine[..., at : at + count * QUARTER].reshape(2, D, count, QUARTER)
        return value.transpose(1, 2, 0, 3).reshape(D, count * HALF)

    out = mine[..., 3 * QUARTER :].reshape(2, place.dp, 2, 2, rows // 4, QUARTER)
    out = out.transpose(2, 0, 1, 4, 3, 5).reshape(2, HALF, HALF)
    return [columns(0, 2), columns(HALF, 1), out]


def head_rows(h):
    return pl.ds(pl.multiple_of(h * HEAD_DIM, HEAD_DIM), HEAD_DIM)


def low_parts(value):
    parts = []
    for _ in range(3):
        part = value.astype(BF)
        parts.append(part)
        value = value - part.astype(F32)
    return parts


def widened(count):
    return lambda rows: (
        lax.broadcasted_iota(jnp.int32, (rows, HEAD_DIM), 1) < count
    ).astype(F32).astype(BF)


def below(head, rows):
    blank = jnp.zeros((HEAD_DIM - len(rows), head.shape[1]), F32)
    rest = jnp.concatenate([row.astype(F32) for row in rows] + [blank], axis=0)
    return jnp.concatenate([head, rest.astype(BF)], axis=0)


def project(left, pair_ref):
    return jnp.concatenate([mm(left, pair_ref[0]), mm(left, pair_ref[1])], axis=1)


def project_t(left, pair_ref):
    return mm_t(left[:, :HALF], pair_ref[0]) + mm_t(left[:, HALF:], pair_ref[1])


def self_forward(hidden, norms, nums, weights, after=()):
    length = hidden.shape[0]

    def body(hidden_ref, norms_ref, nums_ref, *refs):
        w_refs, refs = refs[: len(weights)], refs[len(weights) :]
        part_ref, at_ref, qkv_ref, qt_ref, kt_ref, ot_ref, lse_ref = refs[:7]
        w_qk, w_v, w_out, vt, heads, bias, sems = refs[7:]
        _, xy, _ = where_am_i()
        copies = Copies(sems)
        load_wide(copies, w_refs, 0, xy, w_qk)
        load_wide(copies, w_refs, 1, xy, w_v, HALF)
        load_out(copies, w_refs, xy, w_out)
        unit, _ = norm(hidden_ref[...].astype(F32))
        a = (unit * norms_ref[0:1] + norms_ref[4:5]).astype(BF)
        at_ref[...] = a.T
        keys = lax.broadcasted_iota(jnp.int32, (length, length), 0)
        queries = lax.broadcasted_iota(jnp.int32, (length, length), 1)
        allowed = (keys <= queries) & (keys.astype(F32) < nums_ref[0:1, 0:1])
        bias[...] = jnp.where(allowed, 0.0, -1e30)
        copies.wait()
        qk = mm(a, w_qk[...])
        q = (qk[:, :HALF].astype(BF).astype(F32) * HEAD_DIM ** (-0.5)).astype(BF)
        k = qk[:, HALF:].astype(BF)
        v = mm(a, w_v[...]).astype(BF)
        qkv_ref[:, 0:HALF] = q
        qkv_ref[:, HALF : 2 * HALF] = k
        qkv_ref[:, 2 * HALF :] = v
        qt_ref[...] = q.T
        kt_ref[...] = k.T
        vt[...] = v.T
        for h in range(HEADS):
            heads[h] = k[:, h * HEAD_DIM : (h + 1) * HEAD_DIM]

        def head(h, carry):
            s = mm(heads[h], qt_ref[head_rows(h), :]) + bias[...]
            top = jnp.max(s, axis=0, keepdims=True)
            p = jnp.exp(s - top)
            total = jnp.sum(p, axis=0, keepdims=True)
            o = mm(vt[head_rows(h), :], p.astype(BF))
            ot_ref[head_rows(h), :] = (o / total).astype(BF)
            lse_ref[h] = top + jnp.log(total)
            return carry

        lax.fori_loop(0, HEADS, head, 0)
        part_ref[...] = project(ot_ref[...].T, w_out).astype(BF)

    return run(
        body,
        [
            shaped((length, D)),
            shaped((D, length)),
            shaped((length, 3 * HALF)),
            shaped((HALF, length)),
            shaped((HALF, length)),
            shaped((HALF, length)),
            shaped((HEADS, 1, length), F32),
        ],
        vmem=[hidden, norms, nums],
        hbm=weights,
        scratch=[
            pltpu.VMEM((D, D), BF),
            pltpu.VMEM((D, HALF), BF),
            pltpu.VMEM((2, HALF, HALF), BF),
            pltpu.VMEM((HALF, length), BF),
            pltpu.VMEM((HEADS, length, HEAD_DIM), BF),
            pltpu.VMEM((length, length), F32),
        ],
        copies=ATTENTION_COPIES,
        micros=10,
        after=after,
    )


def turn(value, after=()):
    rows, columns = value.shape

    def body(ref, out_ref):
        for at in range(0, rows, CHUNK):
            out_ref[:, at : at + CHUNK] = ref[at : at + CHUNK, :].T

    return run(body, [shaped((columns, rows))], vmem=[value], micros=4, after=after)[0]


def cross_memory(encoded, weights):
    frames = encoded.shape[0]

    def body(enc_ref, *refs):
        w_refs, refs = refs[: len(weights)], refs[len(weights) :]
        kv_ref, kvt_ref, w_kv, sems = refs
        _, xy, _ = where_am_i()
        copies = Copies(sems)
        load_wide(copies, w_refs, 0, xy, w_kv)
        copies.wait()

        def step(i, carry):
            here = pl.ds(pl.multiple_of(i * CHUNK, CHUNK), CHUNK)
            kv = mm(enc_ref[here, :], w_kv[...]).astype(BF)
            kv_ref[here, :] = kv
            kvt_ref[:, here] = kv.T
            return carry

        lax.fori_loop(0, frames // CHUNK, step, 0)

    return run(
        body,
        [shaped((frames, D)), shaped((D, frames))],
        vmem=[encoded],
        hbm=weights,
        scratch=[pltpu.VMEM((D, D), BF)],
        copies=4,
        micros=6,
    )


def residual(hidden_ref, mine_ref, other_ref):
    return hidden_ref[...].astype(F32) + (mine_ref[...].astype(F32) + other_ref[...].astype(F32))


def cross_forward(hidden, mine, other, norms, nums, kv, kvt, weights):
    length = hidden.shape[0]
    frames = kv.shape[0]

    def body(hidden_ref, mine_ref, other_ref, norms_ref, nums_ref, kv_ref, kvt_ref, *refs):
        w_refs, refs = refs[: len(weights)], refs[len(weights) :]
        part_ref, h_ref, ct_ref, q_ref, qt_ref, ot_ref, lse_ref = refs[:7]
        w_q, w_out, heads, values_t, sems = refs[7:]
        _, xy, _ = where_am_i()
        copies = Copies(sems)
        load_wide(copies, w_refs, 1, xy, w_q, HALF)
        load_out(copies, w_refs, xy, w_out)
        h1 = residual(hidden_ref, mine_ref, other_ref)
        h_ref[...] = h1
        unit, _ = norm(h1)
        c = (unit * norms_ref[1:2] + norms_ref[5:6]).astype(BF)
        ct_ref[...] = c.T
        frame = lax.broadcasted_iota(jnp.int32, (frames, HEAD_DIM), 0).astype(F32)
        lane = lax.broadcasted_iota(jnp.int32, (frames, HEAD_DIM), 1)
        mask = jnp.where(frame < nums_ref[1:2, 0:1], 0.0, -1e30)
        beside = jnp.where(lane == 0, mask, jnp.where(lane == 1, 1.0, 0.0)).astype(BF)
        one = lax.broadcasted_iota(jnp.int32, (16, frames), 0)
        one = jnp.where(one == 0, 1.0, 0.0).astype(BF)
        for h in range(HEADS):
            keys = kv_ref[:, h * HEAD_DIM : (h + 1) * HEAD_DIM]
            heads[h] = jnp.concatenate([keys, beside], axis=1)
            values = kvt_ref[HALF + h * HEAD_DIM : HALF + (h + 1) * HEAD_DIM, :]
            values_t[h] = jnp.concatenate([values, one], axis=0)
        copies.wait()
        q = mm(c, w_q[...]).astype(BF)
        q = (q.astype(F32) * HEAD_DIM ** (-0.5)).astype(BF)
        q_ref[...] = q
        qt_ref[...] = q.T
        ones = jnp.ones((1, length), F32)

        def head(pair, carry):
            for h in (2 * pair, 2 * pair + 1):
                qt = qt_ref[head_rows(h), :]
                plain = below(qt, [ones])
                top = None
                for at in range(0, frames, CHUNK):
                    s = mm(heads[h, at : at + CHUNK], plain)
                    high = jnp.max(s, axis=0, keepdims=True)
                    top = high if top is None else jnp.maximum(top, high)
                top = top.astype(BF).astype(F32)
                lowered = below(qt, [ones, -top])
                o = None
                for at in range(0, frames, CHUNK):
                    p = jnp.exp(mm(heads[h, at : at + CHUNK], lowered)).astype(BF)
                    more = mm(values_t[h, :, at : at + CHUNK], p)
                    o = more if o is None else o + more
                total = o[HEAD_DIM : HEAD_DIM + 1]
                ot_ref[head_rows(h), :] = (o[:HEAD_DIM] / total).astype(BF)
                lse_ref[h] = top + jnp.log(total)
            return carry

        lax.fori_loop(0, HEADS // 2, head, 0)
        part_ref[...] = project(ot_ref[...].T, w_out).astype(BF)

    return run(
        body,
        [
            shaped((length, D)),
            shaped((length, D), F32),
            shaped((D, length)),
            shaped((length, HALF)),
            shaped((HALF, length)),
            shaped((HALF, length)),
            shaped((HEADS, 1, length), F32),
        ],
        vmem=[hidden, mine, other, norms, nums, kv, kvt],
        hbm=weights,
        scratch=[
            pltpu.VMEM((D, HALF), BF),
            pltpu.VMEM((2, HALF, HALF), BF),
            pltpu.VMEM((HEADS, frames, 2 * HEAD_DIM), BF),
            pltpu.VMEM((HEADS, HEAD_DIM + 16, frames), BF),
        ],
        copies=4 + 16,
        micros=10,
    )


def units_forward(hidden, mine, other, norms, weights):
    length = hidden.shape[0]

    def body(hidden_ref, mine_ref, other_ref, norms_ref, *refs):
        w_refs, refs = refs[: len(weights)], refs[len(weights) :]
        part_ref, h_ref, mt_ref, slope_ref, it_ref = refs[:5]
        w_up, w_down, inner, late_sems, sems = refs[5:]
        _, xy, _ = where_am_i()
        copies = Copies(sems)
        load_up(copies, w_refs[0], w_up)
        late = Copies(late_sems)
        load_down(late, w_refs[1], w_down)
        h2 = residual(hidden_ref, mine_ref, other_ref)
        h_ref[...] = h2
        unit, _ = norm(h2)
        m = (unit * norms_ref[2:3] + norms_ref[6:7]).astype(BF)
        mt_ref[...] = m.T
        copies.wait()
        for at in range(0, 2 * D, CHUNK):
            here = slice(at, at + CHUNK)
            z = mm(m, w_up[:, here])
            share = 0.5 * (1.0 + lax.erf(z * 0.7071067811865476))
            slope = share + z * (0.3989422804014327 * jnp.exp(-0.5 * z * z))
            value = (z * share).astype(BF)
            inner[:, here] = value
            it_ref[here, :] = value.T
            slope_ref[:, here] = slope.astype(BF)
        late.wait()
        for at in range(0, D, CHUNK):
            part_ref[:, at : at + CHUNK] = mm(inner[...], w_down[:, at : at + CHUNK]).astype(BF)

    return run(
        body,
        [
            shaped((length, D)),
            shaped((length, D), F32),
            shaped((D, length)),
            shaped((length, 2 * D)),
            shaped((2 * D, length)),
        ],
        vmem=[hidden, mine, other, norms],
        hbm=weights,
        scratch=[
            pltpu.VMEM((D, 2 * D), BF),
            pltpu.VMEM((2 * D, D), BF),
            pltpu.VMEM((length, 2 * D), BF),
            pltpu.SemaphoreType.DMA((UNIT_COPIES,)),
        ],
        copies=UNIT_COPIES,
        micros=9,
    )


def store_blocks(value, blocks, first_ref, second_ref):
    core, _, z = where_am_i()
    for b in range(4):
        blocks[b] = value[:, b * QUARTER : (b + 1) * QUARTER]
    first_ref[...] = blocks[2 * core + z % 2].T
    second_ref[...] = blocks[2 * core + (z + 1) % 2].T


def units_backward(hidden, mine, other, norms, nums, cot, slope, weights):
    length = hidden.shape[0]

    def body(hidden_ref, mine_ref, other_ref, norms_ref, nums_ref, cot_ref, slope_ref, *refs):
        w_refs, refs = refs[: len(weights)], refs[len(weights) :]
        part_ref, d_ref, e_ref, dz_ref, terms_ref, first_ref, second_ref = refs[:7]
        w_up, w_down, blocks, late_sems, sems = refs[7:]
        _, xy, _ = where_am_i()
        copies = Copies(sems)
        load_down(copies, w_refs[1], w_down)
        late = Copies(late_sems)
        load_up(late, w_refs[0], w_up)
        unit, inverse = norm(residual(hidden_ref, mine_ref, other_ref))
        final = (unit * norms_ref[3:4] + norms_ref[7:8]).astype(BF)
        store_blocks(final, blocks, first_ref, second_ref)
        live = lax.broadcasted_iota(jnp.int32, (length, 1), 0).astype(F32) < nums_ref[0:1, 0:1]
        grad = cot_ref[...].astype(F32) * jnp.where(live, nums_ref[2:3, 0:1], 0.0)
        d3, terms = norm_back(grad, unit, inverse, norms_ref[3:4])
        d_ref[...] = d3
        terms_ref[...] = terms
        e = d3.astype(BF)
        e_ref[...] = e
        copies.wait()
        for at in range(0, 2 * D, CHUNK):
            here = slice(at, at + CHUNK)
            d_inner = mm_t(e, w_down[here, :])
            dz_ref[:, here] = (slope_ref[:, here].astype(F32) * d_inner).astype(BF)
        late.wait()
        for at in range(0, D, CHUNK):
            out = mm_t(dz_ref[...], w_up[at : at + CHUNK, :])
            part_ref[:, at : at + CHUNK] = out.astype(BF)

    return run(
        body,
        [
            shaped((length, D)),
            shaped((length, D), F32),
            shaped((length, D)),
            shaped((length, 2 * D)),
            shaped((2, D), F32),
            shaped((QUARTER, length)),
            shaped((QUARTER, length)),
        ],
        vmem=[hidden, mine, other, norms, nums, cot, slope],
        hbm=weights,
        scratch=[
            pltpu.VMEM((D, 2 * D), BF),
            pltpu.VMEM((2 * D, D), BF),
            pltpu.VMEM((4, length, QUARTER), BF),
            pltpu.SemaphoreType.DMA((UNIT_COPIES,)),
        ],
        copies=UNIT_COPIES,
        micros=10,
    )


def step_back(d_ref, hidden_ref, mine_ref, other_ref, gain):
    unit, inverse = norm(hidden_ref[...].astype(F32))
    grad = mine_ref[...].astype(F32) + other_ref[...].astype(F32)
    part, terms = norm_back(grad, unit, inverse, gain)
    return d_ref[...] + part, terms


def cross_backward(d, hidden, mine, other, norms, nums, kv, kvt, q, qt, ot, lse, weights):
    length = hidden.shape[0]
    frames = kv.shape[0]

    def body(
        d_ref, hidden_ref, mine_ref, other_ref, norms_ref, nums_ref, kv_ref, kvt_ref, q_ref,
        qt_ref, ot_ref, lse_ref, *refs
    ):
        w_refs, refs = refs[: len(weights)], refs[len(weights) :]
        part_ref, d_out_ref, e_ref, dq_ref, dkv_ref, terms_ref = refs[:6]
        w_q, w_out, keys, values, queries, grads, dot_t, dk_h, dv_h, dqt, sems = refs[6:]
        _, xy, _ = where_am_i()
        copies = Copies(sems)
        load_wide(copies, w_refs, 1, xy, w_q, HALF)
        load_out(copies, w_refs, xy, w_out)
        d2, terms = step_back(d_ref, hidden_ref, mine_ref, other_ref, norms_ref[2:3])
        d_out_ref[...] = d2
        terms_ref[...] = terms
        e = d2.astype(BF)
        e_ref[...] = e
        frame = lax.broadcasted_iota(jnp.int32, (frames, HEAD_DIM), 0).astype(F32)
        lane = lax.broadcasted_iota(jnp.int32, (frames, HEAD_DIM), 1)
        mask = jnp.where(frame < nums_ref[1:2, 0:1], 0.0, -1e30)
        beside = jnp.where(lane == 0, mask, jnp.where(lane < 4, 1.0, 0.0)).astype(BF)
        three = widened(3)(frames)
        for h in range(HEADS):
            lanes = slice(h * HEAD_DIM, (h + 1) * HEAD_DIM)
            keys[h] = jnp.concatenate([kv_ref[:, lanes], beside], axis=1)
            value = kv_ref[:, HALF + h * HEAD_DIM : HALF + (h + 1) * HEAD_DIM]
            values[h] = jnp.concatenate([value, three], axis=1)
            queries[h] = q_ref[:, lanes]
        copies.wait()
        d_mixed = project_t(e, w_out).astype(BF)
        dot_t[...] = d_mixed.T
        for h in range(HEADS):
            grads[h] = d_mixed[:, h * HEAD_DIM : (h + 1) * HEAD_DIM]
        ones = jnp.ones((1, length), F32)

        def head(h, carry):
            rows = head_rows(h)
            do_t = dot_t[rows, :]
            q_n, do_n = queries[h], grads[h]
            delta = jnp.sum(do_t.astype(F32) * ot_ref[rows, :].astype(F32), axis=0, keepdims=True)
            q_t = below(qt_ref[rows, :], [ones] + low_parts(-lse_ref[h]))
            do_t = below(do_t, low_parts(-delta))
            total = None
            for at in range(0, frames, CHUNK):
                here = slice(at, at + CHUNK)
                p = jnp.exp(mm(keys[h, here], q_t))
                ds = (p * mm(values[h, here], do_t)).astype(BF)
                dv_h[h, here] = mm(p.astype(BF), do_n).astype(BF)
                dk_h[h, here] = mm(ds, q_n).astype(BF)
                more = mm(kvt_ref[rows, here], ds)
                total = more if total is None else total + more
            dqt[rows, :] = (total * HEAD_DIM ** (-0.5)).astype(BF)
            return carry

        lax.fori_loop(0, HEADS, head, 0)
        dq = dqt[...].T
        dq_ref[...] = dq
        part_ref[...] = mm_t(dq, w_q[...]).astype(BF)
        for h in range(HEADS):
            lanes = slice(h * HEAD_DIM, (h + 1) * HEAD_DIM)
            dkv_ref[:, lanes] = dk_h[h]
            dkv_ref[:, HALF + h * HEAD_DIM : HALF + (h + 1) * HEAD_DIM] = dv_h[h]

    return run(
        body,
        [
            shaped((length, D)),
            shaped((length, D), F32),
            shaped((length, D)),
            shaped((length, HALF)),
            shaped((frames, D)),
            shaped((2, D), F32),
        ],
        vmem=[d, hidden, mine, other, norms, nums, kv, kvt, q, qt, ot, lse],
        hbm=weights,
        scratch=[
            pltpu.VMEM((D, HALF), BF),
            pltpu.VMEM((2, HALF, HALF), BF),
            pltpu.VMEM((HEADS, frames, 2 * HEAD_DIM), BF),
            pltpu.VMEM((HEADS, frames, 2 * HEAD_DIM), BF),
            pltpu.VMEM((HEADS, length, HEAD_DIM), BF),
            pltpu.VMEM((HEADS, length, HEAD_DIM), BF),
            pltpu.VMEM((HALF, length), BF),
            pltpu.VMEM((HEADS, frames, HEAD_DIM), BF),
            pltpu.VMEM((HEADS, frames, HEAD_DIM), BF),
            pltpu.VMEM((HALF, length), BF),
        ],
        copies=4 + 16,
        micros=16,
    )


def self_backward(d, hidden, mine, other, norms, nums, qkv, qt, kt, ot, lse, weights, after=()):
    length = hidden.shape[0]

    def body(
        d_ref, hidden_ref, mine_ref, other_ref, norms_ref, nums_ref, qkv_ref, qt_ref, kt_ref,
        ot_ref, lse_ref, *refs
    ):
        w_refs, refs = refs[: len(weights)], refs[len(weights) :]
        part_ref, d_out_ref, e_ref, dqk_ref, dv_ref, terms_ref = refs[:6]
        w_qk, w_v, w_out, queries_h, keys, values, grads, dot_t, dk_h, dv_h, dqt, bias, sems = refs[6:]
        _, xy, _ = where_am_i()
        copies = Copies(sems)
        load_out(copies, w_refs, xy, w_out)
        load_wide(copies, w_refs, 0, xy, w_qk)
        load_wide(copies, w_refs, 1, xy, w_v, HALF)
        d1, terms = step_back(d_ref, hidden_ref, mine_ref, other_ref, norms_ref[1:2])
        d_out_ref[...] = d1
        terms_ref[...] = terms
        e = d1.astype(BF)
        e_ref[...] = e
        places = lax.broadcasted_iota(jnp.int32, (length, length), 0)
        queries = lax.broadcasted_iota(jnp.int32, (length, length), 1)
        allowed = (places <= queries) & (places.astype(F32) < nums_ref[0:1, 0:1])
        bias[...] = jnp.where(allowed, 0.0, -1e30)
        three = widened(3)(length)
        for h in range(HEADS):
            at = h * HEAD_DIM
            queries_h[h] = qkv_ref[:, at : at + HEAD_DIM]
            key = qkv_ref[:, HALF + at : HALF + at + HEAD_DIM]
            keys[h] = jnp.concatenate([key, three], axis=1)
            value = qkv_ref[:, 2 * HALF + at : 2 * HALF + at + HEAD_DIM]
            values[h] = jnp.concatenate([value, three], axis=1)
        copies.wait()
        d_mixed = project_t(e, w_out).astype(BF)
        dot_t[...] = d_mixed.T
        for h in range(HEADS):
            grads[h] = d_mixed[:, h * HEAD_DIM : (h + 1) * HEAD_DIM]

        def head(h, carry):
            rows = head_rows(h)
            do_t, do_n = dot_t[rows, :], grads[h]
            delta = jnp.sum(do_t.astype(F32) * ot_ref[rows, :].astype(F32), axis=0, keepdims=True)
            q_t = below(qt_ref[rows, :], low_parts(-lse_ref[h]))
            do_t = below(do_t, low_parts(-delta))
            p = jnp.exp(mm(keys[h], q_t) + bias[...])
            ds = (p * mm(values[h], do_t)).astype(BF)
            dv_h[h] = mm(p.astype(BF), do_n).astype(BF)
            dk_h[h] = mm(ds, queries_h[h]).astype(BF)
            dqt[rows, :] = (mm(kt_ref[rows, :], ds) * HEAD_DIM ** (-0.5)).astype(BF)
            return carry

        lax.fori_loop(0, HEADS, head, 0)
        dqk_ref[:, 0:HALF] = dqt[...].T
        for h in range(HEADS):
            lanes = slice(HALF + h * HEAD_DIM, HALF + (h + 1) * HEAD_DIM)
            dqk_ref[:, lanes] = dk_h[h]
            dv_ref[:, h * HEAD_DIM : (h + 1) * HEAD_DIM] = dv_h[h]
        out = mm_t(dqk_ref[...], w_qk[...]) + mm_t(dv_ref[...], w_v[...])
        part_ref[...] = out.astype(BF)

    return run(
        body,
        [
            shaped((length, D)),
            shaped((length, D), F32),
            shaped((length, D)),
            shaped((length, D)),
            shaped((length, HALF)),
            shaped((2, D), F32),
        ],
        vmem=[d, hidden, mine, other, norms, nums, qkv, qt, kt, ot, lse],
        hbm=weights,
        scratch=[
            pltpu.VMEM((D, D), BF),
            pltpu.VMEM((D, HALF), BF),
            pltpu.VMEM((2, HALF, HALF), BF),
            pltpu.VMEM((HEADS, length, HEAD_DIM), BF),
            pltpu.VMEM((HEADS, length, 2 * HEAD_DIM), BF),
            pltpu.VMEM((HEADS, length, 2 * HEAD_DIM), BF),
            pltpu.VMEM((HEADS, length, HEAD_DIM), BF),
            pltpu.VMEM((HALF, length), BF),
            pltpu.VMEM((HEADS, length, HEAD_DIM), BF),
            pltpu.VMEM((HEADS, length, HEAD_DIM), BF),
            pltpu.VMEM((HALF, length), BF),
            pltpu.VMEM((length, length), F32),
        ],
        copies=ATTENTION_COPIES,
        micros=12,
        after=after,
    )


def finish_hidden(d, hidden, mine, other, norms, terms1, terms2, terms3):
    length = hidden.shape[0]

    def body(
        d_ref, hidden_ref, mine_ref, other_ref, norms_ref, one, two, three, terms_ref, first_ref,
        second_ref, blocks
    ):
        d0, terms = step_back(d_ref, hidden_ref, mine_ref, other_ref, norms_ref[0:1])
        store_blocks(d0.astype(BF), blocks, first_ref, second_ref)
        for j in range(2):
            here = slice(j, j + 1)
            terms_ref[4 * j : 4 * j + 4] = jnp.concatenate(
                [terms[here], one[here], two[here], three[here]], axis=0
            )

    return run(
        body,
        [shaped((8, D), F32), shaped((QUARTER, length)), shaped((QUARTER, length))],
        vmem=[d, hidden, mine, other, norms, terms1, terms2, terms3],
        scratch=[pltpu.VMEM((4, length, QUARTER), BF)],
        micros=4,
    )


def finish_encoder(keep, other, frames):
    def body(keep_ref, other_ref, first_ref, second_ref):
        _, _, z = where_am_i()
        for ref, k in ((first_ref, 0), (second_ref, 1)):
            here = pl.ds(pl.multiple_of(((z + k) % 2) * QUARTER, QUARTER), QUARTER)
            total = keep_ref[here, :].astype(F32) + other_ref[here, :].astype(F32)
            ref[...] = total.astype(BF)[:, :frames]

    return run(
        body,
        [shaped((QUARTER, frames)), shaped((QUARTER, frames))],
        vmem=[keep, other],
        micros=2,
    )


def block_plan(place):
    if not place.fast:
        return 1, (((1, 0, 0),), ((1, 0, 0),))
    first = ((1, 0, 0), (0, 0, 1), (1, 1, 2), (0, 1, 3))
    second = ((1, 0, 0), (1, 1, 1), (0, 0, 2), (0, 1, 3))
    return 4, (first, second)


def grad_outputs(place, shape):
    if place.fast:
        return [shaped((2,) + shape)] * 4
    return [shaped((1,) + shape)] * 4


def units_grads(place, mt, dz, it, e):
    chips = place.chips
    rows = D // (2 * chips)

    def body(mt_ref, dz_ref, it_ref, e_ref, up_ref, down_ref):
        for xy in range(chips):
            for z in range(4):
                at = z * HALF + xy * rows
                right = mm(it_ref[at : at + rows, :], e_ref[...])
                down_ref[4 * xy + z] = right.astype(BF)
        for xy in range(chips):
            left = mm(mt_ref[2 * rows * xy : 2 * rows * (xy + 1), :], dz_ref[...]).astype(BF)
            for z in range(4):
                up_ref[4 * xy + z] = left[:, z * HALF : (z + 1) * HALF]

    def plain(mt_ref, dz_ref, it_ref, e_ref, left_ref, right_ref):
        left_ref[...] = mm(mt_ref[...], dz_ref[...]).astype(BF)
        right_ref[...] = mm(it_ref[...], e_ref[...]).astype(BF)

    if place.fast:
        return run(
            body,
            [shaped((4 * chips, 2 * rows, HALF)), shaped((4 * chips, rows, D))],
            vmem=[mt, dz, it, e],
            micros=7,
        )
    left, right = run(
        plain, [shaped((D, 2 * D)), shaped((2 * D, D))], vmem=[mt, dz, it, e], micros=7
    )
    left = left.reshape(chips, 2 * rows, 4, HALF).transpose(0, 2, 1, 3)
    right = right.reshape(4, chips, rows, D).transpose(1, 0, 2, 3)
    return left.reshape(4 * chips, 2 * rows, HALF), right.reshape(4 * chips, rows, D)


def attention_grads(place, wide_left, wide_right, left, right, ot, e, after=()):
    count, plan = block_plan(place)
    rows = D // count
    few = rows // 4

    def body(wide_left_ref, wide_right_ref, left_ref, right_ref, ot_ref, e_ref, *outs):
        _, xy, _ = where_am_i()
        for output, slot, offset in plan[0]:
            chip = xy ^ offset if count > 1 else 0
            here = pl.ds(pl.multiple_of(chip * rows, 16), rows)
            outs[output][slot] = mm(wide_left_ref[here, :], wide_right_ref[...]).astype(BF)
        for output, slot, offset in plan[1]:
            chip = xy ^ offset if count > 1 else 0
            here = pl.ds(pl.multiple_of(chip * rows, 16), rows)
            target = outs[2 + output]
            target[slot, :, 0:HALF] = mm(left_ref[here, :], right_ref[...]).astype(BF)
            for hi in range(2):
                here = pl.ds(pl.multiple_of(hi * QUARTER + chip * few, 16), few)
                both = mm(ot_ref[here, :], e_ref[...]).astype(BF)
                for q in range(2):
                    at = (2 * q + hi) * few
                    target[slot, at : at + few, HALF:D] = both[:, q * HALF : (q + 1) * HALF]

    return run(
        body,
        grad_outputs(place, (rows, D)),
        vmem=[wide_left, wide_right, left, right, ot, e],
        micros=6,
        after=after,
    )


def encoder_grad(dkv, weights):
    padded = dkv.shape[0]

    def body(dkv_ref, *refs):
        w_refs, (keep_ref, send_ref, w_kv, sems) = refs[: len(weights)], refs[len(weights) :]
        core, xy, _ = where_am_i()
        copies = Copies(sems)
        load_wide(copies, w_refs, 0, xy, w_kv)
        copies.wait()
        mine = pl.ds(pl.multiple_of(core * HALF, HALF), HALF)
        theirs = pl.ds(pl.multiple_of((1 - core) * HALF, HALF), HALF)
        for ref, rows in ((send_ref, theirs), (keep_ref, mine)):
            for at in range(0, padded, CHUNK):
                value = mm_t(w_kv[rows, :], dkv_ref[at : at + CHUNK, :])
                ref[:, at : at + CHUNK] = value.astype(BF)

    return run(
        body,
        [shaped((HALF, padded)), shaped((HALF, padded))],
        vmem=[dkv],
        hbm=weights,
        scratch=[pltpu.VMEM((D, D), BF)],
        copies=4,
        micros=4,
    )


def leave_plane(place, grads):
    return [place.swap_xy(grads[0], 1), place.swap_xy(grads[2], 2)]


def pass_on(grads, came, after):
    shape = grads[1].shape[1:]

    def body(stay0, came0, stay1, came1, *refs):
        out0, out1, held, sems = refs[-4:]
        copies = Copies(sems)
        for i, ref in enumerate((stay0, came0, stay1, came1)):
            copies.start(ref.at[1], held.at[i])
        copies.wait()
        out0[...] = add_up(held[0], held[1]).astype(BF)
        out1[...] = add_up(held[2], held[3]).astype(BF)

    return run(
        body,
        [shaped(shape), shaped(shape)],
        hbm=[grads[1], came[0], grads[3], came[1]],
        scratch=[pltpu.VMEM((4,) + shape, BF)],
        copies=4,
        micros=2,
        after=after,
    )


def cross_plane(place, onward):
    return [place.swap_xy(onward[0], 2), place.swap_xy(onward[1], 1)]


def column_blocks(grads, came, onward, attention, norm_terms=(), after=()):
    shape = onward[0].shape
    rows = shape[-2] // 2
    width = D if attention else 2 * D
    few = rows // 4
    extra = 16 if norm_terms else 0

    def body(*refs):
        terms_refs, refs = refs[: len(norm_terms)], refs[len(norm_terms) :]
        ins, outs, (held, shards, sems) = refs[:6], refs[-7:-3], refs[-3:]
        home, slots = column_slots()
        copies = Copies(sems)
        for i, ref in enumerate(ins):
            copies.start(ref if i % 3 == 2 else ref.at[0], held.at[i])
        copies.wait()
        sums = [add_up(held[3 * part], held[3 * part + 1], held[3 * part + 2]) for part in range(2)]
        for hi in range(2):
            for cs in range(2):
                here = slice(cs * rows, (cs + 1) * rows)
                if attention:
                    lanes = slice(hi * QUARTER, (hi + 1) * QUARTER)
                    lanes_two = slice(HALF + hi * QUARTER, HALF + (hi + 1) * QUARTER)
                    outs_rows = []
                    for p in range(4):
                        at = (2 * (p // 2) + hi) * 2 * few + cs * few
                        side = HALF + (p % 2) * QUARTER
                        outs_rows.append(sums[1][at : at + few, side : side + QUARTER])
                    value = jnp.concatenate(
                        [
                            sums[0][here, lanes],
                            sums[0][here, lanes_two],
                            sums[1][here, lanes],
                            jnp.concatenate(outs_rows, axis=0),
                        ],
                        axis=1,
                    )
                else:
                    value = jnp.concatenate([sums[0][hi, here], sums[1][hi, here]], axis=1)
                shards[2 * hi + cs, :rows] = value.astype(BF)
        if norm_terms:
            core, xy, _ = where_am_i()
            terms = add_up(*[ref[...] for ref in terms_refs])
            terms = jnp.concatenate([terms, jnp.zeros_like(terms)], axis=0).astype(BF)
            feature = lax.broadcasted_iota(jnp.int32, (D, D), 0)
            lane = lax.broadcasted_iota(jnp.int32, (D, D), 1)
            for hi in range(2):
                for cs in range(2):
                    offset = (2 * core + hi) * QUARTER + (2 * xy + cs) * few
                    pick = jnp.where((feature == lane + offset) & (lane < few), 1.0, 0.0)
                    shards[2 * hi + cs, rows:] = mm(terms, pick.astype(BF)).astype(BF)
        for k in range(4):
            outs[k][...] = shards[slots[k]]

    ins = [grads[1], came[0], onward[0], grads[3], came[1], onward[1]]
    return run(
        body,
        [shaped((rows + extra, width))] * 4,
        vmem=list(norm_terms),
        hbm=ins,
        after=after,
        scratch=[pltpu.VMEM((6,) + shape, BF), pltpu.VMEM((4, rows + extra, width), BF)],
        copies=6,
        micros=4,
    )


def sum_plain(place, grads, attention):
    wide, narrow = grads[1][0], grads[3][0]
    rows = D // place.dp
    if attention:
        value = jnp.stack([wide[:, :HALF], wide[:, HALF:], narrow[:, :HALF]], axis=1)
        value = value.reshape(place.dp, rows, 3, 2, QUARTER).transpose(3, 0, 1, 2, 4)
        value = value.reshape(2, place.dp, rows, 3 * QUARTER)
        outs = narrow[:, HALF:].reshape(2, 2, place.dp, rows // 4, 2, QUARTER)
        outs = outs.transpose(1, 2, 0, 4, 3, 5).reshape(2, place.dp, rows, QUARTER)
        value = jnp.concatenate([value, outs], axis=-1)
    else:
        value = jnp.concatenate(
            [wide.reshape(2, place.dp, rows, D), narrow.reshape(2, place.dp, rows, D)], axis=-1
        )
    whole = jnp.zeros((2,) + value.shape, F32)
    whole = lax.dynamic_update_index_in_dim(whole, value.astype(F32), place.core, 0)
    whole = whole.reshape((4 * place.dp,) + value.shape[2:])
    return lax.psum_scatter(whole, ("mp", "xy", "core"), scatter_dimension=0, tiled=False)


def from_quarters(value):
    few = value.shape[0] // 4
    return value.reshape(4, few, QUARTER).transpose(1, 0, 2).reshape(few, D)


def three_parts(value):
    terms = []
    for _ in range(3):
        term = lax.reduce_precision(value, 8, 7)
        terms.append(term.astype(BF))
        value = value - term
    return jnp.concatenate(terms)


def per_device(
    dp,
    mp,
    hidden_in,
    encoder_states,
    cotangent,
    self_qkv,
    self_out,
    cross_q,
    cross_kv,
    cross_out,
    fc_in,
    fc_out,
    ln_gain,
    ln_bias,
    token_lengths,
    audio_lengths,
    corpus_ids,
    corpus_weights,
):
    place = Place(dp, mp)
    length = hidden_in.shape[2]
    frames = encoder_states.shape[2]
    padded = -(-frames // CHUNK) * CHUNK
    rows = self_qkv.shape[0]

    w_units = gather_units(place, unit_shards(place, fc_in, fc_out))
    first = ()
    if place.fast:
        shard = attention_shard(self_qkv.transpose(1, 0, 2), self_out)
        first = (shard,)
        packed = pack_attention(place.column_out(shard), shard)
        w_self = spread(place, packed)
        encoder_states, packed = lax.optimization_barrier((encoder_states, packed))
        shard = attention_shard(
            jnp.concatenate([cross_kv.reshape(rows, -1), cross_q], axis=1), cross_out, (packed,)
        )
        w_cross = spread(place, pack_attention(place.column_out(shard), shard))
    else:
        quarter = lambda w: w.reshape(-1, 4, QUARTER).transpose(1, 0, 2).reshape(-1, QUARTER)
        flat = lambda w: w.reshape(rows, -1)
        w_self = attention_plain(
            place, jnp.concatenate([flat(self_qkv), quarter(self_out)], axis=1)
        )
        w_cross = attention_plain(
            place, jnp.concatenate([flat(cross_kv), cross_q, quarter(cross_out)], axis=1)
        )

    turned = lambda value: value[:, 0].transpose(0, 2, 1)
    numbers = jnp.concatenate([token_lengths.T, audio_lengths.T, corpus_ids.T])
    blocks = input_blocks(
        turned(hidden_in),
        turned(cotangent),
        three_parts(jnp.concatenate([ln_gain, ln_bias])),
        numbers,
        first,
    )
    got = place.rows_in(blocks)
    hidden, cot, norms, nums = prepare(got, place.swap_core(got), corpus_weights)

    encoded = lax.dynamic_index_in_dim(encoder_states[:, 0], place.micro, 0, keepdims=False)
    other = place.move(encoded, lambda xy, core, z: (xy, 1 - core, z) if core == z // 2 else None)
    encoded = jnp.where(place.home == place.core, encoded, other)
    encoded = jnp.pad(encoded, ((0, padded - frames), (0, 0)))

    et = turn(encoded)
    part1, at, qkv, qt, kt, ot1, lse1 = self_forward(hidden, norms, nums, w_self, (et,))
    other1 = place.swap_core(part1)
    kv, kvt = cross_memory(encoded, w_cross)
    part2, h1, ct, q2, qt2, ot2, lse2 = cross_forward(
        hidden, part1, other1, norms, nums, kv, kvt, w_cross
    )
    other2 = place.swap_core(part2)
    part3, h2, mt, slope, it = units_forward(h1, part2, other2, norms, w_units)
    other3 = place.swap_core(part3)
    part, d3, e3, dz, terms3, out_a, out_b = units_backward(
        h2, part3, other3, norms, nums, cot, slope, w_units
    )
    other = place.swap_core(part)
    g_units = units_grads(place, mt, dz, it, e3)
    s_up, s_down = scatter_units(place, g_units)
    layer_out = place.rows_home((out_a, out_b))
    part, d2, e2, dq2, dkv, terms2 = cross_backward(
        d3, h2, part, other, norms, nums, kv, kvt, q2, qt2, ot2, lse2, w_cross
    )
    other = place.swap_core(part)
    keep, send = encoder_grad(dkv, w_cross)
    came = place.swap_core(send)
    g_cross = attention_grads(place, et, dkv, ct, dq2, ot2, e2, (keep,))
    if place.fast:
        came_cross = leave_plane(place, g_cross)
    encoder_blocks = finish_encoder(keep, came, frames)
    part, d1, e1, dqk, dv, terms1 = self_backward(
        d2, h1, part, other, norms, nums, qkv, qt, kt, ot1, lse1, w_self, encoder_blocks
    )
    other = place.swap_core(part)
    g_self = attention_grads(place, at, dqk, at, dv, ot1, e1)
    if place.fast:
        came_self = leave_plane(place, g_self)
    grad_encoder = place.rows_home(encoder_blocks).astype(F32)
    terms, out_a, out_b = finish_hidden(d1, hidden, part, other, norms, terms1, terms2, terms3)
    grad_hidden = place.rows_home((out_a, out_b)).astype(F32)

    few = D // (place.dp * place.mp)
    if place.fast:
        onward_cross = cross_plane(place, pass_on(g_cross, came_cross, [g_self[0]]))
        terms = terms + place.swap_xy(terms, 1)
        s_cross = place.column_back(column_blocks(g_cross, came_cross, onward_cross, True, (), [terms]))
        onward_self = cross_plane(place, pass_on(g_self, came_self, []))
        s_self = place.column_back(
            column_blocks(
                g_self, came_self, onward_self, True, (terms, place.swap_xy(terms, 2))
            )
        )
        shares = s_self[rows : rows + 8, :few]
    else:
        s_cross = sum_plain(place, g_cross, True)
        s_self = sum_plain(place, g_self, True)
        terms = jnp.where(place.core == 0, terms, 0.0)
        terms = lax.psum(terms, AXES)
        shares = lax.dynamic_slice_in_dim(terms, (place.z * place.dp + place.d) * few, few, 1)
    s_self = s_self[:rows]
    return (
        layer_out,
        grad_hidden,
        grad_encoder,
        s_self[:, : 3 * QUARTER].reshape(rows, 3, QUARTER),
        from_quarters(s_self[:, 3 * QUARTER :]),
        s_cross[:, 2 * QUARTER : 3 * QUARTER],
        s_cross[:, : 2 * QUARTER].reshape(rows, 2, QUARTER),
        from_quarters(s_cross[:, 3 * QUARTER :]),
        s_up,
        s_down,
        shares[:4],
        shares[4:],
    )


def solution(mesh):
    dp, mp = mesh.shape["dp"], mesh.shape["mp"]
    finer = Mesh(mesh.devices.reshape(dp // 2, 2, mp), AXES)
    both = ("xy", "core")
    rows = P(None, both, None, "mp")
    columns = P(both, None, "mp")
    pairs = P(both, "mp")
    units = P(("mp",) + both, None)
    each = P(None, both)
    return jax.shard_map(
        partial(per_device, dp, mp),
        mesh=finer,
        in_specs=(
            rows,
            P(None, both, None, None),
            rows,
            columns,
            units,
            pairs,
            columns,
            units,
            pairs,
            units,
            P(None, "mp"),
            P(None, "mp"),
            each,
            each,
            each,
            P(),
        ),
        out_specs=(
            rows,
            rows,
            rows,
            columns,
            units,
            pairs,
            columns,
            units,
            pairs,
            units,
            P(None, ("mp",) + both),
            P(None, ("mp",) + both),
        ),
        check_vma=False,
    )
```

```python
from functools import partial

import jax
import jax.numpy as jnp
from jax import lax
from jax.experimental import pallas as pl
from jax.experimental.pallas import tpu as pltpu
from jax.sharding import Mesh, PartitionSpec as P

D = 768
HALF = 384
QUARTER = 192
HEAD_DIM = 64
HEADS = 6
CHUNK = 256
BF = jnp.bfloat16
F32 = jnp.float32
AXES = ("xy", "core", "mp")
CHIPS = ("xy", "mp")
VMEM = pl.BlockSpec(memory_space=pltpu.VMEM)
SMEM = pl.BlockSpec(memory_space=pltpu.SMEM)
ANY = pl.BlockSpec(memory_space=pl.ANY)


def mm(left, right):
    return jnp.dot(left, right, preferred_element_type=F32)


def mm_t(left, right):
    return lax.dot_general(left, right, (((1,), (1,)), ((), ())), preferred_element_type=F32)


def shaped(shape, dtype=BF):
    return jax.ShapeDtypeStruct(shape, dtype)


def run(body, outs, vmem=(), hbm=(), smem=(), scratch=(), copies=0, micros=2, after=()):
    args = tuple(smem) + tuple(vmem) + tuple(hbm)
    count = len(args)
    scratch = list(scratch)
    if copies:
        scratch.append(pltpu.SemaphoreType.DMA((copies,)))
    moved = sum(a.size * a.dtype.itemsize for a in args) + sum(
        o.size * o.dtype.itemsize for o in outs
    )
    return pl.pallas_call(
        lambda *refs: body(*refs[:count], *refs[count + len(after) :]),
        out_shape=tuple(outs),
        in_specs=[SMEM] * len(smem) + [VMEM] * len(vmem) + [ANY] * (len(hbm) + len(after)),
        out_specs=(VMEM,) * len(outs),
        scratch_shapes=scratch,
        compiler_params=pltpu.CompilerParams(vmem_limit_bytes=48 * 1024 * 1024),
        cost_estimate=pl.CostEstimate(
            flops=int(micros * 1.15e9), bytes_accessed=moved, transcendentals=0
        ),
    )(*args, *after)


class Copies:
    def __init__(self, sems):
        self.sems, self.open = sems, []

    def start(self, source, target):
        copy = pltpu.make_async_copy(source, target, self.sems.at[len(self.open)])
        copy.start()
        self.open.append(copy)

    def wait(self):
        for copy in self.open:
            copy.wait()


def where_am_i():
    return lax.axis_index("core"), lax.axis_index("xy"), lax.axis_index("mp")


class Place:
    def __init__(self, dp, mp):
        self.dp, self.mp = dp, mp
        self.chips = dp // 2
        self.fast = self.chips == 4
        self.z = lax.axis_index("mp")
        self.core = lax.axis_index("core")
        self.xy = lax.axis_index("xy")
        self.d = 2 * self.xy + self.core
        self.micro = self.z % 2
        self.home = self.z // 2

    def move(self, value, route):
        pairs = []
        for xy in range(self.chips):
            for core in range(2):
                for z in range(self.mp):
                    target = route(xy, core, z)
                    if target is not None:
                        txy, tcore, tz = target
                        pairs.append(
                            ((2 * xy + core) * self.mp + z, (2 * txy + tcore) * self.mp + tz)
                        )
        return lax.ppermute(value, AXES, pairs)

    def swap_core(self, value):
        return self.move(value, lambda xy, core, z: (xy, 1 - core, z))

    def swap_xy(self, value, bit):
        return self.move(value, lambda xy, core, z: (xy ^ bit, core, z))

    def swap_z(self, value, bit):
        return self.move(value, lambda xy, core, z: (xy, core, z ^ bit))

    def column_routes(self):
        def route(step, xy, core, z):
            user, j = z // 2, z % 2
            home = core == user
            near = lambda i: (xy, user, 2 * user + i)
            far = lambda i: (xy, user, 2 * (1 - user) + i)
            if step == 0:
                return near(1 - j) if home else far(1 - j)
            if step == 1:
                return far(j) if home else near(j)
            if step == 2:
                return far(1 - j) if home else near(1 - j)
            return None if home else far(j)

        return [partial(route, step) for step in range(4)]

    def column_out(self, shard):
        return [self.move(shard, route) for route in self.column_routes()]

    def column_back(self, blocks):
        got = []
        for block, route in zip(blocks, self.column_routes()):
            turned = {}
            for xy in range(self.chips):
                for core in range(2):
                    for z in range(self.mp):
                        target = route(xy, core, z)
                        if target is not None:
                            turned[target] = (xy, core, z)
            got.append(self.move(block, lambda xy, core, z: turned.get((xy, core, z))))
        at_home = self.core == self.home
        return add_up(got[0], got[1], got[2], jnp.where(at_home, blocks[3], got[3]))

    def rows_in(self, blocks):
        def route(k, xy, core, z):
            target = (xy, z // 2, 2 * core + (z + k) % 2)
            return None if target == (xy, core, z) else target

        got = [self.move(block, partial(route, k)) for k, block in enumerate(blocks)]
        return jnp.stack([jnp.where(self.core == self.home, blocks[0], got[0]), got[1]])

    def rows_home(self, blocks):
        return self.rows_joined(blocks, self.rows_sent(blocks))

    def rows_sent(self, blocks):
        def route(k, xy, core, z):
            target = (xy, z // 2, 2 * core + (z % 2 - k) % 2)
            return None if target == (xy, core, z) else target

        return [self.move(block, partial(route, k)) for k, block in enumerate(blocks)]

    def rows_joined(self, blocks, got):
        got = [jnp.where(self.core == self.home, blocks[0], got[0]), got[1]]
        even = self.z % 2 == 0
        both = jnp.stack([jnp.where(even, got[0], got[1]), jnp.where(even, got[1], got[0])])
        return both[:, None].transpose(0, 1, 3, 2)


def norm(hidden):
    center = jnp.mean(hidden, axis=-1, keepdims=True)
    spread = jnp.mean(hidden * hidden, axis=-1, keepdims=True) - center * center
    inverse = lax.rsqrt(spread + 1e-05)
    return (hidden - center) * inverse, inverse


def norm_back(grad, unit, inverse, gain):
    scaled = grad * gain
    first = jnp.mean(scaled, axis=-1, keepdims=True)
    second = jnp.mean(scaled * unit, axis=-1, keepdims=True)
    terms = jnp.concatenate(
        [jnp.sum(grad * unit, axis=0, keepdims=True), jnp.sum(grad, axis=0, keepdims=True)], axis=0
    )
    return inverse * (scaled - first - unit * second), terms


def add_up(*terms):
    total = terms[0].astype(F32)
    for term in terms[1:]:
        total = total + term.astype(F32)
    return total


def input_blocks(hidden, terms, numbers, after=()):
    _, width, length = hidden.shape
    total = width + 32

    def body(numbers_ref, hidden_ref, terms_ref, *outs):
        _, _, z = where_am_i()
        lanes = lax.broadcasted_iota(jnp.int32, (8, length), 1)
        for k in range(2):
            micro = (z + k) % 2
            outs[k][0:width] = hidden_ref[micro]
            tok, aud = numbers_ref[0, micro], numbers_ref[1, micro]
            row = jnp.where(lanes == 0, tok // 256, jnp.where(lanes == 1, tok % 256, 0))
            row = jnp.where(lanes == 2, aud // 256, jnp.where(lanes == 3, aud % 256, row))
            row = jnp.where(lanes == 4, numbers_ref[2, micro], row)
            wide = jnp.concatenate(
                [terms_ref[...].astype(F32), jnp.zeros((24, length - width), F32)], axis=1
            )
            outs[k][width:total] = jnp.concatenate([wide, row.astype(F32)], axis=0).astype(BF)

    return run(
        body,
        [shaped((total, length))] * 2,
        smem=[numbers],
        vmem=[hidden, terms],
        micros=1,
        after=after,
    )


def turned_blocks(value, after=()):
    _, width, length = value.shape

    def body(ref, first_ref, second_ref):
        _, _, z = where_am_i()
        first_ref[...] = ref[z % 2]
        second_ref[...] = ref[(z + 1) % 2]

    return run(body, [shaped((width, length))] * 2, vmem=[value], micros=1, after=after)


def bring_blocks(copies, own_ref, other_ref, wide):
    core, _, z = where_am_i()
    found = []
    for k in range(2):
        slot = (z % 2 + k) % 2
        for ref, user in ((own_ref, core), (other_ref, 1 - core)):
            block = 2 * user + slot
            here = pl.ds(pl.multiple_of(block * QUARTER, QUARTER), QUARTER)
            copies.start(ref.at[k, pl.ds(0, QUARTER)], wide.at[here])
            found.append((ref.at[k], block))
    return found


def prepare_cotangent(own, other, after=()):
    length = own.shape[2]

    def body(own_ref, other_ref, cot_ref, wide, sems):
        copies = Copies(sems)
        bring_blocks(copies, own_ref, other_ref, wide)
        copies.wait()
        cot_ref[...] = wide[...].T

    return run(
        body,
        [shaped((length, D))],
        hbm=[own, other],
        scratch=[pltpu.VMEM((D, length), BF)],
        copies=4,
        micros=3,
        after=after,
    )[0]


def prepare(own, other, corpus_weights):
    length = own.shape[2]

    def body(
        weights_ref, own_ref, other_ref, hidden_ref, norms_ref, nums_ref, wide, extra, sems
    ):
        copies = Copies(sems)
        for ref, block in bring_blocks(copies, own_ref, other_ref, wide):
            copies.start(ref.at[pl.ds(QUARTER, 32)], extra.at[block])
        copies.wait()
        hidden_ref[...] = wide[...].T
        parts = [extra[b].astype(F32) for b in range(4)]
        norms_ref[...] = jnp.concatenate(
            [(e[0:8] + e[8:16] + e[16:24])[:, :QUARTER] for e in parts], axis=1
        )
        row = parts[0][24:25]
        tok = 256.0 * row[:, 0:1] + row[:, 1:2]
        aud = 256.0 * row[:, 2:3] + row[:, 3:4]
        weights = weights_ref[...]
        places = lax.broadcasted_iota(jnp.int32, weights.shape, 1).astype(F32)
        weight = jnp.sum(jnp.where(places == row[:, 4:5], weights, 0.0), axis=1, keepdims=True)
        index = lax.broadcasted_iota(jnp.int32, (8, 128), 0)
        nums_ref[...] = jnp.where(index == 0, tok, jnp.where(index == 1, aud, weight))

    return run(
        body,
        [shaped((length, D)), shaped((8, D), F32), shaped((8, 128), F32)],
        vmem=[corpus_weights.reshape(1, -1)],
        hbm=[own, other],
        scratch=[pltpu.VMEM((D, length), BF), pltpu.VMEM((4, 32, length), BF)],
        copies=8,
        micros=3,
    )


def quarters(value):
    return jnp.concatenate([value[:, p * QUARTER : (p + 1) * QUARTER] for p in range(4)], axis=0)


def attention_shard(blocks, out, after=()):
    rows = blocks.shape[-2]

    def body(blocks_ref, out_in_ref, out_ref):
        last = quarters(out_in_ref[...].astype(F32)).astype(BF)
        first = [blocks_ref[...]] if len(blocks.shape) == 2 else [blocks_ref[j] for j in range(3)]
        out_ref[...] = jnp.concatenate(first + [last], axis=1)

    return run(body, [shaped((rows, D))], vmem=[blocks, out], micros=1, after=after)[0]


def column_slots():
    core, _, z = where_am_i()
    j = z % 2
    home = 1 - jnp.abs(z // 2 - core)
    same = core + (1 - 2 * core) * (1 - home)
    return home == 1, (2 * (1 - j) + same, 2 * j + 1 - same, 2 * (1 - j) + 1 - same, 2 * j + same)


def bring_column(part_refs, own_ref, shards, sems):
    home, slots = column_slots()
    copies = Copies(sems)
    for k in range(3):
        copies.start(part_refs[k], shards.at[slots[k]])

    @pl.when(home)
    def _():
        copy = pltpu.make_async_copy(own_ref, shards.at[slots[3]], sems.at[3])
        copy.start()
        copy.wait()

    @pl.when(jnp.logical_not(home))
    def _():
        copy = pltpu.make_async_copy(part_refs[3], shards.at[slots[3]], sems.at[3])
        copy.start()
        copy.wait()

    copies.wait()


def pack_attention(parts, own):
    rows = own.shape[0]
    few = rows // 4

    def body(*refs):
        part_refs, own_ref, (out_ref, shards, sems) = refs[:4], refs[4], refs[5:]
        bring_column(part_refs, own_ref, shards, sems)
        for cs in range(2):
            low, high = shards[cs], shards[2 + cs]

            def both(at):
                return [low[:, at : at + QUARTER], high[:, at : at + QUARTER]]

            here = pl.ds(cs * rows, rows)
            out_ref[0, here, :] = jnp.concatenate(both(0) + both(QUARTER), axis=1)
            out_ref[1, here, 0:HALF] = jnp.concatenate(both(HALF), axis=1)
        outs = [shards[i, :, 3 * QUARTER :].astype(F32) for i in range(4)]
        stack = []
        for q in range(2):
            for i in range(4):
                left = outs[i][2 * q * few : (2 * q + 1) * few]
                right = outs[i][(2 * q + 1) * few : (2 * q + 2) * few]
                stack.append(jnp.concatenate([left, right], axis=1))
        out_ref[1, :, HALF:D] = jnp.concatenate(stack, axis=0).astype(BF)

    return run(
        body,
        [shaped((2, 2 * rows, D))],
        hbm=list(parts) + [own],
        scratch=[pltpu.VMEM((4, rows, D), BF)],
        copies=4,
        micros=2.5,
    )[0]


def unit_shard(place, fc_in, fc_out):
    rows = fc_in.shape[0]
    both = fc_in.reshape(rows, place.chips, 2, rows).transpose(2, 0, 1, 3).reshape(2, rows, HALF)
    kept = lax.dynamic_index_in_dim(both, place.core, 0, keepdims=False)
    sent = lax.dynamic_index_in_dim(both, 1 - place.core, 0, keepdims=False)
    came = place.swap_core(sent)
    first = place.core == 0
    left = jnp.concatenate([jnp.where(first, kept, came), jnp.where(first, came, kept)])
    right = jnp.concatenate([fc_out[:, :HALF], fc_out[:, HALF:]])
    return jnp.concatenate([left, right], axis=1)


def gather_units(place, shard):
    whole = lax.all_gather(shard, CHIPS, axis=0)
    if place.fast:
        return [whole]
    rows = shard.shape[0] // 2
    whole = whole.reshape(place.chips, place.mp, 2 * rows, D)
    up = whole[..., :HALF].transpose(0, 2, 1, 3).reshape(D, 2 * D)
    down = whole[..., HALF:].reshape(place.chips, place.mp, 2, rows, HALF)
    return [up, down.transpose(1, 0, 3, 2, 4).reshape(2 * D, D)]


def scatter_units(place, grads):
    total = lax.psum_scatter(grads, CHIPS, scatter_dimension=0, tiled=False)
    rows = total.shape[0] // 2
    kept = lax.dynamic_slice_in_dim(total, place.core * rows, rows, 0)
    sent = lax.dynamic_slice_in_dim(total[:, :HALF], (1 - place.core) * rows, rows, 0)
    came = place.swap_core(sent)
    kept = kept[:, :HALF]
    first = place.core == 0
    both = jnp.stack([jnp.where(first, kept, came), jnp.where(first, came, kept)])
    both = both.reshape(2, rows, place.chips, rows).transpose(1, 2, 0, 3).reshape(rows, D)
    down = jnp.concatenate([total[:rows, HALF:], total[rows:, HALF:]], axis=1)
    return both.astype(F32), down.astype(F32)


def spread(place, own):
    from_x = place.swap_xy(own, 1)
    from_y = place.swap_xy(own, 2)
    far_one = place.swap_xy(from_y[1], 1)
    far_zero = place.swap_xy(from_x[0], 2)
    return [own, from_x, from_y, far_zero, far_one]


def piece_views(refs, which, xy):
    own, from_x, from_y, far_zero, far_one = refs
    return [
        (own.at[which], xy),
        (from_x.at[which], xy ^ 1),
        (from_y.at[which], xy ^ 2),
        ((far_zero, far_one)[which], xy ^ 3),
    ]


def load_wide(copies, refs, which, xy, target, columns=None):
    if len(refs) != 5:
        copies.start(refs[which], target)
        return
    for view, chip in piece_views(refs, which, xy):
        rows = view.shape[0]
        if columns is not None:
            view = view.at[:, pl.ds(0, columns)]
        copies.start(view, target.at[pl.ds(pl.multiple_of(chip * rows, 16), rows)])


def load_out(copies, refs, xy, target):
    if len(refs) != 5:
        copies.start(refs[2], target)
        return
    for view, chip in piece_views(refs, 1, xy):
        rows = view.shape[0] // 4
        for q in range(2):
            for hi in range(2):
                copies.start(
                    view.at[pl.ds((2 * q + hi) * rows, rows), pl.ds(HALF, HALF)],
                    target.at[q, pl.ds(pl.multiple_of(hi * QUARTER + chip * rows, 16), rows)],
                )


def load_up(copies, refs, w_up):
    if len(refs) == 2:
        copies.start(refs[0], w_up)
        return
    (whole,) = refs
    count, rows, _ = whole.shape
    for i in range(count):
        xy, z = i // 4, i % 4
        copies.start(
            whole.at[i, :, pl.ds(0, HALF)], w_up.at[pl.ds(rows * xy, rows), pl.ds(z * HALF, HALF)]
        )


def load_down(copies, refs, w_down):
    if len(refs) == 2:
        copies.start(refs[1], w_down)
        return
    (whole,) = refs
    count, rows, _ = whole.shape
    rows = rows // 2
    for i in range(count):
        xy, z = i // 4, i % 4
        for q in range(2):
            copies.start(
                whole.at[i, pl.ds(q * rows, rows), pl.ds(HALF, HALF)],
                w_down.at[pl.ds(z * HALF + xy * rows, rows), pl.ds(q * HALF, HALF)],
            )


ATTENTION_COPIES = 4 + 4 + 16
UP_COPIES = 16
DOWN_COPIES = 32


def gather_plain(place, shard):
    whole = lax.all_gather(shard, ("mp", "xy", "core"), axis=0)
    whole = whole.reshape((2, 2, place.dp) + shard.shape)
    return lax.dynamic_index_in_dim(whole, place.core, 0, keepdims=False)


def attention_plain(place, shard):
    mine = gather_plain(place, shard)
    rows = shard.shape[0]

    def columns(at, count):
        value = mine[..., at : at + count * QUARTER].reshape(2, D, count, QUARTER)
        return value.transpose(1, 2, 0, 3).reshape(D, count * HALF)

    out = mine[..., 3 * QUARTER :].reshape(2, place.dp, 2, 2, rows // 4, QUARTER)
    out = out.transpose(2, 0, 1, 4, 3, 5).reshape(2, HALF, HALF)
    return [columns(0, 2), columns(HALF, 1), out]


def head_rows(h):
    return pl.ds(pl.multiple_of(h * HEAD_DIM, HEAD_DIM), HEAD_DIM)


def low_parts(value):
    parts = []
    for _ in range(3):
        part = value.astype(BF)
        parts.append(part)
        value = value - part.astype(F32)
    return parts


def widened(count):
    return lambda rows: (
        lax.broadcasted_iota(jnp.int32, (rows, HEAD_DIM), 1) < count
    ).astype(F32).astype(BF)


def below(head, rows):
    blank = jnp.zeros((HEAD_DIM - len(rows), head.shape[1]), F32)
    rest = jnp.concatenate([row.astype(F32) for row in rows] + [blank], axis=0)
    return jnp.concatenate([head, rest.astype(BF)], axis=0)


def project(left, pair_ref):
    return jnp.concatenate([mm(left, pair_ref[0]), mm(left, pair_ref[1])], axis=1)


def project_t(left, pair_ref):
    return mm_t(left[:, :HALF], pair_ref[0]) + mm_t(left[:, HALF:], pair_ref[1])


def self_forward(hidden, norms, nums, weights, after=()):
    length = hidden.shape[0]

    def body(hidden_ref, norms_ref, nums_ref, *refs):
        w_refs, refs = refs[: len(weights)], refs[len(weights) :]
        part_ref, at_ref, qkv_ref, qt_ref, kt_ref, ot_ref, lse_ref = refs[:7]
        w_qk, w_v, w_out, vt, heads, bias, sems = refs[7:]
        _, xy, _ = where_am_i()
        copies = Copies(sems)
        load_wide(copies, w_refs, 0, xy, w_qk)
        load_wide(copies, w_refs, 1, xy, w_v, HALF)
        load_out(copies, w_refs, xy, w_out)
        unit, _ = norm(hidden_ref[...].astype(F32))
        a = (unit * norms_ref[0:1] + norms_ref[4:5]).astype(BF)
        at_ref[...] = a.T
        keys = lax.broadcasted_iota(jnp.int32, (length, length), 0)
        queries = lax.broadcasted_iota(jnp.int32, (length, length), 1)
        allowed = (keys <= queries) & (keys.astype(F32) < nums_ref[0:1, 0:1])
        bias[...] = jnp.where(allowed, 0.0, -1e30)
        copies.wait()
        qk = mm(a, w_qk[...])
        q = (qk[:, :HALF].astype(BF).astype(F32) * HEAD_DIM ** (-0.5)).astype(BF)
        k = qk[:, HALF:].astype(BF)
        v = mm(a, w_v[...]).astype(BF)
        qkv_ref[:, 0:HALF] = q
        qkv_ref[:, HALF : 2 * HALF] = k
        qkv_ref[:, 2 * HALF :] = v
        qt_ref[...] = q.T
        kt_ref[...] = k.T
        vt[...] = v.T
        for h in range(HEADS):
            heads[h] = k[:, h * HEAD_DIM : (h + 1) * HEAD_DIM]

        def head(h, carry):
            s = mm(heads[h], qt_ref[head_rows(h), :]) + bias[...]
            top = jnp.max(s, axis=0, keepdims=True)
            p = jnp.exp(s - top)
            total = jnp.sum(p, axis=0, keepdims=True)
            o = mm(vt[head_rows(h), :], p.astype(BF))
            ot_ref[head_rows(h), :] = (o / total).astype(BF)
            lse_ref[h] = top + jnp.log(total)
            return carry

        lax.fori_loop(0, HEADS, head, 0)
        part_ref[...] = project(ot_ref[...].T, w_out).astype(BF)

    return run(
        body,
        [
            shaped((length, D)),
            shaped((D, length)),
            shaped((length, 3 * HALF)),
            shaped((HALF, length)),
            shaped((HALF, length)),
            shaped((HALF, length)),
            shaped((HEADS, 1, length), F32),
        ],
        vmem=[hidden, norms, nums],
        hbm=weights,
        scratch=[
            pltpu.VMEM((D, D), BF),
            pltpu.VMEM((D, HALF), BF),
            pltpu.VMEM((2, HALF, HALF), BF),
            pltpu.VMEM((HALF, length), BF),
            pltpu.VMEM((HEADS, length, HEAD_DIM), BF),
            pltpu.VMEM((length, length), F32),
        ],
        copies=ATTENTION_COPIES,
        micros=10,
        after=after,
    )


def turn(value, after=()):
    rows, columns = value.shape

    def body(ref, out_ref):
        for at in range(0, rows, CHUNK):
            out_ref[:, at : at + CHUNK] = ref[at : at + CHUNK, :].T

    return run(body, [shaped((columns, rows))], vmem=[value], micros=4, after=after)[0]


def cross_memory(encoded, weights):
    frames = encoded.shape[0]

    def body(enc_ref, *refs):
        w_refs, refs = refs[: len(weights)], refs[len(weights) :]
        kv_ref, kvt_ref, w_kv, sems = refs
        _, xy, _ = where_am_i()
        copies = Copies(sems)
        load_wide(copies, w_refs, 0, xy, w_kv)
        copies.wait()

        def step(i, carry):
            here = pl.ds(pl.multiple_of(i * CHUNK, CHUNK), CHUNK)
            kv = mm(enc_ref[here, :], w_kv[...]).astype(BF)
            kv_ref[here, :] = kv
            kvt_ref[:, here] = kv.T
            return carry

        lax.fori_loop(0, frames // CHUNK, step, 0)

    return run(
        body,
        [shaped((frames, D)), shaped((D, frames))],
        vmem=[encoded],
        hbm=weights,
        scratch=[pltpu.VMEM((D, D), BF)],
        copies=4,
        micros=6,
    )


def residual(hidden_ref, mine_ref, other_ref):
    return hidden_ref[...].astype(F32) + (mine_ref[...].astype(F32) + other_ref[...].astype(F32))


def cross_forward(hidden, mine, other, norms, nums, kv, kvt, weights):
    length = hidden.shape[0]
    frames = kv.shape[0]

    def body(hidden_ref, mine_ref, other_ref, norms_ref, nums_ref, kv_ref, kvt_ref, *refs):
        w_refs, refs = refs[: len(weights)], refs[len(weights) :]
        part_ref, h_ref, ct_ref, q_ref, qt_ref, ot_ref, lse_ref = refs[:7]
        w_q, w_out, heads, values_t, scores, sems = refs[7:]
        _, xy, _ = where_am_i()
        copies = Copies(sems)
        load_wide(copies, w_refs, 1, xy, w_q, HALF)
        load_out(copies, w_refs, xy, w_out)
        h1 = residual(hidden_ref, mine_ref, other_ref)
        h_ref[...] = h1
        unit, _ = norm(h1)
        c = (unit * norms_ref[1:2] + norms_ref[5:6]).astype(BF)
        ct_ref[...] = c.T
        frame = lax.broadcasted_iota(jnp.int32, (frames, HEAD_DIM), 0).astype(F32)
        lane = lax.broadcasted_iota(jnp.int32, (frames, HEAD_DIM), 1)
        mask = jnp.where(frame < nums_ref[1:2, 0:1], 0.0, -1e30)
        beside = jnp.where(lane == 0, mask, 0.0).astype(BF)
        one = lax.broadcasted_iota(jnp.int32, (16, frames), 0)
        one = jnp.where(one == 0, 1.0, 0.0).astype(BF)
        for h in range(HEADS):
            keys = kv_ref[:, h * HEAD_DIM : (h + 1) * HEAD_DIM]
            heads[h] = jnp.concatenate([keys, beside], axis=1)
            values = kvt_ref[HALF + h * HEAD_DIM : HALF + (h + 1) * HEAD_DIM, :]
            values_t[h] = jnp.concatenate([values, one], axis=0)
        copies.wait()
        q = mm(c, w_q[...]).astype(BF)
        q = (q.astype(F32) * HEAD_DIM ** (-0.5)).astype(BF)
        q_ref[...] = q
        qt_ref[...] = q.T
        ones = jnp.ones((1, length), F32)

        def head(h, carry):
            qt = below(qt_ref[head_rows(h), :], [ones])
            top = None
            for at in range(0, frames, CHUNK):
                s = mm(heads[h, at : at + CHUNK], qt)
                scores[at : at + CHUNK] = s
                high = jnp.max(s, axis=0, keepdims=True)
                top = high if top is None else jnp.maximum(top, high)
            o = None
            for at in range(0, frames, CHUNK):
                p = jnp.exp(scores[at : at + CHUNK] - top).astype(BF)
                more = mm(values_t[h, :, at : at + CHUNK], p)
                o = more if o is None else o + more
            total = o[HEAD_DIM : HEAD_DIM + 1]
            ot_ref[head_rows(h), :] = (o[:HEAD_DIM] / total).astype(BF)
            lse_ref[h] = top + jnp.log(total)
            return carry

        lax.fori_loop(0, HEADS, head, 0)
        part_ref[...] = project(ot_ref[...].T, w_out).astype(BF)

    return run(
        body,
        [
            shaped((length, D)),
            shaped((length, D), F32),
            shaped((D, length)),
            shaped((length, HALF)),
            shaped((HALF, length)),
            shaped((HALF, length)),
            shaped((HEADS, 1, length), F32),
        ],
        vmem=[hidden, mine, other, norms, nums, kv, kvt],
        hbm=weights,
        scratch=[
            pltpu.VMEM((D, HALF), BF),
            pltpu.VMEM((2, HALF, HALF), BF),
            pltpu.VMEM((HEADS, frames, 2 * HEAD_DIM), BF),
            pltpu.VMEM((HEADS, HEAD_DIM + 16, frames), BF),
            pltpu.VMEM((frames, length), F32),
        ],
        copies=4 + 16,
        micros=10,
    )


def units_forward(hidden, mine, other, norms, weights):
    length = hidden.shape[0]

    def body(hidden_ref, mine_ref, other_ref, norms_ref, *refs):
        w_refs, refs = refs[: len(weights)], refs[len(weights) :]
        part_ref, h_ref, mt_ref, slope_ref, it_ref = refs[:5]
        w_up, w_down, inner, late_sems, sems = refs[5:]
        _, xy, _ = where_am_i()
        copies = Copies(sems)
        load_up(copies, w_refs, w_up)
        late = Copies(late_sems)
        load_down(late, w_refs, w_down)
        h2 = residual(hidden_ref, mine_ref, other_ref)
        h_ref[...] = h2
        unit, _ = norm(h2)
        m = (unit * norms_ref[2:3] + norms_ref[6:7]).astype(BF)
        mt_ref[...] = m.T
        copies.wait()
        for at in range(0, 2 * D, CHUNK):
            here = slice(at, at + CHUNK)
            z = mm(m, w_up[:, here])
            share = 0.5 * (1.0 + lax.erf(z * 0.7071067811865476))
            slope = share + z * (0.3989422804014327 * jnp.exp(-0.5 * z * z))
            value = (z * share).astype(BF)
            inner[:, here] = value
            it_ref[here, :] = value.T
            slope_ref[:, here] = slope.astype(BF)
        late.wait()
        for at in range(0, D, CHUNK):
            part_ref[:, at : at + CHUNK] = mm(inner[...], w_down[:, at : at + CHUNK]).astype(BF)

    return run(
        body,
        [
            shaped((length, D)),
            shaped((length, D), F32),
            shaped((D, length)),
            shaped((length, 2 * D)),
            shaped((2 * D, length)),
        ],
        vmem=[hidden, mine, other, norms],
        hbm=weights,
        scratch=[
            pltpu.VMEM((D, 2 * D), BF),
            pltpu.VMEM((2 * D, D), BF),
            pltpu.VMEM((length, 2 * D), BF),
            pltpu.SemaphoreType.DMA((DOWN_COPIES,)),
        ],
        copies=UP_COPIES,
        micros=9,
    )


def store_blocks(value, blocks, first_ref, second_ref):
    core, _, z = where_am_i()
    for b in range(4):
        blocks[b] = value[:, b * QUARTER : (b + 1) * QUARTER]
    first_ref[...] = blocks[2 * core + z % 2].T
    second_ref[...] = blocks[2 * core + (z + 1) % 2].T


def units_backward(hidden, mine, other, norms, nums, cot, slope, weights):
    length = hidden.shape[0]

    def body(hidden_ref, mine_ref, other_ref, norms_ref, nums_ref, cot_ref, slope_ref, *refs):
        w_refs, refs = refs[: len(weights)], refs[len(weights) :]
        part_ref, d_ref, e_ref, dz_ref, terms_ref, first_ref, second_ref = refs[:7]
        w_up, w_down, blocks, late_sems, sems = refs[7:]
        _, xy, _ = where_am_i()
        copies = Copies(sems)
        load_down(copies, w_refs, w_down)
        late = Copies(late_sems)
        load_up(late, w_refs, w_up)
        unit, inverse = norm(residual(hidden_ref, mine_ref, other_ref))
        final = (unit * norms_ref[3:4] + norms_ref[7:8]).astype(BF)
        store_blocks(final, blocks, first_ref, second_ref)
        live = lax.broadcasted_iota(jnp.int32, (length, 1), 0).astype(F32) < nums_ref[0:1, 0:1]
        grad = cot_ref[...].astype(F32) * jnp.where(live, nums_ref[2:3, 0:1], 0.0)
        d3, terms = norm_back(grad, unit, inverse, norms_ref[3:4])
        d_ref[...] = d3
        terms_ref[...] = terms
        e = d3.astype(BF)
        e_ref[...] = e
        copies.wait()
        for at in range(0, 2 * D, CHUNK):
            here = slice(at, at + CHUNK)
            d_inner = mm_t(e, w_down[here, :])
            dz_ref[:, here] = (slope_ref[:, here].astype(F32) * d_inner).astype(BF)
        late.wait()
        for at in range(0, D, CHUNK):
            out = mm_t(dz_ref[...], w_up[at : at + CHUNK, :])
            part_ref[:, at : at + CHUNK] = out.astype(BF)

    return run(
        body,
        [
            shaped((length, D)),
            shaped((length, D), F32),
            shaped((length, D)),
            shaped((length, 2 * D)),
            shaped((2, D), F32),
            shaped((QUARTER, length)),
            shaped((QUARTER, length)),
        ],
        vmem=[hidden, mine, other, norms, nums, cot, slope],
        hbm=weights,
        scratch=[
            pltpu.VMEM((D, 2 * D), BF),
            pltpu.VMEM((2 * D, D), BF),
            pltpu.VMEM((4, length, QUARTER), BF),
            pltpu.SemaphoreType.DMA((UP_COPIES,)),
        ],
        copies=DOWN_COPIES,
        micros=10,
    )


def step_back(d_ref, hidden_ref, mine_ref, other_ref, gain):
    unit, inverse = norm(hidden_ref[...].astype(F32))
    grad = mine_ref[...].astype(F32) + other_ref[...].astype(F32)
    part, terms = norm_back(grad, unit, inverse, gain)
    return d_ref[...] + part, terms


def cross_backward(
    d, hidden, mine, other, norms, nums, kv, kvt, q, qt, ot, lse, weights, after=()
):
    length = hidden.shape[0]
    frames = kv.shape[0]

    def body(
        d_ref, hidden_ref, mine_ref, other_ref, norms_ref, nums_ref, kv_ref, kvt_ref, q_ref,
        qt_ref, ot_ref, lse_ref, *refs
    ):
        w_refs, refs = refs[: len(weights)], refs[len(weights) :]
        part_ref, d_out_ref, e_ref, dq_ref, dkv_ref, terms_ref = refs[:6]
        w_q, w_out, keys, values, queries, grads, dot_t, dk_h, dv_h, dqt, sems = refs[6:]
        _, xy, _ = where_am_i()
        copies = Copies(sems)
        load_wide(copies, w_refs, 1, xy, w_q, HALF)
        load_out(copies, w_refs, xy, w_out)
        d2, terms = step_back(d_ref, hidden_ref, mine_ref, other_ref, norms_ref[2:3])
        d_out_ref[...] = d2
        terms_ref[...] = terms
        e = d2.astype(BF)
        e_ref[...] = e
        frame = lax.broadcasted_iota(jnp.int32, (frames, HEAD_DIM), 0).astype(F32)
        lane = lax.broadcasted_iota(jnp.int32, (frames, HEAD_DIM), 1)
        mask = jnp.where(frame < nums_ref[1:2, 0:1], 0.0, -1e30)
        beside = jnp.where(lane == 0, mask, jnp.where(lane < 4, 1.0, 0.0)).astype(BF)
        three = widened(3)(frames)
        for h in range(HEADS):
            lanes = slice(h * HEAD_DIM, (h + 1) * HEAD_DIM)
            keys[h] = jnp.concatenate([kv_ref[:, lanes], beside], axis=1)
            value = kv_ref[:, HALF + h * HEAD_DIM : HALF + (h + 1) * HEAD_DIM]
            values[h] = jnp.concatenate([value, three], axis=1)
            queries[h] = q_ref[:, lanes]
        copies.wait()
        d_mixed = project_t(e, w_out).astype(BF)
        dot_t[...] = d_mixed.T
        for h in range(HEADS):
            grads[h] = d_mixed[:, h * HEAD_DIM : (h + 1) * HEAD_DIM]
        ones = jnp.ones((1, length), F32)

        def head(h, carry):
            rows = head_rows(h)
            do_t = dot_t[rows, :]
            q_n, do_n = queries[h], grads[h]
            delta = jnp.sum(do_t.astype(F32) * ot_ref[rows, :].astype(F32), axis=0, keepdims=True)
            q_t = below(qt_ref[rows, :], [ones] + low_parts(-lse_ref[h]))
            do_t = below(do_t, low_parts(-delta))
            total = None
            for at in range(0, frames, CHUNK):
                here = slice(at, at + CHUNK)
                p = jnp.exp(mm(keys[h, here], q_t))
                ds = (p * mm(values[h, here], do_t)).astype(BF)
                dv_h[h, here] = mm(p.astype(BF), do_n).astype(BF)
                dk_h[h, here] = mm(ds, q_n).astype(BF)
                more = mm(kvt_ref[rows, here], ds)
                total = more if total is None else total + more
            dqt[rows, :] = (total * HEAD_DIM ** (-0.5)).astype(BF)
            return carry

        lax.fori_loop(0, HEADS, head, 0)
        dq = dqt[...].T
        dq_ref[...] = dq
        part_ref[...] = mm_t(dq, w_q[...]).astype(BF)
        for h in range(HEADS):
            lanes = slice(h * HEAD_DIM, (h + 1) * HEAD_DIM)
            dkv_ref[:, lanes] = dk_h[h]
            dkv_ref[:, HALF + h * HEAD_DIM : HALF + (h + 1) * HEAD_DIM] = dv_h[h]

    return run(
        body,
        [
            shaped((length, D)),
            shaped((length, D), F32),
            shaped((length, D)),
            shaped((length, HALF)),
            shaped((frames, D)),
            shaped((2, D), F32),
        ],
        vmem=[d, hidden, mine, other, norms, nums, kv, kvt, q, qt, ot, lse],
        hbm=weights,
        scratch=[
            pltpu.VMEM((D, HALF), BF),
            pltpu.VMEM((2, HALF, HALF), BF),
            pltpu.VMEM((HEADS, frames, 2 * HEAD_DIM), BF),
            pltpu.VMEM((HEADS, frames, 2 * HEAD_DIM), BF),
            pltpu.VMEM((HEADS, length, HEAD_DIM), BF),
            pltpu.VMEM((HEADS, length, HEAD_DIM), BF),
            pltpu.VMEM((HALF, length), BF),
            pltpu.VMEM((HEADS, frames, HEAD_DIM), BF),
            pltpu.VMEM((HEADS, frames, HEAD_DIM), BF),
            pltpu.VMEM((HALF, length), BF),
        ],
        copies=4 + 16,
        micros=22,
        after=after,
    )


def self_backward(d, hidden, mine, other, norms, nums, qkv, qt, kt, ot, lse, weights, after=()):
    length = hidden.shape[0]

    def body(
        d_ref, hidden_ref, mine_ref, other_ref, norms_ref, nums_ref, qkv_ref, qt_ref, kt_ref,
        ot_ref, lse_ref, *refs
    ):
        w_refs, refs = refs[: len(weights)], refs[len(weights) :]
        part_ref, d_out_ref, e_ref, dqk_ref, dv_ref, terms_ref = refs[:6]
        w_qk, w_v, w_out, queries_h, keys, values, grads, dot_t, dk_h, dv_h, dqt, bias, sems = refs[6:]
        _, xy, _ = where_am_i()
        copies = Copies(sems)
        load_out(copies, w_refs, xy, w_out)
        load_wide(copies, w_refs, 0, xy, w_qk)
        load_wide(copies, w_refs, 1, xy, w_v, HALF)
        d1, terms = step_back(d_ref, hidden_ref, mine_ref, other_ref, norms_ref[1:2])
        d_out_ref[...] = d1
        terms_ref[...] = terms
        e = d1.astype(BF)
        e_ref[...] = e
        places = lax.broadcasted_iota(jnp.int32, (length, length), 0)
        queries = lax.broadcasted_iota(jnp.int32, (length, length), 1)
        allowed = (places <= queries) & (places.astype(F32) < nums_ref[0:1, 0:1])
        bias[...] = jnp.where(allowed, 0.0, -1e30)
        three = widened(3)(length)
        for h in range(HEADS):
            at = h * HEAD_DIM
            queries_h[h] = qkv_ref[:, at : at + HEAD_DIM]
            key = qkv_ref[:, HALF + at : HALF + at + HEAD_DIM]
            keys[h] = jnp.concatenate([key, three], axis=1)
            value = qkv_ref[:, 2 * HALF + at : 2 * HALF + at + HEAD_DIM]
            values[h] = jnp.concatenate([value, three], axis=1)
        copies.wait()
        d_mixed = project_t(e, w_out).astype(BF)
        dot_t[...] = d_mixed.T
        for h in range(HEADS):
            grads[h] = d_mixed[:, h * HEAD_DIM : (h + 1) * HEAD_DIM]

        def head(h, carry):
            rows = head_rows(h)
            do_t, do_n = dot_t[rows, :], grads[h]
            delta = jnp.sum(do_t.astype(F32) * ot_ref[rows, :].astype(F32), axis=0, keepdims=True)
            q_t = below(qt_ref[rows, :], low_parts(-lse_ref[h]))
            do_t = below(do_t, low_parts(-delta))
            p = jnp.exp(mm(keys[h], q_t) + bias[...])
            ds = (p * mm(values[h], do_t)).astype(BF)
            dv_h[h] = mm(p.astype(BF), do_n).astype(BF)
            dk_h[h] = mm(ds, queries_h[h]).astype(BF)
            dqt[rows, :] = (mm(kt_ref[rows, :], ds) * HEAD_DIM ** (-0.5)).astype(BF)
            return carry

        lax.fori_loop(0, HEADS, head, 0)
        dqk_ref[:, 0:HALF] = dqt[...].T
        for h in range(HEADS):
            lanes = slice(HALF + h * HEAD_DIM, HALF + (h + 1) * HEAD_DIM)
            dqk_ref[:, lanes] = dk_h[h]
            dv_ref[:, h * HEAD_DIM : (h + 1) * HEAD_DIM] = dv_h[h]
        out = mm_t(dqk_ref[...], w_qk[...]) + mm_t(dv_ref[...], w_v[...])
        part_ref[...] = out.astype(BF)

    return run(
        body,
        [
            shaped((length, D)),
            shaped((length, D), F32),
            shaped((length, D)),
            shaped((length, D)),
            shaped((length, HALF)),
            shaped((2, D), F32),
        ],
        vmem=[d, hidden, mine, other, norms, nums, qkv, qt, kt, ot, lse],
        hbm=weights,
        scratch=[
            pltpu.VMEM((D, D), BF),
            pltpu.VMEM((D, HALF), BF),
            pltpu.VMEM((2, HALF, HALF), BF),
            pltpu.VMEM((HEADS, length, HEAD_DIM), BF),
            pltpu.VMEM((HEADS, length, 2 * HEAD_DIM), BF),
            pltpu.VMEM((HEADS, length, 2 * HEAD_DIM), BF),
            pltpu.VMEM((HEADS, length, HEAD_DIM), BF),
            pltpu.VMEM((HALF, length), BF),
            pltpu.VMEM((HEADS, length, HEAD_DIM), BF),
            pltpu.VMEM((HEADS, length, HEAD_DIM), BF),
            pltpu.VMEM((HALF, length), BF),
            pltpu.VMEM((length, length), F32),
        ],
        copies=ATTENTION_COPIES,
        micros=12,
        after=after,
    )


def finish_hidden(d, hidden, mine, other, norms, terms1, terms2, terms3, after=()):
    length = hidden.shape[0]

    def body(
        d_ref, hidden_ref, mine_ref, other_ref, norms_ref, one, two, three, terms_ref, first_ref,
        second_ref, blocks
    ):
        d0, terms = step_back(d_ref, hidden_ref, mine_ref, other_ref, norms_ref[0:1])
        store_blocks(d0.astype(BF), blocks, first_ref, second_ref)
        for j in range(2):
            here = slice(j, j + 1)
            terms_ref[4 * j : 4 * j + 4] = jnp.concatenate(
                [terms[here], one[here], two[here], three[here]], axis=0
            )

    return run(
        body,
        [shaped((8, D), F32), shaped((QUARTER, length)), shaped((QUARTER, length))],
        vmem=[d, hidden, mine, other, norms, terms1, terms2, terms3],
        scratch=[pltpu.VMEM((4, length, QUARTER), BF)],
        micros=4,
        after=after,
    )


def finish_encoder(keep, other, frames):
    def body(keep_ref, other_ref, first_ref, second_ref):
        _, _, z = where_am_i()
        for ref, k in ((first_ref, 0), (second_ref, 1)):
            here = pl.ds(pl.multiple_of(((z + k) % 2) * QUARTER, QUARTER), QUARTER)
            total = keep_ref[here, :].astype(F32) + other_ref[here, :].astype(F32)
            ref[...] = total.astype(BF)[:, :frames]

    return run(
        body,
        [shaped((QUARTER, frames)), shaped((QUARTER, frames))],
        vmem=[keep, other],
        micros=2,
    )


def block_plan(place):
    if not place.fast:
        return 1, (((1, 0, 0),), ((1, 0, 0),))
    first = ((1, 0, 0), (0, 0, 1), (1, 1, 2), (0, 1, 3))
    second = ((1, 0, 0), (1, 1, 1), (0, 0, 2), (0, 1, 3))
    return 4, (first, second)


def grad_outputs(place, shape):
    if place.fast:
        return [shaped((2,) + shape)] * 4
    return [shaped((1,) + shape)] * 4


def units_grads(place, mt, dz, it, e):
    chips = place.chips
    rows = D // (2 * chips)

    def body(mt_ref, dz_ref, it_ref, e_ref, out_ref):
        for xy in range(chips):
            left = mm(mt_ref[2 * rows * xy : 2 * rows * (xy + 1), :], dz_ref[...]).astype(BF)
            for z in range(4):
                out_ref[4 * xy + z, :, 0:HALF] = left[:, z * HALF : (z + 1) * HALF]
                at = z * HALF + xy * rows
                right = mm(it_ref[at : at + rows, :], e_ref[...]).astype(BF)
                for q in range(2):
                    out_ref[4 * xy + z, q * rows : (q + 1) * rows, HALF:D] = right[
                        :, q * HALF : (q + 1) * HALF
                    ]

    def plain(mt_ref, dz_ref, it_ref, e_ref, left_ref, right_ref):
        left_ref[...] = mm(mt_ref[...], dz_ref[...]).astype(BF)
        right_ref[...] = mm(it_ref[...], e_ref[...]).astype(BF)

    if place.fast:
        return run(
            body, [shaped((4 * chips, 2 * rows, D))], vmem=[mt, dz, it, e], micros=7
        )[0]
    left, right = run(
        plain, [shaped((D, 2 * D)), shaped((2 * D, D))], vmem=[mt, dz, it, e], micros=7
    )
    left = left.reshape(chips, 2 * rows, 4, HALF).transpose(0, 2, 1, 3)
    right = right.reshape(4, chips, rows, 2, HALF).transpose(1, 0, 3, 2, 4)
    whole = jnp.concatenate([left, right.reshape(chips, 4, 2 * rows, HALF)], axis=-1)
    return whole.reshape(4 * chips, 2 * rows, D)


def attention_grads(place, wide_left, wide_right, left, right, ot, e, after=()):
    count, plan = block_plan(place)
    rows = D // count
    few = rows // 4

    def body(wide_left_ref, wide_right_ref, left_ref, right_ref, ot_ref, e_ref, *outs):
        _, xy, _ = where_am_i()
        for output, slot, offset in plan[0]:
            chip = xy ^ offset if count > 1 else 0
            here = pl.ds(pl.multiple_of(chip * rows, 16), rows)
            outs[output][slot] = mm(wide_left_ref[here, :], wide_right_ref[...]).astype(BF)
        for output, slot, offset in plan[1]:
            chip = xy ^ offset if count > 1 else 0
            here = pl.ds(pl.multiple_of(chip * rows, 16), rows)
            target = outs[2 + output]
            target[slot, :, 0:HALF] = mm(left_ref[here, :], right_ref[...]).astype(BF)
            for hi in range(2):
                here = pl.ds(pl.multiple_of(hi * QUARTER + chip * few, 16), few)
                both = mm(ot_ref[here, :], e_ref[...]).astype(BF)
                for q in range(2):
                    at = (2 * q + hi) * few
                    target[slot, at : at + few, HALF:D] = both[:, q * HALF : (q + 1) * HALF]

    return run(
        body,
        grad_outputs(place, (rows, D)),
        vmem=[wide_left, wide_right, left, right, ot, e],
        micros=6,
        after=after,
    )


def encoder_grad(dkv, weights):
    padded = dkv.shape[0]

    def body(dkv_ref, *refs):
        w_refs, (keep_ref, send_ref, w_kv, sems) = refs[: len(weights)], refs[len(weights) :]
        core, xy, _ = where_am_i()
        copies = Copies(sems)
        load_wide(copies, w_refs, 0, xy, w_kv)
        copies.wait()
        mine = pl.ds(pl.multiple_of(core * HALF, HALF), HALF)
        theirs = pl.ds(pl.multiple_of((1 - core) * HALF, HALF), HALF)
        for ref, rows in ((send_ref, theirs), (keep_ref, mine)):
            for at in range(0, padded, CHUNK):
                value = mm_t(w_kv[rows, :], dkv_ref[at : at + CHUNK, :])
                ref[:, at : at + CHUNK] = value.astype(BF)

    return run(
        body,
        [shaped((HALF, padded)), shaped((HALF, padded))],
        vmem=[dkv],
        hbm=weights,
        scratch=[pltpu.VMEM((D, D), BF)],
        copies=4,
        micros=4,
    )


def leave_plane(place, grads):
    return [place.swap_xy(grads[0], 1), place.swap_xy(grads[2], 2)]


def pass_on(grads, came, after):
    shape = grads[1].shape[1:]

    def body(stay0, came0, stay1, came1, *refs):
        out0, out1, held, sems = refs[-4:]
        copies = Copies(sems)
        for i, ref in enumerate((stay0, came0, stay1, came1)):
            copies.start(ref.at[1], held.at[i])
        copies.wait()
        out0[...] = add_up(held[0], held[1]).astype(BF)
        out1[...] = add_up(held[2], held[3]).astype(BF)

    return run(
        body,
        [shaped(shape), shaped(shape)],
        hbm=[grads[1], came[0], grads[3], came[1]],
        scratch=[pltpu.VMEM((4,) + shape, BF)],
        copies=4,
        micros=2,
        after=after,
    )


def cross_plane(place, onward):
    return [place.swap_xy(onward[0], 2), place.swap_xy(onward[1], 1)]


def column_blocks(grads, came, onward, attention, norm_terms=(), after=()):
    shape = onward[0].shape
    rows = shape[-2] // 2
    width = D if attention else 2 * D
    few = rows // 4
    extra = 16 if norm_terms else 0

    def body(*refs):
        terms_refs, refs = refs[: len(norm_terms)], refs[len(norm_terms) :]
        ins, outs, (held, shards, sems) = refs[:6], refs[-7:-3], refs[-3:]
        home, slots = column_slots()
        copies = Copies(sems)
        for i, ref in enumerate(ins):
            copies.start(ref if i % 3 == 2 else ref.at[0], held.at[i])
        copies.wait()
        sums = [add_up(held[3 * part], held[3 * part + 1], held[3 * part + 2]) for part in range(2)]
        for hi in range(2):
            for cs in range(2):
                here = slice(cs * rows, (cs + 1) * rows)
                if attention:
                    lanes = slice(hi * QUARTER, (hi + 1) * QUARTER)
                    lanes_two = slice(HALF + hi * QUARTER, HALF + (hi + 1) * QUARTER)
                    outs_rows = []
                    for p in range(4):
                        at = (2 * (p // 2) + hi) * 2 * few + cs * few
                        side = HALF + (p % 2) * QUARTER
                        outs_rows.append(sums[1][at : at + few, side : side + QUARTER])
                    value = jnp.concatenate(
                        [
                            sums[0][here, lanes],
                            sums[0][here, lanes_two],
                            sums[1][here, lanes],
                            jnp.concatenate(outs_rows, axis=0),
                        ],
                        axis=1,
                    )
                else:
                    value = jnp.concatenate([sums[0][hi, here], sums[1][hi, here]], axis=1)
                shards[2 * hi + cs, :rows] = value.astype(BF)
        if norm_terms:
            core, xy, _ = where_am_i()
            terms = add_up(*[ref[...] for ref in terms_refs])
            terms = jnp.concatenate([terms, jnp.zeros_like(terms)], axis=0).astype(BF)
            feature = lax.broadcasted_iota(jnp.int32, (D, D), 0)
            lane = lax.broadcasted_iota(jnp.int32, (D, D), 1)
            for hi in range(2):
                for cs in range(2):
                    offset = (2 * core + hi) * QUARTER + (2 * xy + cs) * few
                    pick = jnp.where((feature == lane + offset) & (lane < few), 1.0, 0.0)
                    shards[2 * hi + cs, rows:] = mm(terms, pick.astype(BF)).astype(BF)
        for k in range(4):
            outs[k][...] = shards[slots[k]]

    ins = [grads[1], came[0], onward[0], grads[3], came[1], onward[1]]
    return run(
        body,
        [shaped((rows + extra, width))] * 4,
        vmem=list(norm_terms),
        hbm=ins,
        after=after,
        scratch=[pltpu.VMEM((6,) + shape, BF), pltpu.VMEM((4, rows + extra, width), BF)],
        copies=6,
        micros=4,
    )


def sum_plain(place, grads, attention):
    wide, narrow = grads[1][0], grads[3][0]
    rows = D // place.dp
    if attention:
        value = jnp.stack([wide[:, :HALF], wide[:, HALF:], narrow[:, :HALF]], axis=1)
        value = value.reshape(place.dp, rows, 3, 2, QUARTER).transpose(3, 0, 1, 2, 4)
        value = value.reshape(2, place.dp, rows, 3 * QUARTER)
        outs = narrow[:, HALF:].reshape(2, 2, place.dp, rows // 4, 2, QUARTER)
        outs = outs.transpose(1, 2, 0, 4, 3, 5).reshape(2, place.dp, rows, QUARTER)
        value = jnp.concatenate([value, outs], axis=-1)
    else:
        value = jnp.concatenate(
            [wide.reshape(2, place.dp, rows, D), narrow.reshape(2, place.dp, rows, D)], axis=-1
        )
    whole = jnp.zeros((2,) + value.shape, F32)
    whole = lax.dynamic_update_index_in_dim(whole, value.astype(F32), place.core, 0)
    whole = whole.reshape((4 * place.dp,) + value.shape[2:])
    return lax.psum_scatter(whole, ("mp", "xy", "core"), scatter_dimension=0, tiled=False)


def from_quarters(value):
    few = value.shape[0] // 4
    return value.reshape(4, few, QUARTER).transpose(1, 0, 2).reshape(few, D)


def three_parts(value):
    terms = []
    for _ in range(3):
        term = lax.reduce_precision(value, 8, 7)
        terms.append(term.astype(BF))
        value = value - term
    return jnp.concatenate(terms)


def per_device(
    dp,
    mp,
    hidden_in,
    encoder_states,
    cotangent,
    self_qkv,
    self_out,
    cross_q,
    cross_kv,
    cross_out,
    fc_in,
    fc_out,
    ln_gain,
    ln_bias,
    token_lengths,
    audio_lengths,
    corpus_ids,
    corpus_weights,
):
    place = Place(dp, mp)
    length = hidden_in.shape[2]
    frames = encoder_states.shape[2]
    padded = -(-frames // CHUNK) * CHUNK
    rows = self_qkv.shape[0]

    first = ()
    unit = unit_shard(place, fc_in, fc_out)
    if place.fast:
        shard = attention_shard(self_qkv.transpose(1, 0, 2), self_out)
        first = (shard,)
        packed = pack_attention(place.column_out(shard), shard)
        w_self = spread(place, packed)
        encoder_states, unit, packed = lax.optimization_barrier((encoder_states, unit, packed))
        shard = attention_shard(
            jnp.concatenate([cross_kv.reshape(rows, -1), cross_q], axis=1), cross_out, w_self[1:3]
        )
        w_cross = spread(place, pack_attention(place.column_out(shard), shard))
    else:
        quarter = lambda w: w.reshape(-1, 4, QUARTER).transpose(1, 0, 2).reshape(-1, QUARTER)
        flat = lambda w: w.reshape(rows, -1)
        w_self = attention_plain(
            place, jnp.concatenate([flat(self_qkv), quarter(self_out)], axis=1)
        )
        w_cross = attention_plain(
            place, jnp.concatenate([flat(cross_kv), cross_q, quarter(cross_out)], axis=1)
        )

    w_units = gather_units(place, unit)

    turned = lambda value: value[:, 0].transpose(0, 2, 1)
    numbers = jnp.concatenate([token_lengths.T, audio_lengths.T, corpus_ids.T])
    blocks = input_blocks(
        turned(hidden_in),
        three_parts(jnp.concatenate([ln_gain, ln_bias])),
        numbers,
        first,
    )
    got = place.rows_in(blocks)
    hidden, norms, nums = prepare(got, place.swap_core(got), corpus_weights)

    encoded = lax.dynamic_index_in_dim(encoder_states[:, 0], place.micro, 0, keepdims=False)
    other = place.move(encoded, lambda xy, core, z: (xy, 1 - core, z) if core == z // 2 else None)
    encoded = jnp.where(place.home == place.core, encoded, other)
    encoded = jnp.pad(encoded, ((0, padded - frames), (0, 0)))

    et = turn(encoded)
    part1, at, qkv, qt, kt, ot1, lse1 = self_forward(hidden, norms, nums, w_self, (et,))
    other1 = place.swap_core(part1)
    got = place.rows_in(turned_blocks(turned(cotangent), (at,)))
    kv, kvt = cross_memory(encoded, w_cross)
    part2, h1, ct, q2, qt2, ot2, lse2 = cross_forward(
        hidden, part1, other1, norms, nums, kv, kvt, w_cross
    )
    other2 = place.swap_core(part2)
    cot = prepare_cotangent(got, place.swap_core(got), (part2,))
    part3, h2, mt, slope, it = units_forward(h1, part2, other2, norms, w_units)
    other3 = place.swap_core(part3)
    part, d3, e3, dz, terms3, out_a, out_b = units_backward(
        h2, part3, other3, norms, nums, cot, slope, w_units
    )
    other = place.swap_core(part)
    g_units = units_grads(place, mt, dz, it, e3)
    s_up, s_down = scatter_units(place, g_units)
    layer_got = place.rows_sent((out_a, out_b))
    layer_out = place.rows_joined((out_a, out_b), layer_got)
    part, d2, e2, dq2, dkv, terms2 = cross_backward(
        d3, h2, part, other, norms, nums, kv, kvt, q2, qt2, ot2, lse2, w_cross, layer_got
    )
    other = place.swap_core(part)
    keep, send = encoder_grad(dkv, w_cross)
    encoder_blocks = finish_encoder(keep, place.swap_core(send), frames)
    g_cross = attention_grads(place, et, dkv, ct, dq2, ot2, e2, encoder_blocks)
    encoder_got = place.rows_sent(encoder_blocks)
    if place.fast:
        came_cross = leave_plane(place, g_cross)
    part, d1, e1, dqk, dv, terms1 = self_backward(
        d2, h1, part, other, norms, nums, qkv, qt, kt, ot1, lse1, w_self, (g_cross[0],)
    )
    other = place.swap_core(part)
    passed = encoder_got
    if place.fast:
        passed = pass_on(g_cross, came_cross, [e1] + encoder_got)
    g_self = attention_grads(place, at, dqk, at, dv, ot1, e1, passed)
    if place.fast:
        came_self = leave_plane(place, g_self)
        cross_blocks = column_blocks(
            g_cross, came_cross, cross_plane(place, passed), True, (), (g_self[0],)
        )
        passed = (cross_blocks[0],)
    grad_encoder = place.rows_joined(encoder_blocks, encoder_got).astype(F32)
    terms, out_a, out_b = finish_hidden(
        d1, hidden, part, other, norms, terms1, terms2, terms3, passed
    )
    grad_hidden = place.rows_home((out_a, out_b)).astype(F32)

    few = D // (place.dp * place.mp)
    if place.fast:
        passed = pass_on(g_self, came_self, (terms,))
        onward_self = cross_plane(place, passed)
        terms = terms + place.swap_xy(terms, 1)
        s_cross = place.column_back(cross_blocks)
        s_self = place.column_back(
            column_blocks(
                g_self, came_self, onward_self, True, (terms, place.swap_xy(terms, 2))
            )
        )
        shares = s_self[rows : rows + 8, :few]
    else:
        s_cross = sum_plain(place, g_cross, True)
        s_self = sum_plain(place, g_self, True)
        terms = jnp.where(place.core == 0, terms, 0.0)
        terms = lax.psum(terms, AXES)
        shares = lax.dynamic_slice_in_dim(terms, (place.z * place.dp + place.d) * few, few, 1)
    s_self = s_self[:rows]
    return (
        layer_out,
        grad_hidden,
        grad_encoder,
        s_self[:, : 3 * QUARTER].reshape(rows, 3, QUARTER),
        from_quarters(s_self[:, 3 * QUARTER :]),
        s_cross[:, 2 * QUARTER : 3 * QUARTER],
        s_cross[:, : 2 * QUARTER].reshape(rows, 2, QUARTER),
        from_quarters(s_cross[:, 3 * QUARTER :]),
        s_up,
        s_down,
        shares[:4],
        shares[4:],
    )


def solution(mesh):
    dp, mp = mesh.shape["dp"], mesh.shape["mp"]
    finer = Mesh(mesh.devices.reshape(dp // 2, 2, mp), AXES)
    both = ("xy", "core")
    rows = P(None, both, None, "mp")
    columns = P(both, None, "mp")
    pairs = P(both, "mp")
    units = P(("mp",) + both, None)
    each = P(None, both)
    return jax.shard_map(
        partial(per_device, dp, mp),
        mesh=finer,
        in_specs=(
            rows,
            P(None, both, None, None),
            rows,
            columns,
            units,
            pairs,
            columns,
            units,
            pairs,
            units,
            P(None, "mp"),
            P(None, "mp"),
            each,
            each,
            each,
            P(),
        ),
        out_specs=(
            rows,
            rows,
            rows,
            columns,
            units,
            pairs,
            columns,
            units,
            pairs,
            units,
            P(None, ("mp",) + both),
            P(None, ("mp",) + both),
        ),
        check_vma=False,
    )
```

```python
from functools import partial

import jax
import jax.numpy as jnp
from jax import lax
from jax.experimental import pallas as pl
from jax.experimental.pallas import tpu as pltpu
from jax.sharding import Mesh, PartitionSpec as P

D = 768
HALF = 384
QUARTER = 192
HEAD_DIM = 64
HEADS = 6
CHUNK = 256
BF = jnp.bfloat16
F32 = jnp.float32
AXES = ("xy", "core", "mp")
CHIPS = ("xy", "mp")
VMEM = pl.BlockSpec(memory_space=pltpu.VMEM)
SMEM = pl.BlockSpec(memory_space=pltpu.SMEM)
ANY = pl.BlockSpec(memory_space=pl.ANY)


def mm(left, right):
    return jnp.dot(left, right, preferred_element_type=F32)


def mm_t(left, right):
    return lax.dot_general(left, right, (((1,), (1,)), ((), ())), preferred_element_type=F32)


def shaped(shape, dtype=BF):
    return jax.ShapeDtypeStruct(shape, dtype)


def room(shape, dtype):
    item = jnp.dtype(dtype).itemsize
    shape = (1, 1) + tuple(shape)
    tile = 32 // item
    size = item * (-(-shape[-1] // 128) * 128) * (-(-shape[-2] // tile) * tile)
    for extent in shape[:-2]:
        size *= extent
    return size


def run(body, outs, vmem=(), hbm=(), smem=(), scratch=(), copies=0, micros=2, after=()):
    args = tuple(smem) + tuple(vmem) + tuple(hbm)
    count = len(args)
    scratch = list(scratch)
    if copies:
        scratch.append(pltpu.SemaphoreType.DMA((copies,)))
    need = sum(room(a.shape, a.dtype) for a in tuple(vmem) + tuple(outs))
    need += sum(room(a.shape, a.dtype) for a in scratch if a.memory_space == pltpu.VMEM)
    need = min(need + 12 * 1024 * 1024, 60 * 1024 * 1024)
    moved = sum(a.size * a.dtype.itemsize for a in args) + sum(
        o.size * o.dtype.itemsize for o in outs
    )
    return pl.pallas_call(
        lambda *refs: body(*refs[:count], *refs[count + len(after) :]),
        out_shape=tuple(outs),
        in_specs=[SMEM] * len(smem) + [VMEM] * len(vmem) + [ANY] * (len(hbm) + len(after)),
        out_specs=(VMEM,) * len(outs),
        scratch_shapes=scratch,
        compiler_params=pltpu.CompilerParams(vmem_limit_bytes=need),
        cost_estimate=pl.CostEstimate(
            flops=int(micros * 1.15e9), bytes_accessed=moved, transcendentals=0
        ),
    )(*args, *after)


class Copies:
    def __init__(self, sems):
        self.sems, self.open = sems, []

    def start(self, source, target):
        copy = pltpu.make_async_copy(source, target, self.sems.at[len(self.open)])
        copy.start()
        self.open.append(copy)

    def wait(self):
        for copy in self.open:
            copy.wait()


def where_am_i():
    return lax.axis_index("core"), lax.axis_index("xy"), lax.axis_index("mp")


class Place:
    def __init__(self, dp, mp):
        self.dp, self.mp = dp, mp
        self.chips = dp // 2
        self.fast = self.chips == 4
        self.z = lax.axis_index("mp")
        self.core = lax.axis_index("core")
        self.xy = lax.axis_index("xy")
        self.d = 2 * self.xy + self.core
        self.micro = self.z % 2
        self.home = self.z // 2

    def move(self, value, route):
        pairs = []
        for xy in range(self.chips):
            for core in range(2):
                for z in range(self.mp):
                    target = route(xy, core, z)
                    if target is not None:
                        txy, tcore, tz = target
                        pairs.append(
                            ((2 * xy + core) * self.mp + z, (2 * txy + tcore) * self.mp + tz)
                        )
        return lax.ppermute(value, AXES, pairs)

    def swap_core(self, value):
        return self.move(value, lambda xy, core, z: (xy, 1 - core, z))

    def swap_xy(self, value, bit):
        return self.move(value, lambda xy, core, z: (xy ^ bit, core, z))

    def swap_z(self, value, bit):
        return self.move(value, lambda xy, core, z: (xy, core, z ^ bit))

    def column_routes(self):
        def route(step, xy, core, z):
            user, j = z // 2, z % 2
            home = core == user
            near = lambda i: (xy, user, 2 * user + i)
            far = lambda i: (xy, user, 2 * (1 - user) + i)
            if step == 0:
                return near(1 - j) if home else far(1 - j)
            if step == 1:
                return far(j) if home else near(j)
            if step == 2:
                return far(1 - j) if home else near(1 - j)
            return None if home else far(j)

        return [partial(route, step) for step in range(4)]

    def column_out(self, shard):
        return [self.move(shard, route) for route in self.column_routes()]

    def column_back(self, blocks):
        got = []
        for block, route in zip(blocks, self.column_routes()):
            turned = {}
            for xy in range(self.chips):
                for core in range(2):
                    for z in range(self.mp):
                        target = route(xy, core, z)
                        if target is not None:
                            turned[target] = (xy, core, z)
            got.append(self.move(block, lambda xy, core, z: turned.get((xy, core, z))))
        at_home = self.core == self.home
        return add_up(got[0], got[1], got[2], jnp.where(at_home, blocks[3], got[3]))

    def rows_in(self, blocks):
        def route(k, xy, core, z):
            target = (xy, z // 2, 2 * core + (z + k) % 2)
            return None if target == (xy, core, z) else target

        got = [self.move(block, partial(route, k)) for k, block in enumerate(blocks)]
        return jnp.stack([jnp.where(self.core == self.home, blocks[0], got[0]), got[1]])

    def rows_home(self, blocks):
        return self.rows_joined(blocks, self.rows_sent(blocks))

    def rows_sent(self, blocks):
        def route(k, xy, core, z):
            target = (xy, z // 2, 2 * core + (z % 2 - k) % 2)
            return None if target == (xy, core, z) else target

        return [self.move(block, partial(route, k)) for k, block in enumerate(blocks)]

    def rows_joined(self, blocks, got):
        got = [jnp.where(self.core == self.home, blocks[0], got[0]), got[1]]
        even = self.z % 2 == 0
        both = jnp.stack([jnp.where(even, got[0], got[1]), jnp.where(even, got[1], got[0])])
        return both[:, None].transpose(0, 1, 3, 2)


def norm(hidden):
    center = jnp.mean(hidden, axis=-1, keepdims=True)
    spread = jnp.mean(hidden * hidden, axis=-1, keepdims=True) - center * center
    inverse = lax.rsqrt(spread + 1e-05)
    return (hidden - center) * inverse, inverse


def norm_back(grad, unit, inverse, gain):
    scaled = grad * gain
    first = jnp.mean(scaled, axis=-1, keepdims=True)
    second = jnp.mean(scaled * unit, axis=-1, keepdims=True)
    terms = jnp.concatenate(
        [jnp.sum(grad * unit, axis=0, keepdims=True), jnp.sum(grad, axis=0, keepdims=True)], axis=0
    )
    return inverse * (scaled - first - unit * second), terms


def add_up(*terms):
    total = terms[0].astype(F32)
    for term in terms[1:]:
        total = total + term.astype(F32)
    return total


def input_blocks(hidden, terms, numbers, after=()):
    _, width, length = hidden.shape
    total = width + 32

    def body(numbers_ref, hidden_ref, terms_ref, *outs):
        _, _, z = where_am_i()
        lanes = lax.broadcasted_iota(jnp.int32, (8, length), 1)
        for k in range(2):
            micro = (z + k) % 2
            outs[k][0:width] = hidden_ref[micro]
            tok, aud = numbers_ref[0, micro], numbers_ref[1, micro]
            row = jnp.where(lanes == 0, tok // 256, jnp.where(lanes == 1, tok % 256, 0))
            row = jnp.where(lanes == 2, aud // 256, jnp.where(lanes == 3, aud % 256, row))
            row = jnp.where(lanes == 4, numbers_ref[2, micro], row)
            wide = jnp.concatenate(
                [terms_ref[...].astype(F32), jnp.zeros((24, length - width), F32)], axis=1
            )
            outs[k][width:total] = jnp.concatenate([wide, row.astype(F32)], axis=0).astype(BF)

    return run(
        body,
        [shaped((total, length))] * 2,
        smem=[numbers],
        vmem=[hidden, terms],
        micros=1,
        after=after,
    )


def turned_blocks(value, after=()):
    _, width, length = value.shape

    def body(ref, first_ref, second_ref):
        _, _, z = where_am_i()
        first_ref[...] = ref[z % 2]
        second_ref[...] = ref[(z + 1) % 2]

    return run(body, [shaped((width, length))] * 2, vmem=[value], micros=1, after=after)


def bring_blocks(copies, own_ref, other_ref, wide):
    core, _, z = where_am_i()
    found = []
    for k in range(2):
        slot = (z % 2 + k) % 2
        for ref, user in ((own_ref, core), (other_ref, 1 - core)):
            block = 2 * user + slot
            here = pl.ds(pl.multiple_of(block * QUARTER, QUARTER), QUARTER)
            copies.start(ref.at[k, pl.ds(0, QUARTER)], wide.at[here])
            found.append((ref.at[k], block))
    return found


def prepare_cotangent(own, other, after=()):
    length = own.shape[2]

    def body(own_ref, other_ref, cot_ref, wide, sems):
        copies = Copies(sems)
        bring_blocks(copies, own_ref, other_ref, wide)
        copies.wait()
        cot_ref[...] = wide[...].T

    return run(
        body,
        [shaped((length, D))],
        hbm=[own, other],
        scratch=[pltpu.VMEM((D, length), BF)],
        copies=4,
        micros=3,
        after=after,
    )[0]


def prepare(own, other, corpus_weights):
    length = own.shape[2]

    def body(
        weights_ref, own_ref, other_ref, hidden_ref, norms_ref, nums_ref, wide, extra, sems
    ):
        copies = Copies(sems)
        for ref, block in bring_blocks(copies, own_ref, other_ref, wide):
            copies.start(ref.at[pl.ds(QUARTER, 32)], extra.at[block])
        copies.wait()
        hidden_ref[...] = wide[...].T
        parts = [extra[b].astype(F32) for b in range(4)]
        norms_ref[...] = jnp.concatenate(
            [(e[0:8] + e[8:16] + e[16:24])[:, :QUARTER] for e in parts], axis=1
        )
        row = parts[0][24:25]
        tok = 256.0 * row[:, 0:1] + row[:, 1:2]
        aud = 256.0 * row[:, 2:3] + row[:, 3:4]
        weights = weights_ref[...]
        places = lax.broadcasted_iota(jnp.int32, weights.shape, 1).astype(F32)
        weight = jnp.sum(jnp.where(places == row[:, 4:5], weights, 0.0), axis=1, keepdims=True)
        index = lax.broadcasted_iota(jnp.int32, (8, 128), 0)
        nums_ref[...] = jnp.where(index == 0, tok, jnp.where(index == 1, aud, weight))

    return run(
        body,
        [shaped((length, D)), shaped((8, D), F32), shaped((8, 128), F32)],
        vmem=[corpus_weights.reshape(1, -1)],
        hbm=[own, other],
        scratch=[pltpu.VMEM((D, length), BF), pltpu.VMEM((4, 32, length), BF)],
        copies=8,
        micros=3,
    )


def quarters(value):
    return jnp.concatenate([value[:, p * QUARTER : (p + 1) * QUARTER] for p in range(4)], axis=0)


def attention_shard(self_qkv, self_out, cross_kv, cross_q, cross_out):
    rows = cross_q.shape[0]

    def body(qkv_ref, out_ref, kv_ref, q_ref, cout_ref, shard_ref):
        out = quarters(out_ref[...].astype(F32)).astype(BF)
        cout = quarters(cout_ref[...].astype(F32)).astype(BF)
        shard_ref[...] = jnp.concatenate(
            [qkv_ref[j] for j in range(3)] + [out, kv_ref[...], q_ref[...], cout], axis=1
        )

    return run(
        body,
        [shaped((rows, 2 * D))],
        vmem=[self_qkv.transpose(1, 0, 2), self_out, cross_kv.reshape(rows, -1), cross_q, cross_out],
        micros=2,
    )[0]


def column_slots():
    core, _, z = where_am_i()
    j = z % 2
    home = 1 - jnp.abs(z // 2 - core)
    same = core + (1 - 2 * core) * (1 - home)
    return home == 1, (2 * (1 - j) + same, 2 * j + 1 - same, 2 * (1 - j) + 1 - same, 2 * j + same)


def bring_column(part_refs, own_ref, shards, sems):
    home, slots = column_slots()
    copies = Copies(sems)
    for k in range(3):
        copies.start(part_refs[k], shards.at[slots[k]])

    @pl.when(home)
    def _():
        copy = pltpu.make_async_copy(own_ref, shards.at[slots[3]], sems.at[3])
        copy.start()
        copy.wait()

    @pl.when(jnp.logical_not(home))
    def _():
        copy = pltpu.make_async_copy(part_refs[3], shards.at[slots[3]], sems.at[3])
        copy.start()
        copy.wait()

    copies.wait()


def pack_attention(parts, own):
    rows = own.shape[0]
    few = rows // 4

    def body(*refs):
        part_refs, own_ref, (out_ref, shards, sems) = refs[:4], refs[4], refs[5:]
        bring_column(part_refs, own_ref, shards, sems)
        for which in range(2):
            for cs in range(2):
                low, high = shards[cs], shards[2 + cs]

                def both(at):
                    at = at + which * D
                    return [low[:, at : at + QUARTER], high[:, at : at + QUARTER]]

                here = pl.ds(cs * rows, rows)
                out_ref[0, which, here, :] = jnp.concatenate(both(0) + both(QUARTER), axis=1)
                out_ref[1, which, here, 0:HALF] = jnp.concatenate(both(HALF), axis=1)
            at = 3 * QUARTER + which * D
            outs = [shards[i, :, at : at + QUARTER].astype(F32) for i in range(4)]
            stack = []
            for q in range(2):
                for i in range(4):
                    left = outs[i][2 * q * few : (2 * q + 1) * few]
                    right = outs[i][(2 * q + 1) * few : (2 * q + 2) * few]
                    stack.append(jnp.concatenate([left, right], axis=1))
            out_ref[1, which, :, HALF:D] = jnp.concatenate(stack, axis=0).astype(BF)

    return run(
        body,
        [shaped((2, 2, 2 * rows, D))],
        hbm=list(parts) + [own],
        scratch=[pltpu.VMEM((4, rows, 2 * D), BF)],
        copies=4,
        micros=2,
    )[0]


def unit_shard(place, fc_in, fc_out):
    rows = fc_in.shape[0]
    both = fc_in.reshape(rows, place.chips, 2, rows).transpose(2, 0, 1, 3).reshape(2, rows, HALF)
    kept = lax.dynamic_index_in_dim(both, place.core, 0, keepdims=False)
    sent = lax.dynamic_index_in_dim(both, 1 - place.core, 0, keepdims=False)
    came = place.swap_core(sent)
    first = place.core == 0
    left = jnp.concatenate([jnp.where(first, kept, came), jnp.where(first, came, kept)])
    right = jnp.concatenate([fc_out[:, :HALF], fc_out[:, HALF:]])
    return jnp.concatenate([left, right], axis=1)


def gather_units(place, shard):
    whole = lax.all_gather(shard, CHIPS, axis=0)
    if place.fast:
        return [whole]
    rows = shard.shape[0] // 2
    whole = whole.reshape(place.chips, place.mp, 2 * rows, D)
    up = whole[..., :HALF].transpose(0, 2, 1, 3).reshape(D, 2 * D)
    down = whole[..., HALF:].reshape(place.chips, place.mp, 2, rows, HALF)
    return [up, down.transpose(1, 0, 3, 2, 4).reshape(2 * D, D)]


def scatter_units(place, grads):
    axes = "mp" if place.fast else CHIPS
    total = lax.psum_scatter(grads, axes, scatter_dimension=0, tiled=False)
    rows = total.shape[0] // 2
    kept = lax.dynamic_slice_in_dim(total, place.core * rows, rows, 0)
    sent = lax.dynamic_slice_in_dim(total[:, :HALF], (1 - place.core) * rows, rows, 0)
    came = place.swap_core(sent)
    kept = kept[:, :HALF]
    first = place.core == 0
    both = jnp.stack([jnp.where(first, kept, came), jnp.where(first, came, kept)])
    both = both.reshape(2, rows, place.chips, rows).transpose(1, 2, 0, 3).reshape(rows, D)
    down = jnp.concatenate([total[:rows, HALF:], total[rows:, HALF:]], axis=1)
    return both.astype(F32), down.astype(F32)


def spread(place, own):
    from_x = place.swap_xy(own, 1)
    from_y = place.swap_xy(own, 2)
    far_one = place.swap_xy(from_y[1], 1)
    far_zero = place.swap_xy(from_x[0], 2)
    return [own, from_x, from_y, far_zero, far_one]


def piece_views(refs, message, which, xy):
    own, from_x, from_y, far_zero, far_one = refs
    return [
        (own.at[which, message], xy),
        (from_x.at[which, message], xy ^ 1),
        (from_y.at[which, message], xy ^ 2),
        ((far_zero, far_one)[which].at[message], xy ^ 3),
    ]


def load_wide(copies, refs, message, which, xy, target, columns=None):
    if len(refs) != 5:
        copies.start(refs[which], target)
        return
    for view, chip in piece_views(refs, message, which, xy):
        rows = view.shape[0]
        if columns is not None:
            view = view.at[:, pl.ds(0, columns)]
        copies.start(view, target.at[pl.ds(pl.multiple_of(chip * rows, 16), rows)])


def load_out(copies, refs, message, xy, target):
    if len(refs) != 5:
        copies.start(refs[2], target)
        return
    for view, chip in piece_views(refs, message, 1, xy):
        rows = view.shape[0] // 4
        for q in range(2):
            for hi in range(2):
                copies.start(
                    view.at[pl.ds((2 * q + hi) * rows, rows), pl.ds(HALF, HALF)],
                    target.at[q, pl.ds(pl.multiple_of(hi * QUARTER + chip * rows, 16), rows)],
                )


def load_up(copies, refs, w_up):
    if len(refs) == 2:
        copies.start(refs[0], w_up)
        return
    (whole,) = refs
    count, rows, _ = whole.shape
    for i in range(count):
        xy, z = i // 4, i % 4
        copies.start(
            whole.at[i, :, pl.ds(0, HALF)], w_up.at[pl.ds(rows * xy, rows), pl.ds(z * HALF, HALF)]
        )


def load_down(copies, refs, w_down):
    if len(refs) == 2:
        copies.start(refs[1], w_down)
        return
    (whole,) = refs
    count, rows, _ = whole.shape
    rows = rows // 2
    for i in range(count):
        xy, z = i // 4, i % 4
        for q in range(2):
            copies.start(
                whole.at[i, pl.ds(q * rows, rows), pl.ds(HALF, HALF)],
                w_down.at[pl.ds(z * HALF + xy * rows, rows), pl.ds(q * HALF, HALF)],
            )


ATTENTION_COPIES = 4 + 4 + 16
UP_COPIES = 16
DOWN_COPIES = 32


def gather_plain(place, shard):
    whole = lax.all_gather(shard, ("mp", "xy", "core"), axis=0)
    whole = whole.reshape((2, 2, place.dp) + shard.shape)
    return lax.dynamic_index_in_dim(whole, place.core, 0, keepdims=False)


def attention_plain(place, shard):
    mine = gather_plain(place, shard)
    rows = shard.shape[0]

    def columns(at, count):
        value = mine[..., at : at + count * QUARTER].reshape(2, D, count, QUARTER)
        return value.transpose(1, 2, 0, 3).reshape(D, count * HALF)

    out = mine[..., 3 * QUARTER :].reshape(2, place.dp, 2, 2, rows // 4, QUARTER)
    out = out.transpose(2, 0, 1, 4, 3, 5).reshape(2, HALF, HALF)
    return [columns(0, 2), columns(HALF, 1), out]


def head_rows(h):
    return pl.ds(pl.multiple_of(h * HEAD_DIM, HEAD_DIM), HEAD_DIM)


def low_parts(value):
    parts = []
    for _ in range(3):
        part = value.astype(BF)
        parts.append(part)
        value = value - part.astype(F32)
    return parts


def widened(count):
    return lambda rows: (
        lax.broadcasted_iota(jnp.int32, (rows, HEAD_DIM), 1) < count
    ).astype(F32).astype(BF)


def below(head, rows):
    blank = jnp.zeros((HEAD_DIM - len(rows), head.shape[1]), F32)
    rest = jnp.concatenate([row.astype(F32) for row in rows] + [blank], axis=0)
    return jnp.concatenate([head, rest.astype(BF)], axis=0)


def project(left, pair_ref):
    return jnp.concatenate([mm(left, pair_ref[0]), mm(left, pair_ref[1])], axis=1)


def project_t(left, pair_ref):
    return mm_t(left[:, :HALF], pair_ref[0]) + mm_t(left[:, HALF:], pair_ref[1])


def self_forward(hidden, norms, nums, weights, after=()):
    length = hidden.shape[0]

    def body(hidden_ref, norms_ref, nums_ref, *refs):
        w_refs, refs = refs[: len(weights)], refs[len(weights) :]
        part_ref, at_ref, qkv_ref, qt_ref, kt_ref, ot_ref, lse_ref = refs[:7]
        w_qk, w_v, w_out, vt, heads, bias, sems = refs[7:]
        _, xy, _ = where_am_i()
        copies = Copies(sems)
        load_wide(copies, w_refs, 0, 0, xy, w_qk)
        load_wide(copies, w_refs, 0, 1, xy, w_v, HALF)
        load_out(copies, w_refs, 0, xy, w_out)
        unit, _ = norm(hidden_ref[...].astype(F32))
        a = (unit * norms_ref[0:1] + norms_ref[4:5]).astype(BF)
        at_ref[...] = a.T
        keys = lax.broadcasted_iota(jnp.int32, (length, length), 0)
        queries = lax.broadcasted_iota(jnp.int32, (length, length), 1)
        allowed = (keys <= queries) & (keys.astype(F32) < nums_ref[0:1, 0:1])
        bias[...] = jnp.where(allowed, 0.0, -1e30)
        copies.wait()
        qk = mm(a, w_qk[...])
        q = (qk[:, :HALF].astype(BF).astype(F32) * HEAD_DIM ** (-0.5)).astype(BF)
        k = qk[:, HALF:].astype(BF)
        v = mm(a, w_v[...]).astype(BF)
        qkv_ref[:, 0:HALF] = q
        qkv_ref[:, HALF : 2 * HALF] = k
        qkv_ref[:, 2 * HALF :] = v
        qt_ref[...] = q.T
        kt_ref[...] = k.T
        vt[...] = v.T
        for h in range(HEADS):
            heads[h] = k[:, h * HEAD_DIM : (h + 1) * HEAD_DIM]

        def head(h, carry):
            s = mm(heads[h], qt_ref[head_rows(h), :]) + bias[...]
            top = jnp.max(s, axis=0, keepdims=True)
            p = jnp.exp(s - top)
            total = jnp.sum(p, axis=0, keepdims=True)
            o = mm(vt[head_rows(h), :], p.astype(BF))
            ot_ref[head_rows(h), :] = (o / total).astype(BF)
            lse_ref[h] = top + jnp.log(total)
            return carry

        lax.fori_loop(0, HEADS, head, 0)
        part_ref[...] = project(ot_ref[...].T, w_out).astype(BF)

    return run(
        body,
        [
            shaped((length, D)),
            shaped((D, length)),
            shaped((length, 3 * HALF)),
            shaped((HALF, length)),
            shaped((HALF, length)),
            shaped((HALF, length)),
            shaped((HEADS, 1, length), F32),
        ],
        vmem=[hidden, norms, nums],
        hbm=weights,
        scratch=[
            pltpu.VMEM((D, D), BF),
            pltpu.VMEM((D, HALF), BF),
            pltpu.VMEM((2, HALF, HALF), BF),
            pltpu.VMEM((HALF, length), BF),
            pltpu.VMEM((HEADS, length, HEAD_DIM), BF),
            pltpu.VMEM((length, length), F32),
        ],
        copies=ATTENTION_COPIES,
        micros=10,
        after=after,
    )


def turn(value, after=()):
    rows, columns = value.shape

    def body(ref, out_ref):
        for at in range(0, rows, CHUNK):
            out_ref[:, at : at + CHUNK] = ref[at : at + CHUNK, :].T

    return run(body, [shaped((columns, rows))], vmem=[value], micros=4, after=after)[0]


def cross_memory(encoded, weights):
    frames = encoded.shape[0]

    def body(enc_ref, *refs):
        w_refs, refs = refs[: len(weights)], refs[len(weights) :]
        kv_ref, kvt_ref, w_kv, sems = refs
        _, xy, _ = where_am_i()
        copies = Copies(sems)
        load_wide(copies, w_refs, 1, 0, xy, w_kv)
        copies.wait()

        def step(i, carry):
            here = pl.ds(pl.multiple_of(i * CHUNK, CHUNK), CHUNK)
            kv = mm(enc_ref[here, :], w_kv[...]).astype(BF)
            kv_ref[here, :] = kv
            kvt_ref[:, here] = kv.T
            return carry

        lax.fori_loop(0, frames // CHUNK, step, 0)

    return run(
        body,
        [shaped((frames, D)), shaped((D, frames))],
        vmem=[encoded],
        hbm=weights,
        scratch=[pltpu.VMEM((D, D), BF)],
        copies=4,
        micros=6,
    )


def residual(hidden_ref, mine_ref, other_ref):
    return hidden_ref[...].astype(F32) + (mine_ref[...].astype(F32) + other_ref[...].astype(F32))


def cross_forward(hidden, mine, other, norms, nums, kv, kvt, weights):
    length = hidden.shape[0]
    frames = kv.shape[0]

    def body(hidden_ref, mine_ref, other_ref, norms_ref, nums_ref, kv_ref, kvt_ref, *refs):
        w_refs, refs = refs[: len(weights)], refs[len(weights) :]
        part_ref, h_ref, ct_ref, q_ref, qt_ref, ot_ref, lse_ref = refs[:7]
        w_q, w_out, heads, values_t, scores, sems = refs[7:]
        _, xy, _ = where_am_i()
        copies = Copies(sems)
        load_wide(copies, w_refs, 1, 1, xy, w_q, HALF)
        load_out(copies, w_refs, 1, xy, w_out)
        h1 = residual(hidden_ref, mine_ref, other_ref)
        h_ref[...] = h1
        unit, _ = norm(h1)
        c = (unit * norms_ref[1:2] + norms_ref[5:6]).astype(BF)
        ct_ref[...] = c.T
        frame = lax.broadcasted_iota(jnp.int32, (frames, HEAD_DIM), 0).astype(F32)
        lane = lax.broadcasted_iota(jnp.int32, (frames, HEAD_DIM), 1)
        mask = jnp.where(frame < nums_ref[1:2, 0:1], 0.0, -1e30)
        beside = jnp.where(lane == 0, mask, 0.0).astype(BF)
        one = lax.broadcasted_iota(jnp.int32, (16, frames), 0)
        one = jnp.where(one == 0, 1.0, 0.0).astype(BF)
        for h in range(HEADS):
            keys = kv_ref[:, h * HEAD_DIM : (h + 1) * HEAD_DIM]
            heads[h] = jnp.concatenate([keys, beside], axis=1)
            values = kvt_ref[HALF + h * HEAD_DIM : HALF + (h + 1) * HEAD_DIM, :]
            values_t[h] = jnp.concatenate([values, one], axis=0)
        copies.wait()
        q = mm(c, w_q[...]).astype(BF)
        q = (q.astype(F32) * HEAD_DIM ** (-0.5)).astype(BF)
        q_ref[...] = q
        qt_ref[...] = q.T
        ones = jnp.ones((1, length), F32)

        def head(h, carry):
            qt = below(qt_ref[head_rows(h), :], [ones])
            top = None
            for at in range(0, frames, CHUNK):
                s = mm(heads[h, at : at + CHUNK], qt)
                scores[at : at + CHUNK] = s
                high = jnp.max(s, axis=0, keepdims=True)
                top = high if top is None else jnp.maximum(top, high)
            o = None
            for at in range(0, frames, CHUNK):
                p = jnp.exp(scores[at : at + CHUNK] - top).astype(BF)
                more = mm(values_t[h, :, at : at + CHUNK], p)
                o = more if o is None else o + more
            total = o[HEAD_DIM : HEAD_DIM + 1]
            ot_ref[head_rows(h), :] = (o[:HEAD_DIM] / total).astype(BF)
            lse_ref[h] = top + jnp.log(total)
            return carry

        lax.fori_loop(0, HEADS, head, 0)
        part_ref[...] = project(ot_ref[...].T, w_out).astype(BF)

    return run(
        body,
        [
            shaped((length, D)),
            shaped((length, D), F32),
            shaped((D, length)),
            shaped((length, HALF)),
            shaped((HALF, length)),
            shaped((HALF, length)),
            shaped((HEADS, 1, length), F32),
        ],
        vmem=[hidden, mine, other, norms, nums, kv, kvt],
        hbm=weights,
        scratch=[
            pltpu.VMEM((D, HALF), BF),
            pltpu.VMEM((2, HALF, HALF), BF),
            pltpu.VMEM((HEADS, frames, 2 * HEAD_DIM), BF),
            pltpu.VMEM((HEADS, HEAD_DIM + 16, frames), BF),
            pltpu.VMEM((frames, length), F32),
        ],
        copies=4 + 16,
        micros=10,
    )


def units_forward(hidden, mine, other, norms, weights):
    length = hidden.shape[0]

    def body(hidden_ref, mine_ref, other_ref, norms_ref, *refs):
        w_refs, refs = refs[: len(weights)], refs[len(weights) :]
        part_ref, h_ref, mt_ref, slope_ref, it_ref = refs[:5]
        w_up, w_down, inner, late_sems, sems = refs[5:]
        _, xy, _ = where_am_i()
        copies = Copies(sems)
        load_up(copies, w_refs, w_up)
        late = Copies(late_sems)
        load_down(late, w_refs, w_down)
        h2 = residual(hidden_ref, mine_ref, other_ref)
        h_ref[...] = h2
        unit, _ = norm(h2)
        m = (unit * norms_ref[2:3] + norms_ref[6:7]).astype(BF)
        mt_ref[...] = m.T
        copies.wait()
        for at in range(0, 2 * D, CHUNK):
            here = slice(at, at + CHUNK)
            z = mm(m, w_up[:, here])
            share = 0.5 * (1.0 + lax.erf(z * 0.7071067811865476))
            slope = share + z * (0.3989422804014327 * jnp.exp(-0.5 * z * z))
            value = (z * share).astype(BF)
            inner[:, here] = value
            it_ref[here, :] = value.T
            slope_ref[:, here] = slope.astype(BF)
        late.wait()
        for at in range(0, D, CHUNK):
            part_ref[:, at : at + CHUNK] = mm(inner[...], w_down[:, at : at + CHUNK]).astype(BF)

    return run(
        body,
        [
            shaped((length, D)),
            shaped((length, D), F32),
            shaped((D, length)),
            shaped((length, 2 * D)),
            shaped((2 * D, length)),
        ],
        vmem=[hidden, mine, other, norms],
        hbm=weights,
        scratch=[
            pltpu.VMEM((D, 2 * D), BF),
            pltpu.VMEM((2 * D, D), BF),
            pltpu.VMEM((length, 2 * D), BF),
            pltpu.SemaphoreType.DMA((DOWN_COPIES,)),
        ],
        copies=UP_COPIES,
        micros=9,
    )


def store_blocks(value, blocks, first_ref, second_ref):
    core, _, z = where_am_i()
    for b in range(4):
        blocks[b] = value[:, b * QUARTER : (b + 1) * QUARTER]
    first_ref[...] = blocks[2 * core + z % 2].T
    second_ref[...] = blocks[2 * core + (z + 1) % 2].T


def units_backward(hidden, mine, other, norms, nums, cot, slope, weights):
    length = hidden.shape[0]

    def body(hidden_ref, mine_ref, other_ref, norms_ref, nums_ref, cot_ref, slope_ref, *refs):
        w_refs, refs = refs[: len(weights)], refs[len(weights) :]
        part_ref, d_ref, e_ref, dz_ref, terms_ref, first_ref, second_ref = refs[:7]
        w_up, w_down, blocks, late_sems, sems = refs[7:]
        _, xy, _ = where_am_i()
        copies = Copies(sems)
        load_down(copies, w_refs, w_down)
        late = Copies(late_sems)
        load_up(late, w_refs, w_up)
        unit, inverse = norm(residual(hidden_ref, mine_ref, other_ref))
        final = (unit * norms_ref[3:4] + norms_ref[7:8]).astype(BF)
        store_blocks(final, blocks, first_ref, second_ref)
        live = lax.broadcasted_iota(jnp.int32, (length, 1), 0).astype(F32) < nums_ref[0:1, 0:1]
        grad = cot_ref[...].astype(F32) * jnp.where(live, nums_ref[2:3, 0:1], 0.0)
        d3, terms = norm_back(grad, unit, inverse, norms_ref[3:4])
        d_ref[...] = d3
        terms_ref[...] = terms
        e = d3.astype(BF)
        e_ref[...] = e
        copies.wait()
        for at in range(0, 2 * D, CHUNK):
            here = slice(at, at + CHUNK)
            d_inner = mm_t(e, w_down[here, :])
            dz_ref[:, here] = (slope_ref[:, here].astype(F32) * d_inner).astype(BF)
        late.wait()
        for at in range(0, D, CHUNK):
            out = mm_t(dz_ref[...], w_up[at : at + CHUNK, :])
            part_ref[:, at : at + CHUNK] = out.astype(BF)

    return run(
        body,
        [
            shaped((length, D)),
            shaped((length, D), F32),
            shaped((length, D)),
            shaped((length, 2 * D)),
            shaped((2, D), F32),
            shaped((QUARTER, length)),
            shaped((QUARTER, length)),
        ],
        vmem=[hidden, mine, other, norms, nums, cot, slope],
        hbm=weights,
        scratch=[
            pltpu.VMEM((D, 2 * D), BF),
            pltpu.VMEM((2 * D, D), BF),
            pltpu.VMEM((4, length, QUARTER), BF),
            pltpu.SemaphoreType.DMA((UP_COPIES,)),
        ],
        copies=DOWN_COPIES,
        micros=10,
    )


def step_back(d_ref, hidden_ref, mine_ref, other_ref, gain):
    unit, inverse = norm(hidden_ref[...].astype(F32))
    grad = mine_ref[...].astype(F32) + other_ref[...].astype(F32)
    part, terms = norm_back(grad, unit, inverse, gain)
    return d_ref[...] + part, terms


def cross_backward(
    d, hidden, mine, other, norms, nums, kv, kvt, q, qt, ot, lse, weights, after=()
):
    length = hidden.shape[0]
    frames = kv.shape[0]

    def body(
        d_ref, hidden_ref, mine_ref, other_ref, norms_ref, nums_ref, kv_ref, kvt_ref, q_ref,
        qt_ref, ot_ref, lse_ref, *refs
    ):
        w_refs, refs = refs[: len(weights)], refs[len(weights) :]
        part_ref, d_out_ref, e_ref, dq_ref, dkv_ref, terms_ref = refs[:6]
        w_q, w_out, keys, values, queries, grads, dot_t, dk_h, dv_h, dqt, sems = refs[6:]
        _, xy, _ = where_am_i()
        copies = Copies(sems)
        load_wide(copies, w_refs, 1, 1, xy, w_q, HALF)
        load_out(copies, w_refs, 1, xy, w_out)
        d2, terms = step_back(d_ref, hidden_ref, mine_ref, other_ref, norms_ref[2:3])
        d_out_ref[...] = d2
        terms_ref[...] = terms
        e = d2.astype(BF)
        e_ref[...] = e
        frame = lax.broadcasted_iota(jnp.int32, (frames, HEAD_DIM), 0).astype(F32)
        lane = lax.broadcasted_iota(jnp.int32, (frames, HEAD_DIM), 1)
        mask = jnp.where(frame < nums_ref[1:2, 0:1], 0.0, -1e30)
        beside = jnp.where(lane == 0, mask, jnp.where(lane < 4, 1.0, 0.0)).astype(BF)
        three = widened(3)(frames)
        for h in range(HEADS):
            lanes = slice(h * HEAD_DIM, (h + 1) * HEAD_DIM)
            keys[h] = jnp.concatenate([kv_ref[:, lanes], beside], axis=1)
            value = kv_ref[:, HALF + h * HEAD_DIM : HALF + (h + 1) * HEAD_DIM]
            values[h] = jnp.concatenate([value, three], axis=1)
            queries[h] = q_ref[:, lanes]
        copies.wait()
        d_mixed = project_t(e, w_out).astype(BF)
        dot_t[...] = d_mixed.T
        for h in range(HEADS):
            grads[h] = d_mixed[:, h * HEAD_DIM : (h + 1) * HEAD_DIM]
        ones = jnp.ones((1, length), F32)

        def head(h, carry):
            rows = head_rows(h)
            do_t = dot_t[rows, :]
            q_n, do_n = queries[h], grads[h]
            delta = jnp.sum(do_t.astype(F32) * ot_ref[rows, :].astype(F32), axis=0, keepdims=True)
            q_t = below(qt_ref[rows, :], [ones] + low_parts(-lse_ref[h]))
            do_t = below(do_t, low_parts(-delta))
            total = None
            for at in range(0, frames, CHUNK):
                here = slice(at, at + CHUNK)
                p = jnp.exp(mm(keys[h, here], q_t))
                ds = (p * mm(values[h, here], do_t)).astype(BF)
                dv_h[h, here] = mm(p.astype(BF), do_n).astype(BF)
                dk_h[h, here] = mm(ds, q_n).astype(BF)
                more = mm(kvt_ref[rows, here], ds)
                total = more if total is None else total + more
            dqt[rows, :] = (total * HEAD_DIM ** (-0.5)).astype(BF)
            return carry

        lax.fori_loop(0, HEADS, head, 0)
        dq = dqt[...].T
        dq_ref[...] = dq
        part_ref[...] = mm_t(dq, w_q[...]).astype(BF)
        for h in range(HEADS):
            lanes = slice(h * HEAD_DIM, (h + 1) * HEAD_DIM)
            dkv_ref[:, lanes] = dk_h[h]
            dkv_ref[:, HALF + h * HEAD_DIM : HALF + (h + 1) * HEAD_DIM] = dv_h[h]

    return run(
        body,
        [
            shaped((length, D)),
            shaped((length, D), F32),
            shaped((length, D)),
            shaped((length, HALF)),
            shaped((frames, D)),
            shaped((2, D), F32),
        ],
        vmem=[d, hidden, mine, other, norms, nums, kv, kvt, q, qt, ot, lse],
        hbm=weights,
        scratch=[
            pltpu.VMEM((D, HALF), BF),
            pltpu.VMEM((2, HALF, HALF), BF),
            pltpu.VMEM((HEADS, frames, 2 * HEAD_DIM), BF),
            pltpu.VMEM((HEADS, frames, 2 * HEAD_DIM), BF),
            pltpu.VMEM((HEADS, length, HEAD_DIM), BF),
            pltpu.VMEM((HEADS, length, HEAD_DIM), BF),
            pltpu.VMEM((HALF, length), BF),
            pltpu.VMEM((HEADS, frames, HEAD_DIM), BF),
            pltpu.VMEM((HEADS, frames, HEAD_DIM), BF),
            pltpu.VMEM((HALF, length), BF),
        ],
        copies=4 + 16,
        micros=22,
        after=after,
    )


def self_backward(d, hidden, mine, other, norms, nums, qkv, qt, kt, ot, lse, weights, after=()):
    length = hidden.shape[0]

    def body(
        d_ref, hidden_ref, mine_ref, other_ref, norms_ref, nums_ref, qkv_ref, qt_ref, kt_ref,
        ot_ref, lse_ref, *refs
    ):
        w_refs, refs = refs[: len(weights)], refs[len(weights) :]
        part_ref, d_out_ref, e_ref, dqk_ref, dv_ref, terms_ref = refs[:6]
        w_qk, w_v, w_out, queries_h, keys, values, grads, dot_t, dk_h, dv_h, dqt, bias, sems = refs[6:]
        _, xy, _ = where_am_i()
        copies = Copies(sems)
        load_out(copies, w_refs, 0, xy, w_out)
        load_wide(copies, w_refs, 0, 0, xy, w_qk)
        load_wide(copies, w_refs, 0, 1, xy, w_v, HALF)
        d1, terms = step_back(d_ref, hidden_ref, mine_ref, other_ref, norms_ref[1:2])
        d_out_ref[...] = d1
        terms_ref[...] = terms
        e = d1.astype(BF)
        e_ref[...] = e
        places = lax.broadcasted_iota(jnp.int32, (length, length), 0)
        queries = lax.broadcasted_iota(jnp.int32, (length, length), 1)
        allowed = (places <= queries) & (places.astype(F32) < nums_ref[0:1, 0:1])
        bias[...] = jnp.where(allowed, 0.0, -1e30)
        three = widened(3)(length)
        for h in range(HEADS):
            at = h * HEAD_DIM
            queries_h[h] = qkv_ref[:, at : at + HEAD_DIM]
            key = qkv_ref[:, HALF + at : HALF + at + HEAD_DIM]
            keys[h] = jnp.concatenate([key, three], axis=1)
            value = qkv_ref[:, 2 * HALF + at : 2 * HALF + at + HEAD_DIM]
            values[h] = jnp.concatenate([value, three], axis=1)
        copies.wait()
        d_mixed = project_t(e, w_out).astype(BF)
        dot_t[...] = d_mixed.T
        for h in range(HEADS):
            grads[h] = d_mixed[:, h * HEAD_DIM : (h + 1) * HEAD_DIM]

        def head(h, carry):
            rows = head_rows(h)
            do_t, do_n = dot_t[rows, :], grads[h]
            delta = jnp.sum(do_t.astype(F32) * ot_ref[rows, :].astype(F32), axis=0, keepdims=True)
            q_t = below(qt_ref[rows, :], low_parts(-lse_ref[h]))
            do_t = below(do_t, low_parts(-delta))
            p = jnp.exp(mm(keys[h], q_t) + bias[...])
            ds = (p * mm(values[h], do_t)).astype(BF)
            dv_h[h] = mm(p.astype(BF), do_n).astype(BF)
            dk_h[h] = mm(ds, queries_h[h]).astype(BF)
            dqt[rows, :] = (mm(kt_ref[rows, :], ds) * HEAD_DIM ** (-0.5)).astype(BF)
            return carry

        lax.fori_loop(0, HEADS, head, 0)
        dqk_ref[:, 0:HALF] = dqt[...].T
        for h in range(HEADS):
            lanes = slice(HALF + h * HEAD_DIM, HALF + (h + 1) * HEAD_DIM)
            dqk_ref[:, lanes] = dk_h[h]
            dv_ref[:, h * HEAD_DIM : (h + 1) * HEAD_DIM] = dv_h[h]
        out = mm_t(dqk_ref[...], w_qk[...]) + mm_t(dv_ref[...], w_v[...])
        part_ref[...] = out.astype(BF)

    return run(
        body,
        [
            shaped((length, D)),
            shaped((length, D), F32),
            shaped((length, D)),
            shaped((length, D)),
            shaped((length, HALF)),
            shaped((2, D), F32),
        ],
        vmem=[d, hidden, mine, other, norms, nums, qkv, qt, kt, ot, lse],
        hbm=weights,
        scratch=[
            pltpu.VMEM((D, D), BF),
            pltpu.VMEM((D, HALF), BF),
            pltpu.VMEM((2, HALF, HALF), BF),
            pltpu.VMEM((HEADS, length, HEAD_DIM), BF),
            pltpu.VMEM((HEADS, length, 2 * HEAD_DIM), BF),
            pltpu.VMEM((HEADS, length, 2 * HEAD_DIM), BF),
            pltpu.VMEM((HEADS, length, HEAD_DIM), BF),
            pltpu.VMEM((HALF, length), BF),
            pltpu.VMEM((HEADS, length, HEAD_DIM), BF),
            pltpu.VMEM((HEADS, length, HEAD_DIM), BF),
            pltpu.VMEM((HALF, length), BF),
            pltpu.VMEM((length, length), F32),
        ],
        copies=ATTENTION_COPIES,
        micros=12,
        after=after,
    )


def finish_hidden(d, hidden, mine, other, norms, terms1, terms2, terms3, after=()):
    length = hidden.shape[0]

    def body(
        d_ref, hidden_ref, mine_ref, other_ref, norms_ref, one, two, three, terms_ref, first_ref,
        second_ref, blocks
    ):
        d0, terms = step_back(d_ref, hidden_ref, mine_ref, other_ref, norms_ref[0:1])
        store_blocks(d0.astype(BF), blocks, first_ref, second_ref)
        for j in range(2):
            here = slice(j, j + 1)
            terms_ref[4 * j : 4 * j + 4] = jnp.concatenate(
                [terms[here], one[here], two[here], three[here]], axis=0
            )

    return run(
        body,
        [shaped((8, D), F32), shaped((QUARTER, length)), shaped((QUARTER, length))],
        vmem=[d, hidden, mine, other, norms, terms1, terms2, terms3],
        scratch=[pltpu.VMEM((4, length, QUARTER), BF)],
        micros=4,
        after=after,
    )


def finish_encoder(keep, other, frames):
    def body(keep_ref, other_ref, first_ref, second_ref):
        _, _, z = where_am_i()
        for ref, k in ((first_ref, 0), (second_ref, 1)):
            here = pl.ds(pl.multiple_of(((z + k) % 2) * QUARTER, QUARTER), QUARTER)
            total = keep_ref[here, :].astype(F32) + other_ref[here, :].astype(F32)
            ref[...] = total.astype(BF)[:, :frames]

    return run(
        body,
        [shaped((QUARTER, frames)), shaped((QUARTER, frames))],
        vmem=[keep, other],
        micros=2,
    )


def block_plan(place):
    if not place.fast:
        return 1, (((1, 0, 0),), ((1, 0, 0),))
    first = ((1, 0, 0), (0, 0, 1), (1, 1, 2), (0, 1, 3))
    second = ((1, 0, 0), (1, 1, 1), (0, 0, 2), (0, 1, 3))
    return 4, (first, second)


def grad_outputs(place, shape):
    if place.fast:
        return [shaped((2,) + shape)] * 4
    return [shaped((1,) + shape)] * 4


def units_grads(place, mt, dz, it, e):
    chips = place.chips
    rows = D // (2 * chips)
    _, plan = block_plan(place)

    def body(mt_ref, dz_ref, it_ref, e_ref, *outs):
        _, xy, _ = where_am_i()
        for output, slot, offset in plan[1]:
            chip = xy ^ offset
            for z in range(4):
                here = pl.ds(pl.multiple_of(z * HALF + chip * rows, 16), rows)
                outs[2 + output][slot, z] = mm(it_ref[here, :], e_ref[...]).astype(BF)
        for output, slot, offset in plan[0]:
            here = pl.ds(pl.multiple_of((xy ^ offset) * 2 * rows, 16), 2 * rows)
            left = mm(mt_ref[here, :], dz_ref[...]).astype(BF)
            for z in range(4):
                outs[output][slot, z] = left[:, z * HALF : (z + 1) * HALF]

    def plain(mt_ref, dz_ref, it_ref, e_ref, left_ref, right_ref):
        left_ref[...] = mm(mt_ref[...], dz_ref[...]).astype(BF)
        right_ref[...] = mm(it_ref[...], e_ref[...]).astype(BF)

    if place.fast:
        first, second = shaped((2, 4, 2 * rows, HALF)), shaped((2, 4, rows, D))
        return run(
            body, [first, first, second, second], vmem=[mt, dz, it, e], micros=6
        )
    left, right = run(
        plain, [shaped((D, 2 * D)), shaped((2 * D, D))], vmem=[mt, dz, it, e], micros=7
    )
    left = left.reshape(chips, 2 * rows, 4, HALF).transpose(0, 2, 1, 3)
    right = right.reshape(4, chips, rows, 2, HALF).transpose(1, 0, 3, 2, 4)
    whole = jnp.concatenate([left, right.reshape(chips, 4, 2 * rows, HALF)], axis=-1)
    return whole.reshape(4 * chips, 2 * rows, D)


def units_sum(grads, came, onward, after):
    rows = grads[3].shape[2]

    def body(*refs):
        ins, (out_ref, left, right, sems) = refs[:6], refs[6:]
        copies = Copies(sems)
        for i, ref in enumerate(ins):
            target = (left if i < 3 else right).at[i % 3]
            copies.start(ref if i % 3 == 2 else ref.at[0], target)
        copies.wait()
        for z in range(4):
            out_ref[z, :, 0:HALF] = add_up(*[left[i, z] for i in range(3)]).astype(BF)
            down = add_up(*[right[i, z] for i in range(3)]).astype(BF)
            out_ref[z, 0:rows, HALF:D] = down[:, :HALF]
            out_ref[z, rows : 2 * rows, HALF:D] = down[:, HALF:]

    return run(
        body,
        [shaped((4, 2 * rows, D))],
        hbm=[grads[1], came[0], onward[0], grads[3], came[1], onward[1]],
        scratch=[pltpu.VMEM((3, 4, 2 * rows, HALF), BF), pltpu.VMEM((3, 4, rows, D), BF)],
        copies=6,
        micros=3,
        after=after,
    )[0]


def attention_grads(place, wide_left, wide_right, left, right, ot, e, after=()):
    count, plan = block_plan(place)
    rows = D // count
    few = rows // 4

    def body(wide_left_ref, wide_right_ref, left_ref, right_ref, ot_ref, e_ref, *outs):
        _, xy, _ = where_am_i()
        for output, slot, offset in plan[0]:
            chip = xy ^ offset if count > 1 else 0
            here = pl.ds(pl.multiple_of(chip * rows, 16), rows)
            outs[output][slot] = mm(wide_left_ref[here, :], wide_right_ref[...]).astype(BF)
        for output, slot, offset in plan[1]:
            chip = xy ^ offset if count > 1 else 0
            here = pl.ds(pl.multiple_of(chip * rows, 16), rows)
            target = outs[2 + output]
            target[slot, :, 0:HALF] = mm(left_ref[here, :], right_ref[...]).astype(BF)
            for hi in range(2):
                here = pl.ds(pl.multiple_of(hi * QUARTER + chip * few, 16), few)
                both = mm(ot_ref[here, :], e_ref[...]).astype(BF)
                for q in range(2):
                    at = (2 * q + hi) * few
                    target[slot, at : at + few, HALF:D] = both[:, q * HALF : (q + 1) * HALF]

    return run(
        body,
        grad_outputs(place, (rows, D)),
        vmem=[wide_left, wide_right, left, right, ot, e],
        micros=6,
        after=after,
    )


def encoder_grad(dkv, weights):
    padded = dkv.shape[0]

    def body(dkv_ref, *refs):
        w_refs, (keep_ref, send_ref, w_kv, sems) = refs[: len(weights)], refs[len(weights) :]
        core, xy, _ = where_am_i()
        copies = Copies(sems)
        load_wide(copies, w_refs, 1, 0, xy, w_kv)
        copies.wait()
        mine = pl.ds(pl.multiple_of(core * HALF, HALF), HALF)
        theirs = pl.ds(pl.multiple_of((1 - core) * HALF, HALF), HALF)
        for ref, rows in ((send_ref, theirs), (keep_ref, mine)):
            for at in range(0, padded, CHUNK):
                value = mm_t(w_kv[rows, :], dkv_ref[at : at + CHUNK, :])
                ref[:, at : at + CHUNK] = value.astype(BF)

    return run(
        body,
        [shaped((HALF, padded)), shaped((HALF, padded))],
        vmem=[dkv],
        hbm=weights,
        scratch=[pltpu.VMEM((D, D), BF)],
        copies=4,
        micros=4,
    )


def leave_plane(place, grads):
    return [place.swap_xy(grads[0], 1), place.swap_xy(grads[2], 2)]


def pass_on(grads, came, after):
    shapes = [grads[1].shape[1:], grads[3].shape[1:]]

    def body(stay0, came0, stay1, came1, out0, out1, held0, held1, sems):
        copies = Copies(sems)
        for i, ref in enumerate((stay0, came0, stay1, came1)):
            copies.start(ref.at[1], (held0 if i < 2 else held1).at[i % 2])
        copies.wait()
        out0[...] = add_up(held0[0], held0[1]).astype(BF)
        out1[...] = add_up(held1[0], held1[1]).astype(BF)

    return run(
        body,
        [shaped(shape) for shape in shapes],
        hbm=[grads[1], came[0], grads[3], came[1]],
        scratch=[pltpu.VMEM((2,) + shape, BF) for shape in shapes],
        copies=4,
        micros=1,
        after=after,
    )


def cross_plane(place, onward):
    return [place.swap_xy(onward[0], 2), place.swap_xy(onward[1], 1)]


def column_blocks(grads, came, onward, swapped, norm_terms=(), after=()):
    shape = onward[0].shape
    rows = shape[-2] // 2
    width = D
    few = rows // 4
    extra = 16 if norm_terms else 0

    def body(*refs):
        terms_refs, refs = refs[: len(norm_terms)], refs[len(norm_terms) :]
        ins, outs, (held, shards, sems) = refs[:6], refs[6:-3], refs[-3:]
        home, slots = column_slots()
        copies = Copies(sems)
        for i, ref in enumerate(ins):
            copies.start(ref if i % 3 == 2 else ref.at[0], held.at[i])
        copies.wait()
        sums = [add_up(held[3 * part], held[3 * part + 1], held[3 * part + 2]) for part in range(2)]
        for hi in range(2):
            for cs in range(2):
                here = slice(cs * rows, (cs + 1) * rows)
                lanes = slice(hi * QUARTER, (hi + 1) * QUARTER)
                lanes_two = slice(HALF + hi * QUARTER, HALF + (hi + 1) * QUARTER)
                outs_rows = []
                for p in range(4):
                    at = (2 * (p // 2) + hi) * 2 * few + cs * few
                    side = HALF + (p % 2) * QUARTER
                    outs_rows.append(sums[1][at : at + few, side : side + QUARTER])
                value = jnp.concatenate(
                    [
                        sums[0][here, lanes],
                        sums[0][here, lanes_two],
                        sums[1][here, lanes],
                        jnp.concatenate(outs_rows, axis=0),
                    ],
                    axis=1,
                )
                shards[2 * hi + cs, :rows] = value.astype(BF)
        if norm_terms:
            core, xy, _ = where_am_i()
            terms = add_up(*[ref[...] for ref in terms_refs])
            terms = jnp.concatenate([terms, jnp.zeros_like(terms)], axis=0).astype(BF)
            feature = lax.broadcasted_iota(jnp.int32, (D, D), 0)
            lane = lax.broadcasted_iota(jnp.int32, (D, D), 1)
            for hi in range(2):
                for cs in range(2):
                    offset = (2 * core + hi) * QUARTER + (2 * xy + cs) * few
                    pick = jnp.where((feature == lane + offset) & (lane < few), 1.0, 0.0)
                    shards[2 * hi + cs, rows:] = mm(terms, pick.astype(BF)).astype(BF)
        if swapped:
            core, _, _ = where_am_i()
            for hi in range(2):
                outs[0][hi] = shards[2 * hi + core]
                outs[1][hi] = shards[2 * hi + 1 - core]
        else:
            for k in range(4):
                outs[k][...] = shards[slots[k]]

    ins = [grads[1], came[0], onward[0], grads[3], came[1], onward[1]]
    return run(
        body,
        [shaped((2, rows, width))] * 2 if swapped else [shaped((rows + extra, width))] * 4,
        vmem=list(norm_terms),
        hbm=ins,
        after=after,
        scratch=[pltpu.VMEM((6,) + shape, BF), pltpu.VMEM((4, rows + extra, width), BF)],
        copies=6,
        micros=2,
    )


def scatter_column(place, kept, came):
    first = place.core == 0
    both = jnp.concatenate([jnp.where(first, kept, came), jnp.where(first, came, kept)])
    return lax.psum_scatter(both, "mp", scatter_dimension=0, tiled=False).astype(F32)


def sum_plain(place, grads, attention):
    wide, narrow = grads[1][0], grads[3][0]
    rows = D // place.dp
    if attention:
        value = jnp.stack([wide[:, :HALF], wide[:, HALF:], narrow[:, :HALF]], axis=1)
        value = value.reshape(place.dp, rows, 3, 2, QUARTER).transpose(3, 0, 1, 2, 4)
        value = value.reshape(2, place.dp, rows, 3 * QUARTER)
        outs = narrow[:, HALF:].reshape(2, 2, place.dp, rows // 4, 2, QUARTER)
        outs = outs.transpose(1, 2, 0, 4, 3, 5).reshape(2, place.dp, rows, QUARTER)
        value = jnp.concatenate([value, outs], axis=-1)
    else:
        value = jnp.concatenate(
            [wide.reshape(2, place.dp, rows, D), narrow.reshape(2, place.dp, rows, D)], axis=-1
        )
    whole = jnp.zeros((2,) + value.shape, F32)
    whole = lax.dynamic_update_index_in_dim(whole, value.astype(F32), place.core, 0)
    whole = whole.reshape((4 * place.dp,) + value.shape[2:])
    return lax.psum_scatter(whole, ("mp", "xy", "core"), scatter_dimension=0, tiled=False)


def from_quarters(value):
    few = value.shape[0] // 4
    return value.reshape(4, few, QUARTER).transpose(1, 0, 2).reshape(few, D)


def three_parts(value):
    terms = []
    for _ in range(3):
        term = lax.reduce_precision(value, 8, 7)
        terms.append(term.astype(BF))
        value = value - term
    return jnp.concatenate(terms)


def per_device(
    dp,
    mp,
    hidden_in,
    encoder_states,
    cotangent,
    self_qkv,
    self_out,
    cross_q,
    cross_kv,
    cross_out,
    fc_in,
    fc_out,
    ln_gain,
    ln_bias,
    token_lengths,
    audio_lengths,
    corpus_ids,
    corpus_weights,
):
    place = Place(dp, mp)
    length = hidden_in.shape[2]
    frames = encoder_states.shape[2]
    padded = -(-frames // CHUNK) * CHUNK
    rows = self_qkv.shape[0]

    first = ()
    w_units = gather_units(place, unit_shard(place, fc_in, fc_out))
    if place.fast:
        shard = attention_shard(self_qkv, self_out, cross_kv, cross_q, cross_out)
        packed = pack_attention(place.column_out(shard), shard)
        w_self = w_cross = spread(place, packed)
        first = (shard,)
    else:
        quarter = lambda w: w.reshape(-1, 4, QUARTER).transpose(1, 0, 2).reshape(-1, QUARTER)
        flat = lambda w: w.reshape(rows, -1)
        w_self = attention_plain(
            place, jnp.concatenate([flat(self_qkv), quarter(self_out)], axis=1)
        )
        w_cross = attention_plain(
            place, jnp.concatenate([flat(cross_kv), cross_q, quarter(cross_out)], axis=1)
        )


    turned = lambda value: value[:, 0].transpose(0, 2, 1)
    numbers = jnp.concatenate([token_lengths.T, audio_lengths.T, corpus_ids.T])
    blocks = input_blocks(
        turned(hidden_in),
        three_parts(jnp.concatenate([ln_gain, ln_bias])),
        numbers,
        first,
    )
    got = place.rows_in(blocks)
    hidden, norms, nums = prepare(got, place.swap_core(got), corpus_weights)

    encoded = lax.dynamic_index_in_dim(encoder_states[:, 0], place.micro, 0, keepdims=False)
    other = place.move(encoded, lambda xy, core, z: (xy, 1 - core, z) if core == z // 2 else None)
    encoded = jnp.where(place.home == place.core, encoded, other)
    encoded = jnp.pad(encoded, ((0, padded - frames), (0, 0)))

    et = turn(encoded)
    part1, at, qkv, qt, kt, ot1, lse1 = self_forward(hidden, norms, nums, w_self, (et,))
    other1 = place.swap_core(part1)
    got = place.rows_in(turned_blocks(turned(cotangent), (at,)))
    kv, kvt = cross_memory(encoded, w_cross)
    part2, h1, ct, q2, qt2, ot2, lse2 = cross_forward(
        hidden, part1, other1, norms, nums, kv, kvt, w_cross
    )
    other2 = place.swap_core(part2)
    cot = prepare_cotangent(got, place.swap_core(got), (part2,))
    part3, h2, mt, slope, it = units_forward(h1, part2, other2, norms, w_units)
    other3 = place.swap_core(part3)
    part, d3, e3, dz, terms3, out_a, out_b = units_backward(
        h2, part3, other3, norms, nums, cot, slope, w_units
    )
    other = place.swap_core(part)
    g_units = units_grads(place, mt, dz, it, e3)
    came_units = leave_plane(place, g_units) if place.fast else None
    layer_got = place.rows_sent((out_a, out_b))
    layer_out = place.rows_joined((out_a, out_b), layer_got)
    part, d2, e2, dq2, dkv, terms2 = cross_backward(
        d3, h2, part, other, norms, nums, kv, kvt, q2, qt2, ot2, lse2, w_cross, layer_got
    )
    other = place.swap_core(part)
    keep, send = encoder_grad(dkv, w_cross)
    passed = pass_on(g_units, came_units, (keep,)) if place.fast else ()
    encoder_blocks = finish_encoder(keep, place.swap_core(send), frames)
    g_cross = attention_grads(place, et, dkv, ct, dq2, ot2, e2, encoder_blocks + tuple(passed))
    encoder_got = place.rows_sent(encoder_blocks)
    if place.fast:
        g_units = units_sum(
            g_units, came_units, cross_plane(place, passed), (g_cross[0],)
        )
    s_up, s_down = scatter_units(place, g_units)
    if place.fast:
        came_cross = leave_plane(place, g_cross)
    part, d1, e1, dqk, dv, terms1 = self_backward(
        d2, h1, part, other, norms, nums, qkv, qt, kt, ot1, lse1, w_self, (g_cross[0],)
    )
    other = place.swap_core(part)
    passed = encoder_got
    if place.fast:
        passed = pass_on(g_cross, came_cross, [e1] + encoder_got)
    g_self = attention_grads(place, at, dqk, at, dv, ot1, e1, passed)
    if place.fast:
        came_self = leave_plane(place, g_self)
        cross_blocks = column_blocks(
            g_cross, came_cross, cross_plane(place, passed), True, (), (g_self[0],)
        )
        passed = (cross_blocks[0],)
        s_cross = scatter_column(place, cross_blocks[0], place.swap_core(cross_blocks[1]))
    grad_encoder = place.rows_joined(encoder_blocks, encoder_got).astype(F32)
    terms, out_a, out_b = finish_hidden(
        d1, hidden, part, other, norms, terms1, terms2, terms3, passed
    )
    grad_hidden = place.rows_home((out_a, out_b)).astype(F32)

    few = D // (place.dp * place.mp)
    if place.fast:
        passed = pass_on(g_self, came_self, (terms,))
        onward_self = cross_plane(place, passed)
        terms = terms + place.swap_xy(terms, 1)
        s_self = place.column_back(
            column_blocks(
                g_self, came_self, onward_self, False, (terms, place.swap_xy(terms, 2))
            )
        )
        shares = s_self[rows : rows + 8, :few]
    else:
        s_cross = sum_plain(place, g_cross, True)
        s_self = sum_plain(place, g_self, True)
        terms = jnp.where(place.core == 0, terms, 0.0)
        terms = lax.psum(terms, AXES)
        shares = lax.dynamic_slice_in_dim(terms, (place.z * place.dp + place.d) * few, few, 1)
    s_self = s_self[:rows]
    return (
        layer_out,
        grad_hidden,
        grad_encoder,
        s_self[:, : 3 * QUARTER].reshape(rows, 3, QUARTER),
        from_quarters(s_self[:, 3 * QUARTER :]),
        s_cross[:, 2 * QUARTER : 3 * QUARTER],
        s_cross[:, : 2 * QUARTER].reshape(rows, 2, QUARTER),
        from_quarters(s_cross[:, 3 * QUARTER :]),
        s_up,
        s_down,
        shares[:4],
        shares[4:],
    )


def solution(mesh):
    dp, mp = mesh.shape["dp"], mesh.shape["mp"]
    finer = Mesh(mesh.devices.reshape(dp // 2, 2, mp), AXES)
    both = ("xy", "core")
    rows = P(None, both, None, "mp")
    columns = P(both, None, "mp")
    pairs = P(both, "mp")
    units = P(("mp",) + both, None)
    each = P(None, both)
    return jax.shard_map(
        partial(per_device, dp, mp),
        mesh=finer,
        in_specs=(
            rows,
            P(None, both, None, None),
            rows,
            columns,
            units,
            pairs,
            columns,
            units,
            pairs,
            units,
            P(None, "mp"),
            P(None, "mp"),
            each,
            each,
            each,
            P(),
        ),
        out_specs=(
            rows,
            rows,
            rows,
            columns,
            units,
            pairs,
            columns,
            units,
            pairs,
            units,
            P(None, ("mp",) + both),
            P(None, ("mp",) + both),
        ),
        check_vma=False,
    )
```

```python
from functools import partial

import jax
import jax.numpy as jnp
from jax import lax
from jax.experimental import pallas as pl
from jax.experimental.pallas import tpu as pltpu
from jax.sharding import Mesh, PartitionSpec as P

D = 768
HALF = 384
QUARTER = 192
HEAD_DIM = 64
HEADS = 6
CHUNK = 256
BF = jnp.bfloat16
F32 = jnp.float32
AXES = ("xy", "core", "mp")
CHIPS = ("xy", "mp")
VMEM = pl.BlockSpec(memory_space=pltpu.VMEM)
SMEM = pl.BlockSpec(memory_space=pltpu.SMEM)
ANY = pl.BlockSpec(memory_space=pl.ANY)


def mm(left, right):
    return jnp.dot(left, right, preferred_element_type=F32)


def mm_t(left, right):
    return lax.dot_general(left, right, (((1,), (1,)), ((), ())), preferred_element_type=F32)


def shaped(shape, dtype=BF):
    return jax.ShapeDtypeStruct(shape, dtype)


def room(shape, dtype):
    item = jnp.dtype(dtype).itemsize
    shape = (1, 1) + tuple(shape)
    tile = 32 // item
    size = item * (-(-shape[-1] // 128) * 128) * (-(-shape[-2] // tile) * tile)
    for extent in shape[:-2]:
        size *= extent
    return size


def run(
    body, outs, vmem=(), hbm=(), smem=(), scratch=(), copies=0, micros=2, after=(), staged=False
):
    args = tuple(smem) + tuple(vmem) + tuple(hbm)
    count = len(args)
    scratch = list(scratch)
    if copies:
        scratch.append(pltpu.SemaphoreType.DMA((copies,)))
    need = sum(room(a.shape, a.dtype) for a in tuple(vmem) + tuple(outs))
    need += sum(room(a.shape, a.dtype) for a in scratch if a.memory_space == pltpu.VMEM)
    need = min(need + 12 * 1024 * 1024, 60 * 1024 * 1024)
    moved = sum(a.size * a.dtype.itemsize for a in args) + sum(
        o.size * o.dtype.itemsize for o in outs
    )
    skip = len(scratch)
    if staged:
        scratch += [pltpu.VMEM(a.shape, a.dtype) for a in vmem]
        scratch.append(pltpu.SemaphoreType.DMA((len(vmem),)))

    def whole(*refs):
        ins, rest = list(refs[:count]), refs[count + len(after) :]
        if staged:
            held = rest[len(outs) + skip : -1]
            rest, sems = rest[: len(outs) + skip], rest[-1]
            copies = Copies(sems)
            for i, target in enumerate(held):
                copies.start(ins[len(smem) + i], target)
                ins[len(smem) + i] = target
            copies.wait()
        body(*ins, *rest)

    place = ANY if staged else VMEM
    return pl.pallas_call(
        whole,
        out_shape=tuple(outs),
        in_specs=[SMEM] * len(smem) + [place] * len(vmem) + [ANY] * (len(hbm) + len(after)),
        out_specs=(VMEM,) * len(outs),
        scratch_shapes=scratch,
        compiler_params=pltpu.CompilerParams(vmem_limit_bytes=need),
        cost_estimate=pl.CostEstimate(
            flops=int(micros * 1.15e9), bytes_accessed=moved, transcendentals=0
        ),
    )(*args, *after)


class Copies:
    def __init__(self, sems):
        self.sems, self.open = sems, []

    def start(self, source, target):
        copy = pltpu.make_async_copy(source, target, self.sems.at[len(self.open)])
        copy.start()
        self.open.append(copy)

    def wait(self):
        for copy in self.open:
            copy.wait()


def where_am_i():
    return lax.axis_index("core"), lax.axis_index("xy"), lax.axis_index("mp")


class Place:
    def __init__(self, dp, mp):
        self.dp, self.mp = dp, mp
        self.chips = dp // 2
        self.fast = self.chips == 4
        self.z = lax.axis_index("mp")
        self.core = lax.axis_index("core")
        self.xy = lax.axis_index("xy")
        self.d = 2 * self.xy + self.core
        self.micro = self.z % 2
        self.home = self.z // 2

    def move(self, value, route):
        pairs = []
        for xy in range(self.chips):
            for core in range(2):
                for z in range(self.mp):
                    target = route(xy, core, z)
                    if target is not None:
                        txy, tcore, tz = target
                        pairs.append(
                            ((2 * xy + core) * self.mp + z, (2 * txy + tcore) * self.mp + tz)
                        )
        return lax.ppermute(value, AXES, pairs)

    def swap_core(self, value):
        return self.move(value, lambda xy, core, z: (xy, 1 - core, z))

    def swap_xy(self, value, bit):
        return self.move(value, lambda xy, core, z: (xy ^ bit, core, z))

    def swap_z(self, value, bit):
        return self.move(value, lambda xy, core, z: (xy, core, z ^ bit))

    def column_routes(self):
        def route(step, xy, core, z):
            user, j = z // 2, z % 2
            home = core == user
            near = lambda i: (xy, user, 2 * user + i)
            far = lambda i: (xy, user, 2 * (1 - user) + i)
            if step == 0:
                return near(1 - j) if home else far(1 - j)
            if step == 1:
                return far(j) if home else near(j)
            if step == 2:
                return far(1 - j) if home else near(1 - j)
            return None if home else far(j)

        return [partial(route, step) for step in range(4)]

    def column_out(self, shard):
        return [self.move(shard, route) for route in self.column_routes()]

    def column_back(self, blocks):
        got = []
        for block, route in zip(blocks, self.column_routes()):
            turned = {}
            for xy in range(self.chips):
                for core in range(2):
                    for z in range(self.mp):
                        target = route(xy, core, z)
                        if target is not None:
                            turned[target] = (xy, core, z)
            got.append(self.move(block, lambda xy, core, z: turned.get((xy, core, z))))
        return got

    def rows_in(self, blocks):
        def route(k, xy, core, z):
            target = (xy, z // 2, 2 * core + (z + k) % 2)
            return None if target == (xy, core, z) else target

        got = [self.move(block, partial(route, k)) for k, block in enumerate(blocks)]
        return jnp.stack([jnp.where(self.core == self.home, blocks[0], got[0]), got[1]])

    def rows_home(self, blocks):
        return self.rows_joined(blocks, self.rows_sent(blocks))

    def rows_sent(self, blocks):
        def route(k, xy, core, z):
            target = (xy, z // 2, 2 * core + (z % 2 - k) % 2)
            return None if target == (xy, core, z) else target

        return [self.move(block, partial(route, k)) for k, block in enumerate(blocks)]

    def rows_joined(self, blocks, got):
        got = [jnp.where(self.core == self.home, blocks[0], got[0]), got[1]]
        even = self.z % 2 == 0
        both = jnp.stack([jnp.where(even, got[0], got[1]), jnp.where(even, got[1], got[0])])
        return both[:, None].transpose(0, 1, 3, 2)


def norm(hidden):
    center = jnp.mean(hidden, axis=-1, keepdims=True)
    spread = jnp.mean(hidden * hidden, axis=-1, keepdims=True) - center * center
    inverse = lax.rsqrt(spread + 1e-05)
    return (hidden - center) * inverse, inverse


def norm_back(grad, unit, inverse, gain):
    scaled = grad * gain
    first = jnp.mean(scaled, axis=-1, keepdims=True)
    second = jnp.mean(scaled * unit, axis=-1, keepdims=True)
    terms = jnp.concatenate(
        [jnp.sum(grad * unit, axis=0, keepdims=True), jnp.sum(grad, axis=0, keepdims=True)], axis=0
    )
    return inverse * (scaled - first - unit * second), terms


def add_up(*terms):
    total = terms[0].astype(F32)
    for term in terms[1:]:
        total = total + term.astype(F32)
    return total


def input_blocks(hidden, terms, numbers, after=()):
    _, width, length = hidden.shape
    total = width + 32

    def body(numbers_ref, hidden_ref, terms_ref, *outs):
        _, _, z = where_am_i()
        lanes = lax.broadcasted_iota(jnp.int32, (8, length), 1)
        for k in range(2):
            micro = (z + k) % 2
            outs[k][0:width] = hidden_ref[micro]
            tok, aud = numbers_ref[0, micro], numbers_ref[1, micro]
            row = jnp.where(lanes == 0, tok // 256, jnp.where(lanes == 1, tok % 256, 0))
            row = jnp.where(lanes == 2, aud // 256, jnp.where(lanes == 3, aud % 256, row))
            row = jnp.where(lanes == 4, numbers_ref[2, micro], row)
            wide = jnp.concatenate(
                [terms_ref[...].astype(F32), jnp.zeros((24, length - width), F32)], axis=1
            )
            outs[k][width:total] = jnp.concatenate([wide, row.astype(F32)], axis=0).astype(BF)

    return run(
        body,
        [shaped((total, length))] * 2,
        smem=[numbers],
        vmem=[hidden, terms],
        micros=1,
        after=after,
    )


def turned_blocks(value, after=()):
    _, width, length = value.shape

    def body(ref, first_ref, second_ref):
        _, _, z = where_am_i()
        first_ref[...] = ref[z % 2]
        second_ref[...] = ref[(z + 1) % 2]

    return run(body, [shaped((width, length))] * 2, vmem=[value], micros=1, after=after)


def bring_blocks(copies, own_ref, other_ref, wide):
    core, _, z = where_am_i()
    found = []
    for k in range(2):
        slot = (z % 2 + k) % 2
        for ref, user in ((own_ref, core), (other_ref, 1 - core)):
            block = 2 * user + slot
            here = pl.ds(pl.multiple_of(block * QUARTER, QUARTER), QUARTER)
            copies.start(ref.at[k, pl.ds(0, QUARTER)], wide.at[here])
            found.append((ref.at[k], block))
    return found


def prepare_cotangent(own, other, after=()):
    length = own.shape[2]

    def body(own_ref, other_ref, cot_ref, wide, sems):
        copies = Copies(sems)
        bring_blocks(copies, own_ref, other_ref, wide)
        copies.wait()
        cot_ref[...] = wide[...].T

    return run(
        body,
        [shaped((length, D))],
        hbm=[own, other],
        scratch=[pltpu.VMEM((D, length), BF)],
        copies=4,
        micros=3,
        after=after,
    )[0]


def prepare(own, other, corpus_weights):
    length = own.shape[2]

    def body(
        weights_ref, own_ref, other_ref, hidden_ref, norms_ref, nums_ref, wide, extra, sems
    ):
        copies = Copies(sems)
        for ref, block in bring_blocks(copies, own_ref, other_ref, wide):
            copies.start(ref.at[pl.ds(QUARTER, 32)], extra.at[block])
        copies.wait()
        hidden_ref[...] = wide[...].T
        parts = [extra[b].astype(F32) for b in range(4)]
        norms_ref[...] = jnp.concatenate(
            [(e[0:8] + e[8:16] + e[16:24])[:, :QUARTER] for e in parts], axis=1
        )
        row = parts[0][24:25]
        tok = 256.0 * row[:, 0:1] + row[:, 1:2]
        aud = 256.0 * row[:, 2:3] + row[:, 3:4]
        weights = weights_ref[...]
        places = lax.broadcasted_iota(jnp.int32, weights.shape, 1).astype(F32)
        weight = jnp.sum(jnp.where(places == row[:, 4:5], weights, 0.0), axis=1, keepdims=True)
        index = lax.broadcasted_iota(jnp.int32, (8, 128), 0)
        nums_ref[...] = jnp.where(index == 0, tok, jnp.where(index == 1, aud, weight))

    return run(
        body,
        [shaped((length, D)), shaped((8, D), F32), shaped((8, 128), F32)],
        vmem=[corpus_weights.reshape(1, -1)],
        hbm=[own, other],
        scratch=[pltpu.VMEM((D, length), BF), pltpu.VMEM((4, 32, length), BF)],
        copies=8,
        micros=3,
    )


def quarters(value):
    return jnp.concatenate([value[:, p * QUARTER : (p + 1) * QUARTER] for p in range(4)], axis=0)


def attention_shard(self_qkv, self_out, cross_kv, cross_q, cross_out):
    rows = cross_q.shape[0]

    def body(qkv_ref, out_ref, kv_ref, q_ref, cout_ref, shard_ref):
        out = quarters(out_ref[...].astype(F32)).astype(BF)
        cout = quarters(cout_ref[...].astype(F32)).astype(BF)
        shard_ref[...] = jnp.concatenate(
            [qkv_ref[j] for j in range(3)] + [out, kv_ref[...], q_ref[...], cout], axis=1
        )

    return run(
        body,
        [shaped((rows, 2 * D))],
        vmem=[self_qkv.transpose(1, 0, 2), self_out, cross_kv.reshape(rows, -1), cross_q, cross_out],
        micros=2,
    )[0]


def column_slots():
    core, _, z = where_am_i()
    j = z % 2
    home = 1 - jnp.abs(z // 2 - core)
    same = core + (1 - 2 * core) * (1 - home)
    return home == 1, (2 * (1 - j) + same, 2 * j + 1 - same, 2 * (1 - j) + 1 - same, 2 * j + same)


def bring_column(part_refs, own_ref, shards, sems):
    home, slots = column_slots()
    copies = Copies(sems)
    for k in range(3):
        copies.start(part_refs[k], shards.at[slots[k]])

    @pl.when(home)
    def _():
        copy = pltpu.make_async_copy(own_ref, shards.at[slots[3]], sems.at[3])
        copy.start()
        copy.wait()

    @pl.when(jnp.logical_not(home))
    def _():
        copy = pltpu.make_async_copy(part_refs[3], shards.at[slots[3]], sems.at[3])
        copy.start()
        copy.wait()

    copies.wait()


def pack_attention(parts, own, after):
    rows = own.shape[0]
    few = rows // 4

    def body(*refs):
        part_refs, own_ref, (out_ref, shards, sems) = refs[:4], refs[4], refs[5:]
        bring_column(part_refs, own_ref, shards, sems)
        for which in range(2):
            for cs in range(2):
                low, high = shards[cs], shards[2 + cs]

                def both(at):
                    at = at + which * D
                    return [low[:, at : at + QUARTER], high[:, at : at + QUARTER]]

                here = pl.ds(cs * rows, rows)
                out_ref[0, which, here, :] = jnp.concatenate(both(0) + both(QUARTER), axis=1)
                out_ref[1, which, here, 0:HALF] = jnp.concatenate(both(HALF), axis=1)
            at = 3 * QUARTER + which * D
            outs = [shards[i, :, at : at + QUARTER].astype(F32) for i in range(4)]
            stack = []
            for q in range(2):
                for i in range(4):
                    left = outs[i][2 * q * few : (2 * q + 1) * few]
                    right = outs[i][(2 * q + 1) * few : (2 * q + 2) * few]
                    stack.append(jnp.concatenate([left, right], axis=1))
            out_ref[1, which, :, HALF:D] = jnp.concatenate(stack, axis=0).astype(BF)

    return run(
        body,
        [shaped((2, 2, 2 * rows, D))],
        hbm=list(parts) + [own],
        scratch=[pltpu.VMEM((4, rows, 2 * D), BF)],
        copies=4,
        micros=2,
        after=after,
    )[0]


def unit_shard(place, fc_in, fc_out):
    rows = fc_in.shape[0]
    both = fc_in.reshape(rows, place.chips, 2, rows).transpose(2, 0, 1, 3).reshape(2, rows, HALF)
    kept = lax.dynamic_index_in_dim(both, place.core, 0, keepdims=False)
    sent = lax.dynamic_index_in_dim(both, 1 - place.core, 0, keepdims=False)
    came = place.swap_core(sent)
    first = place.core == 0
    left = jnp.concatenate([jnp.where(first, kept, came), jnp.where(first, came, kept)])
    right = jnp.concatenate([fc_out[:, :HALF], fc_out[:, HALF:]])
    return jnp.concatenate([left, right], axis=1)


def stack_units(blocks, after):
    rows = blocks[0].shape[0]

    def body(*refs):
        for k in range(4):
            refs[4][k // 2, k % 2] = refs[k][...]

    return run(body, [shaped((2, 2, rows, D))], vmem=blocks, micros=1.5, after=after)[0]


def gather_units(place, shard):
    whole = lax.all_gather(shard, CHIPS, axis=0)
    rows = shard.shape[0] // 2
    whole = whole.reshape(place.chips, place.mp, 2 * rows, D)
    up = whole[..., :HALF].transpose(0, 2, 1, 3).reshape(D, 2 * D)
    down = whole[..., HALF:].reshape(place.chips, place.mp, 2, rows, HALF)
    return [up, down.transpose(1, 0, 3, 2, 4).reshape(2 * D, D)]


def scatter_units(place, grads, after=()):
    axes = "mp" if place.fast else CHIPS
    total = lax.psum_scatter(grads, axes, scatter_dimension=0, tiled=False)
    rows = total.shape[0] // 2
    if not place.fast:
        kept = lax.dynamic_slice_in_dim(total, place.core * rows, rows, 0)
        sent = lax.dynamic_slice_in_dim(total[:, :HALF], (1 - place.core) * rows, rows, 0)
        came = place.swap_core(sent)
        kept = kept[:, :HALF]
        first = place.core == 0
        both = jnp.stack([jnp.where(first, kept, came), jnp.where(first, came, kept)])
        both = both.reshape(2, rows, place.chips, rows).transpose(1, 2, 0, 3).reshape(rows, D)
        down = jnp.concatenate([total[:rows, HALF:], total[rows:, HALF:]], axis=1)
        return both.astype(F32), down.astype(F32)

    def cut(total_ref, kept_ref, sent_ref, down_ref):
        core, _, _ = where_am_i()
        mine = pl.ds(pl.multiple_of(core * rows, 16), rows)
        theirs = pl.ds(pl.multiple_of((1 - core) * rows, 16), rows)
        kept_ref[...] = total_ref[mine, 0:HALF]
        sent_ref[...] = total_ref[theirs, 0:HALF]
        down_ref[:, 0:HALF] = total_ref[0:rows, HALF:D].astype(F32)
        down_ref[:, HALF:D] = total_ref[rows : 2 * rows, HALF:D].astype(F32)

    kept, sent, down = run(
        cut,
        [shaped((rows, HALF)), shaped((rows, HALF)), shaped((rows, D), F32)],
        vmem=[total],
        micros=1,
        after=after,
    )

    def join(kept_ref, came_ref, up_ref, both):
        core, _, _ = where_am_i()
        both[core] = kept_ref[...]
        both[1 - core] = came_ref[...]
        blocks = []
        for chip in range(place.chips):
            for parity in range(2):
                blocks.append(both[parity, :, chip * rows : (chip + 1) * rows].astype(F32))
        up_ref[...] = jnp.concatenate(blocks, axis=1)

    up = run(
        join,
        [shaped((rows, D), F32)],
        vmem=[kept, place.swap_core(sent)],
        scratch=[pltpu.VMEM((2, rows, HALF), BF)],
        micros=1,
    )[0]
    return up, down


def spread(place, own):
    from_x = place.swap_xy(own, 1)
    from_y = place.swap_xy(own, 2)
    far_one = place.swap_xy(from_y[1], 1)
    far_zero = place.swap_xy(from_x[0], 2)
    return [own, from_x, from_y, far_zero, far_one]


def piece_views(refs, message, which, xy):
    own, from_x, from_y, far_zero, far_one = refs
    return [
        (own.at[which, message], xy),
        (from_x.at[which, message], xy ^ 1),
        (from_y.at[which, message], xy ^ 2),
        ((far_zero, far_one)[which].at[message], xy ^ 3),
    ]


def load_wide(copies, refs, message, which, xy, target, columns=None):
    if len(refs) != 5:
        copies.start(refs[which], target)
        return
    for view, chip in piece_views(refs, message, which, xy):
        rows = view.shape[0]
        if columns is not None:
            view = view.at[:, pl.ds(0, columns)]
        copies.start(view, target.at[pl.ds(pl.multiple_of(chip * rows, 16), rows)])


def load_out(copies, refs, message, xy, target):
    if len(refs) != 5:
        copies.start(refs[2], target)
        return
    for view, chip in piece_views(refs, message, 1, xy):
        rows = view.shape[0] // 4
        for q in range(2):
            for hi in range(2):
                copies.start(
                    view.at[pl.ds((2 * q + hi) * rows, rows), pl.ds(HALF, HALF)],
                    target.at[q, pl.ds(pl.multiple_of(hi * QUARTER + chip * rows, 16), rows)],
                )


def unit_views(refs):
    _, xy, z = where_am_i()
    views = []
    for part in range(2):
        for view, chip in [
            (refs[0].at[part], xy),
            (refs[1].at[part], xy ^ 1),
            (refs[2].at[part], xy ^ 2),
            (refs[3 + part], xy ^ 3),
        ]:
            for i in range(2):
                views.append((view.at[i], chip, z ^ (2 * part + i)))
    return views


def load_up(copies, refs, w_up):
    if len(refs) == 2:
        copies.start(refs[0], w_up)
        return
    for view, chip, z in unit_views(refs):
        rows = view.shape[0]
        copies.start(
            view.at[:, pl.ds(0, HALF)],
            w_up.at[
                pl.ds(pl.multiple_of(rows * chip, 16), rows), pl.ds(pl.multiple_of(z * HALF, HALF), HALF)
            ],
        )


def load_down(copies, refs, w_down):
    if len(refs) == 2:
        copies.start(refs[1], w_down)
        return
    for view, chip, z in unit_views(refs):
        rows = view.shape[0] // 2
        for q in range(2):
            copies.start(
                view.at[pl.ds(q * rows, rows), pl.ds(HALF, HALF)],
                w_down.at[
                    pl.ds(pl.multiple_of(z * HALF + chip * rows, 16), rows), pl.ds(q * HALF, HALF)
                ],
            )


ATTENTION_COPIES = 4 + 4 + 16
UP_COPIES = 16
DOWN_COPIES = 32


def gather_plain(place, shard):
    whole = lax.all_gather(shard, ("mp", "xy", "core"), axis=0)
    whole = whole.reshape((2, 2, place.dp) + shard.shape)
    return lax.dynamic_index_in_dim(whole, place.core, 0, keepdims=False)


def attention_plain(place, shard):
    mine = gather_plain(place, shard)
    rows = shard.shape[0]

    def columns(at, count):
        value = mine[..., at : at + count * QUARTER].reshape(2, D, count, QUARTER)
        return value.transpose(1, 2, 0, 3).reshape(D, count * HALF)

    out = mine[..., 3 * QUARTER :].reshape(2, place.dp, 2, 2, rows // 4, QUARTER)
    out = out.transpose(2, 0, 1, 4, 3, 5).reshape(2, HALF, HALF)
    return [columns(0, 2), columns(HALF, 1), out]


def head_rows(h):
    return pl.ds(pl.multiple_of(h * HEAD_DIM, HEAD_DIM), HEAD_DIM)


def low_parts(value):
    parts = []
    for _ in range(3):
        part = value.astype(BF)
        parts.append(part)
        value = value - part.astype(F32)
    return parts


def widened(count):
    return lambda rows: (
        lax.broadcasted_iota(jnp.int32, (rows, HEAD_DIM), 1) < count
    ).astype(F32).astype(BF)


def below(head, rows):
    blank = jnp.zeros((HEAD_DIM - len(rows), head.shape[1]), F32)
    rest = jnp.concatenate([row.astype(F32) for row in rows] + [blank], axis=0)
    return jnp.concatenate([head, rest.astype(BF)], axis=0)


def project(left, pair_ref):
    return jnp.concatenate([mm(left, pair_ref[0]), mm(left, pair_ref[1])], axis=1)


def project_t(left, pair_ref):
    return mm_t(left[:, :HALF], pair_ref[0]) + mm_t(left[:, HALF:], pair_ref[1])


def self_forward(hidden, norms, nums, weights, after=()):
    length = hidden.shape[0]

    def body(hidden_ref, norms_ref, nums_ref, *refs):
        w_refs, refs = refs[: len(weights)], refs[len(weights) :]
        part_ref, at_ref, qkv_ref, qt_ref, kt_ref, ot_ref, lse_ref = refs[:7]
        w_qk, w_v, w_out, vt, heads, bias, sems = refs[7:]
        _, xy, _ = where_am_i()
        copies = Copies(sems)
        load_wide(copies, w_refs, 0, 0, xy, w_qk)
        load_wide(copies, w_refs, 0, 1, xy, w_v, HALF)
        load_out(copies, w_refs, 0, xy, w_out)
        unit, _ = norm(hidden_ref[...].astype(F32))
        a = (unit * norms_ref[0:1] + norms_ref[4:5]).astype(BF)
        at_ref[...] = a.T
        keys = lax.broadcasted_iota(jnp.int32, (length, length), 0)
        queries = lax.broadcasted_iota(jnp.int32, (length, length), 1)
        allowed = (keys <= queries) & (keys.astype(F32) < nums_ref[0:1, 0:1])
        bias[...] = jnp.where(allowed, 0.0, -1e30)
        copies.wait()
        qk = mm(a, w_qk[...])
        q = (qk[:, :HALF].astype(BF).astype(F32) * HEAD_DIM ** (-0.5)).astype(BF)
        k = qk[:, HALF:].astype(BF)
        v = mm(a, w_v[...]).astype(BF)
        qkv_ref[:, 0:HALF] = q
        qkv_ref[:, HALF : 2 * HALF] = k
        qkv_ref[:, 2 * HALF :] = v
        qt_ref[...] = q.T
        kt_ref[...] = k.T
        vt[...] = v.T
        for h in range(HEADS):
            heads[h] = k[:, h * HEAD_DIM : (h + 1) * HEAD_DIM]

        def head(h, carry):
            s = mm(heads[h], qt_ref[head_rows(h), :]) + bias[...]
            top = jnp.max(s, axis=0, keepdims=True)
            p = jnp.exp(s - top)
            total = jnp.sum(p, axis=0, keepdims=True)
            o = mm(vt[head_rows(h), :], p.astype(BF))
            ot_ref[head_rows(h), :] = (o / total).astype(BF)
            lse_ref[h] = top + jnp.log(total)
            return carry

        lax.fori_loop(0, HEADS, head, 0)
        part_ref[...] = project(ot_ref[...].T, w_out).astype(BF)

    return run(
        body,
        [
            shaped((length, D)),
            shaped((D, length)),
            shaped((length, 3 * HALF)),
            shaped((HALF, length)),
            shaped((HALF, length)),
            shaped((HALF, length)),
            shaped((HEADS, 1, length), F32),
        ],
        vmem=[hidden, norms, nums],
        hbm=weights,
        scratch=[
            pltpu.VMEM((D, D), BF),
            pltpu.VMEM((D, HALF), BF),
            pltpu.VMEM((2, HALF, HALF), BF),
            pltpu.VMEM((HALF, length), BF),
            pltpu.VMEM((HEADS, length, HEAD_DIM), BF),
            pltpu.VMEM((length, length), F32),
        ],
        copies=ATTENTION_COPIES,
        micros=10,
        after=after,
    )


def turn(value, after=()):
    rows, columns = value.shape

    def body(ref, out_ref):
        for at in range(0, rows, CHUNK):
            out_ref[:, at : at + CHUNK] = ref[at : at + CHUNK, :].T

    return run(body, [shaped((columns, rows))], vmem=[value], micros=4, after=after)[0]


def cross_memory(encoded, weights):
    frames = encoded.shape[0]

    def body(enc_ref, *refs):
        w_refs, refs = refs[: len(weights)], refs[len(weights) :]
        kv_ref, kvt_ref, w_kv, sems = refs
        _, xy, _ = where_am_i()
        copies = Copies(sems)
        load_wide(copies, w_refs, 1, 0, xy, w_kv)
        copies.wait()

        def step(i, carry):
            here = pl.ds(pl.multiple_of(i * CHUNK, CHUNK), CHUNK)
            kv = mm(enc_ref[here, :], w_kv[...]).astype(BF)
            kv_ref[here, :] = kv
            kvt_ref[:, here] = kv.T
            return carry

        lax.fori_loop(0, frames // CHUNK, step, 0)

    return run(
        body,
        [shaped((frames, D)), shaped((D, frames))],
        vmem=[encoded],
        hbm=weights,
        scratch=[pltpu.VMEM((D, D), BF)],
        copies=4,
        micros=6,
    )


def residual(hidden_ref, mine_ref, other_ref):
    return hidden_ref[...].astype(F32) + (mine_ref[...].astype(F32) + other_ref[...].astype(F32))


def cross_forward(hidden, mine, other, norms, nums, kv, kvt, weights):
    length = hidden.shape[0]
    frames = kv.shape[0]

    def body(hidden_ref, mine_ref, other_ref, norms_ref, nums_ref, kv_ref, kvt_ref, *refs):
        w_refs, refs = refs[: len(weights)], refs[len(weights) :]
        part_ref, h_ref, ct_ref, q_ref, qt_ref, ot_ref, lse_ref = refs[:7]
        w_q, w_out, heads, values_t, scores, sems = refs[7:]
        _, xy, _ = where_am_i()
        copies = Copies(sems)
        load_wide(copies, w_refs, 1, 1, xy, w_q, HALF)
        load_out(copies, w_refs, 1, xy, w_out)
        h1 = residual(hidden_ref, mine_ref, other_ref)
        h_ref[...] = h1
        unit, _ = norm(h1)
        c = (unit * norms_ref[1:2] + norms_ref[5:6]).astype(BF)
        ct_ref[...] = c.T
        frame = lax.broadcasted_iota(jnp.int32, (frames, HEAD_DIM), 0).astype(F32)
        lane = lax.broadcasted_iota(jnp.int32, (frames, HEAD_DIM), 1)
        mask = jnp.where(frame < nums_ref[1:2, 0:1], 0.0, -1e30)
        beside = jnp.where(lane == 0, mask, 0.0).astype(BF)
        one = lax.broadcasted_iota(jnp.int32, (16, frames), 0)
        one = jnp.where(one == 0, 1.0, 0.0).astype(BF)
        for h in range(HEADS):
            keys = kv_ref[:, h * HEAD_DIM : (h + 1) * HEAD_DIM]
            heads[h] = jnp.concatenate([keys, beside], axis=1)
            values = kvt_ref[HALF + h * HEAD_DIM : HALF + (h + 1) * HEAD_DIM, :]
            values_t[h] = jnp.concatenate([values, one], axis=0)
        copies.wait()
        q = mm(c, w_q[...]).astype(BF)
        q = (q.astype(F32) * HEAD_DIM ** (-0.5)).astype(BF)
        q_ref[...] = q
        qt_ref[...] = q.T
        ones = jnp.ones((1, length), F32)

        def head(h, carry):
            qt = below(qt_ref[head_rows(h), :], [ones])
            top = None
            for at in range(0, frames, CHUNK):
                s = mm(heads[h, at : at + CHUNK], qt)
                scores[at : at + CHUNK] = s
                high = jnp.max(s, axis=0, keepdims=True)
                top = high if top is None else jnp.maximum(top, high)
            o = None
            for at in range(0, frames, CHUNK):
                p = jnp.exp(scores[at : at + CHUNK] - top).astype(BF)
                more = mm(values_t[h, :, at : at + CHUNK], p)
                o = more if o is None else o + more
            total = o[HEAD_DIM : HEAD_DIM + 1]
            ot_ref[head_rows(h), :] = (o[:HEAD_DIM] / total).astype(BF)
            lse_ref[h] = top + jnp.log(total)
            return carry

        lax.fori_loop(0, HEADS, head, 0)
        part_ref[...] = project(ot_ref[...].T, w_out).astype(BF)

    return run(
        body,
        [
            shaped((length, D)),
            shaped((length, D), F32),
            shaped((D, length)),
            shaped((length, HALF)),
            shaped((HALF, length)),
            shaped((HALF, length)),
            shaped((HEADS, 1, length), F32),
        ],
        vmem=[hidden, mine, other, norms, nums, kv, kvt],
        hbm=weights,
        scratch=[
            pltpu.VMEM((D, HALF), BF),
            pltpu.VMEM((2, HALF, HALF), BF),
            pltpu.VMEM((HEADS, frames, 2 * HEAD_DIM), BF),
            pltpu.VMEM((HEADS, HEAD_DIM + 16, frames), BF),
            pltpu.VMEM((frames, length), F32),
        ],
        copies=4 + 16,
        micros=10,
    )


def units_forward(hidden, mine, other, norms, weights):
    length = hidden.shape[0]

    def body(hidden_ref, mine_ref, other_ref, norms_ref, *refs):
        w_refs, refs = refs[: len(weights)], refs[len(weights) :]
        part_ref, h_ref, mt_ref, slope_ref, it_ref = refs[:5]
        w_up, w_down, inner, late_sems, sems = refs[5:]
        _, xy, _ = where_am_i()
        copies = Copies(sems)
        load_up(copies, w_refs, w_up)
        late = Copies(late_sems)
        load_down(late, w_refs, w_down)
        h2 = residual(hidden_ref, mine_ref, other_ref)
        h_ref[...] = h2
        unit, _ = norm(h2)
        m = (unit * norms_ref[2:3] + norms_ref[6:7]).astype(BF)
        mt_ref[...] = m.T
        copies.wait()
        for at in range(0, 2 * D, CHUNK):
            here = slice(at, at + CHUNK)
            z = mm(m, w_up[:, here])
            share = 0.5 * (1.0 + lax.erf(z * 0.7071067811865476))
            slope = share + z * (0.3989422804014327 * jnp.exp(-0.5 * z * z))
            value = (z * share).astype(BF)
            inner[:, here] = value
            it_ref[here, :] = value.T
            slope_ref[:, here] = slope.astype(BF)
        late.wait()
        for at in range(0, D, CHUNK):
            part_ref[:, at : at + CHUNK] = mm(inner[...], w_down[:, at : at + CHUNK]).astype(BF)

    return run(
        body,
        [
            shaped((length, D)),
            shaped((length, D), F32),
            shaped((D, length)),
            shaped((length, 2 * D)),
            shaped((2 * D, length)),
        ],
        vmem=[hidden, mine, other, norms],
        hbm=weights,
        scratch=[
            pltpu.VMEM((D, 2 * D), BF),
            pltpu.VMEM((2 * D, D), BF),
            pltpu.VMEM((length, 2 * D), BF),
            pltpu.SemaphoreType.DMA((DOWN_COPIES,)),
        ],
        copies=UP_COPIES,
        micros=9,
    )


def store_blocks(value, blocks, first_ref, second_ref):
    core, _, z = where_am_i()
    for b in range(4):
        blocks[b] = value[:, b * QUARTER : (b + 1) * QUARTER]
    first_ref[...] = blocks[2 * core + z % 2].T
    second_ref[...] = blocks[2 * core + (z + 1) % 2].T


def units_backward(hidden, mine, other, norms, nums, cot, slope, weights):
    length = hidden.shape[0]

    def body(hidden_ref, mine_ref, other_ref, norms_ref, nums_ref, cot_ref, slope_ref, *refs):
        w_refs, refs = refs[: len(weights)], refs[len(weights) :]
        part_ref, d_ref, e_ref, dz_ref, terms_ref, first_ref, second_ref = refs[:7]
        w_up, w_down, blocks, late_sems, sems = refs[7:]
        _, xy, _ = where_am_i()
        copies = Copies(sems)
        load_down(copies, w_refs, w_down)
        late = Copies(late_sems)
        load_up(late, w_refs, w_up)
        unit, inverse = norm(residual(hidden_ref, mine_ref, other_ref))
        final = (unit * norms_ref[3:4] + norms_ref[7:8]).astype(BF)
        store_blocks(final, blocks, first_ref, second_ref)
        live = lax.broadcasted_iota(jnp.int32, (length, 1), 0).astype(F32) < nums_ref[0:1, 0:1]
        grad = cot_ref[...].astype(F32) * jnp.where(live, nums_ref[2:3, 0:1], 0.0)
        d3, terms = norm_back(grad, unit, inverse, norms_ref[3:4])
        d_ref[...] = d3
        terms_ref[...] = terms
        e = d3.astype(BF)
        e_ref[...] = e
        copies.wait()
        for at in range(0, 2 * D, CHUNK):
            here = slice(at, at + CHUNK)
            d_inner = mm_t(e, w_down[here, :])
            dz_ref[:, here] = (slope_ref[:, here].astype(F32) * d_inner).astype(BF)
        late.wait()
        for at in range(0, D, CHUNK):
            out = mm_t(dz_ref[...], w_up[at : at + CHUNK, :])
            part_ref[:, at : at + CHUNK] = out.astype(BF)

    return run(
        body,
        [
            shaped((length, D)),
            shaped((length, D), F32),
            shaped((length, D)),
            shaped((length, 2 * D)),
            shaped((2, D), F32),
            shaped((QUARTER, length)),
            shaped((QUARTER, length)),
        ],
        vmem=[hidden, mine, other, norms, nums, cot, slope],
        hbm=weights,
        scratch=[
            pltpu.VMEM((D, 2 * D), BF),
            pltpu.VMEM((2 * D, D), BF),
            pltpu.VMEM((4, length, QUARTER), BF),
            pltpu.SemaphoreType.DMA((UP_COPIES,)),
        ],
        copies=DOWN_COPIES,
        micros=10,
    )


def step_back(d_ref, hidden_ref, mine_ref, other_ref, gain):
    unit, inverse = norm(hidden_ref[...].astype(F32))
    grad = mine_ref[...].astype(F32) + other_ref[...].astype(F32)
    part, terms = norm_back(grad, unit, inverse, gain)
    return d_ref[...] + part, terms


def cross_backward(
    d, hidden, mine, other, norms, nums, kv, kvt, q, qt, ot, lse, weights, after=()
):
    length = hidden.shape[0]
    frames = kv.shape[0]

    def body(
        d_ref, hidden_ref, mine_ref, other_ref, norms_ref, nums_ref, kv_ref, kvt_ref, q_ref,
        qt_ref, ot_ref, lse_ref, *refs
    ):
        w_refs, refs = refs[: len(weights)], refs[len(weights) :]
        part_ref, d_out_ref, e_ref, dq_ref, dkv_ref, terms_ref = refs[:6]
        w_q, w_out, keys, values, queries, grads, dot_t, dk_h, dv_h, dqt, sems = refs[6:]
        _, xy, _ = where_am_i()
        copies = Copies(sems)
        load_wide(copies, w_refs, 1, 1, xy, w_q, HALF)
        load_out(copies, w_refs, 1, xy, w_out)
        d2, terms = step_back(d_ref, hidden_ref, mine_ref, other_ref, norms_ref[2:3])
        d_out_ref[...] = d2
        terms_ref[...] = terms
        e = d2.astype(BF)
        e_ref[...] = e
        frame = lax.broadcasted_iota(jnp.int32, (frames, HEAD_DIM), 0).astype(F32)
        lane = lax.broadcasted_iota(jnp.int32, (frames, HEAD_DIM), 1)
        mask = jnp.where(frame < nums_ref[1:2, 0:1], 0.0, -1e30)
        beside = jnp.where(lane == 0, mask, jnp.where(lane < 4, 1.0, 0.0)).astype(BF)
        three = widened(3)(frames)
        for h in range(HEADS):
            lanes = slice(h * HEAD_DIM, (h + 1) * HEAD_DIM)
            keys[h] = jnp.concatenate([kv_ref[:, lanes], beside], axis=1)
            value = kv_ref[:, HALF + h * HEAD_DIM : HALF + (h + 1) * HEAD_DIM]
            values[h] = jnp.concatenate([value, three], axis=1)
            queries[h] = q_ref[:, lanes]
        copies.wait()
        d_mixed = project_t(e, w_out).astype(BF)
        dot_t[...] = d_mixed.T
        for h in range(HEADS):
            grads[h] = d_mixed[:, h * HEAD_DIM : (h + 1) * HEAD_DIM]
        ones = jnp.ones((1, length), F32)

        def head(h, carry):
            rows = head_rows(h)
            do_t = dot_t[rows, :]
            q_n, do_n = queries[h], grads[h]
            delta = jnp.sum(do_t.astype(F32) * ot_ref[rows, :].astype(F32), axis=0, keepdims=True)
            q_t = below(qt_ref[rows, :], [ones] + low_parts(-lse_ref[h]))
            do_t = below(do_t, low_parts(-delta))
            total = None
            for at in range(0, frames, CHUNK):
                here = slice(at, at + CHUNK)
                p = jnp.exp(mm(keys[h, here], q_t))
                ds = (p * mm(values[h, here], do_t)).astype(BF)
                dv_h[h, here] = mm(p.astype(BF), do_n).astype(BF)
                dk_h[h, here] = mm(ds, q_n).astype(BF)
                more = mm(kvt_ref[rows, here], ds)
                total = more if total is None else total + more
            dqt[rows, :] = (total * HEAD_DIM ** (-0.5)).astype(BF)
            return carry

        lax.fori_loop(0, HEADS, head, 0)
        dq = dqt[...].T
        dq_ref[...] = dq
        part_ref[...] = mm_t(dq, w_q[...]).astype(BF)
        for h in range(HEADS):
            lanes = slice(h * HEAD_DIM, (h + 1) * HEAD_DIM)
            dkv_ref[:, lanes] = dk_h[h]
            dkv_ref[:, HALF + h * HEAD_DIM : HALF + (h + 1) * HEAD_DIM] = dv_h[h]

    return run(
        body,
        [
            shaped((length, D)),
            shaped((length, D), F32),
            shaped((length, D)),
            shaped((length, HALF)),
            shaped((frames, D)),
            shaped((2, D), F32),
        ],
        vmem=[d, hidden, mine, other, norms, nums, kv, kvt, q, qt, ot, lse],
        hbm=weights,
        scratch=[
            pltpu.VMEM((D, HALF), BF),
            pltpu.VMEM((2, HALF, HALF), BF),
            pltpu.VMEM((HEADS, frames, 2 * HEAD_DIM), BF),
            pltpu.VMEM((HEADS, frames, 2 * HEAD_DIM), BF),
            pltpu.VMEM((HEADS, length, HEAD_DIM), BF),
            pltpu.VMEM((HEADS, length, HEAD_DIM), BF),
            pltpu.VMEM((HALF, length), BF),
            pltpu.VMEM((HEADS, frames, HEAD_DIM), BF),
            pltpu.VMEM((HEADS, frames, HEAD_DIM), BF),
            pltpu.VMEM((HALF, length), BF),
        ],
        copies=4 + 16,
        micros=22,
        after=after,
    )


def self_backward(d, hidden, mine, other, norms, nums, qkv, qt, kt, ot, lse, weights, after=()):
    length = hidden.shape[0]

    def body(
        d_ref, hidden_ref, mine_ref, other_ref, norms_ref, nums_ref, qkv_ref, qt_ref, kt_ref,
        ot_ref, lse_ref, *refs
    ):
        w_refs, refs = refs[: len(weights)], refs[len(weights) :]
        part_ref, d_out_ref, e_ref, dqk_ref, dv_ref, terms_ref = refs[:6]
        w_qk, w_v, w_out, queries_h, keys, values, grads, dot_t, dk_h, dv_h, dqt, bias, sems = refs[6:]
        _, xy, _ = where_am_i()
        copies = Copies(sems)
        load_out(copies, w_refs, 0, xy, w_out)
        load_wide(copies, w_refs, 0, 0, xy, w_qk)
        load_wide(copies, w_refs, 0, 1, xy, w_v, HALF)
        d1, terms = step_back(d_ref, hidden_ref, mine_ref, other_ref, norms_ref[1:2])
        d_out_ref[...] = d1
        terms_ref[...] = terms
        e = d1.astype(BF)
        e_ref[...] = e
        places = lax.broadcasted_iota(jnp.int32, (length, length), 0)
        queries = lax.broadcasted_iota(jnp.int32, (length, length), 1)
        allowed = (places <= queries) & (places.astype(F32) < nums_ref[0:1, 0:1])
        bias[...] = jnp.where(allowed, 0.0, -1e30)
        three = widened(3)(length)
        for h in range(HEADS):
            at = h * HEAD_DIM
            queries_h[h] = qkv_ref[:, at : at + HEAD_DIM]
            key = qkv_ref[:, HALF + at : HALF + at + HEAD_DIM]
            keys[h] = jnp.concatenate([key, three], axis=1)
            value = qkv_ref[:, 2 * HALF + at : 2 * HALF + at + HEAD_DIM]
            values[h] = jnp.concatenate([value, three], axis=1)
        copies.wait()
        d_mixed = project_t(e, w_out).astype(BF)
        dot_t[...] = d_mixed.T
        for h in range(HEADS):
            grads[h] = d_mixed[:, h * HEAD_DIM : (h + 1) * HEAD_DIM]

        def head(h, carry):
            rows = head_rows(h)
            do_t, do_n = dot_t[rows, :], grads[h]
            delta = jnp.sum(do_t.astype(F32) * ot_ref[rows, :].astype(F32), axis=0, keepdims=True)
            q_t = below(qt_ref[rows, :], low_parts(-lse_ref[h]))
            do_t = below(do_t, low_parts(-delta))
            p = jnp.exp(mm(keys[h], q_t) + bias[...])
            ds = (p * mm(values[h], do_t)).astype(BF)
            dv_h[h] = mm(p.astype(BF), do_n).astype(BF)
            dk_h[h] = mm(ds, queries_h[h]).astype(BF)
            dqt[rows, :] = (mm(kt_ref[rows, :], ds) * HEAD_DIM ** (-0.5)).astype(BF)
            return carry

        lax.fori_loop(0, HEADS, head, 0)
        dqk_ref[:, 0:HALF] = dqt[...].T
        for h in range(HEADS):
            lanes = slice(HALF + h * HEAD_DIM, HALF + (h + 1) * HEAD_DIM)
            dqk_ref[:, lanes] = dk_h[h]
            dv_ref[:, h * HEAD_DIM : (h + 1) * HEAD_DIM] = dv_h[h]
        out = mm_t(dqk_ref[...], w_qk[...]) + mm_t(dv_ref[...], w_v[...])
        part_ref[...] = out.astype(BF)

    return run(
        body,
        [
            shaped((length, D)),
            shaped((length, D), F32),
            shaped((length, D)),
            shaped((length, D)),
            shaped((length, HALF)),
            shaped((2, D), F32),
        ],
        vmem=[d, hidden, mine, other, norms, nums, qkv, qt, kt, ot, lse],
        hbm=weights,
        scratch=[
            pltpu.VMEM((D, D), BF),
            pltpu.VMEM((D, HALF), BF),
            pltpu.VMEM((2, HALF, HALF), BF),
            pltpu.VMEM((HEADS, length, HEAD_DIM), BF),
            pltpu.VMEM((HEADS, length, 2 * HEAD_DIM), BF),
            pltpu.VMEM((HEADS, length, 2 * HEAD_DIM), BF),
            pltpu.VMEM((HEADS, length, HEAD_DIM), BF),
            pltpu.VMEM((HALF, length), BF),
            pltpu.VMEM((HEADS, length, HEAD_DIM), BF),
            pltpu.VMEM((HEADS, length, HEAD_DIM), BF),
            pltpu.VMEM((HALF, length), BF),
            pltpu.VMEM((length, length), F32),
        ],
        copies=ATTENTION_COPIES,
        micros=12,
        staged=True,
        after=after,
    )


def finish_hidden(d, hidden, mine, other, norms, terms1, terms2, terms3, after=()):
    length = hidden.shape[0]

    def body(
        d_ref, hidden_ref, mine_ref, other_ref, norms_ref, one, two, three, terms_ref, first_ref,
        second_ref, blocks
    ):
        d0, terms = step_back(d_ref, hidden_ref, mine_ref, other_ref, norms_ref[0:1])
        store_blocks(d0.astype(BF), blocks, first_ref, second_ref)
        for j in range(2):
            here = slice(j, j + 1)
            terms_ref[4 * j : 4 * j + 4] = jnp.concatenate(
                [terms[here], one[here], two[here], three[here]], axis=0
            )

    return run(
        body,
        [shaped((8, D), F32), shaped((QUARTER, length)), shaped((QUARTER, length))],
        vmem=[d, hidden, mine, other, norms, terms1, terms2, terms3],
        scratch=[pltpu.VMEM((4, length, QUARTER), BF)],
        micros=4,
        after=after,
    )


def finish_encoder(keep, other, frames, after=()):
    def body(keep_ref, other_ref, first_ref, second_ref):
        _, _, z = where_am_i()
        for ref, k in ((first_ref, 0), (second_ref, 1)):
            here = pl.ds(pl.multiple_of(((z + k) % 2) * QUARTER, QUARTER), QUARTER)
            total = keep_ref[here, :].astype(F32) + other_ref[here, :].astype(F32)
            ref[...] = total.astype(BF)[:, :frames]

    return run(
        body,
        [shaped((QUARTER, frames)), shaped((QUARTER, frames))],
        vmem=[keep, other],
        micros=2,
        after=after,
    )


def block_plan(place):
    if not place.fast:
        return 1, (((1, 0, 0),), ((1, 0, 0),))
    first = ((1, 0, 0), (0, 0, 1), (1, 1, 2), (0, 1, 3))
    second = ((1, 0, 0), (1, 1, 1), (0, 0, 2), (0, 1, 3))
    return 4, (first, second)


def grad_outputs(place, shape):
    if place.fast:
        return [shaped((2,) + shape)] * 4
    return [shaped((1,) + shape)] * 4


def units_grads(place, mt, dz, it, e):
    chips = place.chips
    rows = D // (2 * chips)
    _, plan = block_plan(place)

    def body(mt_ref, dz_ref, it_ref, e_ref, *outs):
        _, xy, _ = where_am_i()
        for output, slot, offset in plan[1]:
            chip = xy ^ offset
            for z in range(4):
                here = pl.ds(pl.multiple_of(z * HALF + chip * rows, 16), rows)
                outs[2 + output][slot, z] = mm(it_ref[here, :], e_ref[...]).astype(BF)
        for output, slot, offset in plan[0]:
            here = pl.ds(pl.multiple_of((xy ^ offset) * 2 * rows, 16), 2 * rows)
            left = mm(mt_ref[here, :], dz_ref[...]).astype(BF)
            for z in range(4):
                outs[output][slot, z] = left[:, z * HALF : (z + 1) * HALF]

    def plain(mt_ref, dz_ref, it_ref, e_ref, left_ref, right_ref):
        left_ref[...] = mm(mt_ref[...], dz_ref[...]).astype(BF)
        right_ref[...] = mm(it_ref[...], e_ref[...]).astype(BF)

    if place.fast:
        first, second = shaped((2, 4, 2 * rows, HALF)), shaped((2, 4, rows, D))
        return run(
            body, [first, first, second, second], vmem=[mt, dz, it, e], micros=6
        )
    left, right = run(
        plain, [shaped((D, 2 * D)), shaped((2 * D, D))], vmem=[mt, dz, it, e], micros=7
    )
    left = left.reshape(chips, 2 * rows, 4, HALF).transpose(0, 2, 1, 3)
    right = right.reshape(4, chips, rows, 2, HALF).transpose(1, 0, 3, 2, 4)
    whole = jnp.concatenate([left, right.reshape(chips, 4, 2 * rows, HALF)], axis=-1)
    return whole.reshape(4 * chips, 2 * rows, D)


def units_sum(grads, came, onward, after):
    rows = grads[3].shape[2]

    def body(*refs):
        ins, (out_ref, left, right, sems) = refs[:6], refs[6:]
        copies = Copies(sems)
        for i, ref in enumerate(ins):
            target = (left if i < 3 else right).at[i % 3]
            copies.start(ref if i % 3 == 2 else ref.at[0], target)
        copies.wait()
        for z in range(4):
            out_ref[z, :, 0:HALF] = add_up(*[left[i, z] for i in range(3)]).astype(BF)
            down = add_up(*[right[i, z] for i in range(3)]).astype(BF)
            out_ref[z, 0:rows, HALF:D] = down[:, :HALF]
            out_ref[z, rows : 2 * rows, HALF:D] = down[:, HALF:]

    return run(
        body,
        [shaped((4, 2 * rows, D))],
        hbm=[grads[1], came[0], onward[0], grads[3], came[1], onward[1]],
        scratch=[pltpu.VMEM((3, 4, 2 * rows, HALF), BF), pltpu.VMEM((3, 4, rows, D), BF)],
        copies=6,
        micros=3,
        after=after,
    )[0]


def attention_grads(place, wide_left, wide_right, left, right, ot, e, after=()):
    count, plan = block_plan(place)
    rows = D // count
    few = rows // 4

    def body(wide_left_ref, wide_right_ref, left_ref, right_ref, ot_ref, e_ref, *outs):
        _, xy, _ = where_am_i()
        for output, slot, offset in plan[0]:
            chip = xy ^ offset if count > 1 else 0
            here = pl.ds(pl.multiple_of(chip * rows, 16), rows)
            outs[output][slot] = mm(wide_left_ref[here, :], wide_right_ref[...]).astype(BF)
        for output, slot, offset in plan[1]:
            chip = xy ^ offset if count > 1 else 0
            here = pl.ds(pl.multiple_of(chip * rows, 16), rows)
            target = outs[2 + output]
            target[slot, :, 0:HALF] = mm(left_ref[here, :], right_ref[...]).astype(BF)
            for hi in range(2):
                here = pl.ds(pl.multiple_of(hi * QUARTER + chip * few, 16), few)
                both = mm(ot_ref[here, :], e_ref[...]).astype(BF)
                for q in range(2):
                    at = (2 * q + hi) * few
                    target[slot, at : at + few, HALF:D] = both[:, q * HALF : (q + 1) * HALF]

    return run(
        body,
        grad_outputs(place, (rows, D)),
        vmem=[wide_left, wide_right, left, right, ot, e],
        micros=6,
        after=after,
    )


def encoder_grad(dkv, weights, after=()):
    padded = dkv.shape[0]

    def body(dkv_ref, *refs):
        w_refs, (keep_ref, send_ref, w_kv, sems) = refs[: len(weights)], refs[len(weights) :]
        core, xy, _ = where_am_i()
        copies = Copies(sems)
        load_wide(copies, w_refs, 1, 0, xy, w_kv)
        copies.wait()
        mine = pl.ds(pl.multiple_of(core * HALF, HALF), HALF)
        theirs = pl.ds(pl.multiple_of((1 - core) * HALF, HALF), HALF)
        for ref, rows in ((send_ref, theirs), (keep_ref, mine)):
            for at in range(0, padded, CHUNK):
                value = mm_t(w_kv[rows, :], dkv_ref[at : at + CHUNK, :])
                ref[:, at : at + CHUNK] = value.astype(BF)

    return run(
        body,
        [shaped((HALF, padded)), shaped((HALF, padded))],
        vmem=[dkv],
        hbm=weights,
        scratch=[pltpu.VMEM((D, D), BF)],
        copies=4,
        micros=3.5,
        after=after,
    )


def leave_plane(place, grads):
    return [place.swap_xy(grads[0], 1), place.swap_xy(grads[2], 2)]


def pass_on(grads, came, after):
    shapes = [grads[1].shape[1:], grads[3].shape[1:]]

    def body(stay0, came0, stay1, came1, out0, out1, held0, held1, sems):
        copies = Copies(sems)
        for i, ref in enumerate((stay0, came0, stay1, came1)):
            copies.start(ref.at[1], (held0 if i < 2 else held1).at[i % 2])
        copies.wait()
        out0[...] = add_up(held0[0], held0[1]).astype(BF)
        out1[...] = add_up(held1[0], held1[1]).astype(BF)

    return run(
        body,
        [shaped(shape) for shape in shapes],
        hbm=[grads[1], came[0], grads[3], came[1]],
        scratch=[pltpu.VMEM((2,) + shape, BF) for shape in shapes],
        copies=4,
        micros=1,
        after=after,
    )


def cross_plane(place, onward):
    return [place.swap_xy(onward[0], 2), place.swap_xy(onward[1], 1)]


def column_blocks(grads, came, onward, swapped, norm_terms=(), after=()):
    shape = onward[0].shape
    rows = shape[-2] // 2
    width = D
    few = rows // 4
    extra = 16 if norm_terms else 0

    def body(*refs):
        terms_refs, refs = refs[: len(norm_terms)], refs[len(norm_terms) :]
        ins, outs, (held, shards, sems) = refs[:6], refs[6:-3], refs[-3:]
        home, slots = column_slots()
        copies = Copies(sems)
        for i, ref in enumerate(ins):
            copies.start(ref if i % 3 == 2 else ref.at[0], held.at[i])
        copies.wait()
        sums = [add_up(held[3 * part], held[3 * part + 1], held[3 * part + 2]) for part in range(2)]
        for hi in range(2):
            for cs in range(2):
                here = slice(cs * rows, (cs + 1) * rows)
                lanes = slice(hi * QUARTER, (hi + 1) * QUARTER)
                lanes_two = slice(HALF + hi * QUARTER, HALF + (hi + 1) * QUARTER)
                outs_rows = []
                for p in range(4):
                    at = (2 * (p // 2) + hi) * 2 * few + cs * few
                    side = HALF + (p % 2) * QUARTER
                    outs_rows.append(sums[1][at : at + few, side : side + QUARTER])
                value = jnp.concatenate(
                    [
                        sums[0][here, lanes],
                        sums[0][here, lanes_two],
                        sums[1][here, lanes],
                        jnp.concatenate(outs_rows, axis=0),
                    ],
                    axis=1,
                )
                shards[2 * hi + cs, :rows] = value.astype(BF)
        if norm_terms:
            core, xy, _ = where_am_i()
            terms = add_up(*[ref[...] for ref in terms_refs])
            terms = jnp.concatenate([terms, jnp.zeros_like(terms)], axis=0).astype(BF)
            feature = lax.broadcasted_iota(jnp.int32, (D, D), 0)
            lane = lax.broadcasted_iota(jnp.int32, (D, D), 1)
            for hi in range(2):
                for cs in range(2):
                    offset = (2 * core + hi) * QUARTER + (2 * xy + cs) * few
                    pick = jnp.where((feature == lane + offset) & (lane < few), 1.0, 0.0)
                    shards[2 * hi + cs, rows:] = mm(terms, pick.astype(BF)).astype(BF)
        if swapped:
            core, _, _ = where_am_i()
            for hi in range(2):
                outs[0][hi] = shards[2 * hi + core]
                outs[1][hi] = shards[2 * hi + 1 - core]
        else:
            for k in range(4):
                outs[k][...] = shards[slots[k]]

    ins = [grads[1], came[0], onward[0], grads[3], came[1], onward[1]]
    return run(
        body,
        [shaped((2, rows, width))] * 2 if swapped else [shaped((rows + extra, width))] * 4,
        vmem=list(norm_terms),
        hbm=ins,
        after=after,
        scratch=[pltpu.VMEM((6,) + shape, BF), pltpu.VMEM((4, rows + extra, width), BF)],
        copies=6,
        micros=2,
    )


def scatter_column(place, kept, came):
    first = place.core == 0
    both = jnp.concatenate([jnp.where(first, kept, came), jnp.where(first, came, kept)])
    return lax.psum_scatter(both, "mp", scatter_dimension=0, tiled=False)


def sum_plain(place, grads, attention):
    wide, narrow = grads[1][0], grads[3][0]
    rows = D // place.dp
    if attention:
        value = jnp.stack([wide[:, :HALF], wide[:, HALF:], narrow[:, :HALF]], axis=1)
        value = value.reshape(place.dp, rows, 3, 2, QUARTER).transpose(3, 0, 1, 2, 4)
        value = value.reshape(2, place.dp, rows, 3 * QUARTER)
        outs = narrow[:, HALF:].reshape(2, 2, place.dp, rows // 4, 2, QUARTER)
        outs = outs.transpose(1, 2, 0, 4, 3, 5).reshape(2, place.dp, rows, QUARTER)
        value = jnp.concatenate([value, outs], axis=-1)
    else:
        value = jnp.concatenate(
            [wide.reshape(2, place.dp, rows, D), narrow.reshape(2, place.dp, rows, D)], axis=-1
        )
    whole = jnp.zeros((2,) + value.shape, F32)
    whole = lax.dynamic_update_index_in_dim(whole, value.astype(F32), place.core, 0)
    whole = whole.reshape((4 * place.dp,) + value.shape[2:])
    return lax.psum_scatter(whole, ("mp", "xy", "core"), scatter_dimension=0, tiled=False)


def attention_outputs(sums, rows, few):
    value = sums[:rows]
    last = value[:, 3 * QUARTER :]
    out = jnp.concatenate([last[p * few : (p + 1) * few] for p in range(4)], axis=1)
    return [value[:, j * QUARTER : (j + 1) * QUARTER] for j in range(3)], out


def finish_self(got, own, few_lanes):
    rows = own.shape[0] - 16
    few = rows // 4

    def body(a, b, c, d, own_ref, qkv_ref, out_ref, gain_ref, bias_ref):
        home, _ = column_slots()
        last = jnp.where(home, own_ref[...].astype(F32), d[...].astype(F32))
        sums = add_up(a[...], b[...], c[...], last)
        blocks, out = attention_outputs(sums, rows, few)
        for j in range(3):
            qkv_ref[j] = blocks[j]
        out_ref[...] = out
        gain_ref[...] = sums[rows : rows + 4, :few_lanes]
        bias_ref[...] = sums[rows + 4 : rows + 8, :few_lanes]

    return run(
        body,
        [
            shaped((3, rows, QUARTER), F32),
            shaped((few, D), F32),
            shaped((4, few_lanes), F32),
            shaped((4, few_lanes), F32),
        ],
        vmem=list(got) + [own],
        micros=1.5,
    )


def finish_cross(total):
    rows = total.shape[0]
    few = rows // 4

    def body(ref, kv_ref, q_ref, out_ref):
        blocks, out = attention_outputs(ref[...].astype(F32), rows, few)
        kv_ref[...] = jnp.concatenate(blocks[:2], axis=1)
        q_ref[...] = blocks[2]
        out_ref[...] = out

    return run(
        body,
        [shaped((rows, HALF), F32), shaped((rows, QUARTER), F32), shaped((few, D), F32)],
        vmem=[total],
        micros=1.5,
    )


def from_quarters(value):
    few = value.shape[0] // 4
    return value.reshape(4, few, QUARTER).transpose(1, 0, 2).reshape(few, D)


def three_parts(value):
    terms = []
    for _ in range(3):
        term = lax.reduce_precision(value, 8, 7)
        terms.append(term.astype(BF))
        value = value - term
    return jnp.concatenate(terms)


def per_device(
    dp,
    mp,
    hidden_in,
    encoder_states,
    cotangent,
    self_qkv,
    self_out,
    cross_q,
    cross_kv,
    cross_out,
    fc_in,
    fc_out,
    ln_gain,
    ln_bias,
    token_lengths,
    audio_lengths,
    corpus_ids,
    corpus_weights,
):
    place = Place(dp, mp)
    length = hidden_in.shape[2]
    frames = encoder_states.shape[2]
    padded = -(-frames // CHUNK) * CHUNK
    rows = self_qkv.shape[0]

    encoded = lax.dynamic_index_in_dim(encoder_states[:, 0], place.micro, 0, keepdims=False)
    first = ()
    if place.fast:
        shard = attention_shard(self_qkv, self_out, cross_kv, cross_q, cross_out)
        packed = pack_attention(place.column_out(shard), shard, (encoded,))
        w_self = w_cross = spread(place, packed)
        first = (shard,)
        fc_in, packed = lax.optimization_barrier((fc_in, packed))
    else:
        quarter = lambda w: w.reshape(-1, 4, QUARTER).transpose(1, 0, 2).reshape(-1, QUARTER)
        flat = lambda w: w.reshape(rows, -1)
        w_self = attention_plain(
            place, jnp.concatenate([flat(self_qkv), quarter(self_out)], axis=1)
        )
        w_cross = attention_plain(
            place, jnp.concatenate([flat(cross_kv), cross_q, quarter(cross_out)], axis=1)
        )


    unit = unit_shard(place, fc_in, fc_out)
    if not place.fast:
        w_units = gather_units(place, unit)

    turned = lambda value: value[:, 0].transpose(0, 2, 1)
    numbers = jnp.concatenate([token_lengths.T, audio_lengths.T, corpus_ids.T])
    blocks = input_blocks(
        turned(hidden_in),
        three_parts(jnp.concatenate([ln_gain, ln_bias])),
        numbers,
        first,
    )
    got = place.rows_in(blocks)
    if place.fast:
        unit, got = lax.optimization_barrier((unit, got))
        stacked = stack_units(
            [unit] + [place.swap_z(unit, k) for k in (1, 2, 3)], tuple(w_self[3:5])
        )
        w_units = spread(place, stacked)
    hidden, norms, nums = prepare(got, place.swap_core(got), corpus_weights)

    other = place.move(encoded, lambda xy, core, z: (xy, 1 - core, z) if core == z // 2 else None)
    encoded = jnp.where(place.home == place.core, encoded, other)
    encoded = jnp.pad(encoded, ((0, padded - frames), (0, 0)))

    et = turn(encoded)
    part1, at, qkv, qt, kt, ot1, lse1 = self_forward(
        hidden, norms, nums, w_self, (et,) + ((stacked,) if place.fast else ())
    )
    other1 = place.swap_core(part1)
    got = place.rows_in(turned_blocks(turned(cotangent), (at,)))
    kv, kvt = cross_memory(encoded, w_cross)
    part2, h1, ct, q2, qt2, ot2, lse2 = cross_forward(
        hidden, part1, other1, norms, nums, kv, kvt, w_cross
    )
    other2 = place.swap_core(part2)
    cot = prepare_cotangent(got, place.swap_core(got), (part2,))
    part3, h2, mt, slope, it = units_forward(h1, part2, other2, norms, w_units)
    other3 = place.swap_core(part3)
    part, d3, e3, dz, terms3, out_a, out_b = units_backward(
        h2, part3, other3, norms, nums, cot, slope, w_units
    )
    other = place.swap_core(part)
    g_units = units_grads(place, mt, dz, it, e3)
    came_units = leave_plane(place, g_units) if place.fast else None
    layer_got = place.rows_sent((out_a, out_b))
    layer_out = place.rows_joined((out_a, out_b), layer_got)
    part, d2, e2, dq2, dkv, terms2 = cross_backward(
        d3, h2, part, other, norms, nums, kv, kvt, q2, qt2, ot2, lse2, w_cross, layer_got
    )
    other = place.swap_core(part)
    g_cross = attention_grads(place, et, dkv, ct, dq2, ot2, e2)
    came_cross = leave_plane(place, g_cross) if place.fast else None
    keep, send = encoder_grad(dkv, w_cross, (g_cross[0],))
    passed = pass_on(g_units, came_units, (keep,)) if place.fast else ()
    encoder_blocks = finish_encoder(keep, place.swap_core(send), frames, passed)
    encoder_got = place.rows_sent(encoder_blocks)
    held = encoder_blocks
    if place.fast:
        onward_units = cross_plane(place, passed)
        passed = pass_on(g_cross, came_cross, encoder_blocks)
        onward_cross = cross_plane(place, passed)
        g_units = units_sum(g_units, came_units, onward_units, passed)
        held = (g_units,)
    part, d1, e1, dqk, dv, terms1 = self_backward(
        d2, h1, part, other, norms, nums, qkv, qt, kt, ot1, lse1, w_self, held
    )
    other = place.swap_core(part)
    g_self = attention_grads(place, at, dqk, at, dv, ot1, e1)
    held = ()
    if place.fast:
        came_self = leave_plane(place, g_self)
        cross_blocks = column_blocks(
            g_cross, came_cross, onward_cross, True, (), [g_self[0]] + encoder_got
        )
        held = (cross_blocks[0],)
        s_cross = scatter_column(place, cross_blocks[0], place.swap_core(cross_blocks[1]))
    grad_encoder = place.rows_joined(encoder_blocks, encoder_got).astype(F32)
    terms, out_a, out_b = finish_hidden(
        d1, hidden, part, other, norms, terms1, terms2, terms3, held
    )
    hidden_got = place.rows_sent((out_a, out_b))
    grad_hidden = place.rows_joined((out_a, out_b), hidden_got).astype(F32)
    s_up, s_down = scatter_units(place, g_units, (terms,))

    few = D // (place.dp * place.mp)
    if place.fast:
        onward_self = cross_plane(place, pass_on(g_self, came_self, (s_down,)))
        terms = terms + place.swap_xy(terms, 1)
        blocks = column_blocks(
            g_self, came_self, onward_self, False, (terms, place.swap_xy(terms, 2)), (s_up,)
        )
        g_qkv, g_out, g_gain, g_bias = finish_self(place.column_back(blocks), blocks[3], few)
        g_ckv, g_cq, g_cout = finish_cross(s_cross)
        g_qkv = g_qkv.transpose(1, 0, 2)
    else:
        s_cross = sum_plain(place, g_cross, True)
        s_self = sum_plain(place, g_self, True)
        terms = jnp.where(place.core == 0, terms, 0.0)
        terms = lax.psum(terms, AXES)
        shares = lax.dynamic_slice_in_dim(terms, (place.z * place.dp + place.d) * few, few, 1)
        g_gain, g_bias = shares[:4], shares[4:]
        g_qkv, g_out = s_self[:, : 3 * QUARTER], from_quarters(s_self[:, 3 * QUARTER :])
        g_ckv, g_cq = s_cross[:, :HALF], s_cross[:, HALF : 3 * QUARTER]
        g_cout = from_quarters(s_cross[:, 3 * QUARTER :])
    return (
        layer_out,
        grad_hidden,
        grad_encoder,
        g_qkv.reshape(rows, 3, QUARTER),
        g_out,
        g_cq,
        g_ckv.reshape(rows, 2, QUARTER),
        g_cout,
        s_up,
        s_down,
        g_gain,
        g_bias,
    )


def solution(mesh):
    dp, mp = mesh.shape["dp"], mesh.shape["mp"]
    finer = Mesh(mesh.devices.reshape(dp // 2, 2, mp), AXES)
    both = ("xy", "core")
    rows = P(None, both, None, "mp")
    columns = P(both, None, "mp")
    pairs = P(both, "mp")
    units = P(("mp",) + both, None)
    each = P(None, both)
    return jax.shard_map(
        partial(per_device, dp, mp),
        mesh=finer,
        in_specs=(
            rows,
            P(None, both, None, None),
            rows,
            columns,
            units,
            pairs,
            columns,
            units,
            pairs,
            units,
            P(None, "mp"),
            P(None, "mp"),
            each,
            each,
            each,
            P(),
        ),
        out_specs=(
            rows,
            rows,
            rows,
            columns,
            units,
            pairs,
            columns,
            units,
            pairs,
            units,
            P(None, ("mp",) + both),
            P(None, ("mp",) + both),
        ),
        check_vma=False,
    )
```

```python
from functools import partial

import jax
import jax.numpy as jnp
from jax import lax
from jax.experimental import pallas as pl
from jax.experimental.pallas import tpu as pltpu
from jax.sharding import Mesh, PartitionSpec as P

D = 768
HALF = 384
QUARTER = 192
HEAD_DIM = 64
HEADS = 6
CHUNK = 256
BF = jnp.bfloat16
F32 = jnp.float32
AXES = ("xy", "core", "mp")
CHIPS = ("xy", "mp")
VMEM = pl.BlockSpec(memory_space=pltpu.VMEM)
SMEM = pl.BlockSpec(memory_space=pltpu.SMEM)
ANY = pl.BlockSpec(memory_space=pl.ANY)
HBM = pl.BlockSpec(memory_space=pltpu.HBM)


def mm(left, right):
    return jnp.dot(left, right, preferred_element_type=F32)


def mm_t(left, right):
    return lax.dot_general(left, right, (((1,), (1,)), ((), ())), preferred_element_type=F32)


def shaped(shape, dtype=BF):
    return jax.ShapeDtypeStruct(shape, dtype)


def room(shape, dtype):
    item = jnp.dtype(dtype).itemsize
    shape = (1, 1) + tuple(shape)
    tile = 32 // item
    size = item * (-(-shape[-1] // 128) * 128) * (-(-shape[-2] // tile) * tile)
    for extent in shape[:-2]:
        size *= extent
    return size


def run(
    body, outs, vmem=(), hbm=(), smem=(), scratch=(), copies=0, micros=2, after=(), staged=False
):
    args = tuple(smem) + tuple(vmem) + tuple(hbm)
    count = len(args)
    scratch = list(scratch)
    if copies:
        scratch.append(pltpu.SemaphoreType.DMA((copies,)))
    need = sum(room(a.shape, a.dtype) for a in tuple(vmem) + tuple(outs))
    need += sum(room(a.shape, a.dtype) for a in scratch if a.memory_space == pltpu.VMEM)
    need = min(need + 12 * 1024 * 1024, 60 * 1024 * 1024)
    moved = sum(a.size * a.dtype.itemsize for a in args) + sum(
        o.size * o.dtype.itemsize for o in outs
    )
    skip = len(scratch)
    if staged:
        scratch += [pltpu.VMEM(a.shape, a.dtype) for a in vmem]
        scratch.append(pltpu.SemaphoreType.DMA((len(vmem),)))

    def whole(*refs):
        ins, rest = list(refs[:count]), refs[count + len(after) :]
        if staged:
            held = rest[len(outs) + skip : -1]
            rest, sems = rest[: len(outs) + skip], rest[-1]
            copies = Copies(sems)
            for i, target in enumerate(held):
                copies.start(ins[len(smem) + i], target)
                ins[len(smem) + i] = target
            copies.wait()
        body(*ins, *rest)

    place = HBM if staged else VMEM
    return pl.pallas_call(
        whole,
        out_shape=tuple(outs),
        in_specs=[SMEM] * len(smem) + [place] * len(vmem) + [ANY] * (len(hbm) + len(after)),
        out_specs=(VMEM,) * len(outs),
        scratch_shapes=scratch,
        compiler_params=pltpu.CompilerParams(vmem_limit_bytes=need),
        cost_estimate=pl.CostEstimate(
            flops=int(micros * 1.15e9), bytes_accessed=moved, transcendentals=0
        ),
    )(*args, *after)


class Copies:
    def __init__(self, sems):
        self.sems, self.open = sems, []

    def start(self, source, target):
        copy = pltpu.make_async_copy(source, target, self.sems.at[len(self.open)])
        copy.start()
        self.open.append(copy)

    def wait(self):
        for copy in self.open:
            copy.wait()


def where_am_i():
    return lax.axis_index("core"), lax.axis_index("xy"), lax.axis_index("mp")


class Place:
    def __init__(self, dp, mp):
        self.dp, self.mp = dp, mp
        self.chips = dp // 2
        self.fast = self.chips == 4
        self.z = lax.axis_index("mp")
        self.core = lax.axis_index("core")
        self.xy = lax.axis_index("xy")
        self.d = 2 * self.xy + self.core
        self.micro = self.z % 2
        self.home = self.z // 2

    def move(self, value, route):
        pairs = []
        for xy in range(self.chips):
            for core in range(2):
                for z in range(self.mp):
                    target = route(xy, core, z)
                    if target is not None:
                        txy, tcore, tz = target
                        pairs.append(
                            ((2 * xy + core) * self.mp + z, (2 * txy + tcore) * self.mp + tz)
                        )
        return lax.ppermute(value, AXES, pairs)

    def swap_core(self, value):
        return self.move(value, lambda xy, core, z: (xy, 1 - core, z))

    def swap_xy(self, value, bit):
        return self.move(value, lambda xy, core, z: (xy ^ bit, core, z))

    def swap_z(self, value, bit):
        return self.move(value, lambda xy, core, z: (xy, core, z ^ bit))

    def column_routes(self):
        def route(step, xy, core, z):
            user, j = z // 2, z % 2
            home = core == user
            near = lambda i: (xy, user, 2 * user + i)
            far = lambda i: (xy, user, 2 * (1 - user) + i)
            if step == 0:
                return near(1 - j) if home else far(1 - j)
            if step == 1:
                return far(j) if home else near(j)
            if step == 2:
                return far(1 - j) if home else near(1 - j)
            return None if home else far(j)

        return [partial(route, step) for step in range(4)]

    def column_out(self, shard):
        return [self.move(shard, route) for route in self.column_routes()]

    def column_back(self, blocks):
        got = []
        for block, route in zip(blocks, self.column_routes()):
            turned = {}
            for xy in range(self.chips):
                for core in range(2):
                    for z in range(self.mp):
                        target = route(xy, core, z)
                        if target is not None:
                            turned[target] = (xy, core, z)
            got.append(self.move(block, lambda xy, core, z: turned.get((xy, core, z))))
        return got

    def rows_in(self, blocks):
        def route(k, xy, core, z):
            target = (xy, z // 2, 2 * core + (z + k) % 2)
            return None if target == (xy, core, z) else target

        got = [self.move(block, partial(route, k)) for k, block in enumerate(blocks)]
        return jnp.stack([jnp.where(self.core == self.home, blocks[0], got[0]), got[1]])

    def rows_home(self, blocks):
        return self.rows_joined(blocks, self.rows_sent(blocks))

    def rows_sent(self, blocks):
        def route(k, xy, core, z):
            target = (xy, z // 2, 2 * core + (z % 2 - k) % 2)
            return None if target == (xy, core, z) else target

        return [self.move(block, partial(route, k)) for k, block in enumerate(blocks)]

    def rows_joined(self, blocks, got):
        got = [jnp.where(self.core == self.home, blocks[0], got[0]), got[1]]
        even = self.z % 2 == 0
        both = jnp.stack([jnp.where(even, got[0], got[1]), jnp.where(even, got[1], got[0])])
        return both[:, None].transpose(0, 1, 3, 2)


def norm(hidden):
    center = jnp.mean(hidden, axis=-1, keepdims=True)
    spread = jnp.mean(hidden * hidden, axis=-1, keepdims=True) - center * center
    inverse = lax.rsqrt(spread + 1e-05)
    return (hidden - center) * inverse, inverse


def norm_back(grad, unit, inverse, gain):
    scaled = grad * gain
    first = jnp.mean(scaled, axis=-1, keepdims=True)
    second = jnp.mean(scaled * unit, axis=-1, keepdims=True)
    terms = jnp.concatenate(
        [jnp.sum(grad * unit, axis=0, keepdims=True), jnp.sum(grad, axis=0, keepdims=True)], axis=0
    )
    return inverse * (scaled - first - unit * second), terms


def add_up(*terms):
    total = terms[0].astype(F32)
    for term in terms[1:]:
        total = total + term.astype(F32)
    return total


def input_blocks(hidden, terms, numbers, after=()):
    _, width, length = hidden.shape
    total = width + 32

    def body(numbers_ref, hidden_ref, terms_ref, *outs):
        _, _, z = where_am_i()
        lanes = lax.broadcasted_iota(jnp.int32, (8, length), 1)
        for k in range(2):
            micro = (z + k) % 2
            outs[k][0:width] = hidden_ref[micro]
            tok, aud = numbers_ref[0, micro], numbers_ref[1, micro]
            row = jnp.where(lanes == 0, tok // 256, jnp.where(lanes == 1, tok % 256, 0))
            row = jnp.where(lanes == 2, aud // 256, jnp.where(lanes == 3, aud % 256, row))
            row = jnp.where(lanes == 4, numbers_ref[2, micro], row)
            wide = jnp.concatenate(
                [terms_ref[...].astype(F32), jnp.zeros((24, length - width), F32)], axis=1
            )
            outs[k][width:total] = jnp.concatenate([wide, row.astype(F32)], axis=0).astype(BF)

    return run(
        body,
        [shaped((total, length))] * 2,
        smem=[numbers],
        vmem=[hidden, terms],
        micros=1,
        after=after,
    )


def turned_blocks(value, after=()):
    _, width, length = value.shape

    def body(ref, first_ref, second_ref):
        _, _, z = where_am_i()
        first_ref[...] = ref[z % 2]
        second_ref[...] = ref[(z + 1) % 2]

    return run(body, [shaped((width, length))] * 2, vmem=[value], micros=1, after=after)


def bring_blocks(copies, own_ref, other_ref, wide):
    core, _, z = where_am_i()
    found = []
    for k in range(2):
        slot = (z % 2 + k) % 2
        for ref, user in ((own_ref, core), (other_ref, 1 - core)):
            block = 2 * user + slot
            here = pl.ds(pl.multiple_of(block * QUARTER, QUARTER), QUARTER)
            copies.start(ref.at[k, pl.ds(0, QUARTER)], wide.at[here])
            found.append((ref.at[k], block))
    return found


def prepare_cotangent(own, other, after=()):
    length = own.shape[2]

    def body(own_ref, other_ref, cot_ref, wide, sems):
        copies = Copies(sems)
        bring_blocks(copies, own_ref, other_ref, wide)
        copies.wait()
        cot_ref[...] = wide[...].T

    return run(
        body,
        [shaped((length, D))],
        hbm=[own, other],
        scratch=[pltpu.VMEM((D, length), BF)],
        copies=4,
        micros=3,
        after=after,
    )[0]


def prepare(own, other, corpus_weights):
    length = own.shape[2]

    def body(
        weights_ref, own_ref, other_ref, hidden_ref, norms_ref, nums_ref, wide, extra, sems
    ):
        copies = Copies(sems)
        for ref, block in bring_blocks(copies, own_ref, other_ref, wide):
            copies.start(ref.at[pl.ds(QUARTER, 32)], extra.at[block])
        copies.wait()
        hidden_ref[...] = wide[...].T
        parts = [extra[b].astype(F32) for b in range(4)]
        norms_ref[...] = jnp.concatenate(
            [(e[0:8] + e[8:16] + e[16:24])[:, :QUARTER] for e in parts], axis=1
        )
        row = parts[0][24:25]
        tok = 256.0 * row[:, 0:1] + row[:, 1:2]
        aud = 256.0 * row[:, 2:3] + row[:, 3:4]
        weights = weights_ref[...]
        places = lax.broadcasted_iota(jnp.int32, weights.shape, 1).astype(F32)
        weight = jnp.sum(jnp.where(places == row[:, 4:5], weights, 0.0), axis=1, keepdims=True)
        index = lax.broadcasted_iota(jnp.int32, (8, 128), 0)
        nums_ref[...] = jnp.where(index == 0, tok, jnp.where(index == 1, aud, weight))

    return run(
        body,
        [shaped((length, D)), shaped((8, D), F32), shaped((8, 128), F32)],
        vmem=[corpus_weights.reshape(1, -1)],
        hbm=[own, other],
        scratch=[pltpu.VMEM((D, length), BF), pltpu.VMEM((4, 32, length), BF)],
        copies=8,
        micros=3,
    )


def quarters(value):
    return jnp.concatenate([value[:, p * QUARTER : (p + 1) * QUARTER] for p in range(4)], axis=0)


def attention_shard(self_qkv, self_out, cross_kv, cross_q, cross_out):
    rows = cross_q.shape[0]

    def body(qkv_ref, out_ref, kv_ref, q_ref, cout_ref, shard_ref):
        out = quarters(out_ref[...].astype(F32)).astype(BF)
        cout = quarters(cout_ref[...].astype(F32)).astype(BF)
        shard_ref[...] = jnp.concatenate(
            [qkv_ref[j] for j in range(3)] + [out, kv_ref[...], q_ref[...], cout], axis=1
        )

    return run(
        body,
        [shaped((rows, 2 * D))],
        vmem=[self_qkv.transpose(1, 0, 2), self_out, cross_kv.reshape(rows, -1), cross_q, cross_out],
        micros=2,
        staged=True,
    )[0]


def column_slots():
    core, _, z = where_am_i()
    j = z % 2
    home = 1 - jnp.abs(z // 2 - core)
    same = core + (1 - 2 * core) * (1 - home)
    return home == 1, (2 * (1 - j) + same, 2 * j + 1 - same, 2 * (1 - j) + 1 - same, 2 * j + same)


def bring_column(part_refs, own_ref, shards, sems):
    home, slots = column_slots()
    copies = Copies(sems)
    for k in range(3):
        copies.start(part_refs[k], shards.at[slots[k]])

    @pl.when(home)
    def _():
        copy = pltpu.make_async_copy(own_ref, shards.at[slots[3]], sems.at[3])
        copy.start()
        copy.wait()

    @pl.when(jnp.logical_not(home))
    def _():
        copy = pltpu.make_async_copy(part_refs[3], shards.at[slots[3]], sems.at[3])
        copy.start()
        copy.wait()

    copies.wait()


def pack_attention(parts, own, after):
    rows = own.shape[0]
    few = rows // 4

    def body(*refs):
        part_refs, own_ref, (out_ref, shards, sems) = refs[:4], refs[4], refs[5:]
        bring_column(part_refs, own_ref, shards, sems)
        for which in range(2):
            for cs in range(2):
                low, high = shards[cs], shards[2 + cs]

                def both(at):
                    at = at + which * D
                    return [low[:, at : at + QUARTER], high[:, at : at + QUARTER]]

                here = pl.ds(cs * rows, rows)
                out_ref[0, which, here, :] = jnp.concatenate(both(0) + both(QUARTER), axis=1)
                out_ref[1, which, here, 0:HALF] = jnp.concatenate(both(HALF), axis=1)
            at = 3 * QUARTER + which * D
            outs = [shards[i, :, at : at + QUARTER].astype(F32) for i in range(4)]
            stack = []
            for q in range(2):
                for i in range(4):
                    left = outs[i][2 * q * few : (2 * q + 1) * few]
                    right = outs[i][(2 * q + 1) * few : (2 * q + 2) * few]
                    stack.append(jnp.concatenate([left, right], axis=1))
            out_ref[1, which, :, HALF:D] = jnp.concatenate(stack, axis=0).astype(BF)

    return run(
        body,
        [shaped((2, 2, 2 * rows, D))],
        hbm=list(parts) + [own],
        scratch=[pltpu.VMEM((4, rows, 2 * D), BF)],
        copies=4,
        micros=2,
        after=after,
    )[0]


def unit_shard(place, fc_in, fc_out):
    rows = fc_in.shape[0]
    both = fc_in.reshape(rows, place.chips, 2, rows).transpose(2, 0, 1, 3).reshape(2, rows, HALF)
    kept = lax.dynamic_index_in_dim(both, place.core, 0, keepdims=False)
    sent = lax.dynamic_index_in_dim(both, 1 - place.core, 0, keepdims=False)
    came = place.swap_core(sent)
    first = place.core == 0
    left = jnp.concatenate([jnp.where(first, kept, came), jnp.where(first, came, kept)])
    right = jnp.concatenate([fc_out[:, :HALF], fc_out[:, HALF:]])
    return jnp.concatenate([left, right], axis=1)


def stack_units(blocks, after):
    rows = blocks[0].shape[0]

    def body(*refs):
        for k in range(4):
            refs[4][k // 2, k % 2] = refs[k][...]

    return run(body, [shaped((2, 2, rows, D))], vmem=blocks, micros=1.5, after=after)[0]


def gather_units(place, shard):
    whole = lax.all_gather(shard, CHIPS, axis=0)
    rows = shard.shape[0] // 2
    whole = whole.reshape(place.chips, place.mp, 2 * rows, D)
    up = whole[..., :HALF].transpose(0, 2, 1, 3).reshape(D, 2 * D)
    down = whole[..., HALF:].reshape(place.chips, place.mp, 2, rows, HALF)
    return [up, down.transpose(1, 0, 3, 2, 4).reshape(2 * D, D)]


def scatter_units(place, grads):
    total = lax.psum_scatter(grads, CHIPS, scatter_dimension=0, tiled=False)
    rows = total.shape[0] // 2
    kept = lax.dynamic_slice_in_dim(total, place.core * rows, rows, 0)
    sent = lax.dynamic_slice_in_dim(total[:, :HALF], (1 - place.core) * rows, rows, 0)
    came = place.swap_core(sent)
    kept = kept[:, :HALF]
    first = place.core == 0
    both = jnp.stack([jnp.where(first, kept, came), jnp.where(first, came, kept)])
    both = both.reshape(2, rows, place.chips, rows).transpose(1, 2, 0, 3).reshape(rows, D)
    down = jnp.concatenate([total[:rows, HALF:], total[rows:, HALF:]], axis=1)
    return both.astype(F32), down.astype(F32)


def spread(place, own):
    from_x = place.swap_xy(own, 1)
    from_y = place.swap_xy(own, 2)
    far_one = place.swap_xy(from_y[1], 1)
    far_zero = place.swap_xy(from_x[0], 2)
    return [own, from_x, from_y, far_zero, far_one]


def piece_views(refs, message, which, xy):
    own, from_x, from_y, far_zero, far_one = refs
    return [
        (own.at[which, message], xy),
        (from_x.at[which, message], xy ^ 1),
        (from_y.at[which, message], xy ^ 2),
        ((far_zero, far_one)[which].at[message], xy ^ 3),
    ]


def load_wide(copies, refs, message, which, xy, target, columns=None):
    if len(refs) != 5:
        copies.start(refs[which], target)
        return
    for view, chip in piece_views(refs, message, which, xy):
        rows = view.shape[0]
        if columns is not None:
            view = view.at[:, pl.ds(0, columns)]
        copies.start(view, target.at[pl.ds(pl.multiple_of(chip * rows, 16), rows)])


def load_out(copies, refs, message, xy, target):
    if len(refs) != 5:
        copies.start(refs[2], target)
        return
    for view, chip in piece_views(refs, message, 1, xy):
        rows = view.shape[0] // 4
        for q in range(2):
            for hi in range(2):
                copies.start(
                    view.at[pl.ds((2 * q + hi) * rows, rows), pl.ds(HALF, HALF)],
                    target.at[q, pl.ds(pl.multiple_of(hi * QUARTER + chip * rows, 16), rows)],
                )


def unit_views(refs):
    _, xy, z = where_am_i()
    views = []
    for part in range(2):
        for view, chip in [
            (refs[0].at[part], xy),
            (refs[1].at[part], xy ^ 1),
            (refs[2].at[part], xy ^ 2),
            (refs[3 + part], xy ^ 3),
        ]:
            for i in range(2):
                views.append((view.at[i], chip, z ^ (2 * part + i)))
    return views


def load_up(copies, refs, w_up):
    if len(refs) == 2:
        copies.start(refs[0], w_up)
        return
    for view, chip, z in unit_views(refs):
        rows = view.shape[0]
        copies.start(
            view.at[:, pl.ds(0, HALF)],
            w_up.at[
                pl.ds(pl.multiple_of(rows * chip, 16), rows), pl.ds(pl.multiple_of(z * HALF, HALF), HALF)
            ],
        )


def load_down(copies, refs, w_down):
    if len(refs) == 2:
        copies.start(refs[1], w_down)
        return
    for view, chip, z in unit_views(refs):
        rows = view.shape[0] // 2
        for q in range(2):
            copies.start(
                view.at[pl.ds(q * rows, rows), pl.ds(HALF, HALF)],
                w_down.at[
                    pl.ds(pl.multiple_of(z * HALF + chip * rows, 16), rows), pl.ds(q * HALF, HALF)
                ],
            )


ATTENTION_COPIES = 4 + 4 + 16
UP_COPIES = 16
DOWN_COPIES = 32


def gather_plain(place, shard):
    whole = lax.all_gather(shard, ("mp", "xy", "core"), axis=0)
    whole = whole.reshape((2, 2, place.dp) + shard.shape)
    return lax.dynamic_index_in_dim(whole, place.core, 0, keepdims=False)


def attention_plain(place, shard):
    mine = gather_plain(place, shard)
    rows = shard.shape[0]

    def columns(at, count):
        value = mine[..., at : at + count * QUARTER].reshape(2, D, count, QUARTER)
        return value.transpose(1, 2, 0, 3).reshape(D, count * HALF)

    out = mine[..., 3 * QUARTER :].reshape(2, place.dp, 2, 2, rows // 4, QUARTER)
    out = out.transpose(2, 0, 1, 4, 3, 5).reshape(2, HALF, HALF)
    return [columns(0, 2), columns(HALF, 1), out]


def head_rows(h):
    return pl.ds(pl.multiple_of(h * HEAD_DIM, HEAD_DIM), HEAD_DIM)


def low_parts(value):
    parts = []
    for _ in range(3):
        part = value.astype(BF)
        parts.append(part)
        value = value - part.astype(F32)
    return parts


def widened(count):
    return lambda rows: (
        lax.broadcasted_iota(jnp.int32, (rows, HEAD_DIM), 1) < count
    ).astype(F32).astype(BF)


def below(head, rows):
    blank = jnp.zeros((HEAD_DIM - len(rows), head.shape[1]), F32)
    rest = jnp.concatenate([row.astype(F32) for row in rows] + [blank], axis=0)
    return jnp.concatenate([head, rest.astype(BF)], axis=0)


def project(left, pair_ref):
    return jnp.concatenate([mm(left, pair_ref[0]), mm(left, pair_ref[1])], axis=1)


def project_t(left, pair_ref):
    return mm_t(left[:, :HALF], pair_ref[0]) + mm_t(left[:, HALF:], pair_ref[1])


def self_forward(hidden, norms, nums, weights, after=()):
    length = hidden.shape[0]

    def body(hidden_ref, norms_ref, nums_ref, *refs):
        w_refs, refs = refs[: len(weights)], refs[len(weights) :]
        part_ref, at_ref, qkv_ref, qt_ref, kt_ref, ot_ref, lse_ref = refs[:7]
        w_qk, w_v, w_out, vt, heads, bias, sems = refs[7:]
        _, xy, _ = where_am_i()
        copies = Copies(sems)
        load_wide(copies, w_refs, 0, 0, xy, w_qk)
        load_wide(copies, w_refs, 0, 1, xy, w_v, HALF)
        load_out(copies, w_refs, 0, xy, w_out)
        unit, _ = norm(hidden_ref[...].astype(F32))
        a = (unit * norms_ref[0:1] + norms_ref[4:5]).astype(BF)
        at_ref[...] = a.T
        keys = lax.broadcasted_iota(jnp.int32, (length, length), 0)
        queries = lax.broadcasted_iota(jnp.int32, (length, length), 1)
        allowed = (keys <= queries) & (keys.astype(F32) < nums_ref[0:1, 0:1])
        bias[...] = jnp.where(allowed, 0.0, -1e30)
        copies.wait()
        qk = mm(a, w_qk[...])
        q = (qk[:, :HALF].astype(BF).astype(F32) * HEAD_DIM ** (-0.5)).astype(BF)
        k = qk[:, HALF:].astype(BF)
        v = mm(a, w_v[...]).astype(BF)
        qkv_ref[:, 0:HALF] = q
        qkv_ref[:, HALF : 2 * HALF] = k
        qkv_ref[:, 2 * HALF :] = v
        qt_ref[...] = q.T
        kt_ref[...] = k.T
        vt[...] = v.T
        for h in range(HEADS):
            heads[h] = k[:, h * HEAD_DIM : (h + 1) * HEAD_DIM]

        def head(h, carry):
            s = mm(heads[h], qt_ref[head_rows(h), :]) + bias[...]
            top = jnp.max(s, axis=0, keepdims=True)
            p = jnp.exp(s - top)
            total = jnp.sum(p, axis=0, keepdims=True)
            o = mm(vt[head_rows(h), :], p.astype(BF))
            ot_ref[head_rows(h), :] = (o / total).astype(BF)
            lse_ref[h] = top + jnp.log(total)
            return carry

        lax.fori_loop(0, HEADS, head, 0)
        part_ref[...] = project(ot_ref[...].T, w_out).astype(BF)

    return run(
        body,
        [
            shaped((length, D)),
            shaped((D, length)),
            shaped((length, 3 * HALF)),
            shaped((HALF, length)),
            shaped((HALF, length)),
            shaped((HALF, length)),
            shaped((HEADS, 1, length), F32),
        ],
        vmem=[hidden, norms, nums],
        hbm=weights,
        scratch=[
            pltpu.VMEM((D, D), BF),
            pltpu.VMEM((D, HALF), BF),
            pltpu.VMEM((2, HALF, HALF), BF),
            pltpu.VMEM((HALF, length), BF),
            pltpu.VMEM((HEADS, length, HEAD_DIM), BF),
            pltpu.VMEM((length, length), F32),
        ],
        copies=ATTENTION_COPIES,
        micros=10,
        after=after,
    )


def turn(value, after=()):
    rows, columns = value.shape

    def body(ref, out_ref):
        for at in range(0, rows, CHUNK):
            out_ref[:, at : at + CHUNK] = ref[at : at + CHUNK, :].T

    return run(body, [shaped((columns, rows))], vmem=[value], micros=4, after=after)[0]


def cross_memory(encoded, weights):
    frames = encoded.shape[0]

    def body(enc_ref, *refs):
        w_refs, refs = refs[: len(weights)], refs[len(weights) :]
        kv_ref, kvt_ref, w_kv, sems = refs
        _, xy, _ = where_am_i()
        copies = Copies(sems)
        load_wide(copies, w_refs, 1, 0, xy, w_kv)
        copies.wait()

        def step(i, carry):
            here = pl.ds(pl.multiple_of(i * CHUNK, CHUNK), CHUNK)
            kv = mm(enc_ref[here, :], w_kv[...]).astype(BF)
            kv_ref[here, :] = kv
            kvt_ref[:, here] = kv.T
            return carry

        lax.fori_loop(0, frames // CHUNK, step, 0)

    return run(
        body,
        [shaped((frames, D)), shaped((D, frames))],
        vmem=[encoded],
        hbm=weights,
        scratch=[pltpu.VMEM((D, D), BF)],
        copies=4,
        micros=2,
    )


def residual(hidden_ref, mine_ref, other_ref):
    return hidden_ref[...].astype(F32) + (mine_ref[...].astype(F32) + other_ref[...].astype(F32))


def cross_forward(hidden, mine, other, norms, nums, kv, kvt, weights):
    length = hidden.shape[0]
    frames = kv.shape[0]

    def body(hidden_ref, mine_ref, other_ref, norms_ref, nums_ref, kv_ref, kvt_ref, *refs):
        w_refs, refs = refs[: len(weights)], refs[len(weights) :]
        part_ref, h_ref, ct_ref, q_ref, qt_ref, ot_ref, lse_ref = refs[:7]
        w_q, w_out, heads, values_t, scores, sems = refs[7:]
        _, xy, _ = where_am_i()
        copies = Copies(sems)
        load_wide(copies, w_refs, 1, 1, xy, w_q, HALF)
        load_out(copies, w_refs, 1, xy, w_out)
        h1 = residual(hidden_ref, mine_ref, other_ref)
        h_ref[...] = h1
        unit, _ = norm(h1)
        c = (unit * norms_ref[1:2] + norms_ref[5:6]).astype(BF)
        ct_ref[...] = c.T
        frame = lax.broadcasted_iota(jnp.int32, (frames, HEAD_DIM), 0).astype(F32)
        lane = lax.broadcasted_iota(jnp.int32, (frames, HEAD_DIM), 1)
        mask = jnp.where(frame < nums_ref[1:2, 0:1], 0.0, -1e30)
        beside = jnp.where(lane == 0, mask, 0.0).astype(BF)
        one = lax.broadcasted_iota(jnp.int32, (16, frames), 0)
        one = jnp.where(one == 0, 1.0, 0.0).astype(BF)
        for h in range(HEADS):
            keys = kv_ref[:, h * HEAD_DIM : (h + 1) * HEAD_DIM]
            heads[h] = jnp.concatenate([keys, beside], axis=1)
            values = kvt_ref[HALF + h * HEAD_DIM : HALF + (h + 1) * HEAD_DIM, :]
            values_t[h] = jnp.concatenate([values, one], axis=0)
        copies.wait()
        q = mm(c, w_q[...]).astype(BF)
        q = (q.astype(F32) * HEAD_DIM ** (-0.5)).astype(BF)
        q_ref[...] = q
        qt_ref[...] = q.T
        ones = jnp.ones((1, length), F32)

        def head(h, carry):
            qt = below(qt_ref[head_rows(h), :], [ones])
            top = None
            for at in range(0, frames, CHUNK):
                s = mm(heads[h, at : at + CHUNK], qt)
                scores[at : at + CHUNK] = s
                high = jnp.max(s, axis=0, keepdims=True)
                top = high if top is None else jnp.maximum(top, high)
            o = None
            for at in range(0, frames, CHUNK):
                p = jnp.exp(scores[at : at + CHUNK] - top).astype(BF)
                more = mm(values_t[h, :, at : at + CHUNK], p)
                o = more if o is None else o + more
            total = o[HEAD_DIM : HEAD_DIM + 1]
            ot_ref[head_rows(h), :] = (o[:HEAD_DIM] / total).astype(BF)
            lse_ref[h] = top + jnp.log(total)
            return carry

        lax.fori_loop(0, HEADS, head, 0)
        part_ref[...] = project(ot_ref[...].T, w_out).astype(BF)

    return run(
        body,
        [
            shaped((length, D)),
            shaped((length, D), F32),
            shaped((D, length)),
            shaped((length, HALF)),
            shaped((HALF, length)),
            shaped((HALF, length)),
            shaped((HEADS, 1, length), F32),
        ],
        vmem=[hidden, mine, other, norms, nums, kv, kvt],
        hbm=weights,
        scratch=[
            pltpu.VMEM((D, HALF), BF),
            pltpu.VMEM((2, HALF, HALF), BF),
            pltpu.VMEM((HEADS, frames, 2 * HEAD_DIM), BF),
            pltpu.VMEM((HEADS, HEAD_DIM + 16, frames), BF),
            pltpu.VMEM((frames, length), F32),
        ],
        copies=4 + 16,
        micros=4,
    )


def units_forward(hidden, mine, other, norms, weights):
    length = hidden.shape[0]

    def body(hidden_ref, mine_ref, other_ref, norms_ref, *refs):
        w_refs, refs = refs[: len(weights)], refs[len(weights) :]
        part_ref, h_ref, mt_ref, slope_ref, it_ref = refs[:5]
        w_up, w_down, inner, late_sems, sems = refs[5:]
        _, xy, _ = where_am_i()
        copies = Copies(sems)
        load_up(copies, w_refs, w_up)
        late = Copies(late_sems)
        load_down(late, w_refs, w_down)
        h2 = residual(hidden_ref, mine_ref, other_ref)
        h_ref[...] = h2
        unit, _ = norm(h2)
        m = (unit * norms_ref[2:3] + norms_ref[6:7]).astype(BF)
        mt_ref[...] = m.T
        copies.wait()
        for at in range(0, 2 * D, CHUNK):
            here = slice(at, at + CHUNK)
            z = mm(m, w_up[:, here])
            share = 0.5 * (1.0 + lax.erf(z * 0.7071067811865476))
            slope = share + z * (0.3989422804014327 * jnp.exp(-0.5 * z * z))
            value = (z * share).astype(BF)
            inner[:, here] = value
            it_ref[here, :] = value.T
            slope_ref[:, here] = slope.astype(BF)
        late.wait()
        for at in range(0, D, CHUNK):
            part_ref[:, at : at + CHUNK] = mm(inner[...], w_down[:, at : at + CHUNK]).astype(BF)

    return run(
        body,
        [
            shaped((length, D)),
            shaped((length, D), F32),
            shaped((D, length)),
            shaped((length, 2 * D)),
            shaped((2 * D, length)),
        ],
        vmem=[hidden, mine, other, norms],
        hbm=weights,
        scratch=[
            pltpu.VMEM((D, 2 * D), BF),
            pltpu.VMEM((2 * D, D), BF),
            pltpu.VMEM((length, 2 * D), BF),
            pltpu.SemaphoreType.DMA((DOWN_COPIES,)),
        ],
        copies=UP_COPIES,
        micros=9,
    )


def store_blocks(value, blocks, first_ref, second_ref):
    core, _, z = where_am_i()
    for b in range(4):
        blocks[b] = value[:, b * QUARTER : (b + 1) * QUARTER]
    first_ref[...] = blocks[2 * core + z % 2].T
    second_ref[...] = blocks[2 * core + (z + 1) % 2].T


def units_backward(hidden, mine, other, norms, nums, cot, slope, weights):
    length = hidden.shape[0]

    def body(hidden_ref, mine_ref, other_ref, norms_ref, nums_ref, cot_ref, slope_ref, *refs):
        w_refs, refs = refs[: len(weights)], refs[len(weights) :]
        part_ref, d_ref, e_ref, dz_ref, terms_ref, first_ref, second_ref = refs[:7]
        w_up, w_down, blocks, late_sems, sems = refs[7:]
        _, xy, _ = where_am_i()
        copies = Copies(sems)
        load_down(copies, w_refs, w_down)
        late = Copies(late_sems)
        load_up(late, w_refs, w_up)
        unit, inverse = norm(residual(hidden_ref, mine_ref, other_ref))
        final = (unit * norms_ref[3:4] + norms_ref[7:8]).astype(BF)
        store_blocks(final, blocks, first_ref, second_ref)
        live = lax.broadcasted_iota(jnp.int32, (length, 1), 0).astype(F32) < nums_ref[0:1, 0:1]
        grad = cot_ref[...].astype(F32) * jnp.where(live, nums_ref[2:3, 0:1], 0.0)
        d3, terms = norm_back(grad, unit, inverse, norms_ref[3:4])
        d_ref[...] = d3
        terms_ref[...] = terms
        e = d3.astype(BF)
        e_ref[...] = e
        copies.wait()
        for at in range(0, 2 * D, CHUNK):
            here = slice(at, at + CHUNK)
            d_inner = mm_t(e, w_down[here, :])
            dz_ref[:, here] = (slope_ref[:, here].astype(F32) * d_inner).astype(BF)
        late.wait()
        for at in range(0, D, CHUNK):
            out = mm_t(dz_ref[...], w_up[at : at + CHUNK, :])
            part_ref[:, at : at + CHUNK] = out.astype(BF)

    return run(
        body,
        [
            shaped((length, D)),
            shaped((length, D), F32),
            shaped((length, D)),
            shaped((length, 2 * D)),
            shaped((2, D), F32),
            shaped((QUARTER, length)),
            shaped((QUARTER, length)),
        ],
        vmem=[hidden, mine, other, norms, nums, cot, slope],
        hbm=weights,
        scratch=[
            pltpu.VMEM((D, 2 * D), BF),
            pltpu.VMEM((2 * D, D), BF),
            pltpu.VMEM((4, length, QUARTER), BF),
            pltpu.SemaphoreType.DMA((UP_COPIES,)),
        ],
        copies=DOWN_COPIES,
        micros=10,
    )


def step_back(d_ref, hidden_ref, mine_ref, other_ref, gain):
    unit, inverse = norm(hidden_ref[...].astype(F32))
    grad = mine_ref[...].astype(F32) + other_ref[...].astype(F32)
    part, terms = norm_back(grad, unit, inverse, gain)
    return d_ref[...] + part, terms


def cross_backward(
    d, hidden, mine, other, norms, nums, kv, kvt, q, qt, ot, lse, weights, after=()
):
    length = hidden.shape[0]
    frames = kv.shape[0]

    def body(
        d_ref, hidden_ref, mine_ref, other_ref, norms_ref, nums_ref, kv_ref, kvt_ref, q_ref,
        qt_ref, ot_ref, lse_ref, *refs
    ):
        w_refs, refs = refs[: len(weights)], refs[len(weights) :]
        part_ref, d_out_ref, e_ref, dq_ref, dkv_ref, terms_ref = refs[:6]
        w_q, w_out, keys, values, queries, grads, dot_t, dk_h, dv_h, dqt, sems = refs[6:]
        _, xy, _ = where_am_i()
        copies = Copies(sems)
        load_wide(copies, w_refs, 1, 1, xy, w_q, HALF)
        load_out(copies, w_refs, 1, xy, w_out)
        d2, terms = step_back(d_ref, hidden_ref, mine_ref, other_ref, norms_ref[2:3])
        d_out_ref[...] = d2
        terms_ref[...] = terms
        e = d2.astype(BF)
        e_ref[...] = e
        frame = lax.broadcasted_iota(jnp.int32, (frames, HEAD_DIM), 0).astype(F32)
        lane = lax.broadcasted_iota(jnp.int32, (frames, HEAD_DIM), 1)
        mask = jnp.where(frame < nums_ref[1:2, 0:1], 0.0, -1e30)
        beside = jnp.where(lane == 0, mask, jnp.where(lane < 4, 1.0, 0.0)).astype(BF)
        three = widened(3)(frames)
        for h in range(HEADS):
            lanes = slice(h * HEAD_DIM, (h + 1) * HEAD_DIM)
            keys[h] = jnp.concatenate([kv_ref[:, lanes], beside], axis=1)
            value = kv_ref[:, HALF + h * HEAD_DIM : HALF + (h + 1) * HEAD_DIM]
            values[h] = jnp.concatenate([value, three], axis=1)
            queries[h] = q_ref[:, lanes]
        copies.wait()
        d_mixed = project_t(e, w_out).astype(BF)
        dot_t[...] = d_mixed.T
        for h in range(HEADS):
            grads[h] = d_mixed[:, h * HEAD_DIM : (h + 1) * HEAD_DIM]
        ones = jnp.ones((1, length), F32)

        def head(h, carry):
            rows = head_rows(h)
            do_t = dot_t[rows, :]
            q_n, do_n = queries[h], grads[h]
            delta = jnp.sum(do_t.astype(F32) * ot_ref[rows, :].astype(F32), axis=0, keepdims=True)
            q_t = below(qt_ref[rows, :], [ones] + low_parts(-lse_ref[h]))
            do_t = below(do_t, low_parts(-delta))
            total = None
            for at in range(0, frames, CHUNK):
                here = slice(at, at + CHUNK)
                p = jnp.exp(mm(keys[h, here], q_t))
                ds = (p * mm(values[h, here], do_t)).astype(BF)
                dv_h[h, here] = mm(p.astype(BF), do_n).astype(BF)
                dk_h[h, here] = mm(ds, q_n).astype(BF)
                more = mm(kvt_ref[rows, here], ds)
                total = more if total is None else total + more
            dqt[rows, :] = (total * HEAD_DIM ** (-0.5)).astype(BF)
            return carry

        lax.fori_loop(0, HEADS, head, 0)
        dq = dqt[...].T
        dq_ref[...] = dq
        part_ref[...] = mm_t(dq, w_q[...]).astype(BF)
        for h in range(HEADS):
            lanes = slice(h * HEAD_DIM, (h + 1) * HEAD_DIM)
            dkv_ref[:, lanes] = dk_h[h]
            dkv_ref[:, HALF + h * HEAD_DIM : HALF + (h + 1) * HEAD_DIM] = dv_h[h]

    return run(
        body,
        [
            shaped((length, D)),
            shaped((length, D), F32),
            shaped((length, D)),
            shaped((length, HALF)),
            shaped((frames, D)),
            shaped((2, D), F32),
        ],
        vmem=[d, hidden, mine, other, norms, nums, kv, kvt, q, qt, ot, lse],
        hbm=weights,
        scratch=[
            pltpu.VMEM((D, HALF), BF),
            pltpu.VMEM((2, HALF, HALF), BF),
            pltpu.VMEM((HEADS, frames, 2 * HEAD_DIM), BF),
            pltpu.VMEM((HEADS, frames, 2 * HEAD_DIM), BF),
            pltpu.VMEM((HEADS, length, HEAD_DIM), BF),
            pltpu.VMEM((HEADS, length, HEAD_DIM), BF),
            pltpu.VMEM((HALF, length), BF),
            pltpu.VMEM((HEADS, frames, HEAD_DIM), BF),
            pltpu.VMEM((HEADS, frames, HEAD_DIM), BF),
            pltpu.VMEM((HALF, length), BF),
        ],
        copies=4 + 16,
        micros=22,
        after=after,
    )


def self_backward(d, hidden, mine, other, norms, nums, qkv, qt, kt, ot, lse, weights, after=()):
    length = hidden.shape[0]

    def body(
        d_ref, hidden_ref, mine_ref, other_ref, norms_ref, nums_ref, qkv_ref, qt_ref, kt_ref,
        ot_ref, lse_ref, *refs
    ):
        w_refs, refs = refs[: len(weights)], refs[len(weights) :]
        part_ref, d_out_ref, e_ref, dqk_ref, dv_ref, terms_ref = refs[:6]
        w_qk, w_v, w_out, queries_h, keys, values, grads, dot_t, dk_h, dv_h, dqt, bias, sems = refs[6:]
        _, xy, _ = where_am_i()
        copies = Copies(sems)
        load_out(copies, w_refs, 0, xy, w_out)
        load_wide(copies, w_refs, 0, 0, xy, w_qk)
        load_wide(copies, w_refs, 0, 1, xy, w_v, HALF)
        d1, terms = step_back(d_ref, hidden_ref, mine_ref, other_ref, norms_ref[1:2])
        d_out_ref[...] = d1
        terms_ref[...] = terms
        e = d1.astype(BF)
        e_ref[...] = e
        places = lax.broadcasted_iota(jnp.int32, (length, length), 0)
        queries = lax.broadcasted_iota(jnp.int32, (length, length), 1)
        allowed = (places <= queries) & (places.astype(F32) < nums_ref[0:1, 0:1])
        bias[...] = jnp.where(allowed, 0.0, -1e30)
        three = widened(3)(length)
        for h in range(HEADS):
            at = h * HEAD_DIM
            queries_h[h] = qkv_ref[:, at : at + HEAD_DIM]
            key = qkv_ref[:, HALF + at : HALF + at + HEAD_DIM]
            keys[h] = jnp.concatenate([key, three], axis=1)
            value = qkv_ref[:, 2 * HALF + at : 2 * HALF + at + HEAD_DIM]
            values[h] = jnp.concatenate([value, three], axis=1)
        copies.wait()
        d_mixed = project_t(e, w_out).astype(BF)
        dot_t[...] = d_mixed.T
        for h in range(HEADS):
            grads[h] = d_mixed[:, h * HEAD_DIM : (h + 1) * HEAD_DIM]

        def head(h, carry):
            rows = head_rows(h)
            do_t, do_n = dot_t[rows, :], grads[h]
            delta = jnp.sum(do_t.astype(F32) * ot_ref[rows, :].astype(F32), axis=0, keepdims=True)
            q_t = below(qt_ref[rows, :], low_parts(-lse_ref[h]))
            do_t = below(do_t, low_parts(-delta))
            p = jnp.exp(mm(keys[h], q_t) + bias[...])
            ds = (p * mm(values[h], do_t)).astype(BF)
            dv_h[h] = mm(p.astype(BF), do_n).astype(BF)
            dk_h[h] = mm(ds, queries_h[h]).astype(BF)
            dqt[rows, :] = (mm(kt_ref[rows, :], ds) * HEAD_DIM ** (-0.5)).astype(BF)
            return carry

        lax.fori_loop(0, HEADS, head, 0)
        dqk_ref[:, 0:HALF] = dqt[...].T
        for h in range(HEADS):
            lanes = slice(HALF + h * HEAD_DIM, HALF + (h + 1) * HEAD_DIM)
            dqk_ref[:, lanes] = dk_h[h]
            dv_ref[:, h * HEAD_DIM : (h + 1) * HEAD_DIM] = dv_h[h]
        out = mm_t(dqk_ref[...], w_qk[...]) + mm_t(dv_ref[...], w_v[...])
        part_ref[...] = out.astype(BF)

    return run(
        body,
        [
            shaped((length, D)),
            shaped((length, D), F32),
            shaped((length, D)),
            shaped((length, D)),
            shaped((length, HALF)),
            shaped((2, D), F32),
        ],
        vmem=[d, hidden, mine, other, norms, nums, qkv, qt, kt, ot, lse],
        hbm=weights,
        scratch=[
            pltpu.VMEM((D, D), BF),
            pltpu.VMEM((D, HALF), BF),
            pltpu.VMEM((2, HALF, HALF), BF),
            pltpu.VMEM((HEADS, length, HEAD_DIM), BF),
            pltpu.VMEM((HEADS, length, 2 * HEAD_DIM), BF),
            pltpu.VMEM((HEADS, length, 2 * HEAD_DIM), BF),
            pltpu.VMEM((HEADS, length, HEAD_DIM), BF),
            pltpu.VMEM((HALF, length), BF),
            pltpu.VMEM((HEADS, length, HEAD_DIM), BF),
            pltpu.VMEM((HEADS, length, HEAD_DIM), BF),
            pltpu.VMEM((HALF, length), BF),
            pltpu.VMEM((length, length), F32),
        ],
        copies=ATTENTION_COPIES,
        micros=12,
        staged=True,
        after=after,
    )


def finish_hidden(d, hidden, mine, other, norms, terms1, terms2, terms3, after=()):
    length = hidden.shape[0]

    def body(
        d_ref, hidden_ref, mine_ref, other_ref, norms_ref, one, two, three, terms_ref, first_ref,
        second_ref, blocks
    ):
        d0, terms = step_back(d_ref, hidden_ref, mine_ref, other_ref, norms_ref[0:1])
        store_blocks(d0.astype(BF), blocks, first_ref, second_ref)
        for j in range(2):
            here = slice(j, j + 1)
            terms_ref[4 * j : 4 * j + 4] = jnp.concatenate(
                [terms[here], one[here], two[here], three[here]], axis=0
            )

    return run(
        body,
        [shaped((8, D), F32), shaped((QUARTER, length)), shaped((QUARTER, length))],
        vmem=[d, hidden, mine, other, norms, terms1, terms2, terms3],
        scratch=[pltpu.VMEM((4, length, QUARTER), BF)],
        micros=4,
        after=after,
    )


def finish_encoder(keep, other, frames, after=()):
    def body(keep_ref, other_ref, first_ref, second_ref):
        _, _, z = where_am_i()
        for ref, k in ((first_ref, 0), (second_ref, 1)):
            here = pl.ds(pl.multiple_of(((z + k) % 2) * QUARTER, QUARTER), QUARTER)
            total = keep_ref[here, :].astype(F32) + other_ref[here, :].astype(F32)
            ref[...] = total.astype(BF)[:, :frames]

    return run(
        body,
        [shaped((QUARTER, frames)), shaped((QUARTER, frames))],
        vmem=[keep, other],
        micros=2,
        after=after,
    )


def block_plan(place):
    if not place.fast:
        return 1, (((1, 0, 0),), ((1, 0, 0),))
    first = ((1, 0, 0), (0, 0, 1), (1, 1, 2), (0, 1, 3))
    second = ((1, 0, 0), (1, 1, 1), (0, 0, 2), (0, 1, 3))
    return 4, (first, second)


def grad_outputs(place, shape):
    if place.fast:
        return [shaped((2,) + shape)] * 4
    return [shaped((1,) + shape)] * 4


def units_grads(place, mt, dz, it, e):
    chips = place.chips
    rows = D // (2 * chips)
    _, plan = block_plan(place)

    def body(mt_ref, dz_ref, it_ref, e_ref, *outs):
        _, xy, _ = where_am_i()
        for output, slot, offset in plan[1]:
            chip = xy ^ offset
            for z in range(4):
                here = pl.ds(pl.multiple_of(z * HALF + chip * rows, 16), rows)
                outs[2 + output][slot, z] = mm(it_ref[here, :], e_ref[...]).astype(BF)
        for output, slot, offset in plan[0]:
            here = pl.ds(pl.multiple_of((xy ^ offset) * 2 * rows, 16), 2 * rows)
            left = mm(mt_ref[here, :], dz_ref[...]).astype(BF)
            for z in range(4):
                outs[output][slot, z] = left[:, z * HALF : (z + 1) * HALF]

    def plain(mt_ref, dz_ref, it_ref, e_ref, left_ref, right_ref):
        left_ref[...] = mm(mt_ref[...], dz_ref[...]).astype(BF)
        right_ref[...] = mm(it_ref[...], e_ref[...]).astype(BF)

    if place.fast:
        first, second = shaped((2, 4, 2 * rows, HALF)), shaped((2, 4, rows, D))
        return run(
            body, [first, first, second, second], vmem=[mt, dz, it, e], micros=6
        )
    left, right = run(
        plain, [shaped((D, 2 * D)), shaped((2 * D, D))], vmem=[mt, dz, it, e], micros=7
    )
    left = left.reshape(chips, 2 * rows, 4, HALF).transpose(0, 2, 1, 3)
    right = right.reshape(4, chips, rows, 2, HALF).transpose(1, 0, 3, 2, 4)
    whole = jnp.concatenate([left, right.reshape(chips, 4, 2 * rows, HALF)], axis=-1)
    return whole.reshape(4 * chips, 2 * rows, D)


def units_sum(grads, came, onward, after):
    rows = grads[3].shape[2]

    def body(*refs):
        ins, (kept_ref, sent_ref, left, right, blocks, sems) = refs[:6], refs[6:]
        _, _, mp = where_am_i()
        copies = Copies(sems)
        for i, ref in enumerate(ins):
            target = (left if i < 3 else right).at[i % 3]
            copies.start(ref if i % 3 == 2 else ref.at[0], target)
        copies.wait()
        for z in range(4):
            blocks[z, :, 0:HALF] = add_up(*[left[i, z] for i in range(3)]).astype(BF)
            down = add_up(*[right[i, z] for i in range(3)]).astype(BF)
            blocks[z, 0:rows, HALF:D] = down[:, :HALF]
            blocks[z, rows : 2 * rows, HALF:D] = down[:, HALF:]
        for i in range(2):
            kept_ref[i] = blocks[mp ^ (2 * i)]
            sent_ref[i] = blocks[mp ^ (2 * i + 1)]

    return run(
        body,
        [shaped((2, 2 * rows, D)), shaped((2, 2 * rows, D))],
        hbm=[grads[1], came[0], onward[0], grads[3], came[1], onward[1]],
        scratch=[
            pltpu.VMEM((3, 4, 2 * rows, HALF), BF),
            pltpu.VMEM((3, 4, rows, D), BF),
            pltpu.VMEM((4, 2 * rows, D), BF),
        ],
        copies=6,
        micros=3,
        after=after,
    )


def add_second(kept, came, after):
    def body(kept_ref, came_ref, out_ref, held, sems):
        copies = Copies(sems)
        copies.start(kept_ref.at[1], held.at[0])
        copies.start(came_ref.at[1], held.at[1])
        copies.wait()
        out_ref[...] = add_up(held[0], held[1]).astype(BF)

    shape = kept.shape[1:]
    return run(
        body,
        [shaped(shape)],
        hbm=[kept, came],
        scratch=[pltpu.VMEM((2,) + shape, BF)],
        copies=2,
        micros=1,
        after=after,
    )[0]


def cut_units(kept, came, last, after):
    rows = last.shape[0] // 2

    def body(kept_ref, came_ref, last_ref, mine_ref, sent_ref, down_ref, held, sems):
        core, _, _ = where_am_i()
        copies = Copies(sems)
        copies.start(kept_ref.at[0], held.at[0])
        copies.start(came_ref.at[0], held.at[1])
        copies.start(last_ref, held.at[2])
        copies.wait()
        mine = pl.ds(pl.multiple_of(core * rows, 16), rows)
        theirs = pl.ds(pl.multiple_of((1 - core) * rows, 16), rows)
        mine_ref[...] = add_up(*[held[i, mine, 0:HALF] for i in range(3)]).astype(BF)
        sent_ref[...] = add_up(*[held[i, theirs, 0:HALF] for i in range(3)]).astype(BF)
        down_ref[:, 0:HALF] = add_up(*[held[i, 0:rows, HALF:D] for i in range(3)])
        down_ref[:, HALF:D] = add_up(*[held[i, rows : 2 * rows, HALF:D] for i in range(3)])

    return run(
        body,
        [shaped((rows, HALF)), shaped((rows, HALF)), shaped((rows, D), F32)],
        hbm=[kept, came, last],
        scratch=[pltpu.VMEM((3, 2 * rows, D), BF)],
        copies=3,
        micros=1,
        after=after,
    )


def join_units(place, kept, came):
    rows = kept.shape[0]

    def body(kept_ref, came_ref, up_ref, both):
        core, _, _ = where_am_i()
        both[core] = kept_ref[...]
        both[1 - core] = came_ref[...]
        blocks = []
        for chip in range(place.chips):
            for parity in range(2):
                blocks.append(both[parity, :, chip * rows : (chip + 1) * rows].astype(F32))
        up_ref[...] = jnp.concatenate(blocks, axis=1)

    return run(
        body,
        [shaped((rows, D), F32)],
        vmem=[kept, came],
        scratch=[pltpu.VMEM((2, rows, HALF), BF)],
        micros=1,
    )[0]


def attention_grads(place, wide_left, wide_right, left, right, ot, e, after=()):
    count, plan = block_plan(place)
    rows = D // count
    few = rows // 4

    def body(wide_left_ref, wide_right_ref, left_ref, right_ref, ot_ref, e_ref, *outs):
        _, xy, _ = where_am_i()
        for output, slot, offset in plan[0]:
            chip = xy ^ offset if count > 1 else 0
            here = pl.ds(pl.multiple_of(chip * rows, 16), rows)
            outs[output][slot] = mm(wide_left_ref[here, :], wide_right_ref[...]).astype(BF)
        for output, slot, offset in plan[1]:
            chip = xy ^ offset if count > 1 else 0
            here = pl.ds(pl.multiple_of(chip * rows, 16), rows)
            target = outs[2 + output]
            target[slot, :, 0:HALF] = mm(left_ref[here, :], right_ref[...]).astype(BF)
            for hi in range(2):
                here = pl.ds(pl.multiple_of(hi * QUARTER + chip * few, 16), few)
                both = mm(ot_ref[here, :], e_ref[...]).astype(BF)
                for q in range(2):
                    at = (2 * q + hi) * few
                    target[slot, at : at + few, HALF:D] = both[:, q * HALF : (q + 1) * HALF]

    return run(
        body,
        grad_outputs(place, (rows, D)),
        vmem=[wide_left, wide_right, left, right, ot, e],
        micros=6,
        after=after,
    )


def encoder_grad(dkv, weights, after=()):
    padded = dkv.shape[0]

    def body(dkv_ref, *refs):
        w_refs, (keep_ref, send_ref, w_kv, sems) = refs[: len(weights)], refs[len(weights) :]
        core, xy, _ = where_am_i()
        copies = Copies(sems)
        load_wide(copies, w_refs, 1, 0, xy, w_kv)
        copies.wait()
        mine = pl.ds(pl.multiple_of(core * HALF, HALF), HALF)
        theirs = pl.ds(pl.multiple_of((1 - core) * HALF, HALF), HALF)
        for ref, rows in ((send_ref, theirs), (keep_ref, mine)):
            for at in range(0, padded, CHUNK):
                value = mm_t(w_kv[rows, :], dkv_ref[at : at + CHUNK, :])
                ref[:, at : at + CHUNK] = value.astype(BF)

    return run(
        body,
        [shaped((HALF, padded)), shaped((HALF, padded))],
        vmem=[dkv],
        hbm=weights,
        scratch=[pltpu.VMEM((D, D), BF)],
        copies=4,
        micros=3.5,
        after=after,
    )


def leave_plane(place, grads):
    return [place.swap_xy(grads[0], 1), place.swap_xy(grads[2], 2)]


def pass_on(grads, came, after):
    shapes = [grads[1].shape[1:], grads[3].shape[1:]]

    def body(stay0, came0, stay1, came1, out0, out1, held0, held1, sems):
        copies = Copies(sems)
        for i, ref in enumerate((stay0, came0, stay1, came1)):
            copies.start(ref.at[1], (held0 if i < 2 else held1).at[i % 2])
        copies.wait()
        out0[...] = add_up(held0[0], held0[1]).astype(BF)
        out1[...] = add_up(held1[0], held1[1]).astype(BF)

    return run(
        body,
        [shaped(shape) for shape in shapes],
        hbm=[grads[1], came[0], grads[3], came[1]],
        scratch=[pltpu.VMEM((2,) + shape, BF) for shape in shapes],
        copies=4,
        micros=1,
        after=after,
    )


def cross_plane(place, onward):
    return [place.swap_xy(onward[0], 2), place.swap_xy(onward[1], 1)]


def column_blocks(grads, came, onward, norm_terms=(), after=()):
    shape = onward[0].shape
    rows = shape[-2] // 2
    width = D
    few = rows // 4
    extra = 16 if norm_terms else 0

    def body(*refs):
        terms_refs, refs = refs[: len(norm_terms)], refs[len(norm_terms) :]
        ins, outs, (held, shards, sems) = refs[:6], refs[6:-3], refs[-3:]
        home, slots = column_slots()
        copies = Copies(sems)
        for i, ref in enumerate(ins):
            copies.start(ref if i % 3 == 2 else ref.at[0], held.at[i])
        copies.wait()
        sums = [add_up(held[3 * part], held[3 * part + 1], held[3 * part + 2]) for part in range(2)]
        for hi in range(2):
            for cs in range(2):
                here = slice(cs * rows, (cs + 1) * rows)
                lanes = slice(hi * QUARTER, (hi + 1) * QUARTER)
                lanes_two = slice(HALF + hi * QUARTER, HALF + (hi + 1) * QUARTER)
                outs_rows = []
                for p in range(4):
                    at = (2 * (p // 2) + hi) * 2 * few + cs * few
                    side = HALF + (p % 2) * QUARTER
                    outs_rows.append(sums[1][at : at + few, side : side + QUARTER])
                value = jnp.concatenate(
                    [
                        sums[0][here, lanes],
                        sums[0][here, lanes_two],
                        sums[1][here, lanes],
                        jnp.concatenate(outs_rows, axis=0),
                    ],
                    axis=1,
                )
                shards[2 * hi + cs, :rows] = value.astype(BF)
        if norm_terms:
            core, xy, _ = where_am_i()
            terms = add_up(*[ref[...] for ref in terms_refs])
            terms = jnp.concatenate([terms, jnp.zeros_like(terms)], axis=0).astype(BF)
            feature = lax.broadcasted_iota(jnp.int32, (D, D), 0)
            lane = lax.broadcasted_iota(jnp.int32, (D, D), 1)
            for hi in range(2):
                for cs in range(2):
                    offset = (2 * core + hi) * QUARTER + (2 * xy + cs) * few
                    pick = jnp.where((feature == lane + offset) & (lane < few), 1.0, 0.0)
                    shards[2 * hi + cs, rows:] = mm(terms, pick.astype(BF)).astype(BF)
        for k in range(4):
            outs[k][...] = shards[slots[k]]

    ins = [grads[1], came[0], onward[0], grads[3], came[1], onward[1]]
    return run(
        body,
        [shaped((rows + extra, width))] * 4,
        vmem=list(norm_terms),
        hbm=ins,
        after=after,
        scratch=[pltpu.VMEM((6,) + shape, BF), pltpu.VMEM((4, rows + extra, width), BF)],
        copies=6,
        micros=2,
    )


def sum_plain(place, grads, attention):
    wide, narrow = grads[1][0], grads[3][0]
    rows = D // place.dp
    if attention:
        value = jnp.stack([wide[:, :HALF], wide[:, HALF:], narrow[:, :HALF]], axis=1)
        value = value.reshape(place.dp, rows, 3, 2, QUARTER).transpose(3, 0, 1, 2, 4)
        value = value.reshape(2, place.dp, rows, 3 * QUARTER)
        outs = narrow[:, HALF:].reshape(2, 2, place.dp, rows // 4, 2, QUARTER)
        outs = outs.transpose(1, 2, 0, 4, 3, 5).reshape(2, place.dp, rows, QUARTER)
        value = jnp.concatenate([value, outs], axis=-1)
    else:
        value = jnp.concatenate(
            [wide.reshape(2, place.dp, rows, D), narrow.reshape(2, place.dp, rows, D)], axis=-1
        )
    whole = jnp.zeros((2,) + value.shape, F32)
    whole = lax.dynamic_update_index_in_dim(whole, value.astype(F32), place.core, 0)
    whole = whole.reshape((4 * place.dp,) + value.shape[2:])
    return lax.psum_scatter(whole, ("mp", "xy", "core"), scatter_dimension=0, tiled=False)


def attention_outputs(sums, rows, few):
    value = sums[:rows]
    last = value[:, 3 * QUARTER :]
    out = jnp.concatenate([last[p * few : (p + 1) * few] for p in range(4)], axis=1)
    return [value[:, j * QUARTER : (j + 1) * QUARTER] for j in range(3)], out


def finish_self(got, own, few_lanes):
    rows = own.shape[0] - 16
    few = rows // 4

    def body(a, b, c, d, own_ref, qkv_ref, out_ref, gain_ref, bias_ref):
        home, _ = column_slots()
        last = jnp.where(home, own_ref[...].astype(F32), d[...].astype(F32))
        sums = add_up(a[...], b[...], c[...], last)
        blocks, out = attention_outputs(sums, rows, few)
        for j in range(3):
            qkv_ref[j] = blocks[j]
        out_ref[...] = out
        gain_ref[...] = sums[rows : rows + 4, :few_lanes]
        bias_ref[...] = sums[rows + 4 : rows + 8, :few_lanes]

    return run(
        body,
        [
            shaped((3, rows, QUARTER), F32),
            shaped((few, D), F32),
            shaped((4, few_lanes), F32),
            shaped((4, few_lanes), F32),
        ],
        vmem=list(got) + [own],
        micros=1.5,
    )


def finish_cross(got, own, after=()):
    rows = own.shape[0]
    few = rows // 4

    def body(a, b, c, d, own_ref, kv_ref, q_ref, out_ref):
        home, _ = column_slots()
        last = jnp.where(home, own_ref[...].astype(F32), d[...].astype(F32))
        blocks, out = attention_outputs(add_up(a[...], b[...], c[...], last), rows, few)
        kv_ref[...] = jnp.concatenate(blocks[:2], axis=1)
        q_ref[...] = blocks[2]
        out_ref[...] = out

    return run(
        body,
        [shaped((rows, HALF), F32), shaped((rows, QUARTER), F32), shaped((few, D), F32)],
        vmem=list(got) + [own],
        micros=1.5,
        after=after,
    )


def join_rows(blocks, got, dtype, after=()):
    width, rows = blocks[0].shape

    def body(block_ref, first_ref, second_ref, out_ref):
        home, _ = column_slots()
        _, _, z = where_am_i()

        @pl.when(home)
        def _():
            out_ref[z % 2] = block_ref[...].astype(dtype)

        @pl.when(jnp.logical_not(home))
        def _():
            out_ref[z % 2] = first_ref[...].astype(dtype)

        out_ref[(z + 1) % 2] = second_ref[...].astype(dtype)

    joined = run(
        body,
        [shaped((2, width, rows), dtype)],
        vmem=[blocks[0]] + list(got),
        micros=2,
        after=after,
    )[0]
    return joined[:, None].transpose(0, 1, 3, 2)


def from_quarters(value):
    few = value.shape[0] // 4
    return value.reshape(4, few, QUARTER).transpose(1, 0, 2).reshape(few, D)


def three_parts(value):
    terms = []
    for _ in range(3):
        term = lax.reduce_precision(value, 8, 7)
        terms.append(term.astype(BF))
        value = value - term
    return jnp.concatenate(terms)


def per_device(
    dp,
    mp,
    hidden_in,
    encoder_states,
    cotangent,
    self_qkv,
    self_out,
    cross_q,
    cross_kv,
    cross_out,
    fc_in,
    fc_out,
    ln_gain,
    ln_bias,
    token_lengths,
    audio_lengths,
    corpus_ids,
    corpus_weights,
):
    place = Place(dp, mp)
    length = hidden_in.shape[2]
    frames = encoder_states.shape[2]
    padded = -(-frames // CHUNK) * CHUNK
    rows = self_qkv.shape[0]

    encoded = lax.dynamic_index_in_dim(encoder_states[:, 0], place.micro, 0, keepdims=False)
    first = ()
    if place.fast:
        shard = attention_shard(self_qkv, self_out, cross_kv, cross_q, cross_out)
        packed = pack_attention(place.column_out(shard), shard, (encoded,))
        w_self = w_cross = spread(place, packed)
        first = (shard,)
    else:
        quarter = lambda w: w.reshape(-1, 4, QUARTER).transpose(1, 0, 2).reshape(-1, QUARTER)
        flat = lambda w: w.reshape(rows, -1)
        w_self = attention_plain(
            place, jnp.concatenate([flat(self_qkv), quarter(self_out)], axis=1)
        )
        w_cross = attention_plain(
            place, jnp.concatenate([flat(cross_kv), cross_q, quarter(cross_out)], axis=1)
        )


    unit = unit_shard(place, fc_in, fc_out)
    if not place.fast:
        w_units = gather_units(place, unit)

    turned = lambda value: value[:, 0].transpose(0, 2, 1)
    numbers = jnp.concatenate([token_lengths.T, audio_lengths.T, corpus_ids.T])
    blocks = input_blocks(
        turned(hidden_in),
        three_parts(jnp.concatenate([ln_gain, ln_bias])),
        numbers,
        first,
    )
    got = place.rows_in(blocks)
    if place.fast:
        unit, packed = lax.optimization_barrier((unit, packed))
        stacked = stack_units(
            [unit] + [place.swap_z(unit, k) for k in (1, 2, 3)], tuple(w_self[3:5])
        )
        w_units = spread(place, stacked)
    hidden, norms, nums = prepare(got, place.swap_core(got), corpus_weights)

    other = place.move(encoded, lambda xy, core, z: (xy, 1 - core, z) if core == z // 2 else None)
    encoded = jnp.where(place.home == place.core, encoded, other)
    encoded = jnp.pad(encoded, ((0, padded - frames), (0, 0)))

    et = turn(encoded)
    part1, at, qkv, qt, kt, ot1, lse1 = self_forward(hidden, norms, nums, w_self, (et,))
    other1 = place.swap_core(part1)
    got = place.rows_in(turned_blocks(turned(cotangent), (at,)))
    kv, kvt = cross_memory(encoded, w_cross)
    part2, h1, ct, q2, qt2, ot2, lse2 = cross_forward(
        hidden, part1, other1, norms, nums, kv, kvt, w_cross
    )
    other2 = place.swap_core(part2)
    cot = prepare_cotangent(got, place.swap_core(got), (part2,))
    part3, h2, mt, slope, it = units_forward(h1, part2, other2, norms, w_units)
    other3 = place.swap_core(part3)
    part, d3, e3, dz, terms3, out_a, out_b = units_backward(
        h2, part3, other3, norms, nums, cot, slope, w_units
    )
    other = place.swap_core(part)
    g_units = units_grads(place, mt, dz, it, e3)
    came_units = leave_plane(place, g_units) if place.fast else None
    layer_got = place.rows_sent((out_a, out_b))
    layer_out = place.rows_joined((out_a, out_b), layer_got)
    part, d2, e2, dq2, dkv, terms2 = cross_backward(
        d3, h2, part, other, norms, nums, kv, kvt, q2, qt2, ot2, lse2, w_cross, layer_got
    )
    other = place.swap_core(part)
    g_cross = attention_grads(place, et, dkv, ct, dq2, ot2, e2)
    came_cross = leave_plane(place, g_cross) if place.fast else None
    keep, send = encoder_grad(dkv, w_cross, (g_cross[0],))
    passed = pass_on(g_units, came_units, (keep,)) if place.fast else ()
    encoder_blocks = finish_encoder(keep, place.swap_core(send), frames, passed)
    encoder_got = place.rows_sent(encoder_blocks)
    held = encoder_blocks
    if place.fast:
        onward_units = cross_plane(place, passed)
        passed = pass_on(g_cross, came_cross, encoder_blocks)
        onward_cross = cross_plane(place, passed)
        kept, sent = units_sum(g_units, came_units, onward_units, passed)
        came_units = place.swap_z(sent, 1)
        held = (kept,)
    part, d1, e1, dqk, dv, terms1 = self_backward(
        d2, h1, part, other, norms, nums, qkv, qt, kt, ot1, lse1, w_self, held
    )
    other = place.swap_core(part)
    g_self = attention_grads(place, at, dqk, at, dv, ot1, e1)
    held = ()
    if place.fast:
        came_self = leave_plane(place, g_self)
        second = add_second(kept, came_units, (g_self[0],))
        last_units = place.swap_z(second, 2)
        cross_blocks = column_blocks(
            g_cross, came_cross, onward_cross, (), [second] + encoder_got
        )
        cross_got = place.column_back(cross_blocks)
        held = (cross_blocks[0],)
    terms, out_a, out_b = finish_hidden(
        d1, hidden, part, other, norms, terms1, terms2, terms3, held
    )
    hidden_got = place.rows_sent((out_a, out_b))

    few = D // (place.dp * place.mp)
    if place.fast:
        passed = pass_on(g_self, came_self, (terms,))
        onward_self = cross_plane(place, passed)
        grad_encoder = join_rows(encoder_blocks, encoder_got, F32, passed)
        mine, sent, s_down = cut_units(kept, came_units, last_units, passed)
        s_up = join_units(place, mine, place.swap_core(sent))
        terms = terms + place.swap_xy(terms, 1)
        blocks = column_blocks(
            g_self, came_self, onward_self, (terms, place.swap_xy(terms, 2)), (s_down,)
        )
        g_qkv, g_out, g_gain, g_bias = finish_self(place.column_back(blocks), blocks[3], few)
        g_ckv, g_cq, g_cout = finish_cross(cross_got, cross_blocks[3], (blocks[0],))
        grad_hidden = join_rows((out_a, out_b), hidden_got, F32, (blocks[0],))
        g_qkv = g_qkv.transpose(1, 0, 2)
    else:
        s_up, s_down = scatter_units(place, g_units)
        grad_encoder = place.rows_joined(encoder_blocks, encoder_got).astype(F32)
        grad_hidden = place.rows_joined((out_a, out_b), hidden_got).astype(F32)
        s_cross = sum_plain(place, g_cross, True)
        s_self = sum_plain(place, g_self, True)
        terms = jnp.where(place.core == 0, terms, 0.0)
        terms = lax.psum(terms, AXES)
        shares = lax.dynamic_slice_in_dim(terms, (place.z * place.dp + place.d) * few, few, 1)
        g_gain, g_bias = shares[:4], shares[4:]
        g_qkv, g_out = s_self[:, : 3 * QUARTER], from_quarters(s_self[:, 3 * QUARTER :])
        g_ckv, g_cq = s_cross[:, :HALF], s_cross[:, HALF : 3 * QUARTER]
        g_cout = from_quarters(s_cross[:, 3 * QUARTER :])
    return (
        layer_out,
        grad_hidden,
        grad_encoder,
        g_qkv.reshape(rows, 3, QUARTER),
        g_out,
        g_cq,
        g_ckv.reshape(rows, 2, QUARTER),
        g_cout,
        s_up,
        s_down,
        g_gain,
        g_bias,
    )


def solution(mesh):
    dp, mp = mesh.shape["dp"], mesh.shape["mp"]
    finer = Mesh(mesh.devices.reshape(dp // 2, 2, mp), AXES)
    both = ("xy", "core")
    rows = P(None, both, None, "mp")
    columns = P(both, None, "mp")
    pairs = P(both, "mp")
    units = P(("mp",) + both, None)
    each = P(None, both)
    return jax.shard_map(
        partial(per_device, dp, mp),
        mesh=finer,
        in_specs=(
            rows,
            P(None, both, None, None),
            rows,
            columns,
            units,
            pairs,
            columns,
            units,
            pairs,
            units,
            P(None, "mp"),
            P(None, "mp"),
            each,
            each,
            each,
            P(),
        ),
        out_specs=(
            rows,
            rows,
            rows,
            columns,
            units,
            pairs,
            columns,
            units,
            pairs,
            units,
            P(None, ("mp",) + both),
            P(None, ("mp",) + both),
        ),
        check_vma=False,
    )
```

```python
from functools import partial

import jax
import jax.numpy as jnp
from jax import lax
from jax.experimental import pallas as pl
from jax.experimental.pallas import tpu as pltpu
from jax.sharding import Mesh, PartitionSpec as P

D = 768
HALF = 384
QUARTER = 192
HEAD_DIM = 64
HEADS = 6
CHUNK = 256
BF = jnp.bfloat16
F32 = jnp.float32
AXES = ("xy", "core", "mp")
CHIPS = ("xy", "mp")
VMEM = pl.BlockSpec(memory_space=pltpu.VMEM)
SMEM = pl.BlockSpec(memory_space=pltpu.SMEM)
ANY = pl.BlockSpec(memory_space=pl.ANY)
HBM = pl.BlockSpec(memory_space=pltpu.HBM)


def mm(left, right):
    return jnp.dot(left, right, preferred_element_type=F32)


def mm_t(left, right):
    return lax.dot_general(left, right, (((1,), (1,)), ((), ())), preferred_element_type=F32)


def shaped(shape, dtype=BF):
    return jax.ShapeDtypeStruct(shape, dtype)


def room(shape, dtype):
    item = jnp.dtype(dtype).itemsize
    shape = (1, 1) + tuple(shape)
    tile = 32 // item
    size = item * (-(-shape[-1] // 128) * 128) * (-(-shape[-2] // tile) * tile)
    for extent in shape[:-2]:
        size *= extent
    return size


def run(
    body, outs, vmem=(), hbm=(), smem=(), scratch=(), copies=0, micros=2, after=(), staged=False
):
    args = tuple(smem) + tuple(vmem) + tuple(hbm)
    count = len(args)
    scratch = list(scratch)
    if copies:
        scratch.append(pltpu.SemaphoreType.DMA((copies,)))
    need = sum(room(a.shape, a.dtype) for a in tuple(vmem) + tuple(outs))
    need += sum(room(a.shape, a.dtype) for a in scratch if a.memory_space == pltpu.VMEM)
    need = min(need + 12 * 1024 * 1024, 60 * 1024 * 1024)
    moved = sum(a.size * a.dtype.itemsize for a in args) + sum(
        o.size * o.dtype.itemsize for o in outs
    )
    skip = len(scratch)
    if staged:
        scratch += [pltpu.VMEM(a.shape, a.dtype) for a in vmem]
        scratch.append(pltpu.SemaphoreType.DMA((len(vmem),)))

    def whole(*refs):
        ins, rest = list(refs[:count]), refs[count + len(after) :]
        if staged:
            held = rest[len(outs) + skip : -1]
            rest, sems = rest[: len(outs) + skip], rest[-1]
            copies = Copies(sems)
            for i, target in enumerate(held):
                copies.start(ins[len(smem) + i], target)
                ins[len(smem) + i] = target
            copies.wait()
        body(*ins, *rest)

    place = HBM if staged else VMEM
    return pl.pallas_call(
        whole,
        out_shape=tuple(outs),
        in_specs=[SMEM] * len(smem) + [place] * len(vmem) + [ANY] * (len(hbm) + len(after)),
        out_specs=(VMEM,) * len(outs),
        scratch_shapes=scratch,
        compiler_params=pltpu.CompilerParams(vmem_limit_bytes=need),
        cost_estimate=pl.CostEstimate(
            flops=int(micros * 1.15e9), bytes_accessed=moved, transcendentals=0
        ),
    )(*args, *after)


class Copies:
    def __init__(self, sems):
        self.sems, self.open = sems, []

    def start(self, source, target):
        copy = pltpu.make_async_copy(source, target, self.sems.at[len(self.open)])
        copy.start()
        self.open.append(copy)

    def wait(self):
        for copy in self.open:
            copy.wait()


def where_am_i():
    return lax.axis_index("core"), lax.axis_index("xy"), lax.axis_index("mp")


class Place:
    def __init__(self, dp, mp):
        self.dp, self.mp = dp, mp
        self.chips = dp // 2
        self.fast = self.chips == 4
        self.z = lax.axis_index("mp")
        self.core = lax.axis_index("core")
        self.xy = lax.axis_index("xy")
        self.d = 2 * self.xy + self.core
        self.micro = self.z % 2
        self.home = self.z // 2

    def move(self, value, route):
        pairs = []
        for xy in range(self.chips):
            for core in range(2):
                for z in range(self.mp):
                    target = route(xy, core, z)
                    if target is not None:
                        txy, tcore, tz = target
                        pairs.append(
                            ((2 * xy + core) * self.mp + z, (2 * txy + tcore) * self.mp + tz)
                        )
        return lax.ppermute(value, AXES, pairs)

    def swap_core(self, value):
        return self.move(value, lambda xy, core, z: (xy, 1 - core, z))

    def swap_xy(self, value, bit):
        return self.move(value, lambda xy, core, z: (xy ^ bit, core, z))

    def swap_z(self, value, bit):
        return self.move(value, lambda xy, core, z: (xy, core, z ^ bit))

    def column_routes(self):
        def route(step, xy, core, z):
            user, j = z // 2, z % 2
            home = core == user
            near = lambda i: (xy, user, 2 * user + i)
            far = lambda i: (xy, user, 2 * (1 - user) + i)
            if step == 0:
                return near(1 - j) if home else far(1 - j)
            if step == 1:
                return far(j) if home else near(j)
            if step == 2:
                return far(1 - j) if home else near(1 - j)
            return None if home else far(j)

        return [partial(route, step) for step in range(4)]

    def column_out(self, shard):
        return [self.move(shard, route) for route in self.column_routes()]

    def column_back(self, blocks):
        got = []
        for block, route in zip(blocks, self.column_routes()):
            turned = {}
            for xy in range(self.chips):
                for core in range(2):
                    for z in range(self.mp):
                        target = route(xy, core, z)
                        if target is not None:
                            turned[target] = (xy, core, z)
            got.append(self.move(block, lambda xy, core, z: turned.get((xy, core, z))))
        return got

    def rows_in(self, blocks):
        def route(k, xy, core, z):
            target = (xy, z // 2, 2 * core + (z + k) % 2)
            return None if target == (xy, core, z) else target

        got = [self.move(block, partial(route, k)) for k, block in enumerate(blocks)]
        return jnp.stack([jnp.where(self.core == self.home, blocks[0], got[0]), got[1]])

    def rows_home(self, blocks):
        return self.rows_joined(blocks, self.rows_sent(blocks))

    def rows_sent(self, blocks):
        def route(k, xy, core, z):
            target = (xy, z // 2, 2 * core + (z % 2 - k) % 2)
            return None if target == (xy, core, z) else target

        return [self.move(block, partial(route, k)) for k, block in enumerate(blocks)]

    def rows_joined(self, blocks, got):
        got = [jnp.where(self.core == self.home, blocks[0], got[0]), got[1]]
        even = self.z % 2 == 0
        both = jnp.stack([jnp.where(even, got[0], got[1]), jnp.where(even, got[1], got[0])])
        return both[:, None].transpose(0, 1, 3, 2)


def norm(hidden):
    center = jnp.mean(hidden, axis=-1, keepdims=True)
    spread = jnp.mean(hidden * hidden, axis=-1, keepdims=True) - center * center
    inverse = lax.rsqrt(spread + 1e-05)
    return (hidden - center) * inverse, inverse


def norm_back(grad, unit, inverse, gain):
    scaled = grad * gain
    first = jnp.mean(scaled, axis=-1, keepdims=True)
    second = jnp.mean(scaled * unit, axis=-1, keepdims=True)
    terms = jnp.concatenate(
        [jnp.sum(grad * unit, axis=0, keepdims=True), jnp.sum(grad, axis=0, keepdims=True)], axis=0
    )
    return inverse * (scaled - first - unit * second), terms


def add_up(*terms):
    total = terms[0].astype(F32)
    for term in terms[1:]:
        total = total + term.astype(F32)
    return total


def input_blocks(hidden, terms, numbers, after=()):
    _, width, length = hidden.shape
    total = width + 32

    def body(numbers_ref, hidden_ref, terms_ref, *outs):
        _, _, z = where_am_i()
        lanes = lax.broadcasted_iota(jnp.int32, (8, length), 1)
        for k in range(2):
            micro = (z + k) % 2
            outs[k][0:width] = hidden_ref[micro]
            tok, aud = numbers_ref[0, micro], numbers_ref[1, micro]
            row = jnp.where(lanes == 0, tok // 256, jnp.where(lanes == 1, tok % 256, 0))
            row = jnp.where(lanes == 2, aud // 256, jnp.where(lanes == 3, aud % 256, row))
            row = jnp.where(lanes == 4, numbers_ref[2, micro], row)
            wide = jnp.concatenate(
                [terms_ref[...].astype(F32), jnp.zeros((24, length - width), F32)], axis=1
            )
            outs[k][width:total] = jnp.concatenate([wide, row.astype(F32)], axis=0).astype(BF)

    return run(
        body,
        [shaped((total, length))] * 2,
        smem=[numbers],
        vmem=[hidden, terms],
        micros=1,
        after=after,
    )


def turned_blocks(value, after=()):
    _, width, length = value.shape

    def body(ref, first_ref, second_ref):
        _, _, z = where_am_i()
        first_ref[...] = ref[z % 2]
        second_ref[...] = ref[(z + 1) % 2]

    return run(body, [shaped((width, length))] * 2, vmem=[value], micros=1, after=after)


def bring_blocks(copies, own_ref, other_ref, wide):
    core, _, z = where_am_i()
    found = []
    for k in range(2):
        slot = (z % 2 + k) % 2
        for ref, user in ((own_ref, core), (other_ref, 1 - core)):
            block = 2 * user + slot
            here = pl.ds(pl.multiple_of(block * QUARTER, QUARTER), QUARTER)
            copies.start(ref.at[k, pl.ds(0, QUARTER)], wide.at[here])
            found.append((ref.at[k], block))
    return found


def prepare_cotangent(own, other, after=()):
    length = own.shape[2]

    def body(own_ref, other_ref, cot_ref, wide, sems):
        copies = Copies(sems)
        bring_blocks(copies, own_ref, other_ref, wide)
        copies.wait()
        cot_ref[...] = wide[...].T

    return run(
        body,
        [shaped((length, D))],
        hbm=[own, other],
        scratch=[pltpu.VMEM((D, length), BF)],
        copies=4,
        micros=3,
        after=after,
    )[0]


def prepare(own, other, corpus_weights):
    length = own.shape[2]

    def body(
        weights_ref, own_ref, other_ref, hidden_ref, norms_ref, nums_ref, wide, extra, sems
    ):
        copies = Copies(sems)
        for ref, block in bring_blocks(copies, own_ref, other_ref, wide):
            copies.start(ref.at[pl.ds(QUARTER, 32)], extra.at[block])
        copies.wait()
        hidden_ref[...] = wide[...].T
        parts = [extra[b].astype(F32) for b in range(4)]
        norms_ref[...] = jnp.concatenate(
            [(e[0:8] + e[8:16] + e[16:24])[:, :QUARTER] for e in parts], axis=1
        )
        row = parts[0][24:25]
        tok = 256.0 * row[:, 0:1] + row[:, 1:2]
        aud = 256.0 * row[:, 2:3] + row[:, 3:4]
        weights = weights_ref[...]
        places = lax.broadcasted_iota(jnp.int32, weights.shape, 1).astype(F32)
        weight = jnp.sum(jnp.where(places == row[:, 4:5], weights, 0.0), axis=1, keepdims=True)
        index = lax.broadcasted_iota(jnp.int32, (8, 128), 0)
        nums_ref[...] = jnp.where(index == 0, tok, jnp.where(index == 1, aud, weight))

    return run(
        body,
        [shaped((length, D)), shaped((8, D), F32), shaped((8, 128), F32)],
        vmem=[corpus_weights.reshape(1, -1)],
        hbm=[own, other],
        scratch=[pltpu.VMEM((D, length), BF), pltpu.VMEM((4, 32, length), BF)],
        copies=8,
        micros=3,
    )


def quarters(value):
    return jnp.concatenate([value[:, p * QUARTER : (p + 1) * QUARTER] for p in range(4)], axis=0)


def attention_shard(self_qkv, self_out, cross_kv, cross_q, cross_out):
    rows = cross_q.shape[0]

    def body(qkv_ref, out_ref, kv_ref, q_ref, cout_ref, shard_ref):
        out = quarters(out_ref[...].astype(F32)).astype(BF)
        cout = quarters(cout_ref[...].astype(F32)).astype(BF)
        shard_ref[...] = jnp.concatenate(
            [qkv_ref[j] for j in range(3)] + [out, kv_ref[...], q_ref[...], cout], axis=1
        )

    return run(
        body,
        [shaped((rows, 2 * D))],
        vmem=[self_qkv.transpose(1, 0, 2), self_out, cross_kv.reshape(rows, -1), cross_q, cross_out],
        micros=2,
        staged=True,
    )[0]


def column_slots():
    core, _, z = where_am_i()
    j = z % 2
    home = 1 - jnp.abs(z // 2 - core)
    same = core + (1 - 2 * core) * (1 - home)
    return home == 1, (2 * (1 - j) + same, 2 * j + 1 - same, 2 * (1 - j) + 1 - same, 2 * j + same)


def bring_column(part_refs, own_ref, shards, sems):
    home, slots = column_slots()
    copies = Copies(sems)
    for k in range(3):
        copies.start(part_refs[k], shards.at[slots[k]])

    @pl.when(home)
    def _():
        copy = pltpu.make_async_copy(own_ref, shards.at[slots[3]], sems.at[3])
        copy.start()
        copy.wait()

    @pl.when(jnp.logical_not(home))
    def _():
        copy = pltpu.make_async_copy(part_refs[3], shards.at[slots[3]], sems.at[3])
        copy.start()
        copy.wait()

    copies.wait()


def pack_attention(parts, own, after):
    rows = own.shape[0]
    few = rows // 4

    def body(*refs):
        part_refs, own_ref, (out_ref, shards, sems) = refs[:4], refs[4], refs[5:]
        bring_column(part_refs, own_ref, shards, sems)
        for which in range(2):
            for cs in range(2):
                low, high = shards[cs], shards[2 + cs]

                def both(at):
                    at = at + which * D
                    return [low[:, at : at + QUARTER], high[:, at : at + QUARTER]]

                here = pl.ds(cs * rows, rows)
                out_ref[0, which, here, :] = jnp.concatenate(both(0) + both(QUARTER), axis=1)
                out_ref[1, which, here, 0:HALF] = jnp.concatenate(both(HALF), axis=1)
            at = 3 * QUARTER + which * D
            outs = [shards[i, :, at : at + QUARTER].astype(F32) for i in range(4)]
            stack = []
            for q in range(2):
                for i in range(4):
                    left = outs[i][2 * q * few : (2 * q + 1) * few]
                    right = outs[i][(2 * q + 1) * few : (2 * q + 2) * few]
                    stack.append(jnp.concatenate([left, right], axis=1))
            out_ref[1, which, :, HALF:D] = jnp.concatenate(stack, axis=0).astype(BF)

    return run(
        body,
        [shaped((2, 2, 2 * rows, D))],
        hbm=list(parts) + [own],
        scratch=[pltpu.VMEM((4, rows, 2 * D), BF)],
        copies=4,
        micros=2,
        after=after,
    )[0]


def unit_shard(place, fc_in, fc_out):
    rows = fc_in.shape[0]
    both = fc_in.reshape(rows, place.chips, 2, rows).transpose(2, 0, 1, 3).reshape(2, rows, HALF)
    kept = lax.dynamic_index_in_dim(both, place.core, 0, keepdims=False)
    sent = lax.dynamic_index_in_dim(both, 1 - place.core, 0, keepdims=False)
    came = place.swap_core(sent)
    first = place.core == 0
    left = jnp.concatenate([jnp.where(first, kept, came), jnp.where(first, came, kept)])
    right = jnp.concatenate([fc_out[:, :HALF], fc_out[:, HALF:]])
    return jnp.concatenate([left, right], axis=1)


def stack_units(blocks, after):
    rows = blocks[0].shape[0]

    def body(*refs):
        for k in range(4):
            refs[4][k // 2, k % 2] = refs[k][...]

    return run(body, [shaped((2, 2, rows, D))], vmem=blocks, micros=1.5, after=after)[0]


def gather_units(place, shard):
    whole = lax.all_gather(shard, CHIPS, axis=0)
    rows = shard.shape[0] // 2
    whole = whole.reshape(place.chips, place.mp, 2 * rows, D)
    up = whole[..., :HALF].transpose(0, 2, 1, 3).reshape(D, 2 * D)
    down = whole[..., HALF:].reshape(place.chips, place.mp, 2, rows, HALF)
    return [up, down.transpose(1, 0, 3, 2, 4).reshape(2 * D, D)]


def scatter_units(place, grads):
    total = lax.psum_scatter(grads, CHIPS, scatter_dimension=0, tiled=False)
    rows = total.shape[0] // 2
    kept = lax.dynamic_slice_in_dim(total, place.core * rows, rows, 0)
    sent = lax.dynamic_slice_in_dim(total[:, :HALF], (1 - place.core) * rows, rows, 0)
    came = place.swap_core(sent)
    kept = kept[:, :HALF]
    first = place.core == 0
    both = jnp.stack([jnp.where(first, kept, came), jnp.where(first, came, kept)])
    both = both.reshape(2, rows, place.chips, rows).transpose(1, 2, 0, 3).reshape(rows, D)
    down = jnp.concatenate([total[:rows, HALF:], total[rows:, HALF:]], axis=1)
    return both.astype(F32), down.astype(F32)


def spread(place, own):
    from_x = place.swap_xy(own, 1)
    from_y = place.swap_xy(own, 2)
    far_one = place.swap_xy(from_y[1], 1)
    far_zero = place.swap_xy(from_x[0], 2)
    return [own, from_x, from_y, far_zero, far_one]


def piece_views(refs, message, which, xy):
    own, from_x, from_y, far_zero, far_one = refs
    return [
        (own.at[which, message], xy),
        (from_x.at[which, message], xy ^ 1),
        (from_y.at[which, message], xy ^ 2),
        ((far_zero, far_one)[which].at[message], xy ^ 3),
    ]


def load_wide(copies, refs, message, which, xy, target, columns=None):
    if len(refs) != 5:
        copies.start(refs[which], target)
        return
    for view, chip in piece_views(refs, message, which, xy):
        rows = view.shape[0]
        if columns is not None:
            view = view.at[:, pl.ds(0, columns)]
        copies.start(view, target.at[pl.ds(pl.multiple_of(chip * rows, 16), rows)])


def load_out(copies, refs, message, xy, target):
    if len(refs) != 5:
        copies.start(refs[2], target)
        return
    for view, chip in piece_views(refs, message, 1, xy):
        rows = view.shape[0] // 4
        for q in range(2):
            for hi in range(2):
                copies.start(
                    view.at[pl.ds((2 * q + hi) * rows, rows), pl.ds(HALF, HALF)],
                    target.at[q, pl.ds(pl.multiple_of(hi * QUARTER + chip * rows, 16), rows)],
                )


def unit_views(refs):
    _, xy, z = where_am_i()
    views = []
    for part in range(2):
        for view, chip in [
            (refs[0].at[part], xy),
            (refs[1].at[part], xy ^ 1),
            (refs[2].at[part], xy ^ 2),
            (refs[3 + part], xy ^ 3),
        ]:
            for i in range(2):
                views.append((view.at[i], chip, z ^ (2 * part + i)))
    return views


def load_up(copies, refs, w_up):
    if len(refs) == 2:
        copies.start(refs[0], w_up)
        return
    for view, chip, z in unit_views(refs):
        rows = view.shape[0]
        copies.start(
            view.at[:, pl.ds(0, HALF)],
            w_up.at[
                pl.ds(pl.multiple_of(rows * chip, 16), rows), pl.ds(pl.multiple_of(z * HALF, HALF), HALF)
            ],
        )


def load_down(copies, refs, w_down):
    if len(refs) == 2:
        copies.start(refs[1], w_down)
        return
    for view, chip, z in unit_views(refs):
        rows = view.shape[0] // 2
        for q in range(2):
            copies.start(
                view.at[pl.ds(q * rows, rows), pl.ds(HALF, HALF)],
                w_down.at[
                    pl.ds(pl.multiple_of(z * HALF + chip * rows, 16), rows), pl.ds(q * HALF, HALF)
                ],
            )


ATTENTION_COPIES = 4 + 4 + 16
UP_COPIES = 16
DOWN_COPIES = 32


def gather_plain(place, shard):
    whole = lax.all_gather(shard, ("mp", "xy", "core"), axis=0)
    whole = whole.reshape((2, 2, place.dp) + shard.shape)
    return lax.dynamic_index_in_dim(whole, place.core, 0, keepdims=False)


def attention_plain(place, shard):
    mine = gather_plain(place, shard)
    rows = shard.shape[0]

    def columns(at, count):
        value = mine[..., at : at + count * QUARTER].reshape(2, D, count, QUARTER)
        return value.transpose(1, 2, 0, 3).reshape(D, count * HALF)

    out = mine[..., 3 * QUARTER :].reshape(2, place.dp, 2, 2, rows // 4, QUARTER)
    out = out.transpose(2, 0, 1, 4, 3, 5).reshape(2, HALF, HALF)
    return [columns(0, 2), columns(HALF, 1), out]


def head_rows(h):
    return pl.ds(pl.multiple_of(h * HEAD_DIM, HEAD_DIM), HEAD_DIM)


def low_parts(value):
    parts = []
    for _ in range(3):
        part = value.astype(BF)
        parts.append(part)
        value = value - part.astype(F32)
    return parts


def widened(count):
    return lambda rows: (
        lax.broadcasted_iota(jnp.int32, (rows, HEAD_DIM), 1) < count
    ).astype(F32).astype(BF)


def below(head, rows):
    blank = jnp.zeros((HEAD_DIM - len(rows), head.shape[1]), F32)
    rest = jnp.concatenate([row.astype(F32) for row in rows] + [blank], axis=0)
    return jnp.concatenate([head, rest.astype(BF)], axis=0)


def project(left, pair_ref):
    return jnp.concatenate([mm(left, pair_ref[0]), mm(left, pair_ref[1])], axis=1)


def project_t(left, pair_ref):
    return mm_t(left[:, :HALF], pair_ref[0]) + mm_t(left[:, HALF:], pair_ref[1])


def self_forward(hidden, norms, nums, weights, after=()):
    length = hidden.shape[0]

    def body(hidden_ref, norms_ref, nums_ref, *refs):
        w_refs, refs = refs[: len(weights)], refs[len(weights) :]
        part_ref, at_ref, qkv_ref, qt_ref, kt_ref, ot_ref, lse_ref = refs[:7]
        w_qk, w_v, w_out, vt, heads, bias, sems = refs[7:]
        _, xy, _ = where_am_i()
        copies = Copies(sems)
        load_wide(copies, w_refs, 0, 0, xy, w_qk)
        load_wide(copies, w_refs, 0, 1, xy, w_v, HALF)
        load_out(copies, w_refs, 0, xy, w_out)
        unit, _ = norm(hidden_ref[...].astype(F32))
        a = (unit * norms_ref[0:1] + norms_ref[4:5]).astype(BF)
        at_ref[...] = a.T
        keys = lax.broadcasted_iota(jnp.int32, (length, length), 0)
        queries = lax.broadcasted_iota(jnp.int32, (length, length), 1)
        allowed = (keys <= queries) & (keys.astype(F32) < nums_ref[0:1, 0:1])
        bias[...] = jnp.where(allowed, 0.0, -1e30)
        copies.wait()
        qk = mm(a, w_qk[...])
        q = (qk[:, :HALF].astype(BF).astype(F32) * HEAD_DIM ** (-0.5)).astype(BF)
        k = qk[:, HALF:].astype(BF)
        v = mm(a, w_v[...]).astype(BF)
        qkv_ref[:, 0:HALF] = q
        qkv_ref[:, HALF : 2 * HALF] = k
        qkv_ref[:, 2 * HALF :] = v
        qt_ref[...] = q.T
        kt_ref[...] = k.T
        vt[...] = v.T
        for h in range(HEADS):
            heads[h] = k[:, h * HEAD_DIM : (h + 1) * HEAD_DIM]

        def head(h, carry):
            s = mm(heads[h], qt_ref[head_rows(h), :]) + bias[...]
            top = jnp.max(s, axis=0, keepdims=True)
            p = jnp.exp(s - top)
            total = jnp.sum(p, axis=0, keepdims=True)
            o = mm(vt[head_rows(h), :], p.astype(BF))
            ot_ref[head_rows(h), :] = (o / total).astype(BF)
            lse_ref[h] = top + jnp.log(total)
            return carry

        lax.fori_loop(0, HEADS, head, 0)
        part_ref[...] = project(ot_ref[...].T, w_out).astype(BF)

    return run(
        body,
        [
            shaped((length, D)),
            shaped((D, length)),
            shaped((length, 3 * HALF)),
            shaped((HALF, length)),
            shaped((HALF, length)),
            shaped((HALF, length)),
            shaped((HEADS, 1, length), F32),
        ],
        vmem=[hidden, norms, nums],
        hbm=weights,
        scratch=[
            pltpu.VMEM((D, D), BF),
            pltpu.VMEM((D, HALF), BF),
            pltpu.VMEM((2, HALF, HALF), BF),
            pltpu.VMEM((HALF, length), BF),
            pltpu.VMEM((HEADS, length, HEAD_DIM), BF),
            pltpu.VMEM((length, length), F32),
        ],
        copies=ATTENTION_COPIES,
        micros=3,
        after=after,
    )


def turn(value, after=()):
    rows, columns = value.shape

    def body(ref, out_ref):
        for at in range(0, rows, CHUNK):
            out_ref[:, at : at + CHUNK] = ref[at : at + CHUNK, :].T

    return run(body, [shaped((columns, rows))], vmem=[value], micros=4, after=after)[0]


def cross_memory(encoded, weights):
    frames = encoded.shape[0]

    def body(enc_ref, *refs):
        w_refs, refs = refs[: len(weights)], refs[len(weights) :]
        kv_ref, kvt_ref, w_kv, sems = refs
        _, xy, _ = where_am_i()
        copies = Copies(sems)
        load_wide(copies, w_refs, 1, 0, xy, w_kv)
        copies.wait()

        def step(i, carry):
            here = pl.ds(pl.multiple_of(i * CHUNK, CHUNK), CHUNK)
            kv = mm(enc_ref[here, :], w_kv[...]).astype(BF)
            kv_ref[here, :] = kv
            kvt_ref[:, here] = kv.T
            return carry

        lax.fori_loop(0, frames // CHUNK, step, 0)

    return run(
        body,
        [shaped((frames, D)), shaped((D, frames))],
        vmem=[encoded],
        hbm=weights,
        scratch=[pltpu.VMEM((D, D), BF)],
        copies=4,
        micros=1,
    )


def residual(hidden_ref, mine_ref, other_ref):
    return hidden_ref[...].astype(F32) + (mine_ref[...].astype(F32) + other_ref[...].astype(F32))


def cross_forward(hidden, mine, other, norms, nums, kv, kvt, weights):
    length = hidden.shape[0]
    frames = kv.shape[0]

    def body(hidden_ref, mine_ref, other_ref, norms_ref, nums_ref, kv_ref, kvt_ref, *refs):
        w_refs, refs = refs[: len(weights)], refs[len(weights) :]
        part_ref, h_ref, ct_ref, q_ref, qt_ref, ot_ref, lse_ref = refs[:7]
        w_q, w_out, heads, values_t, scores, sems = refs[7:]
        _, xy, _ = where_am_i()
        copies = Copies(sems)
        load_wide(copies, w_refs, 1, 1, xy, w_q, HALF)
        load_out(copies, w_refs, 1, xy, w_out)
        h1 = residual(hidden_ref, mine_ref, other_ref)
        h_ref[...] = h1
        unit, _ = norm(h1)
        c = (unit * norms_ref[1:2] + norms_ref[5:6]).astype(BF)
        ct_ref[...] = c.T
        frame = lax.broadcasted_iota(jnp.int32, (frames, HEAD_DIM), 0).astype(F32)
        lane = lax.broadcasted_iota(jnp.int32, (frames, HEAD_DIM), 1)
        mask = jnp.where(frame < nums_ref[1:2, 0:1], 0.0, -1e30)
        beside = jnp.where(lane == 0, mask, 0.0).astype(BF)
        one = lax.broadcasted_iota(jnp.int32, (16, frames), 0)
        one = jnp.where(one == 0, 1.0, 0.0).astype(BF)
        for h in range(HEADS):
            keys = kv_ref[:, h * HEAD_DIM : (h + 1) * HEAD_DIM]
            heads[h] = jnp.concatenate([keys, beside], axis=1)
            values = kvt_ref[HALF + h * HEAD_DIM : HALF + (h + 1) * HEAD_DIM, :]
            values_t[h] = jnp.concatenate([values, one], axis=0)
        copies.wait()
        q = mm(c, w_q[...]).astype(BF)
        q = (q.astype(F32) * HEAD_DIM ** (-0.5)).astype(BF)
        q_ref[...] = q
        qt_ref[...] = q.T
        ones = jnp.ones((1, length), F32)

        def head(h, carry):
            qt = below(qt_ref[head_rows(h), :], [ones])
            top = None
            for at in range(0, frames, CHUNK):
                s = mm(heads[h, at : at + CHUNK], qt)
                scores[at : at + CHUNK] = s
                high = jnp.max(s, axis=0, keepdims=True)
                top = high if top is None else jnp.maximum(top, high)
            o = None
            for at in range(0, frames, CHUNK):
                p = jnp.exp(scores[at : at + CHUNK] - top).astype(BF)
                more = mm(values_t[h, :, at : at + CHUNK], p)
                o = more if o is None else o + more
            total = o[HEAD_DIM : HEAD_DIM + 1]
            ot_ref[head_rows(h), :] = (o[:HEAD_DIM] / total).astype(BF)
            lse_ref[h] = top + jnp.log(total)
            return carry

        lax.fori_loop(0, HEADS, head, 0)
        part_ref[...] = project(ot_ref[...].T, w_out).astype(BF)

    return run(
        body,
        [
            shaped((length, D)),
            shaped((length, D), F32),
            shaped((D, length)),
            shaped((length, HALF)),
            shaped((HALF, length)),
            shaped((HALF, length)),
            shaped((HEADS, 1, length), F32),
        ],
        vmem=[hidden, mine, other, norms, nums, kv, kvt],
        hbm=weights,
        scratch=[
            pltpu.VMEM((D, HALF), BF),
            pltpu.VMEM((2, HALF, HALF), BF),
            pltpu.VMEM((HEADS, frames, 2 * HEAD_DIM), BF),
            pltpu.VMEM((HEADS, HEAD_DIM + 16, frames), BF),
            pltpu.VMEM((frames, length), F32),
        ],
        copies=4 + 16,
        micros=2,
    )


def units_forward(hidden, mine, other, norms, weights):
    length = hidden.shape[0]

    def body(hidden_ref, mine_ref, other_ref, norms_ref, *refs):
        w_refs, refs = refs[: len(weights)], refs[len(weights) :]
        part_ref, h_ref, mt_ref, slope_ref, it_ref = refs[:5]
        w_up, w_down, inner, late_sems, sems = refs[5:]
        _, xy, _ = where_am_i()
        copies = Copies(sems)
        load_up(copies, w_refs, w_up)
        late = Copies(late_sems)
        load_down(late, w_refs, w_down)
        h2 = residual(hidden_ref, mine_ref, other_ref)
        h_ref[...] = h2
        unit, _ = norm(h2)
        m = (unit * norms_ref[2:3] + norms_ref[6:7]).astype(BF)
        mt_ref[...] = m.T
        copies.wait()
        for at in range(0, 2 * D, CHUNK):
            here = slice(at, at + CHUNK)
            z = mm(m, w_up[:, here])
            share = 0.5 * (1.0 + lax.erf(z * 0.7071067811865476))
            slope = share + z * (0.3989422804014327 * jnp.exp(-0.5 * z * z))
            value = (z * share).astype(BF)
            inner[:, here] = value
            it_ref[here, :] = value.T
            slope_ref[:, here] = slope.astype(BF)
        late.wait()
        for at in range(0, D, CHUNK):
            part_ref[:, at : at + CHUNK] = mm(inner[...], w_down[:, at : at + CHUNK]).astype(BF)

    return run(
        body,
        [
            shaped((length, D)),
            shaped((length, D), F32),
            shaped((D, length)),
            shaped((length, 2 * D)),
            shaped((2 * D, length)),
        ],
        vmem=[hidden, mine, other, norms],
        hbm=weights,
        scratch=[
            pltpu.VMEM((D, 2 * D), BF),
            pltpu.VMEM((2 * D, D), BF),
            pltpu.VMEM((length, 2 * D), BF),
            pltpu.SemaphoreType.DMA((DOWN_COPIES,)),
        ],
        copies=UP_COPIES,
        micros=9,
    )


def store_blocks(value, blocks, first_ref, second_ref):
    core, _, z = where_am_i()
    for b in range(4):
        blocks[b] = value[:, b * QUARTER : (b + 1) * QUARTER]
    first_ref[...] = blocks[2 * core + z % 2].T
    second_ref[...] = blocks[2 * core + (z + 1) % 2].T


def units_backward(hidden, mine, other, norms, nums, cot, slope, weights):
    length = hidden.shape[0]

    def body(hidden_ref, mine_ref, other_ref, norms_ref, nums_ref, cot_ref, slope_ref, *refs):
        w_refs, refs = refs[: len(weights)], refs[len(weights) :]
        part_ref, d_ref, e_ref, dz_ref, terms_ref, first_ref, second_ref = refs[:7]
        w_up, w_down, blocks, late_sems, sems = refs[7:]
        _, xy, _ = where_am_i()
        copies = Copies(sems)
        load_down(copies, w_refs, w_down)
        late = Copies(late_sems)
        load_up(late, w_refs, w_up)
        unit, inverse = norm(residual(hidden_ref, mine_ref, other_ref))
        final = (unit * norms_ref[3:4] + norms_ref[7:8]).astype(BF)
        store_blocks(final, blocks, first_ref, second_ref)
        live = lax.broadcasted_iota(jnp.int32, (length, 1), 0).astype(F32) < nums_ref[0:1, 0:1]
        grad = cot_ref[...].astype(F32) * jnp.where(live, nums_ref[2:3, 0:1], 0.0)
        d3, terms = norm_back(grad, unit, inverse, norms_ref[3:4])
        d_ref[...] = d3
        terms_ref[...] = terms
        e = d3.astype(BF)
        e_ref[...] = e
        copies.wait()
        for at in range(0, 2 * D, CHUNK):
            here = slice(at, at + CHUNK)
            d_inner = mm_t(e, w_down[here, :])
            dz_ref[:, here] = (slope_ref[:, here].astype(F32) * d_inner).astype(BF)
        late.wait()
        for at in range(0, D, CHUNK):
            out = mm_t(dz_ref[...], w_up[at : at + CHUNK, :])
            part_ref[:, at : at + CHUNK] = out.astype(BF)

    return run(
        body,
        [
            shaped((length, D)),
            shaped((length, D), F32),
            shaped((length, D)),
            shaped((length, 2 * D)),
            shaped((2, D), F32),
            shaped((QUARTER, length)),
            shaped((QUARTER, length)),
        ],
        vmem=[hidden, mine, other, norms, nums, cot, slope],
        hbm=weights,
        scratch=[
            pltpu.VMEM((D, 2 * D), BF),
            pltpu.VMEM((2 * D, D), BF),
            pltpu.VMEM((4, length, QUARTER), BF),
            pltpu.SemaphoreType.DMA((UP_COPIES,)),
        ],
        copies=DOWN_COPIES,
        micros=10,
    )


def step_back(d_ref, hidden_ref, mine_ref, other_ref, gain):
    unit, inverse = norm(hidden_ref[...].astype(F32))
    grad = mine_ref[...].astype(F32) + other_ref[...].astype(F32)
    part, terms = norm_back(grad, unit, inverse, gain)
    return d_ref[...] + part, terms


def cross_backward(
    d, hidden, mine, other, norms, nums, kv, kvt, q, qt, ot, lse, weights, after=()
):
    length = hidden.shape[0]
    frames = kv.shape[0]

    def body(
        d_ref, hidden_ref, mine_ref, other_ref, norms_ref, nums_ref, kv_ref, kvt_ref, q_ref,
        qt_ref, ot_ref, lse_ref, *refs
    ):
        w_refs, refs = refs[: len(weights)], refs[len(weights) :]
        part_ref, d_out_ref, e_ref, dq_ref, dkv_ref, terms_ref = refs[:6]
        w_q, w_out, keys, values, queries, grads, dot_t, dk_h, dv_h, dqt, sems = refs[6:]
        _, xy, _ = where_am_i()
        copies = Copies(sems)
        load_wide(copies, w_refs, 1, 1, xy, w_q, HALF)
        load_out(copies, w_refs, 1, xy, w_out)
        d2, terms = step_back(d_ref, hidden_ref, mine_ref, other_ref, norms_ref[2:3])
        d_out_ref[...] = d2
        terms_ref[...] = terms
        e = d2.astype(BF)
        e_ref[...] = e
        frame = lax.broadcasted_iota(jnp.int32, (frames, HEAD_DIM), 0).astype(F32)
        lane = lax.broadcasted_iota(jnp.int32, (frames, HEAD_DIM), 1)
        mask = jnp.where(frame < nums_ref[1:2, 0:1], 0.0, -1e30)
        beside = jnp.where(lane == 0, mask, jnp.where(lane < 4, 1.0, 0.0)).astype(BF)
        three = widened(3)(frames)
        for h in range(HEADS):
            lanes = slice(h * HEAD_DIM, (h + 1) * HEAD_DIM)
            keys[h] = jnp.concatenate([kv_ref[:, lanes], beside], axis=1)
            value = kv_ref[:, HALF + h * HEAD_DIM : HALF + (h + 1) * HEAD_DIM]
            values[h] = jnp.concatenate([value, three], axis=1)
            queries[h] = q_ref[:, lanes]
        copies.wait()
        d_mixed = project_t(e, w_out).astype(BF)
        dot_t[...] = d_mixed.T
        for h in range(HEADS):
            grads[h] = d_mixed[:, h * HEAD_DIM : (h + 1) * HEAD_DIM]
        ones = jnp.ones((1, length), F32)

        def head(h, carry):
            rows = head_rows(h)
            do_t = dot_t[rows, :]
            q_n, do_n = queries[h], grads[h]
            delta = jnp.sum(do_t.astype(F32) * ot_ref[rows, :].astype(F32), axis=0, keepdims=True)
            q_t = below(qt_ref[rows, :], [ones] + low_parts(-lse_ref[h]))
            do_t = below(do_t, low_parts(-delta))
            total = None
            for at in range(0, frames, CHUNK):
                here = slice(at, at + CHUNK)
                p = jnp.exp(mm(keys[h, here], q_t))
                ds = (p * mm(values[h, here], do_t)).astype(BF)
                dv_h[h, here] = mm(p.astype(BF), do_n).astype(BF)
                dk_h[h, here] = mm(ds, q_n).astype(BF)
                more = mm(kvt_ref[rows, here], ds)
                total = more if total is None else total + more
            dqt[rows, :] = (total * HEAD_DIM ** (-0.5)).astype(BF)
            return carry

        lax.fori_loop(0, HEADS, head, 0)
        dq = dqt[...].T
        dq_ref[...] = dq
        part_ref[...] = mm_t(dq, w_q[...]).astype(BF)
        for h in range(HEADS):
            lanes = slice(h * HEAD_DIM, (h + 1) * HEAD_DIM)
            dkv_ref[:, lanes] = dk_h[h]
            dkv_ref[:, HALF + h * HEAD_DIM : HALF + (h + 1) * HEAD_DIM] = dv_h[h]

    return run(
        body,
        [
            shaped((length, D)),
            shaped((length, D), F32),
            shaped((length, D)),
            shaped((length, HALF)),
            shaped((frames, D)),
            shaped((2, D), F32),
        ],
        vmem=[d, hidden, mine, other, norms, nums, kv, kvt, q, qt, ot, lse],
        hbm=weights,
        scratch=[
            pltpu.VMEM((D, HALF), BF),
            pltpu.VMEM((2, HALF, HALF), BF),
            pltpu.VMEM((HEADS, frames, 2 * HEAD_DIM), BF),
            pltpu.VMEM((HEADS, frames, 2 * HEAD_DIM), BF),
            pltpu.VMEM((HEADS, length, HEAD_DIM), BF),
            pltpu.VMEM((HEADS, length, HEAD_DIM), BF),
            pltpu.VMEM((HALF, length), BF),
            pltpu.VMEM((HEADS, frames, HEAD_DIM), BF),
            pltpu.VMEM((HEADS, frames, HEAD_DIM), BF),
            pltpu.VMEM((HALF, length), BF),
        ],
        copies=4 + 16,
        micros=22,
        after=after,
    )


def self_backward(d, hidden, mine, other, norms, nums, qkv, qt, kt, ot, lse, weights, after=()):
    length = hidden.shape[0]

    def body(
        d_ref, hidden_ref, mine_ref, other_ref, norms_ref, nums_ref, qkv_ref, qt_ref, kt_ref,
        ot_ref, lse_ref, *refs
    ):
        w_refs, refs = refs[: len(weights)], refs[len(weights) :]
        part_ref, d_out_ref, e_ref, dqk_ref, dv_ref, terms_ref = refs[:6]
        w_qk, w_v, w_out, queries_h, keys, values, grads, dot_t, dk_h, dv_h, dqt, bias, sems = refs[6:]
        _, xy, _ = where_am_i()
        copies = Copies(sems)
        load_out(copies, w_refs, 0, xy, w_out)
        load_wide(copies, w_refs, 0, 0, xy, w_qk)
        load_wide(copies, w_refs, 0, 1, xy, w_v, HALF)
        d1, terms = step_back(d_ref, hidden_ref, mine_ref, other_ref, norms_ref[1:2])
        d_out_ref[...] = d1
        terms_ref[...] = terms
        e = d1.astype(BF)
        e_ref[...] = e
        places = lax.broadcasted_iota(jnp.int32, (length, length), 0)
        queries = lax.broadcasted_iota(jnp.int32, (length, length), 1)
        allowed = (places <= queries) & (places.astype(F32) < nums_ref[0:1, 0:1])
        bias[...] = jnp.where(allowed, 0.0, -1e30)
        three = widened(3)(length)
        for h in range(HEADS):
            at = h * HEAD_DIM
            queries_h[h] = qkv_ref[:, at : at + HEAD_DIM]
            key = qkv_ref[:, HALF + at : HALF + at + HEAD_DIM]
            keys[h] = jnp.concatenate([key, three], axis=1)
            value = qkv_ref[:, 2 * HALF + at : 2 * HALF + at + HEAD_DIM]
            values[h] = jnp.concatenate([value, three], axis=1)
        copies.wait()
        d_mixed = project_t(e, w_out).astype(BF)
        dot_t[...] = d_mixed.T
        for h in range(HEADS):
            grads[h] = d_mixed[:, h * HEAD_DIM : (h + 1) * HEAD_DIM]

        def head(h, carry):
            rows = head_rows(h)
            do_t, do_n = dot_t[rows, :], grads[h]
            delta = jnp.sum(do_t.astype(F32) * ot_ref[rows, :].astype(F32), axis=0, keepdims=True)
            q_t = below(qt_ref[rows, :], low_parts(-lse_ref[h]))
            do_t = below(do_t, low_parts(-delta))
            p = jnp.exp(mm(keys[h], q_t) + bias[...])
            ds = (p * mm(values[h], do_t)).astype(BF)
            dv_h[h] = mm(p.astype(BF), do_n).astype(BF)
            dk_h[h] = mm(ds, queries_h[h]).astype(BF)
            dqt[rows, :] = (mm(kt_ref[rows, :], ds) * HEAD_DIM ** (-0.5)).astype(BF)
            return carry

        lax.fori_loop(0, HEADS, head, 0)
        dqk_ref[:, 0:HALF] = dqt[...].T
        for h in range(HEADS):
            lanes = slice(HALF + h * HEAD_DIM, HALF + (h + 1) * HEAD_DIM)
            dqk_ref[:, lanes] = dk_h[h]
            dv_ref[:, h * HEAD_DIM : (h + 1) * HEAD_DIM] = dv_h[h]
        out = mm_t(dqk_ref[...], w_qk[...]) + mm_t(dv_ref[...], w_v[...])
        part_ref[...] = out.astype(BF)

    return run(
        body,
        [
            shaped((length, D)),
            shaped((length, D), F32),
            shaped((length, D)),
            shaped((length, D)),
            shaped((length, HALF)),
            shaped((2, D), F32),
        ],
        vmem=[d, hidden, mine, other, norms, nums, qkv, qt, kt, ot, lse],
        hbm=weights,
        scratch=[
            pltpu.VMEM((D, D), BF),
            pltpu.VMEM((D, HALF), BF),
            pltpu.VMEM((2, HALF, HALF), BF),
            pltpu.VMEM((HEADS, length, HEAD_DIM), BF),
            pltpu.VMEM((HEADS, length, 2 * HEAD_DIM), BF),
            pltpu.VMEM((HEADS, length, 2 * HEAD_DIM), BF),
            pltpu.VMEM((HEADS, length, HEAD_DIM), BF),
            pltpu.VMEM((HALF, length), BF),
            pltpu.VMEM((HEADS, length, HEAD_DIM), BF),
            pltpu.VMEM((HEADS, length, HEAD_DIM), BF),
            pltpu.VMEM((HALF, length), BF),
            pltpu.VMEM((length, length), F32),
        ],
        copies=ATTENTION_COPIES,
        micros=12,
        staged=True,
        after=after,
    )


def finish_hidden(d, hidden, mine, other, norms, terms1, terms2, terms3, after=()):
    length = hidden.shape[0]

    def body(
        d_ref, hidden_ref, mine_ref, other_ref, norms_ref, one, two, three, terms_ref, first_ref,
        second_ref, blocks
    ):
        d0, terms = step_back(d_ref, hidden_ref, mine_ref, other_ref, norms_ref[0:1])
        store_blocks(d0.astype(BF), blocks, first_ref, second_ref)
        for j in range(2):
            here = slice(j, j + 1)
            terms_ref[4 * j : 4 * j + 4] = jnp.concatenate(
                [terms[here], one[here], two[here], three[here]], axis=0
            )

    return run(
        body,
        [shaped((8, D), F32), shaped((QUARTER, length)), shaped((QUARTER, length))],
        vmem=[d, hidden, mine, other, norms, terms1, terms2, terms3],
        scratch=[pltpu.VMEM((4, length, QUARTER), BF)],
        micros=4,
        after=after,
    )


def finish_encoder(keep, other, frames, after=()):
    def body(keep_ref, other_ref, first_ref, second_ref):
        _, _, z = where_am_i()
        for ref, k in ((first_ref, 0), (second_ref, 1)):
            here = pl.ds(pl.multiple_of(((z + k) % 2) * QUARTER, QUARTER), QUARTER)
            total = keep_ref[here, :].astype(F32) + other_ref[here, :].astype(F32)
            ref[...] = total.astype(BF)[:, :frames]

    return run(
        body,
        [shaped((QUARTER, frames)), shaped((QUARTER, frames))],
        vmem=[keep, other],
        micros=2,
        after=after,
    )


def block_plan(place):
    if not place.fast:
        return 1, (((1, 0, 0),), ((1, 0, 0),))
    first = ((1, 0, 0), (0, 0, 1), (1, 1, 2), (0, 1, 3))
    second = ((1, 0, 0), (1, 1, 1), (0, 0, 2), (0, 1, 3))
    return 4, (first, second)


def grad_outputs(place, shape):
    if place.fast:
        return [shaped((2,) + shape)] * 4
    return [shaped((1,) + shape)] * 4


def units_grads(place, mt, dz, it, e):
    chips = place.chips
    rows = D // (2 * chips)
    _, plan = block_plan(place)

    def body(mt_ref, dz_ref, it_ref, e_ref, *outs):
        _, xy, _ = where_am_i()
        for output, slot, offset in plan[1]:
            chip = xy ^ offset
            for z in range(4):
                here = pl.ds(pl.multiple_of(z * HALF + chip * rows, 16), rows)
                outs[2 + output][slot, z] = mm(it_ref[here, :], e_ref[...]).astype(BF)
        for output, slot, offset in plan[0]:
            here = pl.ds(pl.multiple_of((xy ^ offset) * 2 * rows, 16), 2 * rows)
            left = mm(mt_ref[here, :], dz_ref[...]).astype(BF)
            for z in range(4):
                outs[output][slot, z] = left[:, z * HALF : (z + 1) * HALF]

    def plain(mt_ref, dz_ref, it_ref, e_ref, left_ref, right_ref):
        left_ref[...] = mm(mt_ref[...], dz_ref[...]).astype(BF)
        right_ref[...] = mm(it_ref[...], e_ref[...]).astype(BF)

    if place.fast:
        first, second = shaped((2, 4, 2 * rows, HALF)), shaped((2, 4, rows, D))
        return run(
            body, [first, first, second, second], vmem=[mt, dz, it, e], micros=6
        )
    left, right = run(
        plain, [shaped((D, 2 * D)), shaped((2 * D, D))], vmem=[mt, dz, it, e], micros=7
    )
    left = left.reshape(chips, 2 * rows, 4, HALF).transpose(0, 2, 1, 3)
    right = right.reshape(4, chips, rows, 2, HALF).transpose(1, 0, 3, 2, 4)
    whole = jnp.concatenate([left, right.reshape(chips, 4, 2 * rows, HALF)], axis=-1)
    return whole.reshape(4 * chips, 2 * rows, D)


def units_sum(grads, came, onward, after):
    rows = grads[3].shape[2]

    def body(*refs):
        ins, (kept_ref, sent_ref, left, right, blocks, sems) = refs[:6], refs[6:]
        _, _, mp = where_am_i()
        copies = Copies(sems)
        for i, ref in enumerate(ins):
            target = (left if i < 3 else right).at[i % 3]
            copies.start(ref if i % 3 == 2 else ref.at[0], target)
        copies.wait()
        for z in range(4):
            blocks[z, :, 0:HALF] = add_up(*[left[i, z] for i in range(3)]).astype(BF)
            down = add_up(*[right[i, z] for i in range(3)]).astype(BF)
            blocks[z, 0:rows, HALF:D] = down[:, :HALF]
            blocks[z, rows : 2 * rows, HALF:D] = down[:, HALF:]
        for i in range(2):
            kept_ref[i] = blocks[mp ^ (2 * i)]
            sent_ref[i] = blocks[mp ^ (2 * i + 1)]

    return run(
        body,
        [shaped((2, 2 * rows, D)), shaped((2, 2 * rows, D))],
        hbm=[grads[1], came[0], onward[0], grads[3], came[1], onward[1]],
        scratch=[
            pltpu.VMEM((3, 4, 2 * rows, HALF), BF),
            pltpu.VMEM((3, 4, rows, D), BF),
            pltpu.VMEM((4, 2 * rows, D), BF),
        ],
        copies=6,
        micros=3,
        after=after,
    )


def add_second(kept, came, after):
    def body(kept_ref, came_ref, out_ref, held, sems):
        copies = Copies(sems)
        copies.start(kept_ref.at[1], held.at[0])
        copies.start(came_ref.at[1], held.at[1])
        copies.wait()
        out_ref[...] = add_up(held[0], held[1]).astype(BF)

    shape = kept.shape[1:]
    return run(
        body,
        [shaped(shape)],
        hbm=[kept, came],
        scratch=[pltpu.VMEM((2,) + shape, BF)],
        copies=2,
        micros=1,
        after=after,
    )[0]


def cut_units(kept, came, last, after):
    rows = last.shape[0] // 2

    def body(kept_ref, came_ref, last_ref, mine_ref, sent_ref, down_ref, held, sems):
        core, _, _ = where_am_i()
        copies = Copies(sems)
        copies.start(kept_ref.at[0], held.at[0])
        copies.start(came_ref.at[0], held.at[1])
        copies.start(last_ref, held.at[2])
        copies.wait()
        mine = pl.ds(pl.multiple_of(core * rows, 16), rows)
        theirs = pl.ds(pl.multiple_of((1 - core) * rows, 16), rows)
        mine_ref[...] = add_up(*[held[i, mine, 0:HALF] for i in range(3)]).astype(BF)
        sent_ref[...] = add_up(*[held[i, theirs, 0:HALF] for i in range(3)]).astype(BF)
        down_ref[:, 0:HALF] = add_up(*[held[i, 0:rows, HALF:D] for i in range(3)])
        down_ref[:, HALF:D] = add_up(*[held[i, rows : 2 * rows, HALF:D] for i in range(3)])

    return run(
        body,
        [shaped((rows, HALF)), shaped((rows, HALF)), shaped((rows, D), F32)],
        hbm=[kept, came, last],
        scratch=[pltpu.VMEM((3, 2 * rows, D), BF)],
        copies=3,
        micros=1,
        after=after,
    )


def join_units(place, kept, came):
    rows = kept.shape[0]

    def body(kept_ref, came_ref, up_ref, both):
        core, _, _ = where_am_i()
        both[core] = kept_ref[...]
        both[1 - core] = came_ref[...]
        blocks = []
        for chip in range(place.chips):
            for parity in range(2):
                blocks.append(both[parity, :, chip * rows : (chip + 1) * rows].astype(F32))
        up_ref[...] = jnp.concatenate(blocks, axis=1)

    return run(
        body,
        [shaped((rows, D), F32)],
        vmem=[kept, came],
        scratch=[pltpu.VMEM((2, rows, HALF), BF)],
        micros=1,
    )[0]


def attention_grads(place, wide_left, wide_right, left, right, ot, e, after=()):
    count, plan = block_plan(place)
    rows = D // count
    few = rows // 4

    def body(wide_left_ref, wide_right_ref, left_ref, right_ref, ot_ref, e_ref, *outs):
        _, xy, _ = where_am_i()
        for output, slot, offset in plan[0]:
            chip = xy ^ offset if count > 1 else 0
            here = pl.ds(pl.multiple_of(chip * rows, 16), rows)
            outs[output][slot] = mm(wide_left_ref[here, :], wide_right_ref[...]).astype(BF)
        for output, slot, offset in plan[1]:
            chip = xy ^ offset if count > 1 else 0
            here = pl.ds(pl.multiple_of(chip * rows, 16), rows)
            target = outs[2 + output]
            target[slot, :, 0:HALF] = mm(left_ref[here, :], right_ref[...]).astype(BF)
            for hi in range(2):
                here = pl.ds(pl.multiple_of(hi * QUARTER + chip * few, 16), few)
                both = mm(ot_ref[here, :], e_ref[...]).astype(BF)
                for q in range(2):
                    at = (2 * q + hi) * few
                    target[slot, at : at + few, HALF:D] = both[:, q * HALF : (q + 1) * HALF]

    return run(
        body,
        grad_outputs(place, (rows, D)),
        vmem=[wide_left, wide_right, left, right, ot, e],
        micros=6,
        after=after,
    )


def encoder_grad(dkv, weights, after=()):
    padded = dkv.shape[0]

    def body(dkv_ref, *refs):
        w_refs, (keep_ref, send_ref, w_kv, sems) = refs[: len(weights)], refs[len(weights) :]
        core, xy, _ = where_am_i()
        copies = Copies(sems)
        load_wide(copies, w_refs, 1, 0, xy, w_kv)
        copies.wait()
        mine = pl.ds(pl.multiple_of(core * HALF, HALF), HALF)
        theirs = pl.ds(pl.multiple_of((1 - core) * HALF, HALF), HALF)
        for ref, rows in ((send_ref, theirs), (keep_ref, mine)):
            for at in range(0, padded, CHUNK):
                value = mm_t(w_kv[rows, :], dkv_ref[at : at + CHUNK, :])
                ref[:, at : at + CHUNK] = value.astype(BF)

    return run(
        body,
        [shaped((HALF, padded)), shaped((HALF, padded))],
        vmem=[dkv],
        hbm=weights,
        scratch=[pltpu.VMEM((D, D), BF)],
        copies=4,
        micros=3.5,
        after=after,
    )


def leave_plane(place, grads):
    return [place.swap_xy(grads[0], 1), place.swap_xy(grads[2], 2)]


def pass_on(grads, came, after):
    shapes = [grads[1].shape[1:], grads[3].shape[1:]]

    def body(stay0, came0, stay1, came1, out0, out1, held0, held1, sems):
        copies = Copies(sems)
        for i, ref in enumerate((stay0, came0, stay1, came1)):
            copies.start(ref.at[1], (held0 if i < 2 else held1).at[i % 2])
        copies.wait()
        out0[...] = add_up(held0[0], held0[1]).astype(BF)
        out1[...] = add_up(held1[0], held1[1]).astype(BF)

    return run(
        body,
        [shaped(shape) for shape in shapes],
        hbm=[grads[1], came[0], grads[3], came[1]],
        scratch=[pltpu.VMEM((2,) + shape, BF) for shape in shapes],
        copies=4,
        micros=1,
        after=after,
    )


def cross_plane(place, onward):
    return [place.swap_xy(onward[0], 2), place.swap_xy(onward[1], 1)]


def column_blocks(grads, came, onward, norm_terms=(), after=()):
    shape = onward[0].shape
    rows = shape[-2] // 2
    width = D
    few = rows // 4
    extra = 16 if norm_terms else 0

    def body(*refs):
        terms_refs, refs = refs[: len(norm_terms)], refs[len(norm_terms) :]
        ins, outs, (held, shards, sems) = refs[:6], refs[6:-3], refs[-3:]
        home, slots = column_slots()
        copies = Copies(sems)
        for i, ref in enumerate(ins):
            copies.start(ref if i % 3 == 2 else ref.at[0], held.at[i])
        copies.wait()
        sums = [add_up(held[3 * part], held[3 * part + 1], held[3 * part + 2]) for part in range(2)]
        for hi in range(2):
            for cs in range(2):
                here = slice(cs * rows, (cs + 1) * rows)
                lanes = slice(hi * QUARTER, (hi + 1) * QUARTER)
                lanes_two = slice(HALF + hi * QUARTER, HALF + (hi + 1) * QUARTER)
                outs_rows = []
                for p in range(4):
                    at = (2 * (p // 2) + hi) * 2 * few + cs * few
                    side = HALF + (p % 2) * QUARTER
                    outs_rows.append(sums[1][at : at + few, side : side + QUARTER])
                value = jnp.concatenate(
                    [
                        sums[0][here, lanes],
                        sums[0][here, lanes_two],
                        sums[1][here, lanes],
                        jnp.concatenate(outs_rows, axis=0),
                    ],
                    axis=1,
                )
                shards[2 * hi + cs, :rows] = value.astype(BF)
        if norm_terms:
            core, xy, _ = where_am_i()
            terms = add_up(*[ref[...] for ref in terms_refs])
            terms = jnp.concatenate([terms, jnp.zeros_like(terms)], axis=0).astype(BF)
            feature = lax.broadcasted_iota(jnp.int32, (D, D), 0)
            lane = lax.broadcasted_iota(jnp.int32, (D, D), 1)
            for hi in range(2):
                for cs in range(2):
                    offset = (2 * core + hi) * QUARTER + (2 * xy + cs) * few
                    pick = jnp.where((feature == lane + offset) & (lane < few), 1.0, 0.0)
                    shards[2 * hi + cs, rows:] = mm(terms, pick.astype(BF)).astype(BF)
        for k in range(4):
            outs[k][...] = shards[slots[k]]

    ins = [grads[1], came[0], onward[0], grads[3], came[1], onward[1]]
    return run(
        body,
        [shaped((rows + extra, width))] * 4,
        vmem=list(norm_terms),
        hbm=ins,
        after=after,
        scratch=[pltpu.VMEM((6,) + shape, BF), pltpu.VMEM((4, rows + extra, width), BF)],
        copies=6,
        micros=2,
    )


def sum_plain(place, grads, attention):
    wide, narrow = grads[1][0], grads[3][0]
    rows = D // place.dp
    if attention:
        value = jnp.stack([wide[:, :HALF], wide[:, HALF:], narrow[:, :HALF]], axis=1)
        value = value.reshape(place.dp, rows, 3, 2, QUARTER).transpose(3, 0, 1, 2, 4)
        value = value.reshape(2, place.dp, rows, 3 * QUARTER)
        outs = narrow[:, HALF:].reshape(2, 2, place.dp, rows // 4, 2, QUARTER)
        outs = outs.transpose(1, 2, 0, 4, 3, 5).reshape(2, place.dp, rows, QUARTER)
        value = jnp.concatenate([value, outs], axis=-1)
    else:
        value = jnp.concatenate(
            [wide.reshape(2, place.dp, rows, D), narrow.reshape(2, place.dp, rows, D)], axis=-1
        )
    whole = jnp.zeros((2,) + value.shape, F32)
    whole = lax.dynamic_update_index_in_dim(whole, value.astype(F32), place.core, 0)
    whole = whole.reshape((4 * place.dp,) + value.shape[2:])
    return lax.psum_scatter(whole, ("mp", "xy", "core"), scatter_dimension=0, tiled=False)


def attention_outputs(sums, rows, few):
    value = sums[:rows]
    last = value[:, 3 * QUARTER :]
    out = jnp.concatenate([last[p * few : (p + 1) * few] for p in range(4)], axis=1)
    return [value[:, j * QUARTER : (j + 1) * QUARTER] for j in range(3)], out


def finish_self(got, own, few_lanes):
    rows = own.shape[0] - 16
    few = rows // 4

    def body(a, b, c, d, own_ref, qkv_ref, out_ref, gain_ref, bias_ref):
        home, _ = column_slots()
        last = jnp.where(home, own_ref[...].astype(F32), d[...].astype(F32))
        sums = add_up(a[...], b[...], c[...], last)
        blocks, out = attention_outputs(sums, rows, few)
        for j in range(3):
            qkv_ref[j] = blocks[j]
        out_ref[...] = out
        gain_ref[...] = sums[rows : rows + 4, :few_lanes]
        bias_ref[...] = sums[rows + 4 : rows + 8, :few_lanes]

    return run(
        body,
        [
            shaped((3, rows, QUARTER), F32),
            shaped((few, D), F32),
            shaped((4, few_lanes), F32),
            shaped((4, few_lanes), F32),
        ],
        vmem=list(got) + [own],
        micros=1.5,
    )


def finish_cross(got, own, after=()):
    rows = own.shape[0]
    few = rows // 4

    def body(a, b, c, d, own_ref, kv_ref, q_ref, out_ref):
        home, _ = column_slots()
        last = jnp.where(home, own_ref[...].astype(F32), d[...].astype(F32))
        blocks, out = attention_outputs(add_up(a[...], b[...], c[...], last), rows, few)
        kv_ref[...] = jnp.concatenate(blocks[:2], axis=1)
        q_ref[...] = blocks[2]
        out_ref[...] = out

    return run(
        body,
        [shaped((rows, HALF), F32), shaped((rows, QUARTER), F32), shaped((few, D), F32)],
        vmem=list(got) + [own],
        micros=1.5,
        after=after,
    )


def join_rows(blocks, got, dtype, after=()):
    width, rows = blocks[0].shape

    def body(block_ref, first_ref, second_ref, out_ref):
        home, _ = column_slots()
        _, _, z = where_am_i()

        @pl.when(home)
        def _():
            out_ref[z % 2] = block_ref[...].astype(dtype)

        @pl.when(jnp.logical_not(home))
        def _():
            out_ref[z % 2] = first_ref[...].astype(dtype)

        out_ref[(z + 1) % 2] = second_ref[...].astype(dtype)

    joined = run(
        body,
        [shaped((2, width, rows), dtype)],
        vmem=[blocks[0]] + list(got),
        micros=2,
        after=after,
    )[0]
    return joined[:, None].transpose(0, 1, 3, 2)


def from_quarters(value):
    few = value.shape[0] // 4
    return value.reshape(4, few, QUARTER).transpose(1, 0, 2).reshape(few, D)


def three_parts(value):
    terms = []
    for _ in range(3):
        term = lax.reduce_precision(value, 8, 7)
        terms.append(term.astype(BF))
        value = value - term
    return jnp.concatenate(terms)


def per_device(
    dp,
    mp,
    hidden_in,
    encoder_states,
    cotangent,
    self_qkv,
    self_out,
    cross_q,
    cross_kv,
    cross_out,
    fc_in,
    fc_out,
    ln_gain,
    ln_bias,
    token_lengths,
    audio_lengths,
    corpus_ids,
    corpus_weights,
):
    place = Place(dp, mp)
    length = hidden_in.shape[2]
    frames = encoder_states.shape[2]
    padded = -(-frames // CHUNK) * CHUNK
    rows = self_qkv.shape[0]

    encoded = lax.dynamic_index_in_dim(encoder_states[:, 0], place.micro, 0, keepdims=False)
    first = ()
    if place.fast:
        shard = attention_shard(self_qkv, self_out, cross_kv, cross_q, cross_out)
        packed = pack_attention(place.column_out(shard), shard, (encoded,))
        w_self = w_cross = spread(place, packed)
        first = (shard,)
    else:
        quarter = lambda w: w.reshape(-1, 4, QUARTER).transpose(1, 0, 2).reshape(-1, QUARTER)
        flat = lambda w: w.reshape(rows, -1)
        w_self = attention_plain(
            place, jnp.concatenate([flat(self_qkv), quarter(self_out)], axis=1)
        )
        w_cross = attention_plain(
            place, jnp.concatenate([flat(cross_kv), cross_q, quarter(cross_out)], axis=1)
        )


    unit = unit_shard(place, fc_in, fc_out)
    if not place.fast:
        w_units = gather_units(place, unit)

    if place.fast:
        unit, packed = lax.optimization_barrier((unit, packed))
        column = [unit] + [place.swap_z(unit, k) for k in (1, 2, 3)]
        first = tuple(column[1:])

    turned = lambda value: value[:, 0].transpose(0, 2, 1)
    numbers = jnp.concatenate([token_lengths.T, audio_lengths.T, corpus_ids.T])
    blocks = input_blocks(
        turned(hidden_in),
        three_parts(jnp.concatenate([ln_gain, ln_bias])),
        numbers,
        first,
    )
    got = place.rows_in(blocks)
    if place.fast:
        stacked = stack_units(column, tuple(w_self[3:5]))
        w_units = spread(place, stacked)
    hidden, norms, nums = prepare(got, place.swap_core(got), corpus_weights)

    other = place.move(encoded, lambda xy, core, z: (xy, 1 - core, z) if core == z // 2 else None)
    encoded = jnp.where(place.home == place.core, encoded, other)
    encoded = jnp.pad(encoded, ((0, padded - frames), (0, 0)))

    et = turn(encoded)
    part1, at, qkv, qt, kt, ot1, lse1 = self_forward(hidden, norms, nums, w_self, (et,))
    other1 = place.swap_core(part1)
    got = place.rows_in(turned_blocks(turned(cotangent), (at,)))
    kv, kvt = cross_memory(encoded, w_cross)
    part2, h1, ct, q2, qt2, ot2, lse2 = cross_forward(
        hidden, part1, other1, norms, nums, kv, kvt, w_cross
    )
    other2 = place.swap_core(part2)
    cot = prepare_cotangent(got, place.swap_core(got), (part2,))
    part3, h2, mt, slope, it = units_forward(h1, part2, other2, norms, w_units)
    other3 = place.swap_core(part3)
    part, d3, e3, dz, terms3, out_a, out_b = units_backward(
        h2, part3, other3, norms, nums, cot, slope, w_units
    )
    other = place.swap_core(part)
    g_units = units_grads(place, mt, dz, it, e3)
    came_units = leave_plane(place, g_units) if place.fast else None
    layer_got = place.rows_sent((out_a, out_b))
    layer_out = place.rows_joined((out_a, out_b), layer_got)
    part, d2, e2, dq2, dkv, terms2 = cross_backward(
        d3, h2, part, other, norms, nums, kv, kvt, q2, qt2, ot2, lse2, w_cross, layer_got
    )
    other = place.swap_core(part)
    passed = pass_on(g_units, came_units, (dq2,)) if place.fast else ()
    keep, send = encoder_grad(dkv, w_cross, passed)
    g_cross = attention_grads(place, et, dkv, ct, dq2, ot2, e2, (keep,))
    held = (g_cross[0],)
    if place.fast:
        came_cross = leave_plane(place, g_cross)
        onward_units = cross_plane(place, passed)
        kept, sent = units_sum(g_units, came_units, onward_units, held)
        came_units = place.swap_z(sent, 1)
        held = (kept,)
    encoder_blocks = finish_encoder(keep, place.swap_core(send), frames, held)
    encoder_got = place.rows_sent(encoder_blocks)
    held = encoder_blocks
    part, d1, e1, dqk, dv, terms1 = self_backward(
        d2, h1, part, other, norms, nums, qkv, qt, kt, ot1, lse1, w_self, held
    )
    other = place.swap_core(part)
    held = ()
    if place.fast:
        held = pass_on(g_cross, came_cross, (e1, came_units))
        onward_cross = cross_plane(place, held)
    g_self = attention_grads(place, at, dqk, at, dv, ot1, e1, held)
    terms, out_a, out_b = finish_hidden(
        d1, hidden, part, other, norms, terms1, terms2, terms3, (g_self[0],)
    )
    hidden_got = place.rows_sent((out_a, out_b))
    if place.fast:
        came_self = leave_plane(place, g_self)
        second = add_second(kept, came_units, (terms,))
        last_units = place.swap_z(second, 2)
        cross_blocks = column_blocks(g_cross, came_cross, onward_cross, (), (second,))
        cross_got = place.column_back(cross_blocks)

    few = D // (place.dp * place.mp)
    if place.fast:
        passed = pass_on(g_self, came_self, (cross_blocks[0],))
        onward_self = cross_plane(place, passed)
        grad_encoder = join_rows(encoder_blocks, encoder_got, F32, passed)
        mine, sent, s_down = cut_units(kept, came_units, last_units, passed)
        s_up = join_units(place, mine, place.swap_core(sent))
        terms = terms + place.swap_xy(terms, 1)
        blocks = column_blocks(
            g_self, came_self, onward_self, (terms, place.swap_xy(terms, 2)), (s_down,)
        )
        g_qkv, g_out, g_gain, g_bias = finish_self(place.column_back(blocks), blocks[3], few)
        g_ckv, g_cq, g_cout = finish_cross(cross_got, cross_blocks[3], (blocks[0],))
        grad_hidden = join_rows((out_a, out_b), hidden_got, F32, (blocks[0],))
        g_qkv = g_qkv.transpose(1, 0, 2)
    else:
        s_up, s_down = scatter_units(place, g_units)
        grad_encoder = place.rows_joined(encoder_blocks, encoder_got).astype(F32)
        grad_hidden = place.rows_joined((out_a, out_b), hidden_got).astype(F32)
        s_cross = sum_plain(place, g_cross, True)
        s_self = sum_plain(place, g_self, True)
        terms = jnp.where(place.core == 0, terms, 0.0)
        terms = lax.psum(terms, AXES)
        shares = lax.dynamic_slice_in_dim(terms, (place.z * place.dp + place.d) * few, few, 1)
        g_gain, g_bias = shares[:4], shares[4:]
        g_qkv, g_out = s_self[:, : 3 * QUARTER], from_quarters(s_self[:, 3 * QUARTER :])
        g_ckv, g_cq = s_cross[:, :HALF], s_cross[:, HALF : 3 * QUARTER]
        g_cout = from_quarters(s_cross[:, 3 * QUARTER :])
    return (
        layer_out,
        grad_hidden,
        grad_encoder,
        g_qkv.reshape(rows, 3, QUARTER),
        g_out,
        g_cq,
        g_ckv.reshape(rows, 2, QUARTER),
        g_cout,
        s_up,
        s_down,
        g_gain,
        g_bias,
    )


def solution(mesh):
    dp, mp = mesh.shape["dp"], mesh.shape["mp"]
    finer = Mesh(mesh.devices.reshape(dp // 2, 2, mp), AXES)
    both = ("xy", "core")
    rows = P(None, both, None, "mp")
    columns = P(both, None, "mp")
    pairs = P(both, "mp")
    units = P(("mp",) + both, None)
    each = P(None, both)
    return jax.shard_map(
        partial(per_device, dp, mp),
        mesh=finer,
        in_specs=(
            rows,
            P(None, both, None, None),
            rows,
            columns,
            units,
            pairs,
            columns,
            units,
            pairs,
            units,
            P(None, "mp"),
            P(None, "mp"),
            each,
            each,
            each,
            P(),
        ),
        out_specs=(
            rows,
            rows,
            rows,
            columns,
            units,
            pairs,
            columns,
            units,
            pairs,
            units,
            P(None, ("mp",) + both),
            P(None, ("mp",) + both),
        ),
        check_vma=False,
    )
```

```python
from functools import partial

import jax
import jax.numpy as jnp
from jax import lax
from jax.experimental import pallas as pl
from jax.experimental.pallas import tpu as pltpu
from jax.sharding import Mesh, PartitionSpec as P

D = 768
HALF = 384
QUARTER = 192
HEAD_DIM = 64
HEADS = 6
CHUNK = 256
BF = jnp.bfloat16
F32 = jnp.float32
AXES = ("xy", "core", "mp")
CHIPS = ("xy", "mp")
VMEM = pl.BlockSpec(memory_space=pltpu.VMEM)
SMEM = pl.BlockSpec(memory_space=pltpu.SMEM)
ANY = pl.BlockSpec(memory_space=pl.ANY)
HBM = pl.BlockSpec(memory_space=pltpu.HBM)


def mm(left, right):
    return jnp.dot(left, right, preferred_element_type=F32)


def mm_t(left, right):
    return lax.dot_general(left, right, (((1,), (1,)), ((), ())), preferred_element_type=F32)


def shaped(shape, dtype=BF):
    return jax.ShapeDtypeStruct(shape, dtype)


def room(shape, dtype):
    item = jnp.dtype(dtype).itemsize
    shape = (1, 1) + tuple(shape)
    tile = 32 // item
    size = item * (-(-shape[-1] // 128) * 128) * (-(-shape[-2] // tile) * tile)
    for extent in shape[:-2]:
        size *= extent
    return size


def run(
    body, outs, vmem=(), hbm=(), smem=(), scratch=(), copies=0, micros=2, after=(), staged=False
):
    args = tuple(smem) + tuple(vmem) + tuple(hbm)
    count = len(args)
    scratch = list(scratch)
    if copies:
        scratch.append(pltpu.SemaphoreType.DMA((copies,)))
    need = sum(room(a.shape, a.dtype) for a in tuple(vmem) + tuple(outs))
    need += sum(room(a.shape, a.dtype) for a in scratch if a.memory_space == pltpu.VMEM)
    need = min(need + 6 * 1024 * 1024, 60 * 1024 * 1024)
    moved = sum(a.size * a.dtype.itemsize for a in args) + sum(
        o.size * o.dtype.itemsize for o in outs
    )
    skip = len(scratch)
    if staged:
        scratch += [pltpu.VMEM(a.shape, a.dtype) for a in vmem]
        scratch.append(pltpu.SemaphoreType.DMA((len(vmem),)))

    def whole(*refs):
        ins, rest = list(refs[:count]), refs[count + len(after) :]
        if staged:
            held = rest[len(outs) + skip : -1]
            rest, sems = rest[: len(outs) + skip], rest[-1]
            copies = Copies(sems)
            for i, target in enumerate(held):
                copies.start(ins[len(smem) + i], target)
                ins[len(smem) + i] = target
            copies.wait()
        body(*ins, *rest)

    place = HBM if staged else VMEM
    return pl.pallas_call(
        whole,
        out_shape=tuple(outs),
        in_specs=[SMEM] * len(smem) + [place] * len(vmem) + [ANY] * (len(hbm) + len(after)),
        out_specs=(VMEM,) * len(outs),
        scratch_shapes=scratch,
        compiler_params=pltpu.CompilerParams(vmem_limit_bytes=need),
        cost_estimate=pl.CostEstimate(
            flops=int(micros * 1.15e9), bytes_accessed=moved, transcendentals=0
        ),
    )(*args, *after)


class Copies:
    def __init__(self, sems):
        self.sems, self.open = sems, []

    def start(self, source, target):
        copy = pltpu.make_async_copy(source, target, self.sems.at[len(self.open)])
        copy.start()
        self.open.append(copy)

    def wait(self):
        for copy in self.open:
            copy.wait()


def where_am_i():
    return lax.axis_index("core"), lax.axis_index("xy"), lax.axis_index("mp")


class Place:
    def __init__(self, dp, mp):
        self.dp, self.mp = dp, mp
        self.chips = dp // 2
        self.fast = self.chips == 4
        self.z = lax.axis_index("mp")
        self.core = lax.axis_index("core")
        self.xy = lax.axis_index("xy")
        self.d = 2 * self.xy + self.core
        self.micro = self.z % 2
        self.home = self.z // 2

    def move(self, value, route):
        pairs = []
        for xy in range(self.chips):
            for core in range(2):
                for z in range(self.mp):
                    target = route(xy, core, z)
                    if target is not None:
                        txy, tcore, tz = target
                        pairs.append(
                            ((2 * xy + core) * self.mp + z, (2 * txy + tcore) * self.mp + tz)
                        )
        return lax.ppermute(value, AXES, pairs)

    def swap_core(self, value):
        return self.move(value, lambda xy, core, z: (xy, 1 - core, z))

    def swap_xy(self, value, bit):
        return self.move(value, lambda xy, core, z: (xy ^ bit, core, z))

    def swap_z(self, value, bit):
        return self.move(value, lambda xy, core, z: (xy, core, z ^ bit))

    def column_routes(self):
        def route(step, xy, core, z):
            user, j = z // 2, z % 2
            home = core == user
            near = lambda i: (xy, user, 2 * user + i)
            far = lambda i: (xy, user, 2 * (1 - user) + i)
            if step == 0:
                return near(1 - j) if home else far(1 - j)
            if step == 1:
                return far(j) if home else near(j)
            if step == 2:
                return far(1 - j) if home else near(1 - j)
            return None if home else far(j)

        return [partial(route, step) for step in range(4)]

    def column_out(self, shard):
        return [self.move(shard, route) for route in self.column_routes()]

    def column_back(self, blocks):
        got = []
        for block, route in zip(blocks, self.column_routes()):
            turned = {}
            for xy in range(self.chips):
                for core in range(2):
                    for z in range(self.mp):
                        target = route(xy, core, z)
                        if target is not None:
                            turned[target] = (xy, core, z)
            got.append(self.move(block, lambda xy, core, z: turned.get((xy, core, z))))
        return got

    def rows_in(self, blocks):
        def route(k, xy, core, z):
            target = (xy, z // 2, 2 * core + (z + k) % 2)
            return None if target == (xy, core, z) else target

        got = [self.move(block, partial(route, k)) for k, block in enumerate(blocks)]
        return jnp.stack([jnp.where(self.core == self.home, blocks[0], got[0]), got[1]])

    def rows_home(self, blocks):
        return self.rows_joined(blocks, self.rows_sent(blocks))

    def rows_sent(self, blocks):
        def route(k, xy, core, z):
            target = (xy, z // 2, 2 * core + (z % 2 - k) % 2)
            return None if target == (xy, core, z) else target

        return [self.move(block, partial(route, k)) for k, block in enumerate(blocks)]

    def rows_joined(self, blocks, got):
        got = [jnp.where(self.core == self.home, blocks[0], got[0]), got[1]]
        even = self.z % 2 == 0
        both = jnp.stack([jnp.where(even, got[0], got[1]), jnp.where(even, got[1], got[0])])
        return both[:, None].transpose(0, 1, 3, 2)


def norm(hidden):
    center = jnp.mean(hidden, axis=-1, keepdims=True)
    spread = jnp.mean(hidden * hidden, axis=-1, keepdims=True) - center * center
    inverse = lax.rsqrt(spread + 1e-05)
    return (hidden - center) * inverse, inverse


def norm_back(grad, unit, inverse, gain):
    scaled = grad * gain
    first = jnp.mean(scaled, axis=-1, keepdims=True)
    second = jnp.mean(scaled * unit, axis=-1, keepdims=True)
    terms = jnp.concatenate(
        [jnp.sum(grad * unit, axis=0, keepdims=True), jnp.sum(grad, axis=0, keepdims=True)], axis=0
    )
    return inverse * (scaled - first - unit * second), terms


def add_up(*terms):
    total = terms[0].astype(F32)
    for term in terms[1:]:
        total = total + term.astype(F32)
    return total


def input_blocks(hidden, terms, numbers, after=()):
    _, width, length = hidden.shape
    total = width + 32

    def body(numbers_ref, hidden_ref, terms_ref, *outs):
        _, _, z = where_am_i()
        lanes = lax.broadcasted_iota(jnp.int32, (8, length), 1)
        for k in range(2):
            micro = (z + k) % 2
            outs[k][0:width] = hidden_ref[micro]
            tok, aud = numbers_ref[0, micro], numbers_ref[1, micro]
            row = jnp.where(lanes == 0, tok // 256, jnp.where(lanes == 1, tok % 256, 0))
            row = jnp.where(lanes == 2, aud // 256, jnp.where(lanes == 3, aud % 256, row))
            row = jnp.where(lanes == 4, numbers_ref[2, micro], row)
            wide = jnp.concatenate(
                [terms_ref[...].astype(F32), jnp.zeros((24, length - width), F32)], axis=1
            )
            outs[k][width:total] = jnp.concatenate([wide, row.astype(F32)], axis=0).astype(BF)

    return run(
        body,
        [shaped((total, length))] * 2,
        smem=[numbers],
        vmem=[hidden, terms],
        micros=1,
        after=after,
    )


def turned_blocks(value, after=()):
    _, width, length = value.shape

    def body(ref, first_ref, second_ref):
        _, _, z = where_am_i()
        first_ref[...] = ref[z % 2]
        second_ref[...] = ref[(z + 1) % 2]

    return run(body, [shaped((width, length))] * 2, vmem=[value], micros=1, after=after)


def bring_blocks(copies, own_ref, other_ref, wide):
    core, _, z = where_am_i()
    found = []
    for k in range(2):
        slot = (z % 2 + k) % 2
        for ref, user in ((own_ref, core), (other_ref, 1 - core)):
            block = 2 * user + slot
            here = pl.ds(pl.multiple_of(block * QUARTER, QUARTER), QUARTER)
            copies.start(ref.at[k, pl.ds(0, QUARTER)], wide.at[here])
            found.append((ref.at[k], block))
    return found


def prepare_cotangent(own, other, after=()):
    length = own.shape[2]

    def body(own_ref, other_ref, cot_ref, wide, sems):
        copies = Copies(sems)
        bring_blocks(copies, own_ref, other_ref, wide)
        copies.wait()
        cot_ref[...] = wide[...].T

    return run(
        body,
        [shaped((length, D))],
        hbm=[own, other],
        scratch=[pltpu.VMEM((D, length), BF)],
        copies=4,
        micros=3,
        after=after,
    )[0]


def prepare(own, other, corpus_weights):
    length = own.shape[2]

    def body(
        weights_ref, own_ref, other_ref, hidden_ref, norms_ref, nums_ref, wide, extra, sems
    ):
        copies = Copies(sems)
        for ref, block in bring_blocks(copies, own_ref, other_ref, wide):
            copies.start(ref.at[pl.ds(QUARTER, 32)], extra.at[block])
        copies.wait()
        hidden_ref[...] = wide[...].T
        parts = [extra[b].astype(F32) for b in range(4)]
        norms_ref[...] = jnp.concatenate(
            [(e[0:8] + e[8:16] + e[16:24])[:, :QUARTER] for e in parts], axis=1
        )
        row = parts[0][24:25]
        tok = 256.0 * row[:, 0:1] + row[:, 1:2]
        aud = 256.0 * row[:, 2:3] + row[:, 3:4]
        weights = weights_ref[...]
        places = lax.broadcasted_iota(jnp.int32, weights.shape, 1).astype(F32)
        weight = jnp.sum(jnp.where(places == row[:, 4:5], weights, 0.0), axis=1, keepdims=True)
        index = lax.broadcasted_iota(jnp.int32, (8, 128), 0)
        nums_ref[...] = jnp.where(index == 0, tok, jnp.where(index == 1, aud, weight))

    return run(
        body,
        [shaped((length, D)), shaped((8, D), F32), shaped((8, 128), F32)],
        vmem=[corpus_weights.reshape(1, -1)],
        hbm=[own, other],
        scratch=[pltpu.VMEM((D, length), BF), pltpu.VMEM((4, 32, length), BF)],
        copies=8,
        micros=3,
    )


def quarters(value):
    return jnp.concatenate([value[:, p * QUARTER : (p + 1) * QUARTER] for p in range(4)], axis=0)


def attention_shard(self_qkv, self_out, cross_kv, cross_q, cross_out):
    rows = cross_q.shape[0]

    def body(qkv_ref, out_ref, kv_ref, q_ref, cout_ref, shard_ref):
        out = quarters(out_ref[...].astype(F32)).astype(BF)
        cout = quarters(cout_ref[...].astype(F32)).astype(BF)
        shard_ref[...] = jnp.concatenate(
            [qkv_ref[j] for j in range(3)] + [out, kv_ref[...], q_ref[...], cout], axis=1
        )

    return run(
        body,
        [shaped((rows, 2 * D))],
        vmem=[self_qkv.transpose(1, 0, 2), self_out, cross_kv.reshape(rows, -1), cross_q, cross_out],
        micros=2,
        staged=True,
    )[0]


def column_slots():
    core, _, z = where_am_i()
    j = z % 2
    home = 1 - jnp.abs(z // 2 - core)
    same = core + (1 - 2 * core) * (1 - home)
    return home == 1, (2 * (1 - j) + same, 2 * j + 1 - same, 2 * (1 - j) + 1 - same, 2 * j + same)


def bring_column(part_refs, own_ref, shards, sems):
    home, slots = column_slots()
    copies = Copies(sems)
    for k in range(3):
        copies.start(part_refs[k], shards.at[slots[k]])

    @pl.when(home)
    def _():
        copy = pltpu.make_async_copy(own_ref, shards.at[slots[3]], sems.at[3])
        copy.start()
        copy.wait()

    @pl.when(jnp.logical_not(home))
    def _():
        copy = pltpu.make_async_copy(part_refs[3], shards.at[slots[3]], sems.at[3])
        copy.start()
        copy.wait()

    copies.wait()


def pack_attention(parts, own, after):
    rows = own.shape[0]
    few = rows // 4

    def body(*refs):
        part_refs, own_ref, (out_ref, shards, sems) = refs[:4], refs[4], refs[5:]
        bring_column(part_refs, own_ref, shards, sems)
        for which in range(2):
            for cs in range(2):
                low, high = shards[cs], shards[2 + cs]

                def both(at):
                    at = at + which * D
                    return [low[:, at : at + QUARTER], high[:, at : at + QUARTER]]

                here = pl.ds(cs * rows, rows)
                out_ref[0, which, here, :] = jnp.concatenate(both(0) + both(QUARTER), axis=1)
                out_ref[1, which, here, 0:HALF] = jnp.concatenate(both(HALF), axis=1)
            at = 3 * QUARTER + which * D
            outs = [shards[i, :, at : at + QUARTER].astype(F32) for i in range(4)]
            stack = []
            for q in range(2):
                for i in range(4):
                    left = outs[i][2 * q * few : (2 * q + 1) * few]
                    right = outs[i][(2 * q + 1) * few : (2 * q + 2) * few]
                    stack.append(jnp.concatenate([left, right], axis=1))
            out_ref[1, which, :, HALF:D] = jnp.concatenate(stack, axis=0).astype(BF)

    return run(
        body,
        [shaped((2, 2, 2 * rows, D))],
        hbm=list(parts) + [own],
        scratch=[pltpu.VMEM((4, rows, 2 * D), BF)],
        copies=4,
        micros=2,
        after=after,
    )[0]


def unit_shard(place, fc_in, fc_out):
    rows = fc_in.shape[0]
    both = fc_in.reshape(rows, place.chips, 2, rows).transpose(2, 0, 1, 3).reshape(2, rows, HALF)
    kept = lax.dynamic_index_in_dim(both, place.core, 0, keepdims=False)
    sent = lax.dynamic_index_in_dim(both, 1 - place.core, 0, keepdims=False)
    came = place.swap_core(sent)
    first = place.core == 0
    left = jnp.concatenate([jnp.where(first, kept, came), jnp.where(first, came, kept)])
    right = jnp.concatenate([fc_out[:, :HALF], fc_out[:, HALF:]])
    return jnp.concatenate([left, right], axis=1)


def stack_units(blocks, after):
    rows = blocks[0].shape[0]

    def body(*refs):
        for k in range(4):
            refs[4][k // 2, k % 2] = refs[k][...]

    return run(body, [shaped((2, 2, rows, D))], vmem=blocks, micros=1.5, after=after)[0]


def gather_units(place, shard):
    whole = lax.all_gather(shard, CHIPS, axis=0)
    rows = shard.shape[0] // 2
    whole = whole.reshape(place.chips, place.mp, 2 * rows, D)
    up = whole[..., :HALF].transpose(0, 2, 1, 3).reshape(D, 2 * D)
    down = whole[..., HALF:].reshape(place.chips, place.mp, 2, rows, HALF)
    return [up, down.transpose(1, 0, 3, 2, 4).reshape(2 * D, D)]


def scatter_units(place, grads):
    total = lax.psum_scatter(grads, CHIPS, scatter_dimension=0, tiled=False)
    rows = total.shape[0] // 2
    kept = lax.dynamic_slice_in_dim(total, place.core * rows, rows, 0)
    sent = lax.dynamic_slice_in_dim(total[:, :HALF], (1 - place.core) * rows, rows, 0)
    came = place.swap_core(sent)
    kept = kept[:, :HALF]
    first = place.core == 0
    both = jnp.stack([jnp.where(first, kept, came), jnp.where(first, came, kept)])
    both = both.reshape(2, rows, place.chips, rows).transpose(1, 2, 0, 3).reshape(rows, D)
    down = jnp.concatenate([total[:rows, HALF:], total[rows:, HALF:]], axis=1)
    return both.astype(F32), down.astype(F32)


def spread(place, own):
    from_x = place.swap_xy(own, 1)
    from_y = place.swap_xy(own, 2)
    far_one = place.swap_xy(from_y[1], 1)
    far_zero = place.swap_xy(from_x[0], 2)
    return [own, from_x, from_y, far_zero, far_one]


def piece_views(refs, message, which, xy):
    own, from_x, from_y, far_zero, far_one = refs
    return [
        (own.at[which, message], xy),
        (from_x.at[which, message], xy ^ 1),
        (from_y.at[which, message], xy ^ 2),
        ((far_zero, far_one)[which].at[message], xy ^ 3),
    ]


def load_wide(copies, refs, message, which, xy, target, columns=None):
    if len(refs) != 5:
        copies.start(refs[which], target)
        return
    for view, chip in piece_views(refs, message, which, xy):
        rows = view.shape[0]
        if columns is not None:
            view = view.at[:, pl.ds(0, columns)]
        copies.start(view, target.at[pl.ds(pl.multiple_of(chip * rows, 16), rows)])


def load_out(copies, refs, message, xy, target):
    if len(refs) != 5:
        copies.start(refs[2], target)
        return
    for view, chip in piece_views(refs, message, 1, xy):
        rows = view.shape[0] // 4
        for q in range(2):
            for hi in range(2):
                copies.start(
                    view.at[pl.ds((2 * q + hi) * rows, rows), pl.ds(HALF, HALF)],
                    target.at[q, pl.ds(pl.multiple_of(hi * QUARTER + chip * rows, 16), rows)],
                )


def unit_views(refs):
    _, xy, z = where_am_i()
    views = []
    for part in range(2):
        for view, chip in [
            (refs[0].at[part], xy),
            (refs[1].at[part], xy ^ 1),
            (refs[2].at[part], xy ^ 2),
            (refs[3 + part], xy ^ 3),
        ]:
            for i in range(2):
                views.append((view.at[i], chip, z ^ (2 * part + i)))
    return views


def load_up(copies, refs, w_up):
    if len(refs) == 2:
        copies.start(refs[0], w_up)
        return
    for view, chip, z in unit_views(refs):
        rows = view.shape[0]
        copies.start(
            view.at[:, pl.ds(0, HALF)],
            w_up.at[
                pl.ds(pl.multiple_of(rows * chip, 16), rows), pl.ds(pl.multiple_of(z * HALF, HALF), HALF)
            ],
        )


def load_down(copies, refs, w_down):
    if len(refs) == 2:
        copies.start(refs[1], w_down)
        return
    for view, chip, z in unit_views(refs):
        rows = view.shape[0] // 2
        for q in range(2):
            copies.start(
                view.at[pl.ds(q * rows, rows), pl.ds(HALF, HALF)],
                w_down.at[
                    pl.ds(pl.multiple_of(z * HALF + chip * rows, 16), rows), pl.ds(q * HALF, HALF)
                ],
            )


ATTENTION_COPIES = 4 + 4 + 16
UP_COPIES = 16
DOWN_COPIES = 32


def gather_plain(place, shard):
    whole = lax.all_gather(shard, ("mp", "xy", "core"), axis=0)
    whole = whole.reshape((2, 2, place.dp) + shard.shape)
    return lax.dynamic_index_in_dim(whole, place.core, 0, keepdims=False)


def attention_plain(place, shard):
    mine = gather_plain(place, shard)
    rows = shard.shape[0]

    def columns(at, count):
        value = mine[..., at : at + count * QUARTER].reshape(2, D, count, QUARTER)
        return value.transpose(1, 2, 0, 3).reshape(D, count * HALF)

    out = mine[..., 3 * QUARTER :].reshape(2, place.dp, 2, 2, rows // 4, QUARTER)
    out = out.transpose(2, 0, 1, 4, 3, 5).reshape(2, HALF, HALF)
    return [columns(0, 2), columns(HALF, 1), out]


def head_rows(h):
    return pl.ds(pl.multiple_of(h * HEAD_DIM, HEAD_DIM), HEAD_DIM)


def low_parts(value):
    parts = []
    for _ in range(3):
        part = value.astype(BF)
        parts.append(part)
        value = value - part.astype(F32)
    return parts


def widened(count):
    return lambda rows: (
        lax.broadcasted_iota(jnp.int32, (rows, HEAD_DIM), 1) < count
    ).astype(F32).astype(BF)


def below(head, rows):
    blank = jnp.zeros((HEAD_DIM - len(rows), head.shape[1]), F32)
    rest = jnp.concatenate([row.astype(F32) for row in rows] + [blank], axis=0)
    return jnp.concatenate([head, rest.astype(BF)], axis=0)


def project(left, pair_ref):
    return jnp.concatenate([mm(left, pair_ref[0]), mm(left, pair_ref[1])], axis=1)


def project_t(left, pair_ref):
    return mm_t(left[:, :HALF], pair_ref[0]) + mm_t(left[:, HALF:], pair_ref[1])


def self_forward(hidden, norms, nums, weights, after=()):
    length = hidden.shape[0]

    def body(hidden_ref, norms_ref, nums_ref, *refs):
        w_refs, refs = refs[: len(weights)], refs[len(weights) :]
        part_ref, at_ref, qkv_ref, qt_ref, kt_ref, ot_ref, lse_ref = refs[:7]
        w_qk, w_v, w_out, vt, heads, bias, sems = refs[7:]
        _, xy, _ = where_am_i()
        copies = Copies(sems)
        load_wide(copies, w_refs, 0, 0, xy, w_qk)
        load_wide(copies, w_refs, 0, 1, xy, w_v, HALF)
        load_out(copies, w_refs, 0, xy, w_out)
        unit, _ = norm(hidden_ref[...].astype(F32))
        a = (unit * norms_ref[0:1] + norms_ref[4:5]).astype(BF)
        at_ref[...] = a.T
        keys = lax.broadcasted_iota(jnp.int32, (length, length), 0)
        queries = lax.broadcasted_iota(jnp.int32, (length, length), 1)
        allowed = (keys <= queries) & (keys.astype(F32) < nums_ref[0:1, 0:1])
        bias[...] = jnp.where(allowed, 0.0, -1e30)
        copies.wait()
        qk = mm(a, w_qk[...])
        q = (qk[:, :HALF].astype(BF).astype(F32) * HEAD_DIM ** (-0.5)).astype(BF)
        k = qk[:, HALF:].astype(BF)
        v = mm(a, w_v[...]).astype(BF)
        qkv_ref[:, 0:HALF] = q
        qkv_ref[:, HALF : 2 * HALF] = k
        qkv_ref[:, 2 * HALF :] = v
        qt_ref[...] = q.T
        kt_ref[...] = k.T
        vt[...] = v.T
        for h in range(HEADS):
            heads[h] = k[:, h * HEAD_DIM : (h + 1) * HEAD_DIM]

        def head(h, carry):
            s = mm(heads[h], qt_ref[head_rows(h), :]) + bias[...]
            top = jnp.max(s, axis=0, keepdims=True)
            p = jnp.exp(s - top)
            total = jnp.sum(p, axis=0, keepdims=True)
            o = mm(vt[head_rows(h), :], p.astype(BF))
            ot_ref[head_rows(h), :] = (o / total).astype(BF)
            lse_ref[h] = top + jnp.log(total)
            return carry

        lax.fori_loop(0, HEADS, head, 0)
        part_ref[...] = project(ot_ref[...].T, w_out).astype(BF)

    return run(
        body,
        [
            shaped((length, D)),
            shaped((D, length)),
            shaped((length, 3 * HALF)),
            shaped((HALF, length)),
            shaped((HALF, length)),
            shaped((HALF, length)),
            shaped((HEADS, 1, length), F32),
        ],
        vmem=[hidden, norms, nums],
        hbm=weights,
        scratch=[
            pltpu.VMEM((D, D), BF),
            pltpu.VMEM((D, HALF), BF),
            pltpu.VMEM((2, HALF, HALF), BF),
            pltpu.VMEM((HALF, length), BF),
            pltpu.VMEM((HEADS, length, HEAD_DIM), BF),
            pltpu.VMEM((length, length), F32),
        ],
        copies=ATTENTION_COPIES,
        micros=3,
        after=after,
    )


def turn(value, after=()):
    rows, columns = value.shape

    def body(ref, out_ref):
        for at in range(0, rows, CHUNK):
            out_ref[:, at : at + CHUNK] = ref[at : at + CHUNK, :].T

    return run(body, [shaped((columns, rows))], vmem=[value], micros=4, after=after)[0]


def cross_memory(encoded, weights):
    frames = encoded.shape[0]

    def body(enc_ref, *refs):
        w_refs, refs = refs[: len(weights)], refs[len(weights) :]
        kv_ref, kvt_ref, w_kv, sems = refs
        _, xy, _ = where_am_i()
        copies = Copies(sems)
        load_wide(copies, w_refs, 1, 0, xy, w_kv)
        copies.wait()

        def step(i, carry):
            here = pl.ds(pl.multiple_of(i * CHUNK, CHUNK), CHUNK)
            kv = mm(enc_ref[here, :], w_kv[...]).astype(BF)
            kv_ref[here, :] = kv
            kvt_ref[:, here] = kv.T
            return carry

        lax.fori_loop(0, frames // CHUNK, step, 0)

    return run(
        body,
        [shaped((frames, D)), shaped((D, frames))],
        vmem=[encoded],
        hbm=weights,
        scratch=[pltpu.VMEM((D, D), BF)],
        copies=4,
        micros=1,
    )


def residual(hidden_ref, mine_ref, other_ref):
    return hidden_ref[...].astype(F32) + (mine_ref[...].astype(F32) + other_ref[...].astype(F32))


def cross_forward(hidden, mine, other, norms, nums, kv, kvt, weights):
    length = hidden.shape[0]
    frames = kv.shape[0]

    def body(hidden_ref, mine_ref, other_ref, norms_ref, nums_ref, kv_ref, kvt_ref, *refs):
        w_refs, refs = refs[: len(weights)], refs[len(weights) :]
        part_ref, h_ref, ct_ref, q_ref, qt_ref, ot_ref, lse_ref = refs[:7]
        w_q, w_out, heads, values_t, scores, sems = refs[7:]
        _, xy, _ = where_am_i()
        copies = Copies(sems)
        load_wide(copies, w_refs, 1, 1, xy, w_q, HALF)
        load_out(copies, w_refs, 1, xy, w_out)
        h1 = residual(hidden_ref, mine_ref, other_ref)
        h_ref[...] = h1
        unit, _ = norm(h1)
        c = (unit * norms_ref[1:2] + norms_ref[5:6]).astype(BF)
        ct_ref[...] = c.T
        frame = lax.broadcasted_iota(jnp.int32, (frames, HEAD_DIM), 0).astype(F32)
        lane = lax.broadcasted_iota(jnp.int32, (frames, HEAD_DIM), 1)
        mask = jnp.where(frame < nums_ref[1:2, 0:1], 0.0, -1e30)
        beside = jnp.where(lane == 0, mask, 0.0).astype(BF)
        one = lax.broadcasted_iota(jnp.int32, (16, frames), 0)
        one = jnp.where(one == 0, 1.0, 0.0).astype(BF)
        for h in range(HEADS):
            keys = kv_ref[:, h * HEAD_DIM : (h + 1) * HEAD_DIM]
            heads[h] = jnp.concatenate([keys, beside], axis=1)
            values = kvt_ref[HALF + h * HEAD_DIM : HALF + (h + 1) * HEAD_DIM, :]
            values_t[h] = jnp.concatenate([values, one], axis=0)
        copies.wait()
        q = mm(c, w_q[...]).astype(BF)
        q = (q.astype(F32) * HEAD_DIM ** (-0.5)).astype(BF)
        q_ref[...] = q
        qt_ref[...] = q.T
        ones = jnp.ones((1, length), F32)

        def head(h, carry):
            qt = below(qt_ref[head_rows(h), :], [ones])
            top = None
            for at in range(0, frames, CHUNK):
                s = mm(heads[h, at : at + CHUNK], qt)
                scores[at : at + CHUNK] = s
                high = jnp.max(s, axis=0, keepdims=True)
                top = high if top is None else jnp.maximum(top, high)
            o = None
            for at in range(0, frames, CHUNK):
                p = jnp.exp(scores[at : at + CHUNK] - top).astype(BF)
                more = mm(values_t[h, :, at : at + CHUNK], p)
                o = more if o is None else o + more
            total = o[HEAD_DIM : HEAD_DIM + 1]
            ot_ref[head_rows(h), :] = (o[:HEAD_DIM] / total).astype(BF)
            lse_ref[h] = top + jnp.log(total)
            return carry

        lax.fori_loop(0, HEADS, head, 0)
        part_ref[...] = project(ot_ref[...].T, w_out).astype(BF)

    return run(
        body,
        [
            shaped((length, D)),
            shaped((length, D), F32),
            shaped((D, length)),
            shaped((length, HALF)),
            shaped((HALF, length)),
            shaped((HALF, length)),
            shaped((HEADS, 1, length), F32),
        ],
        vmem=[hidden, mine, other, norms, nums, kv, kvt],
        hbm=weights,
        scratch=[
            pltpu.VMEM((D, HALF), BF),
            pltpu.VMEM((2, HALF, HALF), BF),
            pltpu.VMEM((HEADS, frames, 2 * HEAD_DIM), BF),
            pltpu.VMEM((HEADS, HEAD_DIM + 16, frames), BF),
            pltpu.VMEM((frames, length), F32),
        ],
        copies=4 + 16,
        micros=2,
    )


def units_forward(hidden, mine, other, norms, weights):
    length = hidden.shape[0]

    def body(hidden_ref, mine_ref, other_ref, norms_ref, *refs):
        w_refs, refs = refs[: len(weights)], refs[len(weights) :]
        part_ref, h_ref, mt_ref, slope_ref, it_ref = refs[:5]
        w_up, w_down, inner, late_sems, sems = refs[5:]
        _, xy, _ = where_am_i()
        copies = Copies(sems)
        load_up(copies, w_refs, w_up)
        late = Copies(late_sems)
        load_down(late, w_refs, w_down)
        h2 = residual(hidden_ref, mine_ref, other_ref)
        h_ref[...] = h2
        unit, _ = norm(h2)
        m = (unit * norms_ref[2:3] + norms_ref[6:7]).astype(BF)
        mt_ref[...] = m.T
        copies.wait()
        for at in range(0, 2 * D, CHUNK):
            here = slice(at, at + CHUNK)
            z = mm(m, w_up[:, here])
            share = 0.5 * (1.0 + lax.erf(z * 0.7071067811865476))
            slope = share + z * (0.3989422804014327 * jnp.exp(-0.5 * z * z))
            value = (z * share).astype(BF)
            inner[:, here] = value
            it_ref[here, :] = value.T
            slope_ref[:, here] = slope.astype(BF)
        late.wait()
        for at in range(0, D, CHUNK):
            part_ref[:, at : at + CHUNK] = mm(inner[...], w_down[:, at : at + CHUNK]).astype(BF)

    return run(
        body,
        [
            shaped((length, D)),
            shaped((length, D), F32),
            shaped((D, length)),
            shaped((length, 2 * D)),
            shaped((2 * D, length)),
        ],
        vmem=[hidden, mine, other, norms],
        hbm=weights,
        scratch=[
            pltpu.VMEM((D, 2 * D), BF),
            pltpu.VMEM((2 * D, D), BF),
            pltpu.VMEM((length, 2 * D), BF),
            pltpu.SemaphoreType.DMA((DOWN_COPIES,)),
        ],
        copies=UP_COPIES,
        micros=9,
    )


def store_blocks(value, blocks, first_ref, second_ref):
    core, _, z = where_am_i()
    for b in range(4):
        blocks[b] = value[:, b * QUARTER : (b + 1) * QUARTER]
    first_ref[...] = blocks[2 * core + z % 2].T
    second_ref[...] = blocks[2 * core + (z + 1) % 2].T


def units_backward(hidden, mine, other, norms, nums, cot, slope, weights):
    length = hidden.shape[0]

    def body(hidden_ref, mine_ref, other_ref, norms_ref, nums_ref, cot_ref, slope_ref, *refs):
        w_refs, refs = refs[: len(weights)], refs[len(weights) :]
        part_ref, d_ref, e_ref, dz_ref, terms_ref, first_ref, second_ref = refs[:7]
        w_up, w_down, blocks, late_sems, sems = refs[7:]
        _, xy, _ = where_am_i()
        copies = Copies(sems)
        load_down(copies, w_refs, w_down)
        late = Copies(late_sems)
        load_up(late, w_refs, w_up)
        unit, inverse = norm(residual(hidden_ref, mine_ref, other_ref))
        final = (unit * norms_ref[3:4] + norms_ref[7:8]).astype(BF)
        store_blocks(final, blocks, first_ref, second_ref)
        live = lax.broadcasted_iota(jnp.int32, (length, 1), 0).astype(F32) < nums_ref[0:1, 0:1]
        grad = cot_ref[...].astype(F32) * jnp.where(live, nums_ref[2:3, 0:1], 0.0)
        d3, terms = norm_back(grad, unit, inverse, norms_ref[3:4])
        d_ref[...] = d3
        terms_ref[...] = terms
        e = d3.astype(BF)
        e_ref[...] = e
        copies.wait()
        for at in range(0, 2 * D, CHUNK):
            here = slice(at, at + CHUNK)
            d_inner = mm_t(e, w_down[here, :])
            dz_ref[:, here] = (slope_ref[:, here].astype(F32) * d_inner).astype(BF)
        late.wait()
        for at in range(0, D, CHUNK):
            out = mm_t(dz_ref[...], w_up[at : at + CHUNK, :])
            part_ref[:, at : at + CHUNK] = out.astype(BF)

    return run(
        body,
        [
            shaped((length, D)),
            shaped((length, D), F32),
            shaped((length, D)),
            shaped((length, 2 * D)),
            shaped((2, D), F32),
            shaped((QUARTER, length)),
            shaped((QUARTER, length)),
        ],
        vmem=[hidden, mine, other, norms, nums, cot, slope],
        hbm=weights,
        scratch=[
            pltpu.VMEM((D, 2 * D), BF),
            pltpu.VMEM((2 * D, D), BF),
            pltpu.VMEM((4, length, QUARTER), BF),
            pltpu.SemaphoreType.DMA((UP_COPIES,)),
        ],
        copies=DOWN_COPIES,
        micros=10,
    )


def step_back(d_ref, hidden_ref, mine_ref, other_ref, gain):
    unit, inverse = norm(hidden_ref[...].astype(F32))
    grad = mine_ref[...].astype(F32) + other_ref[...].astype(F32)
    part, terms = norm_back(grad, unit, inverse, gain)
    return d_ref[...] + part, terms


def cross_backward(
    d, hidden, mine, other, norms, nums, kv, kvt, q, qt, ot, lse, weights, after=()
):
    length = hidden.shape[0]
    frames = kv.shape[0]

    def body(
        d_ref, hidden_ref, mine_ref, other_ref, norms_ref, nums_ref, kv_ref, kvt_ref, q_ref,
        qt_ref, ot_ref, lse_ref, *refs
    ):
        w_refs, refs = refs[: len(weights)], refs[len(weights) :]
        part_ref, d_out_ref, e_ref, dq_ref, dkv_ref, terms_ref = refs[:6]
        w_q, w_out, keys, values, queries, grads, dot_t, dk_h, dv_h, dqt, sems = refs[6:]
        _, xy, _ = where_am_i()
        copies = Copies(sems)
        load_wide(copies, w_refs, 1, 1, xy, w_q, HALF)
        load_out(copies, w_refs, 1, xy, w_out)
        d2, terms = step_back(d_ref, hidden_ref, mine_ref, other_ref, norms_ref[2:3])
        d_out_ref[...] = d2
        terms_ref[...] = terms
        e = d2.astype(BF)
        e_ref[...] = e
        frame = lax.broadcasted_iota(jnp.int32, (frames, HEAD_DIM), 0).astype(F32)
        lane = lax.broadcasted_iota(jnp.int32, (frames, HEAD_DIM), 1)
        mask = jnp.where(frame < nums_ref[1:2, 0:1], 0.0, -1e30)
        beside = jnp.where(lane == 0, mask, jnp.where(lane < 4, 1.0, 0.0)).astype(BF)
        three = widened(3)(frames)
        for h in range(HEADS):
            lanes = slice(h * HEAD_DIM, (h + 1) * HEAD_DIM)
            keys[h] = jnp.concatenate([kv_ref[:, lanes], beside], axis=1)
            value = kv_ref[:, HALF + h * HEAD_DIM : HALF + (h + 1) * HEAD_DIM]
            values[h] = jnp.concatenate([value, three], axis=1)
            queries[h] = q_ref[:, lanes]
        copies.wait()
        d_mixed = project_t(e, w_out).astype(BF)
        dot_t[...] = d_mixed.T
        for h in range(HEADS):
            grads[h] = d_mixed[:, h * HEAD_DIM : (h + 1) * HEAD_DIM]
        ones = jnp.ones((1, length), F32)

        def head(h, carry):
            rows = head_rows(h)
            do_t = dot_t[rows, :]
            q_n, do_n = queries[h], grads[h]
            delta = jnp.sum(do_t.astype(F32) * ot_ref[rows, :].astype(F32), axis=0, keepdims=True)
            q_t = below(qt_ref[rows, :], [ones] + low_parts(-lse_ref[h]))
            do_t = below(do_t, low_parts(-delta))
            total = None
            for at in range(0, frames, CHUNK):
                here = slice(at, at + CHUNK)
                p = jnp.exp(mm(keys[h, here], q_t))
                ds = (p * mm(values[h, here], do_t)).astype(BF)
                dv_h[h, here] = mm(p.astype(BF), do_n).astype(BF)
                dk_h[h, here] = mm(ds, q_n).astype(BF)
                more = mm(kvt_ref[rows, here], ds)
                total = more if total is None else total + more
            dqt[rows, :] = (total * HEAD_DIM ** (-0.5)).astype(BF)
            return carry

        lax.fori_loop(0, HEADS, head, 0)
        dq = dqt[...].T
        dq_ref[...] = dq
        part_ref[...] = mm_t(dq, w_q[...]).astype(BF)
        for h in range(HEADS):
            lanes = slice(h * HEAD_DIM, (h + 1) * HEAD_DIM)
            dkv_ref[:, lanes] = dk_h[h]
            dkv_ref[:, HALF + h * HEAD_DIM : HALF + (h + 1) * HEAD_DIM] = dv_h[h]

    return run(
        body,
        [
            shaped((length, D)),
            shaped((length, D), F32),
            shaped((length, D)),
            shaped((length, HALF)),
            shaped((frames, D)),
            shaped((2, D), F32),
        ],
        vmem=[d, hidden, mine, other, norms, nums, kv, kvt, q, qt, ot, lse],
        hbm=weights,
        scratch=[
            pltpu.VMEM((D, HALF), BF),
            pltpu.VMEM((2, HALF, HALF), BF),
            pltpu.VMEM((HEADS, frames, 2 * HEAD_DIM), BF),
            pltpu.VMEM((HEADS, frames, 2 * HEAD_DIM), BF),
            pltpu.VMEM((HEADS, length, HEAD_DIM), BF),
            pltpu.VMEM((HEADS, length, HEAD_DIM), BF),
            pltpu.VMEM((HALF, length), BF),
            pltpu.VMEM((HEADS, frames, HEAD_DIM), BF),
            pltpu.VMEM((HEADS, frames, HEAD_DIM), BF),
            pltpu.VMEM((HALF, length), BF),
        ],
        copies=4 + 16,
        micros=22,
        after=after,
    )


def self_backward(d, hidden, mine, other, norms, nums, qkv, qt, kt, ot, lse, weights, after=()):
    length = hidden.shape[0]

    def body(
        d_ref, hidden_ref, mine_ref, other_ref, norms_ref, nums_ref, qkv_ref, qt_ref, kt_ref,
        ot_ref, lse_ref, *refs
    ):
        w_refs, refs = refs[: len(weights)], refs[len(weights) :]
        part_ref, d_out_ref, e_ref, dqk_ref, dv_ref, terms_ref = refs[:6]
        w_qk, w_v, w_out, queries_h, keys, values, grads, dot_t, dk_h, dv_h, dqt, bias, sems = refs[6:]
        _, xy, _ = where_am_i()
        copies = Copies(sems)
        load_out(copies, w_refs, 0, xy, w_out)
        load_wide(copies, w_refs, 0, 0, xy, w_qk)
        load_wide(copies, w_refs, 0, 1, xy, w_v, HALF)
        d1, terms = step_back(d_ref, hidden_ref, mine_ref, other_ref, norms_ref[1:2])
        d_out_ref[...] = d1
        terms_ref[...] = terms
        e = d1.astype(BF)
        e_ref[...] = e
        places = lax.broadcasted_iota(jnp.int32, (length, length), 0)
        queries = lax.broadcasted_iota(jnp.int32, (length, length), 1)
        allowed = (places <= queries) & (places.astype(F32) < nums_ref[0:1, 0:1])
        bias[...] = jnp.where(allowed, 0.0, -1e30)
        three = widened(3)(length)
        for h in range(HEADS):
            at = h * HEAD_DIM
            queries_h[h] = qkv_ref[:, at : at + HEAD_DIM]
            key = qkv_ref[:, HALF + at : HALF + at + HEAD_DIM]
            keys[h] = jnp.concatenate([key, three], axis=1)
            value = qkv_ref[:, 2 * HALF + at : 2 * HALF + at + HEAD_DIM]
            values[h] = jnp.concatenate([value, three], axis=1)
        copies.wait()
        d_mixed = project_t(e, w_out).astype(BF)
        dot_t[...] = d_mixed.T
        for h in range(HEADS):
            grads[h] = d_mixed[:, h * HEAD_DIM : (h + 1) * HEAD_DIM]

        def head(h, carry):
            rows = head_rows(h)
            do_t, do_n = dot_t[rows, :], grads[h]
            delta = jnp.sum(do_t.astype(F32) * ot_ref[rows, :].astype(F32), axis=0, keepdims=True)
            q_t = below(qt_ref[rows, :], low_parts(-lse_ref[h]))
            do_t = below(do_t, low_parts(-delta))
            p = jnp.exp(mm(keys[h], q_t) + bias[...])
            ds = (p * mm(values[h], do_t)).astype(BF)
            dv_h[h] = mm(p.astype(BF), do_n).astype(BF)
            dk_h[h] = mm(ds, queries_h[h]).astype(BF)
            dqt[rows, :] = (mm(kt_ref[rows, :], ds) * HEAD_DIM ** (-0.5)).astype(BF)
            return carry

        lax.fori_loop(0, HEADS, head, 0)
        dqk_ref[:, 0:HALF] = dqt[...].T
        for h in range(HEADS):
            lanes = slice(HALF + h * HEAD_DIM, HALF + (h + 1) * HEAD_DIM)
            dqk_ref[:, lanes] = dk_h[h]
            dv_ref[:, h * HEAD_DIM : (h + 1) * HEAD_DIM] = dv_h[h]
        out = mm_t(dqk_ref[...], w_qk[...]) + mm_t(dv_ref[...], w_v[...])
        part_ref[...] = out.astype(BF)

    return run(
        body,
        [
            shaped((length, D)),
            shaped((length, D), F32),
            shaped((length, D)),
            shaped((length, D)),
            shaped((length, HALF)),
            shaped((2, D), F32),
        ],
        vmem=[d, hidden, mine, other, norms, nums, qkv, qt, kt, ot, lse],
        hbm=weights,
        scratch=[
            pltpu.VMEM((D, D), BF),
            pltpu.VMEM((D, HALF), BF),
            pltpu.VMEM((2, HALF, HALF), BF),
            pltpu.VMEM((HEADS, length, HEAD_DIM), BF),
            pltpu.VMEM((HEADS, length, 2 * HEAD_DIM), BF),
            pltpu.VMEM((HEADS, length, 2 * HEAD_DIM), BF),
            pltpu.VMEM((HEADS, length, HEAD_DIM), BF),
            pltpu.VMEM((HALF, length), BF),
            pltpu.VMEM((HEADS, length, HEAD_DIM), BF),
            pltpu.VMEM((HEADS, length, HEAD_DIM), BF),
            pltpu.VMEM((HALF, length), BF),
            pltpu.VMEM((length, length), F32),
        ],
        copies=ATTENTION_COPIES,
        micros=12,
        staged=True,
        after=after,
    )


def finish_hidden(d, hidden, mine, other, norms, terms1, terms2, terms3, after=()):
    length = hidden.shape[0]

    def body(
        d_ref, hidden_ref, mine_ref, other_ref, norms_ref, one, two, three, terms_ref, first_ref,
        second_ref, blocks
    ):
        d0, terms = step_back(d_ref, hidden_ref, mine_ref, other_ref, norms_ref[0:1])
        store_blocks(d0.astype(BF), blocks, first_ref, second_ref)
        for j in range(2):
            here = slice(j, j + 1)
            terms_ref[4 * j : 4 * j + 4] = jnp.concatenate(
                [terms[here], one[here], two[here], three[here]], axis=0
            )

    return run(
        body,
        [shaped((8, D), F32), shaped((QUARTER, length)), shaped((QUARTER, length))],
        vmem=[d, hidden, mine, other, norms, terms1, terms2, terms3],
        scratch=[pltpu.VMEM((4, length, QUARTER), BF)],
        micros=4,
        after=after,
    )


def finish_encoder(keep, other, frames, after=()):
    def body(keep_ref, other_ref, first_ref, second_ref):
        _, _, z = where_am_i()
        for ref, k in ((first_ref, 0), (second_ref, 1)):
            here = pl.ds(pl.multiple_of(((z + k) % 2) * QUARTER, QUARTER), QUARTER)
            total = keep_ref[here, :].astype(F32) + other_ref[here, :].astype(F32)
            ref[...] = total.astype(BF)[:, :frames]

    return run(
        body,
        [shaped((QUARTER, frames)), shaped((QUARTER, frames))],
        vmem=[keep, other],
        micros=2,
        after=after,
    )


def block_plan(place):
    if not place.fast:
        return 1, (((1, 0, 0),), ((1, 0, 0),))
    first = ((1, 0, 0), (0, 0, 1), (1, 1, 2), (0, 1, 3))
    second = ((1, 0, 0), (1, 1, 1), (0, 0, 2), (0, 1, 3))
    return 4, (first, second)


def grad_outputs(place, shape):
    if place.fast:
        return [shaped((2,) + shape)] * 4
    return [shaped((1,) + shape)] * 4


def units_grads(place, mt, dz, it, e):
    chips = place.chips
    rows = D // (2 * chips)
    _, plan = block_plan(place)

    def body(mt_ref, dz_ref, it_ref, e_ref, *outs):
        _, xy, _ = where_am_i()
        for output, slot, offset in plan[1]:
            chip = xy ^ offset
            for z in range(4):
                here = pl.ds(pl.multiple_of(z * HALF + chip * rows, 16), rows)
                outs[2 + output][slot, z] = mm(it_ref[here, :], e_ref[...]).astype(BF)
        for output, slot, offset in plan[0]:
            here = pl.ds(pl.multiple_of((xy ^ offset) * 2 * rows, 16), 2 * rows)
            left = mm(mt_ref[here, :], dz_ref[...]).astype(BF)
            for z in range(4):
                outs[output][slot, z] = left[:, z * HALF : (z + 1) * HALF]

    def plain(mt_ref, dz_ref, it_ref, e_ref, left_ref, right_ref):
        left_ref[...] = mm(mt_ref[...], dz_ref[...]).astype(BF)
        right_ref[...] = mm(it_ref[...], e_ref[...]).astype(BF)

    if place.fast:
        first, second = shaped((2, 4, 2 * rows, HALF)), shaped((2, 4, rows, D))
        return run(
            body, [first, first, second, second], vmem=[mt, dz, it, e], micros=6
        )
    left, right = run(
        plain, [shaped((D, 2 * D)), shaped((2 * D, D))], vmem=[mt, dz, it, e], micros=7
    )
    left = left.reshape(chips, 2 * rows, 4, HALF).transpose(0, 2, 1, 3)
    right = right.reshape(4, chips, rows, 2, HALF).transpose(1, 0, 3, 2, 4)
    whole = jnp.concatenate([left, right.reshape(chips, 4, 2 * rows, HALF)], axis=-1)
    return whole.reshape(4 * chips, 2 * rows, D)


def units_sum(grads, came, onward, after):
    rows = grads[3].shape[2]

    def body(*refs):
        ins, (kept_ref, sent_ref, left, right, blocks, sems) = refs[:6], refs[6:]
        _, _, mp = where_am_i()
        copies = Copies(sems)
        for i, ref in enumerate(ins):
            target = (left if i < 3 else right).at[i % 3]
            copies.start(ref if i % 3 == 2 else ref.at[0], target)
        copies.wait()
        for z in range(4):
            blocks[z, :, 0:HALF] = add_up(*[left[i, z] for i in range(3)]).astype(BF)
            down = add_up(*[right[i, z] for i in range(3)]).astype(BF)
            blocks[z, 0:rows, HALF:D] = down[:, :HALF]
            blocks[z, rows : 2 * rows, HALF:D] = down[:, HALF:]
        for i in range(2):
            kept_ref[i] = blocks[mp ^ (2 * i)]
            sent_ref[i] = blocks[mp ^ (2 * i + 1)]

    return run(
        body,
        [shaped((2, 2 * rows, D)), shaped((2, 2 * rows, D))],
        hbm=[grads[1], came[0], onward[0], grads[3], came[1], onward[1]],
        scratch=[
            pltpu.VMEM((3, 4, 2 * rows, HALF), BF),
            pltpu.VMEM((3, 4, rows, D), BF),
            pltpu.VMEM((4, 2 * rows, D), BF),
        ],
        copies=6,
        micros=3,
        after=after,
    )


def add_second(kept, came, after):
    def body(kept_ref, came_ref, out_ref, held, sems):
        copies = Copies(sems)
        copies.start(kept_ref.at[1], held.at[0])
        copies.start(came_ref.at[1], held.at[1])
        copies.wait()
        out_ref[...] = add_up(held[0], held[1]).astype(BF)

    shape = kept.shape[1:]
    return run(
        body,
        [shaped(shape)],
        hbm=[kept, came],
        scratch=[pltpu.VMEM((2,) + shape, BF)],
        copies=2,
        micros=1,
        after=after,
    )[0]


def cut_units(kept, came, last, after):
    rows = last.shape[0] // 2

    def body(kept_ref, came_ref, last_ref, mine_ref, sent_ref, down_ref, held, sems):
        core, _, _ = where_am_i()
        copies = Copies(sems)
        copies.start(kept_ref.at[0], held.at[0])
        copies.start(came_ref.at[0], held.at[1])
        copies.start(last_ref, held.at[2])
        copies.wait()
        mine = pl.ds(pl.multiple_of(core * rows, 16), rows)
        theirs = pl.ds(pl.multiple_of((1 - core) * rows, 16), rows)
        mine_ref[...] = add_up(*[held[i, mine, 0:HALF] for i in range(3)]).astype(BF)
        sent_ref[...] = add_up(*[held[i, theirs, 0:HALF] for i in range(3)]).astype(BF)
        down_ref[:, 0:HALF] = add_up(*[held[i, 0:rows, HALF:D] for i in range(3)])
        down_ref[:, HALF:D] = add_up(*[held[i, rows : 2 * rows, HALF:D] for i in range(3)])

    return run(
        body,
        [shaped((rows, HALF)), shaped((rows, HALF)), shaped((rows, D), F32)],
        hbm=[kept, came, last],
        scratch=[pltpu.VMEM((3, 2 * rows, D), BF)],
        copies=3,
        micros=1,
        after=after,
    )


def join_units(place, kept, came):
    rows = kept.shape[0]

    def body(kept_ref, came_ref, up_ref, both):
        core, _, _ = where_am_i()
        both[core] = kept_ref[...]
        both[1 - core] = came_ref[...]
        blocks = []
        for chip in range(place.chips):
            for parity in range(2):
                blocks.append(both[parity, :, chip * rows : (chip + 1) * rows].astype(F32))
        up_ref[...] = jnp.concatenate(blocks, axis=1)

    return run(
        body,
        [shaped((rows, D), F32)],
        vmem=[kept, came],
        scratch=[pltpu.VMEM((2, rows, HALF), BF)],
        micros=1,
    )[0]


def attention_grads(place, wide_left, wide_right, left, right, ot, e, after=()):
    count, plan = block_plan(place)
    rows = D // count
    few = rows // 4

    def body(wide_left_ref, wide_right_ref, left_ref, right_ref, ot_ref, e_ref, *outs):
        _, xy, _ = where_am_i()
        for output, slot, offset in plan[0]:
            chip = xy ^ offset if count > 1 else 0
            here = pl.ds(pl.multiple_of(chip * rows, 16), rows)
            outs[output][slot] = mm(wide_left_ref[here, :], wide_right_ref[...]).astype(BF)
        for output, slot, offset in plan[1]:
            chip = xy ^ offset if count > 1 else 0
            here = pl.ds(pl.multiple_of(chip * rows, 16), rows)
            target = outs[2 + output]
            target[slot, :, 0:HALF] = mm(left_ref[here, :], right_ref[...]).astype(BF)
            for hi in range(2):
                here = pl.ds(pl.multiple_of(hi * QUARTER + chip * few, 16), few)
                both = mm(ot_ref[here, :], e_ref[...]).astype(BF)
                for q in range(2):
                    at = (2 * q + hi) * few
                    target[slot, at : at + few, HALF:D] = both[:, q * HALF : (q + 1) * HALF]

    return run(
        body,
        grad_outputs(place, (rows, D)),
        vmem=[wide_left, wide_right, left, right, ot, e],
        micros=6,
        after=after,
    )


def encoder_grad(dkv, weights, after=()):
    padded = dkv.shape[0]

    def body(dkv_ref, *refs):
        w_refs, (keep_ref, send_ref, w_kv, sems) = refs[: len(weights)], refs[len(weights) :]
        core, xy, _ = where_am_i()
        copies = Copies(sems)
        load_wide(copies, w_refs, 1, 0, xy, w_kv)
        copies.wait()
        mine = pl.ds(pl.multiple_of(core * HALF, HALF), HALF)
        theirs = pl.ds(pl.multiple_of((1 - core) * HALF, HALF), HALF)
        for ref, rows in ((send_ref, theirs), (keep_ref, mine)):
            for at in range(0, padded, CHUNK):
                value = mm_t(w_kv[rows, :], dkv_ref[at : at + CHUNK, :])
                ref[:, at : at + CHUNK] = value.astype(BF)

    return run(
        body,
        [shaped((HALF, padded)), shaped((HALF, padded))],
        vmem=[dkv],
        hbm=weights,
        scratch=[pltpu.VMEM((D, D), BF)],
        copies=4,
        micros=3.5,
        after=after,
    )


def leave_plane(place, grads):
    return [place.swap_xy(grads[0], 1), place.swap_xy(grads[2], 2)]


def pass_on(grads, came, after):
    shapes = [grads[1].shape[1:], grads[3].shape[1:]]

    def body(stay0, came0, stay1, came1, out0, out1, held0, held1, sems):
        copies = Copies(sems)
        for i, ref in enumerate((stay0, came0, stay1, came1)):
            copies.start(ref.at[1], (held0 if i < 2 else held1).at[i % 2])
        copies.wait()
        out0[...] = add_up(held0[0], held0[1]).astype(BF)
        out1[...] = add_up(held1[0], held1[1]).astype(BF)

    return run(
        body,
        [shaped(shape) for shape in shapes],
        hbm=[grads[1], came[0], grads[3], came[1]],
        scratch=[pltpu.VMEM((2,) + shape, BF) for shape in shapes],
        copies=4,
        micros=1,
        after=after,
    )


def cross_plane(place, onward):
    return [place.swap_xy(onward[0], 2), place.swap_xy(onward[1], 1)]


def column_blocks(grads, came, onward, norm_terms=(), after=()):
    shape = onward[0].shape
    rows = shape[-2] // 2
    width = D
    few = rows // 4
    extra = 16 if norm_terms else 0

    def body(*refs):
        terms_refs, refs = refs[: len(norm_terms)], refs[len(norm_terms) :]
        ins, outs, (held, shards, sems) = refs[:6], refs[6:-3], refs[-3:]
        home, slots = column_slots()
        copies = Copies(sems)
        for i, ref in enumerate(ins):
            copies.start(ref if i % 3 == 2 else ref.at[0], held.at[i])
        copies.wait()
        sums = [add_up(held[3 * part], held[3 * part + 1], held[3 * part + 2]) for part in range(2)]
        for hi in range(2):
            for cs in range(2):
                here = slice(cs * rows, (cs + 1) * rows)
                lanes = slice(hi * QUARTER, (hi + 1) * QUARTER)
                lanes_two = slice(HALF + hi * QUARTER, HALF + (hi + 1) * QUARTER)
                outs_rows = []
                for p in range(4):
                    at = (2 * (p // 2) + hi) * 2 * few + cs * few
                    side = HALF + (p % 2) * QUARTER
                    outs_rows.append(sums[1][at : at + few, side : side + QUARTER])
                value = jnp.concatenate(
                    [
                        sums[0][here, lanes],
                        sums[0][here, lanes_two],
                        sums[1][here, lanes],
                        jnp.concatenate(outs_rows, axis=0),
                    ],
                    axis=1,
                )
                shards[2 * hi + cs, :rows] = value.astype(BF)
        if norm_terms:
            core, xy, _ = where_am_i()
            terms = add_up(*[ref[...] for ref in terms_refs])
            terms = jnp.concatenate([terms, jnp.zeros_like(terms)], axis=0).astype(BF)
            feature = lax.broadcasted_iota(jnp.int32, (D, D), 0)
            lane = lax.broadcasted_iota(jnp.int32, (D, D), 1)
            for hi in range(2):
                for cs in range(2):
                    offset = (2 * core + hi) * QUARTER + (2 * xy + cs) * few
                    pick = jnp.where((feature == lane + offset) & (lane < few), 1.0, 0.0)
                    shards[2 * hi + cs, rows:] = mm(terms, pick.astype(BF)).astype(BF)
        for k in range(4):
            outs[k][...] = shards[slots[k]]

    ins = [grads[1], came[0], onward[0], grads[3], came[1], onward[1]]
    return run(
        body,
        [shaped((rows + extra, width))] * 4,
        vmem=list(norm_terms),
        hbm=ins,
        after=after,
        scratch=[pltpu.VMEM((6,) + shape, BF), pltpu.VMEM((4, rows + extra, width), BF)],
        copies=6,
        micros=2,
    )


def sum_plain(place, grads, attention):
    wide, narrow = grads[1][0], grads[3][0]
    rows = D // place.dp
    if attention:
        value = jnp.stack([wide[:, :HALF], wide[:, HALF:], narrow[:, :HALF]], axis=1)
        value = value.reshape(place.dp, rows, 3, 2, QUARTER).transpose(3, 0, 1, 2, 4)
        value = value.reshape(2, place.dp, rows, 3 * QUARTER)
        outs = narrow[:, HALF:].reshape(2, 2, place.dp, rows // 4, 2, QUARTER)
        outs = outs.transpose(1, 2, 0, 4, 3, 5).reshape(2, place.dp, rows, QUARTER)
        value = jnp.concatenate([value, outs], axis=-1)
    else:
        value = jnp.concatenate(
            [wide.reshape(2, place.dp, rows, D), narrow.reshape(2, place.dp, rows, D)], axis=-1
        )
    whole = jnp.zeros((2,) + value.shape, F32)
    whole = lax.dynamic_update_index_in_dim(whole, value.astype(F32), place.core, 0)
    whole = whole.reshape((4 * place.dp,) + value.shape[2:])
    return lax.psum_scatter(whole, ("mp", "xy", "core"), scatter_dimension=0, tiled=False)


def attention_outputs(sums, rows, few):
    value = sums[:rows]
    last = value[:, 3 * QUARTER :]
    out = jnp.concatenate([last[p * few : (p + 1) * few] for p in range(4)], axis=1)
    return [value[:, j * QUARTER : (j + 1) * QUARTER] for j in range(3)], out


def finish_self(got, own, few_lanes):
    rows = own.shape[0] - 16
    few = rows // 4

    def body(a, b, c, d, own_ref, qkv_ref, out_ref, gain_ref, bias_ref):
        home, _ = column_slots()
        last = jnp.where(home, own_ref[...].astype(F32), d[...].astype(F32))
        sums = add_up(a[...], b[...], c[...], last)
        blocks, out = attention_outputs(sums, rows, few)
        for j in range(3):
            qkv_ref[j] = blocks[j]
        out_ref[...] = out
        gain_ref[...] = sums[rows : rows + 4, :few_lanes]
        bias_ref[...] = sums[rows + 4 : rows + 8, :few_lanes]

    return run(
        body,
        [
            shaped((3, rows, QUARTER), F32),
            shaped((few, D), F32),
            shaped((4, few_lanes), F32),
            shaped((4, few_lanes), F32),
        ],
        vmem=list(got) + [own],
        micros=1.5,
    )


def finish_cross(got, own, after=()):
    rows = own.shape[0]
    few = rows // 4

    def body(a, b, c, d, own_ref, kv_ref, q_ref, out_ref):
        home, _ = column_slots()
        last = jnp.where(home, own_ref[...].astype(F32), d[...].astype(F32))
        blocks, out = attention_outputs(add_up(a[...], b[...], c[...], last), rows, few)
        kv_ref[...] = jnp.concatenate(blocks[:2], axis=1)
        q_ref[...] = blocks[2]
        out_ref[...] = out

    return run(
        body,
        [shaped((rows, HALF), F32), shaped((rows, QUARTER), F32), shaped((few, D), F32)],
        vmem=list(got) + [own],
        micros=1.5,
        after=after,
    )


def join_rows(blocks, got, dtype, after=()):
    width, rows = blocks[0].shape

    def body(block_ref, first_ref, second_ref, out_ref):
        home, _ = column_slots()
        _, _, z = where_am_i()

        @pl.when(home)
        def _():
            out_ref[z % 2] = block_ref[...].astype(dtype)

        @pl.when(jnp.logical_not(home))
        def _():
            out_ref[z % 2] = first_ref[...].astype(dtype)

        out_ref[(z + 1) % 2] = second_ref[...].astype(dtype)

    joined = run(
        body,
        [shaped((2, width, rows), dtype)],
        vmem=[blocks[0]] + list(got),
        micros=2,
        after=after,
    )[0]
    return joined[:, None].transpose(0, 1, 3, 2)


def from_quarters(value):
    few = value.shape[0] // 4
    return value.reshape(4, few, QUARTER).transpose(1, 0, 2).reshape(few, D)


def three_parts(value):
    terms = []
    for _ in range(3):
        term = lax.reduce_precision(value, 8, 7)
        terms.append(term.astype(BF))
        value = value - term
    return jnp.concatenate(terms)


def per_device(
    dp,
    mp,
    hidden_in,
    encoder_states,
    cotangent,
    self_qkv,
    self_out,
    cross_q,
    cross_kv,
    cross_out,
    fc_in,
    fc_out,
    ln_gain,
    ln_bias,
    token_lengths,
    audio_lengths,
    corpus_ids,
    corpus_weights,
):
    place = Place(dp, mp)
    length = hidden_in.shape[2]
    frames = encoder_states.shape[2]
    padded = -(-frames // CHUNK) * CHUNK
    rows = self_qkv.shape[0]

    encoded = lax.dynamic_index_in_dim(encoder_states[:, 0], place.micro, 0, keepdims=False)
    other = place.move(encoded, lambda xy, core, z: (xy, 1 - core, z) if core == z // 2 else None)
    first = ()
    if place.fast:
        shard = attention_shard(self_qkv, self_out, cross_kv, cross_q, cross_out)
        packed = pack_attention(place.column_out(shard), shard, (encoded,))
        w_self = w_cross = spread(place, packed)
        first = (shard,)
    else:
        quarter = lambda w: w.reshape(-1, 4, QUARTER).transpose(1, 0, 2).reshape(-1, QUARTER)
        flat = lambda w: w.reshape(rows, -1)
        w_self = attention_plain(
            place, jnp.concatenate([flat(self_qkv), quarter(self_out)], axis=1)
        )
        w_cross = attention_plain(
            place, jnp.concatenate([flat(cross_kv), cross_q, quarter(cross_out)], axis=1)
        )


    unit = unit_shard(place, fc_in, fc_out)
    if not place.fast:
        w_units = gather_units(place, unit)

    if place.fast:
        unit, packed = lax.optimization_barrier((unit, packed))
        column = [unit] + [place.swap_z(unit, k) for k in (1, 2, 3)]

    turned = lambda value: value[:, 0].transpose(0, 2, 1)
    numbers = jnp.concatenate([token_lengths.T, audio_lengths.T, corpus_ids.T])
    blocks = input_blocks(
        turned(hidden_in),
        three_parts(jnp.concatenate([ln_gain, ln_bias])),
        numbers,
        first,
    )
    got = place.rows_in(blocks)
    if place.fast:
        got, column = lax.optimization_barrier((got, column))
        stacked = stack_units(column, tuple(w_self[3:5]))
        w_units = spread(place, stacked)
    hidden, norms, nums = prepare(got, place.swap_core(got), corpus_weights)

    encoded = jnp.where(place.home == place.core, encoded, other)
    encoded = jnp.pad(encoded, ((0, padded - frames), (0, 0)))

    et = turn(encoded)
    part1, at, qkv, qt, kt, ot1, lse1 = self_forward(hidden, norms, nums, w_self, (et,))
    other1 = place.swap_core(part1)
    got = place.rows_in(turned_blocks(turned(cotangent), (at,)))
    kv, kvt = cross_memory(encoded, w_cross)
    part2, h1, ct, q2, qt2, ot2, lse2 = cross_forward(
        hidden, part1, other1, norms, nums, kv, kvt, w_cross
    )
    other2 = place.swap_core(part2)
    cot = prepare_cotangent(got, place.swap_core(got), (part2,))
    part3, h2, mt, slope, it = units_forward(h1, part2, other2, norms, w_units)
    other3 = place.swap_core(part3)
    part, d3, e3, dz, terms3, out_a, out_b = units_backward(
        h2, part3, other3, norms, nums, cot, slope, w_units
    )
    other = place.swap_core(part)
    g_units = units_grads(place, mt, dz, it, e3)
    came_units = leave_plane(place, g_units) if place.fast else None
    layer_got = place.rows_sent((out_a, out_b))
    layer_out = place.rows_joined((out_a, out_b), layer_got)
    part, d2, e2, dq2, dkv, terms2 = cross_backward(
        d3, h2, part, other, norms, nums, kv, kvt, q2, qt2, ot2, lse2, w_cross, layer_got
    )
    other = place.swap_core(part)
    passed = pass_on(g_units, came_units, (dq2,)) if place.fast else ()
    keep, send = encoder_grad(dkv, w_cross, passed)
    g_cross = attention_grads(place, et, dkv, ct, dq2, ot2, e2, (keep,))
    held = (g_cross[0],)
    if place.fast:
        came_cross = leave_plane(place, g_cross)
        onward_units = cross_plane(place, passed)
        kept, sent = units_sum(g_units, came_units, onward_units, held)
        came_units = place.swap_z(sent, 1)
        held = (kept,)
    encoder_blocks = finish_encoder(keep, place.swap_core(send), frames, held)
    encoder_got = place.rows_sent(encoder_blocks)
    held = encoder_blocks
    part, d1, e1, dqk, dv, terms1 = self_backward(
        d2, h1, part, other, norms, nums, qkv, qt, kt, ot1, lse1, w_self, held
    )
    other = place.swap_core(part)
    held = ()
    if place.fast:
        held = pass_on(g_cross, came_cross, (e1,))
        onward_cross = cross_plane(place, held)
    g_self = attention_grads(place, at, dqk, at, dv, ot1, e1, held)
    terms, out_a, out_b = finish_hidden(
        d1, hidden, part, other, norms, terms1, terms2, terms3, (g_self[0],)
    )
    hidden_got = place.rows_sent((out_a, out_b))
    if place.fast:
        came_self = leave_plane(place, g_self)
        second = add_second(kept, came_units, (terms,))
        last_units = place.swap_z(second, 2)
        cross_blocks = column_blocks(g_cross, came_cross, onward_cross, (), (second,))
        cross_got = place.column_back(cross_blocks)

    few = D // (place.dp * place.mp)
    if place.fast:
        passed = pass_on(g_self, came_self, (cross_blocks[0],))
        onward_self = cross_plane(place, passed)
        grad_encoder = join_rows(encoder_blocks, encoder_got, F32, passed)
        mine, sent, s_down = cut_units(kept, came_units, last_units, passed)
        s_up = join_units(place, mine, place.swap_core(sent))
        terms = terms + place.swap_xy(terms, 1)
        blocks = column_blocks(
            g_self, came_self, onward_self, (terms, place.swap_xy(terms, 2)), (s_down,)
        )
        g_qkv, g_out, g_gain, g_bias = finish_self(place.column_back(blocks), blocks[3], few)
        g_ckv, g_cq, g_cout = finish_cross(cross_got, cross_blocks[3], (blocks[0],))
        grad_hidden = join_rows((out_a, out_b), hidden_got, F32, (blocks[0],))
        g_qkv = g_qkv.transpose(1, 0, 2)
    else:
        s_up, s_down = scatter_units(place, g_units)
        grad_encoder = place.rows_joined(encoder_blocks, encoder_got).astype(F32)
        grad_hidden = place.rows_joined((out_a, out_b), hidden_got).astype(F32)
        s_cross = sum_plain(place, g_cross, True)
        s_self = sum_plain(place, g_self, True)
        terms = jnp.where(place.core == 0, terms, 0.0)
        terms = lax.psum(terms, AXES)
        shares = lax.dynamic_slice_in_dim(terms, (place.z * place.dp + place.d) * few, few, 1)
        g_gain, g_bias = shares[:4], shares[4:]
        g_qkv, g_out = s_self[:, : 3 * QUARTER], from_quarters(s_self[:, 3 * QUARTER :])
        g_ckv, g_cq = s_cross[:, :HALF], s_cross[:, HALF : 3 * QUARTER]
        g_cout = from_quarters(s_cross[:, 3 * QUARTER :])
    return (
        layer_out,
        grad_hidden,
        grad_encoder,
        g_qkv.reshape(rows, 3, QUARTER),
        g_out,
        g_cq,
        g_ckv.reshape(rows, 2, QUARTER),
        g_cout,
        s_up,
        s_down,
        g_gain,
        g_bias,
    )


def solution(mesh):
    dp, mp = mesh.shape["dp"], mesh.shape["mp"]
    finer = Mesh(mesh.devices.reshape(dp // 2, 2, mp), AXES)
    both = ("xy", "core")
    rows = P(None, both, None, "mp")
    columns = P(both, None, "mp")
    pairs = P(both, "mp")
    units = P(("mp",) + both, None)
    each = P(None, both)
    return jax.shard_map(
        partial(per_device, dp, mp),
        mesh=finer,
        in_specs=(
            rows,
            P(None, both, None, None),
            rows,
            columns,
            units,
            pairs,
            columns,
            units,
            pairs,
            units,
            P(None, "mp"),
            P(None, "mp"),
            each,
            each,
            each,
            P(),
        ),
        out_specs=(
            rows,
            rows,
            rows,
            columns,
            units,
            pairs,
            columns,
            units,
            pairs,
            units,
            P(None, ("mp",) + both),
            P(None, ("mp",) + both),
        ),
        check_vma=False,
    )
```

```python
from functools import partial

import jax
import jax.numpy as jnp
from jax import lax
from jax.experimental import pallas as pl
from jax.experimental.pallas import tpu as pltpu
from jax.sharding import Mesh, PartitionSpec as P

D = 768
HALF = 384
QUARTER = 192
HEAD_DIM = 64
HEADS = 6
CHUNK = 256
BF = jnp.bfloat16
F32 = jnp.float32
AXES = ("xy", "core", "mp")
CHIPS = ("xy", "mp")
VMEM = pl.BlockSpec(memory_space=pltpu.VMEM)
SMEM = pl.BlockSpec(memory_space=pltpu.SMEM)
ANY = pl.BlockSpec(memory_space=pl.ANY)
HBM = pl.BlockSpec(memory_space=pltpu.HBM)


def mm(left, right):
    return jnp.dot(left, right, preferred_element_type=F32)


def mm_t(left, right):
    return lax.dot_general(left, right, (((1,), (1,)), ((), ())), preferred_element_type=F32)


def shaped(shape, dtype=BF):
    return jax.ShapeDtypeStruct(shape, dtype)


def room(shape, dtype):
    item = jnp.dtype(dtype).itemsize
    shape = (1, 1) + tuple(shape)
    tile = 32 // item
    size = item * (-(-shape[-1] // 128) * 128) * (-(-shape[-2] // tile) * tile)
    for extent in shape[:-2]:
        size *= extent
    return size


def run(
    body, outs, vmem=(), hbm=(), smem=(), scratch=(), copies=0, micros=2, after=(), staged=False
):
    args = tuple(smem) + tuple(vmem) + tuple(hbm)
    count = len(args)
    scratch = list(scratch)
    if copies:
        scratch.append(pltpu.SemaphoreType.DMA((copies,)))
    need = sum(room(a.shape, a.dtype) for a in (tuple(vmem) if staged else ()) + tuple(outs))
    need += sum(room(a.shape, a.dtype) for a in scratch if a.memory_space == pltpu.VMEM)
    need = min(need + 12 * 1024 * 1024, 60 * 1024 * 1024)
    moved = sum(a.size * a.dtype.itemsize for a in args) + sum(
        o.size * o.dtype.itemsize for o in outs
    )
    skip = len(scratch)
    if staged:
        scratch += [pltpu.VMEM(a.shape, a.dtype) for a in vmem]
        scratch.append(pltpu.SemaphoreType.DMA((len(vmem),)))

    def whole(*refs):
        ins, rest = list(refs[:count]), refs[count + len(after) :]
        if staged:
            held = rest[len(outs) + skip : -1]
            rest, sems = rest[: len(outs) + skip], rest[-1]
            copies = Copies(sems)
            for i, target in enumerate(held):
                copies.start(ins[len(smem) + i], target)
                ins[len(smem) + i] = target
            copies.wait()
        body(*ins, *rest)

    place = HBM if staged else VMEM
    return pl.pallas_call(
        whole,
        out_shape=tuple(outs),
        in_specs=[SMEM] * len(smem) + [place] * len(vmem) + [ANY] * (len(hbm) + len(after)),
        out_specs=(VMEM,) * len(outs),
        scratch_shapes=scratch,
        compiler_params=pltpu.CompilerParams(vmem_limit_bytes=need),
        cost_estimate=pl.CostEstimate(
            flops=int(micros * 1.15e9), bytes_accessed=moved, transcendentals=0
        ),
    )(*args, *after)


class Copies:
    def __init__(self, sems):
        self.sems, self.open = sems, []

    def start(self, source, target):
        copy = pltpu.make_async_copy(source, target, self.sems.at[len(self.open)])
        copy.start()
        self.open.append(copy)

    def wait(self):
        for copy in self.open:
            copy.wait()


def where_am_i():
    return lax.axis_index("core"), lax.axis_index("xy"), lax.axis_index("mp")


class Place:
    def __init__(self, dp, mp):
        self.dp, self.mp = dp, mp
        self.chips = dp // 2
        self.fast = self.chips == 4
        self.z = lax.axis_index("mp")
        self.core = lax.axis_index("core")
        self.xy = lax.axis_index("xy")
        self.d = 2 * self.xy + self.core
        self.micro = self.z % 2
        self.home = self.z // 2

    def move(self, value, route):
        pairs = []
        for xy in range(self.chips):
            for core in range(2):
                for z in range(self.mp):
                    target = route(xy, core, z)
                    if target is not None:
                        txy, tcore, tz = target
                        pairs.append(
                            ((2 * xy + core) * self.mp + z, (2 * txy + tcore) * self.mp + tz)
                        )
        return lax.ppermute(value, AXES, pairs)

    def swap_core(self, value):
        return self.move(value, lambda xy, core, z: (xy, 1 - core, z))

    def swap_xy(self, value, bit):
        return self.move(value, lambda xy, core, z: (xy ^ bit, core, z))

    def swap_z(self, value, bit):
        return self.move(value, lambda xy, core, z: (xy, core, z ^ bit))

    def column_routes(self):
        def route(step, xy, core, z):
            user, j = z // 2, z % 2
            home = core == user
            near = lambda i: (xy, user, 2 * user + i)
            far = lambda i: (xy, user, 2 * (1 - user) + i)
            if step == 0:
                return near(1 - j) if home else far(1 - j)
            if step == 1:
                return far(j) if home else near(j)
            if step == 2:
                return far(1 - j) if home else near(1 - j)
            return None if home else far(j)

        return [partial(route, step) for step in range(4)]

    def column_out(self, shard):
        return [self.move(shard, route) for route in self.column_routes()]

    def column_back(self, blocks):
        got = []
        for block, route in zip(blocks, self.column_routes()):
            turned = {}
            for xy in range(self.chips):
                for core in range(2):
                    for z in range(self.mp):
                        target = route(xy, core, z)
                        if target is not None:
                            turned[target] = (xy, core, z)
            got.append(self.move(block, lambda xy, core, z: turned.get((xy, core, z))))
        return got

    def rows_in(self, blocks):
        def route(k, xy, core, z):
            target = (xy, z // 2, 2 * core + (z + k) % 2)
            return None if target == (xy, core, z) else target

        got = [self.move(block, partial(route, k)) for k, block in enumerate(blocks)]
        return jnp.stack([jnp.where(self.core == self.home, blocks[0], got[0]), got[1]])

    def rows_home(self, blocks):
        return self.rows_joined(blocks, self.rows_sent(blocks))

    def rows_sent(self, blocks):
        def route(k, xy, core, z):
            target = (xy, z // 2, 2 * core + (z % 2 - k) % 2)
            return None if target == (xy, core, z) else target

        return [self.move(block, partial(route, k)) for k, block in enumerate(blocks)]

    def rows_joined(self, blocks, got):
        got = [jnp.where(self.core == self.home, blocks[0], got[0]), got[1]]
        even = self.z % 2 == 0
        both = jnp.stack([jnp.where(even, got[0], got[1]), jnp.where(even, got[1], got[0])])
        return both[:, None].transpose(0, 1, 3, 2)


def norm(hidden):
    center = jnp.mean(hidden, axis=-1, keepdims=True)
    spread = jnp.mean(hidden * hidden, axis=-1, keepdims=True) - center * center
    inverse = lax.rsqrt(spread + 1e-05)
    return (hidden - center) * inverse, inverse


def norm_back(grad, unit, inverse, gain):
    scaled = grad * gain
    first = jnp.mean(scaled, axis=-1, keepdims=True)
    second = jnp.mean(scaled * unit, axis=-1, keepdims=True)
    terms = jnp.concatenate(
        [jnp.sum(grad * unit, axis=0, keepdims=True), jnp.sum(grad, axis=0, keepdims=True)], axis=0
    )
    return inverse * (scaled - first - unit * second), terms


def add_up(*terms):
    total = terms[0].astype(F32)
    for term in terms[1:]:
        total = total + term.astype(F32)
    return total


def input_blocks(hidden, terms, numbers, after=()):
    _, width, length = hidden.shape
    total = width + 32

    def body(numbers_ref, hidden_ref, terms_ref, *outs):
        _, _, z = where_am_i()
        lanes = lax.broadcasted_iota(jnp.int32, (8, length), 1)
        for k in range(2):
            micro = (z + k) % 2
            outs[k][0:width] = hidden_ref[micro]
            tok, aud = numbers_ref[0, micro], numbers_ref[1, micro]
            row = jnp.where(lanes == 0, tok // 256, jnp.where(lanes == 1, tok % 256, 0))
            row = jnp.where(lanes == 2, aud // 256, jnp.where(lanes == 3, aud % 256, row))
            row = jnp.where(lanes == 4, numbers_ref[2, micro], row)
            wide = jnp.concatenate(
                [terms_ref[...].astype(F32), jnp.zeros((24, length - width), F32)], axis=1
            )
            outs[k][width:total] = jnp.concatenate([wide, row.astype(F32)], axis=0).astype(BF)

    return run(
        body,
        [shaped((total, length))] * 2,
        smem=[numbers],
        vmem=[hidden, terms],
        micros=1,
        after=after,
    )


def turned_blocks(value, after=()):
    _, width, length = value.shape

    def body(ref, first_ref, second_ref):
        _, _, z = where_am_i()
        first_ref[...] = ref[z % 2]
        second_ref[...] = ref[(z + 1) % 2]

    return run(body, [shaped((width, length))] * 2, vmem=[value], micros=1, after=after)


def bring_blocks(copies, own_ref, other_ref, wide):
    core, _, z = where_am_i()
    found = []
    for k in range(2):
        slot = (z % 2 + k) % 2
        for ref, user in ((own_ref, core), (other_ref, 1 - core)):
            block = 2 * user + slot
            here = pl.ds(pl.multiple_of(block * QUARTER, QUARTER), QUARTER)
            copies.start(ref.at[k, pl.ds(0, QUARTER)], wide.at[here])
            found.append((ref.at[k], block))
    return found


def prepare_cotangent(own, other, after=()):
    length = own.shape[2]

    def body(own_ref, other_ref, cot_ref, wide, sems):
        copies = Copies(sems)
        bring_blocks(copies, own_ref, other_ref, wide)
        copies.wait()
        cot_ref[...] = wide[...].T

    return run(
        body,
        [shaped((length, D))],
        hbm=[own, other],
        scratch=[pltpu.VMEM((D, length), BF)],
        copies=4,
        micros=3,
        after=after,
    )[0]


def prepare(own, other, corpus_weights):
    length = own.shape[2]

    def body(
        weights_ref, own_ref, other_ref, hidden_ref, norms_ref, nums_ref, wide, extra, sems
    ):
        copies = Copies(sems)
        for ref, block in bring_blocks(copies, own_ref, other_ref, wide):
            copies.start(ref.at[pl.ds(QUARTER, 32)], extra.at[block])
        copies.wait()
        hidden_ref[...] = wide[...].T
        parts = [extra[b].astype(F32) for b in range(4)]
        norms_ref[...] = jnp.concatenate(
            [(e[0:8] + e[8:16] + e[16:24])[:, :QUARTER] for e in parts], axis=1
        )
        row = parts[0][24:25]
        tok = 256.0 * row[:, 0:1] + row[:, 1:2]
        aud = 256.0 * row[:, 2:3] + row[:, 3:4]
        weights = weights_ref[...]
        places = lax.broadcasted_iota(jnp.int32, weights.shape, 1).astype(F32)
        weight = jnp.sum(jnp.where(places == row[:, 4:5], weights, 0.0), axis=1, keepdims=True)
        index = lax.broadcasted_iota(jnp.int32, (8, 128), 0)
        nums_ref[...] = jnp.where(index == 0, tok, jnp.where(index == 1, aud, weight))

    return run(
        body,
        [shaped((length, D)), shaped((8, D), F32), shaped((8, 128), F32)],
        vmem=[corpus_weights.reshape(1, -1)],
        hbm=[own, other],
        scratch=[pltpu.VMEM((D, length), BF), pltpu.VMEM((4, 32, length), BF)],
        copies=8,
        micros=3,
    )


def quarters(value):
    return jnp.concatenate([value[:, p * QUARTER : (p + 1) * QUARTER] for p in range(4)], axis=0)


def attention_shard(self_qkv, self_out, cross_kv, cross_q, cross_out):
    rows = cross_q.shape[0]

    def body(qkv_ref, out_ref, kv_ref, q_ref, cout_ref, shard_ref):
        out = quarters(out_ref[...].astype(F32)).astype(BF)
        cout = quarters(cout_ref[...].astype(F32)).astype(BF)
        shard_ref[...] = jnp.concatenate(
            [qkv_ref[j] for j in range(3)] + [out, kv_ref[...], q_ref[...], cout], axis=1
        )

    return run(
        body,
        [shaped((rows, 2 * D))],
        vmem=[self_qkv.transpose(1, 0, 2), self_out, cross_kv.reshape(rows, -1), cross_q, cross_out],
        micros=2,
        staged=True,
    )[0]


def column_slots():
    core, _, z = where_am_i()
    j = z % 2
    home = 1 - jnp.abs(z // 2 - core)
    same = core + (1 - 2 * core) * (1 - home)
    return home == 1, (2 * (1 - j) + same, 2 * j + 1 - same, 2 * (1 - j) + 1 - same, 2 * j + same)


def bring_column(part_refs, own_ref, shards, sems):
    home, slots = column_slots()
    copies = Copies(sems)
    for k in range(3):
        copies.start(part_refs[k], shards.at[slots[k]])

    @pl.when(home)
    def _():
        copy = pltpu.make_async_copy(own_ref, shards.at[slots[3]], sems.at[3])
        copy.start()
        copy.wait()

    @pl.when(jnp.logical_not(home))
    def _():
        copy = pltpu.make_async_copy(part_refs[3], shards.at[slots[3]], sems.at[3])
        copy.start()
        copy.wait()

    copies.wait()


def pack_attention(parts, own, after):
    rows = own.shape[0]
    few = rows // 4

    def body(*refs):
        part_refs, own_ref, (out_ref, shards, sems) = refs[:4], refs[4], refs[5:]
        bring_column(part_refs, own_ref, shards, sems)
        for which in range(2):
            for cs in range(2):
                low, high = shards[cs], shards[2 + cs]

                def both(at):
                    at = at + which * D
                    return [low[:, at : at + QUARTER], high[:, at : at + QUARTER]]

                here = pl.ds(cs * rows, rows)
                out_ref[0, which, here, :] = jnp.concatenate(both(0) + both(QUARTER), axis=1)
                out_ref[1, which, here, 0:HALF] = jnp.concatenate(both(HALF), axis=1)
            at = 3 * QUARTER + which * D
            outs = [shards[i, :, at : at + QUARTER].astype(F32) for i in range(4)]
            stack = []
            for q in range(2):
                for i in range(4):
                    left = outs[i][2 * q * few : (2 * q + 1) * few]
                    right = outs[i][(2 * q + 1) * few : (2 * q + 2) * few]
                    stack.append(jnp.concatenate([left, right], axis=1))
            out_ref[1, which, :, HALF:D] = jnp.concatenate(stack, axis=0).astype(BF)

    return run(
        body,
        [shaped((2, 2, 2 * rows, D))],
        hbm=list(parts) + [own],
        scratch=[pltpu.VMEM((4, rows, 2 * D), BF)],
        copies=4,
        micros=2,
        after=after,
    )[0]


def unit_shard(place, fc_in, fc_out):
    rows = fc_in.shape[0]
    both = fc_in.reshape(rows, place.chips, 2, rows).transpose(2, 0, 1, 3).reshape(2, rows, HALF)
    kept = lax.dynamic_index_in_dim(both, place.core, 0, keepdims=False)
    sent = lax.dynamic_index_in_dim(both, 1 - place.core, 0, keepdims=False)
    came = place.swap_core(sent)
    first = place.core == 0
    left = jnp.concatenate([jnp.where(first, kept, came), jnp.where(first, came, kept)])
    right = jnp.concatenate([fc_out[:, :HALF], fc_out[:, HALF:]])
    return jnp.concatenate([left, right], axis=1)


def stack_units(blocks, after):
    rows = blocks[0].shape[0]

    def body(*refs):
        for k in range(4):
            refs[4][k // 2, k % 2] = refs[k][...]

    return run(body, [shaped((2, 2, rows, D))], vmem=blocks, micros=1.5, after=after)[0]


def gather_units(place, shard):
    whole = lax.all_gather(shard, CHIPS, axis=0)
    rows = shard.shape[0] // 2
    whole = whole.reshape(place.chips, place.mp, 2 * rows, D)
    up = whole[..., :HALF].transpose(0, 2, 1, 3).reshape(D, 2 * D)
    down = whole[..., HALF:].reshape(place.chips, place.mp, 2, rows, HALF)
    return [up, down.transpose(1, 0, 3, 2, 4).reshape(2 * D, D)]


def scatter_units(place, grads):
    total = lax.psum_scatter(grads, CHIPS, scatter_dimension=0, tiled=False)
    rows = total.shape[0] // 2
    kept = lax.dynamic_slice_in_dim(total, place.core * rows, rows, 0)
    sent = lax.dynamic_slice_in_dim(total[:, :HALF], (1 - place.core) * rows, rows, 0)
    came = place.swap_core(sent)
    kept = kept[:, :HALF]
    first = place.core == 0
    both = jnp.stack([jnp.where(first, kept, came), jnp.where(first, came, kept)])
    both = both.reshape(2, rows, place.chips, rows).transpose(1, 2, 0, 3).reshape(rows, D)
    down = jnp.concatenate([total[:rows, HALF:], total[rows:, HALF:]], axis=1)
    return both.astype(F32), down.astype(F32)


def spread(place, own):
    from_x = place.swap_xy(own, 1)
    from_y = place.swap_xy(own, 2)
    far_one = place.swap_xy(from_y[1], 1)
    far_zero = place.swap_xy(from_x[0], 2)
    return [own, from_x, from_y, far_zero, far_one]


def piece_views(refs, message, which, xy):
    own, from_x, from_y, far_zero, far_one = refs
    return [
        (own.at[which, message], xy),
        (from_x.at[which, message], xy ^ 1),
        (from_y.at[which, message], xy ^ 2),
        ((far_zero, far_one)[which].at[message], xy ^ 3),
    ]


def load_wide(copies, refs, message, which, xy, target, columns=None):
    if len(refs) != 5:
        copies.start(refs[which], target)
        return
    for view, chip in piece_views(refs, message, which, xy):
        rows = view.shape[0]
        if columns is not None:
            view = view.at[:, pl.ds(0, columns)]
        copies.start(view, target.at[pl.ds(pl.multiple_of(chip * rows, 16), rows)])


def load_out(copies, refs, message, xy, target):
    if len(refs) != 5:
        copies.start(refs[2], target)
        return
    for view, chip in piece_views(refs, message, 1, xy):
        rows = view.shape[0] // 4
        for q in range(2):
            for hi in range(2):
                copies.start(
                    view.at[pl.ds((2 * q + hi) * rows, rows), pl.ds(HALF, HALF)],
                    target.at[q, pl.ds(pl.multiple_of(hi * QUARTER + chip * rows, 16), rows)],
                )


def unit_views(refs):
    _, xy, z = where_am_i()
    views = []
    for part in range(2):
        for view, chip in [
            (refs[0].at[part], xy),
            (refs[1].at[part], xy ^ 1),
            (refs[2].at[part], xy ^ 2),
            (refs[3 + part], xy ^ 3),
        ]:
            for i in range(2):
                views.append((view.at[i], chip, z ^ (2 * part + i)))
    return views


def load_up(copies, refs, w_up):
    if len(refs) == 2:
        copies.start(refs[0], w_up)
        return
    for view, chip, z in unit_views(refs):
        rows = view.shape[0]
        copies.start(
            view.at[:, pl.ds(0, HALF)],
            w_up.at[
                pl.ds(pl.multiple_of(rows * chip, 16), rows), pl.ds(pl.multiple_of(z * HALF, HALF), HALF)
            ],
        )


def load_down(copies, refs, w_down):
    if len(refs) == 2:
        copies.start(refs[1], w_down)
        return
    for view, chip, z in unit_views(refs):
        rows = view.shape[0] // 2
        for q in range(2):
            copies.start(
                view.at[pl.ds(q * rows, rows), pl.ds(HALF, HALF)],
                w_down.at[
                    pl.ds(pl.multiple_of(z * HALF + chip * rows, 16), rows), pl.ds(q * HALF, HALF)
                ],
            )


ATTENTION_COPIES = 4 + 4 + 16
UP_COPIES = 16
DOWN_COPIES = 32


def gather_plain(place, shard):
    whole = lax.all_gather(shard, ("mp", "xy", "core"), axis=0)
    whole = whole.reshape((2, 2, place.dp) + shard.shape)
    return lax.dynamic_index_in_dim(whole, place.core, 0, keepdims=False)


def attention_plain(place, shard):
    mine = gather_plain(place, shard)
    rows = shard.shape[0]

    def columns(at, count):
        value = mine[..., at : at + count * QUARTER].reshape(2, D, count, QUARTER)
        return value.transpose(1, 2, 0, 3).reshape(D, count * HALF)

    out = mine[..., 3 * QUARTER :].reshape(2, place.dp, 2, 2, rows // 4, QUARTER)
    out = out.transpose(2, 0, 1, 4, 3, 5).reshape(2, HALF, HALF)
    return [columns(0, 2), columns(HALF, 1), out]


def head_rows(h):
    return pl.ds(pl.multiple_of(h * HEAD_DIM, HEAD_DIM), HEAD_DIM)


def low_parts(value):
    parts = []
    for _ in range(3):
        part = value.astype(BF)
        parts.append(part)
        value = value - part.astype(F32)
    return parts


def widened(count):
    return lambda rows: (
        lax.broadcasted_iota(jnp.int32, (rows, HEAD_DIM), 1) < count
    ).astype(F32).astype(BF)


def below(head, rows):
    blank = jnp.zeros((HEAD_DIM - len(rows), head.shape[1]), F32)
    rest = jnp.concatenate([row.astype(F32) for row in rows] + [blank], axis=0)
    return jnp.concatenate([head, rest.astype(BF)], axis=0)


def project(left, pair_ref):
    return jnp.concatenate([mm(left, pair_ref[0]), mm(left, pair_ref[1])], axis=1)


def project_t(left, pair_ref):
    return mm_t(left[:, :HALF], pair_ref[0]) + mm_t(left[:, HALF:], pair_ref[1])


def self_forward(hidden, norms, nums, weights, after=()):
    length = hidden.shape[0]

    def body(hidden_ref, norms_ref, nums_ref, *refs):
        w_refs, refs = refs[: len(weights)], refs[len(weights) :]
        part_ref, at_ref, qkv_ref, qt_ref, kt_ref, ot_ref, lse_ref = refs[:7]
        w_qk, w_v, w_out, vt, heads, bias, sems = refs[7:]
        _, xy, _ = where_am_i()
        copies = Copies(sems)
        load_wide(copies, w_refs, 0, 0, xy, w_qk)
        load_wide(copies, w_refs, 0, 1, xy, w_v, HALF)
        load_out(copies, w_refs, 0, xy, w_out)
        unit, _ = norm(hidden_ref[...].astype(F32))
        a = (unit * norms_ref[0:1] + norms_ref[4:5]).astype(BF)
        at_ref[...] = a.T
        keys = lax.broadcasted_iota(jnp.int32, (length, length), 0)
        queries = lax.broadcasted_iota(jnp.int32, (length, length), 1)
        allowed = (keys <= queries) & (keys.astype(F32) < nums_ref[0:1, 0:1])
        bias[...] = jnp.where(allowed, 0.0, -1e30)
        copies.wait()
        qk = mm(a, w_qk[...])
        q = (qk[:, :HALF].astype(BF).astype(F32) * HEAD_DIM ** (-0.5)).astype(BF)
        k = qk[:, HALF:].astype(BF)
        v = mm(a, w_v[...]).astype(BF)
        qkv_ref[:, 0:HALF] = q
        qkv_ref[:, HALF : 2 * HALF] = k
        qkv_ref[:, 2 * HALF :] = v
        qt_ref[...] = q.T
        kt_ref[...] = k.T
        vt[...] = v.T
        for h in range(HEADS):
            heads[h] = k[:, h * HEAD_DIM : (h + 1) * HEAD_DIM]

        def head(h, carry):
            s = mm(heads[h], qt_ref[head_rows(h), :]) + bias[...]
            top = jnp.max(s, axis=0, keepdims=True)
            p = jnp.exp(s - top)
            total = jnp.sum(p, axis=0, keepdims=True)
            o = mm(vt[head_rows(h), :], p.astype(BF))
            ot_ref[head_rows(h), :] = (o / total).astype(BF)
            lse_ref[h] = top + jnp.log(total)
            return carry

        lax.fori_loop(0, HEADS, head, 0)
        part_ref[...] = project(ot_ref[...].T, w_out).astype(BF)

    return run(
        body,
        [
            shaped((length, D)),
            shaped((D, length)),
            shaped((length, 3 * HALF)),
            shaped((HALF, length)),
            shaped((HALF, length)),
            shaped((HALF, length)),
            shaped((HEADS, 1, length), F32),
        ],
        vmem=[hidden, norms, nums],
        hbm=weights,
        scratch=[
            pltpu.VMEM((D, D), BF),
            pltpu.VMEM((D, HALF), BF),
            pltpu.VMEM((2, HALF, HALF), BF),
            pltpu.VMEM((HALF, length), BF),
            pltpu.VMEM((HEADS, length, HEAD_DIM), BF),
            pltpu.VMEM((length, length), F32),
        ],
        copies=ATTENTION_COPIES,
        micros=3,
        after=after,
    )


def turn(value, after=()):
    rows, columns = value.shape

    def body(ref, out_ref):
        for at in range(0, rows, CHUNK):
            out_ref[:, at : at + CHUNK] = ref[at : at + CHUNK, :].T

    return run(body, [shaped((columns, rows))], vmem=[value], micros=4, after=after)[0]


def cross_memory(encoded, weights):
    frames = encoded.shape[0]

    def body(enc_ref, *refs):
        w_refs, refs = refs[: len(weights)], refs[len(weights) :]
        kv_ref, kvt_ref, w_kv, sems = refs
        _, xy, _ = where_am_i()
        copies = Copies(sems)
        load_wide(copies, w_refs, 1, 0, xy, w_kv)
        copies.wait()

        def step(i, carry):
            here = pl.ds(pl.multiple_of(i * CHUNK, CHUNK), CHUNK)
            kv = mm(enc_ref[here, :], w_kv[...]).astype(BF)
            kv_ref[here, :] = kv
            kvt_ref[:, here] = kv.T
            return carry

        lax.fori_loop(0, frames // CHUNK, step, 0)

    return run(
        body,
        [shaped((frames, D)), shaped((D, frames))],
        vmem=[encoded],
        hbm=weights,
        scratch=[pltpu.VMEM((D, D), BF)],
        copies=4,
        micros=1,
    )


def residual(hidden_ref, mine_ref, other_ref):
    return hidden_ref[...].astype(F32) + (mine_ref[...].astype(F32) + other_ref[...].astype(F32))


def cross_forward(hidden, mine, other, norms, nums, kv, kvt, weights):
    length = hidden.shape[0]
    frames = kv.shape[0]

    def body(hidden_ref, mine_ref, other_ref, norms_ref, nums_ref, kv_ref, kvt_ref, *refs):
        w_refs, refs = refs[: len(weights)], refs[len(weights) :]
        part_ref, h_ref, ct_ref, q_ref, qt_ref, ot_ref, lse_ref = refs[:7]
        w_q, w_out, heads, values_t, scores, sems = refs[7:]
        _, xy, _ = where_am_i()
        copies = Copies(sems)
        load_wide(copies, w_refs, 1, 1, xy, w_q, HALF)
        load_out(copies, w_refs, 1, xy, w_out)
        h1 = residual(hidden_ref, mine_ref, other_ref)
        h_ref[...] = h1
        unit, _ = norm(h1)
        c = (unit * norms_ref[1:2] + norms_ref[5:6]).astype(BF)
        ct_ref[...] = c.T
        frame = lax.broadcasted_iota(jnp.int32, (frames, HEAD_DIM), 0).astype(F32)
        lane = lax.broadcasted_iota(jnp.int32, (frames, HEAD_DIM), 1)
        mask = jnp.where(frame < nums_ref[1:2, 0:1], 0.0, -1e30)
        beside = jnp.where(lane == 0, mask, 0.0).astype(BF)
        one = lax.broadcasted_iota(jnp.int32, (16, frames), 0)
        one = jnp.where(one == 0, 1.0, 0.0).astype(BF)
        for h in range(HEADS):
            keys = kv_ref[:, h * HEAD_DIM : (h + 1) * HEAD_DIM]
            heads[h] = jnp.concatenate([keys, beside], axis=1)
            values = kvt_ref[HALF + h * HEAD_DIM : HALF + (h + 1) * HEAD_DIM, :]
            values_t[h] = jnp.concatenate([values, one], axis=0)
        copies.wait()
        q = mm(c, w_q[...]).astype(BF)
        q = (q.astype(F32) * HEAD_DIM ** (-0.5)).astype(BF)
        q_ref[...] = q
        qt_ref[...] = q.T
        ones = jnp.ones((1, length), F32)

        def head(h, carry):
            qt = below(qt_ref[head_rows(h), :], [ones])
            top = None
            for at in range(0, frames, CHUNK):
                s = mm(heads[h, at : at + CHUNK], qt)
                scores[at : at + CHUNK] = s
                high = jnp.max(s, axis=0, keepdims=True)
                top = high if top is None else jnp.maximum(top, high)
            o = None
            for at in range(0, frames, CHUNK):
                p = jnp.exp(scores[at : at + CHUNK] - top).astype(BF)
                more = mm(values_t[h, :, at : at + CHUNK], p)
                o = more if o is None else o + more
            total = o[HEAD_DIM : HEAD_DIM + 1]
            ot_ref[head_rows(h), :] = (o[:HEAD_DIM] / total).astype(BF)
            lse_ref[h] = top + jnp.log(total)
            return carry

        lax.fori_loop(0, HEADS, head, 0)
        part_ref[...] = project(ot_ref[...].T, w_out).astype(BF)

    return run(
        body,
        [
            shaped((length, D)),
            shaped((length, D), F32),
            shaped((D, length)),
            shaped((length, HALF)),
            shaped((HALF, length)),
            shaped((HALF, length)),
            shaped((HEADS, 1, length), F32),
        ],
        vmem=[hidden, mine, other, norms, nums, kv, kvt],
        hbm=weights,
        scratch=[
            pltpu.VMEM((D, HALF), BF),
            pltpu.VMEM((2, HALF, HALF), BF),
            pltpu.VMEM((HEADS, frames, 2 * HEAD_DIM), BF),
            pltpu.VMEM((HEADS, HEAD_DIM + 16, frames), BF),
            pltpu.VMEM((frames, length), F32),
        ],
        copies=4 + 16,
        micros=2,
    )


def units_forward(hidden, mine, other, norms, weights):
    length = hidden.shape[0]

    def body(hidden_ref, mine_ref, other_ref, norms_ref, *refs):
        w_refs, refs = refs[: len(weights)], refs[len(weights) :]
        part_ref, h_ref, mt_ref, slope_ref, it_ref = refs[:5]
        w_up, w_down, inner, late_sems, sems = refs[5:]
        _, xy, _ = where_am_i()
        copies = Copies(sems)
        load_up(copies, w_refs, w_up)
        late = Copies(late_sems)
        load_down(late, w_refs, w_down)
        h2 = residual(hidden_ref, mine_ref, other_ref)
        h_ref[...] = h2
        unit, _ = norm(h2)
        m = (unit * norms_ref[2:3] + norms_ref[6:7]).astype(BF)
        mt_ref[...] = m.T
        copies.wait()
        for at in range(0, 2 * D, CHUNK):
            here = slice(at, at + CHUNK)
            z = mm(m, w_up[:, here])
            share = 0.5 * (1.0 + lax.erf(z * 0.7071067811865476))
            slope = share + z * (0.3989422804014327 * jnp.exp(-0.5 * z * z))
            value = (z * share).astype(BF)
            inner[:, here] = value
            it_ref[here, :] = value.T
            slope_ref[:, here] = slope.astype(BF)
        late.wait()
        for at in range(0, D, CHUNK):
            part_ref[:, at : at + CHUNK] = mm(inner[...], w_down[:, at : at + CHUNK]).astype(BF)

    return run(
        body,
        [
            shaped((length, D)),
            shaped((length, D), F32),
            shaped((D, length)),
            shaped((length, 2 * D)),
            shaped((2 * D, length)),
        ],
        vmem=[hidden, mine, other, norms],
        hbm=weights,
        scratch=[
            pltpu.VMEM((D, 2 * D), BF),
            pltpu.VMEM((2 * D, D), BF),
            pltpu.VMEM((length, 2 * D), BF),
            pltpu.SemaphoreType.DMA((DOWN_COPIES,)),
        ],
        copies=UP_COPIES,
        micros=9,
    )


def store_blocks(value, blocks, first_ref, second_ref):
    core, _, z = where_am_i()
    for b in range(4):
        blocks[b] = value[:, b * QUARTER : (b + 1) * QUARTER]
    first_ref[...] = blocks[2 * core + z % 2].T
    second_ref[...] = blocks[2 * core + (z + 1) % 2].T


def units_backward(hidden, mine, other, norms, nums, cot, slope, weights):
    length = hidden.shape[0]

    def body(hidden_ref, mine_ref, other_ref, norms_ref, nums_ref, cot_ref, slope_ref, *refs):
        w_refs, refs = refs[: len(weights)], refs[len(weights) :]
        part_ref, d_ref, e_ref, dz_ref, terms_ref, first_ref, second_ref = refs[:7]
        w_up, w_down, blocks, late_sems, sems = refs[7:]
        _, xy, _ = where_am_i()
        copies = Copies(sems)
        load_down(copies, w_refs, w_down)
        late = Copies(late_sems)
        load_up(late, w_refs, w_up)
        unit, inverse = norm(residual(hidden_ref, mine_ref, other_ref))
        final = (unit * norms_ref[3:4] + norms_ref[7:8]).astype(BF)
        store_blocks(final, blocks, first_ref, second_ref)
        live = lax.broadcasted_iota(jnp.int32, (length, 1), 0).astype(F32) < nums_ref[0:1, 0:1]
        grad = cot_ref[...].astype(F32) * jnp.where(live, nums_ref[2:3, 0:1], 0.0)
        d3, terms = norm_back(grad, unit, inverse, norms_ref[3:4])
        d_ref[...] = d3
        terms_ref[...] = terms
        e = d3.astype(BF)
        e_ref[...] = e
        copies.wait()
        for at in range(0, 2 * D, CHUNK):
            here = slice(at, at + CHUNK)
            d_inner = mm_t(e, w_down[here, :])
            dz_ref[:, here] = (slope_ref[:, here].astype(F32) * d_inner).astype(BF)
        late.wait()
        for at in range(0, D, CHUNK):
            out = mm_t(dz_ref[...], w_up[at : at + CHUNK, :])
            part_ref[:, at : at + CHUNK] = out.astype(BF)

    return run(
        body,
        [
            shaped((length, D)),
            shaped((length, D), F32),
            shaped((length, D)),
            shaped((length, 2 * D)),
            shaped((2, D), F32),
            shaped((QUARTER, length)),
            shaped((QUARTER, length)),
        ],
        vmem=[hidden, mine, other, norms, nums, cot, slope],
        hbm=weights,
        scratch=[
            pltpu.VMEM((D, 2 * D), BF),
            pltpu.VMEM((2 * D, D), BF),
            pltpu.VMEM((4, length, QUARTER), BF),
            pltpu.SemaphoreType.DMA((UP_COPIES,)),
        ],
        copies=DOWN_COPIES,
        micros=10,
    )


def step_back(d_ref, hidden_ref, mine_ref, other_ref, gain):
    unit, inverse = norm(hidden_ref[...].astype(F32))
    grad = mine_ref[...].astype(F32) + other_ref[...].astype(F32)
    part, terms = norm_back(grad, unit, inverse, gain)
    return d_ref[...] + part, terms


def cross_backward(
    d, hidden, mine, other, norms, nums, kv, kvt, q, qt, ot, lse, weights, after=()
):
    length = hidden.shape[0]
    frames = kv.shape[0]

    def body(
        d_ref, hidden_ref, mine_ref, other_ref, norms_ref, nums_ref, kv_ref, kvt_ref, q_ref,
        qt_ref, ot_ref, lse_ref, *refs
    ):
        w_refs, refs = refs[: len(weights)], refs[len(weights) :]
        part_ref, d_out_ref, e_ref, dq_ref, dkv_ref, terms_ref = refs[:6]
        w_q, w_out, keys, values, queries, grads, dot_t, dk_h, dv_h, dqt, sems = refs[6:]
        _, xy, _ = where_am_i()
        copies = Copies(sems)
        load_wide(copies, w_refs, 1, 1, xy, w_q, HALF)
        load_out(copies, w_refs, 1, xy, w_out)
        d2, terms = step_back(d_ref, hidden_ref, mine_ref, other_ref, norms_ref[2:3])
        d_out_ref[...] = d2
        terms_ref[...] = terms
        e = d2.astype(BF)
        e_ref[...] = e
        frame = lax.broadcasted_iota(jnp.int32, (frames, HEAD_DIM), 0).astype(F32)
        lane = lax.broadcasted_iota(jnp.int32, (frames, HEAD_DIM), 1)
        mask = jnp.where(frame < nums_ref[1:2, 0:1], 0.0, -1e30)
        beside = jnp.where(lane == 0, mask, jnp.where(lane < 4, 1.0, 0.0)).astype(BF)
        three = widened(3)(frames)
        for h in range(HEADS):
            lanes = slice(h * HEAD_DIM, (h + 1) * HEAD_DIM)
            keys[h] = jnp.concatenate([kv_ref[:, lanes], beside], axis=1)
            value = kv_ref[:, HALF + h * HEAD_DIM : HALF + (h + 1) * HEAD_DIM]
            values[h] = jnp.concatenate([value, three], axis=1)
            queries[h] = q_ref[:, lanes]
        copies.wait()
        d_mixed = project_t(e, w_out).astype(BF)
        dot_t[...] = d_mixed.T
        for h in range(HEADS):
            grads[h] = d_mixed[:, h * HEAD_DIM : (h + 1) * HEAD_DIM]
        ones = jnp.ones((1, length), F32)

        def head(h, carry):
            rows = head_rows(h)
            do_t = dot_t[rows, :]
            q_n, do_n = queries[h], grads[h]
            delta = jnp.sum(do_t.astype(F32) * ot_ref[rows, :].astype(F32), axis=0, keepdims=True)
            q_t = below(qt_ref[rows, :], [ones] + low_parts(-lse_ref[h]))
            do_t = below(do_t, low_parts(-delta))
            total = None
            for at in range(0, frames, CHUNK):
                here = slice(at, at + CHUNK)
                p = jnp.exp(mm(keys[h, here], q_t))
                ds = (p * mm(values[h, here], do_t)).astype(BF)
                dv_h[h, here] = mm(p.astype(BF), do_n).astype(BF)
                dk_h[h, here] = mm(ds, q_n).astype(BF)
                more = mm(kvt_ref[rows, here], ds)
                total = more if total is None else total + more
            dqt[rows, :] = (total * HEAD_DIM ** (-0.5)).astype(BF)
            return carry

        lax.fori_loop(0, HEADS, head, 0)
        dq = dqt[...].T
        dq_ref[...] = dq
        part_ref[...] = mm_t(dq, w_q[...]).astype(BF)
        for h in range(HEADS):
            lanes = slice(h * HEAD_DIM, (h + 1) * HEAD_DIM)
            dkv_ref[:, lanes] = dk_h[h]
            dkv_ref[:, HALF + h * HEAD_DIM : HALF + (h + 1) * HEAD_DIM] = dv_h[h]

    return run(
        body,
        [
            shaped((length, D)),
            shaped((length, D), F32),
            shaped((length, D)),
            shaped((length, HALF)),
            shaped((frames, D)),
            shaped((2, D), F32),
        ],
        vmem=[d, hidden, mine, other, norms, nums, kv, kvt, q, qt, ot, lse],
        hbm=weights,
        scratch=[
            pltpu.VMEM((D, HALF), BF),
            pltpu.VMEM((2, HALF, HALF), BF),
            pltpu.VMEM((HEADS, frames, 2 * HEAD_DIM), BF),
            pltpu.VMEM((HEADS, frames, 2 * HEAD_DIM), BF),
            pltpu.VMEM((HEADS, length, HEAD_DIM), BF),
            pltpu.VMEM((HEADS, length, HEAD_DIM), BF),
            pltpu.VMEM((HALF, length), BF),
            pltpu.VMEM((HEADS, frames, HEAD_DIM), BF),
            pltpu.VMEM((HEADS, frames, HEAD_DIM), BF),
            pltpu.VMEM((HALF, length), BF),
        ],
        copies=4 + 16,
        micros=22,
        after=after,
    )


def self_backward(d, hidden, mine, other, norms, nums, qkv, qt, kt, ot, lse, weights, after=()):
    length = hidden.shape[0]

    def body(
        d_ref, hidden_ref, mine_ref, other_ref, norms_ref, nums_ref, qkv_ref, qt_ref, kt_ref,
        ot_ref, lse_ref, *refs
    ):
        w_refs, refs = refs[: len(weights)], refs[len(weights) :]
        part_ref, d_out_ref, e_ref, dqk_ref, dv_ref, terms_ref = refs[:6]
        w_qk, w_v, w_out, queries_h, keys, values, grads, dot_t, dk_h, dv_h, dqt, bias, sems = refs[6:]
        _, xy, _ = where_am_i()
        copies = Copies(sems)
        load_out(copies, w_refs, 0, xy, w_out)
        load_wide(copies, w_refs, 0, 0, xy, w_qk)
        load_wide(copies, w_refs, 0, 1, xy, w_v, HALF)
        d1, terms = step_back(d_ref, hidden_ref, mine_ref, other_ref, norms_ref[1:2])
        d_out_ref[...] = d1
        terms_ref[...] = terms
        e = d1.astype(BF)
        e_ref[...] = e
        places = lax.broadcasted_iota(jnp.int32, (length, length), 0)
        queries = lax.broadcasted_iota(jnp.int32, (length, length), 1)
        allowed = (places <= queries) & (places.astype(F32) < nums_ref[0:1, 0:1])
        bias[...] = jnp.where(allowed, 0.0, -1e30)
        three = widened(3)(length)
        for h in range(HEADS):
            at = h * HEAD_DIM
            queries_h[h] = qkv_ref[:, at : at + HEAD_DIM]
            key = qkv_ref[:, HALF + at : HALF + at + HEAD_DIM]
            keys[h] = jnp.concatenate([key, three], axis=1)
            value = qkv_ref[:, 2 * HALF + at : 2 * HALF + at + HEAD_DIM]
            values[h] = jnp.concatenate([value, three], axis=1)
        copies.wait()
        d_mixed = project_t(e, w_out).astype(BF)
        dot_t[...] = d_mixed.T
        for h in range(HEADS):
            grads[h] = d_mixed[:, h * HEAD_DIM : (h + 1) * HEAD_DIM]

        def head(h, carry):
            rows = head_rows(h)
            do_t, do_n = dot_t[rows, :], grads[h]
            delta = jnp.sum(do_t.astype(F32) * ot_ref[rows, :].astype(F32), axis=0, keepdims=True)
            q_t = below(qt_ref[rows, :], low_parts(-lse_ref[h]))
            do_t = below(do_t, low_parts(-delta))
            p = jnp.exp(mm(keys[h], q_t) + bias[...])
            ds = (p * mm(values[h], do_t)).astype(BF)
            dv_h[h] = mm(p.astype(BF), do_n).astype(BF)
            dk_h[h] = mm(ds, queries_h[h]).astype(BF)
            dqt[rows, :] = (mm(kt_ref[rows, :], ds) * HEAD_DIM ** (-0.5)).astype(BF)
            return carry

        lax.fori_loop(0, HEADS, head, 0)
        dqk_ref[:, 0:HALF] = dqt[...].T
        for h in range(HEADS):
            lanes = slice(HALF + h * HEAD_DIM, HALF + (h + 1) * HEAD_DIM)
            dqk_ref[:, lanes] = dk_h[h]
            dv_ref[:, h * HEAD_DIM : (h + 1) * HEAD_DIM] = dv_h[h]
        out = mm_t(dqk_ref[...], w_qk[...]) + mm_t(dv_ref[...], w_v[...])
        part_ref[...] = out.astype(BF)

    return run(
        body,
        [
            shaped((length, D)),
            shaped((length, D), F32),
            shaped((length, D)),
            shaped((length, D)),
            shaped((length, HALF)),
            shaped((2, D), F32),
        ],
        vmem=[d, hidden, mine, other, norms, nums, qkv, qt, kt, ot, lse],
        hbm=weights,
        scratch=[
            pltpu.VMEM((D, D), BF),
            pltpu.VMEM((D, HALF), BF),
            pltpu.VMEM((2, HALF, HALF), BF),
            pltpu.VMEM((HEADS, length, HEAD_DIM), BF),
            pltpu.VMEM((HEADS, length, 2 * HEAD_DIM), BF),
            pltpu.VMEM((HEADS, length, 2 * HEAD_DIM), BF),
            pltpu.VMEM((HEADS, length, HEAD_DIM), BF),
            pltpu.VMEM((HALF, length), BF),
            pltpu.VMEM((HEADS, length, HEAD_DIM), BF),
            pltpu.VMEM((HEADS, length, HEAD_DIM), BF),
            pltpu.VMEM((HALF, length), BF),
            pltpu.VMEM((length, length), F32),
        ],
        copies=ATTENTION_COPIES,
        micros=12,
        staged=True,
        after=after,
    )


def finish_hidden(d, hidden, mine, other, norms, terms1, terms2, terms3, after=()):
    length = hidden.shape[0]

    def body(
        d_ref, hidden_ref, mine_ref, other_ref, norms_ref, one, two, three, terms_ref, first_ref,
        second_ref, blocks
    ):
        d0, terms = step_back(d_ref, hidden_ref, mine_ref, other_ref, norms_ref[0:1])
        store_blocks(d0.astype(BF), blocks, first_ref, second_ref)
        for j in range(2):
            here = slice(j, j + 1)
            terms_ref[4 * j : 4 * j + 4] = jnp.concatenate(
                [terms[here], one[here], two[here], three[here]], axis=0
            )

    return run(
        body,
        [shaped((8, D), F32), shaped((QUARTER, length)), shaped((QUARTER, length))],
        vmem=[d, hidden, mine, other, norms, terms1, terms2, terms3],
        scratch=[pltpu.VMEM((4, length, QUARTER), BF)],
        micros=4,
        after=after,
    )


def finish_encoder(keep, other, frames, after=()):
    def body(keep_ref, other_ref, first_ref, second_ref):
        _, _, z = where_am_i()
        for ref, k in ((first_ref, 0), (second_ref, 1)):
            here = pl.ds(pl.multiple_of(((z + k) % 2) * QUARTER, QUARTER), QUARTER)
            total = keep_ref[here, :].astype(F32) + other_ref[here, :].astype(F32)
            ref[...] = total.astype(BF)[:, :frames]

    return run(
        body,
        [shaped((QUARTER, frames)), shaped((QUARTER, frames))],
        vmem=[keep, other],
        micros=2,
        after=after,
    )


def block_plan(place):
    if not place.fast:
        return 1, (((1, 0, 0),), ((1, 0, 0),))
    first = ((1, 0, 0), (0, 0, 1), (1, 1, 2), (0, 1, 3))
    second = ((1, 0, 0), (1, 1, 1), (0, 0, 2), (0, 1, 3))
    return 4, (first, second)


def grad_outputs(place, shape):
    if place.fast:
        return [shaped((2,) + shape)] * 4
    return [shaped((1,) + shape)] * 4


def units_grads(place, mt, dz, it, e):
    chips = place.chips
    rows = D // (2 * chips)
    _, plan = block_plan(place)

    def body(mt_ref, dz_ref, it_ref, e_ref, *outs):
        _, xy, _ = where_am_i()
        for output, slot, offset in plan[1]:
            chip = xy ^ offset
            for z in range(4):
                here = pl.ds(pl.multiple_of(z * HALF + chip * rows, 16), rows)
                outs[2 + output][slot, z] = mm(it_ref[here, :], e_ref[...]).astype(BF)
        for output, slot, offset in plan[0]:
            here = pl.ds(pl.multiple_of((xy ^ offset) * 2 * rows, 16), 2 * rows)
            left = mm(mt_ref[here, :], dz_ref[...]).astype(BF)
            for z in range(4):
                outs[output][slot, z] = left[:, z * HALF : (z + 1) * HALF]

    def plain(mt_ref, dz_ref, it_ref, e_ref, left_ref, right_ref):
        left_ref[...] = mm(mt_ref[...], dz_ref[...]).astype(BF)
        right_ref[...] = mm(it_ref[...], e_ref[...]).astype(BF)

    if place.fast:
        first, second = shaped((2, 4, 2 * rows, HALF)), shaped((2, 4, rows, D))
        return run(
            body, [first, first, second, second], vmem=[mt, dz, it, e], micros=6
        )
    left, right = run(
        plain, [shaped((D, 2 * D)), shaped((2 * D, D))], vmem=[mt, dz, it, e], micros=7
    )
    left = left.reshape(chips, 2 * rows, 4, HALF).transpose(0, 2, 1, 3)
    right = right.reshape(4, chips, rows, 2, HALF).transpose(1, 0, 3, 2, 4)
    whole = jnp.concatenate([left, right.reshape(chips, 4, 2 * rows, HALF)], axis=-1)
    return whole.reshape(4 * chips, 2 * rows, D)


def units_sum(grads, came, onward, after):
    rows = grads[3].shape[2]

    def body(*refs):
        ins, (kept_ref, sent_ref, left, right, blocks, sems) = refs[:6], refs[6:]
        _, _, mp = where_am_i()
        copies = Copies(sems)
        for i, ref in enumerate(ins):
            target = (left if i < 3 else right).at[i % 3]
            copies.start(ref if i % 3 == 2 else ref.at[0], target)
        copies.wait()
        for z in range(4):
            blocks[z, :, 0:HALF] = add_up(*[left[i, z] for i in range(3)]).astype(BF)
            down = add_up(*[right[i, z] for i in range(3)]).astype(BF)
            blocks[z, 0:rows, HALF:D] = down[:, :HALF]
            blocks[z, rows : 2 * rows, HALF:D] = down[:, HALF:]
        for i in range(2):
            kept_ref[i] = blocks[mp ^ (2 * i)]
            sent_ref[i] = blocks[mp ^ (2 * i + 1)]

    return run(
        body,
        [shaped((2, 2 * rows, D)), shaped((2, 2 * rows, D))],
        hbm=[grads[1], came[0], onward[0], grads[3], came[1], onward[1]],
        scratch=[
            pltpu.VMEM((3, 4, 2 * rows, HALF), BF),
            pltpu.VMEM((3, 4, rows, D), BF),
            pltpu.VMEM((4, 2 * rows, D), BF),
        ],
        copies=6,
        micros=3,
        after=after,
    )


def add_second(kept, came, after):
    def body(kept_ref, came_ref, out_ref, held, sems):
        copies = Copies(sems)
        copies.start(kept_ref.at[1], held.at[0])
        copies.start(came_ref.at[1], held.at[1])
        copies.wait()
        out_ref[...] = add_up(held[0], held[1]).astype(BF)

    shape = kept.shape[1:]
    return run(
        body,
        [shaped(shape)],
        hbm=[kept, came],
        scratch=[pltpu.VMEM((2,) + shape, BF)],
        copies=2,
        micros=1,
        after=after,
    )[0]


def cut_units(kept, came, last, after):
    rows = last.shape[0] // 2

    def body(kept_ref, came_ref, last_ref, mine_ref, sent_ref, down_ref, held, sems):
        core, _, _ = where_am_i()
        copies = Copies(sems)
        copies.start(kept_ref.at[0], held.at[0])
        copies.start(came_ref.at[0], held.at[1])
        copies.start(last_ref, held.at[2])
        copies.wait()
        mine = pl.ds(pl.multiple_of(core * rows, 16), rows)
        theirs = pl.ds(pl.multiple_of((1 - core) * rows, 16), rows)
        mine_ref[...] = add_up(*[held[i, mine, 0:HALF] for i in range(3)]).astype(BF)
        sent_ref[...] = add_up(*[held[i, theirs, 0:HALF] for i in range(3)]).astype(BF)
        down_ref[:, 0:HALF] = add_up(*[held[i, 0:rows, HALF:D] for i in range(3)])
        down_ref[:, HALF:D] = add_up(*[held[i, rows : 2 * rows, HALF:D] for i in range(3)])

    return run(
        body,
        [shaped((rows, HALF)), shaped((rows, HALF)), shaped((rows, D), F32)],
        hbm=[kept, came, last],
        scratch=[pltpu.VMEM((3, 2 * rows, D), BF)],
        copies=3,
        micros=1,
        after=after,
    )


def join_units(place, kept, came):
    rows = kept.shape[0]

    def body(kept_ref, came_ref, up_ref, both):
        core, _, _ = where_am_i()
        both[core] = kept_ref[...]
        both[1 - core] = came_ref[...]
        blocks = []
        for chip in range(place.chips):
            for parity in range(2):
                blocks.append(both[parity, :, chip * rows : (chip + 1) * rows].astype(F32))
        up_ref[...] = jnp.concatenate(blocks, axis=1)

    return run(
        body,
        [shaped((rows, D), F32)],
        vmem=[kept, came],
        scratch=[pltpu.VMEM((2, rows, HALF), BF)],
        micros=1,
    )[0]


def attention_grads(place, wide_left, wide_right, left, right, ot, e, after=()):
    count, plan = block_plan(place)
    rows = D // count
    few = rows // 4

    def body(wide_left_ref, wide_right_ref, left_ref, right_ref, ot_ref, e_ref, *outs):
        _, xy, _ = where_am_i()
        for output, slot, offset in plan[0]:
            chip = xy ^ offset if count > 1 else 0
            here = pl.ds(pl.multiple_of(chip * rows, 16), rows)
            outs[output][slot] = mm(wide_left_ref[here, :], wide_right_ref[...]).astype(BF)
        for output, slot, offset in plan[1]:
            chip = xy ^ offset if count > 1 else 0
            here = pl.ds(pl.multiple_of(chip * rows, 16), rows)
            target = outs[2 + output]
            target[slot, :, 0:HALF] = mm(left_ref[here, :], right_ref[...]).astype(BF)
            for hi in range(2):
                here = pl.ds(pl.multiple_of(hi * QUARTER + chip * few, 16), few)
                both = mm(ot_ref[here, :], e_ref[...]).astype(BF)
                for q in range(2):
                    at = (2 * q + hi) * few
                    target[slot, at : at + few, HALF:D] = both[:, q * HALF : (q + 1) * HALF]

    return run(
        body,
        grad_outputs(place, (rows, D)),
        vmem=[wide_left, wide_right, left, right, ot, e],
        micros=6,
        after=after,
    )


def encoder_grad(dkv, weights, after=()):
    padded = dkv.shape[0]

    def body(dkv_ref, *refs):
        w_refs, (keep_ref, send_ref, w_kv, sems) = refs[: len(weights)], refs[len(weights) :]
        core, xy, _ = where_am_i()
        copies = Copies(sems)
        load_wide(copies, w_refs, 1, 0, xy, w_kv)
        copies.wait()
        mine = pl.ds(pl.multiple_of(core * HALF, HALF), HALF)
        theirs = pl.ds(pl.multiple_of((1 - core) * HALF, HALF), HALF)
        for ref, rows in ((send_ref, theirs), (keep_ref, mine)):
            for at in range(0, padded, CHUNK):
                value = mm_t(w_kv[rows, :], dkv_ref[at : at + CHUNK, :])
                ref[:, at : at + CHUNK] = value.astype(BF)

    return run(
        body,
        [shaped((HALF, padded)), shaped((HALF, padded))],
        vmem=[dkv],
        hbm=weights,
        scratch=[pltpu.VMEM((D, D), BF)],
        copies=4,
        micros=3.5,
        after=after,
    )


def leave_plane(place, grads):
    return [place.swap_xy(grads[0], 1), place.swap_xy(grads[2], 2)]


def pass_on(grads, came, after):
    shapes = [grads[1].shape[1:], grads[3].shape[1:]]

    def body(stay0, came0, stay1, came1, out0, out1, held0, held1, sems):
        copies = Copies(sems)
        for i, ref in enumerate((stay0, came0, stay1, came1)):
            copies.start(ref.at[1], (held0 if i < 2 else held1).at[i % 2])
        copies.wait()
        out0[...] = add_up(held0[0], held0[1]).astype(BF)
        out1[...] = add_up(held1[0], held1[1]).astype(BF)

    return run(
        body,
        [shaped(shape) for shape in shapes],
        hbm=[grads[1], came[0], grads[3], came[1]],
        scratch=[pltpu.VMEM((2,) + shape, BF) for shape in shapes],
        copies=4,
        micros=1,
        after=after,
    )


def cross_plane(place, onward):
    return [place.swap_xy(onward[0], 2), place.swap_xy(onward[1], 1)]


def column_blocks(grads, came, onward, norm_terms=(), after=()):
    shape = onward[0].shape
    rows = shape[-2] // 2
    width = D
    few = rows // 4
    extra = 16 if norm_terms else 0

    def body(*refs):
        terms_refs, refs = refs[: len(norm_terms)], refs[len(norm_terms) :]
        ins, outs, (held, shards, sems) = refs[:6], refs[6:-3], refs[-3:]
        home, slots = column_slots()
        copies = Copies(sems)
        for i, ref in enumerate(ins):
            copies.start(ref if i % 3 == 2 else ref.at[0], held.at[i])
        copies.wait()
        sums = [add_up(held[3 * part], held[3 * part + 1], held[3 * part + 2]) for part in range(2)]
        for hi in range(2):
            for cs in range(2):
                here = slice(cs * rows, (cs + 1) * rows)
                lanes = slice(hi * QUARTER, (hi + 1) * QUARTER)
                lanes_two = slice(HALF + hi * QUARTER, HALF + (hi + 1) * QUARTER)
                outs_rows = []
                for p in range(4):
                    at = (2 * (p // 2) + hi) * 2 * few + cs * few
                    side = HALF + (p % 2) * QUARTER
                    outs_rows.append(sums[1][at : at + few, side : side + QUARTER])
                value = jnp.concatenate(
                    [
                        sums[0][here, lanes],
                        sums[0][here, lanes_two],
                        sums[1][here, lanes],
                        jnp.concatenate(outs_rows, axis=0),
                    ],
                    axis=1,
                )
                shards[2 * hi + cs, :rows] = value.astype(BF)
        if norm_terms:
            core, xy, _ = where_am_i()
            terms = add_up(*[ref[...] for ref in terms_refs])
            terms = jnp.concatenate([terms, jnp.zeros_like(terms)], axis=0).astype(BF)
            feature = lax.broadcasted_iota(jnp.int32, (D, D), 0)
            lane = lax.broadcasted_iota(jnp.int32, (D, D), 1)
            for hi in range(2):
                for cs in range(2):
                    offset = (2 * core + hi) * QUARTER + (2 * xy + cs) * few
                    pick = jnp.where((feature == lane + offset) & (lane < few), 1.0, 0.0)
                    shards[2 * hi + cs, rows:] = mm(terms, pick.astype(BF)).astype(BF)
        for k in range(4):
            outs[k][...] = shards[slots[k]]

    ins = [grads[1], came[0], onward[0], grads[3], came[1], onward[1]]
    return run(
        body,
        [shaped((rows + extra, width))] * 4,
        vmem=list(norm_terms),
        hbm=ins,
        after=after,
        scratch=[pltpu.VMEM((6,) + shape, BF), pltpu.VMEM((4, rows + extra, width), BF)],
        copies=6,
        micros=2,
    )


def sum_plain(place, grads, attention):
    wide, narrow = grads[1][0], grads[3][0]
    rows = D // place.dp
    if attention:
        value = jnp.stack([wide[:, :HALF], wide[:, HALF:], narrow[:, :HALF]], axis=1)
        value = value.reshape(place.dp, rows, 3, 2, QUARTER).transpose(3, 0, 1, 2, 4)
        value = value.reshape(2, place.dp, rows, 3 * QUARTER)
        outs = narrow[:, HALF:].reshape(2, 2, place.dp, rows // 4, 2, QUARTER)
        outs = outs.transpose(1, 2, 0, 4, 3, 5).reshape(2, place.dp, rows, QUARTER)
        value = jnp.concatenate([value, outs], axis=-1)
    else:
        value = jnp.concatenate(
            [wide.reshape(2, place.dp, rows, D), narrow.reshape(2, place.dp, rows, D)], axis=-1
        )
    whole = jnp.zeros((2,) + value.shape, F32)
    whole = lax.dynamic_update_index_in_dim(whole, value.astype(F32), place.core, 0)
    whole = whole.reshape((4 * place.dp,) + value.shape[2:])
    return lax.psum_scatter(whole, ("mp", "xy", "core"), scatter_dimension=0, tiled=False)


def attention_outputs(sums, rows, few):
    value = sums[:rows]
    last = value[:, 3 * QUARTER :]
    out = jnp.concatenate([last[p * few : (p + 1) * few] for p in range(4)], axis=1)
    return [value[:, j * QUARTER : (j + 1) * QUARTER] for j in range(3)], out


def finish_self(got, own, few_lanes):
    rows = own.shape[0] - 16
    few = rows // 4

    def body(a, b, c, d, own_ref, qkv_ref, out_ref, gain_ref, bias_ref):
        home, _ = column_slots()
        last = jnp.where(home, own_ref[...].astype(F32), d[...].astype(F32))
        sums = add_up(a[...], b[...], c[...], last)
        blocks, out = attention_outputs(sums, rows, few)
        for j in range(3):
            qkv_ref[j] = blocks[j]
        out_ref[...] = out
        gain_ref[...] = sums[rows : rows + 4, :few_lanes]
        bias_ref[...] = sums[rows + 4 : rows + 8, :few_lanes]

    return run(
        body,
        [
            shaped((3, rows, QUARTER), F32),
            shaped((few, D), F32),
            shaped((4, few_lanes), F32),
            shaped((4, few_lanes), F32),
        ],
        vmem=list(got) + [own],
        micros=1.5,
    )


def finish_cross(got, own, after=()):
    rows = own.shape[0]
    few = rows // 4

    def body(a, b, c, d, own_ref, kv_ref, q_ref, out_ref):
        home, _ = column_slots()
        last = jnp.where(home, own_ref[...].astype(F32), d[...].astype(F32))
        blocks, out = attention_outputs(add_up(a[...], b[...], c[...], last), rows, few)
        kv_ref[...] = jnp.concatenate(blocks[:2], axis=1)
        q_ref[...] = blocks[2]
        out_ref[...] = out

    return run(
        body,
        [shaped((rows, HALF), F32), shaped((rows, QUARTER), F32), shaped((few, D), F32)],
        vmem=list(got) + [own],
        micros=1.5,
        after=after,
    )


def join_rows(blocks, got, dtype, after=()):
    width, rows = blocks[0].shape

    def body(block_ref, first_ref, second_ref, out_ref):
        home, _ = column_slots()
        _, _, z = where_am_i()

        @pl.when(home)
        def _():
            out_ref[z % 2] = block_ref[...].astype(dtype)

        @pl.when(jnp.logical_not(home))
        def _():
            out_ref[z % 2] = first_ref[...].astype(dtype)

        out_ref[(z + 1) % 2] = second_ref[...].astype(dtype)

    joined = run(
        body,
        [shaped((2, width, rows), dtype)],
        vmem=[blocks[0]] + list(got),
        micros=2,
        after=after,
    )[0]
    return joined[:, None].transpose(0, 1, 3, 2)


def from_quarters(value):
    few = value.shape[0] // 4
    return value.reshape(4, few, QUARTER).transpose(1, 0, 2).reshape(few, D)


def three_parts(value):
    terms = []
    for _ in range(3):
        term = lax.reduce_precision(value, 8, 7)
        terms.append(term.astype(BF))
        value = value - term
    return jnp.concatenate(terms)


def per_device(
    dp,
    mp,
    hidden_in,
    encoder_states,
    cotangent,
    self_qkv,
    self_out,
    cross_q,
    cross_kv,
    cross_out,
    fc_in,
    fc_out,
    ln_gain,
    ln_bias,
    token_lengths,
    audio_lengths,
    corpus_ids,
    corpus_weights,
):
    place = Place(dp, mp)
    length = hidden_in.shape[2]
    frames = encoder_states.shape[2]
    padded = -(-frames // CHUNK) * CHUNK
    rows = self_qkv.shape[0]

    encoded = lax.dynamic_index_in_dim(encoder_states[:, 0], place.micro, 0, keepdims=False)
    first = ()
    if place.fast:
        shard = attention_shard(self_qkv, self_out, cross_kv, cross_q, cross_out)
        packed = pack_attention(place.column_out(shard), shard, (encoded,))
        w_self = w_cross = spread(place, packed)
        first = (shard,)
    else:
        quarter = lambda w: w.reshape(-1, 4, QUARTER).transpose(1, 0, 2).reshape(-1, QUARTER)
        flat = lambda w: w.reshape(rows, -1)
        w_self = attention_plain(
            place, jnp.concatenate([flat(self_qkv), quarter(self_out)], axis=1)
        )
        w_cross = attention_plain(
            place, jnp.concatenate([flat(cross_kv), cross_q, quarter(cross_out)], axis=1)
        )


    unit = unit_shard(place, fc_in, fc_out)
    if not place.fast:
        w_units = gather_units(place, unit)

    turned = lambda value: value[:, 0].transpose(0, 2, 1)
    numbers = jnp.concatenate([token_lengths.T, audio_lengths.T, corpus_ids.T])
    blocks = input_blocks(
        turned(hidden_in),
        three_parts(jnp.concatenate([ln_gain, ln_bias])),
        numbers,
        first,
    )
    got = place.rows_in(blocks)
    if place.fast:
        unit, got = lax.optimization_barrier((unit, got))
        column = [unit] + [place.swap_z(unit, k) for k in (1, 2, 3)]
        got, column, encoded = lax.optimization_barrier((got, column, encoded))
        stacked = stack_units(column, tuple(w_self[3:5]))
        w_units = spread(place, stacked)
    hidden, norms, nums = prepare(got, place.swap_core(got), corpus_weights)

    other = place.move(encoded, lambda xy, core, z: (xy, 1 - core, z) if core == z // 2 else None)
    encoded = jnp.where(place.home == place.core, encoded, other)
    encoded = jnp.pad(encoded, ((0, padded - frames), (0, 0)))

    part1, at, qkv, qt, kt, ot1, lse1 = self_forward(hidden, norms, nums, w_self)
    et = turn(encoded, (part1,))
    other1 = place.swap_core(part1)
    got = place.rows_in(turned_blocks(turned(cotangent), (at,)))
    kv, kvt = cross_memory(encoded, w_cross)
    part2, h1, ct, q2, qt2, ot2, lse2 = cross_forward(
        hidden, part1, other1, norms, nums, kv, kvt, w_cross
    )
    other2 = place.swap_core(part2)
    cot = prepare_cotangent(got, place.swap_core(got), (part2,))
    part3, h2, mt, slope, it = units_forward(h1, part2, other2, norms, w_units)
    other3 = place.swap_core(part3)
    part, d3, e3, dz, terms3, out_a, out_b = units_backward(
        h2, part3, other3, norms, nums, cot, slope, w_units
    )
    other = place.swap_core(part)
    g_units = units_grads(place, mt, dz, it, e3)
    came_units = leave_plane(place, g_units) if place.fast else None
    layer_got = place.rows_sent((out_a, out_b))
    layer_out = place.rows_joined((out_a, out_b), layer_got)
    part, d2, e2, dq2, dkv, terms2 = cross_backward(
        d3, h2, part, other, norms, nums, kv, kvt, q2, qt2, ot2, lse2, w_cross, layer_got
    )
    other = place.swap_core(part)
    keep, send = encoder_grad(dkv, w_cross)
    came = place.swap_core(send)
    passed = pass_on(g_units, came_units, (keep,)) if place.fast else ()
    encoder_blocks = finish_encoder(keep, came, frames, passed)
    encoder_got = place.rows_sent(encoder_blocks)
    part, d1, e1, dqk, dv, terms1 = self_backward(
        d2, h1, part, other, norms, nums, qkv, qt, kt, ot1, lse1, w_self, encoder_blocks
    )
    other = place.swap_core(part)
    held = (e1,)
    if place.fast:
        onward_units = cross_plane(place, passed)
        kept, sent = units_sum(g_units, came_units, onward_units, held)
        came_units = place.swap_z(sent, 1)
        held = (kept,)
    g_self = attention_grads(place, at, dqk, at, dv, ot1, e1, held)
    terms, out_a, out_b = finish_hidden(
        d1, hidden, part, other, norms, terms1, terms2, terms3, (g_self[0],)
    )
    hidden_got = place.rows_sent((out_a, out_b))
    g_cross = attention_grads(place, et, dkv, ct, dq2, ot2, e2, [terms] + encoder_got)
    if place.fast:
        came_self = leave_plane(place, g_self)
        came_cross = leave_plane(place, g_cross)
        passed = pass_on(g_self, came_self, (g_cross[0],))
        onward_self = cross_plane(place, passed)
        second = add_second(kept, came_units, passed)
        last_units = place.swap_z(second, 2)
        passed = pass_on(g_cross, came_cross, (second,))
        onward_cross = cross_plane(place, passed)

    few = D // (place.dp * place.mp)
    if place.fast:
        terms = terms + place.swap_xy(terms, 1)
        blocks = column_blocks(
            g_self, came_self, onward_self, (terms, place.swap_xy(terms, 2)), passed
        )
        self_got = place.column_back(blocks)
        cross_blocks = column_blocks(g_cross, came_cross, onward_cross, (), (blocks[0],))
        cross_got = place.column_back(cross_blocks)
        grad_encoder = join_rows(encoder_blocks, encoder_got, F32, (cross_blocks[0],))
        mine, sent, s_down = cut_units(kept, came_units, last_units, (cross_blocks[0],))
        s_up = join_units(place, mine, place.swap_core(sent))
        grad_hidden = join_rows((out_a, out_b), hidden_got, F32, (cross_blocks[0],))
        g_qkv, g_out, g_gain, g_bias = finish_self(self_got, blocks[3], few)
        g_ckv, g_cq, g_cout = finish_cross(cross_got, cross_blocks[3], (g_out,))
        g_qkv = g_qkv.transpose(1, 0, 2)
    else:
        s_up, s_down = scatter_units(place, g_units)
        grad_encoder = place.rows_joined(encoder_blocks, encoder_got).astype(F32)
        grad_hidden = place.rows_joined((out_a, out_b), hidden_got).astype(F32)
        s_cross = sum_plain(place, g_cross, True)
        s_self = sum_plain(place, g_self, True)
        terms = jnp.where(place.core == 0, terms, 0.0)
        terms = lax.psum(terms, AXES)
        shares = lax.dynamic_slice_in_dim(terms, (place.z * place.dp + place.d) * few, few, 1)
        g_gain, g_bias = shares[:4], shares[4:]
        g_qkv, g_out = s_self[:, : 3 * QUARTER], from_quarters(s_self[:, 3 * QUARTER :])
        g_ckv, g_cq = s_cross[:, :HALF], s_cross[:, HALF : 3 * QUARTER]
        g_cout = from_quarters(s_cross[:, 3 * QUARTER :])
    return (
        layer_out,
        grad_hidden,
        grad_encoder,
        g_qkv.reshape(rows, 3, QUARTER),
        g_out,
        g_cq,
        g_ckv.reshape(rows, 2, QUARTER),
        g_cout,
        s_up,
        s_down,
        g_gain,
        g_bias,
    )


def solution(mesh):
    dp, mp = mesh.shape["dp"], mesh.shape["mp"]
    finer = Mesh(mesh.devices.reshape(dp // 2, 2, mp), AXES)
    both = ("xy", "core")
    rows = P(None, both, None, "mp")
    columns = P(both, None, "mp")
    pairs = P(both, "mp")
    units = P(("mp",) + both, None)
    each = P(None, both)
    return jax.shard_map(
        partial(per_device, dp, mp),
        mesh=finer,
        in_specs=(
            rows,
            P(None, both, None, None),
            rows,
            columns,
            units,
            pairs,
            columns,
            units,
            pairs,
            units,
            P(None, "mp"),
            P(None, "mp"),
            each,
            each,
            each,
            P(),
        ),
        out_specs=(
            rows,
            rows,
            rows,
            columns,
            units,
            pairs,
            columns,
            units,
            pairs,
            units,
            P(None, ("mp",) + both),
            P(None, ("mp",) + both),
        ),
        check_vma=False,
    )
```

```python
from functools import partial

import jax
import jax.numpy as jnp
from jax import lax
from jax.experimental import pallas as pl
from jax.experimental.pallas import tpu as pltpu
from jax.sharding import Mesh, PartitionSpec as P

D = 768
HALF = 384
QUARTER = 192
HEAD_DIM = 64
HEADS = 6
CHUNK = 256
BF = jnp.bfloat16
F32 = jnp.float32
AXES = ("xy", "core", "mp")
CHIPS = ("xy", "mp")
VMEM = pl.BlockSpec(memory_space=pltpu.VMEM)
SMEM = pl.BlockSpec(memory_space=pltpu.SMEM)
ANY = pl.BlockSpec(memory_space=pl.ANY)
HBM = pl.BlockSpec(memory_space=pltpu.HBM)


def mm(left, right):
    return jnp.dot(left, right, preferred_element_type=F32)


def mm_t(left, right):
    return lax.dot_general(left, right, (((1,), (1,)), ((), ())), preferred_element_type=F32)


def shaped(shape, dtype=BF):
    return jax.ShapeDtypeStruct(shape, dtype)


def room(shape, dtype):
    item = jnp.dtype(dtype).itemsize
    shape = (1, 1) + tuple(shape)
    tile = 32 // item
    size = item * (-(-shape[-1] // 128) * 128) * (-(-shape[-2] // tile) * tile)
    for extent in shape[:-2]:
        size *= extent
    return size


def run(
    body, outs, vmem=(), hbm=(), smem=(), scratch=(), copies=0, micros=2, after=(), staged=False
):
    args = tuple(smem) + tuple(vmem) + tuple(hbm)
    count = len(args)
    scratch = list(scratch)
    if copies:
        scratch.append(pltpu.SemaphoreType.DMA((copies,)))
    need = sum(room(a.shape, a.dtype) for a in (tuple(vmem) if staged else ()) + tuple(outs))
    need += sum(room(a.shape, a.dtype) for a in scratch if a.memory_space == pltpu.VMEM)
    need = min(need + 12 * 1024 * 1024, 60 * 1024 * 1024)
    moved = sum(a.size * a.dtype.itemsize for a in args) + sum(
        o.size * o.dtype.itemsize for o in outs
    )
    skip = len(scratch)
    if staged:
        scratch += [pltpu.VMEM(a.shape, a.dtype) for a in vmem]
        scratch.append(pltpu.SemaphoreType.DMA((len(vmem),)))

    def whole(*refs):
        ins, rest = list(refs[:count]), refs[count + len(after) :]
        if staged:
            held = rest[len(outs) + skip : -1]
            rest, sems = rest[: len(outs) + skip], rest[-1]
            copies = Copies(sems)
            for i, target in enumerate(held):
                copies.start(ins[len(smem) + i], target)
                ins[len(smem) + i] = target
            copies.wait()
        body(*ins, *rest)

    place = HBM if staged else VMEM
    return pl.pallas_call(
        whole,
        out_shape=tuple(outs),
        in_specs=[SMEM] * len(smem) + [place] * len(vmem) + [ANY] * (len(hbm) + len(after)),
        out_specs=(VMEM,) * len(outs),
        scratch_shapes=scratch,
        compiler_params=pltpu.CompilerParams(vmem_limit_bytes=need),
        cost_estimate=pl.CostEstimate(
            flops=int(micros * 1.15e9), bytes_accessed=moved, transcendentals=0
        ),
    )(*args, *after)


class Copies:
    def __init__(self, sems):
        self.sems, self.open = sems, []

    def start(self, source, target):
        copy = pltpu.make_async_copy(source, target, self.sems.at[len(self.open)])
        copy.start()
        self.open.append(copy)

    def wait(self):
        for copy in self.open:
            copy.wait()


def where_am_i():
    return lax.axis_index("core"), lax.axis_index("xy"), lax.axis_index("mp")


class Place:
    def __init__(self, dp, mp):
        self.dp, self.mp = dp, mp
        self.chips = dp // 2
        self.fast = self.chips == 4
        self.z = lax.axis_index("mp")
        self.core = lax.axis_index("core")
        self.xy = lax.axis_index("xy")
        self.d = 2 * self.xy + self.core
        self.micro = self.z % 2
        self.home = self.z // 2

    def move(self, value, route):
        pairs = []
        for xy in range(self.chips):
            for core in range(2):
                for z in range(self.mp):
                    target = route(xy, core, z)
                    if target is not None:
                        txy, tcore, tz = target
                        pairs.append(
                            ((2 * xy + core) * self.mp + z, (2 * txy + tcore) * self.mp + tz)
                        )
        return lax.ppermute(value, AXES, pairs)

    def swap_core(self, value):
        return self.move(value, lambda xy, core, z: (xy, 1 - core, z))

    def swap_xy(self, value, bit):
        return self.move(value, lambda xy, core, z: (xy ^ bit, core, z))

    def swap_z(self, value, bit):
        return self.move(value, lambda xy, core, z: (xy, core, z ^ bit))

    def column_routes(self):
        def route(step, xy, core, z):
            user, j = z // 2, z % 2
            home = core == user
            near = lambda i: (xy, user, 2 * user + i)
            far = lambda i: (xy, user, 2 * (1 - user) + i)
            if step == 0:
                return near(1 - j) if home else far(1 - j)
            if step == 1:
                return far(j) if home else near(j)
            if step == 2:
                return far(1 - j) if home else near(1 - j)
            return None if home else far(j)

        return [partial(route, step) for step in range(4)]

    def column_out(self, shard):
        return [self.move(shard, route) for route in self.column_routes()]

    def column_back(self, blocks):
        got = []
        for block, route in zip(blocks, self.column_routes()):
            turned = {}
            for xy in range(self.chips):
                for core in range(2):
                    for z in range(self.mp):
                        target = route(xy, core, z)
                        if target is not None:
                            turned[target] = (xy, core, z)
            got.append(self.move(block, lambda xy, core, z: turned.get((xy, core, z))))
        return got

    def rows_in(self, blocks):
        def route(k, xy, core, z):
            target = (xy, z // 2, 2 * core + (z + k) % 2)
            return None if target == (xy, core, z) else target

        got = [self.move(block, partial(route, k)) for k, block in enumerate(blocks)]
        return jnp.stack([jnp.where(self.core == self.home, blocks[0], got[0]), got[1]])

    def rows_home(self, blocks):
        return self.rows_joined(blocks, self.rows_sent(blocks))

    def rows_sent(self, blocks):
        def route(k, xy, core, z):
            target = (xy, z // 2, 2 * core + (z % 2 - k) % 2)
            return None if target == (xy, core, z) else target

        return [self.move(block, partial(route, k)) for k, block in enumerate(blocks)]

    def rows_joined(self, blocks, got):
        got = [jnp.where(self.core == self.home, blocks[0], got[0]), got[1]]
        even = self.z % 2 == 0
        both = jnp.stack([jnp.where(even, got[0], got[1]), jnp.where(even, got[1], got[0])])
        return both[:, None].transpose(0, 1, 3, 2)


def norm(hidden):
    center = jnp.mean(hidden, axis=-1, keepdims=True)
    spread = jnp.mean(hidden * hidden, axis=-1, keepdims=True) - center * center
    inverse = lax.rsqrt(spread + 1e-05)
    return (hidden - center) * inverse, inverse


def norm_back(grad, unit, inverse, gain):
    scaled = grad * gain
    first = jnp.mean(scaled, axis=-1, keepdims=True)
    second = jnp.mean(scaled * unit, axis=-1, keepdims=True)
    terms = jnp.concatenate(
        [jnp.sum(grad * unit, axis=0, keepdims=True), jnp.sum(grad, axis=0, keepdims=True)], axis=0
    )
    return inverse * (scaled - first - unit * second), terms


def add_up(*terms):
    total = terms[0].astype(F32)
    for term in terms[1:]:
        total = total + term.astype(F32)
    return total


def input_blocks(hidden, terms, numbers, after=()):
    _, width, length = hidden.shape
    total = width + 32

    def body(numbers_ref, hidden_ref, terms_ref, *outs):
        _, _, z = where_am_i()
        lanes = lax.broadcasted_iota(jnp.int32, (8, length), 1)
        for k in range(2):
            micro = (z + k) % 2
            outs[k][0:width] = hidden_ref[micro]
            tok, aud = numbers_ref[0, micro], numbers_ref[1, micro]
            row = jnp.where(lanes == 0, tok // 256, jnp.where(lanes == 1, tok % 256, 0))
            row = jnp.where(lanes == 2, aud // 256, jnp.where(lanes == 3, aud % 256, row))
            row = jnp.where(lanes == 4, numbers_ref[2, micro], row)
            wide = jnp.concatenate(
                [terms_ref[...].astype(F32), jnp.zeros((24, length - width), F32)], axis=1
            )
            outs[k][width:total] = jnp.concatenate([wide, row.astype(F32)], axis=0).astype(BF)

    return run(
        body,
        [shaped((total, length))] * 2,
        smem=[numbers],
        vmem=[hidden, terms],
        micros=1,
        after=after,
    )


def turned_blocks(value, after=()):
    _, width, length = value.shape

    def body(ref, first_ref, second_ref):
        _, _, z = where_am_i()
        first_ref[...] = ref[z % 2]
        second_ref[...] = ref[(z + 1) % 2]

    return run(body, [shaped((width, length))] * 2, vmem=[value], micros=1, after=after)


def bring_blocks(copies, own_ref, other_ref, wide):
    core, _, z = where_am_i()
    found = []
    for k in range(2):
        slot = (z % 2 + k) % 2
        for ref, user in ((own_ref, core), (other_ref, 1 - core)):
            block = 2 * user + slot
            here = pl.ds(pl.multiple_of(block * QUARTER, QUARTER), QUARTER)
            copies.start(ref.at[k, pl.ds(0, QUARTER)], wide.at[here])
            found.append((ref.at[k], block))
    return found


def prepare_cotangent(own, other, after=()):
    length = own.shape[2]

    def body(own_ref, other_ref, cot_ref, wide, sems):
        copies = Copies(sems)
        bring_blocks(copies, own_ref, other_ref, wide)
        copies.wait()
        cot_ref[...] = wide[...].T

    return run(
        body,
        [shaped((length, D))],
        hbm=[own, other],
        scratch=[pltpu.VMEM((D, length), BF)],
        copies=4,
        micros=3,
        after=after,
    )[0]


def prepare(own, other, corpus_weights):
    length = own.shape[2]

    def body(
        weights_ref, own_ref, other_ref, hidden_ref, norms_ref, nums_ref, wide, extra, sems
    ):
        copies = Copies(sems)
        for ref, block in bring_blocks(copies, own_ref, other_ref, wide):
            copies.start(ref.at[pl.ds(QUARTER, 32)], extra.at[block])
        copies.wait()
        hidden_ref[...] = wide[...].T
        parts = [extra[b].astype(F32) for b in range(4)]
        norms_ref[...] = jnp.concatenate(
            [(e[0:8] + e[8:16] + e[16:24])[:, :QUARTER] for e in parts], axis=1
        )
        row = parts[0][24:25]
        tok = 256.0 * row[:, 0:1] + row[:, 1:2]
        aud = 256.0 * row[:, 2:3] + row[:, 3:4]
        weights = weights_ref[...]
        places = lax.broadcasted_iota(jnp.int32, weights.shape, 1).astype(F32)
        weight = jnp.sum(jnp.where(places == row[:, 4:5], weights, 0.0), axis=1, keepdims=True)
        index = lax.broadcasted_iota(jnp.int32, (8, 128), 0)
        nums_ref[...] = jnp.where(index == 0, tok, jnp.where(index == 1, aud, weight))

    return run(
        body,
        [shaped((length, D)), shaped((8, D), F32), shaped((8, 128), F32)],
        vmem=[corpus_weights.reshape(1, -1)],
        hbm=[own, other],
        scratch=[pltpu.VMEM((D, length), BF), pltpu.VMEM((4, 32, length), BF)],
        copies=8,
        micros=3,
    )


def quarters(value):
    return jnp.concatenate([value[:, p * QUARTER : (p + 1) * QUARTER] for p in range(4)], axis=0)


def attention_shard(self_qkv, self_out, cross_kv, cross_q, cross_out):
    rows = cross_q.shape[0]

    def body(qkv_ref, out_ref, kv_ref, q_ref, cout_ref, shard_ref):
        out = quarters(out_ref[...].astype(F32)).astype(BF)
        cout = quarters(cout_ref[...].astype(F32)).astype(BF)
        shard_ref[...] = jnp.concatenate(
            [qkv_ref[j] for j in range(3)] + [out, kv_ref[...], q_ref[...], cout], axis=1
        )

    return run(
        body,
        [shaped((rows, 2 * D))],
        vmem=[self_qkv.transpose(1, 0, 2), self_out, cross_kv.reshape(rows, -1), cross_q, cross_out],
        micros=2,
        staged=True,
    )[0]


def column_slots():
    core, _, z = where_am_i()
    j = z % 2
    home = 1 - jnp.abs(z // 2 - core)
    same = core + (1 - 2 * core) * (1 - home)
    return home == 1, (2 * (1 - j) + same, 2 * j + 1 - same, 2 * (1 - j) + 1 - same, 2 * j + same)


def bring_column(part_refs, own_ref, shards, sems):
    home, slots = column_slots()
    copies = Copies(sems)
    for k in range(3):
        copies.start(part_refs[k], shards.at[slots[k]])

    @pl.when(home)
    def _():
        copy = pltpu.make_async_copy(own_ref, shards.at[slots[3]], sems.at[3])
        copy.start()
        copy.wait()

    @pl.when(jnp.logical_not(home))
    def _():
        copy = pltpu.make_async_copy(part_refs[3], shards.at[slots[3]], sems.at[3])
        copy.start()
        copy.wait()

    copies.wait()


def pack_attention(parts, own, after):
    rows = own.shape[0]
    few = rows // 4

    def body(*refs):
        part_refs, own_ref, (out_ref, shards, sems) = refs[:4], refs[4], refs[5:]
        bring_column(part_refs, own_ref, shards, sems)
        for which in range(2):
            for cs in range(2):
                low, high = shards[cs], shards[2 + cs]

                def both(at):
                    at = at + which * D
                    return [low[:, at : at + QUARTER], high[:, at : at + QUARTER]]

                here = pl.ds(cs * rows, rows)
                out_ref[0, which, here, :] = jnp.concatenate(both(0) + both(QUARTER), axis=1)
                out_ref[1, which, here, 0:HALF] = jnp.concatenate(both(HALF), axis=1)
            at = 3 * QUARTER + which * D
            outs = [shards[i, :, at : at + QUARTER].astype(F32) for i in range(4)]
            stack = []
            for q in range(2):
                for i in range(4):
                    left = outs[i][2 * q * few : (2 * q + 1) * few]
                    right = outs[i][(2 * q + 1) * few : (2 * q + 2) * few]
                    stack.append(jnp.concatenate([left, right], axis=1))
            out_ref[1, which, :, HALF:D] = jnp.concatenate(stack, axis=0).astype(BF)

    return run(
        body,
        [shaped((2, 2, 2 * rows, D))],
        hbm=list(parts) + [own],
        scratch=[pltpu.VMEM((4, rows, 2 * D), BF)],
        copies=4,
        micros=2,
        after=after,
    )[0]


def unit_shard(place, fc_in, fc_out):
    rows = fc_in.shape[0]
    both = fc_in.reshape(rows, place.chips, 2, rows).transpose(2, 0, 1, 3).reshape(2, rows, HALF)
    kept = lax.dynamic_index_in_dim(both, place.core, 0, keepdims=False)
    sent = lax.dynamic_index_in_dim(both, 1 - place.core, 0, keepdims=False)
    came = place.swap_core(sent)
    first = place.core == 0
    left = jnp.concatenate([jnp.where(first, kept, came), jnp.where(first, came, kept)])
    right = jnp.concatenate([fc_out[:, :HALF], fc_out[:, HALF:]])
    return jnp.concatenate([left, right], axis=1)


def stack_units(blocks, after):
    rows = blocks[0].shape[0]

    def body(*refs):
        for k in range(4):
            refs[4][k // 2, k % 2] = refs[k][...]

    return run(body, [shaped((2, 2, rows, D))], vmem=blocks, micros=1.5, after=after)[0]


def gather_units(place, shard):
    whole = lax.all_gather(shard, CHIPS, axis=0)
    rows = shard.shape[0] // 2
    whole = whole.reshape(place.chips, place.mp, 2 * rows, D)
    up = whole[..., :HALF].transpose(0, 2, 1, 3).reshape(D, 2 * D)
    down = whole[..., HALF:].reshape(place.chips, place.mp, 2, rows, HALF)
    return [up, down.transpose(1, 0, 3, 2, 4).reshape(2 * D, D)]


def scatter_units(place, grads):
    total = lax.psum_scatter(grads, CHIPS, scatter_dimension=0, tiled=False)
    rows = total.shape[0] // 2
    kept = lax.dynamic_slice_in_dim(total, place.core * rows, rows, 0)
    sent = lax.dynamic_slice_in_dim(total[:, :HALF], (1 - place.core) * rows, rows, 0)
    came = place.swap_core(sent)
    kept = kept[:, :HALF]
    first = place.core == 0
    both = jnp.stack([jnp.where(first, kept, came), jnp.where(first, came, kept)])
    both = both.reshape(2, rows, place.chips, rows).transpose(1, 2, 0, 3).reshape(rows, D)
    down = jnp.concatenate([total[:rows, HALF:], total[rows:, HALF:]], axis=1)
    return both.astype(F32), down.astype(F32)


def spread(place, own):
    from_x = place.swap_xy(own, 1)
    from_y = place.swap_xy(own, 2)
    far_one = place.swap_xy(from_y[1], 1)
    far_zero = place.swap_xy(from_x[0], 2)
    return [own, from_x, from_y, far_zero, far_one]


def piece_views(refs, message, which, xy):
    own, from_x, from_y, far_zero, far_one = refs
    return [
        (own.at[which, message], xy),
        (from_x.at[which, message], xy ^ 1),
        (from_y.at[which, message], xy ^ 2),
        ((far_zero, far_one)[which].at[message], xy ^ 3),
    ]


def load_wide(copies, refs, message, which, xy, target, columns=None):
    if len(refs) != 5:
        copies.start(refs[which], target)
        return
    for view, chip in piece_views(refs, message, which, xy):
        rows = view.shape[0]
        if columns is not None:
            view = view.at[:, pl.ds(0, columns)]
        copies.start(view, target.at[pl.ds(pl.multiple_of(chip * rows, 16), rows)])


def load_out(copies, refs, message, xy, target):
    if len(refs) != 5:
        copies.start(refs[2], target)
        return
    for view, chip in piece_views(refs, message, 1, xy):
        rows = view.shape[0] // 4
        for q in range(2):
            for hi in range(2):
                copies.start(
                    view.at[pl.ds((2 * q + hi) * rows, rows), pl.ds(HALF, HALF)],
                    target.at[q, pl.ds(pl.multiple_of(hi * QUARTER + chip * rows, 16), rows)],
                )


def unit_views(refs):
    _, xy, z = where_am_i()
    views = []
    for part in range(2):
        for view, chip in [
            (refs[0].at[part], xy),
            (refs[1].at[part], xy ^ 1),
            (refs[2].at[part], xy ^ 2),
            (refs[3 + part], xy ^ 3),
        ]:
            for i in range(2):
                views.append((view.at[i], chip, z ^ (2 * part + i)))
    return views


def load_up(copies, refs, w_up):
    if len(refs) == 2:
        copies.start(refs[0], w_up)
        return
    for view, chip, z in unit_views(refs):
        rows = view.shape[0]
        copies.start(
            view.at[:, pl.ds(0, HALF)],
            w_up.at[
                pl.ds(pl.multiple_of(rows * chip, 16), rows), pl.ds(pl.multiple_of(z * HALF, HALF), HALF)
            ],
        )


def load_down(copies, refs, w_down):
    if len(refs) == 2:
        copies.start(refs[1], w_down)
        return
    for view, chip, z in unit_views(refs):
        rows = view.shape[0] // 2
        for q in range(2):
            copies.start(
                view.at[pl.ds(q * rows, rows), pl.ds(HALF, HALF)],
                w_down.at[
                    pl.ds(pl.multiple_of(z * HALF + chip * rows, 16), rows), pl.ds(q * HALF, HALF)
                ],
            )


ATTENTION_COPIES = 4 + 4 + 16
UP_COPIES = 16
DOWN_COPIES = 32


def gather_plain(place, shard):
    whole = lax.all_gather(shard, ("mp", "xy", "core"), axis=0)
    whole = whole.reshape((2, 2, place.dp) + shard.shape)
    return lax.dynamic_index_in_dim(whole, place.core, 0, keepdims=False)


def attention_plain(place, shard):
    mine = gather_plain(place, shard)
    rows = shard.shape[0]

    def columns(at, count):
        value = mine[..., at : at + count * QUARTER].reshape(2, D, count, QUARTER)
        return value.transpose(1, 2, 0, 3).reshape(D, count * HALF)

    out = mine[..., 3 * QUARTER :].reshape(2, place.dp, 2, 2, rows // 4, QUARTER)
    out = out.transpose(2, 0, 1, 4, 3, 5).reshape(2, HALF, HALF)
    return [columns(0, 2), columns(HALF, 1), out]


def head_rows(h):
    return pl.ds(pl.multiple_of(h * HEAD_DIM, HEAD_DIM), HEAD_DIM)


def low_parts(value):
    parts = []
    for _ in range(3):
        part = value.astype(BF)
        parts.append(part)
        value = value - part.astype(F32)
    return parts


def widened(count):
    return lambda rows: (
        lax.broadcasted_iota(jnp.int32, (rows, HEAD_DIM), 1) < count
    ).astype(F32).astype(BF)


def below(head, rows):
    blank = jnp.zeros((HEAD_DIM - len(rows), head.shape[1]), F32)
    rest = jnp.concatenate([row.astype(F32) for row in rows] + [blank], axis=0)
    return jnp.concatenate([head, rest.astype(BF)], axis=0)


def project(left, pair_ref):
    return jnp.concatenate([mm(left, pair_ref[0]), mm(left, pair_ref[1])], axis=1)


def project_t(left, pair_ref):
    return mm_t(left[:, :HALF], pair_ref[0]) + mm_t(left[:, HALF:], pair_ref[1])


def self_forward(hidden, norms, nums, weights, after=()):
    length = hidden.shape[0]

    def body(hidden_ref, norms_ref, nums_ref, *refs):
        w_refs, refs = refs[: len(weights)], refs[len(weights) :]
        part_ref, at_ref, qkv_ref, qt_ref, kt_ref, ot_ref, lse_ref = refs[:7]
        w_qk, w_v, w_out, vt, heads, bias, sems = refs[7:]
        _, xy, _ = where_am_i()
        copies = Copies(sems)
        load_wide(copies, w_refs, 0, 0, xy, w_qk)
        load_wide(copies, w_refs, 0, 1, xy, w_v, HALF)
        load_out(copies, w_refs, 0, xy, w_out)
        unit, _ = norm(hidden_ref[...].astype(F32))
        a = (unit * norms_ref[0:1] + norms_ref[4:5]).astype(BF)
        at_ref[...] = a.T
        keys = lax.broadcasted_iota(jnp.int32, (length, length), 0)
        queries = lax.broadcasted_iota(jnp.int32, (length, length), 1)
        allowed = (keys <= queries) & (keys.astype(F32) < nums_ref[0:1, 0:1])
        bias[...] = jnp.where(allowed, 0.0, -1e30)
        copies.wait()
        qk = mm(a, w_qk[...])
        q = (qk[:, :HALF].astype(BF).astype(F32) * HEAD_DIM ** (-0.5)).astype(BF)
        k = qk[:, HALF:].astype(BF)
        v = mm(a, w_v[...]).astype(BF)
        qkv_ref[:, 0:HALF] = q
        qkv_ref[:, HALF : 2 * HALF] = k
        qkv_ref[:, 2 * HALF :] = v
        qt_ref[...] = q.T
        kt_ref[...] = k.T
        vt[...] = v.T
        for h in range(HEADS):
            heads[h] = k[:, h * HEAD_DIM : (h + 1) * HEAD_DIM]

        def head(h, carry):
            s = mm(heads[h], qt_ref[head_rows(h), :]) + bias[...]
            top = jnp.max(s, axis=0, keepdims=True)
            p = jnp.exp(s - top)
            total = jnp.sum(p, axis=0, keepdims=True)
            o = mm(vt[head_rows(h), :], p.astype(BF))
            ot_ref[head_rows(h), :] = (o / total).astype(BF)
            lse_ref[h] = top + jnp.log(total)
            return carry

        lax.fori_loop(0, HEADS, head, 0)
        part_ref[...] = project(ot_ref[...].T, w_out).astype(BF)

    return run(
        body,
        [
            shaped((length, D)),
            shaped((D, length)),
            shaped((length, 3 * HALF)),
            shaped((HALF, length)),
            shaped((HALF, length)),
            shaped((HALF, length)),
            shaped((HEADS, 1, length), F32),
        ],
        vmem=[hidden, norms, nums],
        hbm=weights,
        scratch=[
            pltpu.VMEM((D, D), BF),
            pltpu.VMEM((D, HALF), BF),
            pltpu.VMEM((2, HALF, HALF), BF),
            pltpu.VMEM((HALF, length), BF),
            pltpu.VMEM((HEADS, length, HEAD_DIM), BF),
            pltpu.VMEM((length, length), F32),
        ],
        copies=ATTENTION_COPIES,
        micros=3,
        after=after,
    )


def turn(value, after=()):
    rows, columns = value.shape

    def body(ref, out_ref):
        for at in range(0, rows, CHUNK):
            out_ref[:, at : at + CHUNK] = ref[at : at + CHUNK, :].T

    return run(body, [shaped((columns, rows))], vmem=[value], micros=4, after=after)[0]


def cross_memory(encoded, weights):
    frames = encoded.shape[0]

    def body(enc_ref, *refs):
        w_refs, refs = refs[: len(weights)], refs[len(weights) :]
        kv_ref, kvt_ref, w_kv, sems = refs
        _, xy, _ = where_am_i()
        copies = Copies(sems)
        load_wide(copies, w_refs, 1, 0, xy, w_kv)
        copies.wait()

        def step(i, carry):
            here = pl.ds(pl.multiple_of(i * CHUNK, CHUNK), CHUNK)
            kv = mm(enc_ref[here, :], w_kv[...]).astype(BF)
            kv_ref[here, :] = kv
            kvt_ref[:, here] = kv.T
            return carry

        lax.fori_loop(0, frames // CHUNK, step, 0)

    return run(
        body,
        [shaped((frames, D)), shaped((D, frames))],
        vmem=[encoded],
        hbm=weights,
        scratch=[pltpu.VMEM((D, D), BF)],
        copies=4,
        micros=1,
    )


def residual(hidden_ref, mine_ref, other_ref):
    return hidden_ref[...].astype(F32) + (mine_ref[...].astype(F32) + other_ref[...].astype(F32))


def cross_forward(hidden, mine, other, norms, nums, kv, kvt, weights):
    length = hidden.shape[0]
    frames = kv.shape[0]

    def body(hidden_ref, mine_ref, other_ref, norms_ref, nums_ref, kv_ref, kvt_ref, *refs):
        w_refs, refs = refs[: len(weights)], refs[len(weights) :]
        part_ref, h_ref, ct_ref, q_ref, qt_ref, ot_ref, lse_ref = refs[:7]
        w_q, w_out, heads, values_t, scores, sems = refs[7:]
        _, xy, _ = where_am_i()
        copies = Copies(sems)
        load_wide(copies, w_refs, 1, 1, xy, w_q, HALF)
        load_out(copies, w_refs, 1, xy, w_out)
        h1 = residual(hidden_ref, mine_ref, other_ref)
        h_ref[...] = h1
        unit, _ = norm(h1)
        c = (unit * norms_ref[1:2] + norms_ref[5:6]).astype(BF)
        ct_ref[...] = c.T
        frame = lax.broadcasted_iota(jnp.int32, (frames, HEAD_DIM), 0).astype(F32)
        lane = lax.broadcasted_iota(jnp.int32, (frames, HEAD_DIM), 1)
        mask = jnp.where(frame < nums_ref[1:2, 0:1], 0.0, -1e30)
        beside = jnp.where(lane == 0, mask, 0.0).astype(BF)
        one = lax.broadcasted_iota(jnp.int32, (16, frames), 0)
        one = jnp.where(one == 0, 1.0, 0.0).astype(BF)
        for h in range(HEADS):
            keys = kv_ref[:, h * HEAD_DIM : (h + 1) * HEAD_DIM]
            heads[h] = jnp.concatenate([keys, beside], axis=1)
            values = kvt_ref[HALF + h * HEAD_DIM : HALF + (h + 1) * HEAD_DIM, :]
            values_t[h] = jnp.concatenate([values, one], axis=0)
        copies.wait()
        q = mm(c, w_q[...]).astype(BF)
        q = (q.astype(F32) * HEAD_DIM ** (-0.5)).astype(BF)
        q_ref[...] = q
        qt_ref[...] = q.T
        ones = jnp.ones((1, length), F32)

        def head(h, carry):
            qt = below(qt_ref[head_rows(h), :], [ones])
            top = None
            for at in range(0, frames, CHUNK):
                s = mm(heads[h, at : at + CHUNK], qt)
                scores[at : at + CHUNK] = s
                high = jnp.max(s, axis=0, keepdims=True)
                top = high if top is None else jnp.maximum(top, high)
            o = None
            for at in range(0, frames, CHUNK):
                p = jnp.exp(scores[at : at + CHUNK] - top).astype(BF)
                more = mm(values_t[h, :, at : at + CHUNK], p)
                o = more if o is None else o + more
            total = o[HEAD_DIM : HEAD_DIM + 1]
            ot_ref[head_rows(h), :] = (o[:HEAD_DIM] / total).astype(BF)
            lse_ref[h] = top + jnp.log(total)
            return carry

        lax.fori_loop(0, HEADS, head, 0)
        part_ref[...] = project(ot_ref[...].T, w_out).astype(BF)

    return run(
        body,
        [
            shaped((length, D)),
            shaped((length, D), F32),
            shaped((D, length)),
            shaped((length, HALF)),
            shaped((HALF, length)),
            shaped((HALF, length)),
            shaped((HEADS, 1, length), F32),
        ],
        vmem=[hidden, mine, other, norms, nums, kv, kvt],
        hbm=weights,
        scratch=[
            pltpu.VMEM((D, HALF), BF),
            pltpu.VMEM((2, HALF, HALF), BF),
            pltpu.VMEM((HEADS, frames, 2 * HEAD_DIM), BF),
            pltpu.VMEM((HEADS, HEAD_DIM + 16, frames), BF),
            pltpu.VMEM((frames, length), F32),
        ],
        copies=4 + 16,
        micros=2,
    )


def units_forward(hidden, mine, other, norms, weights):
    length = hidden.shape[0]

    def body(hidden_ref, mine_ref, other_ref, norms_ref, *refs):
        w_refs, refs = refs[: len(weights)], refs[len(weights) :]
        part_ref, h_ref, mt_ref, slope_ref, it_ref = refs[:5]
        w_up, w_down, inner, late_sems, sems = refs[5:]
        _, xy, _ = where_am_i()
        copies = Copies(sems)
        load_up(copies, w_refs, w_up)
        late = Copies(late_sems)
        load_down(late, w_refs, w_down)
        h2 = residual(hidden_ref, mine_ref, other_ref)
        h_ref[...] = h2
        unit, _ = norm(h2)
        m = (unit * norms_ref[2:3] + norms_ref[6:7]).astype(BF)
        mt_ref[...] = m.T
        copies.wait()
        for at in range(0, 2 * D, CHUNK):
            here = slice(at, at + CHUNK)
            z = mm(m, w_up[:, here])
            share = 0.5 * (1.0 + lax.erf(z * 0.7071067811865476))
            slope = share + z * (0.3989422804014327 * jnp.exp(-0.5 * z * z))
            value = (z * share).astype(BF)
            inner[:, here] = value
            it_ref[here, :] = value.T
            slope_ref[:, here] = slope.astype(BF)
        late.wait()
        for at in range(0, D, CHUNK):
            part_ref[:, at : at + CHUNK] = mm(inner[...], w_down[:, at : at + CHUNK]).astype(BF)

    return run(
        body,
        [
            shaped((length, D)),
            shaped((length, D), F32),
            shaped((D, length)),
            shaped((length, 2 * D)),
            shaped((2 * D, length)),
        ],
        vmem=[hidden, mine, other, norms],
        hbm=weights,
        scratch=[
            pltpu.VMEM((D, 2 * D), BF),
            pltpu.VMEM((2 * D, D), BF),
            pltpu.VMEM((length, 2 * D), BF),
            pltpu.SemaphoreType.DMA((DOWN_COPIES,)),
        ],
        copies=UP_COPIES,
        micros=9,
    )


def store_blocks(value, blocks, first_ref, second_ref):
    core, _, z = where_am_i()
    for b in range(4):
        blocks[b] = value[:, b * QUARTER : (b + 1) * QUARTER]
    first_ref[...] = blocks[2 * core + z % 2].T
    second_ref[...] = blocks[2 * core + (z + 1) % 2].T


def units_backward(hidden, mine, other, norms, nums, cot, slope, weights):
    length = hidden.shape[0]

    def body(hidden_ref, mine_ref, other_ref, norms_ref, nums_ref, cot_ref, slope_ref, *refs):
        w_refs, refs = refs[: len(weights)], refs[len(weights) :]
        part_ref, d_ref, e_ref, dz_ref, terms_ref, first_ref, second_ref = refs[:7]
        w_up, w_down, blocks, late_sems, sems = refs[7:]
        _, xy, _ = where_am_i()
        copies = Copies(sems)
        load_down(copies, w_refs, w_down)
        late = Copies(late_sems)
        load_up(late, w_refs, w_up)
        unit, inverse = norm(residual(hidden_ref, mine_ref, other_ref))
        final = (unit * norms_ref[3:4] + norms_ref[7:8]).astype(BF)
        store_blocks(final, blocks, first_ref, second_ref)
        live = lax.broadcasted_iota(jnp.int32, (length, 1), 0).astype(F32) < nums_ref[0:1, 0:1]
        grad = cot_ref[...].astype(F32) * jnp.where(live, nums_ref[2:3, 0:1], 0.0)
        d3, terms = norm_back(grad, unit, inverse, norms_ref[3:4])
        d_ref[...] = d3
        terms_ref[...] = terms
        e = d3.astype(BF)
        e_ref[...] = e
        copies.wait()
        for at in range(0, 2 * D, CHUNK):
            here = slice(at, at + CHUNK)
            d_inner = mm_t(e, w_down[here, :])
            dz_ref[:, here] = (slope_ref[:, here].astype(F32) * d_inner).astype(BF)
        late.wait()
        for at in range(0, D, CHUNK):
            out = mm_t(dz_ref[...], w_up[at : at + CHUNK, :])
            part_ref[:, at : at + CHUNK] = out.astype(BF)

    return run(
        body,
        [
            shaped((length, D)),
            shaped((length, D), F32),
            shaped((length, D)),
            shaped((length, 2 * D)),
            shaped((2, D), F32),
            shaped((QUARTER, length)),
            shaped((QUARTER, length)),
        ],
        vmem=[hidden, mine, other, norms, nums, cot, slope],
        hbm=weights,
        scratch=[
            pltpu.VMEM((D, 2 * D), BF),
            pltpu.VMEM((2 * D, D), BF),
            pltpu.VMEM((4, length, QUARTER), BF),
            pltpu.SemaphoreType.DMA((UP_COPIES,)),
        ],
        copies=DOWN_COPIES,
        micros=10,
    )


def step_back(d_ref, hidden_ref, mine_ref, other_ref, gain):
    unit, inverse = norm(hidden_ref[...].astype(F32))
    grad = mine_ref[...].astype(F32) + other_ref[...].astype(F32)
    part, terms = norm_back(grad, unit, inverse, gain)
    return d_ref[...] + part, terms


def cross_backward(
    d, hidden, mine, other, norms, nums, kv, kvt, q, qt, ot, lse, weights, after=()
):
    length = hidden.shape[0]
    frames = kv.shape[0]

    def body(
        d_ref, hidden_ref, mine_ref, other_ref, norms_ref, nums_ref, kv_ref, kvt_ref, q_ref,
        qt_ref, ot_ref, lse_ref, *refs
    ):
        w_refs, refs = refs[: len(weights)], refs[len(weights) :]
        part_ref, d_out_ref, e_ref, dq_ref, dkv_ref, terms_ref = refs[:6]
        w_q, w_out, keys, values, queries, grads, dot_t, dk_h, dv_h, dqt, sems = refs[6:]
        _, xy, _ = where_am_i()
        copies = Copies(sems)
        load_wide(copies, w_refs, 1, 1, xy, w_q, HALF)
        load_out(copies, w_refs, 1, xy, w_out)
        d2, terms = step_back(d_ref, hidden_ref, mine_ref, other_ref, norms_ref[2:3])
        d_out_ref[...] = d2
        terms_ref[...] = terms
        e = d2.astype(BF)
        e_ref[...] = e
        frame = lax.broadcasted_iota(jnp.int32, (frames, HEAD_DIM), 0).astype(F32)
        lane = lax.broadcasted_iota(jnp.int32, (frames, HEAD_DIM), 1)
        mask = jnp.where(frame < nums_ref[1:2, 0:1], 0.0, -1e30)
        beside = jnp.where(lane == 0, mask, jnp.where(lane < 4, 1.0, 0.0)).astype(BF)
        three = widened(3)(frames)
        for h in range(HEADS):
            lanes = slice(h * HEAD_DIM, (h + 1) * HEAD_DIM)
            keys[h] = jnp.concatenate([kv_ref[:, lanes], beside], axis=1)
            value = kv_ref[:, HALF + h * HEAD_DIM : HALF + (h + 1) * HEAD_DIM]
            values[h] = jnp.concatenate([value, three], axis=1)
            queries[h] = q_ref[:, lanes]
        copies.wait()
        d_mixed = project_t(e, w_out).astype(BF)
        dot_t[...] = d_mixed.T
        for h in range(HEADS):
            grads[h] = d_mixed[:, h * HEAD_DIM : (h + 1) * HEAD_DIM]
        ones = jnp.ones((1, length), F32)

        def head(h, carry):
            rows = head_rows(h)
            do_t = dot_t[rows, :]
            q_n, do_n = queries[h], grads[h]
            delta = jnp.sum(do_t.astype(F32) * ot_ref[rows, :].astype(F32), axis=0, keepdims=True)
            q_t = below(qt_ref[rows, :], [ones] + low_parts(-lse_ref[h]))
            do_t = below(do_t, low_parts(-delta))
            total = None
            for at in range(0, frames, CHUNK):
                here = slice(at, at + CHUNK)
                p = jnp.exp(mm(keys[h, here], q_t))
                ds = (p * mm(values[h, here], do_t)).astype(BF)
                dv_h[h, here] = mm(p.astype(BF), do_n).astype(BF)
                dk_h[h, here] = mm(ds, q_n).astype(BF)
                more = mm(kvt_ref[rows, here], ds)
                total = more if total is None else total + more
            dqt[rows, :] = (total * HEAD_DIM ** (-0.5)).astype(BF)
            return carry

        lax.fori_loop(0, HEADS, head, 0)
        dq = dqt[...].T
        dq_ref[...] = dq
        part_ref[...] = mm_t(dq, w_q[...]).astype(BF)
        for h in range(HEADS):
            lanes = slice(h * HEAD_DIM, (h + 1) * HEAD_DIM)
            dkv_ref[:, lanes] = dk_h[h]
            dkv_ref[:, HALF + h * HEAD_DIM : HALF + (h + 1) * HEAD_DIM] = dv_h[h]

    return run(
        body,
        [
            shaped((length, D)),
            shaped((length, D), F32),
            shaped((length, D)),
            shaped((length, HALF)),
            shaped((frames, D)),
            shaped((2, D), F32),
        ],
        vmem=[d, hidden, mine, other, norms, nums, kv, kvt, q, qt, ot, lse],
        hbm=weights,
        scratch=[
            pltpu.VMEM((D, HALF), BF),
            pltpu.VMEM((2, HALF, HALF), BF),
            pltpu.VMEM((HEADS, frames, 2 * HEAD_DIM), BF),
            pltpu.VMEM((HEADS, frames, 2 * HEAD_DIM), BF),
            pltpu.VMEM((HEADS, length, HEAD_DIM), BF),
            pltpu.VMEM((HEADS, length, HEAD_DIM), BF),
            pltpu.VMEM((HALF, length), BF),
            pltpu.VMEM((HEADS, frames, HEAD_DIM), BF),
            pltpu.VMEM((HEADS, frames, HEAD_DIM), BF),
            pltpu.VMEM((HALF, length), BF),
        ],
        copies=4 + 16,
        micros=22,
        after=after,
    )


def self_backward(d, hidden, mine, other, norms, nums, qkv, qt, kt, ot, lse, weights, after=()):
    length = hidden.shape[0]

    def body(
        d_ref, hidden_ref, mine_ref, other_ref, norms_ref, nums_ref, qkv_ref, qt_ref, kt_ref,
        ot_ref, lse_ref, *refs
    ):
        w_refs, refs = refs[: len(weights)], refs[len(weights) :]
        part_ref, d_out_ref, e_ref, dqk_ref, dv_ref, terms_ref = refs[:6]
        w_qk, w_v, w_out, queries_h, keys, values, grads, dot_t, dk_h, dv_h, dqt, bias, sems = refs[6:]
        _, xy, _ = where_am_i()
        copies = Copies(sems)
        load_out(copies, w_refs, 0, xy, w_out)
        load_wide(copies, w_refs, 0, 0, xy, w_qk)
        load_wide(copies, w_refs, 0, 1, xy, w_v, HALF)
        d1, terms = step_back(d_ref, hidden_ref, mine_ref, other_ref, norms_ref[1:2])
        d_out_ref[...] = d1
        terms_ref[...] = terms
        e = d1.astype(BF)
        e_ref[...] = e
        places = lax.broadcasted_iota(jnp.int32, (length, length), 0)
        queries = lax.broadcasted_iota(jnp.int32, (length, length), 1)
        allowed = (places <= queries) & (places.astype(F32) < nums_ref[0:1, 0:1])
        bias[...] = jnp.where(allowed, 0.0, -1e30)
        three = widened(3)(length)
        for h in range(HEADS):
            at = h * HEAD_DIM
            queries_h[h] = qkv_ref[:, at : at + HEAD_DIM]
            key = qkv_ref[:, HALF + at : HALF + at + HEAD_DIM]
            keys[h] = jnp.concatenate([key, three], axis=1)
            value = qkv_ref[:, 2 * HALF + at : 2 * HALF + at + HEAD_DIM]
            values[h] = jnp.concatenate([value, three], axis=1)
        copies.wait()
        d_mixed = project_t(e, w_out).astype(BF)
        dot_t[...] = d_mixed.T
        for h in range(HEADS):
            grads[h] = d_mixed[:, h * HEAD_DIM : (h + 1) * HEAD_DIM]

        def head(h, carry):
            rows = head_rows(h)
            do_t, do_n = dot_t[rows, :], grads[h]
            delta = jnp.sum(do_t.astype(F32) * ot_ref[rows, :].astype(F32), axis=0, keepdims=True)
            q_t = below(qt_ref[rows, :], low_parts(-lse_ref[h]))
            do_t = below(do_t, low_parts(-delta))
            p = jnp.exp(mm(keys[h], q_t) + bias[...])
            ds = (p * mm(values[h], do_t)).astype(BF)
            dv_h[h] = mm(p.astype(BF), do_n).astype(BF)
            dk_h[h] = mm(ds, queries_h[h]).astype(BF)
            dqt[rows, :] = (mm(kt_ref[rows, :], ds) * HEAD_DIM ** (-0.5)).astype(BF)
            return carry

        lax.fori_loop(0, HEADS, head, 0)
        dqk_ref[:, 0:HALF] = dqt[...].T
        for h in range(HEADS):
            lanes = slice(HALF + h * HEAD_DIM, HALF + (h + 1) * HEAD_DIM)
            dqk_ref[:, lanes] = dk_h[h]
            dv_ref[:, h * HEAD_DIM : (h + 1) * HEAD_DIM] = dv_h[h]
        out = mm_t(dqk_ref[...], w_qk[...]) + mm_t(dv_ref[...], w_v[...])
        part_ref[...] = out.astype(BF)

    return run(
        body,
        [
            shaped((length, D)),
            shaped((length, D), F32),
            shaped((length, D)),
            shaped((length, D)),
            shaped((length, HALF)),
            shaped((2, D), F32),
        ],
        vmem=[d, hidden, mine, other, norms, nums, qkv, qt, kt, ot, lse],
        hbm=weights,
        scratch=[
            pltpu.VMEM((D, D), BF),
            pltpu.VMEM((D, HALF), BF),
            pltpu.VMEM((2, HALF, HALF), BF),
            pltpu.VMEM((HEADS, length, HEAD_DIM), BF),
            pltpu.VMEM((HEADS, length, 2 * HEAD_DIM), BF),
            pltpu.VMEM((HEADS, length, 2 * HEAD_DIM), BF),
            pltpu.VMEM((HEADS, length, HEAD_DIM), BF),
            pltpu.VMEM((HALF, length), BF),
            pltpu.VMEM((HEADS, length, HEAD_DIM), BF),
            pltpu.VMEM((HEADS, length, HEAD_DIM), BF),
            pltpu.VMEM((HALF, length), BF),
            pltpu.VMEM((length, length), F32),
        ],
        copies=ATTENTION_COPIES,
        micros=12,
        staged=True,
        after=after,
    )


def finish_hidden(d, hidden, mine, other, norms, terms1, terms2, terms3, after=()):
    length = hidden.shape[0]

    def body(
        d_ref, hidden_ref, mine_ref, other_ref, norms_ref, one, two, three, terms_ref, first_ref,
        second_ref, blocks
    ):
        d0, terms = step_back(d_ref, hidden_ref, mine_ref, other_ref, norms_ref[0:1])
        store_blocks(d0.astype(BF), blocks, first_ref, second_ref)
        for j in range(2):
            here = slice(j, j + 1)
            terms_ref[4 * j : 4 * j + 4] = jnp.concatenate(
                [terms[here], one[here], two[here], three[here]], axis=0
            )

    return run(
        body,
        [shaped((8, D), F32), shaped((QUARTER, length)), shaped((QUARTER, length))],
        vmem=[d, hidden, mine, other, norms, terms1, terms2, terms3],
        scratch=[pltpu.VMEM((4, length, QUARTER), BF)],
        micros=4,
        after=after,
    )


def finish_encoder(keep, other, frames, after=()):
    def body(keep_ref, other_ref, first_ref, second_ref):
        _, _, z = where_am_i()
        for ref, k in ((first_ref, 0), (second_ref, 1)):
            here = pl.ds(pl.multiple_of(((z + k) % 2) * QUARTER, QUARTER), QUARTER)
            total = keep_ref[here, :].astype(F32) + other_ref[here, :].astype(F32)
            ref[...] = total.astype(BF)[:, :frames]

    return run(
        body,
        [shaped((QUARTER, frames)), shaped((QUARTER, frames))],
        vmem=[keep, other],
        micros=2,
        after=after,
    )


def block_plan(place):
    if not place.fast:
        return 1, (((1, 0, 0),), ((1, 0, 0),))
    first = ((1, 0, 0), (0, 0, 1), (1, 1, 2), (0, 1, 3))
    second = ((1, 0, 0), (1, 1, 1), (0, 0, 2), (0, 1, 3))
    return 4, (first, second)


def grad_outputs(place, shape):
    if place.fast:
        return [shaped((2,) + shape)] * 4
    return [shaped((1,) + shape)] * 4


def units_grads(place, mt, dz, it, e):
    chips = place.chips
    rows = D // (2 * chips)
    _, plan = block_plan(place)

    def body(mt_ref, dz_ref, it_ref, e_ref, *outs):
        _, xy, _ = where_am_i()
        for output, slot, offset in plan[1]:
            chip = xy ^ offset
            for z in range(4):
                here = pl.ds(pl.multiple_of(z * HALF + chip * rows, 16), rows)
                outs[2 + output][slot, z] = mm(it_ref[here, :], e_ref[...]).astype(BF)
        for output, slot, offset in plan[0]:
            here = pl.ds(pl.multiple_of((xy ^ offset) * 2 * rows, 16), 2 * rows)
            left = mm(mt_ref[here, :], dz_ref[...]).astype(BF)
            for z in range(4):
                outs[output][slot, z] = left[:, z * HALF : (z + 1) * HALF]

    def plain(mt_ref, dz_ref, it_ref, e_ref, left_ref, right_ref):
        left_ref[...] = mm(mt_ref[...], dz_ref[...]).astype(BF)
        right_ref[...] = mm(it_ref[...], e_ref[...]).astype(BF)

    if place.fast:
        first, second = shaped((2, 4, 2 * rows, HALF)), shaped((2, 4, rows, D))
        return run(
            body, [first, first, second, second], vmem=[mt, dz, it, e], micros=6
        )
    left, right = run(
        plain, [shaped((D, 2 * D)), shaped((2 * D, D))], vmem=[mt, dz, it, e], micros=7
    )
    left = left.reshape(chips, 2 * rows, 4, HALF).transpose(0, 2, 1, 3)
    right = right.reshape(4, chips, rows, 2, HALF).transpose(1, 0, 3, 2, 4)
    whole = jnp.concatenate([left, right.reshape(chips, 4, 2 * rows, HALF)], axis=-1)
    return whole.reshape(4 * chips, 2 * rows, D)


def units_sum(grads, came, onward, after):
    rows = grads[3].shape[2]

    def body(*refs):
        ins, (kept_ref, sent_ref, left, right, blocks, sems) = refs[:6], refs[6:]
        _, _, mp = where_am_i()
        copies = Copies(sems)
        for i, ref in enumerate(ins):
            target = (left if i < 3 else right).at[i % 3]
            copies.start(ref if i % 3 == 2 else ref.at[0], target)
        copies.wait()
        for z in range(4):
            blocks[z, :, 0:HALF] = add_up(*[left[i, z] for i in range(3)]).astype(BF)
            down = add_up(*[right[i, z] for i in range(3)]).astype(BF)
            blocks[z, 0:rows, HALF:D] = down[:, :HALF]
            blocks[z, rows : 2 * rows, HALF:D] = down[:, HALF:]
        for i in range(2):
            kept_ref[i] = blocks[mp ^ (2 * i)]
            sent_ref[i] = blocks[mp ^ (2 * i + 1)]

    return run(
        body,
        [shaped((2, 2 * rows, D)), shaped((2, 2 * rows, D))],
        hbm=[grads[1], came[0], onward[0], grads[3], came[1], onward[1]],
        scratch=[
            pltpu.VMEM((3, 4, 2 * rows, HALF), BF),
            pltpu.VMEM((3, 4, rows, D), BF),
            pltpu.VMEM((4, 2 * rows, D), BF),
        ],
        copies=6,
        micros=3,
        after=after,
    )


def add_second(kept, came, after):
    def body(kept_ref, came_ref, out_ref, held, sems):
        copies = Copies(sems)
        copies.start(kept_ref.at[1], held.at[0])
        copies.start(came_ref.at[1], held.at[1])
        copies.wait()
        out_ref[...] = add_up(held[0], held[1]).astype(BF)

    shape = kept.shape[1:]
    return run(
        body,
        [shaped(shape)],
        hbm=[kept, came],
        scratch=[pltpu.VMEM((2,) + shape, BF)],
        copies=2,
        micros=1,
        after=after,
    )[0]


def cut_units(kept, came, last, after):
    rows = last.shape[0] // 2

    def body(kept_ref, came_ref, last_ref, mine_ref, sent_ref, down_ref, held, sems):
        core, _, _ = where_am_i()
        copies = Copies(sems)
        copies.start(kept_ref.at[0], held.at[0])
        copies.start(came_ref.at[0], held.at[1])
        copies.start(last_ref, held.at[2])
        copies.wait()
        mine = pl.ds(pl.multiple_of(core * rows, 16), rows)
        theirs = pl.ds(pl.multiple_of((1 - core) * rows, 16), rows)
        mine_ref[...] = add_up(*[held[i, mine, 0:HALF] for i in range(3)]).astype(BF)
        sent_ref[...] = add_up(*[held[i, theirs, 0:HALF] for i in range(3)]).astype(BF)
        down_ref[:, 0:HALF] = add_up(*[held[i, 0:rows, HALF:D] for i in range(3)])
        down_ref[:, HALF:D] = add_up(*[held[i, rows : 2 * rows, HALF:D] for i in range(3)])

    return run(
        body,
        [shaped((rows, HALF)), shaped((rows, HALF)), shaped((rows, D), F32)],
        hbm=[kept, came, last],
        scratch=[pltpu.VMEM((3, 2 * rows, D), BF)],
        copies=3,
        micros=1,
        after=after,
    )


def join_units(place, kept, came):
    rows = kept.shape[0]

    def body(kept_ref, came_ref, up_ref, both):
        core, _, _ = where_am_i()
        both[core] = kept_ref[...]
        both[1 - core] = came_ref[...]
        blocks = []
        for chip in range(place.chips):
            for parity in range(2):
                blocks.append(both[parity, :, chip * rows : (chip + 1) * rows].astype(F32))
        up_ref[...] = jnp.concatenate(blocks, axis=1)

    return run(
        body,
        [shaped((rows, D), F32)],
        vmem=[kept, came],
        scratch=[pltpu.VMEM((2, rows, HALF), BF)],
        micros=1,
    )[0]


def attention_grads(place, wide_left, wide_right, left, right, ot, e, after=()):
    count, plan = block_plan(place)
    rows = D // count
    few = rows // 4

    def body(wide_left_ref, wide_right_ref, left_ref, right_ref, ot_ref, e_ref, *outs):
        _, xy, _ = where_am_i()
        for output, slot, offset in plan[0]:
            chip = xy ^ offset if count > 1 else 0
            here = pl.ds(pl.multiple_of(chip * rows, 16), rows)
            outs[output][slot] = mm(wide_left_ref[here, :], wide_right_ref[...]).astype(BF)
        for output, slot, offset in plan[1]:
            chip = xy ^ offset if count > 1 else 0
            here = pl.ds(pl.multiple_of(chip * rows, 16), rows)
            target = outs[2 + output]
            target[slot, :, 0:HALF] = mm(left_ref[here, :], right_ref[...]).astype(BF)
            for hi in range(2):
                here = pl.ds(pl.multiple_of(hi * QUARTER + chip * few, 16), few)
                both = mm(ot_ref[here, :], e_ref[...]).astype(BF)
                for q in range(2):
                    at = (2 * q + hi) * few
                    target[slot, at : at + few, HALF:D] = both[:, q * HALF : (q + 1) * HALF]

    return run(
        body,
        grad_outputs(place, (rows, D)),
        vmem=[wide_left, wide_right, left, right, ot, e],
        micros=6,
        after=after,
    )


def encoder_grad(dkv, weights, after=()):
    padded = dkv.shape[0]

    def body(dkv_ref, *refs):
        w_refs, (keep_ref, send_ref, w_kv, sems) = refs[: len(weights)], refs[len(weights) :]
        core, xy, _ = where_am_i()
        copies = Copies(sems)
        load_wide(copies, w_refs, 1, 0, xy, w_kv)
        copies.wait()
        mine = pl.ds(pl.multiple_of(core * HALF, HALF), HALF)
        theirs = pl.ds(pl.multiple_of((1 - core) * HALF, HALF), HALF)
        for ref, rows in ((send_ref, theirs), (keep_ref, mine)):
            for at in range(0, padded, CHUNK):
                value = mm_t(w_kv[rows, :], dkv_ref[at : at + CHUNK, :])
                ref[:, at : at + CHUNK] = value.astype(BF)

    return run(
        body,
        [shaped((HALF, padded)), shaped((HALF, padded))],
        vmem=[dkv],
        hbm=weights,
        scratch=[pltpu.VMEM((D, D), BF)],
        copies=4,
        micros=3.5,
        after=after,
    )


def leave_plane(place, grads):
    return [place.swap_xy(grads[0], 1), place.swap_xy(grads[2], 2)]


def pass_on(grads, came, after):
    shapes = [grads[1].shape[1:], grads[3].shape[1:]]

    def body(stay0, came0, stay1, came1, out0, out1, held0, held1, sems):
        copies = Copies(sems)
        for i, ref in enumerate((stay0, came0, stay1, came1)):
            copies.start(ref.at[1], (held0 if i < 2 else held1).at[i % 2])
        copies.wait()
        out0[...] = add_up(held0[0], held0[1]).astype(BF)
        out1[...] = add_up(held1[0], held1[1]).astype(BF)

    return run(
        body,
        [shaped(shape) for shape in shapes],
        hbm=[grads[1], came[0], grads[3], came[1]],
        scratch=[pltpu.VMEM((2,) + shape, BF) for shape in shapes],
        copies=4,
        micros=1,
        after=after,
    )


def cross_plane(place, onward):
    return [place.swap_xy(onward[0], 2), place.swap_xy(onward[1], 1)]


def column_blocks(grads, came, onward, norm_terms=(), after=()):
    shape = onward[0].shape
    rows = shape[-2] // 2
    width = D
    few = rows // 4
    extra = 16 if norm_terms else 0

    def body(*refs):
        terms_refs, refs = refs[: len(norm_terms)], refs[len(norm_terms) :]
        ins, outs, (held, shards, sems) = refs[:6], refs[6:-3], refs[-3:]
        home, slots = column_slots()
        copies = Copies(sems)
        for i, ref in enumerate(ins):
            copies.start(ref if i % 3 == 2 else ref.at[0], held.at[i])
        copies.wait()
        sums = [add_up(held[3 * part], held[3 * part + 1], held[3 * part + 2]) for part in range(2)]
        for hi in range(2):
            for cs in range(2):
                here = slice(cs * rows, (cs + 1) * rows)
                lanes = slice(hi * QUARTER, (hi + 1) * QUARTER)
                lanes_two = slice(HALF + hi * QUARTER, HALF + (hi + 1) * QUARTER)
                outs_rows = []
                for p in range(4):
                    at = (2 * (p // 2) + hi) * 2 * few + cs * few
                    side = HALF + (p % 2) * QUARTER
                    outs_rows.append(sums[1][at : at + few, side : side + QUARTER])
                value = jnp.concatenate(
                    [
                        sums[0][here, lanes],
                        sums[0][here, lanes_two],
                        sums[1][here, lanes],
                        jnp.concatenate(outs_rows, axis=0),
                    ],
                    axis=1,
                )
                shards[2 * hi + cs, :rows] = value.astype(BF)
        if norm_terms:
            core, xy, _ = where_am_i()
            terms = add_up(*[ref[...] for ref in terms_refs])
            terms = jnp.concatenate([terms, jnp.zeros_like(terms)], axis=0).astype(BF)
            feature = lax.broadcasted_iota(jnp.int32, (D, D), 0)
            lane = lax.broadcasted_iota(jnp.int32, (D, D), 1)
            for hi in range(2):
                for cs in range(2):
                    offset = (2 * core + hi) * QUARTER + (2 * xy + cs) * few
                    pick = jnp.where((feature == lane + offset) & (lane < few), 1.0, 0.0)
                    shards[2 * hi + cs, rows:] = mm(terms, pick.astype(BF)).astype(BF)
        for k in range(4):
            outs[k][...] = shards[slots[k]]

    ins = [grads[1], came[0], onward[0], grads[3], came[1], onward[1]]
    return run(
        body,
        [shaped((rows + extra, width))] * 4,
        vmem=list(norm_terms),
        hbm=ins,
        after=after,
        scratch=[pltpu.VMEM((6,) + shape, BF), pltpu.VMEM((4, rows + extra, width), BF)],
        copies=6,
        micros=2,
    )


def sum_plain(place, grads, attention):
    wide, narrow = grads[1][0], grads[3][0]
    rows = D // place.dp
    if attention:
        value = jnp.stack([wide[:, :HALF], wide[:, HALF:], narrow[:, :HALF]], axis=1)
        value = value.reshape(place.dp, rows, 3, 2, QUARTER).transpose(3, 0, 1, 2, 4)
        value = value.reshape(2, place.dp, rows, 3 * QUARTER)
        outs = narrow[:, HALF:].reshape(2, 2, place.dp, rows // 4, 2, QUARTER)
        outs = outs.transpose(1, 2, 0, 4, 3, 5).reshape(2, place.dp, rows, QUARTER)
        value = jnp.concatenate([value, outs], axis=-1)
    else:
        value = jnp.concatenate(
            [wide.reshape(2, place.dp, rows, D), narrow.reshape(2, place.dp, rows, D)], axis=-1
        )
    whole = jnp.zeros((2,) + value.shape, F32)
    whole = lax.dynamic_update_index_in_dim(whole, value.astype(F32), place.core, 0)
    whole = whole.reshape((4 * place.dp,) + value.shape[2:])
    return lax.psum_scatter(whole, ("mp", "xy", "core"), scatter_dimension=0, tiled=False)


def attention_outputs(sums, rows, few):
    value = sums[:rows]
    last = value[:, 3 * QUARTER :]
    out = jnp.concatenate([last[p * few : (p + 1) * few] for p in range(4)], axis=1)
    return [value[:, j * QUARTER : (j + 1) * QUARTER] for j in range(3)], out


def finish_self(got, own, few_lanes):
    rows = own.shape[0] - 16
    few = rows // 4

    def body(a, b, c, d, own_ref, qkv_ref, out_ref, gain_ref, bias_ref):
        home, _ = column_slots()
        last = jnp.where(home, own_ref[...].astype(F32), d[...].astype(F32))
        sums = add_up(a[...], b[...], c[...], last)
        blocks, out = attention_outputs(sums, rows, few)
        for j in range(3):
            qkv_ref[j] = blocks[j]
        out_ref[...] = out
        gain_ref[...] = sums[rows : rows + 4, :few_lanes]
        bias_ref[...] = sums[rows + 4 : rows + 8, :few_lanes]

    return run(
        body,
        [
            shaped((3, rows, QUARTER), F32),
            shaped((few, D), F32),
            shaped((4, few_lanes), F32),
            shaped((4, few_lanes), F32),
        ],
        vmem=list(got) + [own],
        micros=1.5,
    )


def finish_cross(got, own, after=()):
    rows = own.shape[0]
    few = rows // 4

    def body(a, b, c, d, own_ref, kv_ref, q_ref, out_ref):
        home, _ = column_slots()
        last = jnp.where(home, own_ref[...].astype(F32), d[...].astype(F32))
        blocks, out = attention_outputs(add_up(a[...], b[...], c[...], last), rows, few)
        kv_ref[...] = jnp.concatenate(blocks[:2], axis=1)
        q_ref[...] = blocks[2]
        out_ref[...] = out

    return run(
        body,
        [shaped((rows, HALF), F32), shaped((rows, QUARTER), F32), shaped((few, D), F32)],
        vmem=list(got) + [own],
        micros=1.5,
        after=after,
    )


def join_rows(blocks, got, dtype, after=()):
    width, rows = blocks[0].shape

    def body(block_ref, first_ref, second_ref, out_ref):
        home, _ = column_slots()
        _, _, z = where_am_i()

        @pl.when(home)
        def _():
            out_ref[z % 2] = block_ref[...].astype(dtype)

        @pl.when(jnp.logical_not(home))
        def _():
            out_ref[z % 2] = first_ref[...].astype(dtype)

        out_ref[(z + 1) % 2] = second_ref[...].astype(dtype)

    joined = run(
        body,
        [shaped((2, width, rows), dtype)],
        vmem=[blocks[0]] + list(got),
        micros=2,
        after=after,
    )[0]
    return joined[:, None].transpose(0, 1, 3, 2)


def from_quarters(value):
    few = value.shape[0] // 4
    return value.reshape(4, few, QUARTER).transpose(1, 0, 2).reshape(few, D)


def three_parts(value):
    terms = []
    for _ in range(3):
        term = lax.reduce_precision(value, 8, 7)
        terms.append(term.astype(BF))
        value = value - term
    return jnp.concatenate(terms)


def per_device(
    dp,
    mp,
    hidden_in,
    encoder_states,
    cotangent,
    self_qkv,
    self_out,
    cross_q,
    cross_kv,
    cross_out,
    fc_in,
    fc_out,
    ln_gain,
    ln_bias,
    token_lengths,
    audio_lengths,
    corpus_ids,
    corpus_weights,
):
    place = Place(dp, mp)
    length = hidden_in.shape[2]
    frames = encoder_states.shape[2]
    padded = -(-frames // CHUNK) * CHUNK
    rows = self_qkv.shape[0]

    encoded = lax.dynamic_index_in_dim(encoder_states[:, 0], place.micro, 0, keepdims=False)
    first = ()
    if place.fast:
        shard = attention_shard(self_qkv, self_out, cross_kv, cross_q, cross_out)
        packed = pack_attention(place.column_out(shard), shard, (encoded,))
        w_self = w_cross = spread(place, packed)
        first = (shard,)
    else:
        quarter = lambda w: w.reshape(-1, 4, QUARTER).transpose(1, 0, 2).reshape(-1, QUARTER)
        flat = lambda w: w.reshape(rows, -1)
        w_self = attention_plain(
            place, jnp.concatenate([flat(self_qkv), quarter(self_out)], axis=1)
        )
        w_cross = attention_plain(
            place, jnp.concatenate([flat(cross_kv), cross_q, quarter(cross_out)], axis=1)
        )


    unit = unit_shard(place, fc_in, fc_out)
    if not place.fast:
        w_units = gather_units(place, unit)

    turned = lambda value: value[:, 0].transpose(0, 2, 1)
    numbers = jnp.concatenate([token_lengths.T, audio_lengths.T, corpus_ids.T])
    blocks = input_blocks(
        turned(hidden_in),
        three_parts(jnp.concatenate([ln_gain, ln_bias])),
        numbers,
        first,
    )
    got = place.rows_in(blocks)
    if place.fast:
        unit, got = lax.optimization_barrier((unit, got))
        column = [unit] + [place.swap_z(unit, k) for k in (1, 2, 3)]
        got, column, encoded = lax.optimization_barrier((got, column, encoded))
        stacked = stack_units(column, tuple(w_self[3:5]))
        w_units = spread(place, stacked)
    hidden, norms, nums = prepare(got, place.swap_core(got), corpus_weights)

    other = place.move(encoded, lambda xy, core, z: (xy, 1 - core, z) if core == z // 2 else None)
    encoded = jnp.where(place.home == place.core, encoded, other)
    encoded = jnp.pad(encoded, ((0, padded - frames), (0, 0)))

    part1, at, qkv, qt, kt, ot1, lse1 = self_forward(hidden, norms, nums, w_self)
    et = turn(encoded, (part1,))
    other1 = place.swap_core(part1)
    got = place.rows_in(turned_blocks(turned(cotangent), (at,)))
    kv, kvt = cross_memory(encoded, w_cross)
    part2, h1, ct, q2, qt2, ot2, lse2 = cross_forward(
        hidden, part1, other1, norms, nums, kv, kvt, w_cross
    )
    other2 = place.swap_core(part2)
    cot = prepare_cotangent(got, place.swap_core(got), (part2,))
    part3, h2, mt, slope, it = units_forward(h1, part2, other2, norms, w_units)
    other3 = place.swap_core(part3)
    part, d3, e3, dz, terms3, out_a, out_b = units_backward(
        h2, part3, other3, norms, nums, cot, slope, w_units
    )
    other = place.swap_core(part)
    g_units = units_grads(place, mt, dz, it, e3)
    came_units = leave_plane(place, g_units) if place.fast else None
    layer_got = place.rows_sent((out_a, out_b))
    layer_out = place.rows_joined((out_a, out_b), layer_got)
    part, d2, e2, dq2, dkv, terms2 = cross_backward(
        d3, h2, part, other, norms, nums, kv, kvt, q2, qt2, ot2, lse2, w_cross, layer_got
    )
    other = place.swap_core(part)
    keep, send = encoder_grad(dkv, w_cross)
    came = place.swap_core(send)
    passed = pass_on(g_units, came_units, (keep,)) if place.fast else ()
    encoder_blocks = finish_encoder(keep, came, frames, passed)
    encoder_got = place.rows_sent(encoder_blocks)
    part, d1, e1, dqk, dv, terms1 = self_backward(
        d2, h1, part, other, norms, nums, qkv, qt, kt, ot1, lse1, w_self, encoder_blocks
    )
    other = place.swap_core(part)
    held = (e1,)
    if place.fast:
        onward_units = cross_plane(place, passed)
        kept, sent = units_sum(g_units, came_units, onward_units, held)
        came_units = place.swap_z(sent, 1)
        held = (kept,)
    g_self = attention_grads(place, at, dqk, at, dv, ot1, e1, held)
    terms, out_a, out_b = finish_hidden(
        d1, hidden, part, other, norms, terms1, terms2, terms3, (g_self[0],)
    )
    hidden_got = place.rows_sent((out_a, out_b))
    g_cross = attention_grads(place, et, dkv, ct, dq2, ot2, e2, [terms] + encoder_got)
    if place.fast:
        came_self = leave_plane(place, g_self)
        near_terms = place.swap_xy(terms, 1)
        g_cross, near_terms = lax.optimization_barrier((g_cross, near_terms))
        came_cross = leave_plane(place, g_cross)
        passed = pass_on(g_self, came_self, (g_cross[0], near_terms))
        onward_self = cross_plane(place, passed)
        second = add_second(kept, came_units, passed)
        last_units = place.swap_z(second, 2)
        passed = pass_on(g_cross, came_cross, (second,))
        onward_cross = cross_plane(place, passed)

    few = D // (place.dp * place.mp)
    if place.fast:
        terms = terms + near_terms
        blocks = column_blocks(
            g_self, came_self, onward_self, (terms, place.swap_xy(terms, 2)), passed
        )
        self_got = place.column_back(blocks)
        cross_blocks = column_blocks(g_cross, came_cross, onward_cross, (), (blocks[0],))
        cross_got = place.column_back(cross_blocks)
        grad_encoder = join_rows(encoder_blocks, encoder_got, F32, (cross_blocks[0],))
        mine, sent, s_down = cut_units(kept, came_units, last_units, (cross_blocks[0],))
        s_up = join_units(place, mine, place.swap_core(sent))
        grad_hidden = join_rows((out_a, out_b), hidden_got, F32, (cross_blocks[0],))
        g_qkv, g_out, g_gain, g_bias = finish_self(self_got, blocks[3], few)
        g_ckv, g_cq, g_cout = finish_cross(cross_got, cross_blocks[3], (g_out,))
        g_qkv = g_qkv.transpose(1, 0, 2)
    else:
        s_up, s_down = scatter_units(place, g_units)
        grad_encoder = place.rows_joined(encoder_blocks, encoder_got).astype(F32)
        grad_hidden = place.rows_joined((out_a, out_b), hidden_got).astype(F32)
        s_cross = sum_plain(place, g_cross, True)
        s_self = sum_plain(place, g_self, True)
        terms = jnp.where(place.core == 0, terms, 0.0)
        terms = lax.psum(terms, AXES)
        shares = lax.dynamic_slice_in_dim(terms, (place.z * place.dp + place.d) * few, few, 1)
        g_gain, g_bias = shares[:4], shares[4:]
        g_qkv, g_out = s_self[:, : 3 * QUARTER], from_quarters(s_self[:, 3 * QUARTER :])
        g_ckv, g_cq = s_cross[:, :HALF], s_cross[:, HALF : 3 * QUARTER]
        g_cout = from_quarters(s_cross[:, 3 * QUARTER :])
    return (
        layer_out,
        grad_hidden,
        grad_encoder,
        g_qkv.reshape(rows, 3, QUARTER),
        g_out,
        g_cq,
        g_ckv.reshape(rows, 2, QUARTER),
        g_cout,
        s_up,
        s_down,
        g_gain,
        g_bias,
    )


def solution(mesh):
    dp, mp = mesh.shape["dp"], mesh.shape["mp"]
    finer = Mesh(mesh.devices.reshape(dp // 2, 2, mp), AXES)
    both = ("xy", "core")
    rows = P(None, both, None, "mp")
    columns = P(both, None, "mp")
    pairs = P(both, "mp")
    units = P(("mp",) + both, None)
    each = P(None, both)
    return jax.shard_map(
        partial(per_device, dp, mp),
        mesh=finer,
        in_specs=(
            rows,
            P(None, both, None, None),
            rows,
            columns,
            units,
            pairs,
            columns,
            units,
            pairs,
            units,
            P(None, "mp"),
            P(None, "mp"),
            each,
            each,
            each,
            P(),
        ),
        out_specs=(
            rows,
            rows,
            rows,
            columns,
            units,
            pairs,
            columns,
            units,
            pairs,
            units,
            P(None, ("mp",) + both),
            P(None, ("mp",) + both),
        ),
        check_vma=False,
    )
```
